32 devices in a mesh: expert: 8 (over z, y), tensor: 4 (over x, core).
Axes of the slice: x: 2, y: 2, z: 4, core: 2. Of those that a mesh axis runs over, the one named last changes fastest.
Arguments:
- tokens_in: bfloat16 [2048, 2048], P('expert'), may hold values from -6 to 6
- out_grad: bfloat16 [2048, 2048], P('expert'), may hold values from -6 to 6
- w_qkv: float32 [3, 2048, 2048], P(None, 'expert', 'tensor'), may hold values from -0.125 to 0.125
- w_attn_out: float32 [2048, 2048], P('tensor', 'expert'), may hold values from -3 to 3
- attn_gain: float32 [2048], P('expert'), may hold values from 0.5 to 2
- ffn_gain: float32 [2048], P('expert'), may hold values from 0.5 to 2
- qk_gain: float32 [2, 16, 128], P(None, 'tensor', 'expert'), may hold values from 0.6 to 1.6
- w_router: float32 [2048, 16], P('expert'), may hold values from -0.0625 to 0.0625
- w_gate: float32 [16, 2048, 1024], P('expert', None, 'tensor'), may hold values from -0.125 to 0.125
- w_up: float32 [16, 2048, 1024], P('expert', None, 'tensor'), may hold values from -0.125 to 0.125
- w_down: float32 [16, 1024, 2048], P('expert', 'tensor'), may hold values from -2.5 to 2.5
- routes: int32 [2048, 8], P('expert'), may hold values from 0 to 15, all different within a row; in each aligned block of 256 rows (0 to 255, 256 to 511, ...) at most 192 rows name the same one
- segments: int32 [2048], replicated, may hold values from 0 to 2, as said below
Outputs:
- block_out: bfloat16 [2048, 2048], P('expert')
- tokens_grad: bfloat16 [2048, 2048], P('expert')
- grad_w_qkv: float32 [3, 2048, 2048], P(None, 'expert', 'tensor')
- grad_w_attn_out: float32 [2048, 2048], P('tensor', 'expert')
- grad_attn_gain: float32 [2048], P('expert')
- grad_ffn_gain: float32 [2048], P('expert')
- grad_qk_gain: float32 [2, 16, 128], P(None, 'tensor', 'expert')
- grad_w_router: float32 [2048, 16], P('expert')
- grad_w_gate: float32 [16, 2048, 1024], P('expert', None, 'tensor')
- grad_w_up: float32 [16, 2048, 1024], P('expert', None, 'tensor')
- grad_w_down: float32 [16, 1024, 2048], P('expert', 'tensor')
The draws below stay inside these ranges and needn't reach their ends.
Inputs may be any that keep to these rules, and one draw needn't show every extreme that they name: `routes`: each row names 8 different experts; among the 256 rows of one device no expert is named more than 192 times, and in every draw some device's rows name some expert exactly 192 times. `segments`: document numbers never fall; every sequence of 2048 tokens holds exactly three documents, the first beginning at its first token, the second within its first 128 tokens and the third within its last 128 tokens.
All inputs are finite; a program needn't handle non-finite values.
Results may differ from the reference program's by a relative error of at most 0.03.
Values may be sent and summed in bfloat16 or wider, within the bound.
A program may use at most 256 MiB of HBM per device.

```python
import math
import jax
import jax.numpy as jnp
import numpy as np
from jax import lax

D = 2048
HEADS = 16
HEAD = 128
HID = 1024
TOP = 8
WINDOW = 1024
SEQ = 2048
TOK_DEV = 256
EXPERTS = 16
TOKENS = 2048
CAP = 192
N_EXPERT = 8
N_TENSOR = 4


def draw_segments(key, part):
    key = jax.random.fold_in(key, 17)
    first_key, second_key = jax.random.split(key)
    sequences = TOKENS // SEQ
    half_block = TOK_DEV // 2
    first_start = jax.random.randint(first_key, (sequences,), 1, half_block)
    second_start = jax.random.randint(second_key, (sequences,), SEQ - half_block, SEQ)
    index = jnp.arange(TOKENS, dtype=jnp.int32)
    within = index % SEQ
    sequence_id = index // SEQ
    later_one = (within >= first_start[sequence_id]).astype(jnp.int32)
    later_two = (within >= second_start[sequence_id]).astype(jnp.int32)
    return (3 * sequence_id + later_one + later_two).astype(jnp.int32)


def block_scale(rng, dims, cuts, least, high):
    gain, own = 1.0, jax.random.fold_in(rng, 6)
    for dim, blocks in cuts:
        heights = jnp.exp(jax.random.uniform(jax.random.fold_in(own, dim), (blocks,), jnp.float32, least / len(cuts), high / len(cuts)))
        gain = gain * jnp.repeat(heights, dims[dim] // blocks).reshape([-1 if axis == dim else 1 for axis in range(len(dims))])
    return gain


def deal_out(own_key, own, number, rows, amount, top, bound, lean):
    ranking = jax.random.permutation(own_key, amount)
    crowded, common = load_shares(amount, rows * top, bound, lean, True), load_shares(amount, rows * top, bound, lean, False)
    places = jnp.arange(amount)

    def named(lengths, offset_by):
        used = int((lengths > 0).sum())
        fixed = max(1, used // 4)
        moved = fixed + (places - fixed + offset_by * (used - fixed)) % max(1, amount - fixed)
        return jnp.zeros((amount,), jnp.int32).at[ranking[jnp.where(places < fixed, places, moved)]].set(jnp.asarray(lengths, jnp.int32))

    lengths = jnp.where(number % 4 == 0, named(crowded, number // 4), named(common, number - number // 4 - 1))
    mixed = jax.random.permutation(jax.random.fold_in(own, 3), amount)
    source_of, receiver = mixed[0:amount // 2 * 2:2], mixed[1:amount // 2 * 2:2]
    room = jnp.minimum(lengths[source_of] - 1, bound - lengths[receiver]) // 2
    room = jnp.where((source_of == ranking[0]) | (receiver == ranking[0]) | (lengths[receiver] == 0), 0, jnp.maximum(room, 0))
    moved = jax.random.randint(jax.random.fold_in(own, 4), (amount // 2,), 0, 1 << 20) % (room + 1)
    lengths = lengths.at[source_of].add(-moved).at[receiver].add(moved)
    items = jnp.searchsorted(jnp.cumsum(lengths), jnp.arange(rows * top), side="right").astype(jnp.int32)
    table = items.reshape(top, rows).T
    table = table[jax.random.permutation(jax.random.fold_in(own, 1), rows)]
    offset_by = jax.random.randint(jax.random.fold_in(own, 2), (rows, 1), 0, top)
    return jnp.take_along_axis(table, (jnp.arange(top)[None, :] + offset_by) % top, axis=1)


def load_shares(count, total, reach, lean, full):
    loads = [(1 << 20) // math.isqrt(grade ** lean) + 1 for grade in range(1, count + 1)]
    largest = reach if full else min(reach, max(-(-total // count), total * loads[0] // sum(loads)))
    least = 1 if total - largest >= count - 1 else 0
    given, rest = [largest] + [least] * (count - 1), total - largest - least * (count - 1)
    while rest > 0:
        candidates = [i for i in range(1, count) if given[i] < largest] or [i for i in range(1, count) if given[i] < reach]
        pool, budget = sum([loads[i] for i in candidates]), rest
        for i in candidates:
            more = min(reach - given[i], max(1, budget * loads[i] // pool), rest)
            given[i] = given[i] + more
            rest = rest - more
    return np.array(given)


def bell_draw(key, shape, deviation, bound, cuts=(), kind=jnp.bfloat16):
    values = jax.random.normal(key, shape, jnp.float32) * deviation
    if len(cuts) > 0:
        values = block_scale(key, shape, cuts, -0.22, 0.18) * values
    return jnp.clip(values, min=-bound, max=bound).astype(kind)


def setup_inputs(seed: int = 0) -> dict:
    keys = jax.random.split(jax.random.key(seed), 14)
    tokens_in = bell_draw(keys[0], (TOKENS, D), 1.0, 6.0, ((0, 8),))
    out_grad = bell_draw(keys[1], (TOKENS, D), 1.0, 6.0, ((0, 8),))
    w_qkv = bell_draw(keys[2], (3, D, D), D ** -0.5, 0.125, ((1, 8), (2, 4)), jnp.float32)
    w_attn_out = bell_draw(keys[3], (D, D), (max(D // 512, 1)) ** -0.5, 3.0, ((0, 4), (1, 8)), jnp.float32)
    attn_gain = jnp.clip(jnp.exp(math.log(2.0) - 1.3862944 * jax.random.uniform(keys[4], (D,), jnp.float32) ** block_scale(keys[4], (D,), ((0, 8),), -0.2, 0.2)), 0.5, 2.0)
    ffn_gain = jnp.clip(jnp.exp(math.log(2.0) - 1.3862944 * jax.random.uniform(keys[5], (D,), jnp.float32) ** block_scale(keys[5], (D,), ((0, 8),), -0.2, 0.2)), 0.5, 2.0)
    qk_gain = jnp.clip(jnp.exp(math.log(1.6) - 0.98082923 * jax.random.uniform(keys[6], (2, HEADS, HEAD), jnp.float32) ** block_scale(keys[6], (2, HEADS, HEAD), ((1, 4), (2, 8)), -0.2, 0.2)), 0.6, 1.6)
    w_router = bell_draw(keys[7], (D, EXPERTS), (4 * D) ** -0.5, 0.0625, ((0, 8),), jnp.float32)
    w_gate = bell_draw(keys[8], (EXPERTS, D, HID), D ** -0.5, 0.125, ((0, 8), (2, 4)), jnp.float32)
    w_up = bell_draw(keys[9], (EXPERTS, D, HID), D ** -0.5, 0.125, ((0, 8), (2, 4)), jnp.float32)
    w_down = bell_draw(keys[10], (EXPERTS, HID, D), (HID // 256 + 1) ** -0.5, 2.5, ((0, 8), (1, 4)), jnp.float32)
    routes_keys = jax.random.split(jax.random.fold_in(keys[11], 1), TOKENS // TOK_DEV)
    routes_turns = jax.random.permutation(jax.random.fold_in(keys[11], 3), TOKENS // TOK_DEV)
    routes = jax.vmap(lambda own, number: deal_out(jax.random.fold_in(keys[11], 2), own, number, TOK_DEV, EXPERTS, TOP, CAP, 1))(routes_keys, routes_turns).reshape((TOKENS, TOP))
    segments = draw_segments(jax.random.fold_in(keys[13], 71), 0)
    return {"tokens_in": tokens_in, "out_grad": out_grad, "w_qkv": w_qkv, "w_attn_out": w_attn_out, "attn_gain": attn_gain, "ffn_gain": ffn_gain, "qk_gain": qk_gain, "w_router": w_router, "w_gate": w_gate, "w_up": w_up, "w_down": w_down, "routes": routes, "segments": segments}


EPS = 1e-05
THETA = 10000.0
HIGH = lax.Precision.HIGHEST

@jax.custom_vjp
def low(v):
    return lax.optimization_barrier(v.astype(jnp.bfloat16)).astype(jnp.float32)

@jax.custom_vjp
def low_back(v):
    return v

def low_keep(v):
    return (low(v), None)

def low_pass(kept, grad):
    return (grad,)

def back_keep(v):
    return (v, None)

def back_low(kept, grad):
    return (low(grad),)
low.defvjp(low_keep, low_pass)
low_back.defvjp(back_keep, back_low)

def rms_scale(matrix):
    return lax.rsqrt(lax.optimization_barrier(jnp.mean(matrix * matrix, axis=-1, keepdims=True)) + EPS)

def angles(position, head_size):
    half_size = head_size // 2
    frequency = THETA ** (-(jnp.arange(half_size, dtype=jnp.float32) * 2.0 / head_size))
    phase_angle = position.astype(jnp.float32)[:, None] * frequency[None, :]
    return (jnp.cos(phase_angle)[:, None, :], jnp.sin(phase_angle)[:, None, :])

def rotate(rotated_in, cosine_table, sine_table):
    half_size = rotated_in.shape[-1] // 2
    first_half = rotated_in[..., :half_size]
    second_half = rotated_in[..., half_size:]
    return jnp.concatenate([first_half * cosine_table - second_half * sine_table, second_half * cosine_table + first_half * sine_table], axis=-1)

def slot_layout(block_routes, experts, capacity):
    flat_routes = block_routes.reshape(-1)
    onehot = (flat_routes[:, None] == jnp.arange(experts, dtype=jnp.int32)[None, :]).astype(jnp.int32)
    before = jnp.cumsum(onehot, axis=0) - onehot
    rank_within = lax.optimization_barrier(jnp.sum(before * onehot, axis=1))
    slot_index = (flat_routes * capacity + rank_within).astype(jnp.int32)
    slot_table = jnp.zeros((experts * capacity,), jnp.int32).at[slot_index].set(jnp.arange(flat_routes.shape[0], dtype=jnp.int32) + 1)
    return (slot_index, slot_table)

def attend(queries, keys_in, values_in, segment_row):
    position = jnp.arange(SEQ)
    distance = position[:, None] - position[None, :]
    allowed = (segment_row[:, None] == segment_row[None, :]) & (distance >= 0) & (distance < WINDOW)
    scores = jnp.einsum('qhd,khd->hqk', queries, keys_in, precision=HIGH)
    scores = jnp.where(allowed[None], low_back(scores) * HEAD ** (-0.5), -1e+30)
    largest = lax.optimization_barrier(jnp.max(scores, axis=-1, keepdims=True))
    weights = jnp.exp(scores - largest)
    weights = weights / lax.optimization_barrier(jnp.sum(weights, axis=-1, keepdims=True))
    return jnp.einsum('hqk,khd->qhd', low(weights), values_in, precision=HIGH)

def attend_pack(packed):
    return attend(packed[0], packed[1], packed[2], packed[3])

def reference(tokens_in, out_grad, w_qkv, w_attn_out, attn_gain, ffn_gain, qk_gain, w_router, w_gate, w_up, w_down, routes, segments):
    blocks = routes.reshape(N_EXPERT, TOK_DEV, TOP)
    block_tables = jax.vmap(lambda block_routes: slot_layout(block_routes, EXPERTS, CAP)[1])(blocks)
    offsets = (jnp.arange(N_EXPERT, dtype=jnp.int32) * (TOK_DEV * TOP))[:, None]
    global_tables = jnp.where(block_tables > 0, block_tables + offsets, 0).astype(jnp.int32)
    global_tables = global_tables.reshape(N_EXPERT, EXPERTS, CAP).transpose(1, 0, 2).reshape(EXPERTS, N_EXPERT * CAP)
    sequences = TOKENS // SEQ
    part_width = HID // N_TENSOR

    def layer(tokens_f, qkv_master, out_master, gain_one, gain_two, gain_qk, router_master, gate_master, up_master, down_master):
        hidden_one = low(tokens_f * rms_scale(tokens_f) * low(gain_one))
        projected = jnp.einsum('td,jde->jte', hidden_one, low(qkv_master), precision=HIGH)
        query_raw = low_back(projected[0])
        key_raw = low_back(projected[1])
        value_all = low(low_back(projected[2]))
        qk_gains = low(gain_qk).reshape(2, D)
        query_norm = query_raw * rms_scale(query_raw) * qk_gains[0]
        key_norm = key_raw * rms_scale(key_raw) * qk_gains[1]
        cosine_table, sine_table = angles(jnp.arange(TOKENS, dtype=jnp.int32) % SEQ, HEAD)
        query_rot = low(rotate(query_norm.reshape(TOKENS, HEADS, HEAD), cosine_table, sine_table))
        key_rot = low(rotate(key_norm.reshape(TOKENS, HEADS, HEAD), cosine_table, sine_table))
        attended_all = lax.map(jax.checkpoint(attend_pack), (query_rot.reshape(sequences, SEQ, HEADS, HEAD), key_rot.reshape(sequences, SEQ, HEADS, HEAD), value_all.reshape(sequences, SEQ, HEADS, HEAD), segments.reshape(sequences, SEQ)))
        attended = low(low_back(attended_all.reshape(TOKENS, D)))
        residual = tokens_f + low_back(jnp.dot(attended, low(out_master), precision=HIGH))
        hidden_two = low(residual * rms_scale(residual) * low(gain_two))
        logits = low_back(jnp.dot(hidden_two, low(router_master), precision=HIGH))
        shifted = jnp.exp(logits - lax.optimization_barrier(jnp.max(logits, axis=-1, keepdims=True)))
        router_probs = shifted / lax.optimization_barrier(jnp.sum(shifted, axis=-1, keepdims=True))
        chosen = routes[:, :, None] == jnp.arange(EXPERTS, dtype=jnp.int32)[None, None, :]
        gate_probs = lax.optimization_barrier(jnp.sum(jnp.where(chosen, router_probs[:, None, :], 0.0), axis=-1)).reshape(-1)

        def expert_step(accumulated, expert_item):
            table_row, gate_mat, up_mat, down_mat = expert_item
            present = table_row > 0
            assigned = jnp.maximum(table_row - 1, 0)
            token_ids = assigned // TOP
            inputs = jnp.where(present[:, None], hidden_two[token_ids], 0.0)
            gate_low = low(gate_mat)
            up_low = low(up_mat)
            down_low = low(down_mat)
            summed = jnp.zeros_like(inputs)
            for portion in range(N_TENSOR):
                first_col = portion * part_width
                last_col = first_col + part_width
                part_in = low_back(inputs)
                gate_act = low_back(jnp.dot(part_in, gate_low[:, first_col:last_col], precision=HIGH))
                up_act = low_back(jnp.dot(part_in, up_low[:, first_col:last_col], precision=HIGH))
                activated = low(gate_act * jax.nn.sigmoid(gate_act) * up_act)
                summed = summed + low(low_back(jnp.dot(activated, down_low[first_col:last_col, :], precision=HIGH)))
            weighted = summed * jnp.where(present, gate_probs[assigned], 0.0)[:, None]
            return (accumulated.at[token_ids].add(weighted), None)
        expert_out, unused = lax.scan(jax.checkpoint(expert_step), jnp.zeros((TOKENS, D), jnp.float32), (global_tables, gate_master, up_master, down_master))
        return residual + expert_out
    float_args = (tokens_in.astype(jnp.float32), w_qkv, w_attn_out, attn_gain, ffn_gain, qk_gain, w_router, w_gate, w_up, w_down)
    result, pullback = jax.vjp(layer, *float_args)
    grads = pullback(out_grad.astype(jnp.float32))
    return (result.astype(jnp.bfloat16), grads[0].astype(jnp.bfloat16), grads[1], grads[2], grads[3], grads[4], grads[5], grads[6], grads[7], grads[8], grads[9])
```

```python
import jax
import jax.numpy as jnp
from jax import lax
from jax.experimental import pallas as pl
from jax.experimental.pallas import tpu as pltpu
from jax.sharding import PartitionSpec as P

HEAD = 128
WINDOW = 1024
SEQ = 2048


EPS = 1e-05
THETA = 10000.0


def from_behind(value, axis, steps):
    count = lax.axis_size(axis)
    initial, last = (max(0, -steps), min(count, count - steps))
    return lax.ppermute(value, axis, [(source, source + steps) for source in range(initial, last)])


def angles(position, head_size):
    half_size = head_size // 2
    frequency = THETA ** (-(jnp.arange(half_size, dtype=jnp.float32) * 2.0 / head_size))
    phase_angle = position.astype(jnp.float32)[:, None] * frequency[None, :]
    return (jnp.cos(phase_angle)[:, None, :], jnp.sin(phase_angle)[:, None, :])


def rotate(rotated_in, cosine_table, sine_table):
    half_size = rotated_in.shape[-1] // 2
    first_half = rotated_in[..., :half_size]
    second_half = rotated_in[..., half_size:]
    return jnp.concatenate(
        [
            first_half * cosine_table - second_half * sine_table,
            second_half * cosine_table + first_half * sine_table,
        ],
        axis=-1,
    )


def slot_layout(block_routes, experts, capacity):
    flat_routes = block_routes.reshape(-1)
    onehot = (flat_routes[:, None] == jnp.arange(experts, dtype=jnp.int32)[None, :]).astype(
        jnp.int32
    )
    before = jnp.cumsum(onehot, axis=0) - onehot
    rank_within = jnp.sum(before * onehot, axis=1)
    slot_index = flat_routes * capacity + rank_within
    slot_table = (
        jnp.zeros((experts * capacity,), jnp.int32)
        .at[slot_index]
        .set(jnp.arange(flat_routes.shape[0], dtype=jnp.int32) + 1)
    )
    return (slot_index, slot_table)


def shards(
    tokens_in,
    out_grad,
    w_qkv,
    w_attn_out,
    attn_gain,
    ffn_gain,
    qk_gain,
    w_router,
    w_gate,
    w_up,
    w_down,
    routes,
    segments,
):
    row_count, model_width = tokens_in.shape
    experts = w_router.shape[1]
    per_token = routes.shape[1]
    local_experts = w_gate.shape[0]
    heads_here = qk_gain.shape[1]
    local_width = heads_here * HEAD
    groups = lax.axis_size("expert")
    device = lax.axis_index("expert")
    capacity = row_count * per_token * 3 // (2 * experts)
    hop_count = WINDOW // row_count
    buffer_shape = (groups, local_experts, capacity, model_width)
    score_scale = HEAD ** (-0.5)

    def fetch_weights():
        return (
            lax.all_gather(w_qkv.astype(jnp.bfloat16), "expert", axis=1, tiled=True),
            lax.all_gather(w_attn_out.astype(jnp.bfloat16), "expert", axis=1, tiled=True),
            lax.all_gather(w_router.astype(jnp.bfloat16), "expert", axis=0, tiled=True),
            lax.all_gather(attn_gain.astype(jnp.bfloat16), "expert", axis=0, tiled=True),
            lax.all_gather(ffn_gain.astype(jnp.bfloat16), "expert", axis=0, tiled=True),
            lax.all_gather(qk_gain.astype(jnp.bfloat16), "expert", axis=2, tiled=True),
        )

    def prepare(pieces):
        return (
            pieces[0],
            pieces[1],
            pieces[2],
            pieces[3].astype(jnp.float32),
            pieces[4].astype(jnp.float32),
            pieces[5].astype(jnp.float32).reshape(2, local_width),
        )

    qkv_low, out_low, router_low, gain_one_f, gain_two_f, qk_gains = prepare(fetch_weights())
    tokens_f = tokens_in.astype(jnp.float32)
    scale_one = lax.rsqrt(jnp.mean(tokens_f * tokens_f, axis=-1, keepdims=True) + EPS)
    hidden_one = (tokens_f * scale_one * gain_one_f).astype(jnp.bfloat16)
    projected = jnp.einsum("td,jde->jte", hidden_one, qkv_low, preferred_element_type=jnp.float32)
    query_raw = projected[0]
    key_raw = projected[1]
    query_sq, key_sq = lax.psum(
        (jnp.sum(query_raw * query_raw, axis=-1), jnp.sum(key_raw * key_raw, axis=-1)), "tensor"
    )
    query_scale = lax.rsqrt(query_sq / model_width + EPS)[:, None]
    key_scale = lax.rsqrt(key_sq / model_width + EPS)[:, None]
    normed_query = query_raw * query_scale
    normed_key = key_raw * key_scale
    global_rows = device * row_count + jnp.arange(row_count, dtype=jnp.int32)
    cosine_table, sine_table = angles(global_rows % SEQ, HEAD)
    query_low = rotate(
        (normed_query * qk_gains[0]).reshape(row_count, heads_here, HEAD), cosine_table, sine_table
    ).astype(jnp.bfloat16)
    key_low = rotate(
        (normed_key * qk_gains[1]).reshape(row_count, heads_here, HEAD), cosine_table, sine_table
    ).astype(jnp.bfloat16)
    value_low = projected[2].astype(jnp.bfloat16).reshape(row_count, heads_here, HEAD)
    own_pair = jnp.stack([key_low, value_low])
    earlier = []
    for steps_back in range(hop_count, 0, -1):
        earlier.append(from_behind(own_pair, "expert", steps_back))
    context = jnp.concatenate(earlier + [own_pair], axis=1)
    key_rows = (device - hop_count) * row_count + jnp.arange(
        (hop_count + 1) * row_count, dtype=jnp.int32
    )
    segment_keys = segments[jnp.maximum(key_rows, 0)]
    segment_query = segments[global_rows]
    distance = global_rows[:, None] - key_rows[None, :]
    allowed = (
        (key_rows[None, :] >= 0)
        & (segment_query[:, None] == segment_keys[None, :])
        & (distance >= 0)
        & (distance < WINDOW)
    )

    def score_block():
        raw_scores = (
            jnp.einsum("qhd,khd->hqk", query_low, context[0], preferred_element_type=jnp.float32)
            * score_scale
        )
        return jnp.where(allowed[None], raw_scores, -1e30)

    scores = score_block()
    largest = jnp.max(scores, axis=-1, keepdims=True)
    exp_scores = jnp.exp(scores - largest)
    exp_total = jnp.sum(exp_scores, axis=-1, keepdims=True)
    log_total = largest + jnp.log(exp_total)
    attn_probs = (exp_scores / exp_total).astype(jnp.bfloat16)
    attended = (
        jnp.einsum("hqk,khd->qhd", attn_probs, context[1], preferred_element_type=jnp.float32)
        .reshape(row_count, local_width)
        .astype(jnp.bfloat16)
    )
    attention_out = lax.psum(
        jnp.dot(attended, out_low, preferred_element_type=jnp.float32).astype(jnp.bfloat16),
        "tensor",
    ).astype(jnp.float32)
    residual = tokens_f + attention_out
    scale_two = lax.rsqrt(jnp.mean(residual * residual, axis=-1, keepdims=True) + EPS)
    normed_two = residual * scale_two
    hidden_two = (normed_two * gain_two_f).astype(jnp.bfloat16)
    logits = jnp.dot(hidden_two, router_low, preferred_element_type=jnp.float32)
    logit_exp = jnp.exp(logits - jnp.max(logits, axis=-1, keepdims=True))
    router_probs = logit_exp / jnp.sum(logit_exp, axis=-1, keepdims=True)
    chosen = routes[:, :, None] == jnp.arange(experts, dtype=jnp.int32)[None, None, :]
    gate_probs = jnp.sum(jnp.where(chosen, router_probs[:, None, :], 0.0), axis=-1)
    slot_index, slot_table = slot_layout(routes, experts, capacity)
    present = (slot_table > 0)[:, None]
    assigned = jnp.maximum(slot_table - 1, 0)
    row_of_slot = assigned // per_token
    gate_low = w_gate.astype(jnp.bfloat16)
    up_low = w_up.astype(jnp.bfloat16)
    down_low = w_down.astype(jnp.bfloat16)

    def send_rows():
        buffer_rows = jnp.where(
            present, hidden_two[row_of_slot], jnp.zeros((), jnp.bfloat16)
        ).reshape(buffer_shape)
        return lax.all_to_all(buffer_rows, "expert", split_axis=0, concat_axis=0, tiled=True)

    def expert_front(arrived):
        gate_pre = jnp.einsum(
            "secd,edh->sech", arrived, gate_low, preferred_element_type=jnp.float32
        )
        up_pre = jnp.einsum("secd,edh->sech", arrived, up_low, preferred_element_type=jnp.float32)
        return (gate_pre, up_pre)

    received = send_rows()
    gate_pre, up_pre = expert_front(received)
    activated = (gate_pre * jax.nn.sigmoid(gate_pre) * up_pre).astype(jnp.bfloat16)
    partial_value = jnp.einsum(
        "sech,ehd->secd", activated, down_low, preferred_element_type=jnp.float32
    ).astype(jnp.bfloat16)
    returned = lax.all_to_all(
        partial_value, "expert", split_axis=0, concat_axis=0, tiled=True
    ).reshape(experts * capacity, model_width)
    expert_rows = returned[slot_index].reshape(row_count, per_token, model_width)
    expert_part = jnp.einsum(
        "tk,tkd->td", gate_probs, expert_rows, preferred_element_type=jnp.float32
    )
    block_out = residual + lax.psum(expert_part.astype(jnp.bfloat16), "tensor").astype(jnp.float32)
    qkv_low, out_low, router_low, gain_one_f, gain_two_f, qk_gains = prepare(fetch_weights())
    grad_out = out_grad.astype(jnp.float32)
    grad_gate_part = jnp.einsum(
        "td,tkd->tk", grad_out, expert_rows, preferred_element_type=jnp.float32
    )
    slot_grads = (
        (gate_probs[:, :, None] * grad_out[:, None, :])
        .astype(jnp.bfloat16)
        .reshape(row_count * per_token, model_width)
    )
    grad_buffer = jnp.where(present, slot_grads[assigned], jnp.zeros((), jnp.bfloat16)).reshape(
        buffer_shape
    )
    grad_received = lax.all_to_all(grad_buffer, "expert", split_axis=0, concat_axis=0, tiled=True)
    received = send_rows()
    gate_pre, up_pre = expert_front(received)
    sigmoid_gate = jax.nn.sigmoid(gate_pre)
    swish_gate = gate_pre * sigmoid_gate
    activated = (swish_gate * up_pre).astype(jnp.bfloat16)
    grad_act = jnp.einsum(
        "secd,ehd->sech", grad_received, down_low, preferred_element_type=jnp.float32
    )
    grad_down = jnp.einsum(
        "sech,secd->ehd", activated, grad_received, preferred_element_type=jnp.float32
    )
    grad_gate_pre = (
        grad_act * up_pre * sigmoid_gate * (1.0 + gate_pre * (1.0 - sigmoid_gate))
    ).astype(jnp.bfloat16)
    grad_up_pre = (grad_act * swish_gate).astype(jnp.bfloat16)
    grad_gate_w = jnp.einsum(
        "secd,sech->edh", received, grad_gate_pre, preferred_element_type=jnp.float32
    )
    grad_up_w = jnp.einsum(
        "secd,sech->edh", received, grad_up_pre, preferred_element_type=jnp.float32
    )
    grad_rows = (
        jnp.einsum("sech,edh->secd", grad_gate_pre, gate_low, preferred_element_type=jnp.float32)
        + jnp.einsum("sech,edh->secd", grad_up_pre, up_low, preferred_element_type=jnp.float32)
    ).astype(jnp.bfloat16)
    grad_back = lax.all_to_all(
        grad_rows, "expert", split_axis=0, concat_axis=0, tiled=True
    ).reshape(experts * capacity, model_width)
    grad_hidden_part = jnp.sum(
        grad_back[slot_index].reshape(row_count, per_token, model_width), axis=1, dtype=jnp.float32
    )
    grad_hidden_sum, grad_gates = (
        lax.psum(grad_hidden_part.astype(jnp.bfloat16), "tensor").astype(jnp.float32),
        lax.psum(grad_gate_part.astype(jnp.bfloat16), "tensor").astype(jnp.float32),
    )
    grad_probs = jnp.sum(jnp.where(chosen, grad_gates[:, :, None], 0.0), axis=1)
    grad_logits = (
        router_probs * (grad_probs - jnp.sum(router_probs * grad_probs, axis=-1, keepdims=True))
    ).astype(jnp.bfloat16)
    grad_hidden_two = grad_hidden_sum + jnp.dot(
        grad_logits, router_low.T, preferred_element_type=jnp.float32
    )
    grad_router = jnp.dot(hidden_two.T, grad_logits, preferred_element_type=jnp.float32)
    grad_gain_two = jnp.sum(grad_hidden_two * normed_two, axis=0)
    scaled_two = grad_hidden_two * gain_two_f
    grad_residual = (
        grad_out
        + scale_two * scaled_two
        - residual
        * (scale_two * scale_two * scale_two)
        * jnp.mean(scaled_two * residual, axis=-1, keepdims=True)
    )
    grad_attn = grad_residual.astype(jnp.bfloat16)
    grad_out_w = jnp.dot(attended.T, grad_attn, preferred_element_type=jnp.float32)
    grad_attended = (
        jnp.dot(grad_attn, out_low.T, preferred_element_type=jnp.float32)
        .astype(jnp.bfloat16)
        .reshape(row_count, heads_here, HEAD)
    )
    attn_weights = jnp.where(allowed[None], jnp.exp(score_block() - log_total), 0.0)
    grad_weights = jnp.einsum(
        "qhd,khd->hqk", grad_attended, context[1], preferred_element_type=jnp.float32
    )
    inner_sum = jnp.sum(attn_weights * grad_weights, axis=-1, keepdims=True)
    grad_scores = (attn_weights * (grad_weights - inner_sum) * score_scale).astype(jnp.bfloat16)
    grad_query = jnp.einsum(
        "hqk,khd->qhd", grad_scores, context[0], preferred_element_type=jnp.float32
    )
    grad_keys = jnp.einsum(
        "hqk,qhd->khd", grad_scores, query_low, preferred_element_type=jnp.float32
    )
    grad_values = jnp.einsum(
        "hqk,qhd->khd",
        attn_weights.astype(jnp.bfloat16),
        grad_attended,
        preferred_element_type=jnp.float32,
    )
    grad_pair = jnp.stack([grad_keys, grad_values]).reshape(
        2, hop_count + 1, row_count, heads_here, HEAD
    )
    own_grad = grad_pair[:, hop_count]
    for steps_back in range(1, hop_count + 1):
        own_grad = own_grad + from_behind(
            grad_pair[:, hop_count - steps_back].astype(jnp.bfloat16), "expert", -steps_back
        ).astype(jnp.float32)
    grad_query_norm = rotate(grad_query, cosine_table, -sine_table).reshape(row_count, local_width)
    grad_key_norm = rotate(own_grad[0], cosine_table, -sine_table).reshape(row_count, local_width)
    grad_gain_query = jnp.sum(grad_query_norm * normed_query, axis=0)
    grad_gain_key = jnp.sum(grad_key_norm * normed_key, axis=0)
    scaled_query = grad_query_norm * qk_gains[0]
    scaled_key = grad_key_norm * qk_gains[1]
    query_inner, key_inner = lax.psum(
        (jnp.sum(scaled_query * query_raw, axis=-1), jnp.sum(scaled_key * key_raw, axis=-1)),
        "tensor",
    )
    grad_query_raw = (
        query_scale * scaled_query
        - query_raw * (query_scale * query_scale * query_scale) * query_inner[:, None] / model_width
    ).astype(jnp.bfloat16)
    grad_key_raw = (
        key_scale * scaled_key
        - key_raw * (key_scale * key_scale * key_scale) * key_inner[:, None] / model_width
    ).astype(jnp.bfloat16)
    grad_value_raw = own_grad[1].reshape(row_count, local_width).astype(jnp.bfloat16)
    grad_proj = jnp.stack([grad_query_raw, grad_key_raw, grad_value_raw])
    grad_qkv = jnp.einsum("td,jte->jde", hidden_one, grad_proj, preferred_element_type=jnp.float32)
    grad_hidden_one = lax.psum(
        jnp.einsum("jte,jde->td", grad_proj, qkv_low, preferred_element_type=jnp.float32).astype(
            jnp.bfloat16
        ),
        "tensor",
    ).astype(jnp.float32)
    grad_gain_one = jnp.sum(grad_hidden_one * tokens_f * scale_one, axis=0)
    scaled_one = grad_hidden_one * gain_one_f
    grad_tokens = (
        grad_residual
        + scale_one * scaled_one
        - tokens_f
        * (scale_one * scale_one * scale_one)
        * jnp.mean(scaled_one * tokens_f, axis=-1, keepdims=True)
    )
    grad_qk = jnp.stack([grad_gain_query, grad_gain_key]).reshape(2, heads_here, HEAD)
    reduced = (
        lax.psum_scatter(
            grad_qkv.astype(jnp.bfloat16), "expert", scatter_dimension=1, tiled=True
        ).astype(jnp.float32),
        lax.psum_scatter(
            grad_out_w.astype(jnp.bfloat16), "expert", scatter_dimension=1, tiled=True
        ).astype(jnp.float32),
        lax.psum_scatter(
            grad_router.astype(jnp.bfloat16), "expert", scatter_dimension=0, tiled=True
        ).astype(jnp.float32),
        lax.psum_scatter(
            grad_gain_one.astype(jnp.bfloat16), "expert", scatter_dimension=0, tiled=True
        ).astype(jnp.float32),
        lax.psum_scatter(
            grad_gain_two.astype(jnp.bfloat16), "expert", scatter_dimension=0, tiled=True
        ).astype(jnp.float32),
        lax.psum_scatter(
            grad_qk.astype(jnp.bfloat16), "expert", scatter_dimension=2, tiled=True
        ).astype(jnp.float32),
    )
    return (
        block_out.astype(jnp.bfloat16),
        grad_tokens.astype(jnp.bfloat16),
        reduced[0],
        reduced[1],
        reduced[3],
        reduced[4],
        reduced[5],
        reduced[2],
        grad_gate_w,
        grad_up_w,
        grad_down,
    )


MESH_ID = pl.DeviceIdType.MESH
HBM = pl.BlockSpec(memory_space=pl.ANY)
VMEM = pl.BlockSpec(memory_space=pltpu.VMEM)
NZ, NY, NX, NC = 4, 2, 2, 2
GROUPS = NZ * NY


def place():
    e = lax.axis_index("expert")
    t = lax.axis_index("tensor")
    return lax.div(e, NY), lax.rem(e, NY), lax.div(t, NC), lax.rem(t, NC)


def device(z, y, x, c):
    return (z * NY + y, x * NC + c)


def run_if(condition, body):
    if condition is None:
        body()
    else:
        pl.when(condition)(body)


def greet(partners):
    barrier = pltpu.get_barrier_semaphore()
    for target, condition in partners:
        run_if(
            condition,
            lambda target=target: pl.semaphore_signal(
                barrier, inc=1, device_id=target, device_id_type=MESH_ID
            ),
        )
    count = sum(1 for _, condition in partners if condition is None)
    for _, condition in partners:
        if condition is not None:
            count = count + condition.astype(jnp.int32)
    pl.semaphore_wait(barrier, count)


def remote(source, target_ref, send_sem, recv_sem, target):
    return pltpu.make_async_remote_copy(
        src_ref=source,
        dst_ref=target_ref,
        send_sem=send_sem,
        recv_sem=recv_sem,
        device_id=target,
        device_id_type=MESH_ID,
    )


def block_rows(block, rows):
    return pl.ds(pl.multiple_of(block * rows, rows), rows)


class LineGather:
    def __init__(self, streams, sources, views, send_sem, recv_sem):
        self.z, self.y, self.x, self.c = place()
        self.streams, self.sources, self.views = streams, sources, views
        self.send_sem, self.recv_sem = send_sem, recv_sem
        self.has_up, self.has_down = self.z < NZ - 1, self.z > 0
        self.pending = []

    def partners(self):
        z, y, x, c = self.z, self.y, self.x, self.c
        return [
            (device(z + 1, y, x, c), z < NZ - 1),
            (device(z - 1, y, x, c), z > 0),
            (device(z, 1 - y, x, c), None),
        ]

    def exists(self, rel):
        rel = rel % 7
        if rel == 0:
            return None
        return self.z >= rel if rel < 4 else self.z + (rel - 3) < NZ

    def block(self, rel):
        y = self.y if rel < 7 else 1 - self.y
        rel = rel % 7
        z = self.z if rel == 0 else (self.z - rel if rel < 4 else self.z + (rel - 3))
        return z * NY + y

    def send(self, stream, rel, way):
        z, y, x, c = self.z, self.y, self.x, self.c
        block = self.block(rel)
        there = self.views[stream](block)
        source = self.sources[stream] if rel == 0 else there
        if way == 0:
            target, landing = device(z + 1, y, x, c), (1 if rel == 0 else rel + 1)
        elif way == 1:
            target, landing = device(z - 1, y, x, c), (4 if rel == 0 else rel + 1)
        else:
            target, landing = device(z, 1 - y, x, c), 7 + rel
        return remote(
            source,
            there,
            self.send_sem.at[stream, rel, way],
            self.recv_sem.at[stream, landing],
            target,
        )

    def start(self, stream, rel):
        if rel < 4:
            run = self.has_up
            run_if(run, lambda: self.send(stream, rel, 0).start())
            self.pending.append((stream, rel, 0, run))
        if rel == 0 or rel >= 4:
            run = self.has_down
            run_if(run, lambda: self.send(stream, rel, 1).start())
            self.pending.append((stream, rel, 1, run))
        self.send(stream, rel, 2).start()
        self.pending.append((stream, rel, 2, None))

    def arrive(self, stream, rel):
        there = self.views[stream](self.block(rel))
        remote(
            there,
            there,
            self.send_sem.at[stream, 0, 0],
            self.recv_sem.at[stream, rel],
            device(self.z, 1 - self.y, self.x, self.c),
        ).wait_recv()

    def order(self):
        return [7, 1, 4, 8, 11, 2, 5, 9, 12, 3, 6, 10, 13]

    def run(self, hook=None):
        for stream in self.streams:
            self.start(stream, 0)
        for rel in self.order():
            def step(rel=rel):
                marks = len(self.pending)
                for stream in self.streams:
                    self.arrive(stream, rel)
                    if rel < 7:
                        self.start(stream, rel)
                    if hook is not None:
                        hook(stream, rel)
                if rel < 7:
                    late = self.pending[marks:]
                    del self.pending[marks:]
                    self.finish_later(late, rel)
            run_if(self.exists(rel), step)

    def finish_later(self, late, rel):
        self.late = getattr(self, "late", []) + [(rel, late)]

    def finish(self):
        for stream, rel, way, run in self.pending:
            run_if(run, lambda s=stream, r=rel, w=way: self.send(s, r, w).wait_send())
        for rel, late in getattr(self, "late", []):
            def body(late=late):
                for stream, rel, way, run in late:
                    run_if(run, lambda s=stream, r=rel, w=way: self.send(s, r, w).wait_send())
            run_if(self.exists(rel), body)


def comm_params(collective_id, megabytes=56):
    return pltpu.CompilerParams(
        collective_id=collective_id,
        has_side_effects=True,
        vmem_limit_bytes=megabytes * 1024 * 1024,
    )


def weight_gather(qkv_low, out_low, smalls, collective_id):
    parts, rows, width = qkv_low.shape
    depth, columns = out_low.shape

    def kernel(qkv, out, small, qkv_all, out_all, small_all, send_sem, recv_sem, local_sem):
        views = [
            lambda b: qkv_all.at[:, block_rows(b, rows), :],
            lambda b: out_all.at[:, block_rows(b, columns)],
            lambda b: small_all.at[b],
        ]
        line = LineGather([2, 0, 1], [qkv, out, small], views, send_sem, recv_sem)
        greet(line.partners())
        own = line.block(0)
        keep = [
            pltpu.make_async_copy(source, view(own), local_sem.at[i])
            for i, (source, view) in enumerate(zip([qkv, out, small], views))
        ]
        for copy in keep:
            copy.start()
        line.run()
        line.finish()
        for copy in keep:
            copy.wait()

    return pl.pallas_call(
        kernel,
        out_shape=(
            jax.ShapeDtypeStruct((parts, rows * GROUPS, width), jnp.bfloat16),
            jax.ShapeDtypeStruct((depth, columns * GROUPS), jnp.bfloat16),
            jax.ShapeDtypeStruct((GROUPS,) + smalls.shape, jnp.float32),
        ),
        in_specs=[HBM] * 3,
        out_specs=(HBM, HBM, HBM),
        scratch_shapes=[
            pltpu.SemaphoreType.DMA((3, 7, 3)),
            pltpu.SemaphoreType.DMA((3, 14)),
            pltpu.SemaphoreType.DMA((3,)),
        ],
        compiler_params=comm_params(collective_id),
        name="weight_gather",
    )(qkv_low, out_low, smalls)


def token_gather(block, collective_id):
    rows, width = block.shape
    a_cols, c_cols = width * 3 // 16, width // 8

    def kernel(own_ref, all_ref, send_sem, recv_sem, x_send, x_recv, core_send, core_recv, local_sem):
        z, y, x, c = place()

        def a_at(xx, cc):
            return pl.ds(pl.multiple_of(xx * (2 * a_cols) + cc * a_cols, 128), a_cols)

        def c_at(cc):
            return pl.ds(pl.multiple_of(4 * a_cols + cc * c_cols, 128), c_cols)

        def view(b, columns):
            return all_ref.at[block_rows(b, rows), columns]

        sources = [own_ref.at[:, a_at(x, c)], own_ref.at[:, c_at(c)]]
        views = [lambda b: view(b, a_at(x, c)), lambda b: view(b, c_at(c))]
        line = LineGather([0, 1], sources, views, send_sem, recv_sem)
        across, twin = device(z, y, 1 - x, c), device(z, y, x, 1 - c)
        greet(line.partners() + [(across, None), (twin, None)])
        keep = pltpu.make_async_copy(own_ref, all_ref.at[block_rows(line.block(0), rows), :], local_sem)
        keep.start()

        def to_twin(rel, stream, landing=False):
            b = line.block(rel)
            columns = [a_at(x, c), c_at(c), a_at(1 - x, c)][stream]
            other = [a_at(x, 1 - c), c_at(1 - c), a_at(1 - x, 1 - c)][stream]
            piece = view(b, other if landing else columns)
            return remote(piece, piece, core_send.at[rel, stream], core_recv.at[rel, stream], twin)

        def to_across(rel, landing=False):
            b = line.block(rel)
            piece = view(b, a_at(1 - x if landing else x, c))
            return remote(piece, piece, x_send.at[rel], x_recv.at[rel], across)

        def hook(stream, rel):
            if stream == 0:
                to_across(rel).start()
            to_twin(rel, stream).start()

        line.run(hook)
        for rel in line.order():
            def relay(rel=rel):
                to_across(rel, True).wait_recv()
                to_twin(rel, 2).start()
            run_if(line.exists(rel), relay)
        for rel in line.order():
            def end(rel=rel):
                to_across(rel).wait_send()
                for stream in range(3):
                    to_twin(rel, stream, True).wait_recv()
                    to_twin(rel, stream).wait_send()
            run_if(line.exists(rel), end)
        line.finish()
        keep.wait()

    return pl.pallas_call(
        kernel,
        out_shape=jax.ShapeDtypeStruct((rows * GROUPS, width), block.dtype),
        in_specs=[HBM],
        out_specs=HBM,
        scratch_shapes=[
            pltpu.SemaphoreType.DMA((2, 7, 3)),
            pltpu.SemaphoreType.DMA((2, 14)),
            pltpu.SemaphoreType.DMA((14,)),
            pltpu.SemaphoreType.DMA((14,)),
            pltpu.SemaphoreType.DMA((14, 3)),
            pltpu.SemaphoreType.DMA((14, 3)),
            pltpu.SemaphoreType.DMA,
        ],
        compiler_params=comm_params(collective_id),
        name="token_gather",
    )(block)


def add_into(rows, step, store):
    def body(i, carry):
        store(pl.ds(pl.multiple_of(i * step, step), step))
        return carry

    lax.fori_loop(0, rows // step, body, 0)


def tensor_sum(part, collective_id):
    rows, width = part.shape
    half, quarter = width // 2, width // 4

    def kernel(part_ref, out_ref, core_buf, x_buf, send_sem, recv_sem):
        z, y, x, c = place()
        across, twin = device(z, y, 1 - x, c), device(z, y, x, 1 - c)
        greet([(across, None), (twin, None)])

        def half_of(cc):
            return pl.ds(pl.multiple_of(cc * half, half), half)

        def quarter_of(xx, cc):
            return pl.ds(pl.multiple_of(cc * half + xx * quarter, quarter), quarter)

        first = remote(part_ref.at[:, half_of(1 - c)], core_buf, send_sem.at[0], recv_sem.at[0], twin)
        first.start()
        first.wait_recv()
        base = pl.multiple_of(c * half, half)

        def add_core(r):
            core_buf[r, :] = (
                core_buf[r, :].astype(jnp.float32) + part_ref[r, pl.ds(base, half)].astype(jnp.float32)
            ).astype(jnp.bfloat16)

        add_into(rows, 32, add_core)
        second = remote(
            core_buf.at[:, pl.ds(pl.multiple_of((1 - x) * quarter, quarter), quarter)],
            x_buf, send_sem.at[1], recv_sem.at[1], across,
        )
        second.start()
        second.wait_recv()
        mine = pl.multiple_of(x * quarter, quarter)
        out_at = pl.multiple_of(c * half + x * quarter, quarter)

        def add_x(r):
            out_ref[r, pl.ds(out_at, quarter)] = (
                core_buf[r, pl.ds(mine, quarter)].astype(jnp.float32) + x_buf[r, :].astype(jnp.float32)
            ).astype(jnp.bfloat16)

        add_into(rows, 32, add_x)
        own = out_ref.at[:, quarter_of(x, c)]
        third = remote(own, own, send_sem.at[2], recv_sem.at[2], across)
        third.start()
        fourth = remote(own, own, send_sem.at[3], recv_sem.at[3], twin)
        fourth.start()
        from_x = out_ref.at[:, quarter_of(1 - x, c)]
        remote(from_x, from_x, send_sem.at[2], recv_sem.at[2], across).wait_recv()
        fifth = remote(from_x, from_x, send_sem.at[4], recv_sem.at[4], twin)
        fifth.start()
        for index, column in ((3, quarter_of(x, 1 - c)), (4, quarter_of(1 - x, 1 - c))):
            landing = out_ref.at[:, column]
            remote(landing, landing, send_sem.at[index], recv_sem.at[index], twin).wait_recv()
        for copy in (first, second, third, fourth, fifth):
            copy.wait_send()

    return pl.pallas_call(
        kernel,
        out_shape=jax.ShapeDtypeStruct((rows, width), jnp.bfloat16),
        in_specs=[VMEM],
        out_specs=VMEM,
        scratch_shapes=[
            pltpu.VMEM((rows, half), jnp.bfloat16),
            pltpu.VMEM((rows, quarter), jnp.bfloat16),
            pltpu.SemaphoreType.DMA((5,)),
            pltpu.SemaphoreType.DMA((5,)),
        ],
        compiler_params=comm_params(collective_id, 16),
        name="tensor_sum",
    )(part)


Z_ORDER = (3, 0, 2, 1)


def accumulate(into, addend, step=64):
    rows = into.shape[0]
    step = min(step, rows)

    def body(i, carry):
        r = pl.ds(pl.multiple_of(i * step, step), step)
        total = into[r, :].astype(jnp.float32) + addend[r, :].astype(jnp.float32)
        into[r, :] = total.astype(into.dtype)
        return carry

    lax.fori_loop(0, rows // step, body, 0)


class LineReduce:
    def __init__(self, streams, own, y_buf, lo_buf, hi_buf, send_sem, recv_sem):
        self.z, self.y, self.x, self.c = place()
        self.streams = streams
        self.own, self.y_buf, self.lo_buf, self.hi_buf = own, y_buf, lo_buf, hi_buf
        self.send_sem, self.recv_sem = send_sem, recv_sem

    def partners(self):
        z, y, x, c = self.z, self.y, self.x, self.c
        return [
            (device(z + 1, y, x, c), z < NZ - 1),
            (device(z - 1, y, x, c), z > 0),
            (device(z, 1 - y, x, c), None),
        ]

    def copy(self, s, zz, way):
        z, y, x, c = self.z, self.y, self.x, self.c
        if way == 0:
            source, landing, target = self.own(s, zz, 1 - y), self.y_buf, device(z, 1 - y, x, c)
        elif way == 1:
            source, landing, target = self.y_buf(s, zz), self.lo_buf, device(z + 1, y, x, c)
        else:
            source, landing, target = self.y_buf(s, zz), self.hi_buf, device(z - 1, y, x, c)
        return remote(
            source, landing(s, zz), self.send_sem.at[s, zz, way], self.recv_sem.at[s, zz, way], target
        )

    def to_y(self, s, zz):
        self.copy(s, zz, 0).start()

    def take(self, s, zz, way):
        self.copy(s, zz, way).wait_recv()
        accumulate(self.y_buf(s, zz), (self.lo_buf if way == 1 else self.hi_buf)(s, zz))

    def along_z(self, s, zz):
        z = self.z
        self.copy(s, zz, 0).wait_recv()
        accumulate(self.y_buf(s, zz), self.own(s, zz, self.y))

        def upward():
            run_if(z > 0, lambda: self.take(s, zz, 1))
            self.copy(s, zz, 1).start()

        def downward():
            run_if(z < NZ - 1, lambda: self.take(s, zz, 2))
            self.copy(s, zz, 2).start()

        run_if(z < zz, upward)
        run_if(z > zz, downward)

    def home(self, done):
        for zz in range(NZ):
            def land(zz=zz):
                for s in self.streams:
                    if zz > 0:
                        self.take(s, zz, 1)
                    if zz < NZ - 1:
                        self.take(s, zz, 2)
                    done(s, self.y_buf(s, zz))
            run_if(self.z == zz, land)

    def finish(self):
        for zz in range(NZ):
            for s in self.streams:
                self.copy(s, zz, 0).wait_send()
                run_if(self.z < zz, lambda s=s, zz=zz: self.copy(s, zz, 1).wait_send())
                run_if(self.z > zz, lambda s=s, zz=zz: self.copy(s, zz, 2).wait_send())


def weight_reduce(qkv, out, smalls, collective_id):
    parts, depth, width = qkv.shape
    rows = depth // GROUPS
    out_rows, columns = out.shape[0], out.shape[1] // GROUPS

    def kernel(qkv_ref, out_ref, small_ref, qkv_sum, out_sum, small_sum,
               qkv_buf, out_buf, small_buf, send_sem, recv_sem):
        def own(s, zz, yy):
            b = zz * NY + yy
            if s < parts:
                return qkv_ref.at[s, block_rows(b, rows), :]
            if s == parts:
                return out_ref.at[:, block_rows(b, columns)]
            return small_ref.at[b]

        def slot(kind):
            def view(s, zz):
                if s < parts:
                    return qkv_buf.at[kind, zz, s]
                if s == parts:
                    return out_buf.at[kind, zz]
                return small_buf.at[kind, zz]
            return view

        streams = list(range(parts + 2))
        line = LineReduce(streams, own, slot(0), slot(1), slot(2), send_sem, recv_sem)
        greet(line.partners())
        work = [(s, zz) for s in [parts + 1, parts] + list(range(parts)) for zz in Z_ORDER]
        for s, zz in work:
            line.to_y(s, zz)
        for s, zz in work:
            line.along_z(s, zz)

        def done(s, total):
            target = qkv_sum.at[s] if s < parts else (out_sum if s == parts else small_sum)
            step = min(64, target.shape[0])

            def body(i, carry):
                r = pl.ds(pl.multiple_of(i * step, step), step)
                target[r, :] = total[r, :].astype(jnp.float32)
                return carry

            lax.fori_loop(0, target.shape[0] // step, body, 0)

        line.home(done)
        line.finish()

    return pl.pallas_call(
        kernel,
        out_shape=(
            jax.ShapeDtypeStruct((parts, rows, width), jnp.float32),
            jax.ShapeDtypeStruct((out_rows, columns), jnp.float32),
            jax.ShapeDtypeStruct(smalls.shape[1:], jnp.float32),
        ),
        in_specs=[VMEM] * 3,
        out_specs=(VMEM,) * 3,
        scratch_shapes=[
            pltpu.VMEM((3, NZ, parts, rows, width), jnp.bfloat16),
            pltpu.VMEM((3, NZ, out_rows, columns), jnp.bfloat16),
            pltpu.VMEM((3, NZ) + smalls.shape[1:], jnp.float32),
            pltpu.SemaphoreType.DMA((parts + 2, NZ, 3)),
            pltpu.SemaphoreType.DMA((parts + 2, NZ, 3)),
        ],
        compiler_params=comm_params(collective_id),
        name="weight_reduce",
    )(qkv, out, smalls)


def token_reduce(part, collective_id, pairs=None):
    tokens, width = part.shape
    rows = tokens // GROUPS
    half, quarter = width // 2, width // 4

    def kernel(part_ref, out_ref, core_buf, x_buf, y_buf, lo_buf, hi_buf,
               core_send, core_recv, x_send, x_recv, send_sem, recv_sem):
        z, y, x, c = place()
        across, twin = device(z, y, 1 - x, c), device(z, y, x, 1 - c)

        line = LineReduce(
            [0], lambda s, zz, yy: x_buf.at[zz * NY + yy], lambda s, zz: y_buf.at[zz],
            lambda s, zz: lo_buf.at[zz], lambda s, zz: hi_buf.at[zz], send_sem, recv_sem,
        )
        greet(line.partners() + [(across, None), (twin, None)])
        order = [(zz, flip) for zz in Z_ORDER for flip in (1, 0)]

        def number(zz, flip):
            return zz * NY + (1 - y if flip else y)

        def to_twin(zz, flip):
            b = number(zz, flip)
            return remote(
                part_ref.at[block_rows(b, rows), pl.ds(pl.multiple_of((1 - c) * half, half), half)],
                core_buf.at[b], core_send.at[zz, flip], core_recv.at[zz, flip], twin,
            )

        def to_across(zz, flip):
            b = number(zz, flip)
            return remote(
                core_buf.at[b, :, pl.ds(pl.multiple_of((1 - x) * quarter, quarter), quarter)],
                x_buf.at[b], x_send.at[zz, flip], x_recv.at[zz, flip], across,
            )

        def add_core(zz, flip):
            b = number(zz, flip)

            def store(r):
                at = pl.ds(pl.multiple_of(b * rows + r.start, 16), r.size)
                core_buf[b, r, :] = (
                    core_buf[b, r, :].astype(jnp.float32)
                    + part_ref[at, pl.ds(pl.multiple_of(c * half, half), half)].astype(jnp.float32)
                ).astype(jnp.bfloat16)

            add_into(rows, 32, store)

        def add_across(zz, flip):
            b = number(zz, flip)

            def store(r):
                x_buf[b, r, :] = (
                    x_buf[b, r, :].astype(jnp.float32)
                    + core_buf[b, r, pl.ds(pl.multiple_of(x * quarter, quarter), quarter)].astype(jnp.float32)
                ).astype(jnp.bfloat16)

            add_into(rows, 64, store)

        def stage_twin(i):
            to_twin(*order[i]).wait_recv()
            add_core(*order[i])
            to_across(*order[i]).start()

        def stage_across(i):
            zz, flip = order[i]
            to_across(zz, flip).wait_recv()
            add_across(zz, flip)
            if flip:
                line.to_y(0, zz)

        def stage_y(zz):
            line.along_z(0, zz)

        for zz, flip in order:
            to_twin(zz, flip).start()
        count = len(order)
        for i in range(count + 4):
            if i < count:
                stage_twin(i)
            if 0 <= i - 1 < count:
                stage_across(i - 1)
            if i >= 3 and (i - 3) % 2 == 0 and (i - 3) // 2 < NZ:
                stage_y(Z_ORDER[(i - 3) // 2])

        def done(s, total):
            def store(r):
                out_ref[r, :] = total[r, :]

            add_into(rows, 64, store)

        line.home(done)
        for zz, flip in order:
            to_twin(zz, flip).wait_send()
            to_across(zz, flip).wait_send()
        line.finish()

    return pl.pallas_call(
        kernel,
        out_shape=jax.ShapeDtypeStruct((rows, quarter), jnp.bfloat16),
        in_specs=[VMEM],
        out_specs=VMEM,
        scratch_shapes=[
            pltpu.VMEM((GROUPS, rows, half), jnp.bfloat16),
            pltpu.VMEM((GROUPS, rows, quarter), jnp.bfloat16),
            pltpu.VMEM((NZ, rows, quarter), jnp.bfloat16),
            pltpu.VMEM((NZ, rows, quarter), jnp.bfloat16),
            pltpu.VMEM((NZ, rows, quarter), jnp.bfloat16),
            pltpu.SemaphoreType.DMA((NZ, 2)),
            pltpu.SemaphoreType.DMA((NZ, 2)),
            pltpu.SemaphoreType.DMA((NZ, 2)),
            pltpu.SemaphoreType.DMA((NZ, 2)),
            pltpu.SemaphoreType.DMA((1, NZ, 3)),
            pltpu.SemaphoreType.DMA((1, NZ, 3)),
        ],
        compiler_params=comm_params(collective_id),
        name="token_reduce",
    )(part)


def gate_exchange(part, collective_id):
    groups = part.shape[0]
    tensors = NX * NC

    def kernel(part_ref, out_ref, landing, total, send_t, recv_t, send_e, recv_e):
        e = lax.axis_index("expert")
        t = lax.axis_index("tensor")
        mates = [(e, lax.rem(t + k, tensors)) for k in range(1, tensors)]
        peers = [(lax.rem(e + k, groups), t) for k in range(1, groups)]
        greet([(target, None) for target in mates + peers])
        near = [
            remote(part_ref, landing.at[k], send_t.at[k], recv_t.at[k], mates[k])
            for k in range(tensors - 1)
        ]
        for copy in near:
            copy.start()
        for copy in near:
            copy.wait_recv()
        value = part_ref[...]
        for k in range(tensors - 1):
            value = value + landing[k]
        total[...] = value
        far = [
            remote(
                total.at[lax.rem(e + k, groups)], out_ref.at[e], send_e.at[k - 1], recv_e.at[k - 1],
                peers[k - 1],
            )
            for k in range(1, groups)
        ]
        for copy in far:
            copy.start()
        out_ref[e] = total[e]
        for k in range(1, groups):
            source = out_ref.at[lax.rem(e + groups - k, groups)]
            remote(source, source, send_e.at[k - 1], recv_e.at[k - 1], peers[k - 1]).wait_recv()
        for copy in near + far:
            copy.wait_send()

    return pl.pallas_call(
        kernel,
        out_shape=jax.ShapeDtypeStruct(part.shape, jnp.float32),
        in_specs=[VMEM],
        out_specs=VMEM,
        scratch_shapes=[
            pltpu.VMEM((tensors - 1,) + part.shape, jnp.float32),
            pltpu.VMEM(part.shape, jnp.float32),
            pltpu.SemaphoreType.DMA((tensors - 1,)),
            pltpu.SemaphoreType.DMA((tensors - 1,)),
            pltpu.SemaphoreType.DMA((groups - 1,)),
            pltpu.SemaphoreType.DMA((groups - 1,)),
        ],
        compiler_params=comm_params(collective_id, 16),
        name="gate_exchange",
    )(part)


def fast_shards(
    tokens_in,
    out_grad,
    w_qkv,
    w_attn_out,
    attn_gain,
    ffn_gain,
    qk_gain,
    w_router,
    w_gate,
    w_up,
    w_down,
    routes,
    segments,
):
    row_count, model_width = tokens_in.shape
    experts = w_router.shape[1]
    local_experts = w_gate.shape[0]
    heads_here = qk_gain.shape[1]
    local_width = heads_here * HEAD
    groups = lax.axis_size("expert")
    device_index = lax.axis_index("expert")
    tensor_index = lax.axis_index("tensor")
    quarter = model_width // lax.axis_size("tensor")
    hop_count = WINDOW // row_count
    score_scale = HEAD ** (-0.5)
    low = jnp.bfloat16

    chosen = jnp.any(
        routes[:, :, None] == jnp.arange(experts, dtype=jnp.int32)[None, None, :], axis=1
    ).astype(jnp.float32)
    qk_row = qk_gain.reshape(1, -1)
    smalls = jnp.concatenate(
        [
            attn_gain[None, :],
            ffn_gain[None, :],
            jnp.pad(qk_row, ((0, 0), (0, row_count - qk_row.shape[1]))),
            jnp.zeros((5, row_count), jnp.float32),
            w_router.T,
            chosen.T,
        ],
        axis=0,
    )
    qkv_low, out_low, small_all = weight_gather(
        w_qkv.astype(low), w_attn_out.astype(low), smalls, 0
    )

    def rounded(v):
        return v.astype(low).astype(jnp.float32)

    gain_one_f = rounded(small_all[:, 0]).reshape(model_width)
    gain_two_f = rounded(small_all[:, 1]).reshape(model_width)
    qk_gains = (
        rounded(small_all[:, 2, : qk_row.shape[1]])
        .reshape(groups, 2, heads_here, HEAD // groups)
        .transpose(1, 2, 0, 3)
        .reshape(2, local_width)
    )
    router_t = small_all[:, 8 : 8 + experts].transpose(1, 0, 2).reshape(experts, model_width).astype(low)
    chosen_all = small_all[:, 8 + experts : 8 + 2 * experts].transpose(0, 2, 1).reshape(
        groups * row_count, experts
    )
    grad_out_all = token_gather(out_grad, 1)

    tokens_f = tokens_in.astype(jnp.float32)
    scale_one = lax.rsqrt(jnp.mean(tokens_f * tokens_f, axis=-1, keepdims=True) + EPS)
    hidden_one = (tokens_f * scale_one * gain_one_f).astype(low)
    projected = jnp.einsum("td,jde->jte", hidden_one, qkv_low, preferred_element_type=jnp.float32)
    query_raw = projected[0]
    key_raw = projected[1]
    query_sq, key_sq = lax.psum(
        (jnp.sum(query_raw * query_raw, axis=-1), jnp.sum(key_raw * key_raw, axis=-1)), "tensor"
    )
    query_scale = lax.rsqrt(query_sq / model_width + EPS)[:, None]
    key_scale = lax.rsqrt(key_sq / model_width + EPS)[:, None]
    normed_query = query_raw * query_scale
    normed_key = key_raw * key_scale
    global_rows = device_index * row_count + jnp.arange(row_count, dtype=jnp.int32)
    cosine_table, sine_table = angles(global_rows % SEQ, HEAD)
    query_low = rotate(
        (normed_query * qk_gains[0]).reshape(row_count, heads_here, HEAD), cosine_table, sine_table
    ).astype(low)
    key_low = rotate(
        (normed_key * qk_gains[1]).reshape(row_count, heads_here, HEAD), cosine_table, sine_table
    ).astype(low)
    value_low = projected[2].astype(low).reshape(row_count, heads_here, HEAD)
    own_pair = jnp.stack([key_low, value_low])
    earlier = []
    for steps_back in range(hop_count, 0, -1):
        earlier.append(from_behind(own_pair, "expert", steps_back))
    context = jnp.concatenate(earlier + [own_pair], axis=1)
    key_rows = (device_index - hop_count) * row_count + jnp.arange(
        (hop_count + 1) * row_count, dtype=jnp.int32
    )
    segment_keys = segments[jnp.maximum(key_rows, 0)]
    segment_query = segments[global_rows]
    distance = global_rows[:, None] - key_rows[None, :]
    allowed = (
        (key_rows[None, :] >= 0)
        & (segment_query[:, None] == segment_keys[None, :])
        & (distance >= 0)
        & (distance < WINDOW)
    )

    def score_block():
        raw_scores = (
            jnp.einsum("qhd,khd->hqk", query_low, context[0], preferred_element_type=jnp.float32)
            * score_scale
        )
        return jnp.where(allowed[None], raw_scores, -1e30)

    scores = score_block()
    largest = jnp.max(scores, axis=-1, keepdims=True)
    exp_scores = jnp.exp(scores - largest)
    exp_total = jnp.sum(exp_scores, axis=-1, keepdims=True)
    log_total = largest + jnp.log(exp_total)
    attn_probs = (exp_scores / exp_total).astype(low)
    attended = (
        jnp.einsum("hqk,khd->qhd", attn_probs, context[1], preferred_element_type=jnp.float32)
        .reshape(row_count, local_width)
        .astype(low)
    )
    attention_out = tensor_sum(
        jnp.dot(attended, out_low, preferred_element_type=jnp.float32).astype(low), 2
    ).astype(jnp.float32)
    residual = tokens_f + attention_out
    scale_two = lax.rsqrt(jnp.mean(residual * residual, axis=-1, keepdims=True) + EPS)
    normed_two = residual * scale_two
    hidden_two = (normed_two * gain_two_f).astype(low)

    hidden_all = token_gather(hidden_two, 3)
    contract_last = (((1,), (1,)), ((), ()))

    def router(rows):
        logits = lax.dot_general(rows, router_t, contract_last, preferred_element_type=jnp.float32)
        logit_exp = jnp.exp(logits - jnp.max(logits, axis=-1, keepdims=True))
        return logit_exp / jnp.sum(logit_exp, axis=-1, keepdims=True)

    gates_here = lax.dynamic_slice_in_dim(
        router(hidden_all) * chosen_all, device_index * local_experts, local_experts, axis=1
    ).T[:, :, None]
    gate_low = w_gate.astype(low)
    up_low = w_up.astype(low)
    down_low = w_down.astype(low)
    gate_pre = jnp.einsum("td,edh->eth", hidden_all, gate_low, preferred_element_type=jnp.float32)
    up_pre = jnp.einsum("td,edh->eth", hidden_all, up_low, preferred_element_type=jnp.float32)
    sigmoid_gate = jax.nn.sigmoid(gate_pre)
    swish_gate = gate_pre * sigmoid_gate
    activated = swish_gate * up_pre
    gated = (activated * gates_here).astype(low)
    expert_part = jnp.einsum(
        "eth,ehd->td", gated, down_low, preferred_element_type=jnp.float32
    ).astype(low)
    grad_gated = jnp.einsum(
        "td,ehd->eth", grad_out_all, down_low, preferred_element_type=jnp.float32
    )
    grad_gates_here = jnp.sum(activated * grad_gated, axis=-1)
    grad_act = grad_gated * gates_here
    grad_gate_pre = (
        grad_act * up_pre * sigmoid_gate * (1.0 + gate_pre * (1.0 - sigmoid_gate))
    ).astype(low)
    grad_up_pre = (grad_act * swish_gate).astype(low)
    grad_rows = (
        jnp.einsum("eth,edh->td", grad_gate_pre, gate_low, preferred_element_type=jnp.float32)
        + jnp.einsum("eth,edh->td", grad_up_pre, up_low, preferred_element_type=jnp.float32)
    ).astype(low)
    grad_gate_sum = gate_exchange(
        jnp.pad(
            grad_gates_here.reshape(local_experts, groups, row_count).transpose(1, 0, 2),
            ((0, 0), (0, 8 - local_experts), (0, 0)),
        ),
        4,
    )
    grad_probs = (
        grad_gate_sum[:, :local_experts].reshape(experts, row_count).T * chosen
    )
    grad_hidden_quarter = token_reduce(grad_rows, 5)
    expert_quarter = token_reduce(expert_part, 6)
    grad_down = jnp.einsum(
        "eth,td->ehd", gated, grad_out_all, preferred_element_type=jnp.float32
    )
    grad_gate_w = jnp.einsum(
        "td,eth->edh", hidden_all, grad_gate_pre, preferred_element_type=jnp.float32
    )
    grad_up_w = jnp.einsum(
        "td,eth->edh", hidden_all, grad_up_pre, preferred_element_type=jnp.float32
    )
    column_order = [0, 2, 1, 3]

    def spread(piece):
        all_pieces = lax.all_gather(piece, "tensor", axis=0)
        return jnp.concatenate([all_pieces[i] for i in column_order], axis=1)

    def quarter_slot(t):
        return (t % 2) * 2 + t // 2

    grad_hidden_sum = spread(grad_hidden_quarter).astype(jnp.float32)
    block_out = residual + spread(expert_quarter).astype(jnp.float32)
    router_probs = router(hidden_two)
    grad_logits = (
        router_probs * (grad_probs - jnp.sum(router_probs * grad_probs, axis=-1, keepdims=True))
    ).astype(low)
    grad_out = out_grad.astype(jnp.float32)
    grad_hidden_two = grad_hidden_sum + jnp.dot(
        grad_logits, router_t, preferred_element_type=jnp.float32
    )
    grad_router_t = lax.dot_general(
        grad_logits, hidden_two, (((0,), (0,)), ((), ())), preferred_element_type=jnp.float32
    )
    grad_gain_two = jnp.sum(grad_hidden_two * normed_two, axis=0)
    scaled_two = grad_hidden_two * gain_two_f
    grad_residual = (
        grad_out
        + scale_two * scaled_two
        - residual
        * (scale_two * scale_two * scale_two)
        * jnp.mean(scaled_two * residual, axis=-1, keepdims=True)
    )
    grad_attn = grad_residual.astype(low)
    grad_out_w = jnp.dot(attended.T, grad_attn, preferred_element_type=jnp.float32)
    grad_attended = (
        lax.dot_general(grad_attn, out_low, contract_last, preferred_element_type=jnp.float32)
        .astype(low)
        .reshape(row_count, heads_here, HEAD)
    )
    attn_weights = jnp.where(allowed[None], jnp.exp(score_block() - log_total), 0.0)
    grad_weights = jnp.einsum(
        "qhd,khd->hqk", grad_attended, context[1], preferred_element_type=jnp.float32
    )
    inner_sum = jnp.sum(attn_weights * grad_weights, axis=-1, keepdims=True)
    grad_scores = (attn_weights * (grad_weights - inner_sum) * score_scale).astype(low)
    grad_query = jnp.einsum(
        "hqk,khd->qhd", grad_scores, context[0], preferred_element_type=jnp.float32
    )
    grad_keys = jnp.einsum(
        "hqk,qhd->khd", grad_scores, query_low, preferred_element_type=jnp.float32
    )
    grad_values = jnp.einsum(
        "hqk,qhd->khd", attn_weights.astype(low), grad_attended, preferred_element_type=jnp.float32
    )
    grad_pair = jnp.stack([grad_keys, grad_values]).reshape(
        2, hop_count + 1, row_count, heads_here, HEAD
    )
    own_grad = grad_pair[:, hop_count]
    for steps_back in range(1, hop_count + 1):
        own_grad = own_grad + from_behind(
            grad_pair[:, hop_count - steps_back].astype(low), "expert", -steps_back
        ).astype(jnp.float32)
    grad_query_norm = rotate(grad_query, cosine_table, -sine_table).reshape(row_count, local_width)
    grad_key_norm = rotate(own_grad[0], cosine_table, -sine_table).reshape(row_count, local_width)
    grad_gain_query = jnp.sum(grad_query_norm * normed_query, axis=0)
    grad_gain_key = jnp.sum(grad_key_norm * normed_key, axis=0)
    scaled_query = grad_query_norm * qk_gains[0]
    scaled_key = grad_key_norm * qk_gains[1]
    query_inner, key_inner = lax.psum(
        (jnp.sum(scaled_query * query_raw, axis=-1), jnp.sum(scaled_key * key_raw, axis=-1)),
        "tensor",
    )
    grad_query_raw = (
        query_scale * scaled_query
        - query_raw * (query_scale * query_scale * query_scale) * query_inner[:, None] / model_width
    ).astype(low)
    grad_key_raw = (
        key_scale * scaled_key
        - key_raw * (key_scale * key_scale * key_scale) * key_inner[:, None] / model_width
    ).astype(low)
    grad_value_raw = own_grad[1].reshape(row_count, local_width).astype(low)
    grad_proj = jnp.stack([grad_query_raw, grad_key_raw, grad_value_raw])
    grad_qkv = jnp.einsum("td,jte->jde", hidden_one, grad_proj, preferred_element_type=jnp.float32)
    grad_hidden_one = tensor_sum(
        jnp.einsum("jte,jde->td", grad_proj, qkv_low, preferred_element_type=jnp.float32).astype(low),
        7,
    ).astype(jnp.float32)
    grad_gain_one = jnp.sum(grad_hidden_one * tokens_f * scale_one, axis=0)
    scaled_one = grad_hidden_one * gain_one_f
    grad_tokens = (
        grad_residual
        + scale_one * scaled_one
        - tokens_f
        * (scale_one * scale_one * scale_one)
        * jnp.mean(scaled_one * tokens_f, axis=-1, keepdims=True)
    )
    grad_qk = (
        jnp.stack([grad_gain_query, grad_gain_key])
        .reshape(2, heads_here, groups, HEAD // groups)
        .transpose(2, 0, 1, 3)
        .reshape(groups, 1, qk_row.shape[1])
    )
    small_grads = jnp.concatenate(
        [
            grad_gain_one.reshape(groups, 1, row_count),
            grad_gain_two.reshape(groups, 1, row_count),
            jnp.pad(grad_qk, ((0, 0), (0, 0), (0, row_count - qk_row.shape[1]))),
            jnp.zeros((groups, 5, row_count), jnp.float32),
            grad_router_t.reshape(experts, groups, row_count).transpose(1, 0, 2),
        ],
        axis=1,
    )
    qkv_sum, out_sum, small_sum = weight_reduce(
        grad_qkv.astype(low), grad_out_w.astype(low), small_grads, 8
    )
    return (
        block_out.astype(low),
        grad_tokens.astype(low),
        qkv_sum,
        out_sum,
        small_sum[0],
        small_sum[1],
        small_sum[2, : qk_row.shape[1]].reshape(qk_gain.shape),
        small_sum[8 : 8 + experts].T,
        grad_gate_w,
        grad_up_w,
        grad_down,
    )


def solution(mesh):
    placed = (
        P("expert", None),
        P("expert", None),
        P(None, "expert", "tensor"),
        P("tensor", "expert"),
        P("expert"),
        P("expert"),
        P(None, "tensor", "expert"),
        P("expert", None),
        P("expert", None, "tensor"),
        P("expert", None, "tensor"),
        P("expert", "tensor", None),
        P("expert", None),
        P(),
    )
    compact = (mesh.shape["expert"], mesh.shape["tensor"]) == (GROUPS, NX * NC)
    return jax.shard_map(
        fast_shards if compact else shards,
        mesh=mesh,
        in_specs=placed,
        out_specs=(
            P("expert", None),
            P("expert", None),
            P(None, "expert", "tensor"),
            P("tensor", "expert"),
            P("expert"),
            P("expert"),
            P(None, "tensor", "expert"),
            P("expert", None),
            P("expert", None, "tensor"),
            P("expert", None, "tensor"),
            P("expert", "tensor", None),
        ),
        check_vma=False,
    )
```

```python
import jax
import jax.numpy as jnp
from jax import lax
from jax.experimental import pallas as pl
from jax.experimental.pallas import tpu as pltpu
from jax.sharding import PartitionSpec as P

HEAD = 128
WINDOW = 1024
SEQ = 2048


EPS = 1e-05
THETA = 10000.0


def from_behind(value, axis, steps):
    count = lax.axis_size(axis)
    initial, last = (max(0, -steps), min(count, count - steps))
    return lax.ppermute(value, axis, [(source, source + steps) for source in range(initial, last)])


def angles(position, head_size):
    half_size = head_size // 2
    frequency = THETA ** (-(jnp.arange(half_size, dtype=jnp.float32) * 2.0 / head_size))
    phase_angle = position.astype(jnp.float32)[:, None] * frequency[None, :]
    return (jnp.cos(phase_angle)[:, None, :], jnp.sin(phase_angle)[:, None, :])


def rotate(rotated_in, cosine_table, sine_table):
    half_size = rotated_in.shape[-1] // 2
    first_half = rotated_in[..., :half_size]
    second_half = rotated_in[..., half_size:]
    return jnp.concatenate(
        [
            first_half * cosine_table - second_half * sine_table,
            second_half * cosine_table + first_half * sine_table,
        ],
        axis=-1,
    )


def slot_layout(block_routes, experts, capacity):
    flat_routes = block_routes.reshape(-1)
    onehot = (flat_routes[:, None] == jnp.arange(experts, dtype=jnp.int32)[None, :]).astype(
        jnp.int32
    )
    before = jnp.cumsum(onehot, axis=0) - onehot
    rank_within = jnp.sum(before * onehot, axis=1)
    slot_index = flat_routes * capacity + rank_within
    slot_table = (
        jnp.zeros((experts * capacity,), jnp.int32)
        .at[slot_index]
        .set(jnp.arange(flat_routes.shape[0], dtype=jnp.int32) + 1)
    )
    return (slot_index, slot_table)


def shards(
    tokens_in,
    out_grad,
    w_qkv,
    w_attn_out,
    attn_gain,
    ffn_gain,
    qk_gain,
    w_router,
    w_gate,
    w_up,
    w_down,
    routes,
    segments,
):
    row_count, model_width = tokens_in.shape
    experts = w_router.shape[1]
    per_token = routes.shape[1]
    local_experts = w_gate.shape[0]
    heads_here = qk_gain.shape[1]
    local_width = heads_here * HEAD
    groups = lax.axis_size("expert")
    device = lax.axis_index("expert")
    capacity = row_count * per_token * 3 // (2 * experts)
    hop_count = WINDOW // row_count
    buffer_shape = (groups, local_experts, capacity, model_width)
    score_scale = HEAD ** (-0.5)

    def fetch_weights():
        return (
            lax.all_gather(w_qkv.astype(jnp.bfloat16), "expert", axis=1, tiled=True),
            lax.all_gather(w_attn_out.astype(jnp.bfloat16), "expert", axis=1, tiled=True),
            lax.all_gather(w_router.astype(jnp.bfloat16), "expert", axis=0, tiled=True),
            lax.all_gather(attn_gain.astype(jnp.bfloat16), "expert", axis=0, tiled=True),
            lax.all_gather(ffn_gain.astype(jnp.bfloat16), "expert", axis=0, tiled=True),
            lax.all_gather(qk_gain.astype(jnp.bfloat16), "expert", axis=2, tiled=True),
        )

    def prepare(pieces):
        return (
            pieces[0],
            pieces[1],
            pieces[2],
            pieces[3].astype(jnp.float32),
            pieces[4].astype(jnp.float32),
            pieces[5].astype(jnp.float32).reshape(2, local_width),
        )

    qkv_low, out_low, router_low, gain_one_f, gain_two_f, qk_gains = prepare(fetch_weights())
    tokens_f = tokens_in.astype(jnp.float32)
    scale_one = lax.rsqrt(jnp.mean(tokens_f * tokens_f, axis=-1, keepdims=True) + EPS)
    hidden_one = (tokens_f * scale_one * gain_one_f).astype(jnp.bfloat16)
    projected = jnp.einsum("td,jde->jte", hidden_one, qkv_low, preferred_element_type=jnp.float32)
    query_raw = projected[0]
    key_raw = projected[1]
    query_sq, key_sq = lax.psum(
        (jnp.sum(query_raw * query_raw, axis=-1), jnp.sum(key_raw * key_raw, axis=-1)), "tensor"
    )
    query_scale = lax.rsqrt(query_sq / model_width + EPS)[:, None]
    key_scale = lax.rsqrt(key_sq / model_width + EPS)[:, None]
    normed_query = query_raw * query_scale
    normed_key = key_raw * key_scale
    global_rows = device * row_count + jnp.arange(row_count, dtype=jnp.int32)
    cosine_table, sine_table = angles(global_rows % SEQ, HEAD)
    query_low = rotate(
        (normed_query * qk_gains[0]).reshape(row_count, heads_here, HEAD), cosine_table, sine_table
    ).astype(jnp.bfloat16)
    key_low = rotate(
        (normed_key * qk_gains[1]).reshape(row_count, heads_here, HEAD), cosine_table, sine_table
    ).astype(jnp.bfloat16)
    value_low = projected[2].astype(jnp.bfloat16).reshape(row_count, heads_here, HEAD)
    own_pair = jnp.stack([key_low, value_low])
    earlier = []
    for steps_back in range(hop_count, 0, -1):
        earlier.append(from_behind(own_pair, "expert", steps_back))
    context = jnp.concatenate(earlier + [own_pair], axis=1)
    key_rows = (device - hop_count) * row_count + jnp.arange(
        (hop_count + 1) * row_count, dtype=jnp.int32
    )
    segment_keys = segments[jnp.maximum(key_rows, 0)]
    segment_query = segments[global_rows]
    distance = global_rows[:, None] - key_rows[None, :]
    allowed = (
        (key_rows[None, :] >= 0)
        & (segment_query[:, None] == segment_keys[None, :])
        & (distance >= 0)
        & (distance < WINDOW)
    )

    def score_block():
        raw_scores = (
            jnp.einsum("qhd,khd->hqk", query_low, context[0], preferred_element_type=jnp.float32)
            * score_scale
        )
        return jnp.where(allowed[None], raw_scores, -1e30)

    scores = score_block()
    largest = jnp.max(scores, axis=-1, keepdims=True)
    exp_scores = jnp.exp(scores - largest)
    exp_total = jnp.sum(exp_scores, axis=-1, keepdims=True)
    log_total = largest + jnp.log(exp_total)
    attn_probs = (exp_scores / exp_total).astype(jnp.bfloat16)
    attended = (
        jnp.einsum("hqk,khd->qhd", attn_probs, context[1], preferred_element_type=jnp.float32)
        .reshape(row_count, local_width)
        .astype(jnp.bfloat16)
    )
    attention_out = lax.psum(
        jnp.dot(attended, out_low, preferred_element_type=jnp.float32).astype(jnp.bfloat16),
        "tensor",
    ).astype(jnp.float32)
    residual = tokens_f + attention_out
    scale_two = lax.rsqrt(jnp.mean(residual * residual, axis=-1, keepdims=True) + EPS)
    normed_two = residual * scale_two
    hidden_two = (normed_two * gain_two_f).astype(jnp.bfloat16)
    logits = jnp.dot(hidden_two, router_low, preferred_element_type=jnp.float32)
    logit_exp = jnp.exp(logits - jnp.max(logits, axis=-1, keepdims=True))
    router_probs = logit_exp / jnp.sum(logit_exp, axis=-1, keepdims=True)
    chosen = routes[:, :, None] == jnp.arange(experts, dtype=jnp.int32)[None, None, :]
    gate_probs = jnp.sum(jnp.where(chosen, router_probs[:, None, :], 0.0), axis=-1)
    slot_index, slot_table = slot_layout(routes, experts, capacity)
    present = (slot_table > 0)[:, None]
    assigned = jnp.maximum(slot_table - 1, 0)
    row_of_slot = assigned // per_token
    gate_low = w_gate.astype(jnp.bfloat16)
    up_low = w_up.astype(jnp.bfloat16)
    down_low = w_down.astype(jnp.bfloat16)

    def send_rows():
        buffer_rows = jnp.where(
            present, hidden_two[row_of_slot], jnp.zeros((), jnp.bfloat16)
        ).reshape(buffer_shape)
        return lax.all_to_all(buffer_rows, "expert", split_axis=0, concat_axis=0, tiled=True)

    def expert_front(arrived):
        gate_pre = jnp.einsum(
            "secd,edh->sech", arrived, gate_low, preferred_element_type=jnp.float32
        )
        up_pre = jnp.einsum("secd,edh->sech", arrived, up_low, preferred_element_type=jnp.float32)
        return (gate_pre, up_pre)

    received = send_rows()
    gate_pre, up_pre = expert_front(received)
    activated = (gate_pre * jax.nn.sigmoid(gate_pre) * up_pre).astype(jnp.bfloat16)
    partial_value = jnp.einsum(
        "sech,ehd->secd", activated, down_low, preferred_element_type=jnp.float32
    ).astype(jnp.bfloat16)
    returned = lax.all_to_all(
        partial_value, "expert", split_axis=0, concat_axis=0, tiled=True
    ).reshape(experts * capacity, model_width)
    expert_rows = returned[slot_index].reshape(row_count, per_token, model_width)
    expert_part = jnp.einsum(
        "tk,tkd->td", gate_probs, expert_rows, preferred_element_type=jnp.float32
    )
    block_out = residual + lax.psum(expert_part.astype(jnp.bfloat16), "tensor").astype(jnp.float32)
    qkv_low, out_low, router_low, gain_one_f, gain_two_f, qk_gains = prepare(fetch_weights())
    grad_out = out_grad.astype(jnp.float32)
    grad_gate_part = jnp.einsum(
        "td,tkd->tk", grad_out, expert_rows, preferred_element_type=jnp.float32
    )
    slot_grads = (
        (gate_probs[:, :, None] * grad_out[:, None, :])
        .astype(jnp.bfloat16)
        .reshape(row_count * per_token, model_width)
    )
    grad_buffer = jnp.where(present, slot_grads[assigned], jnp.zeros((), jnp.bfloat16)).reshape(
        buffer_shape
    )
    grad_received = lax.all_to_all(grad_buffer, "expert", split_axis=0, concat_axis=0, tiled=True)
    received = send_rows()
    gate_pre, up_pre = expert_front(received)
    sigmoid_gate = jax.nn.sigmoid(gate_pre)
    swish_gate = gate_pre * sigmoid_gate
    activated = (swish_gate * up_pre).astype(jnp.bfloat16)
    grad_act = jnp.einsum(
        "secd,ehd->sech", grad_received, down_low, preferred_element_type=jnp.float32
    )
    grad_down = jnp.einsum(
        "sech,secd->ehd", activated, grad_received, preferred_element_type=jnp.float32
    )
    grad_gate_pre = (
        grad_act * up_pre * sigmoid_gate * (1.0 + gate_pre * (1.0 - sigmoid_gate))
    ).astype(jnp.bfloat16)
    grad_up_pre = (grad_act * swish_gate).astype(jnp.bfloat16)
    grad_gate_w = jnp.einsum(
        "secd,sech->edh", received, grad_gate_pre, preferred_element_type=jnp.float32
    )
    grad_up_w = jnp.einsum(
        "secd,sech->edh", received, grad_up_pre, preferred_element_type=jnp.float32
    )
    grad_rows = (
        jnp.einsum("sech,edh->secd", grad_gate_pre, gate_low, preferred_element_type=jnp.float32)
        + jnp.einsum("sech,edh->secd", grad_up_pre, up_low, preferred_element_type=jnp.float32)
    ).astype(jnp.bfloat16)
    grad_back = lax.all_to_all(
        grad_rows, "expert", split_axis=0, concat_axis=0, tiled=True
    ).reshape(experts * capacity, model_width)
    grad_hidden_part = jnp.sum(
        grad_back[slot_index].reshape(row_count, per_token, model_width), axis=1, dtype=jnp.float32
    )
    grad_hidden_sum, grad_gates = (
        lax.psum(grad_hidden_part.astype(jnp.bfloat16), "tensor").astype(jnp.float32),
        lax.psum(grad_gate_part.astype(jnp.bfloat16), "tensor").astype(jnp.float32),
    )
    grad_probs = jnp.sum(jnp.where(chosen, grad_gates[:, :, None], 0.0), axis=1)
    grad_logits = (
        router_probs * (grad_probs - jnp.sum(router_probs * grad_probs, axis=-1, keepdims=True))
    ).astype(jnp.bfloat16)
    grad_hidden_two = grad_hidden_sum + jnp.dot(
        grad_logits, router_low.T, preferred_element_type=jnp.float32
    )
    grad_router = jnp.dot(hidden_two.T, grad_logits, preferred_element_type=jnp.float32)
    grad_gain_two = jnp.sum(grad_hidden_two * normed_two, axis=0)
    scaled_two = grad_hidden_two * gain_two_f
    grad_residual = (
        grad_out
        + scale_two * scaled_two
        - residual
        * (scale_two * scale_two * scale_two)
        * jnp.mean(scaled_two * residual, axis=-1, keepdims=True)
    )
    grad_attn = grad_residual.astype(jnp.bfloat16)
    grad_out_w = jnp.dot(attended.T, grad_attn, preferred_element_type=jnp.float32)
    grad_attended = (
        jnp.dot(grad_attn, out_low.T, preferred_element_type=jnp.float32)
        .astype(jnp.bfloat16)
        .reshape(row_count, heads_here, HEAD)
    )
    attn_weights = jnp.where(allowed[None], jnp.exp(score_block() - log_total), 0.0)
    grad_weights = jnp.einsum(
        "qhd,khd->hqk", grad_attended, context[1], preferred_element_type=jnp.float32
    )
    inner_sum = jnp.sum(attn_weights * grad_weights, axis=-1, keepdims=True)
    grad_scores = (attn_weights * (grad_weights - inner_sum) * score_scale).astype(jnp.bfloat16)
    grad_query = jnp.einsum(
        "hqk,khd->qhd", grad_scores, context[0], preferred_element_type=jnp.float32
    )
    grad_keys = jnp.einsum(
        "hqk,qhd->khd", grad_scores, query_low, preferred_element_type=jnp.float32
    )
    grad_values = jnp.einsum(
        "hqk,qhd->khd",
        attn_weights.astype(jnp.bfloat16),
        grad_attended,
        preferred_element_type=jnp.float32,
    )
    grad_pair = jnp.stack([grad_keys, grad_values]).reshape(
        2, hop_count + 1, row_count, heads_here, HEAD
    )
    own_grad = grad_pair[:, hop_count]
    for steps_back in range(1, hop_count + 1):
        own_grad = own_grad + from_behind(
            grad_pair[:, hop_count - steps_back].astype(jnp.bfloat16), "expert", -steps_back
        ).astype(jnp.float32)
    grad_query_norm = rotate(grad_query, cosine_table, -sine_table).reshape(row_count, local_width)
    grad_key_norm = rotate(own_grad[0], cosine_table, -sine_table).reshape(row_count, local_width)
    grad_gain_query = jnp.sum(grad_query_norm * normed_query, axis=0)
    grad_gain_key = jnp.sum(grad_key_norm * normed_key, axis=0)
    scaled_query = grad_query_norm * qk_gains[0]
    scaled_key = grad_key_norm * qk_gains[1]
    query_inner, key_inner = lax.psum(
        (jnp.sum(scaled_query * query_raw, axis=-1), jnp.sum(scaled_key * key_raw, axis=-1)),
        "tensor",
    )
    grad_query_raw = (
        query_scale * scaled_query
        - query_raw * (query_scale * query_scale * query_scale) * query_inner[:, None] / model_width
    ).astype(jnp.bfloat16)
    grad_key_raw = (
        key_scale * scaled_key
        - key_raw * (key_scale * key_scale * key_scale) * key_inner[:, None] / model_width
    ).astype(jnp.bfloat16)
    grad_value_raw = own_grad[1].reshape(row_count, local_width).astype(jnp.bfloat16)
    grad_proj = jnp.stack([grad_query_raw, grad_key_raw, grad_value_raw])
    grad_qkv = jnp.einsum("td,jte->jde", hidden_one, grad_proj, preferred_element_type=jnp.float32)
    grad_hidden_one = lax.psum(
        jnp.einsum("jte,jde->td", grad_proj, qkv_low, preferred_element_type=jnp.float32).astype(
            jnp.bfloat16
        ),
        "tensor",
    ).astype(jnp.float32)
    grad_gain_one = jnp.sum(grad_hidden_one * tokens_f * scale_one, axis=0)
    scaled_one = grad_hidden_one * gain_one_f
    grad_tokens = (
        grad_residual
        + scale_one * scaled_one
        - tokens_f
        * (scale_one * scale_one * scale_one)
        * jnp.mean(scaled_one * tokens_f, axis=-1, keepdims=True)
    )
    grad_qk = jnp.stack([grad_gain_query, grad_gain_key]).reshape(2, heads_here, HEAD)
    reduced = (
        lax.psum_scatter(
            grad_qkv.astype(jnp.bfloat16), "expert", scatter_dimension=1, tiled=True
        ).astype(jnp.float32),
        lax.psum_scatter(
            grad_out_w.astype(jnp.bfloat16), "expert", scatter_dimension=1, tiled=True
        ).astype(jnp.float32),
        lax.psum_scatter(
            grad_router.astype(jnp.bfloat16), "expert", scatter_dimension=0, tiled=True
        ).astype(jnp.float32),
        lax.psum_scatter(
            grad_gain_one.astype(jnp.bfloat16), "expert", scatter_dimension=0, tiled=True
        ).astype(jnp.float32),
        lax.psum_scatter(
            grad_gain_two.astype(jnp.bfloat16), "expert", scatter_dimension=0, tiled=True
        ).astype(jnp.float32),
        lax.psum_scatter(
            grad_qk.astype(jnp.bfloat16), "expert", scatter_dimension=2, tiled=True
        ).astype(jnp.float32),
    )
    return (
        block_out.astype(jnp.bfloat16),
        grad_tokens.astype(jnp.bfloat16),
        reduced[0],
        reduced[1],
        reduced[3],
        reduced[4],
        reduced[5],
        reduced[2],
        grad_gate_w,
        grad_up_w,
        grad_down,
    )


MESH_ID = pl.DeviceIdType.MESH
HBM = pl.BlockSpec(memory_space=pl.ANY)
VMEM = pl.BlockSpec(memory_space=pltpu.VMEM)
NZ, NY, NX, NC = 4, 2, 2, 2
GROUPS = NZ * NY


def place():
    e = lax.axis_index("expert")
    t = lax.axis_index("tensor")
    return lax.div(e, NY), lax.rem(e, NY), lax.div(t, NC), lax.rem(t, NC)


def device(z, y, x, c):
    return (z * NY + y, x * NC + c)


def run_if(condition, body):
    if condition is None:
        body()
    else:
        pl.when(condition)(body)


def greet(partners):
    barrier = pltpu.get_barrier_semaphore()
    for target, condition in partners:
        run_if(
            condition,
            lambda target=target: pl.semaphore_signal(
                barrier, inc=1, device_id=target, device_id_type=MESH_ID
            ),
        )
    count = sum(1 for _, condition in partners if condition is None)
    for _, condition in partners:
        if condition is not None:
            count = count + condition.astype(jnp.int32)
    pl.semaphore_wait(barrier, count)


def remote(source, target_ref, send_sem, recv_sem, target):
    return pltpu.make_async_remote_copy(
        src_ref=source,
        dst_ref=target_ref,
        send_sem=send_sem,
        recv_sem=recv_sem,
        device_id=target,
        device_id_type=MESH_ID,
    )


def block_rows(block, rows):
    return pl.ds(pl.multiple_of(block * rows, rows), rows)


class LineGather:
    def __init__(self, streams, sources, views, send_sem, recv_sem):
        self.z, self.y, self.x, self.c = place()
        self.streams, self.sources, self.views = streams, sources, views
        self.send_sem, self.recv_sem = send_sem, recv_sem
        self.has_up, self.has_down = self.z < NZ - 1, self.z > 0
        self.pending = []

    def partners(self):
        z, y, x, c = self.z, self.y, self.x, self.c
        return [
            (device(z + 1, y, x, c), z < NZ - 1),
            (device(z - 1, y, x, c), z > 0),
            (device(z, 1 - y, x, c), None),
        ]

    def exists(self, rel):
        rel = rel % 7
        if rel == 0:
            return None
        return self.z >= rel if rel < 4 else self.z + (rel - 3) < NZ

    def block(self, rel):
        y = self.y if rel < 7 else 1 - self.y
        rel = rel % 7
        z = self.z if rel == 0 else (self.z - rel if rel < 4 else self.z + (rel - 3))
        return z * NY + y

    def send(self, stream, rel, way):
        z, y, x, c = self.z, self.y, self.x, self.c
        block = self.block(rel)
        there = self.views[stream](block)
        source = self.sources[stream] if rel == 0 else there
        if way == 0:
            target, landing = device(z + 1, y, x, c), (1 if rel == 0 else rel + 1)
        elif way == 1:
            target, landing = device(z - 1, y, x, c), (4 if rel == 0 else rel + 1)
        else:
            target, landing = device(z, 1 - y, x, c), 7 + rel
        return remote(
            source,
            there,
            self.send_sem.at[stream, rel, way],
            self.recv_sem.at[stream, landing],
            target,
        )

    def start(self, stream, rel):
        if rel < 4:
            run = self.has_up
            run_if(run, lambda: self.send(stream, rel, 0).start())
            self.pending.append((stream, rel, 0, run))
        if rel == 0 or rel >= 4:
            run = self.has_down
            run_if(run, lambda: self.send(stream, rel, 1).start())
            self.pending.append((stream, rel, 1, run))
        self.send(stream, rel, 2).start()
        self.pending.append((stream, rel, 2, None))

    def arrive(self, stream, rel):
        there = self.views[stream](self.block(rel))
        remote(
            there,
            there,
            self.send_sem.at[stream, 0, 0],
            self.recv_sem.at[stream, rel],
            device(self.z, 1 - self.y, self.x, self.c),
        ).wait_recv()

    def order(self):
        return [7, 1, 4, 8, 11, 2, 5, 9, 12, 3, 6, 10, 13]

    def run(self, hook=None):
        for stream in self.streams:
            self.start(stream, 0)
        for rel in self.order():
            def step(rel=rel):
                marks = len(self.pending)
                for stream in self.streams:
                    self.arrive(stream, rel)
                    if rel < 7:
                        self.start(stream, rel)
                    if hook is not None:
                        hook(stream, rel)
                if rel < 7:
                    late = self.pending[marks:]
                    del self.pending[marks:]
                    self.finish_later(late, rel)
            run_if(self.exists(rel), step)

    def finish_later(self, late, rel):
        self.late = getattr(self, "late", []) + [(rel, late)]

    def finish(self):
        for stream, rel, way, run in self.pending:
            run_if(run, lambda s=stream, r=rel, w=way: self.send(s, r, w).wait_send())
        for rel, late in getattr(self, "late", []):
            def body(late=late):
                for stream, rel, way, run in late:
                    run_if(run, lambda s=stream, r=rel, w=way: self.send(s, r, w).wait_send())
            run_if(self.exists(rel), body)


def cost(microseconds):
    return pl.CostEstimate(flops=0, bytes_accessed=int(microseconds * 3.0e6), transcendentals=0)


def comm_params(collective_id, megabytes=56):
    return pltpu.CompilerParams(
        collective_id=collective_id,
        has_side_effects=True,
        vmem_limit_bytes=megabytes * 1024 * 1024,
    )


def weight_gather(qkv_low, out_low, smalls, collective_id):
    parts, rows, width = qkv_low.shape
    depth, columns = out_low.shape

    def kernel(qkv, out, small, qkv_all, out_all, small_all, send_sem, recv_sem, local_sem):
        views = [
            lambda b: qkv_all.at[:, block_rows(b, rows), :],
            lambda b: out_all.at[:, block_rows(b, columns)],
            lambda b: small_all.at[b],
        ]
        line = LineGather([2, 0, 1], [qkv, out, small], views, send_sem, recv_sem)
        greet(line.partners())
        own = line.block(0)
        keep = [
            pltpu.make_async_copy(source, view(own), local_sem.at[i])
            for i, (source, view) in enumerate(zip([qkv, out, small], views))
        ]
        for copy in keep:
            copy.start()
        line.run()
        line.finish()
        for copy in keep:
            copy.wait()

    return pl.pallas_call(
        kernel,
        out_shape=(
            jax.ShapeDtypeStruct((parts, rows * GROUPS, width), jnp.bfloat16),
            jax.ShapeDtypeStruct((depth, columns * GROUPS), jnp.bfloat16),
            jax.ShapeDtypeStruct((GROUPS,) + smalls.shape, jnp.float32),
        ),
        in_specs=[HBM] * 3,
        out_specs=(HBM, HBM, HBM),
        scratch_shapes=[
            pltpu.SemaphoreType.DMA((3, 7, 3)),
            pltpu.SemaphoreType.DMA((3, 14)),
            pltpu.SemaphoreType.DMA((3,)),
        ],
        compiler_params=comm_params(collective_id),
        cost_estimate=cost(100),
        name="weight_gather",
    )(qkv_low, out_low, smalls)


def token_gather(block, collective_id):
    rows, width = block.shape
    a_cols, c_cols = width * 3 // 16, width // 8

    def kernel(own_ref, all_ref, send_sem, recv_sem, x_send, x_recv, core_send, core_recv, local_sem):
        z, y, x, c = place()

        def a_at(xx, cc):
            return pl.ds(pl.multiple_of(xx * (2 * a_cols) + cc * a_cols, 128), a_cols)

        def c_at(cc):
            return pl.ds(pl.multiple_of(4 * a_cols + cc * c_cols, 128), c_cols)

        def view(b, columns):
            return all_ref.at[block_rows(b, rows), columns]

        sources = [own_ref.at[:, a_at(x, c)], own_ref.at[:, c_at(c)]]
        views = [lambda b: view(b, a_at(x, c)), lambda b: view(b, c_at(c))]
        line = LineGather([0, 1], sources, views, send_sem, recv_sem)
        across, twin = device(z, y, 1 - x, c), device(z, y, x, 1 - c)
        greet(line.partners() + [(across, None), (twin, None)])
        keep = pltpu.make_async_copy(own_ref, all_ref.at[block_rows(line.block(0), rows), :], local_sem)
        keep.start()

        def to_twin(rel, stream, landing=False):
            b = line.block(rel)
            columns = [a_at(x, c), c_at(c), a_at(1 - x, c)][stream]
            other = [a_at(x, 1 - c), c_at(1 - c), a_at(1 - x, 1 - c)][stream]
            piece = view(b, other if landing else columns)
            return remote(piece, piece, core_send.at[rel, stream], core_recv.at[rel, stream], twin)

        def to_across(rel, landing=False):
            b = line.block(rel)
            piece = view(b, a_at(1 - x if landing else x, c))
            return remote(piece, piece, x_send.at[rel], x_recv.at[rel], across)

        def hook(stream, rel):
            if stream == 0:
                to_across(rel).start()
            to_twin(rel, stream).start()

        line.run(hook)
        for rel in line.order():
            def relay(rel=rel):
                to_across(rel, True).wait_recv()
                to_twin(rel, 2).start()
            run_if(line.exists(rel), relay)
        for rel in line.order():
            def end(rel=rel):
                to_across(rel).wait_send()
                for stream in range(3):
                    to_twin(rel, stream, True).wait_recv()
                    to_twin(rel, stream).wait_send()
            run_if(line.exists(rel), end)
        line.finish()
        keep.wait()

    return pl.pallas_call(
        kernel,
        out_shape=jax.ShapeDtypeStruct((rows * GROUPS, width), block.dtype),
        in_specs=[HBM],
        out_specs=HBM,
        scratch_shapes=[
            pltpu.SemaphoreType.DMA((2, 7, 3)),
            pltpu.SemaphoreType.DMA((2, 14)),
            pltpu.SemaphoreType.DMA((14,)),
            pltpu.SemaphoreType.DMA((14,)),
            pltpu.SemaphoreType.DMA((14, 3)),
            pltpu.SemaphoreType.DMA((14, 3)),
            pltpu.SemaphoreType.DMA,
        ],
        compiler_params=comm_params(collective_id),
        cost_estimate=cost(45),
        name="token_gather",
    )(block)


def add_into(rows, step, store):
    def body(i, carry):
        store(pl.ds(pl.multiple_of(i * step, step), step))
        return carry

    lax.fori_loop(0, rows // step, body, 0)


def group_sum(part_ref, out_ref, core_buf, x_buf, send_sem, recv_sem, meanwhile=None):
    rows, width = part_ref.shape
    half, quarter = width // 2, width // 4
    z, y, x, c = place()
    across, twin = device(z, y, 1 - x, c), device(z, y, x, 1 - c)

    def half_of(cc):
        return pl.ds(pl.multiple_of(cc * half, half), half)

    def quarter_of(xx, cc):
        return pl.ds(pl.multiple_of(cc * half + xx * quarter, quarter), quarter)

    first = remote(part_ref.at[:, half_of(1 - c)], core_buf, send_sem.at[0], recv_sem.at[0], twin)
    first.start()
    if meanwhile is not None:
        meanwhile()
    first.wait_recv()
    add_to(core_buf, core_buf, part_ref.at[:, half_of(c)], 32)
    second = remote(
        core_buf.at[:, pl.ds(pl.multiple_of((1 - x) * quarter, quarter), quarter)],
        x_buf, send_sem.at[1], recv_sem.at[1], across,
    )
    second.start()
    second.wait_recv()
    own = out_ref.at[:, quarter_of(x, c)]
    add_to(own, x_buf, core_buf.at[:, pl.ds(pl.multiple_of(x * quarter, quarter), quarter)], 32)
    third = remote(own, own, send_sem.at[2], recv_sem.at[2], across)
    third.start()
    fourth = remote(own, own, send_sem.at[3], recv_sem.at[3], twin)
    fourth.start()
    from_x = out_ref.at[:, quarter_of(1 - x, c)]
    remote(from_x, from_x, send_sem.at[2], recv_sem.at[2], across).wait_recv()
    fifth = remote(from_x, from_x, send_sem.at[4], recv_sem.at[4], twin)
    fifth.start()
    for index, column in ((3, quarter_of(x, 1 - c)), (4, quarter_of(1 - x, 1 - c))):
        landing = out_ref.at[:, column]
        remote(landing, landing, send_sem.at[index], recv_sem.at[index], twin).wait_recv()
    for copy in (first, second, third, fourth, fifth):
        copy.wait_send()


def tensor_sum(part, collective_id):
    rows, width = part.shape

    def kernel(part_ref, out_ref, core_buf, x_buf, send_sem, recv_sem):
        z, y, x, c = place()
        greet([(device(z, y, 1 - x, c), None), (device(z, y, x, 1 - c), None)])
        group_sum(part_ref, out_ref, core_buf, x_buf, send_sem, recv_sem)

    return pl.pallas_call(
        kernel,
        out_shape=jax.ShapeDtypeStruct((rows, width), jnp.bfloat16),
        in_specs=[VMEM],
        out_specs=VMEM,
        scratch_shapes=[
            pltpu.VMEM((rows, width // 2), jnp.bfloat16),
            pltpu.VMEM((rows, width // 4), jnp.bfloat16),
            pltpu.SemaphoreType.DMA((5,)),
            pltpu.SemaphoreType.DMA((5,)),
        ],
        compiler_params=comm_params(collective_id, 16),
        cost_estimate=cost(17),
        name="tensor_sum",
    )(part)


Z_ORDER = (3, 0, 2, 1)


def accumulate(into, addend, step=64):
    rows = into.shape[0]
    step = min(step, rows)

    def body(i, carry):
        r = pl.ds(pl.multiple_of(i * step, step), step)
        total = into[r, :].astype(jnp.float32) + addend[r, :].astype(jnp.float32)
        into[r, :] = total.astype(into.dtype)
        return carry

    lax.fori_loop(0, rows // step, body, 0)


class LineReduce:
    def __init__(self, streams, own, y_buf, lo_buf, hi_buf, send_sem, recv_sem):
        self.z, self.y, self.x, self.c = place()
        self.streams = streams
        self.own, self.y_buf, self.lo_buf, self.hi_buf = own, y_buf, lo_buf, hi_buf
        self.send_sem, self.recv_sem = send_sem, recv_sem

    def partners(self):
        z, y, x, c = self.z, self.y, self.x, self.c
        return [
            (device(z + 1, y, x, c), z < NZ - 1),
            (device(z - 1, y, x, c), z > 0),
            (device(z, 1 - y, x, c), None),
        ]

    def copy(self, s, zz, way):
        z, y, x, c = self.z, self.y, self.x, self.c
        if way == 0:
            source, landing, target = self.own(s, zz, 1 - y), self.y_buf, device(z, 1 - y, x, c)
        elif way == 1:
            source, landing, target = self.y_buf(s, zz), self.lo_buf, device(z + 1, y, x, c)
        else:
            source, landing, target = self.y_buf(s, zz), self.hi_buf, device(z - 1, y, x, c)
        return remote(
            source, landing(s, zz), self.send_sem.at[s, zz, way], self.recv_sem.at[s, zz, way], target
        )

    def to_y(self, s, zz):
        self.copy(s, zz, 0).start()

    def take(self, s, zz, way):
        self.copy(s, zz, way).wait_recv()
        accumulate(self.y_buf(s, zz), (self.lo_buf if way == 1 else self.hi_buf)(s, zz))

    def along_z(self, s, zz):
        z = self.z
        self.copy(s, zz, 0).wait_recv()
        accumulate(self.y_buf(s, zz), self.own(s, zz, self.y))

        def upward():
            run_if(z > 0, lambda: self.take(s, zz, 1))
            self.copy(s, zz, 1).start()

        def downward():
            run_if(z < NZ - 1, lambda: self.take(s, zz, 2))
            self.copy(s, zz, 2).start()

        run_if(z < zz, upward)
        run_if(z > zz, downward)

    def home(self, done):
        for zz in range(NZ):
            def land(zz=zz):
                for s in self.streams:
                    if zz > 0:
                        self.take(s, zz, 1)
                    if zz < NZ - 1:
                        self.take(s, zz, 2)
                    done(s, self.y_buf(s, zz))
            run_if(self.z == zz, land)

    def finish(self):
        for zz in range(NZ):
            for s in self.streams:
                self.copy(s, zz, 0).wait_send()
                run_if(self.z < zz, lambda s=s, zz=zz: self.copy(s, zz, 1).wait_send())
                run_if(self.z > zz, lambda s=s, zz=zz: self.copy(s, zz, 2).wait_send())


def weight_reduce(qkv, out, smalls, collective_id):
    parts, depth, width = qkv.shape
    rows = depth // GROUPS
    out_rows, columns = out.shape[0], out.shape[1] // GROUPS

    def kernel(qkv_ref, out_ref, small_ref, qkv_sum, out_sum, small_sum,
               qkv_buf, out_buf, small_buf, send_sem, recv_sem):
        def own(s, zz, yy):
            b = zz * NY + yy
            if s < parts:
                return qkv_ref.at[s, block_rows(b, rows), :]
            if s == parts:
                return out_ref.at[:, block_rows(b, columns)]
            return small_ref.at[b]

        def slot(kind):
            def view(s, zz):
                if s < parts:
                    return qkv_buf.at[kind, zz, s]
                if s == parts:
                    return out_buf.at[kind, zz]
                return small_buf.at[kind, zz]
            return view

        streams = list(range(parts + 2))
        line = LineReduce(streams, own, slot(0), slot(1), slot(2), send_sem, recv_sem)
        greet(line.partners())
        work = [(s, zz) for s in [parts + 1, parts] + list(range(parts)) for zz in Z_ORDER]
        for s, zz in work:
            line.to_y(s, zz)
        for s, zz in work:
            line.along_z(s, zz)

        def done(s, total):
            target = qkv_sum.at[s] if s < parts else (out_sum if s == parts else small_sum)
            step = min(64, target.shape[0])

            def body(i, carry):
                r = pl.ds(pl.multiple_of(i * step, step), step)
                target[r, :] = total[r, :].astype(jnp.float32)
                return carry

            lax.fori_loop(0, target.shape[0] // step, body, 0)

        line.home(done)
        line.finish()

    return pl.pallas_call(
        kernel,
        out_shape=(
            jax.ShapeDtypeStruct((parts, rows, width), jnp.float32),
            jax.ShapeDtypeStruct((out_rows, columns), jnp.float32),
            jax.ShapeDtypeStruct(smalls.shape[1:], jnp.float32),
        ),
        in_specs=[VMEM] * 3,
        out_specs=(VMEM,) * 3,
        scratch_shapes=[
            pltpu.VMEM((3, NZ, parts, rows, width), jnp.bfloat16),
            pltpu.VMEM((3, NZ, out_rows, columns), jnp.bfloat16),
            pltpu.VMEM((3, NZ) + smalls.shape[1:], jnp.float32),
            pltpu.SemaphoreType.DMA((parts + 2, NZ, 3)),
            pltpu.SemaphoreType.DMA((parts + 2, NZ, 3)),
        ],
        compiler_params=comm_params(collective_id),
        cost_estimate=cost(120),
        name="weight_reduce",
    )(qkv, out, smalls)


def token_reduce(part, collective_id, pairs=None):
    tokens, width = part.shape
    rows = tokens // GROUPS
    half, quarter = width // 2, width // 4

    def kernel(part_ref, out_ref, core_buf, x_buf, y_buf, lo_buf, hi_buf,
               core_send, core_recv, x_send, x_recv, send_sem, recv_sem):
        z, y, x, c = place()
        across, twin = device(z, y, 1 - x, c), device(z, y, x, 1 - c)

        line = LineReduce(
            [0], lambda s, zz, yy: x_buf.at[zz * NY + yy], lambda s, zz: y_buf.at[zz],
            lambda s, zz: lo_buf.at[zz], lambda s, zz: hi_buf.at[zz], send_sem, recv_sem,
        )
        greet(line.partners() + [(across, None), (twin, None)])
        order = [(zz, flip) for zz in Z_ORDER for flip in (1, 0)]

        def number(zz, flip):
            return zz * NY + (1 - y if flip else y)

        def to_twin(zz, flip):
            b = number(zz, flip)
            return remote(
                part_ref.at[block_rows(b, rows), pl.ds(pl.multiple_of((1 - c) * half, half), half)],
                core_buf.at[b], core_send.at[zz, flip], core_recv.at[zz, flip], twin,
            )

        def to_across(zz, flip):
            b = number(zz, flip)
            return remote(
                core_buf.at[b, :, pl.ds(pl.multiple_of((1 - x) * quarter, quarter), quarter)],
                x_buf.at[b], x_send.at[zz, flip], x_recv.at[zz, flip], across,
            )

        def add_core(zz, flip):
            b = number(zz, flip)

            def store(r):
                at = pl.ds(pl.multiple_of(b * rows + r.start, 16), r.size)
                core_buf[b, r, :] = (
                    core_buf[b, r, :].astype(jnp.float32)
                    + part_ref[at, pl.ds(pl.multiple_of(c * half, half), half)].astype(jnp.float32)
                ).astype(jnp.bfloat16)

            add_into(rows, 32, store)

        def add_across(zz, flip):
            b = number(zz, flip)

            def store(r):
                x_buf[b, r, :] = (
                    x_buf[b, r, :].astype(jnp.float32)
                    + core_buf[b, r, pl.ds(pl.multiple_of(x * quarter, quarter), quarter)].astype(jnp.float32)
                ).astype(jnp.bfloat16)

            add_into(rows, 64, store)

        def stage_twin(i):
            to_twin(*order[i]).wait_recv()
            add_core(*order[i])
            to_across(*order[i]).start()

        def stage_across(i):
            zz, flip = order[i]
            to_across(zz, flip).wait_recv()
            add_across(zz, flip)
            if flip:
                line.to_y(0, zz)

        def stage_y(zz):
            line.along_z(0, zz)

        for zz, flip in order:
            to_twin(zz, flip).start()
        count = len(order)
        for i in range(count + 4):
            if i < count:
                stage_twin(i)
            if 0 <= i - 1 < count:
                stage_across(i - 1)
            if i >= 3 and (i - 3) % 2 == 0 and (i - 3) // 2 < NZ:
                stage_y(Z_ORDER[(i - 3) // 2])

        def done(s, total):
            def store(r):
                out_ref[r, :] = total[r, :]

            add_into(rows, 64, store)

        line.home(done)
        for zz, flip in order:
            to_twin(zz, flip).wait_send()
            to_across(zz, flip).wait_send()
        line.finish()

    return pl.pallas_call(
        kernel,
        out_shape=jax.ShapeDtypeStruct((rows, quarter), jnp.bfloat16),
        in_specs=[VMEM],
        out_specs=VMEM,
        scratch_shapes=[
            pltpu.VMEM((GROUPS, rows, half), jnp.bfloat16),
            pltpu.VMEM((GROUPS, rows, quarter), jnp.bfloat16),
            pltpu.VMEM((NZ, rows, quarter), jnp.bfloat16),
            pltpu.VMEM((NZ, rows, quarter), jnp.bfloat16),
            pltpu.VMEM((NZ, rows, quarter), jnp.bfloat16),
            pltpu.SemaphoreType.DMA((NZ, 2)),
            pltpu.SemaphoreType.DMA((NZ, 2)),
            pltpu.SemaphoreType.DMA((NZ, 2)),
            pltpu.SemaphoreType.DMA((NZ, 2)),
            pltpu.SemaphoreType.DMA((1, NZ, 3)),
            pltpu.SemaphoreType.DMA((1, NZ, 3)),
        ],
        compiler_params=comm_params(collective_id),
        cost_estimate=cost(60),
        name="token_reduce",
    )(part)


def gate_exchange(part, collective_id):
    groups = part.shape[0]
    tensors = NX * NC

    def kernel(part_ref, out_ref, landing, total, send_t, recv_t, send_e, recv_e):
        e = lax.axis_index("expert")
        t = lax.axis_index("tensor")
        mates = [(e, lax.rem(t + k, tensors)) for k in range(1, tensors)]
        peers = [(lax.rem(e + k, groups), t) for k in range(1, groups)]
        greet([(target, None) for target in mates + peers])
        near = [
            remote(part_ref, landing.at[k], send_t.at[k], recv_t.at[k], mates[k])
            for k in range(tensors - 1)
        ]
        for copy in near:
            copy.start()
        for copy in near:
            copy.wait_recv()
        value = part_ref[...]
        for k in range(tensors - 1):
            value = value + landing[k]
        total[...] = value
        far = [
            remote(
                total.at[lax.rem(e + k, groups)], out_ref.at[e], send_e.at[k - 1], recv_e.at[k - 1],
                peers[k - 1],
            )
            for k in range(1, groups)
        ]
        for copy in far:
            copy.start()
        out_ref[e] = total[e]
        for k in range(1, groups):
            source = out_ref.at[lax.rem(e + groups - k, groups)]
            remote(source, source, send_e.at[k - 1], recv_e.at[k - 1], peers[k - 1]).wait_recv()
        for copy in near + far:
            copy.wait_send()

    return pl.pallas_call(
        kernel,
        out_shape=jax.ShapeDtypeStruct(part.shape, jnp.float32),
        in_specs=[VMEM],
        out_specs=VMEM,
        scratch_shapes=[
            pltpu.VMEM((tensors - 1,) + part.shape, jnp.float32),
            pltpu.VMEM(part.shape, jnp.float32),
            pltpu.SemaphoreType.DMA((tensors - 1,)),
            pltpu.SemaphoreType.DMA((tensors - 1,)),
            pltpu.SemaphoreType.DMA((groups - 1,)),
            pltpu.SemaphoreType.DMA((groups - 1,)),
        ],
        compiler_params=comm_params(collective_id, 16),
        cost_estimate=cost(10),
        name="gate_exchange",
    )(part)


def dot(a, b, dims):
    return lax.dot_general(a, b, ((dims[:1], dims[1:]), ((), ())), preferred_element_type=jnp.float32)


def add_to(target, first, second, step=64):
    rows = target.shape[0]

    def body(i, carry):
        r = pl.ds(pl.multiple_of(i * step, step), step)
        total = first[r, :].astype(jnp.float32) + second[r, :].astype(jnp.float32)
        target[r, :] = total.astype(target.dtype)
        return carry

    lax.fori_loop(0, rows // step, body, 0)


def expert_layer(hidden_all, grad_out_all, gate_up, down, router_t, chosen_all, collective_id):
    tokens, width = hidden_all.shape
    rows = tokens // GROUPS
    units = down.shape[0]
    local = 2
    hidden = units // local
    experts = router_t.shape[0]
    half, part, piece = width // 2, width // 4, width // 8
    tensors = NX * NC
    steps = GROUPS + 4
    low = jnp.bfloat16
    wide = width // 4

    def kernel(
        h_in, dy_in, gu_ref, down_ref, router_ref, chosen_ref,
        y_out, dh_out, gates_out, gate_w, up_w, down_w,
        h, dy, gated, dgu, dx, y_stage, gu_stage, d_stage,
        core_buf, px_buf, py_buf, qy_buf, qx_buf, z_sum, lo_buf, hi_buf, gate_part, gate_land,
        in_sem, y_sem, gu_sem, d_sem, core_s, core_r, px_s, px_r, py_s, py_r, qy_s, qy_r, qx_s, qx_r,
        z_s, z_r, near_s, near_r, far_s, far_r, end_s, end_r,
    ):
        z, y, x, c = place()
        e, t = lax.axis_index("expert"), lax.axis_index("tensor")
        across, twin, beside = device(z, y, 1 - x, c), device(z, y, x, 1 - c), device(z, 1 - y, x, c)
        mates = [(e, lax.rem(t + k, tensors)) for k in range(1, tensors)]
        peers = [(lax.rem(e + k, GROUPS), t) for k in range(1, GROUPS)]
        greet([(target, None) for target in mates + peers])

        def zz_of(j):
            return jnp.where(j == 0, 3, jnp.where(j == 1, 0, jnp.where(j == 2, 2, 1)))

        def block_of(i):
            own = lax.rem(i, 2)
            return zz_of(lax.div(i, 2)) * NY + jnp.where(own == 1, y, 1 - y)

        def load(i):
            r = block_rows(block_of(i), rows)
            return (
                pltpu.make_async_copy(h_in.at[r, :], h.at[r, :], in_sem.at[0, i]),
                pltpu.make_async_copy(dy_in.at[r, :], dy.at[r, :], in_sem.at[1, i]),
            )

        def start_load(i, carry):
            for copy in load(i):
                copy.start()
            return carry

        lax.fori_loop(0, GROUPS, start_load, 0)

        def to_twin(i):
            b = block_of(i)
            return remote(
                dx.at[block_rows(b, rows), pl.ds(pl.multiple_of((1 - c) * half, half), half)],
                core_buf.at[b], core_s.at[i], core_r.at[i], twin,
            )

        def p_across(i):
            b = block_of(i)
            return remote(
                core_buf.at[b, :, pl.ds(pl.multiple_of((1 - x) * piece, piece), piece)],
                px_buf.at[b], px_s.at[i], px_r.at[i], across,
            )

        def p_beside(j):
            return remote(px_buf.at[block_of(2 * j)], py_buf.at[j], py_s.at[j], py_r.at[j], beside)

        def q_beside(j):
            return remote(
                core_buf.at[block_of(2 * j), :, pl.ds(part, part)], qy_buf.at[j], qy_s.at[j], qy_r.at[j], beside
            )

        def q_across(j):
            return remote(
                qy_buf.at[j, :, pl.ds(pl.multiple_of((1 - x) * piece, piece), piece)],
                qx_buf.at[j], qx_s.at[j], qx_r.at[j], across,
            )

        def up(j, s):
            return remote(z_sum.at[s, j], lo_buf.at[s, j], z_s.at[0, s, j], z_r.at[0, s, j], device(z + 1, y, x, c))

        def down_z(j, s):
            return remote(z_sum.at[s, j], hi_buf.at[s, j], z_s.at[1, s, j], z_r.at[1, s, j], device(z - 1, y, x, c))

        def take_twin(i):
            to_twin(i).wait_recv()
            b = block_of(i)
            mine = core_buf.at[b]
            add_to(mine, mine, dx.at[block_rows(b, rows), pl.ds(pl.multiple_of(c * half, half), half)], 32)
            p_across(i).start()
            pl.when(lax.rem(i, 2) == 0)(lambda: q_beside(lax.div(i, 2)).start())

        def take_p_across(i):
            p_across(i).wait_recv()
            b = block_of(i)
            add_to(
                px_buf.at[b], px_buf.at[b],
                core_buf.at[b, :, pl.ds(pl.multiple_of(x * piece, piece), piece)],
            )

        def take_q_beside(j):
            q_beside(j).wait_recv()
            add_to(qy_buf.at[j], qy_buf.at[j], core_buf.at[block_of(2 * j + 1), :, pl.ds(part, part)])
            q_across(j).start()

        def take_q_across(j):
            q_across(j).wait_recv()
            add_to(
                z_sum.at[1, j], qx_buf.at[j], qy_buf.at[j, :, pl.ds(pl.multiple_of(x * piece, piece), piece)]
            )

        def take_p_beside(j):
            p_beside(j).wait_recv()
            add_to(z_sum.at[0, j], py_buf.at[j], px_buf.at[block_of(2 * j + 1)])

        def hop(j, k):
            zz = zz_of(j)

            def upward():
                for s in range(2):
                    if k > 0:
                        up(j, s).wait_recv()
                        add_to(z_sum.at[s, j], z_sum.at[s, j], lo_buf.at[s, j])
                    up(j, s).start()

            def downward():
                for s in range(2):
                    if k > 0:
                        down_z(j, s).wait_recv()
                        add_to(z_sum.at[s, j], z_sum.at[s, j], hi_buf.at[s, j])
                    down_z(j, s).start()

            pl.when((z < zz) & (z == k))(upward)
            pl.when((z > zz) & (NZ - 1 - z == k))(downward)

        def front(i):
            for copy in load(i):
                copy.wait()
            b = block_of(i)
            r = block_rows(b, rows)
            rows_h, rows_dy = h[r, :], dy[r, :]
            logits = dot(rows_h, router_ref[...], (1, 1))
            shifted = jnp.exp(logits - jnp.max(logits, axis=-1, keepdims=True))
            probs = shifted / jnp.sum(shifted, axis=-1, keepdims=True) * chosen_ref[r, :]
            lane = lax.broadcasted_iota(jnp.int32, probs.shape, 1)
            line = lax.broadcasted_iota(jnp.int32, (rows, 128), 1)
            found = jnp.zeros((rows, 128), jnp.float32)
            for expert in range(local):
                at, up_at = pl.ds(expert * hidden, hidden), pl.ds((local + expert) * hidden, hidden)
                gate = jnp.sum(jnp.where(lane == e * local + expert, probs, 0.0), axis=-1, keepdims=True)
                pre = dot(rows_h, gu_ref[:, at], (1, 0))
                scale = dot(rows_h, gu_ref[:, up_at], (1, 0))
                back = dot(rows_dy, down_ref[at, :], (1, 1))
                sigmoid = jax.nn.sigmoid(pre)
                swish = pre * sigmoid
                active = swish * scale
                gated[r, at] = (active * gate).astype(low)
                found = jnp.where(line == expert, jnp.sum(active * back, axis=-1, keepdims=True), found)
                back = back * gate
                dgu[r, at] = (back * scale * sigmoid * (1.0 + pre * (1.0 - sigmoid))).astype(low)
                dgu[r, up_at] = (back * swish).astype(low)
            gate_part[b] = jnp.transpose(found)[:8, :]

        def y_copy(i):
            return pltpu.make_async_copy(
                y_stage.at[lax.rem(i, 2)], y_out.at[block_rows(block_of(i), rows), :], y_sem.at[lax.rem(i, 2)]
            )

        def rear(i):
            r = block_rows(block_of(i), rows)
            slot = lax.rem(i, 2)

            def columns(k, carry):
                at = pl.ds(pl.multiple_of(k * wide, wide), wide)
                dx[r, at] = dot(dgu[r, :], gu_ref[at, :], (1, 1)).astype(low)
                return carry

            lax.fori_loop(0, width // wide, columns, 0)
            to_twin(i).start()
            pl.when(i >= 2)(lambda: y_copy(i - 2).wait())

            def y_columns(k, carry):
                at = pl.ds(pl.multiple_of(k * wide, wide), wide)
                y_stage[slot, :, at] = dot(gated[r, :], down_ref[:, at], (1, 0)).astype(low)
                return carry

            lax.fori_loop(0, width // wide, y_columns, 0)
            y_copy(i).start()

        tiles = width // piece // 4
        d_width = width // 4

        def gu_copies(n):
            slot = lax.rem(n, 2)
            at = pl.ds(pl.multiple_of(n * piece, piece), piece)
            return [
                pltpu.make_async_copy(
                    gu_stage.at[slot, :, pl.ds(k * hidden, hidden)],
                    (gate_w if k < local else up_w).at[k % local, at, :],
                    gu_sem.at[slot, k],
                )
                for k in range(2 * local)
            ]

        def d_copies(n):
            slot = lax.rem(n, 2)
            at = pl.ds(pl.multiple_of(n * d_width, d_width), d_width)
            return [
                pltpu.make_async_copy(
                    d_stage.at[slot, pl.ds(k * hidden, hidden), :], down_w.at[k, :, at], d_sem.at[slot, k]
                )
                for k in range(local)
            ]

        def each(copies, what):
            for copy in copies:
                getattr(copy, what)()

        def weight_grads(q):
            def tile(k, carry):
                n = q * tiles + k
                pl.when(n >= 2)(lambda: each(gu_copies(n - 2), "wait"))
                at = pl.ds(pl.multiple_of(n * piece, piece), piece)
                gu_stage[lax.rem(n, 2)] = dot(h[:, at], dgu[...], (0, 0))
                each(gu_copies(n), "start")
                return carry

            lax.fori_loop(0, tiles, tile, 0)
            pl.when(q >= 2)(lambda: each(d_copies(q - 2), "wait"))
            at = pl.ds(pl.multiple_of(q * d_width, d_width), d_width)
            d_stage[lax.rem(q, 2)] = dot(gated[...], dy[:, at], (0, 0))
            each(d_copies(q), "start")

        near = [
            remote(gate_part, gate_land.at[k], near_s.at[k], near_r.at[k], mates[k])
            for k in range(tensors - 1)
        ]

        def far(k):
            return remote(
                gate_land.at[tensors - 1, lax.rem(e + k, GROUPS)], gates_out.at[e],
                far_s.at[k - 1], far_r.at[k - 1], peers[k - 1],
            )

        def sum_near():
            for copy in near:
                copy.wait_recv()
            total = gate_part[...]
            for k in range(tensors - 1):
                total = total + gate_land[k]
            gate_land[tensors - 1] = total
            for k in range(1, GROUPS):
                far(k).start()
            gates_out[e] = gate_land[tensors - 1, e]

        def step(i, carry):
            j_even, j_odd = lax.div(i, 2) - 1, lax.div(i - 1, 2) - 1
            even = lax.rem(i, 2) == 0
            pl.when(i < GROUPS)(lambda: front(i))
            pl.when((i >= 1) & (i <= GROUPS))(lambda: take_twin(i - 1))
            pl.when(even & (i >= 2) & (i <= GROUPS))(lambda: take_q_beside(j_even))

            def late():
                take_p_across(i - 2)
                take_q_across(j_odd)

            pl.when((lax.rem(i, 2) == 1) & (i >= 3) & (i <= GROUPS + 1))(late)
            pl.when(i == GROUPS)(lambda: each(near, "start"))
            pl.when(i == GROUPS + 1)(sum_near)
            pl.when(i < GROUPS)(lambda: rear(i))
            pl.when(i >= GROUPS)(lambda: weight_grads(i - GROUPS))

            def pass_p():
                take_p_across(i - 2)
                p_beside(j_even).start()

            pl.when(even & (i >= 2) & (i <= GROUPS))(pass_p)

            def join():
                take_p_beside(j_odd)
                hop(j_odd, 0)

            pl.when((lax.rem(i, 2) == 1) & (i >= 3) & (i <= GROUPS + 1))(join)
            pl.when(even & (i >= 4) & (i <= GROUPS + 2))(lambda: hop(j_even - 1, 1))
            pl.when((lax.rem(i, 2) == 1) & (i >= 5) & (i <= GROUPS + 3))(lambda: hop(j_odd - 1, 2))
            return carry

        lax.fori_loop(0, steps, step, 0)

        def columns_of(s, xx, cc):
            return pl.ds(pl.multiple_of(cc * half + s * part + xx * piece, piece), piece)

        mine = jnp.where(z == 3, 0, jnp.where(z == 0, 1, jnp.where(z == 2, 2, 3)))
        for s in range(2):
            def below(s=s):
                up(mine, s).wait_recv()
                add_to(z_sum.at[s, mine], z_sum.at[s, mine], lo_buf.at[s, mine])

            def above(s=s):
                down_z(mine, s).wait_recv()
                add_to(z_sum.at[s, mine], z_sum.at[s, mine], hi_buf.at[s, mine])

            pl.when(z > 0)(below)
            pl.when(z < NZ - 1)(above)
            own = dh_out.at[:, columns_of(s, x, c)]

            def keep(k, carry, s=s, own=own):
                r = pl.ds(pl.multiple_of(k * 64, 64), 64)
                own[r, :] = z_sum[s, mine, r, :]
                return carry

            lax.fori_loop(0, rows // 64, keep, 0)
            remote(own, own, end_s.at[0, s], end_r.at[0, s], across).start()
            remote(own, own, end_s.at[1, s], end_r.at[1, s], twin).start()
        for s in range(2):
            there = dh_out.at[:, columns_of(s, 1 - x, c)]
            remote(there, there, end_s.at[0, s], end_r.at[0, s], across).wait_recv()
            remote(there, there, end_s.at[2, s], end_r.at[2, s], twin).start()
        for s in range(2):
            for k, xx in ((1, x), (2, 1 - x)):
                there = dh_out.at[:, columns_of(s, xx, 1 - c)]
                remote(there, there, end_s.at[k, s], end_r.at[k, s], twin).wait_recv()
            for k, target in ((0, across), (1, twin), (2, twin)):
                there = dh_out.at[:, columns_of(s, 1 - x if k == 2 else x, c)]
                remote(there, there, end_s.at[k, s], end_r.at[k, s], target).wait_send()
        for k in range(1, GROUPS):
            there = gates_out.at[lax.rem(e + GROUPS - k, GROUPS)]
            remote(there, there, far_s.at[k - 1], far_r.at[k - 1], peers[k - 1]).wait_recv()
            far(k).wait_send()
        each(near, "wait_send")

        def drain(i, carry):
            to_twin(i).wait_send()
            p_across(i).wait_send()
            return carry

        lax.fori_loop(0, GROUPS, drain, 0)

        def drain_pair(j, carry):
            p_beside(j).wait_send()
            q_beside(j).wait_send()
            q_across(j).wait_send()
            for s in range(2):
                pl.when(z < zz_of(j))(lambda s=s: up(j, s).wait_send())
                pl.when(z > zz_of(j))(lambda s=s: down_z(j, s).wait_send())
            return carry

        lax.fori_loop(0, NZ, drain_pair, 0)
        for k in range(2):
            y_copy(GROUPS - 2 + k).wait()
            each(gu_copies(4 * tiles - 2 + k), "wait")
            each(d_copies(2 + k), "wait")

    shape = jax.ShapeDtypeStruct
    dma = pltpu.SemaphoreType.DMA
    f32 = jnp.float32
    return pl.pallas_call(
        kernel,
        out_shape=(
            shape((tokens, width), low),
            shape((rows, width), low),
            shape((GROUPS, 8, rows), f32),
            shape((local, width, hidden), f32),
            shape((local, width, hidden), f32),
            shape((local, hidden, width), f32),
        ),
        in_specs=[HBM, HBM, VMEM, VMEM, VMEM, VMEM],
        out_specs=(HBM, VMEM, VMEM, HBM, HBM, HBM),
        scratch_shapes=[
            pltpu.VMEM((tokens, width), low),
            pltpu.VMEM((tokens, width), low),
            pltpu.VMEM((tokens, units), low),
            pltpu.VMEM((tokens, 2 * units), low),
            pltpu.VMEM((tokens, width), low),
            pltpu.VMEM((2, rows, width), low),
            pltpu.VMEM((2, piece, 2 * units), f32),
            pltpu.VMEM((2, units, width // 4), f32),
            pltpu.VMEM((GROUPS, rows, half), low),
            pltpu.VMEM((GROUPS, rows, piece), low),
            pltpu.VMEM((NZ, rows, piece), low),
            pltpu.VMEM((NZ, rows, part), low),
            pltpu.VMEM((NZ, rows, piece), low),
            pltpu.VMEM((2, NZ, rows, piece), low),
            pltpu.VMEM((2, NZ, rows, piece), low),
            pltpu.VMEM((2, NZ, rows, piece), low),
            pltpu.VMEM((GROUPS, 8, rows), f32),
            pltpu.VMEM((tensors, GROUPS, 8, rows), f32),
            dma((2, GROUPS)), dma((2,)), dma((2, 2 * local)), dma((2, local)),
            dma((GROUPS,)), dma((GROUPS,)), dma((GROUPS,)), dma((GROUPS,)),
            dma((NZ,)), dma((NZ,)), dma((NZ,)), dma((NZ,)), dma((NZ,)), dma((NZ,)),
            dma((2, 2, NZ)), dma((2, 2, NZ)),
            dma((tensors - 1,)), dma((tensors - 1,)), dma((GROUPS - 1,)), dma((GROUPS - 1,)),
            dma((3, 2)), dma((3, 2)),
        ],
        compiler_params=comm_params(collective_id, 62),
        cost_estimate=cost(80),
        name="expert_layer",
    )(hidden_all, grad_out_all, gate_up, down, router_t, chosen_all)


def exchange_rows(value, part_ref, land_ref, send_sem, recv_sem, mates):
    rows = value.shape[0]
    line = lax.broadcasted_iota(jnp.int32, (rows, 128), 1)
    part_ref[...] = jnp.transpose(jnp.where(line == 0, value, 0.0))[:8, :]
    for k, mate in enumerate(mates):
        remote(part_ref, land_ref.at[k], send_sem.at[k], recv_sem.at[k], mate).start()


def exchanged_rows(part_ref, land_ref, send_sem, recv_sem, mates):
    total = part_ref[...]
    for k, mate in enumerate(mates):
        remote(part_ref, land_ref.at[k], send_sem.at[k], recv_sem.at[k], mate).wait_recv()
    for k in range(len(mates)):
        total = total + land_ref[k]
    rows = part_ref.shape[1]
    tall = jnp.concatenate([total, jnp.zeros((120, rows), jnp.float32)], axis=0)
    return jnp.transpose(tall)[:, :1]


def drain_rows(part_ref, land_ref, send_sem, recv_sem, mates):
    for k, mate in enumerate(mates):
        remote(part_ref, land_ref.at[k], send_sem.at[k], recv_sem.at[k], mate).wait_send()


def turn(value, cosine, sine):
    return value * cosine + pltpu.roll(value, HEAD // 2, 1) * sine


def project(tokens, w_qkv, smalls, cosine, sine, collective_id):
    rows, width = tokens.shape
    parts, depth, columns = w_qkv.shape
    heads = columns // HEAD
    tensors = NX * NC
    back = WINDOW // rows
    low, f32 = jnp.bfloat16, jnp.float32
    QUERY, KEY, VALUE, SMALL = 0, 1, 2, 3

    def kernel(
        tok_ref, w_ref, small_ref, cos_ref, sin_ref,
        w_all, small_all, h1_ref, raw_ref, scale_ref, q_ref, context,
        own_w, weights, total, part_k, land_k, part_q, land_q,
        send_sem, recv_sem, out_sem, small_sem, ks_s, ks_r, qs_s, qs_r, c_s, c_r,
    ):
        z, y, x, c = place()
        e, t = lax.axis_index("expert"), lax.axis_index("tensor")
        mates = [(e, lax.rem(t + k, tensors)) for k in range(1, tensors)]
        beside, above = device(z, 1 - y, x, c), device(z + 1, y, x, c)
        views = [
            lambda b: weights.at[QUERY, block_rows(b, depth), :],
            lambda b: weights.at[KEY, block_rows(b, depth), :],
            lambda b: weights.at[VALUE, block_rows(b, depth), :],
            lambda b: small_all.at[b],
        ]
        line = LineGather(
            [SMALL, VALUE, KEY, QUERY], [own_w.at[0], own_w.at[1], own_w.at[2], small_ref], views,
            send_sem, recv_sem,
        )
        greet(line.partners() + [(mate, None) for mate in mates])
        line.start(SMALL, 0)
        for part in (VALUE, KEY, QUERY):
            def cast(i, carry, part=part):
                r = pl.ds(pl.multiple_of(i * 32, 32), 32)
                own_w[part, r, :] = w_ref[part, r, :].astype(low)
                return carry

            lax.fori_loop(0, depth // 32, cast, 0)
            if part != QUERY:
                line.start(part, 0)

        def square(i, carry):
            r = pl.ds(pl.multiple_of(i * 32, 32), 32)
            value = tok_ref[r, :].astype(f32)
            scale_ref[r, 0:1] = lax.rsqrt(jnp.mean(value * value, axis=-1, keepdims=True) + EPS)
            return carry

        lax.fori_loop(0, rows // 32, square, 0)
        total[...] = jnp.zeros_like(total)
        own_small = pltpu.make_async_copy(small_ref, small_all.at[line.block(0)], small_sem)
        own_small.start()

        def use(stream, rel):
            b = line.block(rel)
            at = pl.ds(pl.multiple_of(b * depth, depth), depth)
            if stream == SMALL:
                gain = small_ref[0:1, :] if rel == 0 else small_all[b, 0:1, :]
                h1_ref[:, at] = (tok_ref[:, at].astype(f32) * scale_ref[:, 0:1] * gain).astype(low)
                return
            block = own_w[stream] if rel == 0 else weights[stream, block_rows(b, depth), :]
            total[stream] += dot(h1_ref[:, at], block, (1, 0))

        def event(stream, rel):
            def body():
                line.arrive(stream, rel)
                if rel < 7:
                    marks = len(line.pending)
                    line.start(stream, rel)
                    late = line.pending[marks:]
                    del line.pending[marks:]
                    line.finish_later(late, rel)
                use(stream, rel)
            run_if(line.exists(rel), body)

        use(SMALL, 0)
        use(VALUE, 0)
        own_small.wait()
        use(KEY, 0)
        early, late = [7, 1, 4, 8, 11, 2, 5], [9, 12, 3, 6, 10, 13]
        for rel in early:
            event(SMALL, rel)
            event(VALUE, rel)
        line.start(QUERY, 0)
        for rel in late:
            event(SMALL, rel)
            event(VALUE, rel)

        def context_copy(which, k):
            if k == 2:
                source, target = 0, above
            elif k == 4:
                source, target = 2, above
            else:
                source, target = jnp.where(y == 0, k - 1, k + 1), beside
            return remote(
                context.at[source, which], context.at[k, which], c_s.at[which, k], c_r.at[which, k], target
            )

        sends = {2: z < NZ - 1, 4: (z >= 1) & (z < NZ - 1), 1: (y == 0) | (z >= 1), 3: z >= 1 + y}
        takes = {2: z >= 1, 4: z >= 2, 1: (y == 1) | (z >= 1), 3: z >= 2 - y}

        def context_send(which, k):
            run_if(sends[k], lambda: context_copy(which, k).start())

        def context_take(which, k):
            run_if(takes[k], lambda: context_copy(which, k).wait_recv())

        for k in range(1, back + 1):
            def clear(k=k):
                context[k] = jnp.zeros_like(context[k])
            run_if(jnp.logical_not(takes[k]), clear)

        context[0, 1] = total[VALUE].astype(low)
        context_send(1, 2)
        run_if(y == 0, lambda: context_copy(1, 1).start())
        for rel in early:
            event(KEY, rel)
        for rel in late:
            event(KEY, rel)
        key_raw = total[KEY]
        raw_ref[1] = key_raw
        exchange_rows(jnp.sum(key_raw * key_raw, axis=-1, keepdims=True), part_k, land_k, ks_s, ks_r, mates)
        use(QUERY, 0)
        for rel in early[:3]:
            event(QUERY, rel)

        key_scale = lax.rsqrt(exchanged_rows(part_k, land_k, ks_s, ks_r, mates) / width + EPS)
        scale_ref[:, 2:3] = key_scale
        slices = HEAD // GROUPS
        gains = []
        for which in range(2):
            per_head = []
            for head in range(heads):
                start = (which * heads + head) * slices
                per_head.append(
                    jnp.concatenate([small_all[b, 2:3, start : start + slices] for b in range(GROUPS)], axis=1)
                )
            gains.append(per_head)

        def rotated(which, scale, store):
            for head in range(heads):
                at = pl.ds(head * HEAD, HEAD)
                value = total[which, :, at] * scale * gains[which][head]
                store(at, turn(value, cos_ref[...], sin_ref[...]).astype(low))

        def store_key(at, value):
            context[0, 0, :, at] = value

        rotated(KEY, key_scale, store_key)
        context_send(0, 2)
        run_if(y == 0, lambda: context_copy(0, 1).start())

        def relay_two(which):
            context_take(which, 2)
            context_send(which, 4)
            run_if((y == 1) & (z >= 1), lambda: context_copy(which, 1).start())
            run_if((y == 0) & sends[3], lambda: context_copy(which, 3).start())

        def relay_four(which):
            context_take(which, 4)
            run_if((y == 1) & sends[3], lambda: context_copy(which, 3).start())

        relay_two(1)
        for rel in early[3:]:
            event(QUERY, rel)
        relay_four(1)
        for rel in late[:4]:
            event(QUERY, rel)
        relay_two(0)
        for rel in late[4:]:
            event(QUERY, rel)
        query_raw = total[QUERY]
        raw_ref[0] = query_raw
        exchange_rows(jnp.sum(query_raw * query_raw, axis=-1, keepdims=True), part_q, land_q, qs_s, qs_r, mates)
        for part in range(parts):
            weights[part, block_rows(line.block(0), depth), :] = own_w[part]
        keep = pltpu.make_async_copy(weights, w_all, out_sem)
        keep.start()
        relay_four(0)
        query_scale = lax.rsqrt(exchanged_rows(part_q, land_q, qs_s, qs_r, mates) / width + EPS)
        scale_ref[:, 1:2] = query_scale

        def store_query(at, value):
            q_ref[:, at] = value

        rotated(QUERY, query_scale, store_query)
        for which in (1, 0):
            for k in (1, 3):
                context_take(which, k)
        line.finish()
        for which in range(2):
            for k in range(1, back + 1):
                run_if(sends[k], lambda which=which, k=k: context_copy(which, k).wait_send())
        drain_rows(part_k, land_k, ks_s, ks_r, mates)
        drain_rows(part_q, land_q, qs_s, qs_r, mates)
        keep.wait()

    shape, dma = jax.ShapeDtypeStruct, pltpu.SemaphoreType.DMA
    return pl.pallas_call(
        kernel,
        out_shape=(
            shape((parts, depth * GROUPS, columns), low),
            shape((GROUPS,) + smalls.shape, f32),
            shape((rows, width), low),
            shape((2, rows, columns), f32),
            shape((rows, 128), f32),
            shape((rows, columns), low),
            shape((back + 1, 2, rows, columns), low),
        ),
        in_specs=[VMEM] * 5,
        out_specs=(HBM,) + (VMEM,) * 6,
        scratch_shapes=[
            pltpu.VMEM((parts, depth, columns), low),
            pltpu.VMEM((parts, depth * GROUPS, columns), low),
            pltpu.VMEM((parts, rows, columns), f32),
            pltpu.VMEM((8, rows), f32),
            pltpu.VMEM((tensors - 1, 8, rows), f32),
            pltpu.VMEM((8, rows), f32),
            pltpu.VMEM((tensors - 1, 8, rows), f32),
            dma((4, 7, 3)), dma((4, 14)), dma, dma,
            dma((tensors - 1,)), dma((tensors - 1,)), dma((tensors - 1,)), dma((tensors - 1,)),
            dma((2, back + 1)), dma((2, back + 1)),
        ],
        compiler_params=comm_params(collective_id, 48),
        cost_estimate=cost(100),
        name="project",
    )(tokens, w_qkv, smalls, cosine, sine)


def attend(query, context, segment_query, segment_keys, tokens, out_low, gain, collective_id):
    rows, columns = query.shape
    width = tokens.shape[1]
    blocks = context.shape[0]
    heads = columns // HEAD
    half, quarter = width // 2, width // 4
    low, f32 = jnp.bfloat16, jnp.float32

    def kernel(
        q_ref, context_ref, sq_ref, sk_ref, tok_ref, out_ref, gain_ref,
        o_ref, lse_ref, x1_ref, h2_ref, scale_ref,
        part, full, core_buf, x_buf, send_sem, recv_sem,
    ):
        z, y, x, c = place()
        across, twin = device(z, y, 1 - x, c), device(z, y, x, 1 - c)
        greet([(across, None), (twin, None)])
        row = lax.broadcasted_iota(jnp.int32, (rows, rows), 0)
        column = lax.broadcasted_iota(jnp.int32, (rows, rows), 1)
        allowed = []
        for k in range(blocks):
            distance = row - column + k * rows
            allowed.append(
                (sq_ref[...] == sk_ref[k : k + 1, :]) & (distance >= 0) & (distance < WINDOW)
            )
        line = lax.broadcasted_iota(jnp.int32, (rows, 128), 1)
        lse = jnp.zeros((rows, 128), f32)
        for head in range(heads):
            at = pl.ds(head * HEAD, HEAD)
            scores = [
                jnp.where(
                    allowed[k], dot(q_ref[:, at], context_ref[k, 0, :, at], (1, 1)) * HEAD ** (-0.5), -1e30
                )
                for k in range(blocks)
            ]
            largest = scores[0]
            for k in range(1, blocks):
                largest = jnp.maximum(largest, scores[k])
            largest = jnp.max(largest, axis=-1, keepdims=True)
            weights = [jnp.exp(s - largest) for s in scores]
            amount = weights[0]
            for k in range(1, blocks):
                amount = amount + weights[k]
            amount = jnp.sum(amount, axis=-1, keepdims=True)
            inverse = 1.0 / amount
            value = jnp.zeros((rows, HEAD), f32)
            for k in range(blocks):
                value = value + dot((weights[k] * inverse).astype(low), context_ref[k, 1, :, at], (1, 0))
            o_ref[:, at] = value.astype(low)
            lse = jnp.where(line == head, largest + jnp.log(amount), lse)
        lse_ref[...] = lse

        def half_of(cc):
            return pl.ds(pl.multiple_of(cc * half, half), half)

        def fill(cc):
            def body(k, carry):
                at = pl.ds(pl.multiple_of(cc * half + k * quarter, quarter), quarter)
                part[:, at] = dot(o_ref[...], out_ref[:, at], (1, 0)).astype(low)
                return carry

            lax.fori_loop(0, 2, body, 0)

        fill(1 - c)
        group_sum(part, full, core_buf, x_buf, send_sem, recv_sem, lambda: fill(c))

        def norm(i, carry):
            r = pl.ds(pl.multiple_of(i * 32, 32), 32)
            value = tok_ref[r, :].astype(f32) + full[r, :].astype(f32)
            scale = lax.rsqrt(jnp.mean(value * value, axis=-1, keepdims=True) + EPS)
            x1_ref[r, :] = value
            scale_ref[r, :] = jnp.broadcast_to(scale, (32, 128))
            h2_ref[r, :] = (value * scale * gain_ref[...]).astype(low)
            return carry

        lax.fori_loop(0, rows // 32, norm, 0)

    shape, dma = jax.ShapeDtypeStruct, pltpu.SemaphoreType.DMA
    return pl.pallas_call(
        kernel,
        out_shape=(
            shape((rows, columns), low),
            shape((rows, 128), f32),
            shape((rows, width), f32),
            shape((rows, width), low),
            shape((rows, 128), f32),
        ),
        in_specs=[VMEM] * 7,
        out_specs=(VMEM,) * 5,
        scratch_shapes=[
            pltpu.VMEM((rows, width), low),
            pltpu.VMEM((rows, width), low),
            pltpu.VMEM((rows, half), low),
            pltpu.VMEM((rows, quarter), low),
            dma((5,)), dma((5,)),
        ],
        compiler_params=comm_params(collective_id, 40),
        cost_estimate=cost(40),
        name="attend",
    )(query, context, segment_query, segment_keys, tokens, out_low, gain)


def fast_shards(
    tokens_in,
    out_grad,
    w_qkv,
    w_attn_out,
    attn_gain,
    ffn_gain,
    qk_gain,
    w_router,
    w_gate,
    w_up,
    w_down,
    routes,
    segments,
):
    row_count, model_width = tokens_in.shape
    experts = w_router.shape[1]
    local_experts = w_gate.shape[0]
    heads_here = qk_gain.shape[1]
    local_width = heads_here * HEAD
    groups = lax.axis_size("expert")
    device_index = lax.axis_index("expert")
    tensor_index = lax.axis_index("tensor")
    quarter = model_width // lax.axis_size("tensor")
    hop_count = WINDOW // row_count
    score_scale = HEAD ** (-0.5)
    low = jnp.bfloat16

    chosen = jnp.any(
        routes[:, :, None] == jnp.arange(experts, dtype=jnp.int32)[None, None, :], axis=1
    ).astype(jnp.float32)
    qk_row = qk_gain.reshape(1, -1)

    def rounded(v):
        return lax.reduce_precision(v, 8, 7)

    smalls = jnp.concatenate(
        [
            rounded(attn_gain)[None, :],
            rounded(ffn_gain)[None, :],
            jnp.pad(rounded(qk_row), ((0, 0), (0, row_count - qk_row.shape[1]))),
            jnp.zeros((5, row_count), jnp.float32),
            w_router.T,
            chosen.T,
        ],
        axis=0,
    )
    global_rows = device_index * row_count + jnp.arange(row_count, dtype=jnp.int32)
    cosine_table, sine_table = angles(global_rows % SEQ, HEAD)
    wide_cosine = jnp.concatenate([cosine_table[:, 0], cosine_table[:, 0]], axis=1)
    wide_sine = jnp.concatenate([-sine_table[:, 0], sine_table[:, 0]], axis=1)
    grad_out_piece = lax.dynamic_slice_in_dim(out_grad, tensor_index * quarter, quarter, axis=1)
    grad_out_rows = lax.all_gather(grad_out_piece, "expert", axis=0, tiled=True)
    out_low = lax.all_gather(w_attn_out.astype(low), "expert", axis=1, tiled=True)
    qkv_low, small_all, hidden_one, raw, scales, query_low, context_blocks = project(
        tokens_in, w_qkv, smalls, wide_cosine, wide_sine, 0
    )
    grad_out_rows, query_low = lax.optimization_barrier((grad_out_rows, query_low))
    grad_out_all = lax.all_gather(grad_out_rows, "tensor", axis=1, tiled=True)
    gain_one_f = small_all[:, 0].reshape(model_width)
    gain_two_f = small_all[:, 1].reshape(model_width)
    qk_gains = (
        small_all[:, 2, : qk_row.shape[1]]
        .reshape(groups, 2, heads_here, HEAD // groups)
        .transpose(1, 2, 0, 3)
        .reshape(2, local_width)
    )
    router_t = small_all[:, 8 : 8 + experts].transpose(1, 0, 2).reshape(experts, model_width).astype(low)
    chosen_all = small_all[:, 8 + experts : 8 + 2 * experts].transpose(0, 2, 1).reshape(
        groups * row_count, experts
    )
    segment_window = lax.dynamic_slice_in_dim(
        jnp.concatenate([jnp.full((WINDOW,), -1, jnp.int32), segments]),
        device_index * row_count, (hop_count + 1) * row_count,
    )
    segment_query = segment_window[WINDOW:]
    segment_keys = segment_window.reshape(hop_count + 1, row_count)[::-1]
    attended, log_sums, residual, hidden_two, scale_two_wide = attend(
        query_low, context_blocks, segment_query[:, None], segment_keys, tokens_in, out_low,
        gain_two_f[None, :], 2,
    )
    scale_one, query_scale, key_scale = scales[:, 0:1], scales[:, 1:2], scales[:, 2:3]
    scale_two = scale_two_wide[:, :1]
    tokens_f = tokens_in.astype(jnp.float32)
    query_raw, key_raw = raw[0], raw[1]
    normed_query = query_raw * query_scale
    normed_key = key_raw * key_scale
    normed_two = residual * scale_two
    query_low = query_low.reshape(row_count, heads_here, HEAD)
    context = (
        context_blocks[::-1].transpose(1, 0, 2, 3).reshape(2, -1, heads_here, HEAD)
    )
    key_rows = (device_index - hop_count) * row_count + jnp.arange(
        (hop_count + 1) * row_count, dtype=jnp.int32
    )
    distance = global_rows[:, None] - key_rows[None, :]
    allowed = (
        (segment_query[:, None] == segment_window[None, :]) & (distance >= 0) & (distance < WINDOW)
    )
    log_total = log_sums[:, :heads_here].T[:, :, None]

    def score_block():
        raw_scores = (
            jnp.einsum("qhd,khd->hqk", query_low, context[0], preferred_element_type=jnp.float32)
            * score_scale
        )
        return jnp.where(allowed[None], raw_scores, -1e30)

    hidden_all = token_gather(hidden_two, 3)
    contract_last = (((1,), (1,)), ((), ()))

    def router(rows):
        logits = lax.dot_general(rows, router_t, contract_last, preferred_element_type=jnp.float32)
        logit_exp = jnp.exp(logits - jnp.max(logits, axis=-1, keepdims=True))
        return logit_exp / jnp.sum(logit_exp, axis=-1, keepdims=True)

    gate_up = jnp.concatenate(
        [w[i] for w in (w_gate, w_up) for i in range(local_experts)], axis=1
    ).astype(low)
    down_low = w_down.reshape(-1, model_width).astype(low)
    expert_part, grad_hidden_sum, grad_gate_sum, grad_gate_w, grad_up_w, grad_down = expert_layer(
        hidden_all, grad_out_all, gate_up, down_low, router_t, chosen_all, 5
    )
    expert_quarter = token_reduce(expert_part, 6)
    grad_probs = (
        grad_gate_sum[:, :local_experts].reshape(experts, row_count).T * chosen
    )
    grad_hidden_sum = grad_hidden_sum.astype(jnp.float32)
    expert_pieces = lax.all_gather(expert_quarter, "tensor", axis=0)
    block_out = residual + jnp.concatenate(
        [expert_pieces[i] for i in (0, 2, 1, 3)], axis=1
    ).astype(jnp.float32)
    router_probs = router(hidden_two)
    grad_logits = (
        router_probs * (grad_probs - jnp.sum(router_probs * grad_probs, axis=-1, keepdims=True))
    ).astype(low)
    grad_out = out_grad.astype(jnp.float32)
    grad_hidden_two = grad_hidden_sum + jnp.dot(
        grad_logits, router_t, preferred_element_type=jnp.float32
    )
    grad_router_t = lax.dot_general(
        grad_logits, hidden_two, (((0,), (0,)), ((), ())), preferred_element_type=jnp.float32
    )
    grad_gain_two = jnp.sum(grad_hidden_two * normed_two, axis=0)
    scaled_two = grad_hidden_two * gain_two_f
    grad_residual = (
        grad_out
        + scale_two * scaled_two
        - residual
        * (scale_two * scale_two * scale_two)
        * jnp.mean(scaled_two * residual, axis=-1, keepdims=True)
    )
    grad_attn = grad_residual.astype(low)
    grad_out_w = jnp.dot(attended.T, grad_attn, preferred_element_type=jnp.float32)
    grad_attended = (
        lax.dot_general(grad_attn, out_low, contract_last, preferred_element_type=jnp.float32)
        .astype(low)
        .reshape(row_count, heads_here, HEAD)
    )
    attn_weights = jnp.where(allowed[None], jnp.exp(score_block() - log_total), 0.0)
    grad_weights = jnp.einsum(
        "qhd,khd->hqk", grad_attended, context[1], preferred_element_type=jnp.float32
    )
    inner_sum = jnp.sum(attn_weights * grad_weights, axis=-1, keepdims=True)
    grad_scores = (attn_weights * (grad_weights - inner_sum) * score_scale).astype(low)
    grad_query = jnp.einsum(
        "hqk,khd->qhd", grad_scores, context[0], preferred_element_type=jnp.float32
    )
    grad_keys = jnp.einsum(
        "hqk,qhd->khd", grad_scores, query_low, preferred_element_type=jnp.float32
    )
    grad_values = jnp.einsum(
        "hqk,qhd->khd", attn_weights.astype(low), grad_attended, preferred_element_type=jnp.float32
    )
    grad_pair = jnp.stack([grad_keys, grad_values]).reshape(
        2, hop_count + 1, row_count, heads_here, HEAD
    )
    own_grad = grad_pair[:, hop_count]
    for steps_back in range(1, hop_count + 1):
        own_grad = own_grad + from_behind(
            grad_pair[:, hop_count - steps_back].astype(low), "expert", -steps_back
        ).astype(jnp.float32)
    grad_query_norm = rotate(grad_query, cosine_table, -sine_table).reshape(row_count, local_width)
    grad_key_norm = rotate(own_grad[0], cosine_table, -sine_table).reshape(row_count, local_width)
    grad_gain_query = jnp.sum(grad_query_norm * normed_query, axis=0)
    grad_gain_key = jnp.sum(grad_key_norm * normed_key, axis=0)
    scaled_query = grad_query_norm * qk_gains[0]
    scaled_key = grad_key_norm * qk_gains[1]
    query_inner, key_inner = lax.psum(
        (jnp.sum(scaled_query * query_raw, axis=-1), jnp.sum(scaled_key * key_raw, axis=-1)),
        "tensor",
    )
    grad_query_raw = (
        query_scale * scaled_query
        - query_raw * (query_scale * query_scale * query_scale) * query_inner[:, None] / model_width
    ).astype(low)
    grad_key_raw = (
        key_scale * scaled_key
        - key_raw * (key_scale * key_scale * key_scale) * key_inner[:, None] / model_width
    ).astype(low)
    grad_value_raw = own_grad[1].reshape(row_count, local_width).astype(low)
    grad_proj = jnp.stack([grad_query_raw, grad_key_raw, grad_value_raw])
    grad_qkv = jnp.einsum("td,jte->jde", hidden_one, grad_proj, preferred_element_type=jnp.float32)
    grad_hidden_one = tensor_sum(
        jnp.einsum("jte,jde->td", grad_proj, qkv_low, preferred_element_type=jnp.float32).astype(low),
        7,
    ).astype(jnp.float32)
    grad_gain_one = jnp.sum(grad_hidden_one * tokens_f * scale_one, axis=0)
    scaled_one = grad_hidden_one * gain_one_f
    grad_tokens = (
        grad_residual
        + scale_one * scaled_one
        - tokens_f
        * (scale_one * scale_one * scale_one)
        * jnp.mean(scaled_one * tokens_f, axis=-1, keepdims=True)
    )
    grad_qk = (
        jnp.stack([grad_gain_query, grad_gain_key])
        .reshape(2, heads_here, groups, HEAD // groups)
        .transpose(2, 0, 1, 3)
        .reshape(groups, 1, qk_row.shape[1])
    )
    small_grads = jnp.concatenate(
        [
            grad_gain_one.reshape(groups, 1, row_count),
            grad_gain_two.reshape(groups, 1, row_count),
            jnp.pad(grad_qk, ((0, 0), (0, 0), (0, row_count - qk_row.shape[1]))),
            jnp.zeros((groups, 5, row_count), jnp.float32),
            grad_router_t.reshape(experts, groups, row_count).transpose(1, 0, 2),
        ],
        axis=1,
    )
    qkv_sum, out_sum, small_sum = weight_reduce(
        grad_qkv.astype(low), grad_out_w.astype(low), small_grads, 8
    )
    return (
        block_out.astype(low),
        grad_tokens.astype(low),
        qkv_sum,
        out_sum,
        small_sum[0],
        small_sum[1],
        small_sum[2, : qk_row.shape[1]].reshape(qk_gain.shape),
        small_sum[8 : 8 + experts].T,
        grad_gate_w,
        grad_up_w,
        grad_down,
    )


def solution(mesh):
    placed = (
        P("expert", None),
        P("expert", None),
        P(None, "expert", "tensor"),
        P("tensor", "expert"),
        P("expert"),
        P("expert"),
        P(None, "tensor", "expert"),
        P("expert", None),
        P("expert", None, "tensor"),
        P("expert", None, "tensor"),
        P("expert", "tensor", None),
        P("expert", None),
        P(),
    )
    compact = (mesh.shape["expert"], mesh.shape["tensor"]) == (GROUPS, NX * NC)
    return jax.shard_map(
        fast_shards if compact else shards,
        mesh=mesh,
        in_specs=placed,
        out_specs=(
            P("expert", None),
            P("expert", None),
            P(None, "expert", "tensor"),
            P("tensor", "expert"),
            P("expert"),
            P("expert"),
            P(None, "tensor", "expert"),
            P("expert", None),
            P("expert", None, "tensor"),
            P("expert", None, "tensor"),
            P("expert", "tensor", None),
        ),
        check_vma=False,
    )
```

```python
import jax
import jax.numpy as jnp
from jax import lax
from jax.experimental import pallas as pl
from jax.experimental.pallas import tpu as pltpu
from jax.sharding import PartitionSpec as P

HEAD = 128
WINDOW = 1024
SEQ = 2048


EPS = 1e-05
THETA = 10000.0


def from_behind(value, axis, steps):
    count = lax.axis_size(axis)
    initial, last = (max(0, -steps), min(count, count - steps))
    return lax.ppermute(value, axis, [(source, source + steps) for source in range(initial, last)])


def angles(position, head_size):
    half_size = head_size // 2
    frequency = THETA ** (-(jnp.arange(half_size, dtype=jnp.float32) * 2.0 / head_size))
    phase_angle = position.astype(jnp.float32)[:, None] * frequency[None, :]
    return (jnp.cos(phase_angle)[:, None, :], jnp.sin(phase_angle)[:, None, :])


def rotate(rotated_in, cosine_table, sine_table):
    half_size = rotated_in.shape[-1] // 2
    first_half = rotated_in[..., :half_size]
    second_half = rotated_in[..., half_size:]
    return jnp.concatenate(
        [
            first_half * cosine_table - second_half * sine_table,
            second_half * cosine_table + first_half * sine_table,
        ],
        axis=-1,
    )


def slot_layout(block_routes, experts, capacity):
    flat_routes = block_routes.reshape(-1)
    onehot = (flat_routes[:, None] == jnp.arange(experts, dtype=jnp.int32)[None, :]).astype(
        jnp.int32
    )
    before = jnp.cumsum(onehot, axis=0) - onehot
    rank_within = jnp.sum(before * onehot, axis=1)
    slot_index = flat_routes * capacity + rank_within
    slot_table = (
        jnp.zeros((experts * capacity,), jnp.int32)
        .at[slot_index]
        .set(jnp.arange(flat_routes.shape[0], dtype=jnp.int32) + 1)
    )
    return (slot_index, slot_table)


def shards(
    tokens_in,
    out_grad,
    w_qkv,
    w_attn_out,
    attn_gain,
    ffn_gain,
    qk_gain,
    w_router,
    w_gate,
    w_up,
    w_down,
    routes,
    segments,
):
    row_count, model_width = tokens_in.shape
    experts = w_router.shape[1]
    per_token = routes.shape[1]
    local_experts = w_gate.shape[0]
    heads_here = qk_gain.shape[1]
    local_width = heads_here * HEAD
    groups = lax.axis_size("expert")
    device = lax.axis_index("expert")
    capacity = row_count * per_token * 3 // (2 * experts)
    hop_count = WINDOW // row_count
    buffer_shape = (groups, local_experts, capacity, model_width)
    score_scale = HEAD ** (-0.5)

    def fetch_weights():
        return (
            lax.all_gather(w_qkv.astype(jnp.bfloat16), "expert", axis=1, tiled=True),
            lax.all_gather(w_attn_out.astype(jnp.bfloat16), "expert", axis=1, tiled=True),
            lax.all_gather(w_router.astype(jnp.bfloat16), "expert", axis=0, tiled=True),
            lax.all_gather(attn_gain.astype(jnp.bfloat16), "expert", axis=0, tiled=True),
            lax.all_gather(ffn_gain.astype(jnp.bfloat16), "expert", axis=0, tiled=True),
            lax.all_gather(qk_gain.astype(jnp.bfloat16), "expert", axis=2, tiled=True),
        )

    def prepare(pieces):
        return (
            pieces[0],
            pieces[1],
            pieces[2],
            pieces[3].astype(jnp.float32),
            pieces[4].astype(jnp.float32),
            pieces[5].astype(jnp.float32).reshape(2, local_width),
        )

    qkv_low, out_low, router_low, gain_one_f, gain_two_f, qk_gains = prepare(fetch_weights())
    tokens_f = tokens_in.astype(jnp.float32)
    scale_one = lax.rsqrt(jnp.mean(tokens_f * tokens_f, axis=-1, keepdims=True) + EPS)
    hidden_one = (tokens_f * scale_one * gain_one_f).astype(jnp.bfloat16)
    projected = jnp.einsum("td,jde->jte", hidden_one, qkv_low, preferred_element_type=jnp.float32)
    query_raw = projected[0]
    key_raw = projected[1]
    query_sq, key_sq = lax.psum(
        (jnp.sum(query_raw * query_raw, axis=-1), jnp.sum(key_raw * key_raw, axis=-1)), "tensor"
    )
    query_scale = lax.rsqrt(query_sq / model_width + EPS)[:, None]
    key_scale = lax.rsqrt(key_sq / model_width + EPS)[:, None]
    normed_query = query_raw * query_scale
    normed_key = key_raw * key_scale
    global_rows = device * row_count + jnp.arange(row_count, dtype=jnp.int32)
    cosine_table, sine_table = angles(global_rows % SEQ, HEAD)
    query_low = rotate(
        (normed_query * qk_gains[0]).reshape(row_count, heads_here, HEAD), cosine_table, sine_table
    ).astype(jnp.bfloat16)
    key_low = rotate(
        (normed_key * qk_gains[1]).reshape(row_count, heads_here, HEAD), cosine_table, sine_table
    ).astype(jnp.bfloat16)
    value_low = projected[2].astype(jnp.bfloat16).reshape(row_count, heads_here, HEAD)
    own_pair = jnp.stack([key_low, value_low])
    earlier = []
    for steps_back in range(hop_count, 0, -1):
        earlier.append(from_behind(own_pair, "expert", steps_back))
    context = jnp.concatenate(earlier + [own_pair], axis=1)
    key_rows = (device - hop_count) * row_count + jnp.arange(
        (hop_count + 1) * row_count, dtype=jnp.int32
    )
    segment_keys = segments[jnp.maximum(key_rows, 0)]
    segment_query = segments[global_rows]
    distance = global_rows[:, None] - key_rows[None, :]
    allowed = (
        (key_rows[None, :] >= 0)
        & (segment_query[:, None] == segment_keys[None, :])
        & (distance >= 0)
        & (distance < WINDOW)
    )

    def score_block():
        raw_scores = (
            jnp.einsum("qhd,khd->hqk", query_low, context[0], preferred_element_type=jnp.float32)
            * score_scale
        )
        return jnp.where(allowed[None], raw_scores, -1e30)

    scores = score_block()
    largest = jnp.max(scores, axis=-1, keepdims=True)
    exp_scores = jnp.exp(scores - largest)
    exp_total = jnp.sum(exp_scores, axis=-1, keepdims=True)
    log_total = largest + jnp.log(exp_total)
    attn_probs = (exp_scores / exp_total).astype(jnp.bfloat16)
    attended = (
        jnp.einsum("hqk,khd->qhd", attn_probs, context[1], preferred_element_type=jnp.float32)
        .reshape(row_count, local_width)
        .astype(jnp.bfloat16)
    )
    attention_out = lax.psum(
        jnp.dot(attended, out_low, preferred_element_type=jnp.float32).astype(jnp.bfloat16),
        "tensor",
    ).astype(jnp.float32)
    residual = tokens_f + attention_out
    scale_two = lax.rsqrt(jnp.mean(residual * residual, axis=-1, keepdims=True) + EPS)
    normed_two = residual * scale_two
    hidden_two = (normed_two * gain_two_f).astype(jnp.bfloat16)
    logits = jnp.dot(hidden_two, router_low, preferred_element_type=jnp.float32)
    logit_exp = jnp.exp(logits - jnp.max(logits, axis=-1, keepdims=True))
    router_probs = logit_exp / jnp.sum(logit_exp, axis=-1, keepdims=True)
    chosen = routes[:, :, None] == jnp.arange(experts, dtype=jnp.int32)[None, None, :]
    gate_probs = jnp.sum(jnp.where(chosen, router_probs[:, None, :], 0.0), axis=-1)
    slot_index, slot_table = slot_layout(routes, experts, capacity)
    present = (slot_table > 0)[:, None]
    assigned = jnp.maximum(slot_table - 1, 0)
    row_of_slot = assigned // per_token
    gate_low = w_gate.astype(jnp.bfloat16)
    up_low = w_up.astype(jnp.bfloat16)
    down_low = w_down.astype(jnp.bfloat16)

    def send_rows():
        buffer_rows = jnp.where(
            present, hidden_two[row_of_slot], jnp.zeros((), jnp.bfloat16)
        ).reshape(buffer_shape)
        return lax.all_to_all(buffer_rows, "expert", split_axis=0, concat_axis=0, tiled=True)

    def expert_front(arrived):
        gate_pre = jnp.einsum(
            "secd,edh->sech", arrived, gate_low, preferred_element_type=jnp.float32
        )
        up_pre = jnp.einsum("secd,edh->sech", arrived, up_low, preferred_element_type=jnp.float32)
        return (gate_pre, up_pre)

    received = send_rows()
    gate_pre, up_pre = expert_front(received)
    activated = (gate_pre * jax.nn.sigmoid(gate_pre) * up_pre).astype(jnp.bfloat16)
    partial_value = jnp.einsum(
        "sech,ehd->secd", activated, down_low, preferred_element_type=jnp.float32
    ).astype(jnp.bfloat16)
    returned = lax.all_to_all(
        partial_value, "expert", split_axis=0, concat_axis=0, tiled=True
    ).reshape(experts * capacity, model_width)
    expert_rows = returned[slot_index].reshape(row_count, per_token, model_width)
    expert_part = jnp.einsum(
        "tk,tkd->td", gate_probs, expert_rows, preferred_element_type=jnp.float32
    )
    block_out = residual + lax.psum(expert_part.astype(jnp.bfloat16), "tensor").astype(jnp.float32)
    qkv_low, out_low, router_low, gain_one_f, gain_two_f, qk_gains = prepare(fetch_weights())
    grad_out = out_grad.astype(jnp.float32)
    grad_gate_part = jnp.einsum(
        "td,tkd->tk", grad_out, expert_rows, preferred_element_type=jnp.float32
    )
    slot_grads = (
        (gate_probs[:, :, None] * grad_out[:, None, :])
        .astype(jnp.bfloat16)
        .reshape(row_count * per_token, model_width)
    )
    grad_buffer = jnp.where(present, slot_grads[assigned], jnp.zeros((), jnp.bfloat16)).reshape(
        buffer_shape
    )
    grad_received = lax.all_to_all(grad_buffer, "expert", split_axis=0, concat_axis=0, tiled=True)
    received = send_rows()
    gate_pre, up_pre = expert_front(received)
    sigmoid_gate = jax.nn.sigmoid(gate_pre)
    swish_gate = gate_pre * sigmoid_gate
    activated = (swish_gate * up_pre).astype(jnp.bfloat16)
    grad_act = jnp.einsum(
        "secd,ehd->sech", grad_received, down_low, preferred_element_type=jnp.float32
    )
    grad_down = jnp.einsum(
        "sech,secd->ehd", activated, grad_received, preferred_element_type=jnp.float32
    )
    grad_gate_pre = (
        grad_act * up_pre * sigmoid_gate * (1.0 + gate_pre * (1.0 - sigmoid_gate))
    ).astype(jnp.bfloat16)
    grad_up_pre = (grad_act * swish_gate).astype(jnp.bfloat16)
    grad_gate_w = jnp.einsum(
        "secd,sech->edh", received, grad_gate_pre, preferred_element_type=jnp.float32
    )
    grad_up_w = jnp.einsum(
        "secd,sech->edh", received, grad_up_pre, preferred_element_type=jnp.float32
    )
    grad_rows = (
        jnp.einsum("sech,edh->secd", grad_gate_pre, gate_low, preferred_element_type=jnp.float32)
        + jnp.einsum("sech,edh->secd", grad_up_pre, up_low, preferred_element_type=jnp.float32)
    ).astype(jnp.bfloat16)
    grad_back = lax.all_to_all(
        grad_rows, "expert", split_axis=0, concat_axis=0, tiled=True
    ).reshape(experts * capacity, model_width)
    grad_hidden_part = jnp.sum(
        grad_back[slot_index].reshape(row_count, per_token, model_width), axis=1, dtype=jnp.float32
    )
    grad_hidden_sum, grad_gates = (
        lax.psum(grad_hidden_part.astype(jnp.bfloat16), "tensor").astype(jnp.float32),
        lax.psum(grad_gate_part.astype(jnp.bfloat16), "tensor").astype(jnp.float32),
    )
    grad_probs = jnp.sum(jnp.where(chosen, grad_gates[:, :, None], 0.0), axis=1)
    grad_logits = (
        router_probs * (grad_probs - jnp.sum(router_probs * grad_probs, axis=-1, keepdims=True))
    ).astype(jnp.bfloat16)
    grad_hidden_two = grad_hidden_sum + jnp.dot(
        grad_logits, router_low.T, preferred_element_type=jnp.float32
    )
    grad_router = jnp.dot(hidden_two.T, grad_logits, preferred_element_type=jnp.float32)
    grad_gain_two = jnp.sum(grad_hidden_two * normed_two, axis=0)
    scaled_two = grad_hidden_two * gain_two_f
    grad_residual = (
        grad_out
        + scale_two * scaled_two
        - residual
        * (scale_two * scale_two * scale_two)
        * jnp.mean(scaled_two * residual, axis=-1, keepdims=True)
    )
    grad_attn = grad_residual.astype(jnp.bfloat16)
    grad_out_w = jnp.dot(attended.T, grad_attn, preferred_element_type=jnp.float32)
    grad_attended = (
        jnp.dot(grad_attn, out_low.T, preferred_element_type=jnp.float32)
        .astype(jnp.bfloat16)
        .reshape(row_count, heads_here, HEAD)
    )
    attn_weights = jnp.where(allowed[None], jnp.exp(score_block() - log_total), 0.0)
    grad_weights = jnp.einsum(
        "qhd,khd->hqk", grad_attended, context[1], preferred_element_type=jnp.float32
    )
    inner_sum = jnp.sum(attn_weights * grad_weights, axis=-1, keepdims=True)
    grad_scores = (attn_weights * (grad_weights - inner_sum) * score_scale).astype(jnp.bfloat16)
    grad_query = jnp.einsum(
        "hqk,khd->qhd", grad_scores, context[0], preferred_element_type=jnp.float32
    )
    grad_keys = jnp.einsum(
        "hqk,qhd->khd", grad_scores, query_low, preferred_element_type=jnp.float32
    )
    grad_values = jnp.einsum(
        "hqk,qhd->khd",
        attn_weights.astype(jnp.bfloat16),
        grad_attended,
        preferred_element_type=jnp.float32,
    )
    grad_pair = jnp.stack([grad_keys, grad_values]).reshape(
        2, hop_count + 1, row_count, heads_here, HEAD
    )
    own_grad = grad_pair[:, hop_count]
    for steps_back in range(1, hop_count + 1):
        own_grad = own_grad + from_behind(
            grad_pair[:, hop_count - steps_back].astype(jnp.bfloat16), "expert", -steps_back
        ).astype(jnp.float32)
    grad_query_norm = rotate(grad_query, cosine_table, -sine_table).reshape(row_count, local_width)
    grad_key_norm = rotate(own_grad[0], cosine_table, -sine_table).reshape(row_count, local_width)
    grad_gain_query = jnp.sum(grad_query_norm * normed_query, axis=0)
    grad_gain_key = jnp.sum(grad_key_norm * normed_key, axis=0)
    scaled_query = grad_query_norm * qk_gains[0]
    scaled_key = grad_key_norm * qk_gains[1]
    query_inner, key_inner = lax.psum(
        (jnp.sum(scaled_query * query_raw, axis=-1), jnp.sum(scaled_key * key_raw, axis=-1)),
        "tensor",
    )
    grad_query_raw = (
        query_scale * scaled_query
        - query_raw * (query_scale * query_scale * query_scale) * query_inner[:, None] / model_width
    ).astype(jnp.bfloat16)
    grad_key_raw = (
        key_scale * scaled_key
        - key_raw * (key_scale * key_scale * key_scale) * key_inner[:, None] / model_width
    ).astype(jnp.bfloat16)
    grad_value_raw = own_grad[1].reshape(row_count, local_width).astype(jnp.bfloat16)
    grad_proj = jnp.stack([grad_query_raw, grad_key_raw, grad_value_raw])
    grad_qkv = jnp.einsum("td,jte->jde", hidden_one, grad_proj, preferred_element_type=jnp.float32)
    grad_hidden_one = lax.psum(
        jnp.einsum("jte,jde->td", grad_proj, qkv_low, preferred_element_type=jnp.float32).astype(
            jnp.bfloat16
        ),
        "tensor",
    ).astype(jnp.float32)
    grad_gain_one = jnp.sum(grad_hidden_one * tokens_f * scale_one, axis=0)
    scaled_one = grad_hidden_one * gain_one_f
    grad_tokens = (
        grad_residual
        + scale_one * scaled_one
        - tokens_f
        * (scale_one * scale_one * scale_one)
        * jnp.mean(scaled_one * tokens_f, axis=-1, keepdims=True)
    )
    grad_qk = jnp.stack([grad_gain_query, grad_gain_key]).reshape(2, heads_here, HEAD)
    reduced = (
        lax.psum_scatter(
            grad_qkv.astype(jnp.bfloat16), "expert", scatter_dimension=1, tiled=True
        ).astype(jnp.float32),
        lax.psum_scatter(
            grad_out_w.astype(jnp.bfloat16), "expert", scatter_dimension=1, tiled=True
        ).astype(jnp.float32),
        lax.psum_scatter(
            grad_router.astype(jnp.bfloat16), "expert", scatter_dimension=0, tiled=True
        ).astype(jnp.float32),
        lax.psum_scatter(
            grad_gain_one.astype(jnp.bfloat16), "expert", scatter_dimension=0, tiled=True
        ).astype(jnp.float32),
        lax.psum_scatter(
            grad_gain_two.astype(jnp.bfloat16), "expert", scatter_dimension=0, tiled=True
        ).astype(jnp.float32),
        lax.psum_scatter(
            grad_qk.astype(jnp.bfloat16), "expert", scatter_dimension=2, tiled=True
        ).astype(jnp.float32),
    )
    return (
        block_out.astype(jnp.bfloat16),
        grad_tokens.astype(jnp.bfloat16),
        reduced[0],
        reduced[1],
        reduced[3],
        reduced[4],
        reduced[5],
        reduced[2],
        grad_gate_w,
        grad_up_w,
        grad_down,
    )


MESH_ID = pl.DeviceIdType.MESH
HBM = pl.BlockSpec(memory_space=pl.ANY)
VMEM = pl.BlockSpec(memory_space=pltpu.VMEM)
NZ, NY, NX, NC = 4, 2, 2, 2
GROUPS = NZ * NY


def place():
    e = lax.axis_index("expert")
    t = lax.axis_index("tensor")
    return lax.div(e, NY), lax.rem(e, NY), lax.div(t, NC), lax.rem(t, NC)


def device(z, y, x, c):
    return (z * NY + y, x * NC + c)


def run_if(condition, body):
    if condition is None:
        body()
    else:
        pl.when(condition)(body)


def greet(partners):
    barrier = pltpu.get_barrier_semaphore()
    for target, condition in partners:
        run_if(
            condition,
            lambda target=target: pl.semaphore_signal(
                barrier, inc=1, device_id=target, device_id_type=MESH_ID
            ),
        )
    count = sum(1 for _, condition in partners if condition is None)
    for _, condition in partners:
        if condition is not None:
            count = count + condition.astype(jnp.int32)
    pl.semaphore_wait(barrier, count)


def remote(source, target_ref, send_sem, recv_sem, target):
    return pltpu.make_async_remote_copy(
        src_ref=source,
        dst_ref=target_ref,
        send_sem=send_sem,
        recv_sem=recv_sem,
        device_id=target,
        device_id_type=MESH_ID,
    )


def block_rows(block, rows):
    return pl.ds(pl.multiple_of(block * rows, rows), rows)


class LineGather:
    def __init__(self, streams, sources, views, send_sem, recv_sem):
        self.z, self.y, self.x, self.c = place()
        self.streams, self.sources, self.views = streams, sources, views
        self.send_sem, self.recv_sem = send_sem, recv_sem
        self.has_up, self.has_down = self.z < NZ - 1, self.z > 0
        self.pending = []

    def partners(self):
        z, y, x, c = self.z, self.y, self.x, self.c
        return [
            (device(z + 1, y, x, c), z < NZ - 1),
            (device(z - 1, y, x, c), z > 0),
            (device(z, 1 - y, x, c), None),
        ]

    def exists(self, rel):
        rel = rel % 7
        if rel == 0:
            return None
        return self.z >= rel if rel < 4 else self.z + (rel - 3) < NZ

    def block(self, rel):
        y = self.y if rel < 7 else 1 - self.y
        rel = rel % 7
        z = self.z if rel == 0 else (self.z - rel if rel < 4 else self.z + (rel - 3))
        return z * NY + y

    def send(self, stream, rel, way):
        z, y, x, c = self.z, self.y, self.x, self.c
        block = self.block(rel)
        there = self.views[stream](block)
        source = self.sources[stream] if rel == 0 else there
        if way == 0:
            target, landing = device(z + 1, y, x, c), (1 if rel == 0 else rel + 1)
        elif way == 1:
            target, landing = device(z - 1, y, x, c), (4 if rel == 0 else rel + 1)
        else:
            target, landing = device(z, 1 - y, x, c), 7 + rel
        return remote(
            source,
            there,
            self.send_sem.at[stream, rel, way],
            self.recv_sem.at[stream, landing],
            target,
        )

    def start(self, stream, rel):
        if rel < 4:
            run = self.has_up
            run_if(run, lambda: self.send(stream, rel, 0).start())
            self.pending.append((stream, rel, 0, run))
        if rel == 0 or rel >= 4:
            run = self.has_down
            run_if(run, lambda: self.send(stream, rel, 1).start())
            self.pending.append((stream, rel, 1, run))
        self.send(stream, rel, 2).start()
        self.pending.append((stream, rel, 2, None))

    def arrive(self, stream, rel):
        there = self.views[stream](self.block(rel))
        remote(
            there,
            there,
            self.send_sem.at[stream, 0, 0],
            self.recv_sem.at[stream, rel],
            device(self.z, 1 - self.y, self.x, self.c),
        ).wait_recv()

    def order(self):
        return [7, 1, 4, 8, 11, 2, 5, 9, 12, 3, 6, 10, 13]

    def run(self, hook=None):
        for stream in self.streams:
            self.start(stream, 0)
        for rel in self.order():
            def step(rel=rel):
                marks = len(self.pending)
                for stream in self.streams:
                    self.arrive(stream, rel)
                    if rel < 7:
                        self.start(stream, rel)
                    if hook is not None:
                        hook(stream, rel)
                if rel < 7:
                    late = self.pending[marks:]
                    del self.pending[marks:]
                    self.finish_later(late, rel)
            run_if(self.exists(rel), step)

    def finish_later(self, late, rel):
        self.late = getattr(self, "late", []) + [(rel, late)]

    def finish(self):
        for stream, rel, way, run in self.pending:
            run_if(run, lambda s=stream, r=rel, w=way: self.send(s, r, w).wait_send())
        for rel, late in getattr(self, "late", []):
            def body(late=late):
                for stream, rel, way, run in late:
                    run_if(run, lambda s=stream, r=rel, w=way: self.send(s, r, w).wait_send())
            run_if(self.exists(rel), body)


def cost(microseconds):
    return pl.CostEstimate(flops=0, bytes_accessed=int(microseconds * 3.0e6), transcendentals=0)


def comm_params(collective_id, megabytes=56):
    return pltpu.CompilerParams(
        collective_id=collective_id,
        has_side_effects=True,
        vmem_limit_bytes=megabytes * 1024 * 1024,
    )


def weight_gather(qkv_low, out_low, smalls, collective_id):
    parts, rows, width = qkv_low.shape
    depth, columns = out_low.shape

    def kernel(qkv, out, small, qkv_all, out_all, small_all, send_sem, recv_sem, local_sem):
        views = [
            lambda b: qkv_all.at[:, block_rows(b, rows), :],
            lambda b: out_all.at[:, block_rows(b, columns)],
            lambda b: small_all.at[b],
        ]
        line = LineGather([2, 0, 1], [qkv, out, small], views, send_sem, recv_sem)
        greet(line.partners())
        own = line.block(0)
        keep = [
            pltpu.make_async_copy(source, view(own), local_sem.at[i])
            for i, (source, view) in enumerate(zip([qkv, out, small], views))
        ]
        for copy in keep:
            copy.start()
        line.run()
        line.finish()
        for copy in keep:
            copy.wait()

    return pl.pallas_call(
        kernel,
        out_shape=(
            jax.ShapeDtypeStruct((parts, rows * GROUPS, width), jnp.bfloat16),
            jax.ShapeDtypeStruct((depth, columns * GROUPS), jnp.bfloat16),
            jax.ShapeDtypeStruct((GROUPS,) + smalls.shape, jnp.float32),
        ),
        in_specs=[HBM] * 3,
        out_specs=(HBM, HBM, HBM),
        scratch_shapes=[
            pltpu.SemaphoreType.DMA((3, 7, 3)),
            pltpu.SemaphoreType.DMA((3, 14)),
            pltpu.SemaphoreType.DMA((3,)),
        ],
        compiler_params=comm_params(collective_id),
        cost_estimate=cost(100),
        name="weight_gather",
    )(qkv_low, out_low, smalls)


def token_gather(block, collective_id):
    rows, width = block.shape
    a_cols, c_cols = width * 3 // 16, width // 8

    def kernel(own_ref, all_ref, send_sem, recv_sem, x_send, x_recv, core_send, core_recv, local_sem):
        z, y, x, c = place()

        def a_at(xx, cc):
            return pl.ds(pl.multiple_of(xx * (2 * a_cols) + cc * a_cols, 128), a_cols)

        def c_at(cc):
            return pl.ds(pl.multiple_of(4 * a_cols + cc * c_cols, 128), c_cols)

        def view(b, columns):
            return all_ref.at[block_rows(b, rows), columns]

        sources = [own_ref.at[:, a_at(x, c)], own_ref.at[:, c_at(c)]]
        views = [lambda b: view(b, a_at(x, c)), lambda b: view(b, c_at(c))]
        line = LineGather([0, 1], sources, views, send_sem, recv_sem)
        across, twin = device(z, y, 1 - x, c), device(z, y, x, 1 - c)
        greet(line.partners() + [(across, None), (twin, None)])
        keep = pltpu.make_async_copy(own_ref, all_ref.at[block_rows(line.block(0), rows), :], local_sem)
        keep.start()

        def to_twin(rel, stream, landing=False):
            b = line.block(rel)
            columns = [a_at(x, c), c_at(c), a_at(1 - x, c)][stream]
            other = [a_at(x, 1 - c), c_at(1 - c), a_at(1 - x, 1 - c)][stream]
            piece = view(b, other if landing else columns)
            return remote(piece, piece, core_send.at[rel, stream], core_recv.at[rel, stream], twin)

        def to_across(rel, landing=False):
            b = line.block(rel)
            piece = view(b, a_at(1 - x if landing else x, c))
            return remote(piece, piece, x_send.at[rel], x_recv.at[rel], across)

        def hook(stream, rel):
            if stream == 0:
                to_across(rel).start()
            to_twin(rel, stream).start()

        line.run(hook)
        for rel in line.order():
            def relay(rel=rel):
                to_across(rel, True).wait_recv()
                to_twin(rel, 2).start()
            run_if(line.exists(rel), relay)
        for rel in line.order():
            def end(rel=rel):
                to_across(rel).wait_send()
                for stream in range(3):
                    to_twin(rel, stream, True).wait_recv()
                    to_twin(rel, stream).wait_send()
            run_if(line.exists(rel), end)
        line.finish()
        keep.wait()

    return pl.pallas_call(
        kernel,
        out_shape=jax.ShapeDtypeStruct((rows * GROUPS, width), block.dtype),
        in_specs=[HBM],
        out_specs=HBM,
        scratch_shapes=[
            pltpu.SemaphoreType.DMA((2, 7, 3)),
            pltpu.SemaphoreType.DMA((2, 14)),
            pltpu.SemaphoreType.DMA((14,)),
            pltpu.SemaphoreType.DMA((14,)),
            pltpu.SemaphoreType.DMA((14, 3)),
            pltpu.SemaphoreType.DMA((14, 3)),
            pltpu.SemaphoreType.DMA,
        ],
        compiler_params=comm_params(collective_id),
        cost_estimate=cost(45),
        name="token_gather",
    )(block)


def add_into(rows, step, store):
    def body(i, carry):
        store(pl.ds(pl.multiple_of(i * step, step), step))
        return carry

    lax.fori_loop(0, rows // step, body, 0)


def group_stages(part_ref, out_ref, core_buf, x_buf, send_sem, recv_sem):
    rows, width = part_ref.shape
    half, quarter = width // 2, width // 4
    z, y, x, c = place()
    across, twin = device(z, y, 1 - x, c), device(z, y, x, 1 - c)

    def half_of(cc):
        return pl.ds(pl.multiple_of(cc * half, half), half)

    def quarter_of(xx, cc):
        return pl.ds(pl.multiple_of(cc * half + xx * quarter, quarter), quarter)

    own, from_x = out_ref.at[:, quarter_of(x, c)], out_ref.at[:, quarter_of(1 - x, c)]
    to_x = core_buf.at[:, pl.ds(pl.multiple_of((1 - x) * quarter, quarter), quarter)]
    sources = [part_ref.at[:, half_of(1 - c)], to_x, own, own, from_x]
    landings = [core_buf, x_buf, own, own, from_x]
    targets = [twin, across, across, twin, twin]

    def copy(k):
        return remote(sources[k], landings[k], send_sem.at[k], recv_sem.at[k], targets[k])

    def arrive(k, landing):
        remote(landing, landing, send_sem.at[k], recv_sem.at[k], targets[k]).wait_recv()

    def begin():
        copy(0).start()

    def core_step():
        copy(0).wait_recv()
        add_to(core_buf, core_buf, part_ref.at[:, half_of(c)], 32)
        copy(1).start()

    def x_step():
        copy(1).wait_recv()
        add_to(own, x_buf, core_buf.at[:, pl.ds(pl.multiple_of(x * quarter, quarter), quarter)], 32)
        copy(2).start()
        copy(3).start()

    def spread():
        arrive(2, from_x)
        copy(4).start()

    def end():
        arrive(3, out_ref.at[:, quarter_of(x, 1 - c)])
        arrive(4, out_ref.at[:, quarter_of(1 - x, 1 - c)])
        for k in range(5):
            copy(k).wait_send()

    return [begin, core_step, x_step, spread, end]


def group_sum(part_ref, out_ref, core_buf, x_buf, send_sem, recv_sem, meanwhile=None):
    stages = group_stages(part_ref, out_ref, core_buf, x_buf, send_sem, recv_sem)
    stages[0]()
    if meanwhile is not None:
        meanwhile()
    for stage in stages[1:]:
        stage()


def tensor_sum(part, collective_id):
    rows, width = part.shape

    def kernel(part_ref, out_ref, core_buf, x_buf, send_sem, recv_sem):
        z, y, x, c = place()
        greet([(device(z, y, 1 - x, c), None), (device(z, y, x, 1 - c), None)])
        group_sum(part_ref, out_ref, core_buf, x_buf, send_sem, recv_sem)

    return pl.pallas_call(
        kernel,
        out_shape=jax.ShapeDtypeStruct((rows, width), jnp.bfloat16),
        in_specs=[VMEM],
        out_specs=VMEM,
        scratch_shapes=[
            pltpu.VMEM((rows, width // 2), jnp.bfloat16),
            pltpu.VMEM((rows, width // 4), jnp.bfloat16),
            pltpu.SemaphoreType.DMA((5,)),
            pltpu.SemaphoreType.DMA((5,)),
        ],
        compiler_params=comm_params(collective_id, 16),
        cost_estimate=cost(17),
        name="tensor_sum",
    )(part)


Z_ORDER = (3, 0, 2, 1)


def accumulate(into, addend, step=64):
    rows = into.shape[0]
    step = min(step, rows)

    def body(i, carry):
        r = pl.ds(pl.multiple_of(i * step, step), step)
        total = into[r, :].astype(jnp.float32) + addend[r, :].astype(jnp.float32)
        into[r, :] = total.astype(into.dtype)
        return carry

    lax.fori_loop(0, rows // step, body, 0)


class LineReduce:
    def __init__(self, streams, own, y_buf, lo_buf, hi_buf, send_sem, recv_sem):
        self.z, self.y, self.x, self.c = place()
        self.streams = streams
        self.own, self.y_buf, self.lo_buf, self.hi_buf = own, y_buf, lo_buf, hi_buf
        self.send_sem, self.recv_sem = send_sem, recv_sem

    def partners(self):
        z, y, x, c = self.z, self.y, self.x, self.c
        return [
            (device(z + 1, y, x, c), z < NZ - 1),
            (device(z - 1, y, x, c), z > 0),
            (device(z, 1 - y, x, c), None),
        ]

    def copy(self, s, zz, way):
        z, y, x, c = self.z, self.y, self.x, self.c
        if way == 0:
            source, landing, target = self.own(s, zz, 1 - y), self.y_buf, device(z, 1 - y, x, c)
        elif way == 1:
            source, landing, target = self.y_buf(s, zz), self.lo_buf, device(z + 1, y, x, c)
        else:
            source, landing, target = self.y_buf(s, zz), self.hi_buf, device(z - 1, y, x, c)
        return remote(
            source, landing(s, zz), self.send_sem.at[s, zz, way], self.recv_sem.at[s, zz, way], target
        )

    def to_y(self, s, zz):
        self.copy(s, zz, 0).start()

    def take(self, s, zz, way):
        self.copy(s, zz, way).wait_recv()
        accumulate(self.y_buf(s, zz), (self.lo_buf if way == 1 else self.hi_buf)(s, zz))

    def along_z(self, s, zz):
        z = self.z
        self.copy(s, zz, 0).wait_recv()
        accumulate(self.y_buf(s, zz), self.own(s, zz, self.y))

        def upward():
            run_if(z > 0, lambda: self.take(s, zz, 1))
            self.copy(s, zz, 1).start()

        def downward():
            run_if(z < NZ - 1, lambda: self.take(s, zz, 2))
            self.copy(s, zz, 2).start()

        run_if(z < zz, upward)
        run_if(z > zz, downward)

    def home(self, done):
        for zz in range(NZ):
            def land(zz=zz):
                for s in self.streams:
                    if zz > 0:
                        self.take(s, zz, 1)
                    if zz < NZ - 1:
                        self.take(s, zz, 2)
                    done(s, self.y_buf(s, zz))
            run_if(self.z == zz, land)

    def finish(self):
        for zz in range(NZ):
            for s in self.streams:
                self.copy(s, zz, 0).wait_send()
                run_if(self.z < zz, lambda s=s, zz=zz: self.copy(s, zz, 1).wait_send())
                run_if(self.z > zz, lambda s=s, zz=zz: self.copy(s, zz, 2).wait_send())


def weight_reduce(qkv, out, smalls, collective_id):
    parts, depth, width = qkv.shape
    rows = depth // GROUPS
    out_rows, columns = out.shape[0], out.shape[1] // GROUPS

    def kernel(qkv_ref, out_ref, small_ref, qkv_sum, out_sum, small_sum,
               qkv_buf, out_buf, small_buf, send_sem, recv_sem):
        def own(s, zz, yy):
            b = zz * NY + yy
            if s < parts:
                return qkv_ref.at[s, block_rows(b, rows), :]
            if s == parts:
                return out_ref.at[:, block_rows(b, columns)]
            return small_ref.at[b]

        def slot(kind):
            def view(s, zz):
                if s < parts:
                    return qkv_buf.at[kind, zz, s]
                if s == parts:
                    return out_buf.at[kind, zz]
                return small_buf.at[kind, zz]
            return view

        streams = list(range(parts + 2))
        line = LineReduce(streams, own, slot(0), slot(1), slot(2), send_sem, recv_sem)
        greet(line.partners())
        work = [(s, zz) for s in [parts + 1, parts] + list(range(parts)) for zz in Z_ORDER]
        for s, zz in work:
            line.to_y(s, zz)
        for s, zz in work:
            line.along_z(s, zz)

        def done(s, total):
            target = qkv_sum.at[s] if s < parts else (out_sum if s == parts else small_sum)
            step = min(64, target.shape[0])

            def body(i, carry):
                r = pl.ds(pl.multiple_of(i * step, step), step)
                target[r, :] = total[r, :].astype(jnp.float32)
                return carry

            lax.fori_loop(0, target.shape[0] // step, body, 0)

        line.home(done)
        line.finish()

    return pl.pallas_call(
        kernel,
        out_shape=(
            jax.ShapeDtypeStruct((parts, rows, width), jnp.float32),
            jax.ShapeDtypeStruct((out_rows, columns), jnp.float32),
            jax.ShapeDtypeStruct(smalls.shape[1:], jnp.float32),
        ),
        in_specs=[VMEM] * 3,
        out_specs=(VMEM,) * 3,
        scratch_shapes=[
            pltpu.VMEM((3, NZ, parts, rows, width), jnp.bfloat16),
            pltpu.VMEM((3, NZ, out_rows, columns), jnp.bfloat16),
            pltpu.VMEM((3, NZ) + smalls.shape[1:], jnp.float32),
            pltpu.SemaphoreType.DMA((parts + 2, NZ, 3)),
            pltpu.SemaphoreType.DMA((parts + 2, NZ, 3)),
        ],
        compiler_params=comm_params(collective_id),
        cost_estimate=cost(120),
        name="weight_reduce",
    )(qkv, out, smalls)


def token_reduce(part, collective_id, pairs=None):
    tokens, width = part.shape
    rows = tokens // GROUPS
    half, quarter = width // 2, width // 4

    def kernel(part_ref, out_ref, core_buf, x_buf, y_buf, lo_buf, hi_buf,
               core_send, core_recv, x_send, x_recv, send_sem, recv_sem):
        z, y, x, c = place()
        across, twin = device(z, y, 1 - x, c), device(z, y, x, 1 - c)

        line = LineReduce(
            [0], lambda s, zz, yy: x_buf.at[zz * NY + yy], lambda s, zz: y_buf.at[zz],
            lambda s, zz: lo_buf.at[zz], lambda s, zz: hi_buf.at[zz], send_sem, recv_sem,
        )
        greet(line.partners() + [(across, None), (twin, None)])
        order = [(zz, flip) for zz in Z_ORDER for flip in (1, 0)]

        def number(zz, flip):
            return zz * NY + (1 - y if flip else y)

        def to_twin(zz, flip):
            b = number(zz, flip)
            return remote(
                part_ref.at[block_rows(b, rows), pl.ds(pl.multiple_of((1 - c) * half, half), half)],
                core_buf.at[b], core_send.at[zz, flip], core_recv.at[zz, flip], twin,
            )

        def to_across(zz, flip):
            b = number(zz, flip)
            return remote(
                core_buf.at[b, :, pl.ds(pl.multiple_of((1 - x) * quarter, quarter), quarter)],
                x_buf.at[b], x_send.at[zz, flip], x_recv.at[zz, flip], across,
            )

        def add_core(zz, flip):
            b = number(zz, flip)

            def store(r):
                at = pl.ds(pl.multiple_of(b * rows + r.start, 16), r.size)
                core_buf[b, r, :] = (
                    core_buf[b, r, :].astype(jnp.float32)
                    + part_ref[at, pl.ds(pl.multiple_of(c * half, half), half)].astype(jnp.float32)
                ).astype(jnp.bfloat16)

            add_into(rows, 32, store)

        def add_across(zz, flip):
            b = number(zz, flip)

            def store(r):
                x_buf[b, r, :] = (
                    x_buf[b, r, :].astype(jnp.float32)
                    + core_buf[b, r, pl.ds(pl.multiple_of(x * quarter, quarter), quarter)].astype(jnp.float32)
                ).astype(jnp.bfloat16)

            add_into(rows, 64, store)

        def stage_twin(i):
            to_twin(*order[i]).wait_recv()
            add_core(*order[i])
            to_across(*order[i]).start()

        def stage_across(i):
            zz, flip = order[i]
            to_across(zz, flip).wait_recv()
            add_across(zz, flip)
            if flip:
                line.to_y(0, zz)

        def stage_y(zz):
            line.along_z(0, zz)

        for zz, flip in order:
            to_twin(zz, flip).start()
        count = len(order)
        for i in range(count + 4):
            if i < count:
                stage_twin(i)
            if 0 <= i - 1 < count:
                stage_across(i - 1)
            if i >= 3 and (i - 3) % 2 == 0 and (i - 3) // 2 < NZ:
                stage_y(Z_ORDER[(i - 3) // 2])

        def done(s, total):
            def store(r):
                out_ref[r, :] = total[r, :]

            add_into(rows, 64, store)

        line.home(done)
        for zz, flip in order:
            to_twin(zz, flip).wait_send()
            to_across(zz, flip).wait_send()
        line.finish()

    return pl.pallas_call(
        kernel,
        out_shape=jax.ShapeDtypeStruct((rows, quarter), jnp.bfloat16),
        in_specs=[VMEM],
        out_specs=VMEM,
        scratch_shapes=[
            pltpu.VMEM((GROUPS, rows, half), jnp.bfloat16),
            pltpu.VMEM((GROUPS, rows, quarter), jnp.bfloat16),
            pltpu.VMEM((NZ, rows, quarter), jnp.bfloat16),
            pltpu.VMEM((NZ, rows, quarter), jnp.bfloat16),
            pltpu.VMEM((NZ, rows, quarter), jnp.bfloat16),
            pltpu.SemaphoreType.DMA((NZ, 2)),
            pltpu.SemaphoreType.DMA((NZ, 2)),
            pltpu.SemaphoreType.DMA((NZ, 2)),
            pltpu.SemaphoreType.DMA((NZ, 2)),
            pltpu.SemaphoreType.DMA((1, NZ, 3)),
            pltpu.SemaphoreType.DMA((1, NZ, 3)),
        ],
        compiler_params=comm_params(collective_id),
        cost_estimate=cost(60),
        name="token_reduce",
    )(part)


def gate_exchange(part, collective_id):
    groups = part.shape[0]
    tensors = NX * NC

    def kernel(part_ref, out_ref, landing, total, send_t, recv_t, send_e, recv_e):
        e = lax.axis_index("expert")
        t = lax.axis_index("tensor")
        mates = [(e, lax.rem(t + k, tensors)) for k in range(1, tensors)]
        peers = [(lax.rem(e + k, groups), t) for k in range(1, groups)]
        greet([(target, None) for target in mates + peers])
        near = [
            remote(part_ref, landing.at[k], send_t.at[k], recv_t.at[k], mates[k])
            for k in range(tensors - 1)
        ]
        for copy in near:
            copy.start()
        for copy in near:
            copy.wait_recv()
        value = part_ref[...]
        for k in range(tensors - 1):
            value = value + landing[k]
        total[...] = value
        far = [
            remote(
                total.at[lax.rem(e + k, groups)], out_ref.at[e], send_e.at[k - 1], recv_e.at[k - 1],
                peers[k - 1],
            )
            for k in range(1, groups)
        ]
        for copy in far:
            copy.start()
        out_ref[e] = total[e]
        for k in range(1, groups):
            source = out_ref.at[lax.rem(e + groups - k, groups)]
            remote(source, source, send_e.at[k - 1], recv_e.at[k - 1], peers[k - 1]).wait_recv()
        for copy in near + far:
            copy.wait_send()

    return pl.pallas_call(
        kernel,
        out_shape=jax.ShapeDtypeStruct(part.shape, jnp.float32),
        in_specs=[VMEM],
        out_specs=VMEM,
        scratch_shapes=[
            pltpu.VMEM((tensors - 1,) + part.shape, jnp.float32),
            pltpu.VMEM(part.shape, jnp.float32),
            pltpu.SemaphoreType.DMA((tensors - 1,)),
            pltpu.SemaphoreType.DMA((tensors - 1,)),
            pltpu.SemaphoreType.DMA((groups - 1,)),
            pltpu.SemaphoreType.DMA((groups - 1,)),
        ],
        compiler_params=comm_params(collective_id, 16),
        cost_estimate=cost(10),
        name="gate_exchange",
    )(part)


def dot(a, b, dims):
    return lax.dot_general(a, b, ((dims[:1], dims[1:]), ((), ())), preferred_element_type=jnp.float32)


def add_to(target, first, second, step=64):
    rows = target.shape[0]

    def body(i, carry):
        r = pl.ds(pl.multiple_of(i * step, step), step)
        total = first[r, :].astype(jnp.float32) + second[r, :].astype(jnp.float32)
        target[r, :] = total.astype(target.dtype)
        return carry

    lax.fori_loop(0, rows // step, body, 0)


def expert_layer(hidden_all, grad_out_all, gate_up, down, router_t, chosen_all, collective_id):
    tokens, width = hidden_all.shape
    rows = tokens // GROUPS
    units = down.shape[0]
    local = 2
    hidden = units // local
    experts = router_t.shape[0]
    half, part, piece = width // 2, width // 4, width // 8
    tensors = NX * NC
    steps = GROUPS + 4
    low = jnp.bfloat16
    wide = width // 4

    def kernel(
        h_in, dy_in, gu_ref, down_ref, router_ref, chosen_ref,
        y_out, dh_out, gates_out, gate_w, up_w, down_w,
        h, dy, gated, dgu, dx, y_stage, gu_stage, d_stage,
        core_buf, px_buf, py_buf, qy_buf, qx_buf, z_sum, lo_buf, hi_buf, gate_part, gate_land,
        in_sem, y_sem, gu_sem, d_sem, core_s, core_r, px_s, px_r, py_s, py_r, qy_s, qy_r, qx_s, qx_r,
        z_s, z_r, near_s, near_r, far_s, far_r, end_s, end_r,
    ):
        z, y, x, c = place()
        e, t = lax.axis_index("expert"), lax.axis_index("tensor")
        across, twin, beside = device(z, y, 1 - x, c), device(z, y, x, 1 - c), device(z, 1 - y, x, c)
        mates = [(e, lax.rem(t + k, tensors)) for k in range(1, tensors)]
        peers = [(lax.rem(e + k, GROUPS), t) for k in range(1, GROUPS)]
        greet([(target, None) for target in mates + peers])

        def zz_of(j):
            return jnp.where(j == 0, 3, jnp.where(j == 1, 0, jnp.where(j == 2, 2, 1)))

        def block_of(i):
            own = lax.rem(i, 2)
            return zz_of(lax.div(i, 2)) * NY + jnp.where(own == 1, y, 1 - y)

        def load(i):
            r = block_rows(block_of(i), rows)
            return (
                pltpu.make_async_copy(h_in.at[r, :], h.at[r, :], in_sem.at[0, i]),
                pltpu.make_async_copy(dy_in.at[r, :], dy.at[r, :], in_sem.at[1, i]),
            )

        def start_load(i, carry):
            for copy in load(i):
                copy.start()
            return carry

        lax.fori_loop(0, GROUPS, start_load, 0)

        def to_twin(i):
            b = block_of(i)
            return remote(
                dx.at[block_rows(b, rows), pl.ds(pl.multiple_of((1 - c) * half, half), half)],
                core_buf.at[b], core_s.at[i], core_r.at[i], twin,
            )

        def p_across(i):
            b = block_of(i)
            return remote(
                core_buf.at[b, :, pl.ds(pl.multiple_of((1 - x) * piece, piece), piece)],
                px_buf.at[b], px_s.at[i], px_r.at[i], across,
            )

        def p_beside(j):
            return remote(px_buf.at[block_of(2 * j)], py_buf.at[j], py_s.at[j], py_r.at[j], beside)

        def q_beside(j):
            return remote(
                core_buf.at[block_of(2 * j), :, pl.ds(part, part)], qy_buf.at[j], qy_s.at[j], qy_r.at[j], beside
            )

        def q_across(j):
            return remote(
                qy_buf.at[j, :, pl.ds(pl.multiple_of((1 - x) * piece, piece), piece)],
                qx_buf.at[j], qx_s.at[j], qx_r.at[j], across,
            )

        def up(j, s):
            return remote(z_sum.at[s, j], lo_buf.at[s, j], z_s.at[0, s, j], z_r.at[0, s, j], device(z + 1, y, x, c))

        def down_z(j, s):
            return remote(z_sum.at[s, j], hi_buf.at[s, j], z_s.at[1, s, j], z_r.at[1, s, j], device(z - 1, y, x, c))

        def take_twin(i):
            to_twin(i).wait_recv()
            b = block_of(i)
            mine = core_buf.at[b]
            add_to(mine, mine, dx.at[block_rows(b, rows), pl.ds(pl.multiple_of(c * half, half), half)], 32)
            p_across(i).start()
            pl.when(lax.rem(i, 2) == 0)(lambda: q_beside(lax.div(i, 2)).start())

        def take_p_across(i):
            p_across(i).wait_recv()
            b = block_of(i)
            add_to(
                px_buf.at[b], px_buf.at[b],
                core_buf.at[b, :, pl.ds(pl.multiple_of(x * piece, piece), piece)],
            )

        def take_q_beside(j):
            q_beside(j).wait_recv()
            add_to(qy_buf.at[j], qy_buf.at[j], core_buf.at[block_of(2 * j + 1), :, pl.ds(part, part)])
            q_across(j).start()

        def take_q_across(j):
            q_across(j).wait_recv()
            add_to(
                z_sum.at[1, j], qx_buf.at[j], qy_buf.at[j, :, pl.ds(pl.multiple_of(x * piece, piece), piece)]
            )

        def take_p_beside(j):
            p_beside(j).wait_recv()
            add_to(z_sum.at[0, j], py_buf.at[j], px_buf.at[block_of(2 * j + 1)])

        def hop(j, k):
            zz = zz_of(j)

            def upward():
                for s in range(2):
                    if k > 0:
                        up(j, s).wait_recv()
                        add_to(z_sum.at[s, j], z_sum.at[s, j], lo_buf.at[s, j])
                    up(j, s).start()

            def downward():
                for s in range(2):
                    if k > 0:
                        down_z(j, s).wait_recv()
                        add_to(z_sum.at[s, j], z_sum.at[s, j], hi_buf.at[s, j])
                    down_z(j, s).start()

            pl.when((z < zz) & (z == k))(upward)
            pl.when((z > zz) & (NZ - 1 - z == k))(downward)

        def front(i):
            for copy in load(i):
                copy.wait()
            b = block_of(i)
            r = block_rows(b, rows)
            rows_h, rows_dy = h[r, :], dy[r, :]
            logits = dot(rows_h, router_ref[...], (1, 1))
            shifted = jnp.exp(logits - jnp.max(logits, axis=-1, keepdims=True))
            probs = shifted / jnp.sum(shifted, axis=-1, keepdims=True) * chosen_ref[r, :]
            lane = lax.broadcasted_iota(jnp.int32, probs.shape, 1)
            line = lax.broadcasted_iota(jnp.int32, (rows, 128), 1)
            found = jnp.zeros((rows, 128), jnp.float32)
            for expert in range(local):
                at, up_at = pl.ds(expert * hidden, hidden), pl.ds((local + expert) * hidden, hidden)
                gate = jnp.sum(jnp.where(lane == e * local + expert, probs, 0.0), axis=-1, keepdims=True)
                pre = dot(rows_h, gu_ref[:, at], (1, 0))
                scale = dot(rows_h, gu_ref[:, up_at], (1, 0))
                back = dot(rows_dy, down_ref[at, :], (1, 1))
                sigmoid = jax.nn.sigmoid(pre)
                swish = pre * sigmoid
                active = swish * scale
                gated[r, at] = (active * gate).astype(low)
                found = jnp.where(line == expert, jnp.sum(active * back, axis=-1, keepdims=True), found)
                back = back * gate
                dgu[r, at] = (back * scale * sigmoid * (1.0 + pre * (1.0 - sigmoid))).astype(low)
                dgu[r, up_at] = (back * swish).astype(low)
            gate_part[b] = jnp.transpose(found)[:8, :]

        def y_copy(i):
            return pltpu.make_async_copy(
                y_stage.at[lax.rem(i, 2)], y_out.at[block_rows(block_of(i), rows), :], y_sem.at[lax.rem(i, 2)]
            )

        def rear(i):
            r = block_rows(block_of(i), rows)
            slot = lax.rem(i, 2)

            def columns(k, carry):
                at = pl.ds(pl.multiple_of(k * wide, wide), wide)
                dx[r, at] = dot(dgu[r, :], gu_ref[at, :], (1, 1)).astype(low)
                return carry

            lax.fori_loop(0, width // wide, columns, 0)
            to_twin(i).start()
            pl.when(i >= 2)(lambda: y_copy(i - 2).wait())

            def y_columns(k, carry):
                at = pl.ds(pl.multiple_of(k * wide, wide), wide)
                y_stage[slot, :, at] = dot(gated[r, :], down_ref[:, at], (1, 0)).astype(low)
                return carry

            lax.fori_loop(0, width // wide, y_columns, 0)
            y_copy(i).start()

        tiles = width // piece // 4
        d_width = width // 4

        def gu_copies(n):
            slot = lax.rem(n, 2)
            at = pl.ds(pl.multiple_of(n * piece, piece), piece)
            return [
                pltpu.make_async_copy(
                    gu_stage.at[slot, :, pl.ds(k * hidden, hidden)],
                    (gate_w if k < local else up_w).at[k % local, at, :],
                    gu_sem.at[slot, k],
                )
                for k in range(2 * local)
            ]

        def d_copies(n):
            slot = lax.rem(n, 2)
            at = pl.ds(pl.multiple_of(n * d_width, d_width), d_width)
            return [
                pltpu.make_async_copy(
                    d_stage.at[slot, pl.ds(k * hidden, hidden), :], down_w.at[k, :, at], d_sem.at[slot, k]
                )
                for k in range(local)
            ]

        def each(copies, what):
            for copy in copies:
                getattr(copy, what)()

        def weight_grads(q):
            def tile(k, carry):
                n = q * tiles + k
                pl.when(n >= 2)(lambda: each(gu_copies(n - 2), "wait"))
                at = pl.ds(pl.multiple_of(n * piece, piece), piece)
                gu_stage[lax.rem(n, 2)] = dot(h[:, at], dgu[...], (0, 0))
                each(gu_copies(n), "start")
                return carry

            lax.fori_loop(0, tiles, tile, 0)
            pl.when(q >= 2)(lambda: each(d_copies(q - 2), "wait"))
            at = pl.ds(pl.multiple_of(q * d_width, d_width), d_width)
            d_stage[lax.rem(q, 2)] = dot(gated[...], dy[:, at], (0, 0))
            each(d_copies(q), "start")

        near = [
            remote(gate_part, gate_land.at[k], near_s.at[k], near_r.at[k], mates[k])
            for k in range(tensors - 1)
        ]

        def far(k):
            return remote(
                gate_land.at[tensors - 1, lax.rem(e + k, GROUPS)], gates_out.at[e],
                far_s.at[k - 1], far_r.at[k - 1], peers[k - 1],
            )

        def sum_near():
            for copy in near:
                copy.wait_recv()
            total = gate_part[...]
            for k in range(tensors - 1):
                total = total + gate_land[k]
            gate_land[tensors - 1] = total
            for k in range(1, GROUPS):
                far(k).start()
            gates_out[e] = gate_land[tensors - 1, e]

        def step(i, carry):
            j_even, j_odd = lax.div(i, 2) - 1, lax.div(i - 1, 2) - 1
            even = lax.rem(i, 2) == 0
            pl.when(i < GROUPS)(lambda: front(i))
            pl.when((i >= 1) & (i <= GROUPS))(lambda: take_twin(i - 1))
            pl.when(even & (i >= 2) & (i <= GROUPS))(lambda: take_q_beside(j_even))

            def late():
                take_p_across(i - 2)
                take_q_across(j_odd)

            pl.when((lax.rem(i, 2) == 1) & (i >= 3) & (i <= GROUPS + 1))(late)
            pl.when(i == GROUPS)(lambda: each(near, "start"))
            pl.when(i == GROUPS + 1)(sum_near)
            pl.when(i < GROUPS)(lambda: rear(i))
            pl.when(i >= GROUPS)(lambda: weight_grads(i - GROUPS))

            def pass_p():
                take_p_across(i - 2)
                p_beside(j_even).start()

            pl.when(even & (i >= 2) & (i <= GROUPS))(pass_p)

            def join():
                take_p_beside(j_odd)
                hop(j_odd, 0)

            pl.when((lax.rem(i, 2) == 1) & (i >= 3) & (i <= GROUPS + 1))(join)
            pl.when(even & (i >= 4) & (i <= GROUPS + 2))(lambda: hop(j_even - 1, 1))
            pl.when((lax.rem(i, 2) == 1) & (i >= 5) & (i <= GROUPS + 3))(lambda: hop(j_odd - 1, 2))
            return carry

        lax.fori_loop(0, steps, step, 0)

        def columns_of(s, xx, cc):
            return pl.ds(pl.multiple_of(cc * half + s * part + xx * piece, piece), piece)

        mine = jnp.where(z == 3, 0, jnp.where(z == 0, 1, jnp.where(z == 2, 2, 3)))
        for s in range(2):
            def below(s=s):
                up(mine, s).wait_recv()
                add_to(z_sum.at[s, mine], z_sum.at[s, mine], lo_buf.at[s, mine])

            def above(s=s):
                down_z(mine, s).wait_recv()
                add_to(z_sum.at[s, mine], z_sum.at[s, mine], hi_buf.at[s, mine])

            pl.when(z > 0)(below)
            pl.when(z < NZ - 1)(above)
            own = dh_out.at[:, columns_of(s, x, c)]

            def keep(k, carry, s=s, own=own):
                r = pl.ds(pl.multiple_of(k * 64, 64), 64)
                own[r, :] = z_sum[s, mine, r, :]
                return carry

            lax.fori_loop(0, rows // 64, keep, 0)
            remote(own, own, end_s.at[0, s], end_r.at[0, s], across).start()
            remote(own, own, end_s.at[1, s], end_r.at[1, s], twin).start()
        for s in range(2):
            there = dh_out.at[:, columns_of(s, 1 - x, c)]
            remote(there, there, end_s.at[0, s], end_r.at[0, s], across).wait_recv()
            remote(there, there, end_s.at[2, s], end_r.at[2, s], twin).start()
        for s in range(2):
            for k, xx in ((1, x), (2, 1 - x)):
                there = dh_out.at[:, columns_of(s, xx, 1 - c)]
                remote(there, there, end_s.at[k, s], end_r.at[k, s], twin).wait_recv()
            for k, target in ((0, across), (1, twin), (2, twin)):
                there = dh_out.at[:, columns_of(s, 1 - x if k == 2 else x, c)]
                remote(there, there, end_s.at[k, s], end_r.at[k, s], target).wait_send()
        for k in range(1, GROUPS):
            there = gates_out.at[lax.rem(e + GROUPS - k, GROUPS)]
            remote(there, there, far_s.at[k - 1], far_r.at[k - 1], peers[k - 1]).wait_recv()
            far(k).wait_send()
        each(near, "wait_send")

        def drain(i, carry):
            to_twin(i).wait_send()
            p_across(i).wait_send()
            return carry

        lax.fori_loop(0, GROUPS, drain, 0)

        def drain_pair(j, carry):
            p_beside(j).wait_send()
            q_beside(j).wait_send()
            q_across(j).wait_send()
            for s in range(2):
                pl.when(z < zz_of(j))(lambda s=s: up(j, s).wait_send())
                pl.when(z > zz_of(j))(lambda s=s: down_z(j, s).wait_send())
            return carry

        lax.fori_loop(0, NZ, drain_pair, 0)
        for k in range(2):
            y_copy(GROUPS - 2 + k).wait()
            each(gu_copies(4 * tiles - 2 + k), "wait")
            each(d_copies(2 + k), "wait")

    shape = jax.ShapeDtypeStruct
    dma = pltpu.SemaphoreType.DMA
    f32 = jnp.float32
    return pl.pallas_call(
        kernel,
        out_shape=(
            shape((tokens, width), low),
            shape((rows, width), low),
            shape((GROUPS, 8, rows), f32),
            shape((local, width, hidden), f32),
            shape((local, width, hidden), f32),
            shape((local, hidden, width), f32),
        ),
        in_specs=[HBM, HBM, VMEM, VMEM, VMEM, VMEM],
        out_specs=(HBM, VMEM, VMEM, HBM, HBM, HBM),
        scratch_shapes=[
            pltpu.VMEM((tokens, width), low),
            pltpu.VMEM((tokens, width), low),
            pltpu.VMEM((tokens, units), low),
            pltpu.VMEM((tokens, 2 * units), low),
            pltpu.VMEM((tokens, width), low),
            pltpu.VMEM((2, rows, width), low),
            pltpu.VMEM((2, piece, 2 * units), f32),
            pltpu.VMEM((2, units, width // 4), f32),
            pltpu.VMEM((GROUPS, rows, half), low),
            pltpu.VMEM((GROUPS, rows, piece), low),
            pltpu.VMEM((NZ, rows, piece), low),
            pltpu.VMEM((NZ, rows, part), low),
            pltpu.VMEM((NZ, rows, piece), low),
            pltpu.VMEM((2, NZ, rows, piece), low),
            pltpu.VMEM((2, NZ, rows, piece), low),
            pltpu.VMEM((2, NZ, rows, piece), low),
            pltpu.VMEM((GROUPS, 8, rows), f32),
            pltpu.VMEM((tensors, GROUPS, 8, rows), f32),
            dma((2, GROUPS)), dma((2,)), dma((2, 2 * local)), dma((2, local)),
            dma((GROUPS,)), dma((GROUPS,)), dma((GROUPS,)), dma((GROUPS,)),
            dma((NZ,)), dma((NZ,)), dma((NZ,)), dma((NZ,)), dma((NZ,)), dma((NZ,)),
            dma((2, 2, NZ)), dma((2, 2, NZ)),
            dma((tensors - 1,)), dma((tensors - 1,)), dma((GROUPS - 1,)), dma((GROUPS - 1,)),
            dma((3, 2)), dma((3, 2)),
        ],
        compiler_params=comm_params(collective_id, 62),
        cost_estimate=cost(80),
        name="expert_layer",
    )(hidden_all, grad_out_all, gate_up, down, router_t, chosen_all)


def exchange_rows(value, part_ref, land_ref, send_sem, recv_sem, mates):
    rows = value.shape[0]
    line = lax.broadcasted_iota(jnp.int32, (rows, 128), 1)
    part_ref[...] = jnp.transpose(jnp.where(line == 0, value, 0.0))[:8, :]
    for k, mate in enumerate(mates):
        remote(part_ref, land_ref.at[k], send_sem.at[k], recv_sem.at[k], mate).start()


def exchanged_rows(part_ref, land_ref, send_sem, recv_sem, mates):
    total = part_ref[...]
    for k, mate in enumerate(mates):
        remote(part_ref, land_ref.at[k], send_sem.at[k], recv_sem.at[k], mate).wait_recv()
    for k in range(len(mates)):
        total = total + land_ref[k]
    rows = part_ref.shape[1]
    tall = jnp.concatenate([total, jnp.zeros((120, rows), jnp.float32)], axis=0)
    return jnp.transpose(tall)[:, :1]


def drain_rows(part_ref, land_ref, send_sem, recv_sem, mates):
    for k, mate in enumerate(mates):
        remote(part_ref, land_ref.at[k], send_sem.at[k], recv_sem.at[k], mate).wait_send()


def turn(value, cosine, sine):
    return value * cosine + pltpu.roll(value, HEAD // 2, 1) * sine


def project(tokens, w_qkv, smalls, cosine, sine, collective_id):
    rows, width = tokens.shape
    parts, depth, columns = w_qkv.shape
    heads = columns // HEAD
    tensors = NX * NC
    back = WINDOW // rows
    low, f32 = jnp.bfloat16, jnp.float32
    QUERY, KEY, VALUE, SMALL = 0, 1, 2, 3

    def kernel(
        tok_ref, w_ref, small_ref, cos_ref, sin_ref,
        w_all, small_all, h1_ref, raw_ref, scale_ref, q_ref, context,
        own_w, weights, total, part_k, land_k, part_q, land_q,
        send_sem, recv_sem, out_sem, small_sem, ks_s, ks_r, qs_s, qs_r, c_s, c_r,
    ):
        z, y, x, c = place()
        e, t = lax.axis_index("expert"), lax.axis_index("tensor")
        mates = [(e, lax.rem(t + k, tensors)) for k in range(1, tensors)]
        beside, above = device(z, 1 - y, x, c), device(z + 1, y, x, c)
        views = [
            lambda b: weights.at[QUERY, block_rows(b, depth), :],
            lambda b: weights.at[KEY, block_rows(b, depth), :],
            lambda b: weights.at[VALUE, block_rows(b, depth), :],
            lambda b: small_all.at[b],
        ]
        line = LineGather(
            [SMALL, VALUE, KEY, QUERY], [own_w.at[0], own_w.at[1], own_w.at[2], small_ref], views,
            send_sem, recv_sem,
        )
        greet(line.partners() + [(mate, None) for mate in mates])
        line.start(SMALL, 0)
        for part in (VALUE, KEY, QUERY):
            def cast(i, carry, part=part):
                r = pl.ds(pl.multiple_of(i * 32, 32), 32)
                own_w[part, r, :] = w_ref[part, r, :].astype(low)
                return carry

            lax.fori_loop(0, depth // 32, cast, 0)
            if part != QUERY:
                line.start(part, 0)

        def square(i, carry):
            r = pl.ds(pl.multiple_of(i * 32, 32), 32)
            value = tok_ref[r, :].astype(f32)
            scale_ref[r, 0:1] = lax.rsqrt(jnp.mean(value * value, axis=-1, keepdims=True) + EPS)
            return carry

        lax.fori_loop(0, rows // 32, square, 0)
        total[...] = jnp.zeros_like(total)
        own_small = pltpu.make_async_copy(small_ref, small_all.at[line.block(0)], small_sem)
        own_small.start()

        def use(stream, rel):
            b = line.block(rel)
            at = pl.ds(pl.multiple_of(b * depth, depth), depth)
            if stream == SMALL:
                gain = small_ref[0:1, :] if rel == 0 else small_all[b, 0:1, :]
                h1_ref[:, at] = (tok_ref[:, at].astype(f32) * scale_ref[:, 0:1] * gain).astype(low)
                return
            block = own_w[stream] if rel == 0 else weights[stream, block_rows(b, depth), :]
            total[stream] += dot(h1_ref[:, at], block, (1, 0))

        def event(stream, rel):
            def body():
                line.arrive(stream, rel)
                if rel < 7:
                    marks = len(line.pending)
                    line.start(stream, rel)
                    late = line.pending[marks:]
                    del line.pending[marks:]
                    line.finish_later(late, rel)
                use(stream, rel)
            run_if(line.exists(rel), body)

        use(SMALL, 0)
        use(VALUE, 0)
        own_small.wait()
        use(KEY, 0)
        early, late = [7, 1, 4, 8, 11, 2, 5], [9, 12, 3, 6, 10, 13]
        for rel in early:
            event(SMALL, rel)
            event(VALUE, rel)
        line.start(QUERY, 0)
        for rel in late:
            event(SMALL, rel)
            event(VALUE, rel)

        def context_copy(which, k):
            if k == 2:
                source, target = 0, above
            elif k == 4:
                source, target = 2, above
            else:
                source, target = jnp.where(y == 0, k - 1, k + 1), beside
            return remote(
                context.at[source, which], context.at[k, which], c_s.at[which, k], c_r.at[which, k], target
            )

        sends = {2: z < NZ - 1, 4: (z >= 1) & (z < NZ - 1), 1: (y == 0) | (z >= 1), 3: z >= 1 + y}
        takes = {2: z >= 1, 4: z >= 2, 1: (y == 1) | (z >= 1), 3: z >= 2 - y}

        def context_send(which, k):
            run_if(sends[k], lambda: context_copy(which, k).start())

        def context_take(which, k):
            run_if(takes[k], lambda: context_copy(which, k).wait_recv())

        for k in range(1, back + 1):
            def clear(k=k):
                context[k] = jnp.zeros_like(context[k])
            run_if(jnp.logical_not(takes[k]), clear)

        context[0, 1] = total[VALUE].astype(low)
        context_send(1, 2)
        run_if(y == 0, lambda: context_copy(1, 1).start())
        for rel in early:
            event(KEY, rel)
        for rel in late:
            event(KEY, rel)
        key_raw = total[KEY]
        raw_ref[1] = key_raw
        exchange_rows(jnp.sum(key_raw * key_raw, axis=-1, keepdims=True), part_k, land_k, ks_s, ks_r, mates)
        use(QUERY, 0)
        for rel in early[:3]:
            event(QUERY, rel)

        key_scale = lax.rsqrt(exchanged_rows(part_k, land_k, ks_s, ks_r, mates) / width + EPS)
        scale_ref[:, 2:3] = key_scale
        slices = HEAD // GROUPS
        gains = []
        for which in range(2):
            per_head = []
            for head in range(heads):
                start = (which * heads + head) * slices
                per_head.append(
                    jnp.concatenate([small_all[b, 2:3, start : start + slices] for b in range(GROUPS)], axis=1)
                )
            gains.append(per_head)

        def rotated(which, scale, store):
            for head in range(heads):
                at = pl.ds(head * HEAD, HEAD)
                value = total[which, :, at] * scale * gains[which][head]
                store(at, turn(value, cos_ref[...], sin_ref[...]).astype(low))

        def store_key(at, value):
            context[0, 0, :, at] = value

        rotated(KEY, key_scale, store_key)
        context_send(0, 2)
        run_if(y == 0, lambda: context_copy(0, 1).start())

        def relay_two(which):
            context_take(which, 2)
            context_send(which, 4)
            run_if((y == 1) & (z >= 1), lambda: context_copy(which, 1).start())
            run_if((y == 0) & sends[3], lambda: context_copy(which, 3).start())

        def relay_four(which):
            context_take(which, 4)
            run_if((y == 1) & sends[3], lambda: context_copy(which, 3).start())

        relay_two(1)
        for rel in early[3:]:
            event(QUERY, rel)
        relay_four(1)
        for rel in late[:4]:
            event(QUERY, rel)
        relay_two(0)
        for rel in late[4:]:
            event(QUERY, rel)
        query_raw = total[QUERY]
        raw_ref[0] = query_raw
        exchange_rows(jnp.sum(query_raw * query_raw, axis=-1, keepdims=True), part_q, land_q, qs_s, qs_r, mates)
        for part in range(parts):
            weights[part, block_rows(line.block(0), depth), :] = own_w[part]
        keep = pltpu.make_async_copy(weights, w_all, out_sem)
        keep.start()
        relay_four(0)
        query_scale = lax.rsqrt(exchanged_rows(part_q, land_q, qs_s, qs_r, mates) / width + EPS)
        scale_ref[:, 1:2] = query_scale

        def store_query(at, value):
            q_ref[:, at] = value

        rotated(QUERY, query_scale, store_query)
        for which in (1, 0):
            for k in (1, 3):
                context_take(which, k)
        line.finish()
        for which in range(2):
            for k in range(1, back + 1):
                run_if(sends[k], lambda which=which, k=k: context_copy(which, k).wait_send())
        drain_rows(part_k, land_k, ks_s, ks_r, mates)
        drain_rows(part_q, land_q, qs_s, qs_r, mates)
        keep.wait()

    shape, dma = jax.ShapeDtypeStruct, pltpu.SemaphoreType.DMA
    return pl.pallas_call(
        kernel,
        out_shape=(
            shape((parts, depth * GROUPS, columns), low),
            shape((GROUPS,) + smalls.shape, f32),
            shape((rows, width), low),
            shape((2, rows, columns), f32),
            shape((rows, 128), f32),
            shape((rows, columns), low),
            shape((back + 1, 2, rows, columns), low),
        ),
        in_specs=[VMEM] * 5,
        out_specs=(HBM,) + (VMEM,) * 6,
        scratch_shapes=[
            pltpu.VMEM((parts, depth, columns), low),
            pltpu.VMEM((parts, depth * GROUPS, columns), low),
            pltpu.VMEM((parts, rows, columns), f32),
            pltpu.VMEM((8, rows), f32),
            pltpu.VMEM((tensors - 1, 8, rows), f32),
            pltpu.VMEM((8, rows), f32),
            pltpu.VMEM((tensors - 1, 8, rows), f32),
            dma((4, 7, 3)), dma((4, 14)), dma, dma,
            dma((tensors - 1,)), dma((tensors - 1,)), dma((tensors - 1,)), dma((tensors - 1,)),
            dma((2, back + 1)), dma((2, back + 1)),
        ],
        compiler_params=comm_params(collective_id, 48),
        cost_estimate=cost(100),
        name="project",
    )(tokens, w_qkv, smalls, cosine, sine)


def attend(query, context, segment_query, segment_keys, tokens, out_low, gain, collective_id):
    rows, columns = query.shape
    width = tokens.shape[1]
    blocks = context.shape[0]
    heads = columns // HEAD
    half, quarter = width // 2, width // 4
    low, f32 = jnp.bfloat16, jnp.float32

    def kernel(
        q_ref, context_ref, sq_ref, sk_ref, tok_ref, out_ref, gain_ref,
        o_ref, lse_ref, x1_ref, h2_ref, scale_ref,
        part, full, core_buf, x_buf, send_sem, recv_sem,
    ):
        z, y, x, c = place()
        across, twin = device(z, y, 1 - x, c), device(z, y, x, 1 - c)
        greet([(across, None), (twin, None)])
        row = lax.broadcasted_iota(jnp.int32, (rows, rows), 0)
        column = lax.broadcasted_iota(jnp.int32, (rows, rows), 1)
        allowed = []
        for k in range(blocks):
            distance = row - column + k * rows
            allowed.append(
                (sq_ref[...] == sk_ref[k : k + 1, :]) & (distance >= 0) & (distance < WINDOW)
            )
        line = lax.broadcasted_iota(jnp.int32, (rows, 128), 1)
        lse = jnp.zeros((rows, 128), f32)
        for head in range(heads):
            at = pl.ds(head * HEAD, HEAD)
            scores = [
                jnp.where(
                    allowed[k], dot(q_ref[:, at], context_ref[k, 0, :, at], (1, 1)) * HEAD ** (-0.5), -1e30
                )
                for k in range(blocks)
            ]
            largest = scores[0]
            for k in range(1, blocks):
                largest = jnp.maximum(largest, scores[k])
            largest = jnp.max(largest, axis=-1, keepdims=True)
            weights = [jnp.exp(s - largest) for s in scores]
            amount = weights[0]
            for k in range(1, blocks):
                amount = amount + weights[k]
            amount = jnp.sum(amount, axis=-1, keepdims=True)
            inverse = 1.0 / amount
            value = jnp.zeros((rows, HEAD), f32)
            for k in range(blocks):
                value = value + dot((weights[k] * inverse).astype(low), context_ref[k, 1, :, at], (1, 0))
            o_ref[:, at] = value.astype(low)
            lse = jnp.where(line == head, largest + jnp.log(amount), lse)
        lse_ref[...] = lse

        def half_of(cc):
            return pl.ds(pl.multiple_of(cc * half, half), half)

        def fill(cc):
            def body(k, carry):
                at = pl.ds(pl.multiple_of(cc * half + k * quarter, quarter), quarter)
                part[:, at] = dot(o_ref[...], out_ref[:, at], (1, 0)).astype(low)
                return carry

            lax.fori_loop(0, 2, body, 0)

        fill(1 - c)
        group_sum(part, full, core_buf, x_buf, send_sem, recv_sem, lambda: fill(c))

        def norm(i, carry):
            r = pl.ds(pl.multiple_of(i * 32, 32), 32)
            value = tok_ref[r, :].astype(f32) + full[r, :].astype(f32)
            scale = lax.rsqrt(jnp.mean(value * value, axis=-1, keepdims=True) + EPS)
            x1_ref[r, :] = value
            scale_ref[r, :] = jnp.broadcast_to(scale, (32, 128))
            h2_ref[r, :] = (value * scale * gain_ref[...]).astype(low)
            return carry

        lax.fori_loop(0, rows // 32, norm, 0)

    shape, dma = jax.ShapeDtypeStruct, pltpu.SemaphoreType.DMA
    return pl.pallas_call(
        kernel,
        out_shape=(
            shape((rows, columns), low),
            shape((rows, 128), f32),
            shape((rows, width), f32),
            shape((rows, width), low),
            shape((rows, 128), f32),
        ),
        in_specs=[VMEM] * 7,
        out_specs=(VMEM,) * 5,
        scratch_shapes=[
            pltpu.VMEM((rows, width), low),
            pltpu.VMEM((rows, width), low),
            pltpu.VMEM((rows, half), low),
            pltpu.VMEM((rows, quarter), low),
            dma((5,)), dma((5,)),
        ],
        compiler_params=comm_params(collective_id, 40),
        cost_estimate=cost(40),
        name="attend",
    )(query, context, segment_query, segment_keys, tokens, out_low, gain)


def attend_back(
    grad_hidden, grad_probs, router_t, hidden_two, residual, scale_two, gain_two, out_grad,
    query, context, segment_query, segment_keys, attended, log_sums, raw, scales, qk_gains,
    cosine, sine, hidden_one, tokens, gain_one, qkv_low, out_low, collective_id,
):
    rows, width = tokens.shape
    columns = query.shape[1]
    heads = columns // HEAD
    experts = router_t.shape[0]
    blocks = context.shape[0]
    depth = width // GROUPS
    small_rows = 8 + experts
    tensors = NX * NC
    half, quarter = width // 2, width // 4
    low, f32 = jnp.bfloat16, jnp.float32
    QUERY, KEY, VALUE, OUT, SMALL = 0, 1, 2, 3, 4

    def kernel(
        dh_ref, gates_ref, router_ref, h2_ref, x1_ref, s2_ref, g2_ref, dy_ref,
        q_ref, context_ref, sq_ref, sk_ref, o_ref, lse_ref, raw_ref, scale_ref, qkg_ref,
        cos_ref, sin_ref, h1_ref, tok_ref, g1_ref, w_hbm, out_ref,
        tok_grad, qkv_sum, out_sum, small_sum,
        weights, dx1, da, do, dot_sums, dq, dkv, proj, send_kv, land_y, land_z,
        part, full, core_buf, x_buf, small, line_sum,
        main_buf, out_buf, small_buf, part_k, land_k, part_q, land_q,
        w_sem, y_s, y_r, z_s, z_r, group_s, group_r, ks_s, ks_r, qs_s, qs_r, line_s, line_r,
    ):
        z, y, x, c = place()
        e, t = lax.axis_index("expert"), lax.axis_index("tensor")
        mates = [(e, lax.rem(t + k, tensors)) for k in range(1, tensors)]
        beside, below = device(z, 1 - y, x, c), device(z - 1, y, x, c)
        fetch = pltpu.make_async_copy(w_hbm, weights, w_sem)
        fetch.start()

        def own_part(s, b):
            if s == SMALL:
                return small[b]
            at = pl.ds(pl.multiple_of(b * depth, depth), depth)
            if s == OUT:
                return dot(o_ref[...], da[:, at], (0, 0))
            return dot(h1_ref[:, at], proj[s], (0, 0))

        def slot(kind):
            def view(s, zz):
                if s == SMALL:
                    return small_buf.at[kind, zz]
                return out_buf.at[kind, zz] if s == OUT else main_buf.at[kind, zz, s]
            return view

        line = LineReduce([], lambda s, zz, yy: slot(3)(s, zz), slot(0), slot(1), slot(2), line_s, line_r)
        greet(line.partners() + [(mate, None) for mate in mates])

        grad_probs = gates_ref[...]
        logits = dot(h2_ref[...], router_ref[...], (1, 1))
        shifted = jnp.exp(logits - jnp.max(logits, axis=-1, keepdims=True))
        probs = shifted / jnp.sum(shifted, axis=-1, keepdims=True)
        grad_logits = probs * (grad_probs - jnp.sum(probs * grad_probs, axis=-1, keepdims=True))
        tall = jnp.transpose(
            jnp.concatenate([grad_logits, jnp.zeros((rows, 128 - experts), f32)], axis=1)
        )
        grad_logits = grad_logits.astype(low)
        tall = tall.astype(low)
        for b in range(GROUPS):
            small[b] = jnp.zeros_like(small[b])
            small[b, 8 : 8 + experts, :] = dot(tall, h2_ref[:, pl.ds(b * depth, depth)], (1, 0))[:experts]
        dx1[...] = dot(grad_logits, router_ref[...], (1, 0))
        line_sum[...] = jnp.zeros_like(line_sum)

        def norm_two(i, carry):
            r = pl.ds(pl.multiple_of(i * 32, 32), 32)
            grad = dh_ref[r, :].astype(f32) + dx1[r, :]
            value, scale = x1_ref[r, :], s2_ref[r, 0:1]
            line_sum[0:1, :] += jnp.sum(grad * (value * scale), axis=0, keepdims=True)
            grad = grad * g2_ref[...]
            inner = jnp.mean(grad * value, axis=-1, keepdims=True)
            result = dy_ref[r, :].astype(f32) + scale * grad - value * (scale * scale * scale) * inner
            dx1[r, :] = result
            da[r, :] = result.astype(low)
            return carry

        lax.fori_loop(0, rows // 32, norm_two, 0)

        do[...] = dot(da[...], out_ref[...], (1, 1)).astype(low)
        wide = lax.broadcasted_iota(jnp.int32, (rows, 128), 1)
        sums = jnp.zeros((rows, 128), f32)
        for head in range(heads):
            at = pl.ds(head * HEAD, HEAD)
            inner = jnp.sum(do[:, at].astype(f32) * o_ref[:, at].astype(f32), axis=-1, keepdims=True)
            sums = jnp.where(wide == head, inner, sums)
        dot_sums[...] = sums
        dq[...] = jnp.zeros_like(dq)
        row = lax.broadcasted_iota(jnp.int32, (rows, rows), 0)
        column = lax.broadcasted_iota(jnp.int32, (rows, rows), 1)

        def attention_block(k):
            distance = row - column + k * rows
            allowed = (sq_ref[...] == sk_ref[k : k + 1, :]) & (distance >= 0) & (distance < WINDOW)
            for head in range(heads):
                at = pl.ds(head * HEAD, HEAD)
                queries, keys, values = q_ref[:, at], context_ref[k, 0, :, at], context_ref[k, 1, :, at]
                scores = dot(queries, keys, (1, 1)) * HEAD ** (-0.5)
                weight = jnp.where(allowed, jnp.exp(scores - lse_ref[:, head : head + 1]), 0.0)
                grad_weight = dot(do[:, at], values, (1, 1))
                grad_score = (
                    weight * (grad_weight - dot_sums[:, head : head + 1]) * HEAD ** (-0.5)
                ).astype(low)
                dq[:, at] += dot(grad_score, keys, (1, 0))
                dkv[k, 0, :, at] = dot(grad_score, queries, (0, 0))
                dkv[k, 1, :, at] = dot(weight.astype(low), do[:, at], (0, 0))

        exists = {0: None, 1: (y == 1) | (z >= 1), 2: z >= 1, 3: z >= 2 - y, 4: z >= 2}
        comes = {1: (y == 0) | (z >= 1), 3: z >= 1 + y}

        def kv_copy(which, k):
            if k in (1, 3):
                landing, target = land_y.at[k // 2, which], beside
                return remote(send_kv.at[k - 1, which], landing, y_s.at[k // 2, which], y_r.at[k // 2, which], target)
            landing = land_z.at[k // 2 - 1, which]
            return remote(
                send_kv.at[k - 1, which], landing, z_s.at[k // 2 - 1, which], z_r.at[k // 2 - 1, which], below
            )

        def kv_send(which, k):
            send_kv[k - 1, which] = dkv[k, which].astype(low)
            kv_copy(which, k).start()

        def merge(into, which, landed):
            add_to(dkv.at[into, which], dkv.at[into, which], landed, 32)

        for k in (3, 1, 4, 2, 0):
            def one(k=k):
                attention_block(k)
                if k in (1, 3):
                    kv_send(1, k)
                    kv_send(0, k)
            run_if(exists[k], one)

        def take_three(which):
            def land():
                kv_copy(which, 3).wait_recv()
                pl.when(y == 1)(lambda: merge(4, which, land_y.at[1, which]))
                pl.when(y == 0)(lambda: merge(2, which, land_y.at[1, which]))
            run_if(comes[3], land)
            run_if(exists[4], lambda: kv_send(which, 4))

        def take_one(which):
            def land():
                kv_copy(which, 1).wait_recv()
                pl.when(y == 1)(lambda: merge(2, which, land_y.at[0, which]))
                pl.when(y == 0)(lambda: merge(0, which, land_y.at[0, which]))
            run_if(comes[1], land)

        def take_four(which):
            def land():
                kv_copy(which, 4).wait_recv()
                merge(2, which, land_z.at[1, which])
            run_if((z >= 1) & (z < NZ - 1), land)
            run_if(exists[2], lambda: kv_send(which, 2))

        def take_two(which):
            def land():
                kv_copy(which, 2).wait_recv()
                merge(0, which, land_z.at[0, which])
            run_if(z < NZ - 1, land)

        def unturn(which, grad_of):
            inner = jnp.zeros((rows, 1), f32)
            for head in range(heads):
                at = pl.ds(head * HEAD, HEAD)
                grad = turn(grad_of(at), cos_ref[...], -sin_ref[...])
                value = raw_ref[which, :, at]
                line_sum[1 + which : 2 + which, at] = jnp.sum(
                    grad * (value * scale_ref[:, 1 + which : 2 + which]), axis=0, keepdims=True
                )
                grad = grad * qkg_ref[which : which + 1, at]
                dkv[1 + which, 0, :, at] = grad
                inner = inner + jnp.sum(grad * value, axis=-1, keepdims=True)
            return inner

        def denorm(which, inner):
            scale = scale_ref[:, 1 + which : 2 + which]
            rest = scale * scale * scale * inner / width
            for head in range(heads):
                at = pl.ds(head * HEAD, HEAD)
                proj[which, :, at] = (
                    scale * dkv[1 + which, 0, :, at] - raw_ref[which, :, at] * rest
                ).astype(low)

        def send_beside(s):
            for zz in Z_ORDER:
                buffer = slot(3)(s, zz)
                buffer[...] = own_part(s, zz * NY + 1 - y).astype(buffer.dtype)
                line.to_y(s, zz)

        take_three(1)
        take_three(0)
        take_one(1)
        take_one(0)
        take_four(1)
        take_four(0)
        exchange_rows(unturn(QUERY, lambda at: dq[:, at]), part_q, land_q, qs_s, qs_r, mates)
        take_two(1)
        proj[VALUE] = dkv[0, 1].astype(low)
        denorm(QUERY, exchanged_rows(part_q, land_q, qs_s, qs_r, mates))
        send_beside(QUERY)
        send_beside(VALUE)
        take_two(0)
        exchange_rows(unturn(KEY, lambda at: dkv[0, 0, :, at]), part_k, land_k, ks_s, ks_r, mates)
        denorm(KEY, exchanged_rows(part_k, land_k, ks_s, ks_r, mates))
        send_beside(KEY)
        send_beside(OUT)
        fetch.wait()

        def half_of(cc):
            def body(i, carry):
                at = pl.ds(pl.multiple_of(cc * half + i * quarter, quarter), quarter)
                value = dot(proj[0], weights[0, at, :], (1, 1))
                for s in (1, 2):
                    value = value + dot(proj[s], weights[s, at, :], (1, 1))
                part[:, at] = value.astype(low)
                return carry

            lax.fori_loop(0, 2, body, 0)

        stages = group_stages(part, full, core_buf, x_buf, group_s, group_r)
        half_of(1 - c)
        stages[0]()
        half_of(c)
        stages[1]()

        def hop(s, zz, k):
            def upward():
                if k > 0:
                    line.take(s, zz, 1)
                line.copy(s, zz, 1).start()

            def downward():
                if k > 0:
                    line.take(s, zz, 2)
                line.copy(s, zz, 2).start()

            if k < zz:
                run_if((z < zz) & (z == k), upward)
            if NZ - 1 - k > zz:
                run_if((z > zz) & (NZ - 1 - z == k), downward)

        def receive(s, zz):
            line.copy(s, zz, 0).wait_recv()
            buffer = slot(0)(s, zz)
            buffer[...] = (buffer[...].astype(f32) + own_part(s, zz * NY + y)).astype(buffer.dtype)

        units = []

        def run_units(s):
            for zz in Z_ORDER:
                receive(s, zz)
                hop(s, zz, 0)
                units.append((s, zz))
                for k in (1, 2):
                    if len(units) > k:
                        hop(*units[-1 - k], k)

        def norm_one(i, carry):
            r = pl.ds(pl.multiple_of(i * 32, 32), 32)
            grad, value, scale = full[r, :].astype(f32), tok_ref[r, :].astype(f32), scale_ref[r, 0:1]
            line_sum[3:4, :] += jnp.sum(grad * (value * scale), axis=0, keepdims=True)
            grad = grad * g1_ref[...]
            inner = jnp.mean(grad * value, axis=-1, keepdims=True)
            tok_grad[r, :] = (
                dx1[r, :] + scale * grad - value * (scale * scale * scale) * inner
            ).astype(low)
            return carry

        run_units(QUERY)
        stages[2]()
        run_units(VALUE)
        stages[3]()
        stages[4]()
        lax.fori_loop(0, rows // 32, norm_one, 0)
        for b in range(GROUPS):
            at = pl.ds(b * depth, depth)
            small[b, 0:1, :] = line_sum[3:4, at]
            small[b, 1:2, :] = line_sum[0:1, at]
            for which in range(2):
                for k in range(columns // depth):
                    small[b, 2 + 2 * which + k : 3 + 2 * which + k, :] = line_sum[
                        1 + which : 2 + which, pl.ds(k * depth, depth)
                    ]
        send_beside(SMALL)
        run_units(KEY)
        run_units(SMALL)
        run_units(OUT)
        hop(*units[-1], 1)
        hop(*units[-2], 2)
        hop(*units[-1], 2)

        def done(s, total):
            target = qkv_sum.at[s] if s < OUT else (out_sum if s == OUT else small_sum)
            target[...] = total[...].astype(f32)

        line.streams = [QUERY, VALUE, KEY, SMALL, OUT]
        line.home(done)
        line.finish()
        for which in range(2):
            for k in (1, 2, 3, 4):
                run_if(exists[k], lambda which=which, k=k: kv_copy(which, k).wait_send())
        drain_rows(part_k, land_k, ks_s, ks_r, mates)
        drain_rows(part_q, land_q, qs_s, qs_r, mates)

    shape, dma, vmem = jax.ShapeDtypeStruct, pltpu.SemaphoreType.DMA, pltpu.VMEM
    return pl.pallas_call(
        kernel,
        out_shape=(
            shape((rows, width), low),
            shape((3, depth, columns), f32),
            shape((columns, depth), f32),
            shape((small_rows, depth), f32),
        ),
        in_specs=[VMEM] * 22 + [HBM, VMEM],
        out_specs=(VMEM,) * 4,
        scratch_shapes=[
            vmem(qkv_low.shape, low),
            vmem((rows, width), f32),
            vmem((rows, width), low),
            vmem((rows, columns), low),
            vmem((rows, 128), f32),
            vmem((rows, columns), f32),
            vmem((blocks, 2, rows, columns), f32),
            vmem((3, rows, columns), low),
            vmem((blocks - 1, 2, rows, columns), low),
            vmem((2, 2, rows, columns), low),
            vmem((2, 2, rows, columns), low),
            vmem((rows, width), low),
            vmem((rows, width), low),
            vmem((rows, half), low),
            vmem((rows, quarter), low),
            vmem((GROUPS, small_rows, depth), f32),
            vmem((8, width), f32),
            vmem((4, NZ, 3, depth, columns), low),
            vmem((4, NZ, columns, depth), low),
            vmem((4, NZ, small_rows, depth), f32),
            vmem((8, rows), f32),
            vmem((tensors - 1, 8, rows), f32),
            vmem((8, rows), f32),
            vmem((tensors - 1, 8, rows), f32),
            dma, dma((2, 2)), dma((2, 2)), dma((2, 2)), dma((2, 2)), dma((5,)), dma((5,)),
            dma((tensors - 1,)), dma((tensors - 1,)), dma((tensors - 1,)), dma((tensors - 1,)),
            dma((5, NZ, 3)), dma((5, NZ, 3)),
        ],
        compiler_params=comm_params(collective_id, 62),
        cost_estimate=cost(130),
        name="attend_back",
    )(
        grad_hidden, grad_probs, router_t, hidden_two, residual, scale_two, gain_two, out_grad,
        query, context, segment_query, segment_keys, attended, log_sums, raw, scales, qk_gains,
        cosine, sine, hidden_one, tokens, gain_one, qkv_low, out_low,
    )


def fast_shards(
    tokens_in,
    out_grad,
    w_qkv,
    w_attn_out,
    attn_gain,
    ffn_gain,
    qk_gain,
    w_router,
    w_gate,
    w_up,
    w_down,
    routes,
    segments,
):
    row_count, model_width = tokens_in.shape
    experts = w_router.shape[1]
    local_experts = w_gate.shape[0]
    heads_here = qk_gain.shape[1]
    local_width = heads_here * HEAD
    groups = lax.axis_size("expert")
    device_index = lax.axis_index("expert")
    tensor_index = lax.axis_index("tensor")
    quarter = model_width // lax.axis_size("tensor")
    hop_count = WINDOW // row_count
    score_scale = HEAD ** (-0.5)
    low = jnp.bfloat16

    chosen = jnp.any(
        routes[:, :, None] == jnp.arange(experts, dtype=jnp.int32)[None, None, :], axis=1
    ).astype(jnp.float32)
    qk_row = qk_gain.reshape(1, -1)

    def rounded(v):
        return lax.reduce_precision(v, 8, 7)

    smalls = jnp.concatenate(
        [
            rounded(attn_gain)[None, :],
            rounded(ffn_gain)[None, :],
            jnp.pad(rounded(qk_row), ((0, 0), (0, row_count - qk_row.shape[1]))),
            jnp.zeros((5, row_count), jnp.float32),
            w_router.T,
            chosen.T,
        ],
        axis=0,
    )
    global_rows = device_index * row_count + jnp.arange(row_count, dtype=jnp.int32)
    cosine_table, sine_table = angles(global_rows % SEQ, HEAD)
    wide_cosine = jnp.concatenate([cosine_table[:, 0], cosine_table[:, 0]], axis=1)
    wide_sine = jnp.concatenate([-sine_table[:, 0], sine_table[:, 0]], axis=1)
    grad_out_piece = lax.dynamic_slice_in_dim(out_grad, tensor_index * quarter, quarter, axis=1)
    grad_out_rows = lax.all_gather(grad_out_piece, "expert", axis=0, tiled=True)
    out_low = lax.all_gather(w_attn_out.astype(low), "expert", axis=1, tiled=True)
    qkv_low, small_all, hidden_one, raw, scales, query_low, context_blocks = project(
        tokens_in, w_qkv, smalls, wide_cosine, wide_sine, 0
    )
    grad_out_rows, query_low = lax.optimization_barrier((grad_out_rows, query_low))
    grad_out_all = lax.all_gather(grad_out_rows, "tensor", axis=1, tiled=True)
    gain_one_f = small_all[:, 0].reshape(model_width)
    gain_two_f = small_all[:, 1].reshape(model_width)
    qk_gains = (
        small_all[:, 2, : qk_row.shape[1]]
        .reshape(groups, 2, heads_here, HEAD // groups)
        .transpose(1, 2, 0, 3)
        .reshape(2, local_width)
    )
    router_t = small_all[:, 8 : 8 + experts].transpose(1, 0, 2).reshape(experts, model_width).astype(low)
    chosen_all = small_all[:, 8 + experts : 8 + 2 * experts].transpose(0, 2, 1).reshape(
        groups * row_count, experts
    )
    segment_window = lax.dynamic_slice_in_dim(
        jnp.concatenate([jnp.full((WINDOW,), -1, jnp.int32), segments]),
        device_index * row_count, (hop_count + 1) * row_count,
    )
    segment_query = segment_window[WINDOW:]
    segment_keys = segment_window.reshape(hop_count + 1, row_count)[::-1]
    attended, log_sums, residual, hidden_two, scale_two_wide = attend(
        query_low, context_blocks, segment_query[:, None], segment_keys, tokens_in, out_low,
        gain_two_f[None, :], 2,
    )
    hidden_all = token_gather(hidden_two, 3)
    gate_up = jnp.concatenate(
        [w[i] for w in (w_gate, w_up) for i in range(local_experts)], axis=1
    ).astype(low)
    down_low = w_down.reshape(-1, model_width).astype(low)
    expert_part, grad_hidden_sum, grad_gate_sum, grad_gate_w, grad_up_w, grad_down = expert_layer(
        hidden_all, grad_out_all, gate_up, down_low, router_t, chosen_all, 5
    )
    expert_quarter = token_reduce(expert_part, 6)
    expert_pieces = lax.all_gather(expert_quarter, "tensor", axis=0)
    block_out = residual + jnp.concatenate(
        [expert_pieces[i] for i in (0, 2, 1, 3)], axis=1
    ).astype(jnp.float32)
    grad_probs = grad_gate_sum[:, :local_experts].reshape(experts, row_count).T * chosen
    grad_tokens, qkv_sum, out_sum, small_sum = attend_back(
        grad_hidden_sum, grad_probs, router_t, hidden_two, residual, scale_two_wide,
        gain_two_f[None, :], out_grad, query_low, context_blocks, segment_query[:, None], segment_keys,
        attended, log_sums, raw, scales, qk_gains, wide_cosine, wide_sine, hidden_one, tokens_in,
        gain_one_f[None, :], qkv_low, out_low, 8,
    )
    return (
        block_out.astype(low),
        grad_tokens,
        qkv_sum,
        out_sum,
        small_sum[0],
        small_sum[1],
        lax.dynamic_slice_in_dim(
            small_sum[2:6].reshape(2, heads_here, HEAD),
            device_index * qk_gain.shape[2], qk_gain.shape[2], axis=2,
        ),
        small_sum[8 : 8 + experts].T,
        grad_gate_w,
        grad_up_w,
        grad_down,
    )


def solution(mesh):
    placed = (
        P("expert", None),
        P("expert", None),
        P(None, "expert", "tensor"),
        P("tensor", "expert"),
        P("expert"),
        P("expert"),
        P(None, "tensor", "expert"),
        P("expert", None),
        P("expert", None, "tensor"),
        P("expert", None, "tensor"),
        P("expert", "tensor", None),
        P("expert", None),
        P(),
    )
    compact = (mesh.shape["expert"], mesh.shape["tensor"]) == (GROUPS, NX * NC)
    return jax.shard_map(
        fast_shards if compact else shards,
        mesh=mesh,
        in_specs=placed,
        out_specs=(
            P("expert", None),
            P("expert", None),
            P(None, "expert", "tensor"),
            P("tensor", "expert"),
            P("expert"),
            P("expert"),
            P(None, "tensor", "expert"),
            P("expert", None),
            P("expert", None, "tensor"),
            P("expert", None, "tensor"),
            P("expert", "tensor", None),
        ),
        check_vma=False,
    )
```

```python
import jax
import jax.numpy as jnp
from jax import lax
from jax.experimental import pallas as pl
from jax.experimental.pallas import tpu as pltpu
from jax.sharding import PartitionSpec as P

HEAD = 128
WINDOW = 1024
SEQ = 2048


EPS = 1e-05
THETA = 10000.0


def from_behind(value, axis, steps):
    count = lax.axis_size(axis)
    initial, last = (max(0, -steps), min(count, count - steps))
    return lax.ppermute(value, axis, [(source, source + steps) for source in range(initial, last)])


def angles(position, head_size):
    half_size = head_size // 2
    frequency = THETA ** (-(jnp.arange(half_size, dtype=jnp.float32) * 2.0 / head_size))
    phase_angle = position.astype(jnp.float32)[:, None] * frequency[None, :]
    return (jnp.cos(phase_angle)[:, None, :], jnp.sin(phase_angle)[:, None, :])


def rotate(rotated_in, cosine_table, sine_table):
    half_size = rotated_in.shape[-1] // 2
    first_half = rotated_in[..., :half_size]
    second_half = rotated_in[..., half_size:]
    return jnp.concatenate(
        [
            first_half * cosine_table - second_half * sine_table,
            second_half * cosine_table + first_half * sine_table,
        ],
        axis=-1,
    )


def slot_layout(block_routes, experts, capacity):
    flat_routes = block_routes.reshape(-1)
    onehot = (flat_routes[:, None] == jnp.arange(experts, dtype=jnp.int32)[None, :]).astype(
        jnp.int32
    )
    before = jnp.cumsum(onehot, axis=0) - onehot
    rank_within = jnp.sum(before * onehot, axis=1)
    slot_index = flat_routes * capacity + rank_within
    slot_table = (
        jnp.zeros((experts * capacity,), jnp.int32)
        .at[slot_index]
        .set(jnp.arange(flat_routes.shape[0], dtype=jnp.int32) + 1)
    )
    return (slot_index, slot_table)


def shards(
    tokens_in,
    out_grad,
    w_qkv,
    w_attn_out,
    attn_gain,
    ffn_gain,
    qk_gain,
    w_router,
    w_gate,
    w_up,
    w_down,
    routes,
    segments,
):
    row_count, model_width = tokens_in.shape
    experts = w_router.shape[1]
    per_token = routes.shape[1]
    local_experts = w_gate.shape[0]
    heads_here = qk_gain.shape[1]
    local_width = heads_here * HEAD
    groups = lax.axis_size("expert")
    device = lax.axis_index("expert")
    capacity = row_count * per_token * 3 // (2 * experts)
    hop_count = WINDOW // row_count
    buffer_shape = (groups, local_experts, capacity, model_width)
    score_scale = HEAD ** (-0.5)

    def fetch_weights():
        return (
            lax.all_gather(w_qkv.astype(jnp.bfloat16), "expert", axis=1, tiled=True),
            lax.all_gather(w_attn_out.astype(jnp.bfloat16), "expert", axis=1, tiled=True),
            lax.all_gather(w_router.astype(jnp.bfloat16), "expert", axis=0, tiled=True),
            lax.all_gather(attn_gain.astype(jnp.bfloat16), "expert", axis=0, tiled=True),
            lax.all_gather(ffn_gain.astype(jnp.bfloat16), "expert", axis=0, tiled=True),
            lax.all_gather(qk_gain.astype(jnp.bfloat16), "expert", axis=2, tiled=True),
        )

    def prepare(pieces):
        return (
            pieces[0],
            pieces[1],
            pieces[2],
            pieces[3].astype(jnp.float32),
            pieces[4].astype(jnp.float32),
            pieces[5].astype(jnp.float32).reshape(2, local_width),
        )

    qkv_low, out_low, router_low, gain_one_f, gain_two_f, qk_gains = prepare(fetch_weights())
    tokens_f = tokens_in.astype(jnp.float32)
    scale_one = lax.rsqrt(jnp.mean(tokens_f * tokens_f, axis=-1, keepdims=True) + EPS)
    hidden_one = (tokens_f * scale_one * gain_one_f).astype(jnp.bfloat16)
    projected = jnp.einsum("td,jde->jte", hidden_one, qkv_low, preferred_element_type=jnp.float32)
    query_raw = projected[0]
    key_raw = projected[1]
    query_sq, key_sq = lax.psum(
        (jnp.sum(query_raw * query_raw, axis=-1), jnp.sum(key_raw * key_raw, axis=-1)), "tensor"
    )
    query_scale = lax.rsqrt(query_sq / model_width + EPS)[:, None]
    key_scale = lax.rsqrt(key_sq / model_width + EPS)[:, None]
    normed_query = query_raw * query_scale
    normed_key = key_raw * key_scale
    global_rows = device * row_count + jnp.arange(row_count, dtype=jnp.int32)
    cosine_table, sine_table = angles(global_rows % SEQ, HEAD)
    query_low = rotate(
        (normed_query * qk_gains[0]).reshape(row_count, heads_here, HEAD), cosine_table, sine_table
    ).astype(jnp.bfloat16)
    key_low = rotate(
        (normed_key * qk_gains[1]).reshape(row_count, heads_here, HEAD), cosine_table, sine_table
    ).astype(jnp.bfloat16)
    value_low = projected[2].astype(jnp.bfloat16).reshape(row_count, heads_here, HEAD)
    own_pair = jnp.stack([key_low, value_low])
    earlier = []
    for steps_back in range(hop_count, 0, -1):
        earlier.append(from_behind(own_pair, "expert", steps_back))
    context = jnp.concatenate(earlier + [own_pair], axis=1)
    key_rows = (device - hop_count) * row_count + jnp.arange(
        (hop_count + 1) * row_count, dtype=jnp.int32
    )
    segment_keys = segments[jnp.maximum(key_rows, 0)]
    segment_query = segments[global_rows]
    distance = global_rows[:, None] - key_rows[None, :]
    allowed = (
        (key_rows[None, :] >= 0)
        & (segment_query[:, None] == segment_keys[None, :])
        & (distance >= 0)
        & (distance < WINDOW)
    )

    def score_block():
        raw_scores = (
            jnp.einsum("qhd,khd->hqk", query_low, context[0], preferred_element_type=jnp.float32)
            * score_scale
        )
        return jnp.where(allowed[None], raw_scores, -1e30)

    scores = score_block()
    largest = jnp.max(scores, axis=-1, keepdims=True)
    exp_scores = jnp.exp(scores - largest)
    exp_total = jnp.sum(exp_scores, axis=-1, keepdims=True)
    log_total = largest + jnp.log(exp_total)
    attn_probs = (exp_scores / exp_total).astype(jnp.bfloat16)
    attended = (
        jnp.einsum("hqk,khd->qhd", attn_probs, context[1], preferred_element_type=jnp.float32)
        .reshape(row_count, local_width)
        .astype(jnp.bfloat16)
    )
    attention_out = lax.psum(
        jnp.dot(attended, out_low, preferred_element_type=jnp.float32).astype(jnp.bfloat16),
        "tensor",
    ).astype(jnp.float32)
    residual = tokens_f + attention_out
    scale_two = lax.rsqrt(jnp.mean(residual * residual, axis=-1, keepdims=True) + EPS)
    normed_two = residual * scale_two
    hidden_two = (normed_two * gain_two_f).astype(jnp.bfloat16)
    logits = jnp.dot(hidden_two, router_low, preferred_element_type=jnp.float32)
    logit_exp = jnp.exp(logits - jnp.max(logits, axis=-1, keepdims=True))
    router_probs = logit_exp / jnp.sum(logit_exp, axis=-1, keepdims=True)
    chosen = routes[:, :, None] == jnp.arange(experts, dtype=jnp.int32)[None, None, :]
    gate_probs = jnp.sum(jnp.where(chosen, router_probs[:, None, :], 0.0), axis=-1)
    slot_index, slot_table = slot_layout(routes, experts, capacity)
    present = (slot_table > 0)[:, None]
    assigned = jnp.maximum(slot_table - 1, 0)
    row_of_slot = assigned // per_token
    gate_low = w_gate.astype(jnp.bfloat16)
    up_low = w_up.astype(jnp.bfloat16)
    down_low = w_down.astype(jnp.bfloat16)

    def send_rows():
        buffer_rows = jnp.where(
            present, hidden_two[row_of_slot], jnp.zeros((), jnp.bfloat16)
        ).reshape(buffer_shape)
        return lax.all_to_all(buffer_rows, "expert", split_axis=0, concat_axis=0, tiled=True)

    def expert_front(arrived):
        gate_pre = jnp.einsum(
            "secd,edh->sech", arrived, gate_low, preferred_element_type=jnp.float32
        )
        up_pre = jnp.einsum("secd,edh->sech", arrived, up_low, preferred_element_type=jnp.float32)
        return (gate_pre, up_pre)

    received = send_rows()
    gate_pre, up_pre = expert_front(received)
    activated = (gate_pre * jax.nn.sigmoid(gate_pre) * up_pre).astype(jnp.bfloat16)
    partial_value = jnp.einsum(
        "sech,ehd->secd", activated, down_low, preferred_element_type=jnp.float32
    ).astype(jnp.bfloat16)
    returned = lax.all_to_all(
        partial_value, "expert", split_axis=0, concat_axis=0, tiled=True
    ).reshape(experts * capacity, model_width)
    expert_rows = returned[slot_index].reshape(row_count, per_token, model_width)
    expert_part = jnp.einsum(
        "tk,tkd->td", gate_probs, expert_rows, preferred_element_type=jnp.float32
    )
    block_out = residual + lax.psum(expert_part.astype(jnp.bfloat16), "tensor").astype(jnp.float32)
    qkv_low, out_low, router_low, gain_one_f, gain_two_f, qk_gains = prepare(fetch_weights())
    grad_out = out_grad.astype(jnp.float32)
    grad_gate_part = jnp.einsum(
        "td,tkd->tk", grad_out, expert_rows, preferred_element_type=jnp.float32
    )
    slot_grads = (
        (gate_probs[:, :, None] * grad_out[:, None, :])
        .astype(jnp.bfloat16)
        .reshape(row_count * per_token, model_width)
    )
    grad_buffer = jnp.where(present, slot_grads[assigned], jnp.zeros((), jnp.bfloat16)).reshape(
        buffer_shape
    )
    grad_received = lax.all_to_all(grad_buffer, "expert", split_axis=0, concat_axis=0, tiled=True)
    received = send_rows()
    gate_pre, up_pre = expert_front(received)
    sigmoid_gate = jax.nn.sigmoid(gate_pre)
    swish_gate = gate_pre * sigmoid_gate
    activated = (swish_gate * up_pre).astype(jnp.bfloat16)
    grad_act = jnp.einsum(
        "secd,ehd->sech", grad_received, down_low, preferred_element_type=jnp.float32
    )
    grad_down = jnp.einsum(
        "sech,secd->ehd", activated, grad_received, preferred_element_type=jnp.float32
    )
    grad_gate_pre = (
        grad_act * up_pre * sigmoid_gate * (1.0 + gate_pre * (1.0 - sigmoid_gate))
    ).astype(jnp.bfloat16)
    grad_up_pre = (grad_act * swish_gate).astype(jnp.bfloat16)
    grad_gate_w = jnp.einsum(
        "secd,sech->edh", received, grad_gate_pre, preferred_element_type=jnp.float32
    )
    grad_up_w = jnp.einsum(
        "secd,sech->edh", received, grad_up_pre, preferred_element_type=jnp.float32
    )
    grad_rows = (
        jnp.einsum("sech,edh->secd", grad_gate_pre, gate_low, preferred_element_type=jnp.float32)
        + jnp.einsum("sech,edh->secd", grad_up_pre, up_low, preferred_element_type=jnp.float32)
    ).astype(jnp.bfloat16)
    grad_back = lax.all_to_all(
        grad_rows, "expert", split_axis=0, concat_axis=0, tiled=True
    ).reshape(experts * capacity, model_width)
    grad_hidden_part = jnp.sum(
        grad_back[slot_index].reshape(row_count, per_token, model_width), axis=1, dtype=jnp.float32
    )
    grad_hidden_sum, grad_gates = (
        lax.psum(grad_hidden_part.astype(jnp.bfloat16), "tensor").astype(jnp.float32),
        lax.psum(grad_gate_part.astype(jnp.bfloat16), "tensor").astype(jnp.float32),
    )
    grad_probs = jnp.sum(jnp.where(chosen, grad_gates[:, :, None], 0.0), axis=1)
    grad_logits = (
        router_probs * (grad_probs - jnp.sum(router_probs * grad_probs, axis=-1, keepdims=True))
    ).astype(jnp.bfloat16)
    grad_hidden_two = grad_hidden_sum + jnp.dot(
        grad_logits, router_low.T, preferred_element_type=jnp.float32
    )
    grad_router = jnp.dot(hidden_two.T, grad_logits, preferred_element_type=jnp.float32)
    grad_gain_two = jnp.sum(grad_hidden_two * normed_two, axis=0)
    scaled_two = grad_hidden_two * gain_two_f
    grad_residual = (
        grad_out
        + scale_two * scaled_two
        - residual
        * (scale_two * scale_two * scale_two)
        * jnp.mean(scaled_two * residual, axis=-1, keepdims=True)
    )
    grad_attn = grad_residual.astype(jnp.bfloat16)
    grad_out_w = jnp.dot(attended.T, grad_attn, preferred_element_type=jnp.float32)
    grad_attended = (
        jnp.dot(grad_attn, out_low.T, preferred_element_type=jnp.float32)
        .astype(jnp.bfloat16)
        .reshape(row_count, heads_here, HEAD)
    )
    attn_weights = jnp.where(allowed[None], jnp.exp(score_block() - log_total), 0.0)
    grad_weights = jnp.einsum(
        "qhd,khd->hqk", grad_attended, context[1], preferred_element_type=jnp.float32
    )
    inner_sum = jnp.sum(attn_weights * grad_weights, axis=-1, keepdims=True)
    grad_scores = (attn_weights * (grad_weights - inner_sum) * score_scale).astype(jnp.bfloat16)
    grad_query = jnp.einsum(
        "hqk,khd->qhd", grad_scores, context[0], preferred_element_type=jnp.float32
    )
    grad_keys = jnp.einsum(
        "hqk,qhd->khd", grad_scores, query_low, preferred_element_type=jnp.float32
    )
    grad_values = jnp.einsum(
        "hqk,qhd->khd",
        attn_weights.astype(jnp.bfloat16),
        grad_attended,
        preferred_element_type=jnp.float32,
    )
    grad_pair = jnp.stack([grad_keys, grad_values]).reshape(
        2, hop_count + 1, row_count, heads_here, HEAD
    )
    own_grad = grad_pair[:, hop_count]
    for steps_back in range(1, hop_count + 1):
        own_grad = own_grad + from_behind(
            grad_pair[:, hop_count - steps_back].astype(jnp.bfloat16), "expert", -steps_back
        ).astype(jnp.float32)
    grad_query_norm = rotate(grad_query, cosine_table, -sine_table).reshape(row_count, local_width)
    grad_key_norm = rotate(own_grad[0], cosine_table, -sine_table).reshape(row_count, local_width)
    grad_gain_query = jnp.sum(grad_query_norm * normed_query, axis=0)
    grad_gain_key = jnp.sum(grad_key_norm * normed_key, axis=0)
    scaled_query = grad_query_norm * qk_gains[0]
    scaled_key = grad_key_norm * qk_gains[1]
    query_inner, key_inner = lax.psum(
        (jnp.sum(scaled_query * query_raw, axis=-1), jnp.sum(scaled_key * key_raw, axis=-1)),
        "tensor",
    )
    grad_query_raw = (
        query_scale * scaled_query
        - query_raw * (query_scale * query_scale * query_scale) * query_inner[:, None] / model_width
    ).astype(jnp.bfloat16)
    grad_key_raw = (
        key_scale * scaled_key
        - key_raw * (key_scale * key_scale * key_scale) * key_inner[:, None] / model_width
    ).astype(jnp.bfloat16)
    grad_value_raw = own_grad[1].reshape(row_count, local_width).astype(jnp.bfloat16)
    grad_proj = jnp.stack([grad_query_raw, grad_key_raw, grad_value_raw])
    grad_qkv = jnp.einsum("td,jte->jde", hidden_one, grad_proj, preferred_element_type=jnp.float32)
    grad_hidden_one = lax.psum(
        jnp.einsum("jte,jde->td", grad_proj, qkv_low, preferred_element_type=jnp.float32).astype(
            jnp.bfloat16
        ),
        "tensor",
    ).astype(jnp.float32)
    grad_gain_one = jnp.sum(grad_hidden_one * tokens_f * scale_one, axis=0)
    scaled_one = grad_hidden_one * gain_one_f
    grad_tokens = (
        grad_residual
        + scale_one * scaled_one
        - tokens_f
        * (scale_one * scale_one * scale_one)
        * jnp.mean(scaled_one * tokens_f, axis=-1, keepdims=True)
    )
    grad_qk = jnp.stack([grad_gain_query, grad_gain_key]).reshape(2, heads_here, HEAD)
    reduced = (
        lax.psum_scatter(
            grad_qkv.astype(jnp.bfloat16), "expert", scatter_dimension=1, tiled=True
        ).astype(jnp.float32),
        lax.psum_scatter(
            grad_out_w.astype(jnp.bfloat16), "expert", scatter_dimension=1, tiled=True
        ).astype(jnp.float32),
        lax.psum_scatter(
            grad_router.astype(jnp.bfloat16), "expert", scatter_dimension=0, tiled=True
        ).astype(jnp.float32),
        lax.psum_scatter(
            grad_gain_one.astype(jnp.bfloat16), "expert", scatter_dimension=0, tiled=True
        ).astype(jnp.float32),
        lax.psum_scatter(
            grad_gain_two.astype(jnp.bfloat16), "expert", scatter_dimension=0, tiled=True
        ).astype(jnp.float32),
        lax.psum_scatter(
            grad_qk.astype(jnp.bfloat16), "expert", scatter_dimension=2, tiled=True
        ).astype(jnp.float32),
    )
    return (
        block_out.astype(jnp.bfloat16),
        grad_tokens.astype(jnp.bfloat16),
        reduced[0],
        reduced[1],
        reduced[3],
        reduced[4],
        reduced[5],
        reduced[2],
        grad_gate_w,
        grad_up_w,
        grad_down,
    )


MESH_ID = pl.DeviceIdType.MESH
HBM = pl.BlockSpec(memory_space=pl.ANY)
VMEM = pl.BlockSpec(memory_space=pltpu.VMEM)
NZ, NY, NX, NC = 4, 2, 2, 2
GROUPS = NZ * NY


def place():
    e = lax.axis_index("expert")
    t = lax.axis_index("tensor")
    return lax.div(e, NY), lax.rem(e, NY), lax.div(t, NC), lax.rem(t, NC)


def device(z, y, x, c):
    return (z * NY + y, x * NC + c)


def run_if(condition, body):
    if condition is None:
        body()
    else:
        pl.when(condition)(body)


def greet(partners):
    barrier = pltpu.get_barrier_semaphore()
    for target, condition in partners:
        run_if(
            condition,
            lambda target=target: pl.semaphore_signal(
                barrier, inc=1, device_id=target, device_id_type=MESH_ID
            ),
        )
    count = sum(1 for _, condition in partners if condition is None)
    for _, condition in partners:
        if condition is not None:
            count = count + condition.astype(jnp.int32)
    pl.semaphore_wait(barrier, count)


def remote(source, target_ref, send_sem, recv_sem, target):
    return pltpu.make_async_remote_copy(
        src_ref=source,
        dst_ref=target_ref,
        send_sem=send_sem,
        recv_sem=recv_sem,
        device_id=target,
        device_id_type=MESH_ID,
    )


def block_rows(block, rows):
    return pl.ds(pl.multiple_of(block * rows, rows), rows)


class LineGather:
    def __init__(self, streams, sources, views, send_sem, recv_sem):
        self.z, self.y, self.x, self.c = place()
        self.streams, self.sources, self.views = streams, sources, views
        self.send_sem, self.recv_sem = send_sem, recv_sem
        self.has_up, self.has_down = self.z < NZ - 1, self.z > 0
        self.pending = []

    def partners(self):
        z, y, x, c = self.z, self.y, self.x, self.c
        return [
            (device(z + 1, y, x, c), z < NZ - 1),
            (device(z - 1, y, x, c), z > 0),
            (device(z, 1 - y, x, c), None),
        ]

    def exists(self, rel):
        rel = rel % 7
        if rel == 0:
            return None
        return self.z >= rel if rel < 4 else self.z + (rel - 3) < NZ

    def block(self, rel):
        y = self.y if rel < 7 else 1 - self.y
        rel = rel % 7
        z = self.z if rel == 0 else (self.z - rel if rel < 4 else self.z + (rel - 3))
        return z * NY + y

    def send(self, stream, rel, way):
        z, y, x, c = self.z, self.y, self.x, self.c
        block = self.block(rel)
        there = self.views[stream](block)
        source = self.sources[stream] if rel == 0 else there
        if way == 0:
            target, landing = device(z + 1, y, x, c), (1 if rel == 0 else rel + 1)
        elif way == 1:
            target, landing = device(z - 1, y, x, c), (4 if rel == 0 else rel + 1)
        else:
            target, landing = device(z, 1 - y, x, c), 7 + rel
        return remote(
            source,
            there,
            self.send_sem.at[stream, rel, way],
            self.recv_sem.at[stream, landing],
            target,
        )

    def start(self, stream, rel):
        if rel < 4:
            run = self.has_up
            run_if(run, lambda: self.send(stream, rel, 0).start())
            self.pending.append((stream, rel, 0, run))
        if rel == 0 or rel >= 4:
            run = self.has_down
            run_if(run, lambda: self.send(stream, rel, 1).start())
            self.pending.append((stream, rel, 1, run))
        self.send(stream, rel, 2).start()
        self.pending.append((stream, rel, 2, None))

    def arrive(self, stream, rel):
        there = self.views[stream](self.block(rel))
        remote(
            there,
            there,
            self.send_sem.at[stream, 0, 0],
            self.recv_sem.at[stream, rel],
            device(self.z, 1 - self.y, self.x, self.c),
        ).wait_recv()

    def order(self):
        return [7, 1, 4, 8, 11, 2, 5, 9, 12, 3, 6, 10, 13]

    def run(self, hook=None):
        for stream in self.streams:
            self.start(stream, 0)
        for rel in self.order():
            def step(rel=rel):
                marks = len(self.pending)
                for stream in self.streams:
                    self.arrive(stream, rel)
                    if rel < 7:
                        self.start(stream, rel)
                    if hook is not None:
                        hook(stream, rel)
                if rel < 7:
                    late = self.pending[marks:]
                    del self.pending[marks:]
                    self.finish_later(late, rel)
            run_if(self.exists(rel), step)

    def finish_later(self, late, rel):
        self.late = getattr(self, "late", []) + [(rel, late)]

    def finish(self):
        for stream, rel, way, run in self.pending:
            run_if(run, lambda s=stream, r=rel, w=way: self.send(s, r, w).wait_send())
        for rel, late in getattr(self, "late", []):
            def body(late=late):
                for stream, rel, way, run in late:
                    run_if(run, lambda s=stream, r=rel, w=way: self.send(s, r, w).wait_send())
            run_if(self.exists(rel), body)


def cost(microseconds):
    return pl.CostEstimate(flops=0, bytes_accessed=int(microseconds * 3.0e6), transcendentals=0)


def comm_params(collective_id, megabytes=56):
    return pltpu.CompilerParams(
        collective_id=collective_id,
        has_side_effects=True,
        vmem_limit_bytes=megabytes * 1024 * 1024,
    )


def weight_gather(qkv_low, out_low, smalls, collective_id):
    parts, rows, width = qkv_low.shape
    depth, columns = out_low.shape

    def kernel(qkv, out, small, qkv_all, out_all, small_all, send_sem, recv_sem, local_sem):
        views = [
            lambda b: qkv_all.at[:, block_rows(b, rows), :],
            lambda b: out_all.at[:, block_rows(b, columns)],
            lambda b: small_all.at[b],
        ]
        line = LineGather([2, 0, 1], [qkv, out, small], views, send_sem, recv_sem)
        greet(line.partners())
        own = line.block(0)
        keep = [
            pltpu.make_async_copy(source, view(own), local_sem.at[i])
            for i, (source, view) in enumerate(zip([qkv, out, small], views))
        ]
        for copy in keep:
            copy.start()
        line.run()
        line.finish()
        for copy in keep:
            copy.wait()

    return pl.pallas_call(
        kernel,
        out_shape=(
            jax.ShapeDtypeStruct((parts, rows * GROUPS, width), jnp.bfloat16),
            jax.ShapeDtypeStruct((depth, columns * GROUPS), jnp.bfloat16),
            jax.ShapeDtypeStruct((GROUPS,) + smalls.shape, jnp.float32),
        ),
        in_specs=[HBM] * 3,
        out_specs=(HBM, HBM, HBM),
        scratch_shapes=[
            pltpu.SemaphoreType.DMA((3, 7, 3)),
            pltpu.SemaphoreType.DMA((3, 14)),
            pltpu.SemaphoreType.DMA((3,)),
        ],
        compiler_params=comm_params(collective_id),
        cost_estimate=cost(100),
        name="weight_gather",
    )(qkv_low, out_low, smalls)


def token_gather(block, collective_id):
    rows, width = block.shape
    a_cols, c_cols = width * 3 // 16, width // 8

    def kernel(own_ref, all_ref, send_sem, recv_sem, x_send, x_recv, core_send, core_recv, local_sem):
        z, y, x, c = place()

        def a_at(xx, cc):
            return pl.ds(pl.multiple_of(xx * (2 * a_cols) + cc * a_cols, 128), a_cols)

        def c_at(cc):
            return pl.ds(pl.multiple_of(4 * a_cols + cc * c_cols, 128), c_cols)

        def view(b, columns):
            return all_ref.at[block_rows(b, rows), columns]

        sources = [own_ref.at[:, a_at(x, c)], own_ref.at[:, c_at(c)]]
        views = [lambda b: view(b, a_at(x, c)), lambda b: view(b, c_at(c))]
        line = LineGather([0, 1], sources, views, send_sem, recv_sem)
        across, twin = device(z, y, 1 - x, c), device(z, y, x, 1 - c)
        greet(line.partners() + [(across, None), (twin, None)])
        keep = pltpu.make_async_copy(own_ref, all_ref.at[block_rows(line.block(0), rows), :], local_sem)
        keep.start()

        def to_twin(rel, stream, landing=False):
            b = line.block(rel)
            columns = [a_at(x, c), c_at(c), a_at(1 - x, c)][stream]
            other = [a_at(x, 1 - c), c_at(1 - c), a_at(1 - x, 1 - c)][stream]
            piece = view(b, other if landing else columns)
            return remote(piece, piece, core_send.at[rel, stream], core_recv.at[rel, stream], twin)

        def to_across(rel, landing=False):
            b = line.block(rel)
            piece = view(b, a_at(1 - x if landing else x, c))
            return remote(piece, piece, x_send.at[rel], x_recv.at[rel], across)

        def hook(stream, rel):
            if stream == 0:
                to_across(rel).start()
            to_twin(rel, stream).start()

        line.run(hook)
        for rel in line.order():
            def relay(rel=rel):
                to_across(rel, True).wait_recv()
                to_twin(rel, 2).start()
            run_if(line.exists(rel), relay)
        for rel in line.order():
            def end(rel=rel):
                to_across(rel).wait_send()
                for stream in range(3):
                    to_twin(rel, stream, True).wait_recv()
                    to_twin(rel, stream).wait_send()
            run_if(line.exists(rel), end)
        line.finish()
        keep.wait()

    return pl.pallas_call(
        kernel,
        out_shape=jax.ShapeDtypeStruct((rows * GROUPS, width), block.dtype),
        in_specs=[HBM],
        out_specs=HBM,
        scratch_shapes=[
            pltpu.SemaphoreType.DMA((2, 7, 3)),
            pltpu.SemaphoreType.DMA((2, 14)),
            pltpu.SemaphoreType.DMA((14,)),
            pltpu.SemaphoreType.DMA((14,)),
            pltpu.SemaphoreType.DMA((14, 3)),
            pltpu.SemaphoreType.DMA((14, 3)),
            pltpu.SemaphoreType.DMA,
        ],
        compiler_params=comm_params(collective_id),
        cost_estimate=cost(45),
        name="token_gather",
    )(block)


def add_into(rows, step, store):
    def body(i, carry):
        store(pl.ds(pl.multiple_of(i * step, step), step))
        return carry

    lax.fori_loop(0, rows // step, body, 0)


def group_stages(part_ref, out_ref, core_buf, x_buf, send_sem, recv_sem):
    rows, width = part_ref.shape
    half, quarter = width // 2, width // 4
    z, y, x, c = place()
    across, twin = device(z, y, 1 - x, c), device(z, y, x, 1 - c)

    def half_of(cc):
        return pl.ds(pl.multiple_of(cc * half, half), half)

    def quarter_of(xx, cc):
        return pl.ds(pl.multiple_of(cc * half + xx * quarter, quarter), quarter)

    own, from_x = out_ref.at[:, quarter_of(x, c)], out_ref.at[:, quarter_of(1 - x, c)]
    to_x = core_buf.at[:, pl.ds(pl.multiple_of((1 - x) * quarter, quarter), quarter)]
    sources = [part_ref.at[:, half_of(1 - c)], to_x, own, own, from_x]
    landings = [core_buf, x_buf, own, own, from_x]
    targets = [twin, across, across, twin, twin]

    def copy(k):
        return remote(sources[k], landings[k], send_sem.at[k], recv_sem.at[k], targets[k])

    def arrive(k, landing):
        remote(landing, landing, send_sem.at[k], recv_sem.at[k], targets[k]).wait_recv()

    def begin():
        copy(0).start()

    def core_step():
        copy(0).wait_recv()
        add_to(core_buf, core_buf, part_ref.at[:, half_of(c)], 32)
        copy(1).start()

    def x_step():
        copy(1).wait_recv()
        add_to(own, x_buf, core_buf.at[:, pl.ds(pl.multiple_of(x * quarter, quarter), quarter)], 32)
        copy(2).start()
        copy(3).start()

    def spread():
        arrive(2, from_x)
        copy(4).start()

    def end():
        arrive(3, out_ref.at[:, quarter_of(x, 1 - c)])
        arrive(4, out_ref.at[:, quarter_of(1 - x, 1 - c)])
        for k in range(5):
            copy(k).wait_send()

    return [begin, core_step, x_step, spread, end]


def group_sum(part_ref, out_ref, core_buf, x_buf, send_sem, recv_sem, meanwhile=None):
    stages = group_stages(part_ref, out_ref, core_buf, x_buf, send_sem, recv_sem)
    stages[0]()
    if meanwhile is not None:
        meanwhile()
    for stage in stages[1:]:
        stage()


def tensor_sum(part, collective_id):
    rows, width = part.shape

    def kernel(part_ref, out_ref, core_buf, x_buf, send_sem, recv_sem):
        z, y, x, c = place()
        greet([(device(z, y, 1 - x, c), None), (device(z, y, x, 1 - c), None)])
        group_sum(part_ref, out_ref, core_buf, x_buf, send_sem, recv_sem)

    return pl.pallas_call(
        kernel,
        out_shape=jax.ShapeDtypeStruct((rows, width), jnp.bfloat16),
        in_specs=[VMEM],
        out_specs=VMEM,
        scratch_shapes=[
            pltpu.VMEM((rows, width // 2), jnp.bfloat16),
            pltpu.VMEM((rows, width // 4), jnp.bfloat16),
            pltpu.SemaphoreType.DMA((5,)),
            pltpu.SemaphoreType.DMA((5,)),
        ],
        compiler_params=comm_params(collective_id, 16),
        cost_estimate=cost(17),
        name="tensor_sum",
    )(part)


Z_ORDER = (3, 0, 2, 1)


def accumulate(into, addend, step=64):
    rows = into.shape[0]
    step = min(step, rows)

    def body(i, carry):
        r = pl.ds(pl.multiple_of(i * step, step), step)
        total = into[r, :].astype(jnp.float32) + addend[r, :].astype(jnp.float32)
        into[r, :] = total.astype(into.dtype)
        return carry

    lax.fori_loop(0, rows // step, body, 0)


class LineReduce:
    def __init__(self, streams, own, y_buf, lo_buf, hi_buf, send_sem, recv_sem):
        self.z, self.y, self.x, self.c = place()
        self.streams = streams
        self.own, self.y_buf, self.lo_buf, self.hi_buf = own, y_buf, lo_buf, hi_buf
        self.send_sem, self.recv_sem = send_sem, recv_sem

    def partners(self):
        z, y, x, c = self.z, self.y, self.x, self.c
        return [
            (device(z + 1, y, x, c), z < NZ - 1),
            (device(z - 1, y, x, c), z > 0),
            (device(z, 1 - y, x, c), None),
        ]

    def copy(self, s, zz, way):
        z, y, x, c = self.z, self.y, self.x, self.c
        if way == 0:
            source, landing, target = self.own(s, zz, 1 - y), self.y_buf, device(z, 1 - y, x, c)
        elif way == 1:
            source, landing, target = self.y_buf(s, zz), self.lo_buf, device(z + 1, y, x, c)
        else:
            source, landing, target = self.y_buf(s, zz), self.hi_buf, device(z - 1, y, x, c)
        return remote(
            source, landing(s, zz), self.send_sem.at[s, zz, way], self.recv_sem.at[s, zz, way], target
        )

    def to_y(self, s, zz):
        self.copy(s, zz, 0).start()

    def take(self, s, zz, way):
        self.copy(s, zz, way).wait_recv()
        accumulate(self.y_buf(s, zz), (self.lo_buf if way == 1 else self.hi_buf)(s, zz))

    def along_z(self, s, zz):
        z = self.z
        self.copy(s, zz, 0).wait_recv()
        accumulate(self.y_buf(s, zz), self.own(s, zz, self.y))

        def upward():
            run_if(z > 0, lambda: self.take(s, zz, 1))
            self.copy(s, zz, 1).start()

        def downward():
            run_if(z < NZ - 1, lambda: self.take(s, zz, 2))
            self.copy(s, zz, 2).start()

        run_if(z < zz, upward)
        run_if(z > zz, downward)

    def home(self, done):
        for zz in range(NZ):
            def land(zz=zz):
                for s in self.streams:
                    if zz > 0:
                        self.take(s, zz, 1)
                    if zz < NZ - 1:
                        self.take(s, zz, 2)
                    done(s, self.y_buf(s, zz))
            run_if(self.z == zz, land)

    def finish(self):
        for zz in range(NZ):
            for s in self.streams:
                self.copy(s, zz, 0).wait_send()
                run_if(self.z < zz, lambda s=s, zz=zz: self.copy(s, zz, 1).wait_send())
                run_if(self.z > zz, lambda s=s, zz=zz: self.copy(s, zz, 2).wait_send())


def weight_reduce(qkv, out, smalls, collective_id):
    parts, depth, width = qkv.shape
    rows = depth // GROUPS
    out_rows, columns = out.shape[0], out.shape[1] // GROUPS

    def kernel(qkv_ref, out_ref, small_ref, qkv_sum, out_sum, small_sum,
               qkv_buf, out_buf, small_buf, send_sem, recv_sem):
        def own(s, zz, yy):
            b = zz * NY + yy
            if s < parts:
                return qkv_ref.at[s, block_rows(b, rows), :]
            if s == parts:
                return out_ref.at[:, block_rows(b, columns)]
            return small_ref.at[b]

        def slot(kind):
            def view(s, zz):
                if s < parts:
                    return qkv_buf.at[kind, zz, s]
                if s == parts:
                    return out_buf.at[kind, zz]
                return small_buf.at[kind, zz]
            return view

        streams = list(range(parts + 2))
        line = LineReduce(streams, own, slot(0), slot(1), slot(2), send_sem, recv_sem)
        greet(line.partners())
        work = [(s, zz) for s in [parts + 1, parts] + list(range(parts)) for zz in Z_ORDER]
        for s, zz in work:
            line.to_y(s, zz)
        for s, zz in work:
            line.along_z(s, zz)

        def done(s, total):
            target = qkv_sum.at[s] if s < parts else (out_sum if s == parts else small_sum)
            step = min(64, target.shape[0])

            def body(i, carry):
                r = pl.ds(pl.multiple_of(i * step, step), step)
                target[r, :] = total[r, :].astype(jnp.float32)
                return carry

            lax.fori_loop(0, target.shape[0] // step, body, 0)

        line.home(done)
        line.finish()

    return pl.pallas_call(
        kernel,
        out_shape=(
            jax.ShapeDtypeStruct((parts, rows, width), jnp.float32),
            jax.ShapeDtypeStruct((out_rows, columns), jnp.float32),
            jax.ShapeDtypeStruct(smalls.shape[1:], jnp.float32),
        ),
        in_specs=[VMEM] * 3,
        out_specs=(VMEM,) * 3,
        scratch_shapes=[
            pltpu.VMEM((3, NZ, parts, rows, width), jnp.bfloat16),
            pltpu.VMEM((3, NZ, out_rows, columns), jnp.bfloat16),
            pltpu.VMEM((3, NZ) + smalls.shape[1:], jnp.float32),
            pltpu.SemaphoreType.DMA((parts + 2, NZ, 3)),
            pltpu.SemaphoreType.DMA((parts + 2, NZ, 3)),
        ],
        compiler_params=comm_params(collective_id),
        cost_estimate=cost(120),
        name="weight_reduce",
    )(qkv, out, smalls)


def token_reduce(part, collective_id, pairs=None):
    tokens, width = part.shape
    rows = tokens // GROUPS
    half, quarter = width // 2, width // 4

    def kernel(part_ref, out_ref, core_buf, x_buf, y_buf, lo_buf, hi_buf,
               core_send, core_recv, x_send, x_recv, send_sem, recv_sem):
        z, y, x, c = place()
        across, twin = device(z, y, 1 - x, c), device(z, y, x, 1 - c)

        line = LineReduce(
            [0], lambda s, zz, yy: x_buf.at[zz * NY + yy], lambda s, zz: y_buf.at[zz],
            lambda s, zz: lo_buf.at[zz], lambda s, zz: hi_buf.at[zz], send_sem, recv_sem,
        )
        greet(line.partners() + [(across, None), (twin, None)])
        order = [(zz, flip) for zz in Z_ORDER for flip in (1, 0)]

        def number(zz, flip):
            return zz * NY + (1 - y if flip else y)

        def to_twin(zz, flip):
            b = number(zz, flip)
            return remote(
                part_ref.at[block_rows(b, rows), pl.ds(pl.multiple_of((1 - c) * half, half), half)],
                core_buf.at[b], core_send.at[zz, flip], core_recv.at[zz, flip], twin,
            )

        def to_across(zz, flip):
            b = number(zz, flip)
            return remote(
                core_buf.at[b, :, pl.ds(pl.multiple_of((1 - x) * quarter, quarter), quarter)],
                x_buf.at[b], x_send.at[zz, flip], x_recv.at[zz, flip], across,
            )

        def add_core(zz, flip):
            b = number(zz, flip)

            def store(r):
                at = pl.ds(pl.multiple_of(b * rows + r.start, 16), r.size)
                core_buf[b, r, :] = (
                    core_buf[b, r, :].astype(jnp.float32)
                    + part_ref[at, pl.ds(pl.multiple_of(c * half, half), half)].astype(jnp.float32)
                ).astype(jnp.bfloat16)

            add_into(rows, 32, store)

        def add_across(zz, flip):
            b = number(zz, flip)

            def store(r):
                x_buf[b, r, :] = (
                    x_buf[b, r, :].astype(jnp.float32)
                    + core_buf[b, r, pl.ds(pl.multiple_of(x * quarter, quarter), quarter)].astype(jnp.float32)
                ).astype(jnp.bfloat16)

            add_into(rows, 64, store)

        def stage_twin(i):
            to_twin(*order[i]).wait_recv()
            add_core(*order[i])
            to_across(*order[i]).start()

        def stage_across(i):
            zz, flip = order[i]
            to_across(zz, flip).wait_recv()
            add_across(zz, flip)
            if flip:
                line.to_y(0, zz)

        def stage_y(zz):
            line.along_z(0, zz)

        for zz, flip in order:
            to_twin(zz, flip).start()
        count = len(order)
        for i in range(count + 4):
            if i < count:
                stage_twin(i)
            if 0 <= i - 1 < count:
                stage_across(i - 1)
            if i >= 3 and (i - 3) % 2 == 0 and (i - 3) // 2 < NZ:
                stage_y(Z_ORDER[(i - 3) // 2])

        def done(s, total):
            def store(r):
                out_ref[r, :] = total[r, :]

            add_into(rows, 64, store)

        line.home(done)
        for zz, flip in order:
            to_twin(zz, flip).wait_send()
            to_across(zz, flip).wait_send()
        line.finish()

    return pl.pallas_call(
        kernel,
        out_shape=jax.ShapeDtypeStruct((rows, quarter), jnp.bfloat16),
        in_specs=[VMEM],
        out_specs=VMEM,
        scratch_shapes=[
            pltpu.VMEM((GROUPS, rows, half), jnp.bfloat16),
            pltpu.VMEM((GROUPS, rows, quarter), jnp.bfloat16),
            pltpu.VMEM((NZ, rows, quarter), jnp.bfloat16),
            pltpu.VMEM((NZ, rows, quarter), jnp.bfloat16),
            pltpu.VMEM((NZ, rows, quarter), jnp.bfloat16),
            pltpu.SemaphoreType.DMA((NZ, 2)),
            pltpu.SemaphoreType.DMA((NZ, 2)),
            pltpu.SemaphoreType.DMA((NZ, 2)),
            pltpu.SemaphoreType.DMA((NZ, 2)),
            pltpu.SemaphoreType.DMA((1, NZ, 3)),
            pltpu.SemaphoreType.DMA((1, NZ, 3)),
        ],
        compiler_params=comm_params(collective_id),
        cost_estimate=cost(60),
        name="token_reduce",
    )(part)


def gate_exchange(part, collective_id):
    groups = part.shape[0]
    tensors = NX * NC

    def kernel(part_ref, out_ref, landing, total, send_t, recv_t, send_e, recv_e):
        e = lax.axis_index("expert")
        t = lax.axis_index("tensor")
        mates = [(e, lax.rem(t + k, tensors)) for k in range(1, tensors)]
        peers = [(lax.rem(e + k, groups), t) for k in range(1, groups)]
        greet([(target, None) for target in mates + peers])
        near = [
            remote(part_ref, landing.at[k], send_t.at[k], recv_t.at[k], mates[k])
            for k in range(tensors - 1)
        ]
        for copy in near:
            copy.start()
        for copy in near:
            copy.wait_recv()
        value = part_ref[...]
        for k in range(tensors - 1):
            value = value + landing[k]
        total[...] = value
        far = [
            remote(
                total.at[lax.rem(e + k, groups)], out_ref.at[e], send_e.at[k - 1], recv_e.at[k - 1],
                peers[k - 1],
            )
            for k in range(1, groups)
        ]
        for copy in far:
            copy.start()
        out_ref[e] = total[e]
        for k in range(1, groups):
            source = out_ref.at[lax.rem(e + groups - k, groups)]
            remote(source, source, send_e.at[k - 1], recv_e.at[k - 1], peers[k - 1]).wait_recv()
        for copy in near + far:
            copy.wait_send()

    return pl.pallas_call(
        kernel,
        out_shape=jax.ShapeDtypeStruct(part.shape, jnp.float32),
        in_specs=[VMEM],
        out_specs=VMEM,
        scratch_shapes=[
            pltpu.VMEM((tensors - 1,) + part.shape, jnp.float32),
            pltpu.VMEM(part.shape, jnp.float32),
            pltpu.SemaphoreType.DMA((tensors - 1,)),
            pltpu.SemaphoreType.DMA((tensors - 1,)),
            pltpu.SemaphoreType.DMA((groups - 1,)),
            pltpu.SemaphoreType.DMA((groups - 1,)),
        ],
        compiler_params=comm_params(collective_id, 16),
        cost_estimate=cost(10),
        name="gate_exchange",
    )(part)


def dot(a, b, dims):
    return lax.dot_general(a, b, ((dims[:1], dims[1:]), ((), ())), preferred_element_type=jnp.float32)


def add_to(target, first, second, step=64):
    rows = target.shape[0]

    def body(i, carry):
        r = pl.ds(pl.multiple_of(i * step, step), step)
        total = first[r, :].astype(jnp.float32) + second[r, :].astype(jnp.float32)
        target[r, :] = total.astype(target.dtype)
        return carry

    lax.fori_loop(0, rows // step, body, 0)


def expert_layer(
    hidden_all, grad_out_all, gate_up, down, router_t, chosen_all, residual, collective_id
):
    tokens, width = hidden_all.shape
    rows = tokens // GROUPS
    units = down.shape[0]
    local = 2
    hidden = units // local
    experts = router_t.shape[0]
    half, part, piece = width // 2, width // 4, width // 8
    tensors = NX * NC
    steps = GROUPS + 5
    low = jnp.bfloat16
    wide = width // 4

    def kernel(
        h_in, dy_in, gu_ref, down_ref, router_ref, chosen_ref, x1_in,
        block_out, dh_out, gates_out, gate_w, up_w, down_w,
        h, dy, gated, dgu, dx, y_part, yc_buf, yx_buf, yy_buf, ylo_buf, yhi_buf, x1, gu_stage, d_stage,
        core_buf, px_buf, py_buf, qy_buf, qx_buf, z_sum, lo_buf, hi_buf, gate_part, gate_land,
        in_sem, x1_sem, yc_s, yc_r, yx_s, yx_r, yy_s, yy_r, yz_s, yz_r, gu_sem, d_sem, core_s, core_r, px_s, px_r, py_s, py_r, qy_s, qy_r, qx_s, qx_r,
        z_s, z_r, near_s, near_r, far_s, far_r, end_s, end_r,
    ):
        z, y, x, c = place()
        e, t = lax.axis_index("expert"), lax.axis_index("tensor")
        across, twin, beside = device(z, y, 1 - x, c), device(z, y, x, 1 - c), device(z, 1 - y, x, c)
        mates = [(e, lax.rem(t + k, tensors)) for k in range(1, tensors)]
        peers = [(lax.rem(e + k, GROUPS), t) for k in range(1, GROUPS)]
        greet([(target, None) for target in mates + peers])

        def zz_of(j):
            return jnp.where(j == 0, 3, jnp.where(j == 1, 0, jnp.where(j == 2, 2, 1)))

        def block_of(i):
            own = lax.rem(i, 2)
            return zz_of(lax.div(i, 2)) * NY + jnp.where(own == 1, y, 1 - y)

        def load(i):
            r = block_rows(block_of(i), rows)
            return (
                pltpu.make_async_copy(h_in.at[r, :], h.at[r, :], in_sem.at[0, i]),
                pltpu.make_async_copy(dy_in.at[r, :], dy.at[r, :], in_sem.at[1, i]),
            )

        def start_load(i, carry):
            for copy in load(i):
                copy.start()
            return carry

        lax.fori_loop(0, GROUPS, start_load, 0)
        x1_copy = pltpu.make_async_copy(
            x1_in.at[:, pl.ds(pl.multiple_of(c * half + x * part, part), part)], x1, x1_sem
        )
        x1_copy.start()

        def to_twin(i):
            b = block_of(i)
            return remote(
                dx.at[lax.rem(i, 2), :, pl.ds(pl.multiple_of((1 - c) * half, half), half)],
                core_buf.at[b], core_s.at[i], core_r.at[i], twin,
            )

        def p_across(i):
            b = block_of(i)
            return remote(
                core_buf.at[b, :, pl.ds(pl.multiple_of((1 - x) * piece, piece), piece)],
                px_buf.at[b], px_s.at[i], px_r.at[i], across,
            )

        def p_beside(j):
            return remote(px_buf.at[block_of(2 * j)], py_buf.at[j], py_s.at[j], py_r.at[j], beside)

        def q_beside(j):
            return remote(
                core_buf.at[block_of(2 * j), :, pl.ds(part, part)], qy_buf.at[j], qy_s.at[j], qy_r.at[j], beside
            )

        def q_across(j):
            return remote(
                qy_buf.at[j, :, pl.ds(pl.multiple_of((1 - x) * piece, piece), piece)],
                qx_buf.at[j], qx_s.at[j], qx_r.at[j], across,
            )

        def up(j, s):
            return remote(z_sum.at[s, j], lo_buf.at[s, j], z_s.at[0, s, j], z_r.at[0, s, j], device(z + 1, y, x, c))

        def down_z(j, s):
            return remote(z_sum.at[s, j], hi_buf.at[s, j], z_s.at[1, s, j], z_r.at[1, s, j], device(z - 1, y, x, c))

        def take_twin(i):
            to_twin(i).wait_recv()
            b = block_of(i)
            mine = core_buf.at[b]
            add_to(mine, mine, dx.at[lax.rem(i, 2), :, pl.ds(pl.multiple_of(c * half, half), half)], 32)
            p_across(i).start()
            pl.when(lax.rem(i, 2) == 0)(lambda: q_beside(lax.div(i, 2)).start())

        def take_p_across(i):
            p_across(i).wait_recv()
            b = block_of(i)
            add_to(
                px_buf.at[b], px_buf.at[b],
                core_buf.at[b, :, pl.ds(pl.multiple_of(x * piece, piece), piece)],
            )

        def take_q_beside(j):
            q_beside(j).wait_recv()
            add_to(qy_buf.at[j], qy_buf.at[j], core_buf.at[block_of(2 * j + 1), :, pl.ds(part, part)])
            q_across(j).start()

        def take_q_across(j):
            q_across(j).wait_recv()
            add_to(
                z_sum.at[1, j], qx_buf.at[j], qy_buf.at[j, :, pl.ds(pl.multiple_of(x * piece, piece), piece)]
            )

        def take_p_beside(j):
            p_beside(j).wait_recv()
            add_to(z_sum.at[0, j], py_buf.at[j], px_buf.at[block_of(2 * j + 1)])

        def hop(j, k):
            zz = zz_of(j)

            def upward():
                for s in range(2):
                    if k > 0:
                        up(j, s).wait_recv()
                        add_to(z_sum.at[s, j], z_sum.at[s, j], lo_buf.at[s, j])
                    up(j, s).start()

            def downward():
                for s in range(2):
                    if k > 0:
                        down_z(j, s).wait_recv()
                        add_to(z_sum.at[s, j], z_sum.at[s, j], hi_buf.at[s, j])
                    down_z(j, s).start()

            pl.when((z < zz) & (z == k))(upward)
            pl.when((z > zz) & (NZ - 1 - z == k))(downward)

        def y_twin(i):
            return remote(
                y_part.at[lax.rem(i, 2), :, pl.ds(pl.multiple_of((1 - c) * half, half), half)],
                yc_buf.at[block_of(i)], yc_s.at[i], yc_r.at[i], twin,
            )

        def y_across(i):
            b = block_of(i)
            return remote(
                yc_buf.at[b, :, pl.ds(pl.multiple_of((1 - x) * part, part), part)],
                yx_buf.at[b], yx_s.at[i], yx_r.at[i], across,
            )

        def y_beside(j):
            return remote(yx_buf.at[block_of(2 * j)], yy_buf.at[j], yy_s.at[j], yy_r.at[j], beside)

        def y_up(j):
            return remote(yy_buf.at[j], ylo_buf.at[j], yz_s.at[0, j], yz_r.at[0, j], device(z + 1, y, x, c))

        def y_down(j):
            return remote(yy_buf.at[j], yhi_buf.at[j], yz_s.at[1, j], yz_r.at[1, j], device(z - 1, y, x, c))

        def take_y_twin(i):
            y_twin(i).wait_recv()
            mine = yc_buf.at[block_of(i)]
            add_to(mine, mine, y_part.at[lax.rem(i, 2), :, pl.ds(pl.multiple_of(c * half, half), half)], 32)
            y_across(i).start()

        def take_y_across(i):
            y_across(i).wait_recv()
            b = block_of(i)
            mine = yx_buf.at[b]
            add_to(mine, mine, yc_buf.at[b, :, pl.ds(pl.multiple_of(x * part, part), part)])
            pl.when(lax.rem(i, 2) == 0)(lambda: y_beside(lax.div(i, 2)).start())

        def take_y_beside(j):
            y_beside(j).wait_recv()
            add_to(yy_buf.at[j], yy_buf.at[j], yx_buf.at[block_of(2 * j + 1)])

        def y_hop(j, k):
            zz = zz_of(j)

            def upward():
                if k > 0:
                    y_up(j).wait_recv()
                    add_to(yy_buf.at[j], yy_buf.at[j], ylo_buf.at[j])
                y_up(j).start()

            def downward():
                if k > 0:
                    y_down(j).wait_recv()
                    add_to(yy_buf.at[j], yy_buf.at[j], yhi_buf.at[j])
                y_down(j).start()

            pl.when((z < zz) & (z == k))(upward)
            pl.when((z > zz) & (NZ - 1 - z == k))(downward)

        def front(i):
            for copy in load(i):
                copy.wait()
            b = block_of(i)
            r = block_rows(b, rows)
            rows_h, rows_dy = h[r, :], dy[r, :]
            logits = dot(rows_h, router_ref[...], (1, 1))
            shifted = jnp.exp(logits - jnp.max(logits, axis=-1, keepdims=True))
            probs = shifted / jnp.sum(shifted, axis=-1, keepdims=True) * chosen_ref[r, :].astype(jnp.float32)
            lane = lax.broadcasted_iota(jnp.int32, probs.shape, 1)
            line = lax.broadcasted_iota(jnp.int32, (rows, 128), 1)
            found = jnp.zeros((rows, 128), jnp.float32)
            for expert in range(local):
                at, up_at = pl.ds(expert * hidden, hidden), pl.ds((local + expert) * hidden, hidden)
                gate = jnp.sum(jnp.where(lane == e * local + expert, probs, 0.0), axis=-1, keepdims=True)
                pre = dot(rows_h, gu_ref[:, at], (1, 0))
                scale = dot(rows_h, gu_ref[:, up_at], (1, 0))
                back = dot(rows_dy, down_ref[at, :], (1, 1))
                sigmoid = jax.nn.sigmoid(pre)
                swish = pre * sigmoid
                active = swish * scale
                gated[r, at] = (active * gate).astype(low)
                found = jnp.where(line == expert, jnp.sum(active * back, axis=-1, keepdims=True), found)
                back = back * gate
                dgu[r, at] = (back * scale * sigmoid * (1.0 + pre * (1.0 - sigmoid))).astype(low)
                dgu[r, up_at] = (back * swish).astype(low)
            gate_part[b] = jnp.transpose(found)[:8, :]

        def rear(i):
            r = block_rows(block_of(i), rows)
            slot = lax.rem(i, 2)
            pl.when(i >= 2)(lambda: to_twin(i - 2).wait_send())

            def columns(k, carry):
                at = pl.ds(pl.multiple_of(k * wide, wide), wide)
                dx[slot, :, at] = dot(dgu[r, :], gu_ref[at, :], (1, 1)).astype(low)
                return carry

            lax.fori_loop(0, width // wide, columns, 0)
            to_twin(i).start()
            pl.when(i >= 2)(lambda: y_twin(i - 2).wait_send())

            def y_columns(k, carry):
                at = pl.ds(pl.multiple_of(k * wide, wide), wide)
                y_part[slot, :, at] = dot(gated[r, :], down_ref[:, at], (1, 0)).astype(low)
                return carry

            lax.fori_loop(0, width // wide, y_columns, 0)
            y_twin(i).start()

        tiles = width // piece // 4
        d_width = width // 8

        def gu_copies(n):
            slot = lax.rem(n, 2)
            at = pl.ds(pl.multiple_of(n * piece, piece), piece)
            return [
                pltpu.make_async_copy(
                    gu_stage.at[slot, :, pl.ds(k * hidden, hidden)],
                    (gate_w if k < local else up_w).at[k % local, at, :],
                    gu_sem.at[slot, k],
                )
                for k in range(2 * local)
            ]

        def d_copies(n):
            slot = lax.rem(n, 2)
            at = pl.ds(pl.multiple_of(n * d_width, d_width), d_width)
            return [
                pltpu.make_async_copy(
                    d_stage.at[slot, pl.ds(k * hidden, hidden), :], down_w.at[k, :, at], d_sem.at[slot, k]
                )
                for k in range(local)
            ]

        def each(copies, what):
            for copy in copies:
                getattr(copy, what)()

        def weight_grads(q):
            def tile(k, carry):
                n = q * tiles + k
                pl.when(n >= 2)(lambda: each(gu_copies(n - 2), "wait"))
                at = pl.ds(pl.multiple_of(n * piece, piece), piece)
                gu_stage[lax.rem(n, 2)] = dot(h[:, at], dgu[...], (0, 0))
                each(gu_copies(n), "start")
                return carry

            lax.fori_loop(0, tiles, tile, 0)

            def d_tile(k, carry):
                n = q * 2 + k
                pl.when(n >= 2)(lambda: each(d_copies(n - 2), "wait"))
                at = pl.ds(pl.multiple_of(n * d_width, d_width), d_width)
                d_stage[lax.rem(n, 2)] = dot(gated[...], dy[:, at], (0, 0))
                each(d_copies(n), "start")
                return carry

            lax.fori_loop(0, 2, d_tile, 0)

        near = [
            remote(gate_part, gate_land.at[k], near_s.at[k], near_r.at[k], mates[k])
            for k in range(tensors - 1)
        ]

        def far(k):
            return remote(
                gate_land.at[tensors - 1, lax.rem(e + k, GROUPS)], gates_out.at[e],
                far_s.at[k - 1], far_r.at[k - 1], peers[k - 1],
            )

        def sum_near():
            for copy in near:
                copy.wait_recv()
            total = gate_part[...]
            for k in range(tensors - 1):
                total = total + gate_land[k]
            gate_land[tensors - 1] = total
            for k in range(1, GROUPS):
                far(k).start()
            gates_out[e] = gate_land[tensors - 1, e]

        def step(i, carry):
            j_even, j_odd = lax.div(i, 2) - 1, lax.div(i - 1, 2) - 1
            even = lax.rem(i, 2) == 0
            pl.when(i < GROUPS)(lambda: front(i))
            pl.when((i >= 1) & (i <= GROUPS))(lambda: take_twin(i - 1))
            pl.when((i >= 1) & (i <= GROUPS))(lambda: take_y_twin(i - 1))
            pl.when(even & (i >= 2) & (i <= GROUPS))(lambda: take_q_beside(j_even))

            def late():
                take_p_across(i - 2)
                take_q_across(j_odd)

            pl.when((lax.rem(i, 2) == 1) & (i >= 3) & (i <= GROUPS + 1))(late)
            pl.when(i == GROUPS)(lambda: each(near, "start"))
            pl.when(i == GROUPS + 1)(sum_near)
            pl.when(i < GROUPS)(lambda: rear(i))
            pl.when((i >= GROUPS) & (i < GROUPS + 4))(lambda: weight_grads(i - GROUPS))

            def pass_p():
                take_p_across(i - 2)
                p_beside(j_even).start()

            pl.when(even & (i >= 2) & (i <= GROUPS))(pass_p)

            def join():
                take_p_beside(j_odd)
                hop(j_odd, 0)

            pl.when((lax.rem(i, 2) == 1) & (i >= 3) & (i <= GROUPS + 1))(join)
            pl.when(even & (i >= 4) & (i <= GROUPS + 2))(lambda: hop(j_even - 1, 1))
            pl.when((lax.rem(i, 2) == 1) & (i >= 5) & (i <= GROUPS + 3))(lambda: hop(j_odd - 1, 2))
            pl.when((i >= 2) & (i <= GROUPS + 1))(lambda: take_y_across(i - 2))

            def join_y():
                take_y_beside(j_even - 1)
                y_hop(j_even - 1, 0)

            pl.when(even & (i >= 4) & (i <= GROUPS + 2))(join_y)
            pl.when((lax.rem(i, 2) == 1) & (i >= 5) & (i <= GROUPS + 3))(lambda: y_hop(j_odd - 1, 1))
            pl.when(even & (i >= 6) & (i <= GROUPS + 4))(lambda: y_hop(j_even - 2, 2))
            return carry

        lax.fori_loop(0, steps, step, 0)

        def columns_of(s, xx, cc):
            return pl.ds(pl.multiple_of(cc * half + s * part + xx * piece, piece), piece)

        mine = jnp.where(z == 3, 0, jnp.where(z == 0, 1, jnp.where(z == 2, 2, 3)))
        for s in range(2):
            def below(s=s):
                up(mine, s).wait_recv()
                add_to(z_sum.at[s, mine], z_sum.at[s, mine], lo_buf.at[s, mine])

            def above(s=s):
                down_z(mine, s).wait_recv()
                add_to(z_sum.at[s, mine], z_sum.at[s, mine], hi_buf.at[s, mine])

            pl.when(z > 0)(below)
            pl.when(z < NZ - 1)(above)
            own = dh_out.at[:, columns_of(s, x, c)]

            def keep(k, carry, s=s, own=own):
                r = pl.ds(pl.multiple_of(k * 64, 64), 64)
                own[r, :] = z_sum[s, mine, r, :]
                return carry

            lax.fori_loop(0, rows // 64, keep, 0)
            remote(own, own, end_s.at[0, s], end_r.at[0, s], across).start()
            remote(own, own, end_s.at[1, s], end_r.at[1, s], twin).start()
        def y_columns_of(xx, cc):
            return pl.ds(pl.multiple_of(cc * half + xx * part, part), part)

        def y_below():
            y_up(mine).wait_recv()
            add_to(yy_buf.at[mine], yy_buf.at[mine], ylo_buf.at[mine])

        def y_above():
            y_down(mine).wait_recv()
            add_to(yy_buf.at[mine], yy_buf.at[mine], yhi_buf.at[mine])

        pl.when(z > 0)(y_below)
        pl.when(z < NZ - 1)(y_above)
        x1_copy.wait()
        y_own = block_out.at[:, y_columns_of(x, c)]

        def finish(k, carry):
            r = pl.ds(pl.multiple_of(k * 64, 64), 64)
            y_own[r, :] = (x1[r, :] + yy_buf[mine, r, :].astype(jnp.float32)).astype(low)
            return carry

        lax.fori_loop(0, rows // 64, finish, 0)
        remote(y_own, y_own, end_s.at[0, 2], end_r.at[0, 2], across).start()
        remote(y_own, y_own, end_s.at[1, 2], end_r.at[1, 2], twin).start()
        for s in range(2):
            there = dh_out.at[:, columns_of(s, 1 - x, c)]
            remote(there, there, end_s.at[0, s], end_r.at[0, s], across).wait_recv()
            remote(there, there, end_s.at[2, s], end_r.at[2, s], twin).start()
        there = block_out.at[:, y_columns_of(1 - x, c)]
        remote(there, there, end_s.at[0, 2], end_r.at[0, 2], across).wait_recv()
        remote(there, there, end_s.at[2, 2], end_r.at[2, 2], twin).start()
        for k, xx in ((1, x), (2, 1 - x)):
            there = block_out.at[:, y_columns_of(xx, 1 - c)]
            remote(there, there, end_s.at[k, 2], end_r.at[k, 2], twin).wait_recv()
        for k, target in ((0, across), (1, twin), (2, twin)):
            there = block_out.at[:, y_columns_of(1 - x if k == 2 else x, c)]
            remote(there, there, end_s.at[k, 2], end_r.at[k, 2], target).wait_send()
        for s in range(2):
            for k, xx in ((1, x), (2, 1 - x)):
                there = dh_out.at[:, columns_of(s, xx, 1 - c)]
                remote(there, there, end_s.at[k, s], end_r.at[k, s], twin).wait_recv()
            for k, target in ((0, across), (1, twin), (2, twin)):
                there = dh_out.at[:, columns_of(s, 1 - x if k == 2 else x, c)]
                remote(there, there, end_s.at[k, s], end_r.at[k, s], target).wait_send()
        for k in range(1, GROUPS):
            there = gates_out.at[lax.rem(e + GROUPS - k, GROUPS)]
            remote(there, there, far_s.at[k - 1], far_r.at[k - 1], peers[k - 1]).wait_recv()
            far(k).wait_send()
        each(near, "wait_send")

        def drain(i, carry):
            pl.when(i >= GROUPS - 2)(lambda: to_twin(i).wait_send())
            pl.when(i >= GROUPS - 2)(lambda: y_twin(i).wait_send())
            p_across(i).wait_send()
            y_across(i).wait_send()
            return carry

        lax.fori_loop(0, GROUPS, drain, 0)

        def drain_pair(j, carry):
            p_beside(j).wait_send()
            q_beside(j).wait_send()
            q_across(j).wait_send()
            y_beside(j).wait_send()
            pl.when(z < zz_of(j))(lambda: y_up(j).wait_send())
            pl.when(z > zz_of(j))(lambda: y_down(j).wait_send())
            for s in range(2):
                pl.when(z < zz_of(j))(lambda s=s: up(j, s).wait_send())
                pl.when(z > zz_of(j))(lambda s=s: down_z(j, s).wait_send())
            return carry

        lax.fori_loop(0, NZ, drain_pair, 0)
        for k in range(2):
            each(gu_copies(4 * tiles - 2 + k), "wait")
            each(d_copies(6 + k), "wait")

    shape = jax.ShapeDtypeStruct
    dma = pltpu.SemaphoreType.DMA
    f32 = jnp.float32
    return pl.pallas_call(
        kernel,
        out_shape=(
            shape((rows, width), low),
            shape((rows, width), low),
            shape((GROUPS, 8, rows), f32),
            shape((local, width, hidden), f32),
            shape((local, width, hidden), f32),
            shape((local, hidden, width), f32),
        ),
        in_specs=[HBM, HBM, VMEM, VMEM, VMEM, VMEM, HBM],
        out_specs=(VMEM, VMEM, VMEM, HBM, HBM, HBM),
        scratch_shapes=[
            pltpu.VMEM((tokens, width), low),
            pltpu.VMEM((tokens, width), low),
            pltpu.VMEM((tokens, units), low),
            pltpu.VMEM((tokens, 2 * units), low),
            pltpu.VMEM((2, rows, width), low),
            pltpu.VMEM((2, rows, width), low),
            pltpu.VMEM((GROUPS, rows, half), low),
            pltpu.VMEM((GROUPS, rows, part), low),
            pltpu.VMEM((NZ, rows, part), low),
            pltpu.VMEM((NZ, rows, part), low),
            pltpu.VMEM((NZ, rows, part), low),
            pltpu.VMEM((rows, part), f32),
            pltpu.VMEM((2, piece, 2 * units), f32),
            pltpu.VMEM((2, units, width // 8), f32),
            pltpu.VMEM((GROUPS, rows, half), low),
            pltpu.VMEM((GROUPS, rows, piece), low),
            pltpu.VMEM((NZ, rows, piece), low),
            pltpu.VMEM((NZ, rows, part), low),
            pltpu.VMEM((NZ, rows, piece), low),
            pltpu.VMEM((2, NZ, rows, piece), low),
            pltpu.VMEM((2, NZ, rows, piece), low),
            pltpu.VMEM((2, NZ, rows, piece), low),
            pltpu.VMEM((GROUPS, 8, rows), f32),
            pltpu.VMEM((tensors, GROUPS, 8, rows), f32),
            dma((2, GROUPS)), dma, dma((GROUPS,)), dma((GROUPS,)), dma((GROUPS,)), dma((GROUPS,)),
            dma((NZ,)), dma((NZ,)), dma((2, NZ)), dma((2, NZ)), dma((2, 2 * local)), dma((2, local)),
            dma((GROUPS,)), dma((GROUPS,)), dma((GROUPS,)), dma((GROUPS,)),
            dma((NZ,)), dma((NZ,)), dma((NZ,)), dma((NZ,)), dma((NZ,)), dma((NZ,)),
            dma((2, 2, NZ)), dma((2, 2, NZ)),
            dma((tensors - 1,)), dma((tensors - 1,)), dma((GROUPS - 1,)), dma((GROUPS - 1,)),
            dma((3, 3)), dma((3, 3)),
        ],
        compiler_params=comm_params(collective_id, 62),
        cost_estimate=cost(80),
        name="expert_layer",
    )(hidden_all, grad_out_all, gate_up, down, router_t, chosen_all, residual)


def exchange_rows(value, part_ref, land_ref, send_sem, recv_sem, mates):
    rows = value.shape[0]
    line = lax.broadcasted_iota(jnp.int32, (rows, 128), 1)
    part_ref[...] = jnp.transpose(jnp.where(line == 0, value, 0.0))[:8, :]
    for k, mate in enumerate(mates):
        remote(part_ref, land_ref.at[k], send_sem.at[k], recv_sem.at[k], mate).start()


def exchanged_rows(part_ref, land_ref, send_sem, recv_sem, mates):
    total = part_ref[...]
    for k, mate in enumerate(mates):
        remote(part_ref, land_ref.at[k], send_sem.at[k], recv_sem.at[k], mate).wait_recv()
    for k in range(len(mates)):
        total = total + land_ref[k]
    rows = part_ref.shape[1]
    tall = jnp.concatenate([total, jnp.zeros((120, rows), jnp.float32)], axis=0)
    return jnp.transpose(tall)[:, :1]


def drain_rows(part_ref, land_ref, send_sem, recv_sem, mates):
    for k, mate in enumerate(mates):
        remote(part_ref, land_ref.at[k], send_sem.at[k], recv_sem.at[k], mate).wait_send()


def turn(value, cosine, sine):
    return value * cosine + pltpu.roll(value, HEAD // 2, 1) * sine


def project(tokens, w_qkv, smalls, cosine, sine, collective_id):
    rows, width = tokens.shape
    parts, depth, columns = w_qkv.shape
    heads = columns // HEAD
    tensors = NX * NC
    back = WINDOW // rows
    low, f32 = jnp.bfloat16, jnp.float32
    QUERY, KEY, VALUE, SMALL = 0, 1, 2, 3

    def kernel(
        tok_ref, w_ref, small_ref, cos_ref, sin_ref,
        w_all, small_all, h1_ref, raw_ref, scale_ref, q_ref, context,
        own_w, weights, total, part_k, land_k, part_q, land_q,
        send_sem, recv_sem, out_sem, small_sem, ks_s, ks_r, qs_s, qs_r, c_s, c_r,
    ):
        z, y, x, c = place()
        e, t = lax.axis_index("expert"), lax.axis_index("tensor")
        mates = [(e, lax.rem(t + k, tensors)) for k in range(1, tensors)]
        beside, above = device(z, 1 - y, x, c), device(z + 1, y, x, c)
        views = [
            lambda b: weights.at[QUERY, block_rows(b, depth), :],
            lambda b: weights.at[KEY, block_rows(b, depth), :],
            lambda b: weights.at[VALUE, block_rows(b, depth), :],
            lambda b: small_all.at[b],
        ]
        line = LineGather(
            [SMALL, VALUE, KEY, QUERY], [own_w.at[0], own_w.at[1], own_w.at[2], small_ref], views,
            send_sem, recv_sem,
        )
        greet(line.partners() + [(mate, None) for mate in mates])
        line.start(SMALL, 0)
        for part in (VALUE, KEY, QUERY):
            def cast(i, carry, part=part):
                r = pl.ds(pl.multiple_of(i * 32, 32), 32)
                own_w[part, r, :] = w_ref[part, r, :].astype(low)
                return carry

            lax.fori_loop(0, depth // 32, cast, 0)
            if part != QUERY:
                line.start(part, 0)

        def square(i, carry):
            r = pl.ds(pl.multiple_of(i * 32, 32), 32)
            value = tok_ref[r, :].astype(f32)
            scale_ref[r, 0:1] = lax.rsqrt(jnp.mean(value * value, axis=-1, keepdims=True) + EPS)
            return carry

        lax.fori_loop(0, rows // 32, square, 0)
        total[...] = jnp.zeros_like(total)
        own_small = pltpu.make_async_copy(small_ref, small_all.at[line.block(0)], small_sem)
        own_small.start()

        def use(stream, rel):
            b = line.block(rel)
            at = pl.ds(pl.multiple_of(b * depth, depth), depth)
            if stream == SMALL:
                gain = small_ref[0:1, :] if rel == 0 else small_all[b, 0:1, :]
                h1_ref[:, at] = (tok_ref[:, at].astype(f32) * scale_ref[:, 0:1] * gain).astype(low)
                return
            block = own_w[stream] if rel == 0 else weights[stream, block_rows(b, depth), :]
            total[stream] += dot(h1_ref[:, at], block, (1, 0))

        def event(stream, rel):
            def body():
                line.arrive(stream, rel)
                if rel < 7:
                    marks = len(line.pending)
                    line.start(stream, rel)
                    late = line.pending[marks:]
                    del line.pending[marks:]
                    line.finish_later(late, rel)
                use(stream, rel)
            run_if(line.exists(rel), body)

        use(SMALL, 0)
        use(VALUE, 0)
        own_small.wait()
        use(KEY, 0)
        early, late = [7, 1, 4, 8, 11, 2, 5], [9, 12, 3, 6, 10, 13]
        for rel in early:
            event(SMALL, rel)
            event(VALUE, rel)
        line.start(QUERY, 0)
        for rel in late:
            event(SMALL, rel)
            event(VALUE, rel)

        def context_copy(which, k):
            if k == 2:
                source, target = 0, above
            elif k == 4:
                source, target = 2, above
            else:
                source, target = jnp.where(y == 0, k - 1, k + 1), beside
            return remote(
                context.at[source, which], context.at[k, which], c_s.at[which, k], c_r.at[which, k], target
            )

        sends = {2: z < NZ - 1, 4: (z >= 1) & (z < NZ - 1), 1: (y == 0) | (z >= 1), 3: z >= 1 + y}
        takes = {2: z >= 1, 4: z >= 2, 1: (y == 1) | (z >= 1), 3: z >= 2 - y}

        def context_send(which, k):
            run_if(sends[k], lambda: context_copy(which, k).start())

        def context_take(which, k):
            run_if(takes[k], lambda: context_copy(which, k).wait_recv())

        for k in range(1, back + 1):
            def clear(k=k):
                context[k] = jnp.zeros_like(context[k])
            run_if(jnp.logical_not(takes[k]), clear)

        context[0, 1] = total[VALUE].astype(low)
        context_send(1, 2)
        run_if(y == 0, lambda: context_copy(1, 1).start())
        for rel in early:
            event(KEY, rel)
        for rel in late:
            event(KEY, rel)
        key_raw = total[KEY]
        raw_ref[1] = key_raw
        exchange_rows(jnp.sum(key_raw * key_raw, axis=-1, keepdims=True), part_k, land_k, ks_s, ks_r, mates)
        use(QUERY, 0)
        for rel in early[:3]:
            event(QUERY, rel)

        key_scale = lax.rsqrt(exchanged_rows(part_k, land_k, ks_s, ks_r, mates) / width + EPS)
        scale_ref[:, 2:3] = key_scale
        slices = HEAD // GROUPS
        gains = []
        for which in range(2):
            per_head = []
            for head in range(heads):
                start = (which * heads + head) * slices
                per_head.append(
                    jnp.concatenate([small_all[b, 2:3, start : start + slices] for b in range(GROUPS)], axis=1)
                )
            gains.append(per_head)

        def rotated(which, scale, store):
            for head in range(heads):
                at = pl.ds(head * HEAD, HEAD)
                value = total[which, :, at] * scale * gains[which][head]
                store(at, turn(value, cos_ref[...], sin_ref[...]).astype(low))

        def store_key(at, value):
            context[0, 0, :, at] = value

        rotated(KEY, key_scale, store_key)
        context_send(0, 2)
        run_if(y == 0, lambda: context_copy(0, 1).start())

        def relay_two(which):
            context_take(which, 2)
            context_send(which, 4)
            run_if((y == 1) & (z >= 1), lambda: context_copy(which, 1).start())
            run_if((y == 0) & sends[3], lambda: context_copy(which, 3).start())

        def relay_four(which):
            context_take(which, 4)
            run_if((y == 1) & sends[3], lambda: context_copy(which, 3).start())

        relay_two(1)
        for rel in early[3:]:
            event(QUERY, rel)
        relay_four(1)
        for rel in late[:4]:
            event(QUERY, rel)
        relay_two(0)
        for rel in late[4:]:
            event(QUERY, rel)
        query_raw = total[QUERY]
        raw_ref[0] = query_raw
        exchange_rows(jnp.sum(query_raw * query_raw, axis=-1, keepdims=True), part_q, land_q, qs_s, qs_r, mates)
        for part in range(parts):
            weights[part, block_rows(line.block(0), depth), :] = own_w[part]
        keep = pltpu.make_async_copy(weights, w_all, out_sem)
        keep.start()
        relay_four(0)
        query_scale = lax.rsqrt(exchanged_rows(part_q, land_q, qs_s, qs_r, mates) / width + EPS)
        scale_ref[:, 1:2] = query_scale

        def store_query(at, value):
            q_ref[:, at] = value

        rotated(QUERY, query_scale, store_query)
        for which in (1, 0):
            for k in (1, 3):
                context_take(which, k)
        line.finish()
        for which in range(2):
            for k in range(1, back + 1):
                run_if(sends[k], lambda which=which, k=k: context_copy(which, k).wait_send())
        drain_rows(part_k, land_k, ks_s, ks_r, mates)
        drain_rows(part_q, land_q, qs_s, qs_r, mates)
        keep.wait()

    shape, dma = jax.ShapeDtypeStruct, pltpu.SemaphoreType.DMA
    return pl.pallas_call(
        kernel,
        out_shape=(
            shape((parts, depth * GROUPS, columns), low),
            shape((GROUPS,) + smalls.shape, f32),
            shape((rows, width), low),
            shape((2, rows, columns), f32),
            shape((rows, 128), f32),
            shape((rows, columns), low),
            shape((back + 1, 2, rows, columns), low),
        ),
        in_specs=[VMEM] * 5,
        out_specs=(HBM,) + (VMEM,) * 6,
        scratch_shapes=[
            pltpu.VMEM((parts, depth, columns), low),
            pltpu.VMEM((parts, depth * GROUPS, columns), low),
            pltpu.VMEM((parts, rows, columns), f32),
            pltpu.VMEM((8, rows), f32),
            pltpu.VMEM((tensors - 1, 8, rows), f32),
            pltpu.VMEM((8, rows), f32),
            pltpu.VMEM((tensors - 1, 8, rows), f32),
            dma((4, 7, 3)), dma((4, 14)), dma, dma,
            dma((tensors - 1,)), dma((tensors - 1,)), dma((tensors - 1,)), dma((tensors - 1,)),
            dma((2, back + 1)), dma((2, back + 1)),
        ],
        compiler_params=comm_params(collective_id, 48),
        cost_estimate=cost(100),
        name="project",
    )(tokens, w_qkv, smalls, cosine, sine)


def attend(query, context, segment_query, segment_keys, tokens, out_low, gain, collective_id):
    rows, columns = query.shape
    width = tokens.shape[1]
    blocks = context.shape[0]
    heads = columns // HEAD
    half, quarter = width // 2, width // 4
    low, f32 = jnp.bfloat16, jnp.float32

    def kernel(
        q_ref, context_ref, sq_ref, sk_ref, tok_ref, out_ref, gain_ref,
        o_ref, lse_ref, x1_ref, h2_ref, scale_ref,
        part, full, core_buf, x_buf, send_sem, recv_sem,
    ):
        z, y, x, c = place()
        across, twin = device(z, y, 1 - x, c), device(z, y, x, 1 - c)
        greet([(across, None), (twin, None)])
        row = lax.broadcasted_iota(jnp.int32, (rows, rows), 0)
        column = lax.broadcasted_iota(jnp.int32, (rows, rows), 1)
        allowed = []
        for k in range(blocks):
            distance = row - column + k * rows
            allowed.append(
                (sq_ref[...] == sk_ref[k : k + 1, :]) & (distance >= 0) & (distance < WINDOW)
            )
        line = lax.broadcasted_iota(jnp.int32, (rows, 128), 1)
        lse = jnp.zeros((rows, 128), f32)
        for head in range(heads):
            at = pl.ds(head * HEAD, HEAD)
            scores = [
                jnp.where(
                    allowed[k], dot(q_ref[:, at], context_ref[k, 0, :, at], (1, 1)) * HEAD ** (-0.5), -1e30
                )
                for k in range(blocks)
            ]
            largest = scores[0]
            for k in range(1, blocks):
                largest = jnp.maximum(largest, scores[k])
            largest = jnp.max(largest, axis=-1, keepdims=True)
            weights = [jnp.exp(s - largest) for s in scores]
            amount = weights[0]
            for k in range(1, blocks):
                amount = amount + weights[k]
            amount = jnp.sum(amount, axis=-1, keepdims=True)
            inverse = 1.0 / amount
            value = jnp.zeros((rows, HEAD), f32)
            for k in range(blocks):
                value = value + dot((weights[k] * inverse).astype(low), context_ref[k, 1, :, at], (1, 0))
            o_ref[:, at] = value.astype(low)
            lse = jnp.where(line == head, largest + jnp.log(amount), lse)
        lse_ref[...] = lse

        def half_of(cc):
            return pl.ds(pl.multiple_of(cc * half, half), half)

        def fill(cc):
            def body(k, carry):
                at = pl.ds(pl.multiple_of(cc * half + k * quarter, quarter), quarter)
                part[:, at] = dot(o_ref[...], out_ref[:, at], (1, 0)).astype(low)
                return carry

            lax.fori_loop(0, 2, body, 0)

        fill(1 - c)
        group_sum(part, full, core_buf, x_buf, send_sem, recv_sem, lambda: fill(c))

        def norm(i, carry):
            r = pl.ds(pl.multiple_of(i * 32, 32), 32)
            value = tok_ref[r, :].astype(f32) + full[r, :].astype(f32)
            scale = lax.rsqrt(jnp.mean(value * value, axis=-1, keepdims=True) + EPS)
            x1_ref[r, :] = value
            scale_ref[r, :] = jnp.broadcast_to(scale, (32, 128))
            h2_ref[r, :] = (value * scale * gain_ref[...]).astype(low)
            return carry

        lax.fori_loop(0, rows // 32, norm, 0)

    shape, dma = jax.ShapeDtypeStruct, pltpu.SemaphoreType.DMA
    return pl.pallas_call(
        kernel,
        out_shape=(
            shape((rows, columns), low),
            shape((rows, 128), f32),
            shape((rows, width), f32),
            shape((rows, width), low),
            shape((rows, 128), f32),
        ),
        in_specs=[VMEM] * 7,
        out_specs=(VMEM,) * 5,
        scratch_shapes=[
            pltpu.VMEM((rows, width), low),
            pltpu.VMEM((rows, width), low),
            pltpu.VMEM((rows, half), low),
            pltpu.VMEM((rows, quarter), low),
            dma((5,)), dma((5,)),
        ],
        compiler_params=comm_params(collective_id, 40),
        cost_estimate=cost(40),
        name="attend",
    )(query, context, segment_query, segment_keys, tokens, out_low, gain)


def attend_back(
    grad_hidden, grad_probs, router_t, hidden_two, residual, scale_two, gain_two, out_grad,
    query, context, segment_query, segment_keys, attended, log_sums, raw, scales, qk_gains,
    cosine, sine, hidden_one, tokens, gain_one, qkv_low, out_low, collective_id,
):
    rows, width = tokens.shape
    columns = query.shape[1]
    heads = columns // HEAD
    experts = router_t.shape[0]
    blocks = context.shape[0]
    depth = width // GROUPS
    small_rows = 8 + experts
    tensors = NX * NC
    half, quarter = width // 2, width // 4
    low, f32 = jnp.bfloat16, jnp.float32
    QUERY, KEY, VALUE, OUT, SMALL = 0, 1, 2, 3, 4

    def kernel(
        dh_ref, gates_ref, router_ref, h2_ref, x1_ref, s2_ref, g2_ref, dy_ref,
        q_ref, context_ref, sq_ref, sk_ref, o_ref, lse_ref, raw_ref, scale_ref, qkg_ref,
        cos_ref, sin_ref, h1_ref, tok_ref, g1_ref, w_hbm, out_ref,
        tok_grad, qkv_sum, out_sum, small_sum,
        weights, dx1, da, do, dot_sums, dq, dkv, proj, send_kv, land_y, land_z,
        part, full, core_buf, x_buf, small, line_sum,
        main_buf, out_acc, out_lo, out_hi, out_land, small_buf, part_k, land_k, part_q, land_q,
        w_sem, y_s, y_r, z_s, z_r, group_s, group_r, ks_s, ks_r, qs_s, qs_r, line_s, line_r, out_s, out_r, out_y_s, out_y_r,
    ):
        z, y, x, c = place()
        e, t = lax.axis_index("expert"), lax.axis_index("tensor")
        mates = [(e, lax.rem(t + k, tensors)) for k in range(1, tensors)]
        beside, below = device(z, 1 - y, x, c), device(z - 1, y, x, c)
        fetch = pltpu.make_async_copy(w_hbm, weights, w_sem)
        fetch.start()

        def own_part(s, b):
            if s == SMALL:
                return small[b]
            at = pl.ds(pl.multiple_of(b * depth, depth), depth)
            return dot(h1_ref[:, at], proj[s], (0, 0))

        def out_copy(zz, yy, way):
            landing = (out_lo if way == 0 else out_hi).at[zz, yy]
            target = device(z + 1, y, x, c) if way == 0 else below
            return remote(out_acc.at[zz, yy], landing, out_s.at[zz, yy, way], out_r.at[zz, yy, way], target)

        def out_take(zz, yy, way):
            out_copy(zz, yy, way).wait_recv()
            total = out_acc.at[zz, yy]
            add_to(total, total, (out_lo if way == 0 else out_hi).at[zz, yy])

        def out_hop(k):
            for zz in Z_ORDER:
                for yy in range(NY):
                    def upward(zz=zz, yy=yy):
                        if k > 0:
                            out_take(zz, yy, 0)
                        out_copy(zz, yy, 0).start()

                    def downward(zz=zz, yy=yy):
                        if k > 0:
                            out_take(zz, yy, 1)
                        out_copy(zz, yy, 1).start()

                    if k < zz:
                        run_if((z < zz) & (z == k), upward)
                    if NZ - 1 - k > zz:
                        run_if((z > zz) & (NZ - 1 - z == k), downward)

        def out_beside():
            return remote(out_acc.at[z, 1 - y], out_land, out_y_s, out_y_r, beside)

        def out_start():
            for zz in range(NZ):
                for yy in range(NY):
                    at = pl.ds((zz * NY + yy) * depth, depth)
                    out_acc[zz, yy] = dot(o_ref[...], da[:, at], (0, 0)).astype(low)

        def out_home():
            for yy in range(NY):
                run_if(z > 0, lambda yy=yy: out_take(z, yy, 0))
                run_if(z < NZ - 1, lambda yy=yy: out_take(z, yy, 1))
            out_beside().start()

        def out_end():
            out_beside().wait_recv()
            out_sum[...] = out_acc[z, y].astype(f32) + out_land[...].astype(f32)
            out_beside().wait_send()
            for zz in range(NZ):
                for yy in range(NY):
                    run_if(z < zz, lambda zz=zz, yy=yy: out_copy(zz, yy, 0).wait_send())
                    run_if(z > zz, lambda zz=zz, yy=yy: out_copy(zz, yy, 1).wait_send())

        def slot(kind):
            def view(s, zz):
                if s == SMALL:
                    return small_buf.at[kind, zz]
                return main_buf.at[kind, zz, s]
            return view

        line = LineReduce([], lambda s, zz, yy: slot(3)(s, zz), slot(0), slot(1), slot(2), line_s, line_r)
        greet(line.partners() + [(mate, None) for mate in mates])

        grad_probs = gates_ref[...]
        logits = dot(h2_ref[...], router_ref[...], (1, 1))
        shifted = jnp.exp(logits - jnp.max(logits, axis=-1, keepdims=True))
        probs = shifted / jnp.sum(shifted, axis=-1, keepdims=True)
        grad_logits = probs * (grad_probs - jnp.sum(probs * grad_probs, axis=-1, keepdims=True))
        tall = jnp.transpose(
            jnp.concatenate([grad_logits, jnp.zeros((rows, 128 - experts), f32)], axis=1)
        )
        grad_logits = grad_logits.astype(low)
        tall = tall.astype(low)
        for b in range(GROUPS):
            small[b] = jnp.zeros_like(small[b])
            small[b, 8 : 8 + experts, :] = dot(tall, h2_ref[:, pl.ds(b * depth, depth)], (1, 0))[:experts]
        dx1[...] = dot(grad_logits, router_ref[...], (1, 0))
        line_sum[...] = jnp.zeros_like(line_sum)

        def norm_two(i, carry):
            r = pl.ds(pl.multiple_of(i * 32, 32), 32)
            grad = dh_ref[r, :].astype(f32) + dx1[r, :]
            value, scale = x1_ref[r, :], s2_ref[r, 0:1]
            line_sum[0:1, :] += jnp.sum(grad * (value * scale), axis=0, keepdims=True)
            grad = grad * g2_ref[...]
            inner = jnp.mean(grad * value, axis=-1, keepdims=True)
            result = dy_ref[r, :].astype(f32) + scale * grad - value * (scale * scale * scale) * inner
            dx1[r, :] = result
            da[r, :] = result.astype(low)
            return carry

        lax.fori_loop(0, rows // 32, norm_two, 0)

        out_start()
        out_hop(0)

        do[...] = dot(da[...], out_ref[...], (1, 1)).astype(low)
        wide = lax.broadcasted_iota(jnp.int32, (rows, 128), 1)
        sums = jnp.zeros((rows, 128), f32)
        for head in range(heads):
            at = pl.ds(head * HEAD, HEAD)
            inner = jnp.sum(do[:, at].astype(f32) * o_ref[:, at].astype(f32), axis=-1, keepdims=True)
            sums = jnp.where(wide == head, inner, sums)
        dot_sums[...] = sums
        dq[...] = jnp.zeros_like(dq)
        row = lax.broadcasted_iota(jnp.int32, (rows, rows), 0)
        column = lax.broadcasted_iota(jnp.int32, (rows, rows), 1)

        def attention_block(k):
            distance = row - column + k * rows
            allowed = (sq_ref[...] == sk_ref[k : k + 1, :]) & (distance >= 0) & (distance < WINDOW)
            for head in range(heads):
                at = pl.ds(head * HEAD, HEAD)
                queries, keys, values = q_ref[:, at], context_ref[k, 0, :, at], context_ref[k, 1, :, at]
                scores = dot(queries, keys, (1, 1)) * HEAD ** (-0.5)
                weight = jnp.where(allowed, jnp.exp(scores - lse_ref[:, head : head + 1]), 0.0)
                grad_weight = dot(do[:, at], values, (1, 1))
                grad_score = (
                    weight * (grad_weight - dot_sums[:, head : head + 1]) * HEAD ** (-0.5)
                ).astype(low)
                dq[:, at] += dot(grad_score, keys, (1, 0))
                dkv[k, 0, :, at] = dot(grad_score, queries, (0, 0))
                dkv[k, 1, :, at] = dot(weight.astype(low), do[:, at], (0, 0))

        exists = {0: None, 1: (y == 1) | (z >= 1), 2: z >= 1, 3: z >= 2 - y, 4: z >= 2}
        comes = {1: (y == 0) | (z >= 1), 3: z >= 1 + y}

        def kv_copy(which, k):
            if k in (1, 3):
                landing, target = land_y.at[k // 2, which], beside
                return remote(send_kv.at[k - 1, which], landing, y_s.at[k // 2, which], y_r.at[k // 2, which], target)
            landing = land_z.at[k // 2 - 1, which]
            return remote(
                send_kv.at[k - 1, which], landing, z_s.at[k // 2 - 1, which], z_r.at[k // 2 - 1, which], below
            )

        def kv_send(which, k):
            send_kv[k - 1, which] = dkv[k, which].astype(low)
            kv_copy(which, k).start()

        def merge(into, which, landed):
            add_to(dkv.at[into, which], dkv.at[into, which], landed, 32)

        for k in (3, 1, 4, 2, 0):
            def one(k=k):
                attention_block(k)
                if k in (1, 3):
                    kv_send(1, k)
                    kv_send(0, k)
            run_if(exists[k], one)

        def take_three(which):
            def land():
                kv_copy(which, 3).wait_recv()
                pl.when(y == 1)(lambda: merge(4, which, land_y.at[1, which]))
                pl.when(y == 0)(lambda: merge(2, which, land_y.at[1, which]))
            run_if(comes[3], land)
            run_if(exists[4], lambda: kv_send(which, 4))

        def take_one(which):
            def land():
                kv_copy(which, 1).wait_recv()
                pl.when(y == 1)(lambda: merge(2, which, land_y.at[0, which]))
                pl.when(y == 0)(lambda: merge(0, which, land_y.at[0, which]))
            run_if(comes[1], land)

        def take_four(which):
            def land():
                kv_copy(which, 4).wait_recv()
                merge(2, which, land_z.at[1, which])
            run_if((z >= 1) & (z < NZ - 1), land)
            run_if(exists[2], lambda: kv_send(which, 2))

        def take_two(which):
            def land():
                kv_copy(which, 2).wait_recv()
                merge(0, which, land_z.at[0, which])
            run_if(z < NZ - 1, land)

        def unturn(which, grad_of):
            inner = jnp.zeros((rows, 1), f32)
            for head in range(heads):
                at = pl.ds(head * HEAD, HEAD)
                grad = turn(grad_of(at), cos_ref[...], -sin_ref[...])
                value = raw_ref[which, :, at]
                line_sum[1 + which : 2 + which, at] = jnp.sum(
                    grad * (value * scale_ref[:, 1 + which : 2 + which]), axis=0, keepdims=True
                )
                grad = grad * qkg_ref[which : which + 1, at]
                dkv[1 + which, 0, :, at] = grad
                inner = inner + jnp.sum(grad * value, axis=-1, keepdims=True)
            return inner

        def denorm(which, inner):
            scale = scale_ref[:, 1 + which : 2 + which]
            rest = scale * scale * scale * inner / width
            for head in range(heads):
                at = pl.ds(head * HEAD, HEAD)
                proj[which, :, at] = (
                    scale * dkv[1 + which, 0, :, at] - raw_ref[which, :, at] * rest
                ).astype(low)

        def send_beside(s):
            for zz in Z_ORDER:
                buffer = slot(3)(s, zz)
                buffer[...] = own_part(s, zz * NY + 1 - y).astype(buffer.dtype)
                line.to_y(s, zz)

        take_three(1)
        take_three(0)
        out_hop(1)
        take_one(1)
        take_one(0)
        take_four(1)
        take_four(0)
        exchange_rows(unturn(QUERY, lambda at: dq[:, at]), part_q, land_q, qs_s, qs_r, mates)
        take_two(1)
        proj[VALUE] = dkv[0, 1].astype(low)
        denorm(QUERY, exchanged_rows(part_q, land_q, qs_s, qs_r, mates))
        send_beside(QUERY)
        send_beside(VALUE)
        take_two(0)
        out_hop(2)
        exchange_rows(unturn(KEY, lambda at: dkv[0, 0, :, at]), part_k, land_k, ks_s, ks_r, mates)
        denorm(KEY, exchanged_rows(part_k, land_k, ks_s, ks_r, mates))
        send_beside(KEY)
        out_home()
        fetch.wait()

        def half_of(cc):
            def body(i, carry):
                at = pl.ds(pl.multiple_of(cc * half + i * quarter, quarter), quarter)
                value = dot(proj[0], weights[0, at, :], (1, 1))
                for s in (1, 2):
                    value = value + dot(proj[s], weights[s, at, :], (1, 1))
                part[:, at] = value.astype(low)
                return carry

            lax.fori_loop(0, 2, body, 0)

        stages = group_stages(part, full, core_buf, x_buf, group_s, group_r)
        half_of(1 - c)
        stages[0]()
        half_of(c)
        stages[1]()

        def hop(s, zz, k):
            def upward():
                if k > 0:
                    line.take(s, zz, 1)
                line.copy(s, zz, 1).start()

            def downward():
                if k > 0:
                    line.take(s, zz, 2)
                line.copy(s, zz, 2).start()

            if k < zz:
                run_if((z < zz) & (z == k), upward)
            if NZ - 1 - k > zz:
                run_if((z > zz) & (NZ - 1 - z == k), downward)

        def receive(s, zz):
            line.copy(s, zz, 0).wait_recv()
            buffer = slot(0)(s, zz)
            buffer[...] = (buffer[...].astype(f32) + own_part(s, zz * NY + y)).astype(buffer.dtype)

        units = []

        def run_units(s):
            for zz in Z_ORDER:
                receive(s, zz)
                hop(s, zz, 0)
                units.append((s, zz))
                for k in (1, 2):
                    if len(units) > k:
                        hop(*units[-1 - k], k)

        def norm_one(i, carry):
            r = pl.ds(pl.multiple_of(i * 32, 32), 32)
            grad, value, scale = full[r, :].astype(f32), tok_ref[r, :].astype(f32), scale_ref[r, 0:1]
            line_sum[3:4, :] += jnp.sum(grad * (value * scale), axis=0, keepdims=True)
            grad = grad * g1_ref[...]
            inner = jnp.mean(grad * value, axis=-1, keepdims=True)
            tok_grad[r, :] = (
                dx1[r, :] + scale * grad - value * (scale * scale * scale) * inner
            ).astype(low)
            return carry

        run_units(QUERY)
        stages[2]()
        run_units(VALUE)
        stages[3]()
        stages[4]()
        lax.fori_loop(0, rows // 32, norm_one, 0)
        for b in range(GROUPS):
            at = pl.ds(b * depth, depth)
            small[b, 0:1, :] = line_sum[3:4, at]
            small[b, 1:2, :] = line_sum[0:1, at]
            for which in range(2):
                for k in range(columns // depth):
                    small[b, 2 + 2 * which + k : 3 + 2 * which + k, :] = line_sum[
                        1 + which : 2 + which, pl.ds(k * depth, depth)
                    ]
        send_beside(SMALL)
        run_units(KEY)
        run_units(SMALL)
        out_end()
        hop(*units[-1], 1)
        hop(*units[-2], 2)
        hop(*units[-1], 2)

        def done(s, total):
            target = qkv_sum.at[s] if s < OUT else small_sum
            target[...] = total[...].astype(f32)

        line.streams = [QUERY, VALUE, KEY, SMALL]
        line.home(done)
        line.finish()
        for which in range(2):
            for k in (1, 2, 3, 4):
                run_if(exists[k], lambda which=which, k=k: kv_copy(which, k).wait_send())
        drain_rows(part_k, land_k, ks_s, ks_r, mates)
        drain_rows(part_q, land_q, qs_s, qs_r, mates)

    shape, dma, vmem = jax.ShapeDtypeStruct, pltpu.SemaphoreType.DMA, pltpu.VMEM
    return pl.pallas_call(
        kernel,
        out_shape=(
            shape((rows, width), low),
            shape((3, depth, columns), f32),
            shape((columns, depth), f32),
            shape((small_rows, depth), f32),
        ),
        in_specs=[VMEM] * 22 + [HBM, VMEM],
        out_specs=(VMEM,) * 4,
        scratch_shapes=[
            vmem(qkv_low.shape, low),
            vmem((rows, width), f32),
            vmem((rows, width), low),
            vmem((rows, columns), low),
            vmem((rows, 128), f32),
            vmem((rows, columns), f32),
            vmem((blocks, 2, rows, columns), f32),
            vmem((3, rows, columns), low),
            vmem((blocks - 1, 2, rows, columns), low),
            vmem((2, 2, rows, columns), low),
            vmem((2, 2, rows, columns), low),
            vmem((rows, width), low),
            vmem((rows, width), low),
            vmem((rows, half), low),
            vmem((rows, quarter), low),
            vmem((GROUPS, small_rows, depth), f32),
            vmem((8, width), f32),
            vmem((4, NZ, 3, depth, columns), low),
            vmem((NZ, NY, columns, depth), low),
            vmem((NZ, NY, columns, depth), low),
            vmem((NZ, NY, columns, depth), low),
            vmem((columns, depth), low),
            vmem((4, NZ, small_rows, depth), f32),
            vmem((8, rows), f32),
            vmem((tensors - 1, 8, rows), f32),
            vmem((8, rows), f32),
            vmem((tensors - 1, 8, rows), f32),
            dma, dma((2, 2)), dma((2, 2)), dma((2, 2)), dma((2, 2)), dma((5,)), dma((5,)),
            dma((tensors - 1,)), dma((tensors - 1,)), dma((tensors - 1,)), dma((tensors - 1,)),
            dma((5, NZ, 3)), dma((5, NZ, 3)), dma((NZ, NY, 2)), dma((NZ, NY, 2)), dma, dma,
        ],
        compiler_params=comm_params(collective_id, 62),
        cost_estimate=cost(130),
        name="attend_back",
    )(
        grad_hidden, grad_probs, router_t, hidden_two, residual, scale_two, gain_two, out_grad,
        query, context, segment_query, segment_keys, attended, log_sums, raw, scales, qk_gains,
        cosine, sine, hidden_one, tokens, gain_one, qkv_low, out_low,
    )


def fast_shards(
    tokens_in,
    out_grad,
    w_qkv,
    w_attn_out,
    attn_gain,
    ffn_gain,
    qk_gain,
    w_router,
    w_gate,
    w_up,
    w_down,
    routes,
    segments,
):
    row_count, model_width = tokens_in.shape
    experts = w_router.shape[1]
    local_experts = w_gate.shape[0]
    heads_here = qk_gain.shape[1]
    local_width = heads_here * HEAD
    groups = lax.axis_size("expert")
    device_index = lax.axis_index("expert")
    tensor_index = lax.axis_index("tensor")
    quarter = model_width // lax.axis_size("tensor")
    hop_count = WINDOW // row_count
    score_scale = HEAD ** (-0.5)
    low = jnp.bfloat16

    chosen = jnp.any(
        routes[:, :, None] == jnp.arange(experts, dtype=jnp.int32)[None, None, :], axis=1
    ).astype(jnp.float32)
    qk_row = qk_gain.reshape(1, -1)

    def rounded(v):
        return lax.reduce_precision(v, 8, 7)

    smalls = jnp.concatenate(
        [
            rounded(attn_gain)[None, :],
            rounded(ffn_gain)[None, :],
            jnp.pad(rounded(qk_row), ((0, 0), (0, row_count - qk_row.shape[1]))),
            jnp.zeros((5, row_count), jnp.float32),
            w_router.T,
            chosen.T,
        ],
        axis=0,
    )
    global_rows = device_index * row_count + jnp.arange(row_count, dtype=jnp.int32)
    cosine_table, sine_table = angles(global_rows % SEQ, HEAD)
    wide_cosine = jnp.concatenate([cosine_table[:, 0], cosine_table[:, 0]], axis=1)
    wide_sine = jnp.concatenate([-sine_table[:, 0], sine_table[:, 0]], axis=1)
    grad_out_piece = lax.dynamic_slice_in_dim(out_grad, tensor_index * quarter, quarter, axis=1)
    grad_out_rows = lax.all_gather(grad_out_piece, "expert", axis=0, tiled=True)
    out_low = lax.all_gather(w_attn_out.astype(low), "expert", axis=1, tiled=True)
    qkv_low, small_all, hidden_one, raw, scales, query_low, context_blocks = project(
        tokens_in, w_qkv, smalls, wide_cosine, wide_sine, 0
    )
    grad_out_rows, query_low = lax.optimization_barrier((grad_out_rows, query_low))
    grad_out_all = lax.all_gather(grad_out_rows, "tensor", axis=1, tiled=True)
    gain_one_f = small_all[:, 0].reshape(model_width)
    gain_two_f = small_all[:, 1].reshape(model_width)
    qk_gains = (
        small_all[:, 2, : qk_row.shape[1]]
        .reshape(groups, 2, heads_here, HEAD // groups)
        .transpose(1, 2, 0, 3)
        .reshape(2, local_width)
    )
    router_t = small_all[:, 8 : 8 + experts].transpose(1, 0, 2).reshape(experts, model_width).astype(low)
    chosen_all = small_all[:, 8 + experts : 8 + 2 * experts].transpose(0, 2, 1).reshape(
        groups * row_count, experts
    )
    segment_window = lax.dynamic_slice_in_dim(
        jnp.concatenate([jnp.full((WINDOW,), -1, jnp.int32), segments]),
        device_index * row_count, (hop_count + 1) * row_count,
    )
    segment_query = segment_window[WINDOW:]
    segment_keys = segment_window.reshape(hop_count + 1, row_count)[::-1]
    attended, log_sums, residual, hidden_two, scale_two_wide = attend(
        query_low, context_blocks, segment_query[:, None], segment_keys, tokens_in, out_low,
        gain_two_f[None, :], 2,
    )
    hidden_all = token_gather(hidden_two, 3)
    gate_up = jnp.concatenate(
        [w[i] for w in (w_gate, w_up) for i in range(local_experts)], axis=1
    ).astype(low)
    down_low = w_down.reshape(-1, model_width).astype(low)
    block_out, grad_hidden_sum, grad_gate_sum, grad_gate_w, grad_up_w, grad_down = expert_layer(
        hidden_all, grad_out_all, gate_up, down_low, router_t, chosen_all.astype(low), residual, 5
    )
    grad_probs = grad_gate_sum[:, :local_experts].reshape(experts, row_count).T * chosen
    grad_tokens, qkv_sum, out_sum, small_sum = attend_back(
        grad_hidden_sum, grad_probs, router_t, hidden_two, residual, scale_two_wide,
        gain_two_f[None, :], out_grad, query_low, context_blocks, segment_query[:, None], segment_keys,
        attended, log_sums, raw, scales, qk_gains, wide_cosine, wide_sine, hidden_one, tokens_in,
        gain_one_f[None, :], qkv_low, out_low, 8,
    )
    return (
        block_out,
        grad_tokens,
        qkv_sum,
        out_sum,
        small_sum[0],
        small_sum[1],
        lax.dynamic_slice_in_dim(
            small_sum[2:6].reshape(2, heads_here, HEAD),
            device_index * qk_gain.shape[2], qk_gain.shape[2], axis=2,
        ),
        small_sum[8 : 8 + experts].T,
        grad_gate_w,
        grad_up_w,
        grad_down,
    )


def solution(mesh):
    placed = (
        P("expert", None),
        P("expert", None),
        P(None, "expert", "tensor"),
        P("tensor", "expert"),
        P("expert"),
        P("expert"),
        P(None, "tensor", "expert"),
        P("expert", None),
        P("expert", None, "tensor"),
        P("expert", None, "tensor"),
        P("expert", "tensor", None),
        P("expert", None),
        P(),
    )
    compact = (mesh.shape["expert"], mesh.shape["tensor"]) == (GROUPS, NX * NC)
    return jax.shard_map(
        fast_shards if compact else shards,
        mesh=mesh,
        in_specs=placed,
        out_specs=(
            P("expert", None),
            P("expert", None),
            P(None, "expert", "tensor"),
            P("tensor", "expert"),
            P("expert"),
            P("expert"),
            P(None, "tensor", "expert"),
            P("expert", None),
            P("expert", None, "tensor"),
            P("expert", None, "tensor"),
            P("expert", "tensor", None),
        ),
        check_vma=False,
    )
```

```python
import jax
import jax.numpy as jnp
from jax import lax
from jax.experimental import pallas as pl
from jax.experimental.pallas import tpu as pltpu
from jax.sharding import PartitionSpec as P

HEAD = 128
WINDOW = 1024
SEQ = 2048


EPS = 1e-05
THETA = 10000.0


def from_behind(value, axis, steps):
    count = lax.axis_size(axis)
    initial, last = (max(0, -steps), min(count, count - steps))
    return lax.ppermute(value, axis, [(source, source + steps) for source in range(initial, last)])


def angles(position, head_size):
    half_size = head_size // 2
    frequency = THETA ** (-(jnp.arange(half_size, dtype=jnp.float32) * 2.0 / head_size))
    phase_angle = position.astype(jnp.float32)[:, None] * frequency[None, :]
    return (jnp.cos(phase_angle)[:, None, :], jnp.sin(phase_angle)[:, None, :])


def rotate(rotated_in, cosine_table, sine_table):
    half_size = rotated_in.shape[-1] // 2
    first_half = rotated_in[..., :half_size]
    second_half = rotated_in[..., half_size:]
    return jnp.concatenate(
        [
            first_half * cosine_table - second_half * sine_table,
            second_half * cosine_table + first_half * sine_table,
        ],
        axis=-1,
    )


def slot_layout(block_routes, experts, capacity):
    flat_routes = block_routes.reshape(-1)
    onehot = (flat_routes[:, None] == jnp.arange(experts, dtype=jnp.int32)[None, :]).astype(
        jnp.int32
    )
    before = jnp.cumsum(onehot, axis=0) - onehot
    rank_within = jnp.sum(before * onehot, axis=1)
    slot_index = flat_routes * capacity + rank_within
    slot_table = (
        jnp.zeros((experts * capacity,), jnp.int32)
        .at[slot_index]
        .set(jnp.arange(flat_routes.shape[0], dtype=jnp.int32) + 1)
    )
    return (slot_index, slot_table)


def shards(
    tokens_in,
    out_grad,
    w_qkv,
    w_attn_out,
    attn_gain,
    ffn_gain,
    qk_gain,
    w_router,
    w_gate,
    w_up,
    w_down,
    routes,
    segments,
):
    row_count, model_width = tokens_in.shape
    experts = w_router.shape[1]
    per_token = routes.shape[1]
    local_experts = w_gate.shape[0]
    heads_here = qk_gain.shape[1]
    local_width = heads_here * HEAD
    groups = lax.axis_size("expert")
    device = lax.axis_index("expert")
    capacity = row_count * per_token * 3 // (2 * experts)
    hop_count = WINDOW // row_count
    buffer_shape = (groups, local_experts, capacity, model_width)
    score_scale = HEAD ** (-0.5)

    def fetch_weights():
        return (
            lax.all_gather(w_qkv.astype(jnp.bfloat16), "expert", axis=1, tiled=True),
            lax.all_gather(w_attn_out.astype(jnp.bfloat16), "expert", axis=1, tiled=True),
            lax.all_gather(w_router.astype(jnp.bfloat16), "expert", axis=0, tiled=True),
            lax.all_gather(attn_gain.astype(jnp.bfloat16), "expert", axis=0, tiled=True),
            lax.all_gather(ffn_gain.astype(jnp.bfloat16), "expert", axis=0, tiled=True),
            lax.all_gather(qk_gain.astype(jnp.bfloat16), "expert", axis=2, tiled=True),
        )

    def prepare(pieces):
        return (
            pieces[0],
            pieces[1],
            pieces[2],
            pieces[3].astype(jnp.float32),
            pieces[4].astype(jnp.float32),
            pieces[5].astype(jnp.float32).reshape(2, local_width),
        )

    qkv_low, out_low, router_low, gain_one_f, gain_two_f, qk_gains = prepare(fetch_weights())
    tokens_f = tokens_in.astype(jnp.float32)
    scale_one = lax.rsqrt(jnp.mean(tokens_f * tokens_f, axis=-1, keepdims=True) + EPS)
    hidden_one = (tokens_f * scale_one * gain_one_f).astype(jnp.bfloat16)
    projected = jnp.einsum("td,jde->jte", hidden_one, qkv_low, preferred_element_type=jnp.float32)
    query_raw = projected[0]
    key_raw = projected[1]
    query_sq, key_sq = lax.psum(
        (jnp.sum(query_raw * query_raw, axis=-1), jnp.sum(key_raw * key_raw, axis=-1)), "tensor"
    )
    query_scale = lax.rsqrt(query_sq / model_width + EPS)[:, None]
    key_scale = lax.rsqrt(key_sq / model_width + EPS)[:, None]
    normed_query = query_raw * query_scale
    normed_key = key_raw * key_scale
    global_rows = device * row_count + jnp.arange(row_count, dtype=jnp.int32)
    cosine_table, sine_table = angles(global_rows % SEQ, HEAD)
    query_low = rotate(
        (normed_query * qk_gains[0]).reshape(row_count, heads_here, HEAD), cosine_table, sine_table
    ).astype(jnp.bfloat16)
    key_low = rotate(
        (normed_key * qk_gains[1]).reshape(row_count, heads_here, HEAD), cosine_table, sine_table
    ).astype(jnp.bfloat16)
    value_low = projected[2].astype(jnp.bfloat16).reshape(row_count, heads_here, HEAD)
    own_pair = jnp.stack([key_low, value_low])
    earlier = []
    for steps_back in range(hop_count, 0, -1):
        earlier.append(from_behind(own_pair, "expert", steps_back))
    context = jnp.concatenate(earlier + [own_pair], axis=1)
    key_rows = (device - hop_count) * row_count + jnp.arange(
        (hop_count + 1) * row_count, dtype=jnp.int32
    )
    segment_keys = segments[jnp.maximum(key_rows, 0)]
    segment_query = segments[global_rows]
    distance = global_rows[:, None] - key_rows[None, :]
    allowed = (
        (key_rows[None, :] >= 0)
        & (segment_query[:, None] == segment_keys[None, :])
        & (distance >= 0)
        & (distance < WINDOW)
    )

    def score_block():
        raw_scores = (
            jnp.einsum("qhd,khd->hqk", query_low, context[0], preferred_element_type=jnp.float32)
            * score_scale
        )
        return jnp.where(allowed[None], raw_scores, -1e30)

    scores = score_block()
    largest = jnp.max(scores, axis=-1, keepdims=True)
    exp_scores = jnp.exp(scores - largest)
    exp_total = jnp.sum(exp_scores, axis=-1, keepdims=True)
    log_total = largest + jnp.log(exp_total)
    attn_probs = (exp_scores / exp_total).astype(jnp.bfloat16)
    attended = (
        jnp.einsum("hqk,khd->qhd", attn_probs, context[1], preferred_element_type=jnp.float32)
        .reshape(row_count, local_width)
        .astype(jnp.bfloat16)
    )
    attention_out = lax.psum(
        jnp.dot(attended, out_low, preferred_element_type=jnp.float32).astype(jnp.bfloat16),
        "tensor",
    ).astype(jnp.float32)
    residual = tokens_f + attention_out
    scale_two = lax.rsqrt(jnp.mean(residual * residual, axis=-1, keepdims=True) + EPS)
    normed_two = residual * scale_two
    hidden_two = (normed_two * gain_two_f).astype(jnp.bfloat16)
    logits = jnp.dot(hidden_two, router_low, preferred_element_type=jnp.float32)
    logit_exp = jnp.exp(logits - jnp.max(logits, axis=-1, keepdims=True))
    router_probs = logit_exp / jnp.sum(logit_exp, axis=-1, keepdims=True)
    chosen = routes[:, :, None] == jnp.arange(experts, dtype=jnp.int32)[None, None, :]
    gate_probs = jnp.sum(jnp.where(chosen, router_probs[:, None, :], 0.0), axis=-1)
    slot_index, slot_table = slot_layout(routes, experts, capacity)
    present = (slot_table > 0)[:, None]
    assigned = jnp.maximum(slot_table - 1, 0)
    row_of_slot = assigned // per_token
    gate_low = w_gate.astype(jnp.bfloat16)
    up_low = w_up.astype(jnp.bfloat16)
    down_low = w_down.astype(jnp.bfloat16)

    def send_rows():
        buffer_rows = jnp.where(
            present, hidden_two[row_of_slot], jnp.zeros((), jnp.bfloat16)
        ).reshape(buffer_shape)
        return lax.all_to_all(buffer_rows, "expert", split_axis=0, concat_axis=0, tiled=True)

    def expert_front(arrived):
        gate_pre = jnp.einsum(
            "secd,edh->sech", arrived, gate_low, preferred_element_type=jnp.float32
        )
        up_pre = jnp.einsum("secd,edh->sech", arrived, up_low, preferred_element_type=jnp.float32)
        return (gate_pre, up_pre)

    received = send_rows()
    gate_pre, up_pre = expert_front(received)
    activated = (gate_pre * jax.nn.sigmoid(gate_pre) * up_pre).astype(jnp.bfloat16)
    partial_value = jnp.einsum(
        "sech,ehd->secd", activated, down_low, preferred_element_type=jnp.float32
    ).astype(jnp.bfloat16)
    returned = lax.all_to_all(
        partial_value, "expert", split_axis=0, concat_axis=0, tiled=True
    ).reshape(experts * capacity, model_width)
    expert_rows = returned[slot_index].reshape(row_count, per_token, model_width)
    expert_part = jnp.einsum(
        "tk,tkd->td", gate_probs, expert_rows, preferred_element_type=jnp.float32
    )
    block_out = residual + lax.psum(expert_part.astype(jnp.bfloat16), "tensor").astype(jnp.float32)
    qkv_low, out_low, router_low, gain_one_f, gain_two_f, qk_gains = prepare(fetch_weights())
    grad_out = out_grad.astype(jnp.float32)
    grad_gate_part = jnp.einsum(
        "td,tkd->tk", grad_out, expert_rows, preferred_element_type=jnp.float32
    )
    slot_grads = (
        (gate_probs[:, :, None] * grad_out[:, None, :])
        .astype(jnp.bfloat16)
        .reshape(row_count * per_token, model_width)
    )
    grad_buffer = jnp.where(present, slot_grads[assigned], jnp.zeros((), jnp.bfloat16)).reshape(
        buffer_shape
    )
    grad_received = lax.all_to_all(grad_buffer, "expert", split_axis=0, concat_axis=0, tiled=True)
    received = send_rows()
    gate_pre, up_pre = expert_front(received)
    sigmoid_gate = jax.nn.sigmoid(gate_pre)
    swish_gate = gate_pre * sigmoid_gate
    activated = (swish_gate * up_pre).astype(jnp.bfloat16)
    grad_act = jnp.einsum(
        "secd,ehd->sech", grad_received, down_low, preferred_element_type=jnp.float32
    )
    grad_down = jnp.einsum(
        "sech,secd->ehd", activated, grad_received, preferred_element_type=jnp.float32
    )
    grad_gate_pre = (
        grad_act * up_pre * sigmoid_gate * (1.0 + gate_pre * (1.0 - sigmoid_gate))
    ).astype(jnp.bfloat16)
    grad_up_pre = (grad_act * swish_gate).astype(jnp.bfloat16)
    grad_gate_w = jnp.einsum(
        "secd,sech->edh", received, grad_gate_pre, preferred_element_type=jnp.float32
    )
    grad_up_w = jnp.einsum(
        "secd,sech->edh", received, grad_up_pre, preferred_element_type=jnp.float32
    )
    grad_rows = (
        jnp.einsum("sech,edh->secd", grad_gate_pre, gate_low, preferred_element_type=jnp.float32)
        + jnp.einsum("sech,edh->secd", grad_up_pre, up_low, preferred_element_type=jnp.float32)
    ).astype(jnp.bfloat16)
    grad_back = lax.all_to_all(
        grad_rows, "expert", split_axis=0, concat_axis=0, tiled=True
    ).reshape(experts * capacity, model_width)
    grad_hidden_part = jnp.sum(
        grad_back[slot_index].reshape(row_count, per_token, model_width), axis=1, dtype=jnp.float32
    )
    grad_hidden_sum, grad_gates = (
        lax.psum(grad_hidden_part.astype(jnp.bfloat16), "tensor").astype(jnp.float32),
        lax.psum(grad_gate_part.astype(jnp.bfloat16), "tensor").astype(jnp.float32),
    )
    grad_probs = jnp.sum(jnp.where(chosen, grad_gates[:, :, None], 0.0), axis=1)
    grad_logits = (
        router_probs * (grad_probs - jnp.sum(router_probs * grad_probs, axis=-1, keepdims=True))
    ).astype(jnp.bfloat16)
    grad_hidden_two = grad_hidden_sum + jnp.dot(
        grad_logits, router_low.T, preferred_element_type=jnp.float32
    )
    grad_router = jnp.dot(hidden_two.T, grad_logits, preferred_element_type=jnp.float32)
    grad_gain_two = jnp.sum(grad_hidden_two * normed_two, axis=0)
    scaled_two = grad_hidden_two * gain_two_f
    grad_residual = (
        grad_out
        + scale_two * scaled_two
        - residual
        * (scale_two * scale_two * scale_two)
        * jnp.mean(scaled_two * residual, axis=-1, keepdims=True)
    )
    grad_attn = grad_residual.astype(jnp.bfloat16)
    grad_out_w = jnp.dot(attended.T, grad_attn, preferred_element_type=jnp.float32)
    grad_attended = (
        jnp.dot(grad_attn, out_low.T, preferred_element_type=jnp.float32)
        .astype(jnp.bfloat16)
        .reshape(row_count, heads_here, HEAD)
    )
    attn_weights = jnp.where(allowed[None], jnp.exp(score_block() - log_total), 0.0)
    grad_weights = jnp.einsum(
        "qhd,khd->hqk", grad_attended, context[1], preferred_element_type=jnp.float32
    )
    inner_sum = jnp.sum(attn_weights * grad_weights, axis=-1, keepdims=True)
    grad_scores = (attn_weights * (grad_weights - inner_sum) * score_scale).astype(jnp.bfloat16)
    grad_query = jnp.einsum(
        "hqk,khd->qhd", grad_scores, context[0], preferred_element_type=jnp.float32
    )
    grad_keys = jnp.einsum(
        "hqk,qhd->khd", grad_scores, query_low, preferred_element_type=jnp.float32
    )
    grad_values = jnp.einsum(
        "hqk,qhd->khd",
        attn_weights.astype(jnp.bfloat16),
        grad_attended,
        preferred_element_type=jnp.float32,
    )
    grad_pair = jnp.stack([grad_keys, grad_values]).reshape(
        2, hop_count + 1, row_count, heads_here, HEAD
    )
    own_grad = grad_pair[:, hop_count]
    for steps_back in range(1, hop_count + 1):
        own_grad = own_grad + from_behind(
            grad_pair[:, hop_count - steps_back].astype(jnp.bfloat16), "expert", -steps_back
        ).astype(jnp.float32)
    grad_query_norm = rotate(grad_query, cosine_table, -sine_table).reshape(row_count, local_width)
    grad_key_norm = rotate(own_grad[0], cosine_table, -sine_table).reshape(row_count, local_width)
    grad_gain_query = jnp.sum(grad_query_norm * normed_query, axis=0)
    grad_gain_key = jnp.sum(grad_key_norm * normed_key, axis=0)
    scaled_query = grad_query_norm * qk_gains[0]
    scaled_key = grad_key_norm * qk_gains[1]
    query_inner, key_inner = lax.psum(
        (jnp.sum(scaled_query * query_raw, axis=-1), jnp.sum(scaled_key * key_raw, axis=-1)),
        "tensor",
    )
    grad_query_raw = (
        query_scale * scaled_query
        - query_raw * (query_scale * query_scale * query_scale) * query_inner[:, None] / model_width
    ).astype(jnp.bfloat16)
    grad_key_raw = (
        key_scale * scaled_key
        - key_raw * (key_scale * key_scale * key_scale) * key_inner[:, None] / model_width
    ).astype(jnp.bfloat16)
    grad_value_raw = own_grad[1].reshape(row_count, local_width).astype(jnp.bfloat16)
    grad_proj = jnp.stack([grad_query_raw, grad_key_raw, grad_value_raw])
    grad_qkv = jnp.einsum("td,jte->jde", hidden_one, grad_proj, preferred_element_type=jnp.float32)
    grad_hidden_one = lax.psum(
        jnp.einsum("jte,jde->td", grad_proj, qkv_low, preferred_element_type=jnp.float32).astype(
            jnp.bfloat16
        ),
        "tensor",
    ).astype(jnp.float32)
    grad_gain_one = jnp.sum(grad_hidden_one * tokens_f * scale_one, axis=0)
    scaled_one = grad_hidden_one * gain_one_f
    grad_tokens = (
        grad_residual
        + scale_one * scaled_one
        - tokens_f
        * (scale_one * scale_one * scale_one)
        * jnp.mean(scaled_one * tokens_f, axis=-1, keepdims=True)
    )
    grad_qk = jnp.stack([grad_gain_query, grad_gain_key]).reshape(2, heads_here, HEAD)
    reduced = (
        lax.psum_scatter(
            grad_qkv.astype(jnp.bfloat16), "expert", scatter_dimension=1, tiled=True
        ).astype(jnp.float32),
        lax.psum_scatter(
            grad_out_w.astype(jnp.bfloat16), "expert", scatter_dimension=1, tiled=True
        ).astype(jnp.float32),
        lax.psum_scatter(
            grad_router.astype(jnp.bfloat16), "expert", scatter_dimension=0, tiled=True
        ).astype(jnp.float32),
        lax.psum_scatter(
            grad_gain_one.astype(jnp.bfloat16), "expert", scatter_dimension=0, tiled=True
        ).astype(jnp.float32),
        lax.psum_scatter(
            grad_gain_two.astype(jnp.bfloat16), "expert", scatter_dimension=0, tiled=True
        ).astype(jnp.float32),
        lax.psum_scatter(
            grad_qk.astype(jnp.bfloat16), "expert", scatter_dimension=2, tiled=True
        ).astype(jnp.float32),
    )
    return (
        block_out.astype(jnp.bfloat16),
        grad_tokens.astype(jnp.bfloat16),
        reduced[0],
        reduced[1],
        reduced[3],
        reduced[4],
        reduced[5],
        reduced[2],
        grad_gate_w,
        grad_up_w,
        grad_down,
    )


MESH_ID = pl.DeviceIdType.MESH
HBM = pl.BlockSpec(memory_space=pl.ANY)
VMEM = pl.BlockSpec(memory_space=pltpu.VMEM)
NZ, NY, NX, NC = 4, 2, 2, 2
GROUPS = NZ * NY


def place():
    e = lax.axis_index("expert")
    t = lax.axis_index("tensor")
    return lax.div(e, NY), lax.rem(e, NY), lax.div(t, NC), lax.rem(t, NC)


def device(z, y, x, c):
    return (z * NY + y, x * NC + c)


def run_if(condition, body):
    if condition is None:
        body()
    else:
        pl.when(condition)(body)


def greet(partners):
    barrier = pltpu.get_barrier_semaphore()
    for target, condition in partners:
        run_if(
            condition,
            lambda target=target: pl.semaphore_signal(
                barrier, inc=1, device_id=target, device_id_type=MESH_ID
            ),
        )
    count = sum(1 for _, condition in partners if condition is None)
    for _, condition in partners:
        if condition is not None:
            count = count + condition.astype(jnp.int32)
    pl.semaphore_wait(barrier, count)


def remote(source, target_ref, send_sem, recv_sem, target):
    return pltpu.make_async_remote_copy(
        src_ref=source,
        dst_ref=target_ref,
        send_sem=send_sem,
        recv_sem=recv_sem,
        device_id=target,
        device_id_type=MESH_ID,
    )


def block_rows(block, rows):
    return pl.ds(pl.multiple_of(block * rows, rows), rows)


class LineGather:
    def __init__(self, streams, sources, views, send_sem, recv_sem, y_first=()):
        self.z, self.y, self.x, self.c = place()
        self.streams, self.sources, self.views = streams, sources, views
        self.send_sem, self.recv_sem = send_sem, recv_sem
        self.y_first = y_first
        self.has_up, self.has_down = self.z < NZ - 1, self.z > 0
        self.pending = []

    def partners(self):
        z, y, x, c = self.z, self.y, self.x, self.c
        return [
            (device(z + 1, y, x, c), z < NZ - 1),
            (device(z - 1, y, x, c), z > 0),
            (device(z, 1 - y, x, c), None),
        ]

    def exists(self, rel):
        rel = rel % 7
        if rel == 0:
            return None
        return self.z >= rel if rel < 4 else self.z + (rel - 3) < NZ

    def block(self, rel):
        y = self.y if rel < 7 else 1 - self.y
        rel = rel % 7
        z = self.z if rel == 0 else (self.z - rel if rel < 4 else self.z + (rel - 3))
        return z * NY + y

    def send(self, stream, rel, way):
        z, y, x, c = self.z, self.y, self.x, self.c
        block = self.block(rel)
        there = self.views[stream](block)
        source = self.sources[stream] if rel == 0 else there
        near = rel % 7 == 0
        if way == 0:
            target, landing = device(z + 1, y, x, c), rel + 1
        elif way == 1:
            target, landing = device(z - 1, y, x, c), rel + (4 if near else 1)
        else:
            target, landing = device(z, 1 - y, x, c), 7 + rel
        return remote(
            source,
            there,
            self.send_sem.at[stream, rel, way],
            self.recv_sem.at[stream, landing],
            target,
        )

    def forwards(self, stream, rel):
        return rel < 7 or stream in self.y_first

    def start(self, stream, rel):
        if rel % 7 < 4:
            run = self.has_up
            run_if(run, lambda: self.send(stream, rel, 0).start())
            self.pending.append((stream, rel, 0, run))
        if rel % 7 == 0 or rel % 7 >= 4:
            run = self.has_down
            run_if(run, lambda: self.send(stream, rel, 1).start())
            self.pending.append((stream, rel, 1, run))
        if rel == 0 or stream not in self.y_first:
            self.send(stream, rel, 2).start()
            self.pending.append((stream, rel, 2, None))

    def arrive(self, stream, rel):
        there = self.views[stream](self.block(rel))
        remote(
            there,
            there,
            self.send_sem.at[stream, 0, 0],
            self.recv_sem.at[stream, rel],
            device(self.z, 1 - self.y, self.x, self.c),
        ).wait_recv()

    def order(self):
        return [7, 1, 4, 8, 11, 2, 5, 9, 12, 3, 6, 10, 13]

    def run(self, hook=None):
        for stream in self.streams:
            self.start(stream, 0)
        for rel in self.order():
            def step(rel=rel):
                marks = len(self.pending)
                for stream in self.streams:
                    self.arrive(stream, rel)
                    if rel < 7:
                        self.start(stream, rel)
                    if hook is not None:
                        hook(stream, rel)
                if rel < 7:
                    late = self.pending[marks:]
                    del self.pending[marks:]
                    self.finish_later(late, rel)
            run_if(self.exists(rel), step)

    def finish_later(self, late, rel):
        self.late = getattr(self, "late", []) + [(rel, late)]

    def finish(self):
        for stream, rel, way, run in self.pending:
            run_if(run, lambda s=stream, r=rel, w=way: self.send(s, r, w).wait_send())
        for rel, late in getattr(self, "late", []):
            def body(late=late):
                for stream, rel, way, run in late:
                    run_if(run, lambda s=stream, r=rel, w=way: self.send(s, r, w).wait_send())
            run_if(self.exists(rel), body)


def cost(microseconds):
    return pl.CostEstimate(flops=0, bytes_accessed=int(microseconds * 3.0e6), transcendentals=0)


def comm_params(collective_id, megabytes=56):
    return pltpu.CompilerParams(
        collective_id=collective_id,
        has_side_effects=True,
        vmem_limit_bytes=megabytes * 1024 * 1024,
    )


def weight_gather(qkv_low, out_low, smalls, collective_id):
    parts, rows, width = qkv_low.shape
    depth, columns = out_low.shape

    def kernel(qkv, out, small, qkv_all, out_all, small_all, send_sem, recv_sem, local_sem):
        views = [
            lambda b: qkv_all.at[:, block_rows(b, rows), :],
            lambda b: out_all.at[:, block_rows(b, columns)],
            lambda b: small_all.at[b],
        ]
        line = LineGather([2, 0, 1], [qkv, out, small], views, send_sem, recv_sem)
        greet(line.partners())
        own = line.block(0)
        keep = [
            pltpu.make_async_copy(source, view(own), local_sem.at[i])
            for i, (source, view) in enumerate(zip([qkv, out, small], views))
        ]
        for copy in keep:
            copy.start()
        line.run()
        line.finish()
        for copy in keep:
            copy.wait()

    return pl.pallas_call(
        kernel,
        out_shape=(
            jax.ShapeDtypeStruct((parts, rows * GROUPS, width), jnp.bfloat16),
            jax.ShapeDtypeStruct((depth, columns * GROUPS), jnp.bfloat16),
            jax.ShapeDtypeStruct((GROUPS,) + smalls.shape, jnp.float32),
        ),
        in_specs=[HBM] * 3,
        out_specs=(HBM, HBM, HBM),
        scratch_shapes=[
            pltpu.SemaphoreType.DMA((3, 14, 3)),
            pltpu.SemaphoreType.DMA((3, 14)),
            pltpu.SemaphoreType.DMA((3,)),
        ],
        compiler_params=comm_params(collective_id),
        cost_estimate=cost(100),
        name="weight_gather",
    )(qkv_low, out_low, smalls)


def token_gather(block, collective_id):
    rows, width = block.shape
    a_cols, c_cols = width * 3 // 16, width // 8

    def kernel(own_ref, all_ref, send_sem, recv_sem, x_send, x_recv, core_send, core_recv, local_sem):
        z, y, x, c = place()

        def a_at(xx, cc):
            return pl.ds(pl.multiple_of(xx * (2 * a_cols) + cc * a_cols, 128), a_cols)

        def c_at(cc):
            return pl.ds(pl.multiple_of(4 * a_cols + cc * c_cols, 128), c_cols)

        def view(b, columns):
            return all_ref.at[block_rows(b, rows), columns]

        sources = [own_ref.at[:, a_at(x, c)], own_ref.at[:, c_at(c)]]
        views = [lambda b: view(b, a_at(x, c)), lambda b: view(b, c_at(c))]
        line = LineGather([0, 1], sources, views, send_sem, recv_sem)
        across, twin = device(z, y, 1 - x, c), device(z, y, x, 1 - c)
        greet(line.partners() + [(across, None), (twin, None)])
        keep = pltpu.make_async_copy(own_ref, all_ref.at[block_rows(line.block(0), rows), :], local_sem)
        keep.start()

        def to_twin(rel, stream, landing=False):
            b = line.block(rel)
            columns = [a_at(x, c), c_at(c), a_at(1 - x, c)][stream]
            other = [a_at(x, 1 - c), c_at(1 - c), a_at(1 - x, 1 - c)][stream]
            piece = view(b, other if landing else columns)
            return remote(piece, piece, core_send.at[rel, stream], core_recv.at[rel, stream], twin)

        def to_across(rel, landing=False):
            b = line.block(rel)
            piece = view(b, a_at(1 - x if landing else x, c))
            return remote(piece, piece, x_send.at[rel], x_recv.at[rel], across)

        def hook(stream, rel):
            if stream == 0:
                to_across(rel).start()
            to_twin(rel, stream).start()

        line.run(hook)
        for rel in line.order():
            def relay(rel=rel):
                to_across(rel, True).wait_recv()
                to_twin(rel, 2).start()
            run_if(line.exists(rel), relay)
        for rel in line.order():
            def end(rel=rel):
                to_across(rel).wait_send()
                for stream in range(3):
                    to_twin(rel, stream, True).wait_recv()
                    to_twin(rel, stream).wait_send()
            run_if(line.exists(rel), end)
        line.finish()
        keep.wait()

    return pl.pallas_call(
        kernel,
        out_shape=jax.ShapeDtypeStruct((rows * GROUPS, width), block.dtype),
        in_specs=[HBM],
        out_specs=HBM,
        scratch_shapes=[
            pltpu.SemaphoreType.DMA((2, 14, 3)),
            pltpu.SemaphoreType.DMA((2, 14)),
            pltpu.SemaphoreType.DMA((14,)),
            pltpu.SemaphoreType.DMA((14,)),
            pltpu.SemaphoreType.DMA((14, 3)),
            pltpu.SemaphoreType.DMA((14, 3)),
            pltpu.SemaphoreType.DMA,
        ],
        compiler_params=comm_params(collective_id),
        cost_estimate=cost(45),
        name="token_gather",
    )(block)


def add_into(rows, step, store):
    def body(i, carry):
        store(pl.ds(pl.multiple_of(i * step, step), step))
        return carry

    lax.fori_loop(0, rows // step, body, 0)


def group_stages(part_ref, out_ref, core_buf, x_buf, send_sem, recv_sem):
    rows, width = part_ref.shape
    half, quarter = width // 2, width // 4
    z, y, x, c = place()
    across, twin = device(z, y, 1 - x, c), device(z, y, x, 1 - c)

    def half_of(cc):
        return pl.ds(pl.multiple_of(cc * half, half), half)

    def quarter_of(xx, cc):
        return pl.ds(pl.multiple_of(cc * half + xx * quarter, quarter), quarter)

    own, from_x = out_ref.at[:, quarter_of(x, c)], out_ref.at[:, quarter_of(1 - x, c)]
    to_x = core_buf.at[:, pl.ds(pl.multiple_of((1 - x) * quarter, quarter), quarter)]
    sources = [part_ref.at[:, half_of(1 - c)], to_x, own, own, from_x]
    landings = [core_buf, x_buf, own, own, from_x]
    targets = [twin, across, across, twin, twin]

    def copy(k):
        return remote(sources[k], landings[k], send_sem.at[k], recv_sem.at[k], targets[k])

    def arrive(k, landing):
        remote(landing, landing, send_sem.at[k], recv_sem.at[k], targets[k]).wait_recv()

    def begin():
        copy(0).start()

    def core_step():
        copy(0).wait_recv()
        add_to(core_buf, core_buf, part_ref.at[:, half_of(c)], 32)
        copy(1).start()

    def x_step():
        copy(1).wait_recv()
        add_to(own, x_buf, core_buf.at[:, pl.ds(pl.multiple_of(x * quarter, quarter), quarter)], 32)
        copy(2).start()
        copy(3).start()

    def spread():
        arrive(2, from_x)
        copy(4).start()

    def end():
        arrive(3, out_ref.at[:, quarter_of(x, 1 - c)])
        arrive(4, out_ref.at[:, quarter_of(1 - x, 1 - c)])
        for k in range(5):
            copy(k).wait_send()

    return [begin, core_step, x_step, spread, end]


def group_sum(part_ref, out_ref, core_buf, x_buf, send_sem, recv_sem, meanwhile=None):
    stages = group_stages(part_ref, out_ref, core_buf, x_buf, send_sem, recv_sem)
    stages[0]()
    if meanwhile is not None:
        meanwhile()
    for stage in stages[1:]:
        stage()


def tensor_sum(part, collective_id):
    rows, width = part.shape

    def kernel(part_ref, out_ref, core_buf, x_buf, send_sem, recv_sem):
        z, y, x, c = place()
        greet([(device(z, y, 1 - x, c), None), (device(z, y, x, 1 - c), None)])
        group_sum(part_ref, out_ref, core_buf, x_buf, send_sem, recv_sem)

    return pl.pallas_call(
        kernel,
        out_shape=jax.ShapeDtypeStruct((rows, width), jnp.bfloat16),
        in_specs=[VMEM],
        out_specs=VMEM,
        scratch_shapes=[
            pltpu.VMEM((rows, width // 2), jnp.bfloat16),
            pltpu.VMEM((rows, width // 4), jnp.bfloat16),
            pltpu.SemaphoreType.DMA((5,)),
            pltpu.SemaphoreType.DMA((5,)),
        ],
        compiler_params=comm_params(collective_id, 16),
        cost_estimate=cost(17),
        name="tensor_sum",
    )(part)


Z_ORDER = (3, 0, 2, 1)


def accumulate(into, addend, step=64):
    rows = into.shape[0]
    step = min(step, rows)

    def body(i, carry):
        r = pl.ds(pl.multiple_of(i * step, step), step)
        total = into[r, :].astype(jnp.float32) + addend[r, :].astype(jnp.float32)
        into[r, :] = total.astype(into.dtype)
        return carry

    lax.fori_loop(0, rows // step, body, 0)


class LineReduce:
    def __init__(self, streams, own, y_buf, lo_buf, hi_buf, send_sem, recv_sem):
        self.z, self.y, self.x, self.c = place()
        self.streams = streams
        self.own, self.y_buf, self.lo_buf, self.hi_buf = own, y_buf, lo_buf, hi_buf
        self.send_sem, self.recv_sem = send_sem, recv_sem

    def partners(self):
        z, y, x, c = self.z, self.y, self.x, self.c
        return [
            (device(z + 1, y, x, c), z < NZ - 1),
            (device(z - 1, y, x, c), z > 0),
            (device(z, 1 - y, x, c), None),
        ]

    def copy(self, s, zz, way):
        z, y, x, c = self.z, self.y, self.x, self.c
        if way == 0:
            source, landing, target = self.own(s, zz, 1 - y), self.y_buf, device(z, 1 - y, x, c)
        elif way == 1:
            source, landing, target = self.y_buf(s, zz), self.lo_buf, device(z + 1, y, x, c)
        else:
            source, landing, target = self.y_buf(s, zz), self.hi_buf, device(z - 1, y, x, c)
        return remote(
            source, landing(s, zz), self.send_sem.at[s, zz, way], self.recv_sem.at[s, zz, way], target
        )

    def to_y(self, s, zz):
        self.copy(s, zz, 0).start()

    def take(self, s, zz, way):
        self.copy(s, zz, way).wait_recv()
        accumulate(self.y_buf(s, zz), (self.lo_buf if way == 1 else self.hi_buf)(s, zz))

    def along_z(self, s, zz):
        z = self.z
        self.copy(s, zz, 0).wait_recv()
        accumulate(self.y_buf(s, zz), self.own(s, zz, self.y))

        def upward():
            run_if(z > 0, lambda: self.take(s, zz, 1))
            self.copy(s, zz, 1).start()

        def downward():
            run_if(z < NZ - 1, lambda: self.take(s, zz, 2))
            self.copy(s, zz, 2).start()

        run_if(z < zz, upward)
        run_if(z > zz, downward)

    def home(self, done):
        for zz in range(NZ):
            def land(zz=zz):
                for s in self.streams:
                    if zz > 0:
                        self.take(s, zz, 1)
                    if zz < NZ - 1:
                        self.take(s, zz, 2)
                    done(s, self.y_buf(s, zz))
            run_if(self.z == zz, land)

    def finish(self):
        for zz in range(NZ):
            for s in self.streams:
                self.copy(s, zz, 0).wait_send()
                run_if(self.z < zz, lambda s=s, zz=zz: self.copy(s, zz, 1).wait_send())
                run_if(self.z > zz, lambda s=s, zz=zz: self.copy(s, zz, 2).wait_send())


def weight_reduce(qkv, out, smalls, collective_id):
    parts, depth, width = qkv.shape
    rows = depth // GROUPS
    out_rows, columns = out.shape[0], out.shape[1] // GROUPS

    def kernel(qkv_ref, out_ref, small_ref, qkv_sum, out_sum, small_sum,
               qkv_buf, out_buf, small_buf, send_sem, recv_sem):
        def own(s, zz, yy):
            b = zz * NY + yy
            if s < parts:
                return qkv_ref.at[s, block_rows(b, rows), :]
            if s == parts:
                return out_ref.at[:, block_rows(b, columns)]
            return small_ref.at[b]

        def slot(kind):
            def view(s, zz):
                if s < parts:
                    return qkv_buf.at[kind, zz, s]
                if s == parts:
                    return out_buf.at[kind, zz]
                return small_buf.at[kind, zz]
            return view

        streams = list(range(parts + 2))
        line = LineReduce(streams, own, slot(0), slot(1), slot(2), send_sem, recv_sem)
        greet(line.partners())
        work = [(s, zz) for s in [parts + 1, parts] + list(range(parts)) for zz in Z_ORDER]
        for s, zz in work:
            line.to_y(s, zz)
        for s, zz in work:
            line.along_z(s, zz)

        def done(s, total):
            target = qkv_sum.at[s] if s < parts else (out_sum if s == parts else small_sum)
            step = min(64, target.shape[0])

            def body(i, carry):
                r = pl.ds(pl.multiple_of(i * step, step), step)
                target[r, :] = total[r, :].astype(jnp.float32)
                return carry

            lax.fori_loop(0, target.shape[0] // step, body, 0)

        line.home(done)
        line.finish()

    return pl.pallas_call(
        kernel,
        out_shape=(
            jax.ShapeDtypeStruct((parts, rows, width), jnp.float32),
            jax.ShapeDtypeStruct((out_rows, columns), jnp.float32),
            jax.ShapeDtypeStruct(smalls.shape[1:], jnp.float32),
        ),
        in_specs=[VMEM] * 3,
        out_specs=(VMEM,) * 3,
        scratch_shapes=[
            pltpu.VMEM((3, NZ, parts, rows, width), jnp.bfloat16),
            pltpu.VMEM((3, NZ, out_rows, columns), jnp.bfloat16),
            pltpu.VMEM((3, NZ) + smalls.shape[1:], jnp.float32),
            pltpu.SemaphoreType.DMA((parts + 2, NZ, 3)),
            pltpu.SemaphoreType.DMA((parts + 2, NZ, 3)),
        ],
        compiler_params=comm_params(collective_id),
        cost_estimate=cost(120),
        name="weight_reduce",
    )(qkv, out, smalls)


def token_reduce(part, collective_id, pairs=None):
    tokens, width = part.shape
    rows = tokens // GROUPS
    half, quarter = width // 2, width // 4

    def kernel(part_ref, out_ref, core_buf, x_buf, y_buf, lo_buf, hi_buf,
               core_send, core_recv, x_send, x_recv, send_sem, recv_sem):
        z, y, x, c = place()
        across, twin = device(z, y, 1 - x, c), device(z, y, x, 1 - c)

        line = LineReduce(
            [0], lambda s, zz, yy: x_buf.at[zz * NY + yy], lambda s, zz: y_buf.at[zz],
            lambda s, zz: lo_buf.at[zz], lambda s, zz: hi_buf.at[zz], send_sem, recv_sem,
        )
        greet(line.partners() + [(across, None), (twin, None)])
        order = [(zz, flip) for zz in Z_ORDER for flip in (1, 0)]

        def number(zz, flip):
            return zz * NY + (1 - y if flip else y)

        def to_twin(zz, flip):
            b = number(zz, flip)
            return remote(
                part_ref.at[block_rows(b, rows), pl.ds(pl.multiple_of((1 - c) * half, half), half)],
                core_buf.at[b], core_send.at[zz, flip], core_recv.at[zz, flip], twin,
            )

        def to_across(zz, flip):
            b = number(zz, flip)
            return remote(
                core_buf.at[b, :, pl.ds(pl.multiple_of((1 - x) * quarter, quarter), quarter)],
                x_buf.at[b], x_send.at[zz, flip], x_recv.at[zz, flip], across,
            )

        def add_core(zz, flip):
            b = number(zz, flip)

            def store(r):
                at = pl.ds(pl.multiple_of(b * rows + r.start, 16), r.size)
                core_buf[b, r, :] = (
                    core_buf[b, r, :].astype(jnp.float32)
                    + part_ref[at, pl.ds(pl.multiple_of(c * half, half), half)].astype(jnp.float32)
                ).astype(jnp.bfloat16)

            add_into(rows, 32, store)

        def add_across(zz, flip):
            b = number(zz, flip)

            def store(r):
                x_buf[b, r, :] = (
                    x_buf[b, r, :].astype(jnp.float32)
                    + core_buf[b, r, pl.ds(pl.multiple_of(x * quarter, quarter), quarter)].astype(jnp.float32)
                ).astype(jnp.bfloat16)

            add_into(rows, 64, store)

        def stage_twin(i):
            to_twin(*order[i]).wait_recv()
            add_core(*order[i])
            to_across(*order[i]).start()

        def stage_across(i):
            zz, flip = order[i]
            to_across(zz, flip).wait_recv()
            add_across(zz, flip)
            if flip:
                line.to_y(0, zz)

        def stage_y(zz):
            line.along_z(0, zz)

        for zz, flip in order:
            to_twin(zz, flip).start()
        count = len(order)
        for i in range(count + 4):
            if i < count:
                stage_twin(i)
            if 0 <= i - 1 < count:
                stage_across(i - 1)
            if i >= 3 and (i - 3) % 2 == 0 and (i - 3) // 2 < NZ:
                stage_y(Z_ORDER[(i - 3) // 2])

        def done(s, total):
            def store(r):
                out_ref[r, :] = total[r, :]

            add_into(rows, 64, store)

        line.home(done)
        for zz, flip in order:
            to_twin(zz, flip).wait_send()
            to_across(zz, flip).wait_send()
        line.finish()

    return pl.pallas_call(
        kernel,
        out_shape=jax.ShapeDtypeStruct((rows, quarter), jnp.bfloat16),
        in_specs=[VMEM],
        out_specs=VMEM,
        scratch_shapes=[
            pltpu.VMEM((GROUPS, rows, half), jnp.bfloat16),
            pltpu.VMEM((GROUPS, rows, quarter), jnp.bfloat16),
            pltpu.VMEM((NZ, rows, quarter), jnp.bfloat16),
            pltpu.VMEM((NZ, rows, quarter), jnp.bfloat16),
            pltpu.VMEM((NZ, rows, quarter), jnp.bfloat16),
            pltpu.SemaphoreType.DMA((NZ, 2)),
            pltpu.SemaphoreType.DMA((NZ, 2)),
            pltpu.SemaphoreType.DMA((NZ, 2)),
            pltpu.SemaphoreType.DMA((NZ, 2)),
            pltpu.SemaphoreType.DMA((1, NZ, 3)),
            pltpu.SemaphoreType.DMA((1, NZ, 3)),
        ],
        compiler_params=comm_params(collective_id),
        cost_estimate=cost(60),
        name="token_reduce",
    )(part)


def gate_exchange(part, collective_id):
    groups = part.shape[0]
    tensors = NX * NC

    def kernel(part_ref, out_ref, landing, total, send_t, recv_t, send_e, recv_e):
        e = lax.axis_index("expert")
        t = lax.axis_index("tensor")
        mates = [(e, lax.rem(t + k, tensors)) for k in range(1, tensors)]
        peers = [(lax.rem(e + k, groups), t) for k in range(1, groups)]
        greet([(target, None) for target in mates + peers])
        near = [
            remote(part_ref, landing.at[k], send_t.at[k], recv_t.at[k], mates[k])
            for k in range(tensors - 1)
        ]
        for copy in near:
            copy.start()
        for copy in near:
            copy.wait_recv()
        value = part_ref[...]
        for k in range(tensors - 1):
            value = value + landing[k]
        total[...] = value
        far = [
            remote(
                total.at[lax.rem(e + k, groups)], out_ref.at[e], send_e.at[k - 1], recv_e.at[k - 1],
                peers[k - 1],
            )
            for k in range(1, groups)
        ]
        for copy in far:
            copy.start()
        out_ref[e] = total[e]
        for k in range(1, groups):
            source = out_ref.at[lax.rem(e + groups - k, groups)]
            remote(source, source, send_e.at[k - 1], recv_e.at[k - 1], peers[k - 1]).wait_recv()
        for copy in near + far:
            copy.wait_send()

    return pl.pallas_call(
        kernel,
        out_shape=jax.ShapeDtypeStruct(part.shape, jnp.float32),
        in_specs=[VMEM],
        out_specs=VMEM,
        scratch_shapes=[
            pltpu.VMEM((tensors - 1,) + part.shape, jnp.float32),
            pltpu.VMEM(part.shape, jnp.float32),
            pltpu.SemaphoreType.DMA((tensors - 1,)),
            pltpu.SemaphoreType.DMA((tensors - 1,)),
            pltpu.SemaphoreType.DMA((groups - 1,)),
            pltpu.SemaphoreType.DMA((groups - 1,)),
        ],
        compiler_params=comm_params(collective_id, 16),
        cost_estimate=cost(10),
        name="gate_exchange",
    )(part)


def dot(a, b, dims):
    return lax.dot_general(a, b, ((dims[:1], dims[1:]), ((), ())), preferred_element_type=jnp.float32)


def add_to(target, first, second, step=64):
    rows = target.shape[0]

    def body(i, carry):
        r = pl.ds(pl.multiple_of(i * step, step), step)
        total = first[r, :].astype(jnp.float32) + second[r, :].astype(jnp.float32)
        target[r, :] = total.astype(target.dtype)
        return carry

    lax.fori_loop(0, rows // step, body, 0)


def expert_layer(
    hidden_two, grad_out_all, gate_up, down, router_t, chosen_all, residual, collective_id
):
    rows, width = hidden_two.shape
    tokens = rows * GROUPS
    units = down.shape[0]
    local = 2
    hidden = units // local
    experts = router_t.shape[0]
    half, part, piece = width // 2, width // 4, width // 8
    tensors = NX * NC
    steps = GROUPS + 4
    a_cols, c_cols = width * 3 // 16, width // 8
    low = jnp.bfloat16
    wide = width // 4

    def kernel(
        own_in, dy_in, gu_ref, down_ref, router_ref, chosen_ref, x1_in,
        block_out, dh_out, gates_out, gate_w, up_w, down_w,
        h, dy, gated, dgu, dx, y_part, yc_buf, yx_buf, yy_buf, ylo_buf, yhi_buf, x1, gu_stage, d_stage,
        core_buf, px_buf, py_buf, qy_buf, qx_buf, z_sum, lo_buf, hi_buf, gate_part, gate_land,
        in_sem, own_sem, line_s, line_r, hx_s, hx_r, hc_s, hc_r, x1_sem, yc_s, yc_r, yx_s, yx_r, yy_s, yy_r, yz_s, yz_r, gu_sem, d_sem, core_s, core_r, px_s, px_r, py_s, py_r, qy_s, qy_r, qx_s, qx_r,
        z_s, z_r, near_s, near_r, far_s, far_r, end_s, end_r,
    ):
        z, y, x, c = place()
        e, t = lax.axis_index("expert"), lax.axis_index("tensor")
        across, twin, beside = device(z, y, 1 - x, c), device(z, y, x, 1 - c), device(z, 1 - y, x, c)
        mates = [(e, lax.rem(t + k, tensors)) for k in range(1, tensors)]
        peers = [(lax.rem(e + k, GROUPS), t) for k in range(1, GROUPS)]
        greet([(target, None) for target in mates + peers])

        def pick(values, index):
            result = values[-1]
            for k in range(len(values) - 1):
                result = jnp.where(index == k, values[k], result)
            return result

        def zz_of(j):
            return pick([z, pick([1, 0, 3, 2], z), pick([3, 3, 0, 0], z), pick([2, 2, 1, 1], z)], j)

        def is_own(i):
            return (i == 0) | ((i >= 2) & (lax.rem(i, 2) == 1))

        def block_of(i):
            return zz_of(lax.div(i, 2)) * NY + jnp.where(is_own(i), y, 1 - y)

        def flip_block(j):
            return zz_of(j) * NY + 1 - y

        def own_block(j):
            return zz_of(j) * NY + y

        def a_at(xx, cc):
            return pl.ds(pl.multiple_of(xx * (2 * a_cols) + cc * a_cols, 128), a_cols)

        def c_at(cc):
            return pl.ds(pl.multiple_of(4 * a_cols + cc * c_cols, 128), c_cols)

        def h_view(b, columns):
            return h.at[block_rows(b, rows), columns]

        line = LineGather(
            [0, 1], [own_in.at[:, a_at(x, c)], own_in.at[:, c_at(c)]],
            [lambda b: h_view(b, a_at(x, c)), lambda b: h_view(b, c_at(c))], line_s, line_r,
        )

        def h_twin(b, stream, landing=False):
            cc = 1 - c if landing else c
            piece = h_view(b, [a_at(x, cc), c_at(cc), a_at(1 - x, cc)][stream])
            return remote(piece, piece, hc_s.at[b, stream], hc_r.at[b, stream], twin)

        def h_across(b, landing=False):
            piece = h_view(b, a_at(1 - x if landing else x, c))
            return remote(piece, piece, hx_s.at[b], hx_r.at[b], across)

        def gather_event(rel):
            def body():
                b = line.block(rel)
                marks = len(line.pending)
                for stream in (0, 1):
                    line.arrive(stream, rel)
                    if rel < 7:
                        line.start(stream, rel)
                    if stream == 0:
                        h_across(b).start()
                    h_twin(b, stream).start()
                late = line.pending[marks:]
                del line.pending[marks:]
                line.finish_later(late, rel)
            run_if(line.exists(rel), body)

        def relay(i):
            b = block_of(i)
            h_across(b, True).wait_recv()
            h_twin(b, 2).start()

        for stream in (0, 1):
            line.start(stream, 0)
        keep = pltpu.make_async_copy(own_in, h.at[block_rows(z * NY + y, rows), :], own_sem)
        keep.start()

        def load(i):
            r = block_rows(block_of(i), rows)
            return pltpu.make_async_copy(dy_in.at[r, :], dy.at[r, :], in_sem.at[i])

        def start_load(i, carry):
            load(i).start()
            return carry

        lax.fori_loop(0, GROUPS, start_load, 0)
        x1_copy = pltpu.make_async_copy(
            x1_in.at[:, pl.ds(pl.multiple_of(c * half + x * part, part), part)], x1, x1_sem
        )
        x1_copy.start()

        def to_twin(i):
            b = block_of(i)
            return remote(
                dx.at[lax.rem(i, 2), :, pl.ds(pl.multiple_of((1 - c) * half, half), half)],
                core_buf.at[b], core_s.at[i], core_r.at[i], twin,
            )

        def p_across(i):
            b = block_of(i)
            return remote(
                core_buf.at[b, :, pl.ds(pl.multiple_of((1 - x) * piece, piece), piece)],
                px_buf.at[b], px_s.at[i], px_r.at[i], across,
            )

        def p_beside(j):
            return remote(px_buf.at[flip_block(j)], py_buf.at[j], py_s.at[j], py_r.at[j], beside)

        def q_beside(j):
            return remote(
                core_buf.at[flip_block(j), :, pl.ds(part, part)], qy_buf.at[j], qy_s.at[j], qy_r.at[j], beside
            )

        def q_across(j):
            return remote(
                qy_buf.at[j, :, pl.ds(pl.multiple_of((1 - x) * piece, piece), piece)],
                qx_buf.at[j], qx_s.at[j], qx_r.at[j], across,
            )

        def up(j, s):
            return remote(z_sum.at[s, j], lo_buf.at[s, j], z_s.at[0, s, j], z_r.at[0, s, j], device(z + 1, y, x, c))

        def down_z(j, s):
            return remote(z_sum.at[s, j], hi_buf.at[s, j], z_s.at[1, s, j], z_r.at[1, s, j], device(z - 1, y, x, c))

        def take_twin(i):
            to_twin(i).wait_recv()
            b = block_of(i)
            mine = core_buf.at[b]
            add_to(mine, mine, dx.at[lax.rem(i, 2), :, pl.ds(pl.multiple_of(c * half, half), half)], 32)
            p_across(i).start()
            pl.when(jnp.logical_not(is_own(i)))(lambda: q_beside(lax.div(i, 2)).start())

        def take_p_across(i):
            p_across(i).wait_recv()
            b = block_of(i)
            add_to(
                px_buf.at[b], px_buf.at[b],
                core_buf.at[b, :, pl.ds(pl.multiple_of(x * piece, piece), piece)],
            )

        def take_q_beside(j):
            q_beside(j).wait_recv()
            add_to(qy_buf.at[j], qy_buf.at[j], core_buf.at[own_block(j), :, pl.ds(part, part)])
            q_across(j).start()

        def take_q_across(j):
            q_across(j).wait_recv()
            add_to(
                z_sum.at[1, zz_of(j)], qx_buf.at[j], qy_buf.at[j, :, pl.ds(pl.multiple_of(x * piece, piece), piece)]
            )

        def take_p_beside(j):
            p_beside(j).wait_recv()
            add_to(z_sum.at[0, zz_of(j)], py_buf.at[j], px_buf.at[own_block(j)])

        def hop(j, k):
            zz = zz_of(j)

            def upward():
                for s in range(2):
                    if k > 0:
                        up(zz, s).wait_recv()
                        add_to(z_sum.at[s, zz], z_sum.at[s, zz], lo_buf.at[s, zz])
                    up(zz, s).start()

            def downward():
                for s in range(2):
                    if k > 0:
                        down_z(zz, s).wait_recv()
                        add_to(z_sum.at[s, zz], z_sum.at[s, zz], hi_buf.at[s, zz])
                    down_z(zz, s).start()

            pl.when((z < zz) & (z == k))(upward)
            pl.when((z > zz) & (NZ - 1 - z == k))(downward)

        def y_twin(i):
            return remote(
                y_part.at[lax.rem(i, 2), :, pl.ds(pl.multiple_of((1 - c) * half, half), half)],
                yc_buf.at[block_of(i)], yc_s.at[i], yc_r.at[i], twin,
            )

        def y_across(i):
            b = block_of(i)
            return remote(
                yc_buf.at[b, :, pl.ds(pl.multiple_of((1 - x) * part, part), part)],
                yx_buf.at[b], yx_s.at[i], yx_r.at[i], across,
            )

        def y_beside(j):
            return remote(yx_buf.at[flip_block(j)], yy_buf.at[zz_of(j)], yy_s.at[j], yy_r.at[j], beside)

        def y_up(j):
            return remote(yy_buf.at[j], ylo_buf.at[j], yz_s.at[0, j], yz_r.at[0, j], device(z + 1, y, x, c))

        def y_down(j):
            return remote(yy_buf.at[j], yhi_buf.at[j], yz_s.at[1, j], yz_r.at[1, j], device(z - 1, y, x, c))

        def take_y_twin(i):
            y_twin(i).wait_recv()
            mine = yc_buf.at[block_of(i)]
            add_to(mine, mine, y_part.at[lax.rem(i, 2), :, pl.ds(pl.multiple_of(c * half, half), half)], 32)
            y_across(i).start()

        def take_y_across(i):
            y_across(i).wait_recv()
            b = block_of(i)
            mine = yx_buf.at[b]
            add_to(mine, mine, yc_buf.at[b, :, pl.ds(pl.multiple_of(x * part, part), part)])
            pl.when(jnp.logical_not(is_own(i)))(lambda: y_beside(lax.div(i, 2)).start())

        def take_y_beside(j):
            y_beside(j).wait_recv()
            add_to(yy_buf.at[zz_of(j)], yy_buf.at[zz_of(j)], yx_buf.at[own_block(j)])

        def y_hop(j, k):
            zz = zz_of(j)

            def upward():
                if k > 0:
                    y_up(zz).wait_recv()
                    add_to(yy_buf.at[zz], yy_buf.at[zz], ylo_buf.at[zz])
                y_up(zz).start()

            def downward():
                if k > 0:
                    y_down(zz).wait_recv()
                    add_to(yy_buf.at[zz], yy_buf.at[zz], yhi_buf.at[zz])
                y_down(zz).start()

            pl.when((z < zz) & (z == k))(upward)
            pl.when((z > zz) & (NZ - 1 - z == k))(downward)

        def front(i):
            load(i).wait()
            b = block_of(i)
            pl.when(i == 0)(keep.wait)

            def landed():
                for stream in range(3):
                    h_twin(b, stream, True).wait_recv()

            pl.when(i > 0)(landed)
            r = block_rows(b, rows)
            rows_h, rows_dy = h[r, :], dy[r, :]
            logits = dot(rows_h, router_ref[...], (1, 1))
            shifted = jnp.exp(logits - jnp.max(logits, axis=-1, keepdims=True))
            probs = shifted / jnp.sum(shifted, axis=-1, keepdims=True) * chosen_ref[r, :].astype(jnp.float32)
            lane = lax.broadcasted_iota(jnp.int32, probs.shape, 1)
            line = lax.broadcasted_iota(jnp.int32, (rows, 128), 1)
            found = jnp.zeros((rows, 128), jnp.float32)
            for expert in range(local):
                at, up_at = pl.ds(expert * hidden, hidden), pl.ds((local + expert) * hidden, hidden)
                gate = jnp.sum(jnp.where(lane == e * local + expert, probs, 0.0), axis=-1, keepdims=True)
                pre = dot(rows_h, gu_ref[:, at], (1, 0))
                scale = dot(rows_h, gu_ref[:, up_at], (1, 0))
                back = dot(rows_dy, down_ref[at, :], (1, 1))
                sigmoid = jax.nn.sigmoid(pre)
                swish = pre * sigmoid
                active = swish * scale
                gated[r, at] = (active * gate).astype(low)
                found = jnp.where(line == expert, jnp.sum(active * back, axis=-1, keepdims=True), found)
                back = back * gate
                dgu[r, at] = (back * scale * sigmoid * (1.0 + pre * (1.0 - sigmoid))).astype(low)
                dgu[r, up_at] = (back * swish).astype(low)
            gate_part[b] = jnp.transpose(found)[:8, :]

        def rear(i):
            r = block_rows(block_of(i), rows)
            slot = lax.rem(i, 2)
            pl.when(i >= 2)(lambda: to_twin(i - 2).wait_send())

            def columns(k, carry):
                at = pl.ds(pl.multiple_of(k * wide, wide), wide)
                dx[slot, :, at] = dot(dgu[r, :], gu_ref[at, :], (1, 1)).astype(low)
                return carry

            lax.fori_loop(0, width // wide, columns, 0)
            to_twin(i).start()
            pl.when(i >= 2)(lambda: y_twin(i - 2).wait_send())

            def y_columns(k, carry):
                at = pl.ds(pl.multiple_of(k * wide, wide), wide)
                y_part[slot, :, at] = dot(gated[r, :], down_ref[:, at], (1, 0)).astype(low)
                return carry

            lax.fori_loop(0, width // wide, y_columns, 0)
            y_twin(i).start()

        tiles = width // piece // 4
        d_width = width // 8

        def gu_copies(n):
            slot = lax.rem(n, 2)
            at = pl.ds(pl.multiple_of(n * piece, piece), piece)
            return [
                pltpu.make_async_copy(
                    gu_stage.at[slot, :, pl.ds(k * hidden, hidden)],
                    (gate_w if k < local else up_w).at[k % local, at, :],
                    gu_sem.at[slot, k],
                )
                for k in range(2 * local)
            ]

        def d_copies(n):
            slot = lax.rem(n, 2)
            at = pl.ds(pl.multiple_of(n * d_width, d_width), d_width)
            return [
                pltpu.make_async_copy(
                    d_stage.at[slot, pl.ds(k * hidden, hidden), :], down_w.at[k, :, at], d_sem.at[slot, k]
                )
                for k in range(local)
            ]

        def each(copies, what):
            for copy in copies:
                getattr(copy, what)()

        def weight_grads(q):
            def tile(k, carry):
                n = q * tiles + k
                pl.when(n >= 2)(lambda: each(gu_copies(n - 2), "wait"))
                at = pl.ds(pl.multiple_of(n * piece, piece), piece)
                gu_stage[lax.rem(n, 2)] = dot(h[:, at], dgu[...], (0, 0))
                each(gu_copies(n), "start")
                return carry

            lax.fori_loop(0, tiles, tile, 0)

            def d_tile(k, carry):
                n = q * 2 + k
                pl.when(n >= 2)(lambda: each(d_copies(n - 2), "wait"))
                at = pl.ds(pl.multiple_of(n * d_width, d_width), d_width)
                d_stage[lax.rem(n, 2)] = dot(gated[...], dy[:, at], (0, 0))
                each(d_copies(n), "start")
                return carry

            lax.fori_loop(0, 2, d_tile, 0)

        near = [
            remote(gate_part, gate_land.at[k], near_s.at[k], near_r.at[k], mates[k])
            for k in range(tensors - 1)
        ]

        def far(k):
            return remote(
                gate_land.at[tensors - 1, lax.rem(e + k, GROUPS)], gates_out.at[e],
                far_s.at[k - 1], far_r.at[k - 1], peers[k - 1],
            )

        def sum_near():
            for copy in near:
                copy.wait_recv()
            total = gate_part[...]
            for k in range(tensors - 1):
                total = total + gate_land[k]
            gate_land[tensors - 1] = total
            for k in range(1, GROUPS):
                far(k).start()
            gates_out[e] = gate_land[tensors - 1, e]

        def step(i, carry):
            def at(number, body):
                pl.when(i == number)(body)

            odd, even = lax.rem(i, 2) == 1, lax.rem(i, 2) == 0
            j_even, j_odd = lax.div(i, 2) - 1, lax.div(i - 1, 2) - 1
            pl.when(i < GROUPS)(lambda: front(i))

            def events(*rels):
                for rel in rels:
                    gather_event(rel)

            at(1, lambda: events(2, 5, 8, 11))
            at(2, lambda: events(3, 6))
            at(3, lambda: events(10, 13))

            def twins():
                take_twin(i - 1)
                take_y_twin(i - 1)

            pl.when((i >= 1) & (i <= GROUPS))(twins)
            pl.when(even & (i >= 4) & (i <= GROUPS))(lambda: take_q_beside(j_even))
            at(3, lambda: take_q_beside(0))
            at(4, lambda: take_q_across(0))

            def late():
                take_p_across(i - 2)
                pl.when(i > 3)(lambda: take_q_across(j_odd))
                pl.when(i == 3)(lambda: p_beside(0).start())

            pl.when(odd & (i >= 3) & (i <= GROUPS + 1))(late)
            at(GROUPS, lambda: each(near, "start"))
            at(GROUPS + 1, sum_near)
            pl.when(i < GROUPS)(lambda: rear(i))
            pl.when(i >= GROUPS)(lambda: weight_grads(i - GROUPS))
            at(0, lambda: events(7, 1, 4))
            at(2, lambda: events(9, 12))
            pl.when(i < GROUPS - 1)(lambda: relay(i + 1))

            def pass_p():
                take_p_across(i - 2)
                pl.when(i > 2)(lambda: p_beside(j_even).start())

            pl.when(even & (i >= 2) & (i <= GROUPS))(pass_p)
            at(4, lambda: take_p_beside(0))

            def join():
                take_p_beside(j_odd)
                hop(j_odd, 0)

            pl.when(odd & (i >= 5) & (i <= GROUPS + 1))(join)
            pl.when((i == GROUPS) | (i == GROUPS + 2))(lambda: hop(j_even - 1, 1))
            at(GROUPS + 1, lambda: hop(1, 2))
            pl.when((i >= 2) & (i <= GROUPS + 1))(lambda: take_y_across(i - 2))
            at(5, lambda: take_y_beside(0))

            def join_y():
                take_y_beside(j_even - 1)
                y_hop(j_even - 1, 0)

            pl.when(even & (i >= 6) & (i <= GROUPS + 2))(join_y)
            pl.when((i == GROUPS + 1) | (i == GROUPS + 3))(lambda: y_hop(j_odd - 1, 1))
            at(GROUPS + 2, lambda: y_hop(1, 2))
            return carry

        lax.fori_loop(0, steps, step, 0)

        def columns_of(s, xx, cc):
            return pl.ds(pl.multiple_of(cc * half + s * part + xx * piece, piece), piece)

        mine = z
        for s in range(2):
            def below(s=s):
                up(mine, s).wait_recv()
                add_to(z_sum.at[s, mine], z_sum.at[s, mine], lo_buf.at[s, mine])

            def above(s=s):
                down_z(mine, s).wait_recv()
                add_to(z_sum.at[s, mine], z_sum.at[s, mine], hi_buf.at[s, mine])

            pl.when(z > 0)(below)
            pl.when(z < NZ - 1)(above)
            own = dh_out.at[:, columns_of(s, x, c)]

            def keep(k, carry, s=s, own=own):
                r = pl.ds(pl.multiple_of(k * 64, 64), 64)
                own[r, :] = z_sum[s, mine, r, :]
                return carry

            lax.fori_loop(0, rows // 64, keep, 0)
            remote(own, own, end_s.at[0, s], end_r.at[0, s], across).start()
            remote(own, own, end_s.at[1, s], end_r.at[1, s], twin).start()
        def y_columns_of(xx, cc):
            return pl.ds(pl.multiple_of(cc * half + xx * part, part), part)

        def y_below():
            y_up(mine).wait_recv()
            add_to(yy_buf.at[mine], yy_buf.at[mine], ylo_buf.at[mine])

        def y_above():
            y_down(mine).wait_recv()
            add_to(yy_buf.at[mine], yy_buf.at[mine], yhi_buf.at[mine])

        pl.when(z > 0)(y_below)
        pl.when(z < NZ - 1)(y_above)
        x1_copy.wait()
        y_own = block_out.at[:, y_columns_of(x, c)]

        def finish(k, carry):
            r = pl.ds(pl.multiple_of(k * 64, 64), 64)
            y_own[r, :] = (x1[r, :] + yy_buf[mine, r, :].astype(jnp.float32)).astype(low)
            return carry

        lax.fori_loop(0, rows // 64, finish, 0)
        remote(y_own, y_own, end_s.at[0, 2], end_r.at[0, 2], across).start()
        remote(y_own, y_own, end_s.at[1, 2], end_r.at[1, 2], twin).start()
        for s in range(2):
            there = dh_out.at[:, columns_of(s, 1 - x, c)]
            remote(there, there, end_s.at[0, s], end_r.at[0, s], across).wait_recv()
            remote(there, there, end_s.at[2, s], end_r.at[2, s], twin).start()
        there = block_out.at[:, y_columns_of(1 - x, c)]
        remote(there, there, end_s.at[0, 2], end_r.at[0, 2], across).wait_recv()
        remote(there, there, end_s.at[2, 2], end_r.at[2, 2], twin).start()
        for k, xx in ((1, x), (2, 1 - x)):
            there = block_out.at[:, y_columns_of(xx, 1 - c)]
            remote(there, there, end_s.at[k, 2], end_r.at[k, 2], twin).wait_recv()
        for k, target in ((0, across), (1, twin), (2, twin)):
            there = block_out.at[:, y_columns_of(1 - x if k == 2 else x, c)]
            remote(there, there, end_s.at[k, 2], end_r.at[k, 2], target).wait_send()
        for s in range(2):
            for k, xx in ((1, x), (2, 1 - x)):
                there = dh_out.at[:, columns_of(s, xx, 1 - c)]
                remote(there, there, end_s.at[k, s], end_r.at[k, s], twin).wait_recv()
            for k, target in ((0, across), (1, twin), (2, twin)):
                there = dh_out.at[:, columns_of(s, 1 - x if k == 2 else x, c)]
                remote(there, there, end_s.at[k, s], end_r.at[k, s], target).wait_send()
        for k in range(1, GROUPS):
            there = gates_out.at[lax.rem(e + GROUPS - k, GROUPS)]
            remote(there, there, far_s.at[k - 1], far_r.at[k - 1], peers[k - 1]).wait_recv()
            far(k).wait_send()
        each(near, "wait_send")

        def drain(i, carry):
            pl.when(i >= GROUPS - 2)(lambda: to_twin(i).wait_send())
            pl.when(i >= GROUPS - 2)(lambda: y_twin(i).wait_send())
            p_across(i).wait_send()
            y_across(i).wait_send()
            return carry

        lax.fori_loop(0, GROUPS, drain, 0)

        def drain_pair(j, carry):
            p_beside(j).wait_send()
            q_beside(j).wait_send()
            q_across(j).wait_send()
            y_beside(j).wait_send()
            pl.when(z < j)(lambda: y_up(j).wait_send())
            pl.when(z > j)(lambda: y_down(j).wait_send())
            for s in range(2):
                pl.when(z < j)(lambda s=s: up(j, s).wait_send())
                pl.when(z > j)(lambda s=s: down_z(j, s).wait_send())
            return carry

        lax.fori_loop(0, NZ, drain_pair, 0)

        def drain_rows_of(i, carry):
            b = block_of(i)
            h_across(b).wait_send()
            for stream in range(3):
                h_twin(b, stream).wait_send()
            return carry

        lax.fori_loop(1, GROUPS, drain_rows_of, 0)
        line.finish()
        for k in range(2):
            each(gu_copies(4 * tiles - 2 + k), "wait")
            each(d_copies(6 + k), "wait")

    shape = jax.ShapeDtypeStruct
    dma = pltpu.SemaphoreType.DMA
    f32 = jnp.float32
    return pl.pallas_call(
        kernel,
        out_shape=(
            shape((rows, width), low),
            shape((rows, width), low),
            shape((GROUPS, 8, rows), f32),
            shape((local, width, hidden), f32),
            shape((local, width, hidden), f32),
            shape((local, hidden, width), f32),
        ),
        in_specs=[HBM, HBM, VMEM, VMEM, VMEM, VMEM, HBM],
        out_specs=(VMEM, VMEM, VMEM, HBM, HBM, HBM),
        scratch_shapes=[
            pltpu.VMEM((tokens, width), low),
            pltpu.VMEM((tokens, width), low),
            pltpu.VMEM((tokens, units), low),
            pltpu.VMEM((tokens, 2 * units), low),
            pltpu.VMEM((2, rows, width), low),
            pltpu.VMEM((2, rows, width), low),
            pltpu.VMEM((GROUPS, rows, half), low),
            pltpu.VMEM((GROUPS, rows, part), low),
            pltpu.VMEM((NZ, rows, part), low),
            pltpu.VMEM((NZ, rows, part), low),
            pltpu.VMEM((NZ, rows, part), low),
            pltpu.VMEM((rows, part), f32),
            pltpu.VMEM((2, piece, 2 * units), f32),
            pltpu.VMEM((2, units, width // 8), f32),
            pltpu.VMEM((GROUPS, rows, half), low),
            pltpu.VMEM((GROUPS, rows, piece), low),
            pltpu.VMEM((NZ, rows, piece), low),
            pltpu.VMEM((NZ, rows, part), low),
            pltpu.VMEM((NZ, rows, piece), low),
            pltpu.VMEM((2, NZ, rows, piece), low),
            pltpu.VMEM((2, NZ, rows, piece), low),
            pltpu.VMEM((2, NZ, rows, piece), low),
            pltpu.VMEM((GROUPS, 8, rows), f32),
            pltpu.VMEM((tensors, GROUPS, 8, rows), f32),
            dma((GROUPS,)), dma, dma((2, 14, 3)), dma((2, 14)), dma((GROUPS,)), dma((GROUPS,)),
            dma((GROUPS, 3)), dma((GROUPS, 3)), dma, dma((GROUPS,)), dma((GROUPS,)), dma((GROUPS,)), dma((GROUPS,)),
            dma((NZ,)), dma((NZ,)), dma((2, NZ)), dma((2, NZ)), dma((2, 2 * local)), dma((2, local)),
            dma((GROUPS,)), dma((GROUPS,)), dma((GROUPS,)), dma((GROUPS,)),
            dma((NZ,)), dma((NZ,)), dma((NZ,)), dma((NZ,)), dma((NZ,)), dma((NZ,)),
            dma((2, 2, NZ)), dma((2, 2, NZ)),
            dma((tensors - 1,)), dma((tensors - 1,)), dma((GROUPS - 1,)), dma((GROUPS - 1,)),
            dma((3, 3)), dma((3, 3)),
        ],
        compiler_params=comm_params(collective_id, 62),
        cost_estimate=cost(80),
        name="expert_layer",
    )(hidden_two, grad_out_all, gate_up, down, router_t, chosen_all, residual)


def exchange_rows(value, part_ref, land_ref, send_sem, recv_sem, mates):
    rows = value.shape[0]
    line = lax.broadcasted_iota(jnp.int32, (rows, 128), 1)
    part_ref[...] = jnp.transpose(jnp.where(line == 0, value, 0.0))[:8, :]
    for k, mate in enumerate(mates):
        remote(part_ref, land_ref.at[k], send_sem.at[k], recv_sem.at[k], mate).start()


def exchanged_rows(part_ref, land_ref, send_sem, recv_sem, mates):
    total = part_ref[...]
    for k, mate in enumerate(mates):
        remote(part_ref, land_ref.at[k], send_sem.at[k], recv_sem.at[k], mate).wait_recv()
    for k in range(len(mates)):
        total = total + land_ref[k]
    rows = part_ref.shape[1]
    tall = jnp.concatenate([total, jnp.zeros((120, rows), jnp.float32)], axis=0)
    return jnp.transpose(tall)[:, :1]


def drain_rows(part_ref, land_ref, send_sem, recv_sem, mates):
    for k, mate in enumerate(mates):
        remote(part_ref, land_ref.at[k], send_sem.at[k], recv_sem.at[k], mate).wait_send()


def turn(value, cosine, sine):
    return value * cosine + pltpu.roll(value, HEAD // 2, 1) * sine


def project(tokens, w_qkv, w_out, out_grad, smalls, cosine, sine, collective_id):
    rows, width = tokens.shape
    parts, depth, columns = w_qkv.shape
    heads = columns // HEAD
    tensors = NX * NC
    back = WINDOW // rows
    low, f32 = jnp.bfloat16, jnp.float32
    QUERY, KEY, VALUE, SMALL, OUT, GRAD = 0, 1, 2, 3, 4, 5
    out_rows, out_columns = w_out.shape
    quarter = width // tensors

    def kernel(
        tok_ref, w_ref, out_ref, grad_in, small_ref, cos_ref, sin_ref,
        w_all, out_all, grad_all, small_all, h1_ref, raw_ref, scale_ref, q_ref, context,
        own_w, own_out, weights, total, part_k, land_k, part_q, land_q,
        send_sem, recv_sem, out_sem, small_sem, kept, ks_s, ks_r, qs_s, qs_r, c_s, c_r, hx_s, hx_r, hc_s, hc_r,
    ):
        z, y, x, c = place()
        e, t = lax.axis_index("expert"), lax.axis_index("tensor")
        mates = [(e, lax.rem(t + k, tensors)) for k in range(1, tensors)]
        beside, above = device(z, 1 - y, x, c), device(z + 1, y, x, c)
        views = [
            lambda b: weights.at[QUERY, block_rows(b, depth), :],
            lambda b: weights.at[KEY, block_rows(b, depth), :],
            lambda b: weights.at[VALUE, block_rows(b, depth), :],
            lambda b: small_all.at[b],
            lambda b: out_all.at[:, block_rows(b, out_columns)],
            lambda b: grad_view(b, x, c),
        ]
        across, twin = device(z, y, 1 - x, c), device(z, y, x, 1 - c)

        def quarter_at(xx, cc):
            return pl.ds(pl.multiple_of((xx * NC + cc) * quarter, quarter), quarter)

        def grad_view(b, xx, cc):
            return grad_all.at[block_rows(b, rows), quarter_at(xx, cc)]

        def grad_across(b, landing=False):
            piece = grad_view(b, 1 - x if landing else x, c)
            return remote(piece, piece, hx_s.at[b], hx_r.at[b], across)

        def grad_twin(b, relayed, landing=False):
            piece = grad_view(b, 1 - x if relayed else x, 1 - c if landing else c)
            return remote(piece, piece, hc_s.at[b, relayed], hc_r.at[b, relayed], twin)

        line = LineGather(
            [SMALL, VALUE, KEY, QUERY, OUT, GRAD],
            [own_w.at[0], own_w.at[1], own_w.at[2], small_ref, own_out, grad_in.at[:, quarter_at(x, c)]],
            views, send_sem, recv_sem, y_first=(OUT,),
        )
        greet(line.partners() + [(mate, None) for mate in mates])
        line.start(SMALL, 0)
        for part in (VALUE, KEY, QUERY):
            def cast(i, carry, part=part):
                r = pl.ds(pl.multiple_of(i * 32, 32), 32)
                own_w[part, r, :] = w_ref[part, r, :].astype(low)
                return carry

            lax.fori_loop(0, depth // 32, cast, 0)
            if part != QUERY:
                line.start(part, 0)

        def cast_out(i, carry):
            r = pl.ds(pl.multiple_of(i * 32, 32), 32)
            own_out[r, :] = out_ref[r, :].astype(low)
            return carry

        lax.fori_loop(0, out_rows // 32, cast_out, 0)
        keep_out = pltpu.make_async_copy(own_out, out_all.at[:, block_rows(line.block(0), out_columns)], kept.at[0])
        keep_out.start()
        keep_grad = pltpu.make_async_copy(grad_in, grad_all.at[block_rows(line.block(0), rows), :], kept.at[1])
        keep_grad.start()

        def square(i, carry):
            r = pl.ds(pl.multiple_of(i * 32, 32), 32)
            value = tok_ref[r, :].astype(f32)
            scale_ref[r, 0:1] = lax.rsqrt(jnp.mean(value * value, axis=-1, keepdims=True) + EPS)
            return carry

        lax.fori_loop(0, rows // 32, square, 0)
        total[...] = jnp.zeros_like(total)
        own_small = pltpu.make_async_copy(small_ref, small_all.at[line.block(0)], small_sem)
        own_small.start()

        def use(stream, rel):
            b = line.block(rel)
            at = pl.ds(pl.multiple_of(b * depth, depth), depth)
            if stream == SMALL:
                gain = small_ref[0:1, :] if rel == 0 else small_all[b, 0:1, :]
                h1_ref[:, at] = (tok_ref[:, at].astype(f32) * scale_ref[:, 0:1] * gain).astype(low)
                return
            block = own_w[stream] if rel == 0 else weights[stream, block_rows(b, depth), :]
            total[stream] += dot(h1_ref[:, at], block, (1, 0))

        def event(stream, rel):
            def body():
                line.arrive(stream, rel)
                if line.forwards(stream, rel):
                    marks = len(line.pending)
                    line.start(stream, rel)
                    late = line.pending[marks:]
                    del line.pending[marks:]
                    line.finish_later(late, rel)
                if stream == GRAD:
                    b = line.block(rel)
                    grad_across(b).start()
                    grad_twin(b, 0).start()
                elif stream != OUT:
                    use(stream, rel)
            run_if(line.exists(rel), body)

        use(SMALL, 0)
        use(VALUE, 0)
        own_small.wait()
        use(KEY, 0)
        early, late = [7, 1, 4, 8, 11, 2, 5], [9, 12, 3, 6, 10, 13]
        for rel in early:
            event(SMALL, rel)
            event(VALUE, rel)
        line.start(QUERY, 0)
        for rel in late:
            event(SMALL, rel)
            event(VALUE, rel)

        def context_copy(which, k):
            if k == 2:
                source, target = 0, above
            elif k == 4:
                source, target = 2, above
            else:
                source, target = jnp.where(y == 0, k - 1, k + 1), beside
            return remote(
                context.at[source, which], context.at[k, which], c_s.at[which, k], c_r.at[which, k], target
            )

        sends = {2: z < NZ - 1, 4: (z >= 1) & (z < NZ - 1), 1: (y == 0) | (z >= 1), 3: z >= 1 + y}
        takes = {2: z >= 1, 4: z >= 2, 1: (y == 1) | (z >= 1), 3: z >= 2 - y}

        def context_send(which, k):
            run_if(sends[k], lambda: context_copy(which, k).start())

        def context_take(which, k):
            run_if(takes[k], lambda: context_copy(which, k).wait_recv())

        for k in range(1, back + 1):
            def clear(k=k):
                context[k] = jnp.zeros_like(context[k])
            run_if(jnp.logical_not(takes[k]), clear)

        context[0, 1] = total[VALUE].astype(low)
        context_send(1, 2)
        run_if(y == 0, lambda: context_copy(1, 1).start())
        for rel in early:
            event(KEY, rel)
        for rel in late:
            event(KEY, rel)
        line.start(OUT, 0)
        key_raw = total[KEY]
        raw_ref[1] = key_raw
        exchange_rows(jnp.sum(key_raw * key_raw, axis=-1, keepdims=True), part_k, land_k, ks_s, ks_r, mates)
        use(QUERY, 0)
        for rel in early[:3]:
            event(QUERY, rel)

        key_scale = lax.rsqrt(exchanged_rows(part_k, land_k, ks_s, ks_r, mates) / width + EPS)
        scale_ref[:, 2:3] = key_scale
        slices = HEAD // GROUPS
        gains = []
        for which in range(2):
            per_head = []
            for head in range(heads):
                start = (which * heads + head) * slices
                per_head.append(
                    jnp.concatenate([small_all[b, 2:3, start : start + slices] for b in range(GROUPS)], axis=1)
                )
            gains.append(per_head)

        def rotated(which, scale, store):
            for head in range(heads):
                at = pl.ds(head * HEAD, HEAD)
                value = total[which, :, at] * scale * gains[which][head]
                store(at, turn(value, cos_ref[...], sin_ref[...]).astype(low))

        def store_key(at, value):
            context[0, 0, :, at] = value

        rotated(KEY, key_scale, store_key)
        context_send(0, 2)
        run_if(y == 0, lambda: context_copy(0, 1).start())

        def relay_two(which):
            context_take(which, 2)
            context_send(which, 4)
            run_if((y == 1) & (z >= 1), lambda: context_copy(which, 1).start())
            run_if((y == 0) & sends[3], lambda: context_copy(which, 3).start())

        def relay_four(which):
            context_take(which, 4)
            run_if((y == 1) & sends[3], lambda: context_copy(which, 3).start())

        relay_two(1)
        for rel in early[3:]:
            event(QUERY, rel)
        relay_four(1)
        for rel in late[:4]:
            event(QUERY, rel)
        relay_two(0)
        for rel in late[4:]:
            event(QUERY, rel)
        line.start(GRAD, 0)
        query_raw = total[QUERY]
        raw_ref[0] = query_raw
        exchange_rows(jnp.sum(query_raw * query_raw, axis=-1, keepdims=True), part_q, land_q, qs_s, qs_r, mates)
        for part in range(parts):
            weights[part, block_rows(line.block(0), depth), :] = own_w[part]
        keep = pltpu.make_async_copy(weights, w_all, out_sem)
        keep.start()
        relay_four(0)
        query_scale = lax.rsqrt(exchanged_rows(part_q, land_q, qs_s, qs_r, mates) / width + EPS)
        scale_ref[:, 1:2] = query_scale

        def store_query(at, value):
            q_ref[:, at] = value

        rotated(QUERY, query_scale, store_query)
        for rel in early:
            event(OUT, rel)
            event(GRAD, rel)
        for which in (1, 0):
            for k in (1, 3):
                context_take(which, k)
        for rel in late:
            event(OUT, rel)
            event(GRAD, rel)
        for rel in early + late:
            def relay(rel=rel):
                b = line.block(rel)
                grad_across(b, True).wait_recv()
                grad_twin(b, 1).start()
            run_if(line.exists(rel), relay)
        for rel in early + late:
            def landed(rel=rel):
                b = line.block(rel)
                grad_across(b).wait_send()
                for relayed in range(2):
                    grad_twin(b, relayed, True).wait_recv()
                    grad_twin(b, relayed).wait_send()
            run_if(line.exists(rel), landed)
        line.finish()
        keep_out.wait()
        keep_grad.wait()
        for which in range(2):
            for k in range(1, back + 1):
                run_if(sends[k], lambda which=which, k=k: context_copy(which, k).wait_send())
        drain_rows(part_k, land_k, ks_s, ks_r, mates)
        drain_rows(part_q, land_q, qs_s, qs_r, mates)
        keep.wait()

    shape, dma = jax.ShapeDtypeStruct, pltpu.SemaphoreType.DMA
    return pl.pallas_call(
        kernel,
        out_shape=(
            shape((parts, depth * GROUPS, columns), low),
            shape((out_rows, out_columns * GROUPS), low),
            shape((rows * GROUPS, width), low),
            shape((GROUPS,) + smalls.shape, f32),
            shape((rows, width), low),
            shape((2, rows, columns), f32),
            shape((rows, 128), f32),
            shape((rows, columns), low),
            shape((back + 1, 2, rows, columns), low),
        ),
        in_specs=[VMEM, VMEM, VMEM, HBM, VMEM, VMEM, VMEM],
        out_specs=(HBM,) * 3 + (VMEM,) * 6,
        scratch_shapes=[
            pltpu.VMEM((parts, depth, columns), low),
            pltpu.VMEM((out_rows, out_columns), low),
            pltpu.VMEM((parts, depth * GROUPS, columns), low),
            pltpu.VMEM((parts, rows, columns), f32),
            pltpu.VMEM((8, rows), f32),
            pltpu.VMEM((tensors - 1, 8, rows), f32),
            pltpu.VMEM((8, rows), f32),
            pltpu.VMEM((tensors - 1, 8, rows), f32),
            dma((6, 14, 3)), dma((6, 14)), dma, dma, dma((2,)),
            dma((tensors - 1,)), dma((tensors - 1,)), dma((tensors - 1,)), dma((tensors - 1,)),
            dma((2, back + 1)), dma((2, back + 1)),
            dma((GROUPS,)), dma((GROUPS,)), dma((GROUPS, 2)), dma((GROUPS, 2)),
        ],
        compiler_params=comm_params(collective_id, 48),
        cost_estimate=cost(100),
        name="project",
    )(tokens, w_qkv, w_out, out_grad, smalls, cosine, sine)


def attend(query, context, segment_query, segment_keys, tokens, out_low, gain, collective_id):
    rows, columns = query.shape
    width = tokens.shape[1]
    blocks = context.shape[0]
    heads = columns // HEAD
    half, quarter = width // 2, width // 4
    low, f32 = jnp.bfloat16, jnp.float32

    def kernel(
        q_ref, context_ref, sq_ref, sk_ref, tok_ref, out_ref, gain_ref,
        o_ref, lse_ref, x1_ref, h2_ref, scale_ref,
        part, full, core_buf, x_buf, send_sem, recv_sem,
    ):
        z, y, x, c = place()
        across, twin = device(z, y, 1 - x, c), device(z, y, x, 1 - c)
        greet([(across, None), (twin, None)])
        row = lax.broadcasted_iota(jnp.int32, (rows, rows), 0)
        column = lax.broadcasted_iota(jnp.int32, (rows, rows), 1)
        allowed = []
        for k in range(blocks):
            distance = row - column + k * rows
            allowed.append(
                (sq_ref[...] == sk_ref[k : k + 1, :]) & (distance >= 0) & (distance < WINDOW)
            )
        line = lax.broadcasted_iota(jnp.int32, (rows, 128), 1)
        lse = jnp.zeros((rows, 128), f32)
        for head in range(heads):
            at = pl.ds(head * HEAD, HEAD)
            scores = [
                jnp.where(
                    allowed[k], dot(q_ref[:, at], context_ref[k, 0, :, at], (1, 1)) * HEAD ** (-0.5), -1e30
                )
                for k in range(blocks)
            ]
            largest = scores[0]
            for k in range(1, blocks):
                largest = jnp.maximum(largest, scores[k])
            largest = jnp.max(largest, axis=-1, keepdims=True)
            weights = [jnp.exp(s - largest) for s in scores]
            amount = weights[0]
            for k in range(1, blocks):
                amount = amount + weights[k]
            amount = jnp.sum(amount, axis=-1, keepdims=True)
            inverse = 1.0 / amount
            value = jnp.zeros((rows, HEAD), f32)
            for k in range(blocks):
                value = value + dot((weights[k] * inverse).astype(low), context_ref[k, 1, :, at], (1, 0))
            o_ref[:, at] = value.astype(low)
            lse = jnp.where(line == head, largest + jnp.log(amount), lse)
        lse_ref[...] = lse

        def half_of(cc):
            return pl.ds(pl.multiple_of(cc * half, half), half)

        def fill(cc):
            def body(k, carry):
                at = pl.ds(pl.multiple_of(cc * half + k * quarter, quarter), quarter)
                part[:, at] = dot(o_ref[...], out_ref[:, at], (1, 0)).astype(low)
                return carry

            lax.fori_loop(0, 2, body, 0)

        fill(1 - c)
        group_sum(part, full, core_buf, x_buf, send_sem, recv_sem, lambda: fill(c))

        def norm(i, carry):
            r = pl.ds(pl.multiple_of(i * 32, 32), 32)
            value = tok_ref[r, :].astype(f32) + full[r, :].astype(f32)
            scale = lax.rsqrt(jnp.mean(value * value, axis=-1, keepdims=True) + EPS)
            x1_ref[r, :] = value
            scale_ref[r, :] = jnp.broadcast_to(scale, (32, 128))
            h2_ref[r, :] = (value * scale * gain_ref[...]).astype(low)
            return carry

        lax.fori_loop(0, rows // 32, norm, 0)

    shape, dma = jax.ShapeDtypeStruct, pltpu.SemaphoreType.DMA
    return pl.pallas_call(
        kernel,
        out_shape=(
            shape((rows, columns), low),
            shape((rows, 128), f32),
            shape((rows, width), f32),
            shape((rows, width), low),
            shape((rows, 128), f32),
        ),
        in_specs=[VMEM] * 7,
        out_specs=(VMEM,) * 5,
        scratch_shapes=[
            pltpu.VMEM((rows, width), low),
            pltpu.VMEM((rows, width), low),
            pltpu.VMEM((rows, half), low),
            pltpu.VMEM((rows, quarter), low),
            dma((5,)), dma((5,)),
        ],
        compiler_params=comm_params(collective_id, 40),
        cost_estimate=cost(40),
        name="attend",
    )(query, context, segment_query, segment_keys, tokens, out_low, gain)


def attend_back(
    grad_hidden, grad_probs, router_t, hidden_two, residual, scale_two, gain_two, out_grad,
    query, context, segment_query, segment_keys, attended, log_sums, raw, scales, qk_gains,
    cosine, sine, hidden_one, tokens, gain_one, qkv_low, out_low, collective_id,
):
    rows, width = tokens.shape
    columns = query.shape[1]
    heads = columns // HEAD
    experts = router_t.shape[0]
    blocks = context.shape[0]
    depth = width // GROUPS
    small_rows = 8 + experts
    tensors = NX * NC
    half, quarter = width // 2, width // 4
    low, f32 = jnp.bfloat16, jnp.float32
    QUERY, KEY, VALUE, OUT, SMALL = 0, 1, 2, 3, 4

    def kernel(
        dh_ref, gates_ref, router_ref, h2_ref, x1_ref, s2_ref, g2_ref, dy_ref,
        q_ref, context_ref, sq_ref, sk_ref, o_ref, lse_ref, raw_ref, scale_ref, qkg_ref,
        cos_ref, sin_ref, h1_ref, tok_ref, g1_ref, w_hbm, out_ref,
        tok_grad, qkv_sum, out_sum, small_sum,
        weights, dx1, da, do, dot_sums, dq, dkv, proj, send_kv, land_y, land_z,
        part, full, core_buf, x_buf, small, line_sum,
        main_buf, out_acc, out_lo, out_hi, out_land, small_buf, part_k, land_k, part_q, land_q,
        w_sem, y_s, y_r, z_s, z_r, group_s, group_r, ks_s, ks_r, qs_s, qs_r, line_s, line_r, out_s, out_r, out_y_s, out_y_r,
    ):
        z, y, x, c = place()
        e, t = lax.axis_index("expert"), lax.axis_index("tensor")
        mates = [(e, lax.rem(t + k, tensors)) for k in range(1, tensors)]
        beside, below = device(z, 1 - y, x, c), device(z - 1, y, x, c)
        fetch = pltpu.make_async_copy(w_hbm, weights, w_sem)
        fetch.start()

        def own_part(s, b):
            if s == SMALL:
                return small[b]
            at = pl.ds(pl.multiple_of(b * depth, depth), depth)
            return dot(h1_ref[:, at], proj[s], (0, 0))

        def out_copy(zz, yy, way):
            landing = (out_lo if way == 0 else out_hi).at[zz, yy]
            target = device(z + 1, y, x, c) if way == 0 else below
            return remote(out_acc.at[zz, yy], landing, out_s.at[zz, yy, way], out_r.at[zz, yy, way], target)

        def out_take(zz, yy, way):
            out_copy(zz, yy, way).wait_recv()
            total = out_acc.at[zz, yy]
            add_to(total, total, (out_lo if way == 0 else out_hi).at[zz, yy])

        def out_hop(k):
            for zz in Z_ORDER:
                for yy in range(NY):
                    def upward(zz=zz, yy=yy):
                        if k > 0:
                            out_take(zz, yy, 0)
                        out_copy(zz, yy, 0).start()

                    def downward(zz=zz, yy=yy):
                        if k > 0:
                            out_take(zz, yy, 1)
                        out_copy(zz, yy, 1).start()

                    if k < zz:
                        run_if((z < zz) & (z == k), upward)
                    if NZ - 1 - k > zz:
                        run_if((z > zz) & (NZ - 1 - z == k), downward)

        def out_beside():
            return remote(out_acc.at[z, 1 - y], out_land, out_y_s, out_y_r, beside)

        def out_start():
            for zz in range(NZ):
                for yy in range(NY):
                    at = pl.ds((zz * NY + yy) * depth, depth)
                    out_acc[zz, yy] = dot(o_ref[...], da[:, at], (0, 0)).astype(low)

        def out_home():
            for yy in range(NY):
                run_if(z > 0, lambda yy=yy: out_take(z, yy, 0))
                run_if(z < NZ - 1, lambda yy=yy: out_take(z, yy, 1))
            out_beside().start()

        def out_end():
            out_beside().wait_recv()
            out_sum[...] = out_acc[z, y].astype(f32) + out_land[...].astype(f32)
            out_beside().wait_send()
            for zz in range(NZ):
                for yy in range(NY):
                    run_if(z < zz, lambda zz=zz, yy=yy: out_copy(zz, yy, 0).wait_send())
                    run_if(z > zz, lambda zz=zz, yy=yy: out_copy(zz, yy, 1).wait_send())

        def slot(kind):
            def view(s, zz):
                if s == SMALL:
                    return small_buf.at[kind, zz]
                return main_buf.at[kind, zz, s]
            return view

        line = LineReduce([], lambda s, zz, yy: slot(3)(s, zz), slot(0), slot(1), slot(2), line_s, line_r)
        greet(line.partners() + [(mate, None) for mate in mates])

        grad_probs = gates_ref[...]
        logits = dot(h2_ref[...], router_ref[...], (1, 1))
        shifted = jnp.exp(logits - jnp.max(logits, axis=-1, keepdims=True))
        probs = shifted / jnp.sum(shifted, axis=-1, keepdims=True)
        grad_logits = probs * (grad_probs - jnp.sum(probs * grad_probs, axis=-1, keepdims=True))
        tall = jnp.transpose(
            jnp.concatenate([grad_logits, jnp.zeros((rows, 128 - experts), f32)], axis=1)
        )
        grad_logits = grad_logits.astype(low)
        tall = tall.astype(low)
        for b in range(GROUPS):
            small[b] = jnp.zeros_like(small[b])
            small[b, 8 : 8 + experts, :] = dot(tall, h2_ref[:, pl.ds(b * depth, depth)], (1, 0))[:experts]
        dx1[...] = dot(grad_logits, router_ref[...], (1, 0))
        line_sum[...] = jnp.zeros_like(line_sum)

        def norm_two(i, carry):
            r = pl.ds(pl.multiple_of(i * 32, 32), 32)
            grad = dh_ref[r, :].astype(f32) + dx1[r, :]
            value, scale = x1_ref[r, :], s2_ref[r, 0:1]
            line_sum[0:1, :] += jnp.sum(grad * (value * scale), axis=0, keepdims=True)
            grad = grad * g2_ref[...]
            inner = jnp.mean(grad * value, axis=-1, keepdims=True)
            result = dy_ref[r, :].astype(f32) + scale * grad - value * (scale * scale * scale) * inner
            dx1[r, :] = result
            da[r, :] = result.astype(low)
            return carry

        lax.fori_loop(0, rows // 32, norm_two, 0)

        out_start()
        out_hop(0)

        do[...] = dot(da[...], out_ref[...], (1, 1)).astype(low)
        wide = lax.broadcasted_iota(jnp.int32, (rows, 128), 1)
        sums = jnp.zeros((rows, 128), f32)
        for head in range(heads):
            at = pl.ds(head * HEAD, HEAD)
            inner = jnp.sum(do[:, at].astype(f32) * o_ref[:, at].astype(f32), axis=-1, keepdims=True)
            sums = jnp.where(wide == head, inner, sums)
        dot_sums[...] = sums
        dq[...] = jnp.zeros_like(dq)
        row = lax.broadcasted_iota(jnp.int32, (rows, rows), 0)
        column = lax.broadcasted_iota(jnp.int32, (rows, rows), 1)

        def attention_block(k):
            distance = row - column + k * rows
            allowed = (sq_ref[...] == sk_ref[k : k + 1, :]) & (distance >= 0) & (distance < WINDOW)
            for head in range(heads):
                at = pl.ds(head * HEAD, HEAD)
                queries, keys, values = q_ref[:, at], context_ref[k, 0, :, at], context_ref[k, 1, :, at]
                scores = dot(queries, keys, (1, 1)) * HEAD ** (-0.5)
                weight = jnp.where(allowed, jnp.exp(scores - lse_ref[:, head : head + 1]), 0.0)
                grad_weight = dot(do[:, at], values, (1, 1))
                grad_score = (
                    weight * (grad_weight - dot_sums[:, head : head + 1]) * HEAD ** (-0.5)
                ).astype(low)
                dq[:, at] += dot(grad_score, keys, (1, 0))
                dkv[k, 0, :, at] = dot(grad_score, queries, (0, 0))
                dkv[k, 1, :, at] = dot(weight.astype(low), do[:, at], (0, 0))

        exists = {0: None, 1: (y == 1) | (z >= 1), 2: z >= 1, 3: z >= 2 - y, 4: z >= 2}
        comes = {1: (y == 0) | (z >= 1), 3: z >= 1 + y}

        def kv_copy(which, k):
            if k in (1, 3):
                landing, target = land_y.at[k // 2, which], beside
                return remote(send_kv.at[k - 1, which], landing, y_s.at[k // 2, which], y_r.at[k // 2, which], target)
            landing = land_z.at[k // 2 - 1, which]
            return remote(
                send_kv.at[k - 1, which], landing, z_s.at[k // 2 - 1, which], z_r.at[k // 2 - 1, which], below
            )

        def kv_send(which, k):
            send_kv[k - 1, which] = dkv[k, which].astype(low)
            kv_copy(which, k).start()

        def merge(into, which, landed):
            add_to(dkv.at[into, which], dkv.at[into, which], landed, 32)

        for k in (3, 1, 4, 2, 0):
            def one(k=k):
                attention_block(k)
                if k in (1, 3):
                    kv_send(1, k)
                    kv_send(0, k)
            run_if(exists[k], one)

        def take_three(which):
            def land():
                kv_copy(which, 3).wait_recv()
                pl.when(y == 1)(lambda: merge(4, which, land_y.at[1, which]))
                pl.when(y == 0)(lambda: merge(2, which, land_y.at[1, which]))
            run_if(comes[3], land)
            run_if(exists[4], lambda: kv_send(which, 4))

        def take_one(which):
            def land():
                kv_copy(which, 1).wait_recv()
                pl.when(y == 1)(lambda: merge(2, which, land_y.at[0, which]))
                pl.when(y == 0)(lambda: merge(0, which, land_y.at[0, which]))
            run_if(comes[1], land)

        def take_four(which):
            def land():
                kv_copy(which, 4).wait_recv()
                merge(2, which, land_z.at[1, which])
            run_if((z >= 1) & (z < NZ - 1), land)
            run_if(exists[2], lambda: kv_send(which, 2))

        def take_two(which):
            def land():
                kv_copy(which, 2).wait_recv()
                merge(0, which, land_z.at[0, which])
            run_if(z < NZ - 1, land)

        def unturn(which, grad_of):
            inner = jnp.zeros((rows, 1), f32)
            for head in range(heads):
                at = pl.ds(head * HEAD, HEAD)
                grad = turn(grad_of(at), cos_ref[...], -sin_ref[...])
                value = raw_ref[which, :, at]
                line_sum[1 + which : 2 + which, at] = jnp.sum(
                    grad * (value * scale_ref[:, 1 + which : 2 + which]), axis=0, keepdims=True
                )
                grad = grad * qkg_ref[which : which + 1, at]
                dkv[1 + which, 0, :, at] = grad
                inner = inner + jnp.sum(grad * value, axis=-1, keepdims=True)
            return inner

        def denorm(which, inner):
            scale = scale_ref[:, 1 + which : 2 + which]
            rest = scale * scale * scale * inner / width
            for head in range(heads):
                at = pl.ds(head * HEAD, HEAD)
                proj[which, :, at] = (
                    scale * dkv[1 + which, 0, :, at] - raw_ref[which, :, at] * rest
                ).astype(low)

        def send_beside(s):
            for zz in Z_ORDER:
                buffer = slot(3)(s, zz)
                buffer[...] = own_part(s, zz * NY + 1 - y).astype(buffer.dtype)
                line.to_y(s, zz)

        take_three(1)
        take_three(0)
        out_hop(1)
        take_one(1)
        take_one(0)
        take_four(1)
        take_four(0)
        exchange_rows(unturn(QUERY, lambda at: dq[:, at]), part_q, land_q, qs_s, qs_r, mates)
        take_two(1)
        proj[VALUE] = dkv[0, 1].astype(low)
        denorm(QUERY, exchanged_rows(part_q, land_q, qs_s, qs_r, mates))
        send_beside(QUERY)
        send_beside(VALUE)
        take_two(0)
        out_hop(2)
        exchange_rows(unturn(KEY, lambda at: dkv[0, 0, :, at]), part_k, land_k, ks_s, ks_r, mates)
        denorm(KEY, exchanged_rows(part_k, land_k, ks_s, ks_r, mates))
        send_beside(KEY)
        out_home()
        fetch.wait()

        def half_of(cc):
            def body(i, carry):
                at = pl.ds(pl.multiple_of(cc * half + i * quarter, quarter), quarter)
                value = dot(proj[0], weights[0, at, :], (1, 1))
                for s in (1, 2):
                    value = value + dot(proj[s], weights[s, at, :], (1, 1))
                part[:, at] = value.astype(low)
                return carry

            lax.fori_loop(0, 2, body, 0)

        stages = group_stages(part, full, core_buf, x_buf, group_s, group_r)
        half_of(1 - c)
        stages[0]()
        half_of(c)
        stages[1]()

        def hop(s, zz, k):
            def upward():
                if k > 0:
                    line.take(s, zz, 1)
                line.copy(s, zz, 1).start()

            def downward():
                if k > 0:
                    line.take(s, zz, 2)
                line.copy(s, zz, 2).start()

            if k < zz:
                run_if((z < zz) & (z == k), upward)
            if NZ - 1 - k > zz:
                run_if((z > zz) & (NZ - 1 - z == k), downward)

        def receive(s, zz):
            line.copy(s, zz, 0).wait_recv()
            buffer = slot(0)(s, zz)
            buffer[...] = (buffer[...].astype(f32) + own_part(s, zz * NY + y)).astype(buffer.dtype)

        units = []

        def run_units(s):
            for zz in Z_ORDER:
                receive(s, zz)
                hop(s, zz, 0)
                units.append((s, zz))
                for k in (1, 2):
                    if len(units) > k:
                        hop(*units[-1 - k], k)

        def norm_one(i, carry):
            r = pl.ds(pl.multiple_of(i * 32, 32), 32)
            grad, value, scale = full[r, :].astype(f32), tok_ref[r, :].astype(f32), scale_ref[r, 0:1]
            line_sum[3:4, :] += jnp.sum(grad * (value * scale), axis=0, keepdims=True)
            grad = grad * g1_ref[...]
            inner = jnp.mean(grad * value, axis=-1, keepdims=True)
            tok_grad[r, :] = (
                dx1[r, :] + scale * grad - value * (scale * scale * scale) * inner
            ).astype(low)
            return carry

        run_units(QUERY)
        stages[2]()
        run_units(VALUE)
        stages[3]()
        stages[4]()
        lax.fori_loop(0, rows // 32, norm_one, 0)
        for b in range(GROUPS):
            at = pl.ds(b * depth, depth)
            small[b, 0:1, :] = line_sum[3:4, at]
            small[b, 1:2, :] = line_sum[0:1, at]
            for which in range(2):
                for k in range(columns // depth):
                    small[b, 2 + 2 * which + k : 3 + 2 * which + k, :] = line_sum[
                        1 + which : 2 + which, pl.ds(k * depth, depth)
                    ]
        send_beside(SMALL)
        run_units(KEY)
        run_units(SMALL)
        out_end()
        hop(*units[-1], 1)
        hop(*units[-2], 2)
        hop(*units[-1], 2)

        def done(s, total):
            target = qkv_sum.at[s] if s < OUT else small_sum
            target[...] = total[...].astype(f32)

        line.streams = [QUERY, VALUE, KEY, SMALL]
        line.home(done)
        line.finish()
        for which in range(2):
            for k in (1, 2, 3, 4):
                run_if(exists[k], lambda which=which, k=k: kv_copy(which, k).wait_send())
        drain_rows(part_k, land_k, ks_s, ks_r, mates)
        drain_rows(part_q, land_q, qs_s, qs_r, mates)

    shape, dma, vmem = jax.ShapeDtypeStruct, pltpu.SemaphoreType.DMA, pltpu.VMEM
    return pl.pallas_call(
        kernel,
        out_shape=(
            shape((rows, width), low),
            shape((3, depth, columns), f32),
            shape((columns, depth), f32),
            shape((small_rows, depth), f32),
        ),
        in_specs=[VMEM] * 22 + [HBM, VMEM],
        out_specs=(VMEM,) * 4,
        scratch_shapes=[
            vmem(qkv_low.shape, low),
            vmem((rows, width), f32),
            vmem((rows, width), low),
            vmem((rows, columns), low),
            vmem((rows, 128), f32),
            vmem((rows, columns), f32),
            vmem((blocks, 2, rows, columns), f32),
            vmem((3, rows, columns), low),
            vmem((blocks - 1, 2, rows, columns), low),
            vmem((2, 2, rows, columns), low),
            vmem((2, 2, rows, columns), low),
            vmem((rows, width), low),
            vmem((rows, width), low),
            vmem((rows, half), low),
            vmem((rows, quarter), low),
            vmem((GROUPS, small_rows, depth), f32),
            vmem((8, width), f32),
            vmem((4, NZ, 3, depth, columns), low),
            vmem((NZ, NY, columns, depth), low),
            vmem((NZ, NY, columns, depth), low),
            vmem((NZ, NY, columns, depth), low),
            vmem((columns, depth), low),
            vmem((4, NZ, small_rows, depth), f32),
            vmem((8, rows), f32),
            vmem((tensors - 1, 8, rows), f32),
            vmem((8, rows), f32),
            vmem((tensors - 1, 8, rows), f32),
            dma, dma((2, 2)), dma((2, 2)), dma((2, 2)), dma((2, 2)), dma((5,)), dma((5,)),
            dma((tensors - 1,)), dma((tensors - 1,)), dma((tensors - 1,)), dma((tensors - 1,)),
            dma((5, NZ, 3)), dma((5, NZ, 3)), dma((NZ, NY, 2)), dma((NZ, NY, 2)), dma, dma,
        ],
        compiler_params=comm_params(collective_id, 62),
        cost_estimate=cost(130),
        name="attend_back",
    )(
        grad_hidden, grad_probs, router_t, hidden_two, residual, scale_two, gain_two, out_grad,
        query, context, segment_query, segment_keys, attended, log_sums, raw, scales, qk_gains,
        cosine, sine, hidden_one, tokens, gain_one, qkv_low, out_low,
    )


def fast_shards(
    tokens_in,
    out_grad,
    w_qkv,
    w_attn_out,
    attn_gain,
    ffn_gain,
    qk_gain,
    w_router,
    w_gate,
    w_up,
    w_down,
    routes,
    segments,
):
    row_count, model_width = tokens_in.shape
    experts = w_router.shape[1]
    local_experts = w_gate.shape[0]
    heads_here = qk_gain.shape[1]
    local_width = heads_here * HEAD
    groups = lax.axis_size("expert")
    device_index = lax.axis_index("expert")
    tensor_index = lax.axis_index("tensor")
    quarter = model_width // lax.axis_size("tensor")
    hop_count = WINDOW // row_count
    score_scale = HEAD ** (-0.5)
    low = jnp.bfloat16

    chosen = jnp.any(
        routes[:, :, None] == jnp.arange(experts, dtype=jnp.int32)[None, None, :], axis=1
    ).astype(jnp.float32)
    qk_row = qk_gain.reshape(1, -1)

    def rounded(v):
        return lax.reduce_precision(v, 8, 7)

    smalls = jnp.concatenate(
        [
            rounded(attn_gain)[None, :],
            rounded(ffn_gain)[None, :],
            jnp.pad(rounded(qk_row), ((0, 0), (0, row_count - qk_row.shape[1]))),
            jnp.zeros((5, row_count), jnp.float32),
            w_router.T,
            chosen.T,
        ],
        axis=0,
    )
    global_rows = device_index * row_count + jnp.arange(row_count, dtype=jnp.int32)
    cosine_table, sine_table = angles(global_rows % SEQ, HEAD)
    wide_cosine = jnp.concatenate([cosine_table[:, 0], cosine_table[:, 0]], axis=1)
    wide_sine = jnp.concatenate([-sine_table[:, 0], sine_table[:, 0]], axis=1)
    (
        qkv_low, out_low, grad_out_all, small_all, hidden_one, raw, scales, query_low, context_blocks
    ) = project(tokens_in, w_qkv, w_attn_out, out_grad, smalls, wide_cosine, wide_sine, 0)
    gain_one_f = small_all[:, 0].reshape(model_width)
    gain_two_f = small_all[:, 1].reshape(model_width)
    qk_gains = (
        small_all[:, 2, : qk_row.shape[1]]
        .reshape(groups, 2, heads_here, HEAD // groups)
        .transpose(1, 2, 0, 3)
        .reshape(2, local_width)
    )
    router_t = small_all[:, 8 : 8 + experts].transpose(1, 0, 2).reshape(experts, model_width).astype(low)
    chosen_all = small_all[:, 8 + experts : 8 + 2 * experts].transpose(0, 2, 1).reshape(
        groups * row_count, experts
    )
    segment_window = lax.dynamic_slice_in_dim(
        jnp.concatenate([jnp.full((WINDOW,), -1, jnp.int32), segments]),
        device_index * row_count, (hop_count + 1) * row_count,
    )
    segment_query = segment_window[WINDOW:]
    segment_keys = segment_window.reshape(hop_count + 1, row_count)[::-1]
    attended, log_sums, residual, hidden_two, scale_two_wide = attend(
        query_low, context_blocks, segment_query[:, None], segment_keys, tokens_in, out_low,
        gain_two_f[None, :], 2,
    )
    gate_up = jnp.concatenate(
        [w[i] for w in (w_gate, w_up) for i in range(local_experts)], axis=1
    ).astype(low)
    down_low = w_down.reshape(-1, model_width).astype(low)
    block_out, grad_hidden_sum, grad_gate_sum, grad_gate_w, grad_up_w, grad_down = expert_layer(
        hidden_two, grad_out_all, gate_up, down_low, router_t, chosen_all.astype(low), residual, 5
    )
    grad_probs = grad_gate_sum[:, :local_experts].reshape(experts, row_count).T * chosen
    grad_tokens, qkv_sum, out_sum, small_sum = attend_back(
        grad_hidden_sum, grad_probs, router_t, hidden_two, residual, scale_two_wide,
        gain_two_f[None, :], out_grad, query_low, context_blocks, segment_query[:, None], segment_keys,
        attended, log_sums, raw, scales, qk_gains, wide_cosine, wide_sine, hidden_one, tokens_in,
        gain_one_f[None, :], qkv_low, out_low, 8,
    )
    return (
        block_out,
        grad_tokens,
        qkv_sum,
        out_sum,
        small_sum[0],
        small_sum[1],
        lax.dynamic_slice_in_dim(
            small_sum[2:6].reshape(2, heads_here, HEAD),
            device_index * qk_gain.shape[2], qk_gain.shape[2], axis=2,
        ),
        small_sum[8 : 8 + experts].T,
        grad_gate_w,
        grad_up_w,
        grad_down,
    )


def solution(mesh):
    placed = (
        P("expert", None),
        P("expert", None),
        P(None, "expert", "tensor"),
        P("tensor", "expert"),
        P("expert"),
        P("expert"),
        P(None, "tensor", "expert"),
        P("expert", None),
        P("expert", None, "tensor"),
        P("expert", None, "tensor"),
        P("expert", "tensor", None),
        P("expert", None),
        P(),
    )
    compact = (mesh.shape["expert"], mesh.shape["tensor"]) == (GROUPS, NX * NC)
    return jax.shard_map(
        fast_shards if compact else shards,
        mesh=mesh,
        in_specs=placed,
        out_specs=(
            P("expert", None),
            P("expert", None),
            P(None, "expert", "tensor"),
            P("tensor", "expert"),
            P("expert"),
            P("expert"),
            P(None, "tensor", "expert"),
            P("expert", None),
            P("expert", None, "tensor"),
            P("expert", None, "tensor"),
            P("expert", "tensor", None),
        ),
        check_vma=False,
    )
```

```python
import jax
import jax.numpy as jnp
from jax import lax
from jax.experimental import pallas as pl
from jax.experimental.pallas import tpu as pltpu
from jax.sharding import PartitionSpec as P

HEAD = 128
WINDOW = 1024
SEQ = 2048


EPS = 1e-05
THETA = 10000.0


def from_behind(value, axis, steps):
    count = lax.axis_size(axis)
    initial, last = (max(0, -steps), min(count, count - steps))
    return lax.ppermute(value, axis, [(source, source + steps) for source in range(initial, last)])


def angles(position, head_size):
    half_size = head_size // 2
    frequency = THETA ** (-(jnp.arange(half_size, dtype=jnp.float32) * 2.0 / head_size))
    phase_angle = position.astype(jnp.float32)[:, None] * frequency[None, :]
    return (jnp.cos(phase_angle)[:, None, :], jnp.sin(phase_angle)[:, None, :])


def rotate(rotated_in, cosine_table, sine_table):
    half_size = rotated_in.shape[-1] // 2
    first_half = rotated_in[..., :half_size]
    second_half = rotated_in[..., half_size:]
    return jnp.concatenate(
        [
            first_half * cosine_table - second_half * sine_table,
            second_half * cosine_table + first_half * sine_table,
        ],
        axis=-1,
    )


def slot_layout(block_routes, experts, capacity):
    flat_routes = block_routes.reshape(-1)
    onehot = (flat_routes[:, None] == jnp.arange(experts, dtype=jnp.int32)[None, :]).astype(
        jnp.int32
    )
    before = jnp.cumsum(onehot, axis=0) - onehot
    rank_within = jnp.sum(before * onehot, axis=1)
    slot_index = flat_routes * capacity + rank_within
    slot_table = (
        jnp.zeros((experts * capacity,), jnp.int32)
        .at[slot_index]
        .set(jnp.arange(flat_routes.shape[0], dtype=jnp.int32) + 1)
    )
    return (slot_index, slot_table)


def shards(
    tokens_in,
    out_grad,
    w_qkv,
    w_attn_out,
    attn_gain,
    ffn_gain,
    qk_gain,
    w_router,
    w_gate,
    w_up,
    w_down,
    routes,
    segments,
):
    row_count, model_width = tokens_in.shape
    experts = w_router.shape[1]
    per_token = routes.shape[1]
    local_experts = w_gate.shape[0]
    heads_here = qk_gain.shape[1]
    local_width = heads_here * HEAD
    groups = lax.axis_size("expert")
    device = lax.axis_index("expert")
    capacity = row_count * per_token * 3 // (2 * experts)
    hop_count = WINDOW // row_count
    buffer_shape = (groups, local_experts, capacity, model_width)
    score_scale = HEAD ** (-0.5)

    def fetch_weights():
        return (
            lax.all_gather(w_qkv.astype(jnp.bfloat16), "expert", axis=1, tiled=True),
            lax.all_gather(w_attn_out.astype(jnp.bfloat16), "expert", axis=1, tiled=True),
            lax.all_gather(w_router.astype(jnp.bfloat16), "expert", axis=0, tiled=True),
            lax.all_gather(attn_gain.astype(jnp.bfloat16), "expert", axis=0, tiled=True),
            lax.all_gather(ffn_gain.astype(jnp.bfloat16), "expert", axis=0, tiled=True),
            lax.all_gather(qk_gain.astype(jnp.bfloat16), "expert", axis=2, tiled=True),
        )

    def prepare(pieces):
        return (
            pieces[0],
            pieces[1],
            pieces[2],
            pieces[3].astype(jnp.float32),
            pieces[4].astype(jnp.float32),
            pieces[5].astype(jnp.float32).reshape(2, local_width),
        )

    qkv_low, out_low, router_low, gain_one_f, gain_two_f, qk_gains = prepare(fetch_weights())
    tokens_f = tokens_in.astype(jnp.float32)
    scale_one = lax.rsqrt(jnp.mean(tokens_f * tokens_f, axis=-1, keepdims=True) + EPS)
    hidden_one = (tokens_f * scale_one * gain_one_f).astype(jnp.bfloat16)
    projected = jnp.einsum("td,jde->jte", hidden_one, qkv_low, preferred_element_type=jnp.float32)
    query_raw = projected[0]
    key_raw = projected[1]
    query_sq, key_sq = lax.psum(
        (jnp.sum(query_raw * query_raw, axis=-1), jnp.sum(key_raw * key_raw, axis=-1)), "tensor"
    )
    query_scale = lax.rsqrt(query_sq / model_width + EPS)[:, None]
    key_scale = lax.rsqrt(key_sq / model_width + EPS)[:, None]
    normed_query = query_raw * query_scale
    normed_key = key_raw * key_scale
    global_rows = device * row_count + jnp.arange(row_count, dtype=jnp.int32)
    cosine_table, sine_table = angles(global_rows % SEQ, HEAD)
    query_low = rotate(
        (normed_query * qk_gains[0]).reshape(row_count, heads_here, HEAD), cosine_table, sine_table
    ).astype(jnp.bfloat16)
    key_low = rotate(
        (normed_key * qk_gains[1]).reshape(row_count, heads_here, HEAD), cosine_table, sine_table
    ).astype(jnp.bfloat16)
    value_low = projected[2].astype(jnp.bfloat16).reshape(row_count, heads_here, HEAD)
    own_pair = jnp.stack([key_low, value_low])
    earlier = []
    for steps_back in range(hop_count, 0, -1):
        earlier.append(from_behind(own_pair, "expert", steps_back))
    context = jnp.concatenate(earlier + [own_pair], axis=1)
    key_rows = (device - hop_count) * row_count + jnp.arange(
        (hop_count + 1) * row_count, dtype=jnp.int32
    )
    segment_keys = segments[jnp.maximum(key_rows, 0)]
    segment_query = segments[global_rows]
    distance = global_rows[:, None] - key_rows[None, :]
    allowed = (
        (key_rows[None, :] >= 0)
        & (segment_query[:, None] == segment_keys[None, :])
        & (distance >= 0)
        & (distance < WINDOW)
    )

    def score_block():
        raw_scores = (
            jnp.einsum("qhd,khd->hqk", query_low, context[0], preferred_element_type=jnp.float32)
            * score_scale
        )
        return jnp.where(allowed[None], raw_scores, -1e30)

    scores = score_block()
    largest = jnp.max(scores, axis=-1, keepdims=True)
    exp_scores = jnp.exp(scores - largest)
    exp_total = jnp.sum(exp_scores, axis=-1, keepdims=True)
    log_total = largest + jnp.log(exp_total)
    attn_probs = (exp_scores / exp_total).astype(jnp.bfloat16)
    attended = (
        jnp.einsum("hqk,khd->qhd", attn_probs, context[1], preferred_element_type=jnp.float32)
        .reshape(row_count, local_width)
        .astype(jnp.bfloat16)
    )
    attention_out = lax.psum(
        jnp.dot(attended, out_low, preferred_element_type=jnp.float32).astype(jnp.bfloat16),
        "tensor",
    ).astype(jnp.float32)
    residual = tokens_f + attention_out
    scale_two = lax.rsqrt(jnp.mean(residual * residual, axis=-1, keepdims=True) + EPS)
    normed_two = residual * scale_two
    hidden_two = (normed_two * gain_two_f).astype(jnp.bfloat16)
    logits = jnp.dot(hidden_two, router_low, preferred_element_type=jnp.float32)
    logit_exp = jnp.exp(logits - jnp.max(logits, axis=-1, keepdims=True))
    router_probs = logit_exp / jnp.sum(logit_exp, axis=-1, keepdims=True)
    chosen = routes[:, :, None] == jnp.arange(experts, dtype=jnp.int32)[None, None, :]
    gate_probs = jnp.sum(jnp.where(chosen, router_probs[:, None, :], 0.0), axis=-1)
    slot_index, slot_table = slot_layout(routes, experts, capacity)
    present = (slot_table > 0)[:, None]
    assigned = jnp.maximum(slot_table - 1, 0)
    row_of_slot = assigned // per_token
    gate_low = w_gate.astype(jnp.bfloat16)
    up_low = w_up.astype(jnp.bfloat16)
    down_low = w_down.astype(jnp.bfloat16)

    def send_rows():
        buffer_rows = jnp.where(
            present, hidden_two[row_of_slot], jnp.zeros((), jnp.bfloat16)
        ).reshape(buffer_shape)
        return lax.all_to_all(buffer_rows, "expert", split_axis=0, concat_axis=0, tiled=True)

    def expert_front(arrived):
        gate_pre = jnp.einsum(
            "secd,edh->sech", arrived, gate_low, preferred_element_type=jnp.float32
        )
        up_pre = jnp.einsum("secd,edh->sech", arrived, up_low, preferred_element_type=jnp.float32)
        return (gate_pre, up_pre)

    received = send_rows()
    gate_pre, up_pre = expert_front(received)
    activated = (gate_pre * jax.nn.sigmoid(gate_pre) * up_pre).astype(jnp.bfloat16)
    partial_value = jnp.einsum(
        "sech,ehd->secd", activated, down_low, preferred_element_type=jnp.float32
    ).astype(jnp.bfloat16)
    returned = lax.all_to_all(
        partial_value, "expert", split_axis=0, concat_axis=0, tiled=True
    ).reshape(experts * capacity, model_width)
    expert_rows = returned[slot_index].reshape(row_count, per_token, model_width)
    expert_part = jnp.einsum(
        "tk,tkd->td", gate_probs, expert_rows, preferred_element_type=jnp.float32
    )
    block_out = residual + lax.psum(expert_part.astype(jnp.bfloat16), "tensor").astype(jnp.float32)
    qkv_low, out_low, router_low, gain_one_f, gain_two_f, qk_gains = prepare(fetch_weights())
    grad_out = out_grad.astype(jnp.float32)
    grad_gate_part = jnp.einsum(
        "td,tkd->tk", grad_out, expert_rows, preferred_element_type=jnp.float32
    )
    slot_grads = (
        (gate_probs[:, :, None] * grad_out[:, None, :])
        .astype(jnp.bfloat16)
        .reshape(row_count * per_token, model_width)
    )
    grad_buffer = jnp.where(present, slot_grads[assigned], jnp.zeros((), jnp.bfloat16)).reshape(
        buffer_shape
    )
    grad_received = lax.all_to_all(grad_buffer, "expert", split_axis=0, concat_axis=0, tiled=True)
    received = send_rows()
    gate_pre, up_pre = expert_front(received)
    sigmoid_gate = jax.nn.sigmoid(gate_pre)
    swish_gate = gate_pre * sigmoid_gate
    activated = (swish_gate * up_pre).astype(jnp.bfloat16)
    grad_act = jnp.einsum(
        "secd,ehd->sech", grad_received, down_low, preferred_element_type=jnp.float32
    )
    grad_down = jnp.einsum(
        "sech,secd->ehd", activated, grad_received, preferred_element_type=jnp.float32
    )
    grad_gate_pre = (
        grad_act * up_pre * sigmoid_gate * (1.0 + gate_pre * (1.0 - sigmoid_gate))
    ).astype(jnp.bfloat16)
    grad_up_pre = (grad_act * swish_gate).astype(jnp.bfloat16)
    grad_gate_w = jnp.einsum(
        "secd,sech->edh", received, grad_gate_pre, preferred_element_type=jnp.float32
    )
    grad_up_w = jnp.einsum(
        "secd,sech->edh", received, grad_up_pre, preferred_element_type=jnp.float32
    )
    grad_rows = (
        jnp.einsum("sech,edh->secd", grad_gate_pre, gate_low, preferred_element_type=jnp.float32)
        + jnp.einsum("sech,edh->secd", grad_up_pre, up_low, preferred_element_type=jnp.float32)
    ).astype(jnp.bfloat16)
    grad_back = lax.all_to_all(
        grad_rows, "expert", split_axis=0, concat_axis=0, tiled=True
    ).reshape(experts * capacity, model_width)
    grad_hidden_part = jnp.sum(
        grad_back[slot_index].reshape(row_count, per_token, model_width), axis=1, dtype=jnp.float32
    )
    grad_hidden_sum, grad_gates = (
        lax.psum(grad_hidden_part.astype(jnp.bfloat16), "tensor").astype(jnp.float32),
        lax.psum(grad_gate_part.astype(jnp.bfloat16), "tensor").astype(jnp.float32),
    )
    grad_probs = jnp.sum(jnp.where(chosen, grad_gates[:, :, None], 0.0), axis=1)
    grad_logits = (
        router_probs * (grad_probs - jnp.sum(router_probs * grad_probs, axis=-1, keepdims=True))
    ).astype(jnp.bfloat16)
    grad_hidden_two = grad_hidden_sum + jnp.dot(
        grad_logits, router_low.T, preferred_element_type=jnp.float32
    )
    grad_router = jnp.dot(hidden_two.T, grad_logits, preferred_element_type=jnp.float32)
    grad_gain_two = jnp.sum(grad_hidden_two * normed_two, axis=0)
    scaled_two = grad_hidden_two * gain_two_f
    grad_residual = (
        grad_out
        + scale_two * scaled_two
        - residual
        * (scale_two * scale_two * scale_two)
        * jnp.mean(scaled_two * residual, axis=-1, keepdims=True)
    )
    grad_attn = grad_residual.astype(jnp.bfloat16)
    grad_out_w = jnp.dot(attended.T, grad_attn, preferred_element_type=jnp.float32)
    grad_attended = (
        jnp.dot(grad_attn, out_low.T, preferred_element_type=jnp.float32)
        .astype(jnp.bfloat16)
        .reshape(row_count, heads_here, HEAD)
    )
    attn_weights = jnp.where(allowed[None], jnp.exp(score_block() - log_total), 0.0)
    grad_weights = jnp.einsum(
        "qhd,khd->hqk", grad_attended, context[1], preferred_element_type=jnp.float32
    )
    inner_sum = jnp.sum(attn_weights * grad_weights, axis=-1, keepdims=True)
    grad_scores = (attn_weights * (grad_weights - inner_sum) * score_scale).astype(jnp.bfloat16)
    grad_query = jnp.einsum(
        "hqk,khd->qhd", grad_scores, context[0], preferred_element_type=jnp.float32
    )
    grad_keys = jnp.einsum(
        "hqk,qhd->khd", grad_scores, query_low, preferred_element_type=jnp.float32
    )
    grad_values = jnp.einsum(
        "hqk,qhd->khd",
        attn_weights.astype(jnp.bfloat16),
        grad_attended,
        preferred_element_type=jnp.float32,
    )
    grad_pair = jnp.stack([grad_keys, grad_values]).reshape(
        2, hop_count + 1, row_count, heads_here, HEAD
    )
    own_grad = grad_pair[:, hop_count]
    for steps_back in range(1, hop_count + 1):
        own_grad = own_grad + from_behind(
            grad_pair[:, hop_count - steps_back].astype(jnp.bfloat16), "expert", -steps_back
        ).astype(jnp.float32)
    grad_query_norm = rotate(grad_query, cosine_table, -sine_table).reshape(row_count, local_width)
    grad_key_norm = rotate(own_grad[0], cosine_table, -sine_table).reshape(row_count, local_width)
    grad_gain_query = jnp.sum(grad_query_norm * normed_query, axis=0)
    grad_gain_key = jnp.sum(grad_key_norm * normed_key, axis=0)
    scaled_query = grad_query_norm * qk_gains[0]
    scaled_key = grad_key_norm * qk_gains[1]
    query_inner, key_inner = lax.psum(
        (jnp.sum(scaled_query * query_raw, axis=-1), jnp.sum(scaled_key * key_raw, axis=-1)),
        "tensor",
    )
    grad_query_raw = (
        query_scale * scaled_query
        - query_raw * (query_scale * query_scale * query_scale) * query_inner[:, None] / model_width
    ).astype(jnp.bfloat16)
    grad_key_raw = (
        key_scale * scaled_key
        - key_raw * (key_scale * key_scale * key_scale) * key_inner[:, None] / model_width
    ).astype(jnp.bfloat16)
    grad_value_raw = own_grad[1].reshape(row_count, local_width).astype(jnp.bfloat16)
    grad_proj = jnp.stack([grad_query_raw, grad_key_raw, grad_value_raw])
    grad_qkv = jnp.einsum("td,jte->jde", hidden_one, grad_proj, preferred_element_type=jnp.float32)
    grad_hidden_one = lax.psum(
        jnp.einsum("jte,jde->td", grad_proj, qkv_low, preferred_element_type=jnp.float32).astype(
            jnp.bfloat16
        ),
        "tensor",
    ).astype(jnp.float32)
    grad_gain_one = jnp.sum(grad_hidden_one * tokens_f * scale_one, axis=0)
    scaled_one = grad_hidden_one * gain_one_f
    grad_tokens = (
        grad_residual
        + scale_one * scaled_one
        - tokens_f
        * (scale_one * scale_one * scale_one)
        * jnp.mean(scaled_one * tokens_f, axis=-1, keepdims=True)
    )
    grad_qk = jnp.stack([grad_gain_query, grad_gain_key]).reshape(2, heads_here, HEAD)
    reduced = (
        lax.psum_scatter(
            grad_qkv.astype(jnp.bfloat16), "expert", scatter_dimension=1, tiled=True
        ).astype(jnp.float32),
        lax.psum_scatter(
            grad_out_w.astype(jnp.bfloat16), "expert", scatter_dimension=1, tiled=True
        ).astype(jnp.float32),
        lax.psum_scatter(
            grad_router.astype(jnp.bfloat16), "expert", scatter_dimension=0, tiled=True
        ).astype(jnp.float32),
        lax.psum_scatter(
            grad_gain_one.astype(jnp.bfloat16), "expert", scatter_dimension=0, tiled=True
        ).astype(jnp.float32),
        lax.psum_scatter(
            grad_gain_two.astype(jnp.bfloat16), "expert", scatter_dimension=0, tiled=True
        ).astype(jnp.float32),
        lax.psum_scatter(
            grad_qk.astype(jnp.bfloat16), "expert", scatter_dimension=2, tiled=True
        ).astype(jnp.float32),
    )
    return (
        block_out.astype(jnp.bfloat16),
        grad_tokens.astype(jnp.bfloat16),
        reduced[0],
        reduced[1],
        reduced[3],
        reduced[4],
        reduced[5],
        reduced[2],
        grad_gate_w,
        grad_up_w,
        grad_down,
    )


MESH_ID = pl.DeviceIdType.MESH
HBM = pl.BlockSpec(memory_space=pl.ANY)
VMEM = pl.BlockSpec(memory_space=pltpu.VMEM)
NZ, NY, NX, NC = 4, 2, 2, 2
GROUPS = NZ * NY


def place():
    e = lax.axis_index("expert")
    t = lax.axis_index("tensor")
    return lax.div(e, NY), lax.rem(e, NY), lax.div(t, NC), lax.rem(t, NC)


def device(z, y, x, c):
    return (z * NY + y, x * NC + c)


def run_if(condition, body):
    if condition is None:
        body()
    else:
        pl.when(condition)(body)


def greet(partners):
    barrier = pltpu.get_barrier_semaphore()
    for target, condition in partners:
        run_if(
            condition,
            lambda target=target: pl.semaphore_signal(
                barrier, inc=1, device_id=target, device_id_type=MESH_ID
            ),
        )
    count = sum(1 for _, condition in partners if condition is None)
    for _, condition in partners:
        if condition is not None:
            count = count + condition.astype(jnp.int32)
    pl.semaphore_wait(barrier, count)


def remote(source, target_ref, send_sem, recv_sem, target):
    return pltpu.make_async_remote_copy(
        src_ref=source,
        dst_ref=target_ref,
        send_sem=send_sem,
        recv_sem=recv_sem,
        device_id=target,
        device_id_type=MESH_ID,
    )


def block_rows(block, rows):
    return pl.ds(pl.multiple_of(block * rows, rows), rows)


class LineGather:
    def __init__(self, streams, sources, views, send_sem, recv_sem, y_first=()):
        self.z, self.y, self.x, self.c = place()
        self.streams, self.sources, self.views = streams, sources, views
        self.send_sem, self.recv_sem = send_sem, recv_sem
        self.y_first = y_first
        self.has_up, self.has_down = self.z < NZ - 1, self.z > 0
        self.pending = []

    def partners(self):
        z, y, x, c = self.z, self.y, self.x, self.c
        return [
            (device(z + 1, y, x, c), z < NZ - 1),
            (device(z - 1, y, x, c), z > 0),
            (device(z, 1 - y, x, c), None),
        ]

    def exists(self, rel):
        rel = rel % 7
        if rel == 0:
            return None
        return self.z >= rel if rel < 4 else self.z + (rel - 3) < NZ

    def block(self, rel):
        y = self.y if rel < 7 else 1 - self.y
        rel = rel % 7
        z = self.z if rel == 0 else (self.z - rel if rel < 4 else self.z + (rel - 3))
        return z * NY + y

    def send(self, stream, rel, way):
        z, y, x, c = self.z, self.y, self.x, self.c
        block = self.block(rel)
        there = self.views[stream](block)
        source = self.sources[stream] if rel == 0 else there
        near = rel % 7 == 0
        if way == 0:
            target, landing = device(z + 1, y, x, c), rel + 1
        elif way == 1:
            target, landing = device(z - 1, y, x, c), rel + (4 if near else 1)
        else:
            target, landing = device(z, 1 - y, x, c), 7 + rel
        return remote(
            source,
            there,
            self.send_sem.at[stream, rel, way],
            self.recv_sem.at[stream, landing],
            target,
        )

    def forwards(self, stream, rel):
        return rel < 7 or stream in self.y_first

    def start(self, stream, rel):
        if rel % 7 < 4:
            run = self.has_up
            run_if(run, lambda: self.send(stream, rel, 0).start())
            self.pending.append((stream, rel, 0, run))
        if rel % 7 == 0 or rel % 7 >= 4:
            run = self.has_down
            run_if(run, lambda: self.send(stream, rel, 1).start())
            self.pending.append((stream, rel, 1, run))
        if rel == 0 or stream not in self.y_first:
            self.send(stream, rel, 2).start()
            self.pending.append((stream, rel, 2, None))

    def arrive(self, stream, rel):
        there = self.views[stream](self.block(rel))
        remote(
            there,
            there,
            self.send_sem.at[stream, 0, 0],
            self.recv_sem.at[stream, rel],
            device(self.z, 1 - self.y, self.x, self.c),
        ).wait_recv()

    def order(self):
        return [7, 1, 4, 8, 11, 2, 5, 9, 12, 3, 6, 10, 13]

    def run(self, hook=None):
        for stream in self.streams:
            self.start(stream, 0)
        for rel in self.order():
            def step(rel=rel):
                marks = len(self.pending)
                for stream in self.streams:
                    self.arrive(stream, rel)
                    if rel < 7:
                        self.start(stream, rel)
                    if hook is not None:
                        hook(stream, rel)
                if rel < 7:
                    late = self.pending[marks:]
                    del self.pending[marks:]
                    self.finish_later(late, rel)
            run_if(self.exists(rel), step)

    def finish_later(self, late, rel):
        self.late = getattr(self, "late", []) + [(rel, late)]

    def finish(self):
        for stream, rel, way, run in self.pending:
            run_if(run, lambda s=stream, r=rel, w=way: self.send(s, r, w).wait_send())
        for rel, late in getattr(self, "late", []):
            def body(late=late):
                for stream, rel, way, run in late:
                    run_if(run, lambda s=stream, r=rel, w=way: self.send(s, r, w).wait_send())
            run_if(self.exists(rel), body)


def cost(microseconds):
    return pl.CostEstimate(flops=0, bytes_accessed=int(microseconds * 3.0e6), transcendentals=0)


def comm_params(collective_id, megabytes=56):
    return pltpu.CompilerParams(
        collective_id=collective_id,
        has_side_effects=True,
        vmem_limit_bytes=megabytes * 1024 * 1024,
    )


def weight_gather(qkv_low, out_low, smalls, collective_id):
    parts, rows, width = qkv_low.shape
    depth, columns = out_low.shape

    def kernel(qkv, out, small, qkv_all, out_all, small_all, send_sem, recv_sem, local_sem):
        views = [
            lambda b: qkv_all.at[:, block_rows(b, rows), :],
            lambda b: out_all.at[:, block_rows(b, columns)],
            lambda b: small_all.at[b],
        ]
        line = LineGather([2, 0, 1], [qkv, out, small], views, send_sem, recv_sem)
        greet(line.partners())
        own = line.block(0)
        keep = [
            pltpu.make_async_copy(source, view(own), local_sem.at[i])
            for i, (source, view) in enumerate(zip([qkv, out, small], views))
        ]
        for copy in keep:
            copy.start()
        line.run()
        line.finish()
        for copy in keep:
            copy.wait()

    return pl.pallas_call(
        kernel,
        out_shape=(
            jax.ShapeDtypeStruct((parts, rows * GROUPS, width), jnp.bfloat16),
            jax.ShapeDtypeStruct((depth, columns * GROUPS), jnp.bfloat16),
            jax.ShapeDtypeStruct((GROUPS,) + smalls.shape, jnp.float32),
        ),
        in_specs=[HBM] * 3,
        out_specs=(HBM, HBM, HBM),
        scratch_shapes=[
            pltpu.SemaphoreType.DMA((3, 14, 3)),
            pltpu.SemaphoreType.DMA((3, 14)),
            pltpu.SemaphoreType.DMA((3,)),
        ],
        compiler_params=comm_params(collective_id),
        cost_estimate=cost(100),
        name="weight_gather",
    )(qkv_low, out_low, smalls)


def token_gather(block, collective_id):
    rows, width = block.shape
    a_cols, c_cols = width * 3 // 16, width // 8

    def kernel(own_ref, all_ref, send_sem, recv_sem, x_send, x_recv, core_send, core_recv, local_sem):
        z, y, x, c = place()

        def a_at(xx, cc):
            return pl.ds(pl.multiple_of(xx * (2 * a_cols) + cc * a_cols, 128), a_cols)

        def c_at(cc):
            return pl.ds(pl.multiple_of(4 * a_cols + cc * c_cols, 128), c_cols)

        def view(b, columns):
            return all_ref.at[block_rows(b, rows), columns]

        sources = [own_ref.at[:, a_at(x, c)], own_ref.at[:, c_at(c)]]
        views = [lambda b: view(b, a_at(x, c)), lambda b: view(b, c_at(c))]
        line = LineGather([0, 1], sources, views, send_sem, recv_sem)
        across, twin = device(z, y, 1 - x, c), device(z, y, x, 1 - c)
        greet(line.partners() + [(across, None), (twin, None)])
        keep = pltpu.make_async_copy(own_ref, all_ref.at[block_rows(line.block(0), rows), :], local_sem)
        keep.start()

        def to_twin(rel, stream, landing=False):
            b = line.block(rel)
            columns = [a_at(x, c), c_at(c), a_at(1 - x, c)][stream]
            other = [a_at(x, 1 - c), c_at(1 - c), a_at(1 - x, 1 - c)][stream]
            piece = view(b, other if landing else columns)
            return remote(piece, piece, core_send.at[rel, stream], core_recv.at[rel, stream], twin)

        def to_across(rel, landing=False):
            b = line.block(rel)
            piece = view(b, a_at(1 - x if landing else x, c))
            return remote(piece, piece, x_send.at[rel], x_recv.at[rel], across)

        def hook(stream, rel):
            if stream == 0:
                to_across(rel).start()
            to_twin(rel, stream).start()

        line.run(hook)
        for rel in line.order():
            def relay(rel=rel):
                to_across(rel, True).wait_recv()
                to_twin(rel, 2).start()
            run_if(line.exists(rel), relay)
        for rel in line.order():
            def end(rel=rel):
                to_across(rel).wait_send()
                for stream in range(3):
                    to_twin(rel, stream, True).wait_recv()
                    to_twin(rel, stream).wait_send()
            run_if(line.exists(rel), end)
        line.finish()
        keep.wait()

    return pl.pallas_call(
        kernel,
        out_shape=jax.ShapeDtypeStruct((rows * GROUPS, width), block.dtype),
        in_specs=[HBM],
        out_specs=HBM,
        scratch_shapes=[
            pltpu.SemaphoreType.DMA((2, 14, 3)),
            pltpu.SemaphoreType.DMA((2, 14)),
            pltpu.SemaphoreType.DMA((14,)),
            pltpu.SemaphoreType.DMA((14,)),
            pltpu.SemaphoreType.DMA((14, 3)),
            pltpu.SemaphoreType.DMA((14, 3)),
            pltpu.SemaphoreType.DMA,
        ],
        compiler_params=comm_params(collective_id),
        cost_estimate=cost(45),
        name="token_gather",
    )(block)


def add_into(rows, step, store):
    def body(i, carry):
        store(pl.ds(pl.multiple_of(i * step, step), step))
        return carry

    lax.fori_loop(0, rows // step, body, 0)


def group_stages(part_ref, out_ref, core_buf, x_buf, send_sem, recv_sem):
    rows, width = part_ref.shape
    half, quarter = width // 2, width // 4
    z, y, x, c = place()
    across, twin = device(z, y, 1 - x, c), device(z, y, x, 1 - c)

    def half_of(cc):
        return pl.ds(pl.multiple_of(cc * half, half), half)

    def quarter_of(xx, cc):
        return pl.ds(pl.multiple_of(cc * half + xx * quarter, quarter), quarter)

    own, from_x = out_ref.at[:, quarter_of(x, c)], out_ref.at[:, quarter_of(1 - x, c)]
    to_x = core_buf.at[:, pl.ds(pl.multiple_of((1 - x) * quarter, quarter), quarter)]
    sources = [part_ref.at[:, half_of(1 - c)], to_x, own, own, from_x]
    landings = [core_buf, x_buf, own, own, from_x]
    targets = [twin, across, across, twin, twin]

    def copy(k):
        return remote(sources[k], landings[k], send_sem.at[k], recv_sem.at[k], targets[k])

    def arrive(k, landing):
        remote(landing, landing, send_sem.at[k], recv_sem.at[k], targets[k]).wait_recv()

    def begin():
        copy(0).start()

    def core_step():
        copy(0).wait_recv()
        add_to(core_buf, core_buf, part_ref.at[:, half_of(c)], 32)
        copy(1).start()

    def x_step():
        copy(1).wait_recv()
        add_to(own, x_buf, core_buf.at[:, pl.ds(pl.multiple_of(x * quarter, quarter), quarter)], 32)
        copy(2).start()
        copy(3).start()

    def spread():
        arrive(2, from_x)
        copy(4).start()

    def end():
        arrive(3, out_ref.at[:, quarter_of(x, 1 - c)])
        arrive(4, out_ref.at[:, quarter_of(1 - x, 1 - c)])
        for k in range(5):
            copy(k).wait_send()

    return [begin, core_step, x_step, spread, end]


def group_sum(part_ref, out_ref, core_buf, x_buf, send_sem, recv_sem, meanwhile=None):
    stages = group_stages(part_ref, out_ref, core_buf, x_buf, send_sem, recv_sem)
    stages[0]()
    if meanwhile is not None:
        meanwhile()
    for stage in stages[1:]:
        stage()


def tensor_sum(part, collective_id):
    rows, width = part.shape

    def kernel(part_ref, out_ref, core_buf, x_buf, send_sem, recv_sem):
        z, y, x, c = place()
        greet([(device(z, y, 1 - x, c), None), (device(z, y, x, 1 - c), None)])
        group_sum(part_ref, out_ref, core_buf, x_buf, send_sem, recv_sem)

    return pl.pallas_call(
        kernel,
        out_shape=jax.ShapeDtypeStruct((rows, width), jnp.bfloat16),
        in_specs=[VMEM],
        out_specs=VMEM,
        scratch_shapes=[
            pltpu.VMEM((rows, width // 2), jnp.bfloat16),
            pltpu.VMEM((rows, width // 4), jnp.bfloat16),
            pltpu.SemaphoreType.DMA((5,)),
            pltpu.SemaphoreType.DMA((5,)),
        ],
        compiler_params=comm_params(collective_id, 16),
        cost_estimate=cost(17),
        name="tensor_sum",
    )(part)


Z_ORDER = (3, 0, 2, 1)


def accumulate(into, addend, step=64):
    rows = into.shape[0]
    step = min(step, rows)

    def body(i, carry):
        r = pl.ds(pl.multiple_of(i * step, step), step)
        total = into[r, :].astype(jnp.float32) + addend[r, :].astype(jnp.float32)
        into[r, :] = total.astype(into.dtype)
        return carry

    lax.fori_loop(0, rows // step, body, 0)


class LineReduce:
    def __init__(self, streams, own, y_buf, lo_buf, hi_buf, send_sem, recv_sem):
        self.z, self.y, self.x, self.c = place()
        self.streams = streams
        self.own, self.y_buf, self.lo_buf, self.hi_buf = own, y_buf, lo_buf, hi_buf
        self.send_sem, self.recv_sem = send_sem, recv_sem

    def partners(self):
        z, y, x, c = self.z, self.y, self.x, self.c
        return [
            (device(z + 1, y, x, c), z < NZ - 1),
            (device(z - 1, y, x, c), z > 0),
            (device(z, 1 - y, x, c), None),
        ]

    def copy(self, s, zz, way):
        z, y, x, c = self.z, self.y, self.x, self.c
        if way == 0:
            source, landing, target = self.own(s, zz, 1 - y), self.y_buf, device(z, 1 - y, x, c)
        elif way == 1:
            source, landing, target = self.y_buf(s, zz), self.lo_buf, device(z + 1, y, x, c)
        else:
            source, landing, target = self.y_buf(s, zz), self.hi_buf, device(z - 1, y, x, c)
        return remote(
            source, landing(s, zz), self.send_sem.at[s, zz, way], self.recv_sem.at[s, zz, way], target
        )

    def to_y(self, s, zz):
        self.copy(s, zz, 0).start()

    def take(self, s, zz, way):
        self.copy(s, zz, way).wait_recv()
        accumulate(self.y_buf(s, zz), (self.lo_buf if way == 1 else self.hi_buf)(s, zz))

    def along_z(self, s, zz):
        z = self.z
        self.copy(s, zz, 0).wait_recv()
        accumulate(self.y_buf(s, zz), self.own(s, zz, self.y))

        def upward():
            run_if(z > 0, lambda: self.take(s, zz, 1))
            self.copy(s, zz, 1).start()

        def downward():
            run_if(z < NZ - 1, lambda: self.take(s, zz, 2))
            self.copy(s, zz, 2).start()

        run_if(z < zz, upward)
        run_if(z > zz, downward)

    def home(self, done):
        for zz in range(NZ):
            def land(zz=zz):
                for s in self.streams:
                    if zz > 0:
                        self.take(s, zz, 1)
                    if zz < NZ - 1:
                        self.take(s, zz, 2)
                    done(s, self.y_buf(s, zz))
            run_if(self.z == zz, land)

    def finish(self):
        for zz in range(NZ):
            for s in self.streams:
                self.copy(s, zz, 0).wait_send()
                run_if(self.z < zz, lambda s=s, zz=zz: self.copy(s, zz, 1).wait_send())
                run_if(self.z > zz, lambda s=s, zz=zz: self.copy(s, zz, 2).wait_send())


def weight_reduce(qkv, out, smalls, collective_id):
    parts, depth, width = qkv.shape
    rows = depth // GROUPS
    out_rows, columns = out.shape[0], out.shape[1] // GROUPS

    def kernel(qkv_ref, out_ref, small_ref, qkv_sum, out_sum, small_sum,
               qkv_buf, out_buf, small_buf, send_sem, recv_sem):
        def own(s, zz, yy):
            b = zz * NY + yy
            if s < parts:
                return qkv_ref.at[s, block_rows(b, rows), :]
            if s == parts:
                return out_ref.at[:, block_rows(b, columns)]
            return small_ref.at[b]

        def slot(kind):
            def view(s, zz):
                if s < parts:
                    return qkv_buf.at[kind, zz, s]
                if s == parts:
                    return out_buf.at[kind, zz]
                return small_buf.at[kind, zz]
            return view

        streams = list(range(parts + 2))
        line = LineReduce(streams, own, slot(0), slot(1), slot(2), send_sem, recv_sem)
        greet(line.partners())
        work = [(s, zz) for s in [parts + 1, parts] + list(range(parts)) for zz in Z_ORDER]
        for s, zz in work:
            line.to_y(s, zz)
        for s, zz in work:
            line.along_z(s, zz)

        def done(s, total):
            target = qkv_sum.at[s] if s < parts else (out_sum if s == parts else small_sum)
            step = min(64, target.shape[0])

            def body(i, carry):
                r = pl.ds(pl.multiple_of(i * step, step), step)
                target[r, :] = total[r, :].astype(jnp.float32)
                return carry

            lax.fori_loop(0, target.shape[0] // step, body, 0)

        line.home(done)
        line.finish()

    return pl.pallas_call(
        kernel,
        out_shape=(
            jax.ShapeDtypeStruct((parts, rows, width), jnp.float32),
            jax.ShapeDtypeStruct((out_rows, columns), jnp.float32),
            jax.ShapeDtypeStruct(smalls.shape[1:], jnp.float32),
        ),
        in_specs=[VMEM] * 3,
        out_specs=(VMEM,) * 3,
        scratch_shapes=[
            pltpu.VMEM((3, NZ, parts, rows, width), jnp.bfloat16),
            pltpu.VMEM((3, NZ, out_rows, columns), jnp.bfloat16),
            pltpu.VMEM((3, NZ) + smalls.shape[1:], jnp.float32),
            pltpu.SemaphoreType.DMA((parts + 2, NZ, 3)),
            pltpu.SemaphoreType.DMA((parts + 2, NZ, 3)),
        ],
        compiler_params=comm_params(collective_id),
        cost_estimate=cost(120),
        name="weight_reduce",
    )(qkv, out, smalls)


def token_reduce(part, collective_id, pairs=None):
    tokens, width = part.shape
    rows = tokens // GROUPS
    half, quarter = width // 2, width // 4

    def kernel(part_ref, out_ref, core_buf, x_buf, y_buf, lo_buf, hi_buf,
               core_send, core_recv, x_send, x_recv, send_sem, recv_sem):
        z, y, x, c = place()
        across, twin = device(z, y, 1 - x, c), device(z, y, x, 1 - c)

        line = LineReduce(
            [0], lambda s, zz, yy: x_buf.at[zz * NY + yy], lambda s, zz: y_buf.at[zz],
            lambda s, zz: lo_buf.at[zz], lambda s, zz: hi_buf.at[zz], send_sem, recv_sem,
        )
        greet(line.partners() + [(across, None), (twin, None)])
        order = [(zz, flip) for zz in Z_ORDER for flip in (1, 0)]

        def number(zz, flip):
            return zz * NY + (1 - y if flip else y)

        def to_twin(zz, flip):
            b = number(zz, flip)
            return remote(
                part_ref.at[block_rows(b, rows), pl.ds(pl.multiple_of((1 - c) * half, half), half)],
                core_buf.at[b], core_send.at[zz, flip], core_recv.at[zz, flip], twin,
            )

        def to_across(zz, flip):
            b = number(zz, flip)
            return remote(
                core_buf.at[b, :, pl.ds(pl.multiple_of((1 - x) * quarter, quarter), quarter)],
                x_buf.at[b], x_send.at[zz, flip], x_recv.at[zz, flip], across,
            )

        def add_core(zz, flip):
            b = number(zz, flip)

            def store(r):
                at = pl.ds(pl.multiple_of(b * rows + r.start, 16), r.size)
                core_buf[b, r, :] = (
                    core_buf[b, r, :].astype(jnp.float32)
                    + part_ref[at, pl.ds(pl.multiple_of(c * half, half), half)].astype(jnp.float32)
                ).astype(jnp.bfloat16)

            add_into(rows, 32, store)

        def add_across(zz, flip):
            b = number(zz, flip)

            def store(r):
                x_buf[b, r, :] = (
                    x_buf[b, r, :].astype(jnp.float32)
                    + core_buf[b, r, pl.ds(pl.multiple_of(x * quarter, quarter), quarter)].astype(jnp.float32)
                ).astype(jnp.bfloat16)

            add_into(rows, 64, store)

        def stage_twin(i):
            to_twin(*order[i]).wait_recv()
            add_core(*order[i])
            to_across(*order[i]).start()

        def stage_across(i):
            zz, flip = order[i]
            to_across(zz, flip).wait_recv()
            add_across(zz, flip)
            if flip:
                line.to_y(0, zz)

        def stage_y(zz):
            line.along_z(0, zz)

        for zz, flip in order:
            to_twin(zz, flip).start()
        count = len(order)
        for i in range(count + 4):
            if i < count:
                stage_twin(i)
            if 0 <= i - 1 < count:
                stage_across(i - 1)
            if i >= 3 and (i - 3) % 2 == 0 and (i - 3) // 2 < NZ:
                stage_y(Z_ORDER[(i - 3) // 2])

        def done(s, total):
            def store(r):
                out_ref[r, :] = total[r, :]

            add_into(rows, 64, store)

        line.home(done)
        for zz, flip in order:
            to_twin(zz, flip).wait_send()
            to_across(zz, flip).wait_send()
        line.finish()

    return pl.pallas_call(
        kernel,
        out_shape=jax.ShapeDtypeStruct((rows, quarter), jnp.bfloat16),
        in_specs=[VMEM],
        out_specs=VMEM,
        scratch_shapes=[
            pltpu.VMEM((GROUPS, rows, half), jnp.bfloat16),
            pltpu.VMEM((GROUPS, rows, quarter), jnp.bfloat16),
            pltpu.VMEM((NZ, rows, quarter), jnp.bfloat16),
            pltpu.VMEM((NZ, rows, quarter), jnp.bfloat16),
            pltpu.VMEM((NZ, rows, quarter), jnp.bfloat16),
            pltpu.SemaphoreType.DMA((NZ, 2)),
            pltpu.SemaphoreType.DMA((NZ, 2)),
            pltpu.SemaphoreType.DMA((NZ, 2)),
            pltpu.SemaphoreType.DMA((NZ, 2)),
            pltpu.SemaphoreType.DMA((1, NZ, 3)),
            pltpu.SemaphoreType.DMA((1, NZ, 3)),
        ],
        compiler_params=comm_params(collective_id),
        cost_estimate=cost(60),
        name="token_reduce",
    )(part)


def gate_exchange(part, collective_id):
    groups = part.shape[0]
    tensors = NX * NC

    def kernel(part_ref, out_ref, landing, total, send_t, recv_t, send_e, recv_e):
        e = lax.axis_index("expert")
        t = lax.axis_index("tensor")
        mates = [(e, lax.rem(t + k, tensors)) for k in range(1, tensors)]
        peers = [(lax.rem(e + k, groups), t) for k in range(1, groups)]
        greet([(target, None) for target in mates + peers])
        near = [
            remote(part_ref, landing.at[k], send_t.at[k], recv_t.at[k], mates[k])
            for k in range(tensors - 1)
        ]
        for copy in near:
            copy.start()
        for copy in near:
            copy.wait_recv()
        value = part_ref[...]
        for k in range(tensors - 1):
            value = value + landing[k]
        total[...] = value
        far = [
            remote(
                total.at[lax.rem(e + k, groups)], out_ref.at[e], send_e.at[k - 1], recv_e.at[k - 1],
                peers[k - 1],
            )
            for k in range(1, groups)
        ]
        for copy in far:
            copy.start()
        out_ref[e] = total[e]
        for k in range(1, groups):
            source = out_ref.at[lax.rem(e + groups - k, groups)]
            remote(source, source, send_e.at[k - 1], recv_e.at[k - 1], peers[k - 1]).wait_recv()
        for copy in near + far:
            copy.wait_send()

    return pl.pallas_call(
        kernel,
        out_shape=jax.ShapeDtypeStruct(part.shape, jnp.float32),
        in_specs=[VMEM],
        out_specs=VMEM,
        scratch_shapes=[
            pltpu.VMEM((tensors - 1,) + part.shape, jnp.float32),
            pltpu.VMEM(part.shape, jnp.float32),
            pltpu.SemaphoreType.DMA((tensors - 1,)),
            pltpu.SemaphoreType.DMA((tensors - 1,)),
            pltpu.SemaphoreType.DMA((groups - 1,)),
            pltpu.SemaphoreType.DMA((groups - 1,)),
        ],
        compiler_params=comm_params(collective_id, 16),
        cost_estimate=cost(10),
        name="gate_exchange",
    )(part)


def dot(a, b, dims):
    return lax.dot_general(a, b, ((dims[:1], dims[1:]), ((), ())), preferred_element_type=jnp.float32)


def add_to(target, first, second, step=64):
    rows = target.shape[0]

    def body(i, carry):
        r = pl.ds(pl.multiple_of(i * step, step), step)
        total = first[r, :].astype(jnp.float32) + second[r, :].astype(jnp.float32)
        target[r, :] = total.astype(target.dtype)
        return carry

    lax.fori_loop(0, rows // step, body, 0)


def expert_layer(
    hidden_two, grad_out_all, gate_up, down, router_t, chosen_all, residual, collective_id
):
    rows, width = hidden_two.shape
    tokens = rows * GROUPS
    units = down.shape[0]
    local = 2
    hidden = units // local
    experts = router_t.shape[0]
    half, part, piece = width // 2, width // 4, width // 8
    tensors = NX * NC
    steps = GROUPS + 4
    a_cols, c_cols = width * 3 // 16, width // 8
    low = jnp.bfloat16
    wide = width // 4

    def kernel(
        own_in, dy_in, gu_ref, down_ref, router_ref, chosen_ref, x1_in,
        block_out, dh_out, gates_out, gate_w, up_w, down_w,
        h, dy, gated, dgu, dx, y_part, yc_buf, yx_buf, yy_buf, ylo_buf, yhi_buf, x1, gu_stage, d_stage,
        core_buf, px_buf, py_buf, qy_buf, qx_buf, z_sum, lo_buf, hi_buf, gate_part, gate_land,
        in_sem, own_sem, line_s, line_r, hx_s, hx_r, hc_s, hc_r, x1_sem, yc_s, yc_r, yx_s, yx_r, yy_s, yy_r, yz_s, yz_r, gu_sem, d_sem, core_s, core_r, px_s, px_r, py_s, py_r, qy_s, qy_r, qx_s, qx_r,
        z_s, z_r, near_s, near_r, far_s, far_r, end_s, end_r,
    ):
        z, y, x, c = place()
        e, t = lax.axis_index("expert"), lax.axis_index("tensor")
        across, twin, beside = device(z, y, 1 - x, c), device(z, y, x, 1 - c), device(z, 1 - y, x, c)
        mates = [(e, lax.rem(t + k, tensors)) for k in range(1, tensors)]
        peers = [(lax.rem(e + k, GROUPS), t) for k in range(1, GROUPS)]
        greet([(target, None) for target in mates + peers])

        def pick(values, index):
            result = values[-1]
            for k in range(len(values) - 1):
                result = jnp.where(index == k, values[k], result)
            return result

        def zz_of(j):
            return pick([z, pick([1, 0, 3, 2], z), pick([3, 3, 0, 0], z), pick([2, 2, 1, 1], z)], j)

        def is_own(i):
            return (i == 0) | ((i >= 2) & (lax.rem(i, 2) == 1))

        def block_of(i):
            return zz_of(lax.div(i, 2)) * NY + jnp.where(is_own(i), y, 1 - y)

        def flip_block(j):
            return zz_of(j) * NY + 1 - y

        def own_block(j):
            return zz_of(j) * NY + y

        def a_at(xx, cc):
            return pl.ds(pl.multiple_of(xx * (2 * a_cols) + cc * a_cols, 128), a_cols)

        def c_at(cc):
            return pl.ds(pl.multiple_of(4 * a_cols + cc * c_cols, 128), c_cols)

        def h_view(b, columns):
            return h.at[block_rows(b, rows), columns]

        line = LineGather(
            [0, 1], [own_in.at[:, a_at(x, c)], own_in.at[:, c_at(c)]],
            [lambda b: h_view(b, a_at(x, c)), lambda b: h_view(b, c_at(c))], line_s, line_r,
        )

        def h_twin(b, stream, landing=False):
            cc = 1 - c if landing else c
            piece = h_view(b, [a_at(x, cc), c_at(cc), a_at(1 - x, cc)][stream])
            return remote(piece, piece, hc_s.at[b, stream], hc_r.at[b, stream], twin)

        def h_across(b, landing=False):
            piece = h_view(b, a_at(1 - x if landing else x, c))
            return remote(piece, piece, hx_s.at[b], hx_r.at[b], across)

        def gather_event(rel):
            def body():
                b = line.block(rel)
                marks = len(line.pending)
                for stream in (0, 1):
                    line.arrive(stream, rel)
                    if rel < 7:
                        line.start(stream, rel)
                    if stream == 0:
                        h_across(b).start()
                    h_twin(b, stream).start()
                late = line.pending[marks:]
                del line.pending[marks:]
                line.finish_later(late, rel)
            run_if(line.exists(rel), body)

        def relay(i):
            b = block_of(i)
            h_across(b, True).wait_recv()
            h_twin(b, 2).start()

        for stream in (0, 1):
            line.start(stream, 0)
        keep = pltpu.make_async_copy(own_in, h.at[block_rows(z * NY + y, rows), :], own_sem)
        keep.start()

        def load(i):
            r = block_rows(block_of(i), rows)
            return pltpu.make_async_copy(dy_in.at[r, :], dy.at[r, :], in_sem.at[i])

        def start_load(i, carry):
            load(i).start()
            return carry

        lax.fori_loop(0, GROUPS, start_load, 0)
        x1_copy = pltpu.make_async_copy(
            x1_in.at[:, pl.ds(pl.multiple_of(c * half + x * part, part), part)], x1, x1_sem
        )
        x1_copy.start()

        def to_twin(i):
            b = block_of(i)
            return remote(
                dx.at[lax.rem(i, 2), :, pl.ds(pl.multiple_of((1 - c) * half, half), half)],
                core_buf.at[b], core_s.at[i], core_r.at[i], twin,
            )

        def p_across(i):
            b = block_of(i)
            return remote(
                core_buf.at[b, :, pl.ds(pl.multiple_of((1 - x) * piece, piece), piece)],
                px_buf.at[b], px_s.at[i], px_r.at[i], across,
            )

        def p_beside(j):
            return remote(px_buf.at[flip_block(j)], py_buf.at[j], py_s.at[j], py_r.at[j], beside)

        def q_beside(j):
            return remote(
                core_buf.at[flip_block(j), :, pl.ds(part, part)], qy_buf.at[j], qy_s.at[j], qy_r.at[j], beside
            )

        def q_across(j):
            return remote(
                qy_buf.at[j, :, pl.ds(pl.multiple_of((1 - x) * piece, piece), piece)],
                qx_buf.at[j], qx_s.at[j], qx_r.at[j], across,
            )

        def up(j, s):
            return remote(z_sum.at[s, j], lo_buf.at[s, j], z_s.at[0, s, j], z_r.at[0, s, j], device(z + 1, y, x, c))

        def down_z(j, s):
            return remote(z_sum.at[s, j], hi_buf.at[s, j], z_s.at[1, s, j], z_r.at[1, s, j], device(z - 1, y, x, c))

        def take_twin(i):
            to_twin(i).wait_recv()
            b = block_of(i)
            mine = core_buf.at[b]
            add_to(mine, mine, dx.at[lax.rem(i, 2), :, pl.ds(pl.multiple_of(c * half, half), half)], 32)
            p_across(i).start()
            pl.when(jnp.logical_not(is_own(i)))(lambda: q_beside(lax.div(i, 2)).start())

        def take_p_across(i):
            p_across(i).wait_recv()
            b = block_of(i)
            add_to(
                px_buf.at[b], px_buf.at[b],
                core_buf.at[b, :, pl.ds(pl.multiple_of(x * piece, piece), piece)],
            )

        def take_q_beside(j):
            q_beside(j).wait_recv()
            add_to(qy_buf.at[j], qy_buf.at[j], core_buf.at[own_block(j), :, pl.ds(part, part)])
            q_across(j).start()

        def take_q_across(j):
            q_across(j).wait_recv()
            add_to(
                z_sum.at[1, zz_of(j)], qx_buf.at[j], qy_buf.at[j, :, pl.ds(pl.multiple_of(x * piece, piece), piece)]
            )

        def take_p_beside(j):
            p_beside(j).wait_recv()
            add_to(z_sum.at[0, zz_of(j)], py_buf.at[j], px_buf.at[own_block(j)])

        def hop(j, k):
            zz = zz_of(j)

            def upward():
                for s in range(2):
                    if k > 0:
                        up(zz, s).wait_recv()
                        add_to(z_sum.at[s, zz], z_sum.at[s, zz], lo_buf.at[s, zz])
                    up(zz, s).start()

            def downward():
                for s in range(2):
                    if k > 0:
                        down_z(zz, s).wait_recv()
                        add_to(z_sum.at[s, zz], z_sum.at[s, zz], hi_buf.at[s, zz])
                    down_z(zz, s).start()

            pl.when((z < zz) & (z == k))(upward)
            pl.when((z > zz) & (NZ - 1 - z == k))(downward)

        def y_twin(i):
            return remote(
                y_part.at[lax.rem(i, 2), :, pl.ds(pl.multiple_of((1 - c) * half, half), half)],
                yc_buf.at[block_of(i)], yc_s.at[i], yc_r.at[i], twin,
            )

        def y_across(i):
            b = block_of(i)
            return remote(
                yc_buf.at[b, :, pl.ds(pl.multiple_of((1 - x) * part, part), part)],
                yx_buf.at[b], yx_s.at[i], yx_r.at[i], across,
            )

        def y_beside(j):
            return remote(yx_buf.at[flip_block(j)], yy_buf.at[zz_of(j)], yy_s.at[j], yy_r.at[j], beside)

        def y_up(j):
            return remote(yy_buf.at[j], ylo_buf.at[j], yz_s.at[0, j], yz_r.at[0, j], device(z + 1, y, x, c))

        def y_down(j):
            return remote(yy_buf.at[j], yhi_buf.at[j], yz_s.at[1, j], yz_r.at[1, j], device(z - 1, y, x, c))

        def take_y_twin(i):
            y_twin(i).wait_recv()
            mine = yc_buf.at[block_of(i)]
            add_to(mine, mine, y_part.at[lax.rem(i, 2), :, pl.ds(pl.multiple_of(c * half, half), half)], 32)
            y_across(i).start()

        def take_y_across(i):
            y_across(i).wait_recv()
            b = block_of(i)
            mine = yx_buf.at[b]
            add_to(mine, mine, yc_buf.at[b, :, pl.ds(pl.multiple_of(x * part, part), part)])
            pl.when(jnp.logical_not(is_own(i)))(lambda: y_beside(lax.div(i, 2)).start())

        def take_y_beside(j):
            y_beside(j).wait_recv()
            add_to(yy_buf.at[zz_of(j)], yy_buf.at[zz_of(j)], yx_buf.at[own_block(j)])

        def y_hop(j, k):
            zz = zz_of(j)

            def upward():
                if k > 0:
                    y_up(zz).wait_recv()
                    add_to(yy_buf.at[zz], yy_buf.at[zz], ylo_buf.at[zz])
                y_up(zz).start()

            def downward():
                if k > 0:
                    y_down(zz).wait_recv()
                    add_to(yy_buf.at[zz], yy_buf.at[zz], yhi_buf.at[zz])
                y_down(zz).start()

            pl.when((z < zz) & (z == k))(upward)
            pl.when((z > zz) & (NZ - 1 - z == k))(downward)

        def front(i):
            load(i).wait()
            b = block_of(i)
            pl.when(i == 0)(keep.wait)

            def landed():
                for stream in range(3):
                    h_twin(b, stream, True).wait_recv()

            pl.when(i > 0)(landed)
            r = block_rows(b, rows)
            rows_h, rows_dy = h[r, :], dy[r, :]
            logits = dot(rows_h, router_ref[...], (1, 1))
            shifted = jnp.exp(logits - jnp.max(logits, axis=-1, keepdims=True))
            probs = shifted / jnp.sum(shifted, axis=-1, keepdims=True) * chosen_ref[r, :].astype(jnp.float32)
            lane = lax.broadcasted_iota(jnp.int32, probs.shape, 1)
            line = lax.broadcasted_iota(jnp.int32, (rows, 128), 1)
            found = jnp.zeros((rows, 128), jnp.float32)
            for expert in range(local):
                at, up_at = pl.ds(expert * hidden, hidden), pl.ds((local + expert) * hidden, hidden)
                gate = jnp.sum(jnp.where(lane == e * local + expert, probs, 0.0), axis=-1, keepdims=True)
                pre = dot(rows_h, gu_ref[:, at], (1, 0))
                scale = dot(rows_h, gu_ref[:, up_at], (1, 0))
                back = dot(rows_dy, down_ref[at, :], (1, 1))
                sigmoid = jax.nn.sigmoid(pre)
                swish = pre * sigmoid
                active = swish * scale
                gated[r, at] = (active * gate).astype(low)
                found = jnp.where(line == expert, jnp.sum(active * back, axis=-1, keepdims=True), found)
                back = back * gate
                dgu[r, at] = (back * scale * sigmoid * (1.0 + pre * (1.0 - sigmoid))).astype(low)
                dgu[r, up_at] = (back * swish).astype(low)
            gate_part[b] = jnp.transpose(found)[:8, :]

        def rear(i):
            r = block_rows(block_of(i), rows)
            slot = lax.rem(i, 2)
            pl.when(i >= 2)(lambda: to_twin(i - 2).wait_send())

            def columns(k, carry):
                at = pl.ds(pl.multiple_of(k * wide, wide), wide)
                dx[slot, :, at] = dot(dgu[r, :], gu_ref[at, :], (1, 1)).astype(low)
                return carry

            lax.fori_loop(0, width // wide, columns, 0)
            to_twin(i).start()
            pl.when(i >= 2)(lambda: y_twin(i - 2).wait_send())

            def y_columns(k, carry):
                at = pl.ds(pl.multiple_of(k * wide, wide), wide)
                y_part[slot, :, at] = dot(gated[r, :], down_ref[:, at], (1, 0)).astype(low)
                return carry

            lax.fori_loop(0, width // wide, y_columns, 0)
            y_twin(i).start()

        tiles = width // piece // 4
        d_width = width // 8

        def gu_copies(n):
            slot = lax.rem(n, 2)
            at = pl.ds(pl.multiple_of(n * piece, piece), piece)
            return [
                pltpu.make_async_copy(
                    gu_stage.at[slot, :, pl.ds(k * hidden, hidden)],
                    (gate_w if k < local else up_w).at[k % local, at, :],
                    gu_sem.at[slot, k],
                )
                for k in range(2 * local)
            ]

        def d_copies(n):
            slot = lax.rem(n, 2)
            at = pl.ds(pl.multiple_of(n * d_width, d_width), d_width)
            return [
                pltpu.make_async_copy(
                    d_stage.at[slot, pl.ds(k * hidden, hidden), :], down_w.at[k, :, at], d_sem.at[slot, k]
                )
                for k in range(local)
            ]

        def each(copies, what):
            for copy in copies:
                getattr(copy, what)()

        def weight_grads(q):
            def tile(k, carry):
                n = q * tiles + k
                pl.when(n >= 2)(lambda: each(gu_copies(n - 2), "wait"))
                at = pl.ds(pl.multiple_of(n * piece, piece), piece)
                gu_stage[lax.rem(n, 2)] = dot(h[:, at], dgu[...], (0, 0))
                each(gu_copies(n), "start")
                return carry

            lax.fori_loop(0, tiles, tile, 0)

            def d_tile(k, carry):
                n = q * 2 + k
                pl.when(n >= 2)(lambda: each(d_copies(n - 2), "wait"))
                at = pl.ds(pl.multiple_of(n * d_width, d_width), d_width)
                d_stage[lax.rem(n, 2)] = dot(gated[...], dy[:, at], (0, 0))
                each(d_copies(n), "start")
                return carry

            lax.fori_loop(0, 2, d_tile, 0)

        near = [
            remote(gate_part, gate_land.at[k], near_s.at[k], near_r.at[k], mates[k])
            for k in range(tensors - 1)
        ]

        def far(k):
            return remote(
                gate_land.at[tensors - 1, lax.rem(e + k, GROUPS)], gates_out.at[e],
                far_s.at[k - 1], far_r.at[k - 1], peers[k - 1],
            )

        def sum_near():
            for copy in near:
                copy.wait_recv()
            total = gate_part[...]
            for k in range(tensors - 1):
                total = total + gate_land[k]
            gate_land[tensors - 1] = total
            for k in range(1, GROUPS):
                far(k).start()
            gates_out[e] = gate_land[tensors - 1, e]

        def step(i, carry):
            def at(number, body):
                pl.when(i == number)(body)

            odd, even = lax.rem(i, 2) == 1, lax.rem(i, 2) == 0
            j_even, j_odd = lax.div(i, 2) - 1, lax.div(i - 1, 2) - 1
            pl.when(i < GROUPS)(lambda: front(i))

            def events(*rels):
                for rel in rels:
                    gather_event(rel)

            at(1, lambda: events(2, 5, 8, 11))
            at(2, lambda: events(3, 6))
            at(3, lambda: events(10, 13))

            def twins():
                take_twin(i - 1)
                take_y_twin(i - 1)

            pl.when((i >= 1) & (i <= GROUPS))(twins)
            pl.when(even & (i >= 4) & (i <= GROUPS))(lambda: take_q_beside(j_even))
            at(3, lambda: take_q_beside(0))
            at(4, lambda: take_q_across(0))

            def late():
                take_p_across(i - 2)
                pl.when(i > 3)(lambda: take_q_across(j_odd))
                pl.when(i == 3)(lambda: p_beside(0).start())

            pl.when(odd & (i >= 3) & (i <= GROUPS + 1))(late)
            at(GROUPS, lambda: each(near, "start"))
            at(GROUPS + 1, sum_near)
            pl.when(i < GROUPS)(lambda: rear(i))
            pl.when(i >= GROUPS)(lambda: weight_grads(i - GROUPS))
            at(0, lambda: events(7, 1, 4))
            at(2, lambda: events(9, 12))
            pl.when(i < GROUPS - 1)(lambda: relay(i + 1))

            def pass_p():
                take_p_across(i - 2)
                pl.when(i > 2)(lambda: p_beside(j_even).start())

            pl.when(even & (i >= 2) & (i <= GROUPS))(pass_p)
            at(4, lambda: take_p_beside(0))

            def join():
                take_p_beside(j_odd)
                hop(j_odd, 0)

            pl.when(odd & (i >= 5) & (i <= GROUPS + 1))(join)
            pl.when((i == GROUPS) | (i == GROUPS + 2))(lambda: hop(j_even - 1, 1))
            at(GROUPS + 1, lambda: hop(1, 2))
            pl.when((i >= 2) & (i <= GROUPS + 1))(lambda: take_y_across(i - 2))
            at(5, lambda: take_y_beside(0))

            def join_y():
                take_y_beside(j_even - 1)
                y_hop(j_even - 1, 0)

            pl.when(even & (i >= 6) & (i <= GROUPS + 2))(join_y)
            pl.when((i == GROUPS + 1) | (i == GROUPS + 3))(lambda: y_hop(j_odd - 1, 1))
            at(GROUPS + 2, lambda: y_hop(1, 2))
            return carry

        lax.fori_loop(0, steps, step, 0)

        def columns_of(s, xx, cc):
            return pl.ds(pl.multiple_of(cc * half + s * part + xx * piece, piece), piece)

        mine = z
        for s in range(2):
            def below(s=s):
                up(mine, s).wait_recv()
                add_to(z_sum.at[s, mine], z_sum.at[s, mine], lo_buf.at[s, mine])

            def above(s=s):
                down_z(mine, s).wait_recv()
                add_to(z_sum.at[s, mine], z_sum.at[s, mine], hi_buf.at[s, mine])

            pl.when(z > 0)(below)
            pl.when(z < NZ - 1)(above)
            own = dh_out.at[:, columns_of(s, x, c)]

            def keep(k, carry, s=s, own=own):
                r = pl.ds(pl.multiple_of(k * 64, 64), 64)
                own[r, :] = z_sum[s, mine, r, :]
                return carry

            lax.fori_loop(0, rows // 64, keep, 0)
            remote(own, own, end_s.at[0, s], end_r.at[0, s], across).start()
            remote(own, own, end_s.at[1, s], end_r.at[1, s], twin).start()
        def y_columns_of(xx, cc):
            return pl.ds(pl.multiple_of(cc * half + xx * part, part), part)

        def y_below():
            y_up(mine).wait_recv()
            add_to(yy_buf.at[mine], yy_buf.at[mine], ylo_buf.at[mine])

        def y_above():
            y_down(mine).wait_recv()
            add_to(yy_buf.at[mine], yy_buf.at[mine], yhi_buf.at[mine])

        pl.when(z > 0)(y_below)
        pl.when(z < NZ - 1)(y_above)
        x1_copy.wait()
        y_own = block_out.at[:, y_columns_of(x, c)]

        def finish(k, carry):
            r = pl.ds(pl.multiple_of(k * 64, 64), 64)
            y_own[r, :] = (x1[r, :] + yy_buf[mine, r, :].astype(jnp.float32)).astype(low)
            return carry

        lax.fori_loop(0, rows // 64, finish, 0)
        remote(y_own, y_own, end_s.at[0, 2], end_r.at[0, 2], across).start()
        remote(y_own, y_own, end_s.at[1, 2], end_r.at[1, 2], twin).start()
        for s in range(2):
            there = dh_out.at[:, columns_of(s, 1 - x, c)]
            remote(there, there, end_s.at[0, s], end_r.at[0, s], across).wait_recv()
            remote(there, there, end_s.at[2, s], end_r.at[2, s], twin).start()
        there = block_out.at[:, y_columns_of(1 - x, c)]
        remote(there, there, end_s.at[0, 2], end_r.at[0, 2], across).wait_recv()
        remote(there, there, end_s.at[2, 2], end_r.at[2, 2], twin).start()
        for k, xx in ((1, x), (2, 1 - x)):
            there = block_out.at[:, y_columns_of(xx, 1 - c)]
            remote(there, there, end_s.at[k, 2], end_r.at[k, 2], twin).wait_recv()
        for k, target in ((0, across), (1, twin), (2, twin)):
            there = block_out.at[:, y_columns_of(1 - x if k == 2 else x, c)]
            remote(there, there, end_s.at[k, 2], end_r.at[k, 2], target).wait_send()
        for s in range(2):
            for k, xx in ((1, x), (2, 1 - x)):
                there = dh_out.at[:, columns_of(s, xx, 1 - c)]
                remote(there, there, end_s.at[k, s], end_r.at[k, s], twin).wait_recv()
            for k, target in ((0, across), (1, twin), (2, twin)):
                there = dh_out.at[:, columns_of(s, 1 - x if k == 2 else x, c)]
                remote(there, there, end_s.at[k, s], end_r.at[k, s], target).wait_send()
        for k in range(1, GROUPS):
            there = gates_out.at[lax.rem(e + GROUPS - k, GROUPS)]
            remote(there, there, far_s.at[k - 1], far_r.at[k - 1], peers[k - 1]).wait_recv()
            far(k).wait_send()
        each(near, "wait_send")

        def drain(i, carry):
            pl.when(i >= GROUPS - 2)(lambda: to_twin(i).wait_send())
            pl.when(i >= GROUPS - 2)(lambda: y_twin(i).wait_send())
            p_across(i).wait_send()
            y_across(i).wait_send()
            return carry

        lax.fori_loop(0, GROUPS, drain, 0)

        def drain_pair(j, carry):
            p_beside(j).wait_send()
            q_beside(j).wait_send()
            q_across(j).wait_send()
            y_beside(j).wait_send()
            pl.when(z < j)(lambda: y_up(j).wait_send())
            pl.when(z > j)(lambda: y_down(j).wait_send())
            for s in range(2):
                pl.when(z < j)(lambda s=s: up(j, s).wait_send())
                pl.when(z > j)(lambda s=s: down_z(j, s).wait_send())
            return carry

        lax.fori_loop(0, NZ, drain_pair, 0)

        def drain_rows_of(i, carry):
            b = block_of(i)
            h_across(b).wait_send()
            for stream in range(3):
                h_twin(b, stream).wait_send()
            return carry

        lax.fori_loop(1, GROUPS, drain_rows_of, 0)
        line.finish()
        for k in range(2):
            each(gu_copies(4 * tiles - 2 + k), "wait")
            each(d_copies(6 + k), "wait")

    shape = jax.ShapeDtypeStruct
    dma = pltpu.SemaphoreType.DMA
    f32 = jnp.float32
    return pl.pallas_call(
        kernel,
        out_shape=(
            shape((rows, width), low),
            shape((rows, width), low),
            shape((GROUPS, 8, rows), f32),
            shape((local, width, hidden), f32),
            shape((local, width, hidden), f32),
            shape((local, hidden, width), f32),
        ),
        in_specs=[HBM, HBM, VMEM, VMEM, VMEM, VMEM, HBM],
        out_specs=(VMEM, VMEM, VMEM, HBM, HBM, HBM),
        scratch_shapes=[
            pltpu.VMEM((tokens, width), low),
            pltpu.VMEM((tokens, width), low),
            pltpu.VMEM((tokens, units), low),
            pltpu.VMEM((tokens, 2 * units), low),
            pltpu.VMEM((2, rows, width), low),
            pltpu.VMEM((2, rows, width), low),
            pltpu.VMEM((GROUPS, rows, half), low),
            pltpu.VMEM((GROUPS, rows, part), low),
            pltpu.VMEM((NZ, rows, part), low),
            pltpu.VMEM((NZ, rows, part), low),
            pltpu.VMEM((NZ, rows, part), low),
            pltpu.VMEM((rows, part), f32),
            pltpu.VMEM((2, piece, 2 * units), f32),
            pltpu.VMEM((2, units, width // 8), f32),
            pltpu.VMEM((GROUPS, rows, half), low),
            pltpu.VMEM((GROUPS, rows, piece), low),
            pltpu.VMEM((NZ, rows, piece), low),
            pltpu.VMEM((NZ, rows, part), low),
            pltpu.VMEM((NZ, rows, piece), low),
            pltpu.VMEM((2, NZ, rows, piece), low),
            pltpu.VMEM((2, NZ, rows, piece), low),
            pltpu.VMEM((2, NZ, rows, piece), low),
            pltpu.VMEM((GROUPS, 8, rows), f32),
            pltpu.VMEM((tensors, GROUPS, 8, rows), f32),
            dma((GROUPS,)), dma, dma((2, 14, 3)), dma((2, 14)), dma((GROUPS,)), dma((GROUPS,)),
            dma((GROUPS, 3)), dma((GROUPS, 3)), dma, dma((GROUPS,)), dma((GROUPS,)), dma((GROUPS,)), dma((GROUPS,)),
            dma((NZ,)), dma((NZ,)), dma((2, NZ)), dma((2, NZ)), dma((2, 2 * local)), dma((2, local)),
            dma((GROUPS,)), dma((GROUPS,)), dma((GROUPS,)), dma((GROUPS,)),
            dma((NZ,)), dma((NZ,)), dma((NZ,)), dma((NZ,)), dma((NZ,)), dma((NZ,)),
            dma((2, 2, NZ)), dma((2, 2, NZ)),
            dma((tensors - 1,)), dma((tensors - 1,)), dma((GROUPS - 1,)), dma((GROUPS - 1,)),
            dma((3, 3)), dma((3, 3)),
        ],
        compiler_params=comm_params(collective_id, 62),
        cost_estimate=cost(80),
        name="expert_layer",
    )(hidden_two, grad_out_all, gate_up, down, router_t, chosen_all, residual)


def exchange_rows(value, part_ref, land_ref, send_sem, recv_sem, mates):
    rows = value.shape[0]
    line = lax.broadcasted_iota(jnp.int32, (rows, 128), 1)
    part_ref[...] = jnp.transpose(jnp.where(line == 0, value, 0.0))[:8, :]
    for k, mate in enumerate(mates):
        remote(part_ref, land_ref.at[k], send_sem.at[k], recv_sem.at[k], mate).start()


def exchanged_rows(part_ref, land_ref, send_sem, recv_sem, mates):
    total = part_ref[...]
    for k, mate in enumerate(mates):
        remote(part_ref, land_ref.at[k], send_sem.at[k], recv_sem.at[k], mate).wait_recv()
    for k in range(len(mates)):
        total = total + land_ref[k]
    rows = part_ref.shape[1]
    tall = jnp.concatenate([total, jnp.zeros((120, rows), jnp.float32)], axis=0)
    return jnp.transpose(tall)[:, :1]


def drain_rows(part_ref, land_ref, send_sem, recv_sem, mates):
    for k, mate in enumerate(mates):
        remote(part_ref, land_ref.at[k], send_sem.at[k], recv_sem.at[k], mate).wait_send()


def turn(value, cosine, sine):
    return value * cosine + pltpu.roll(value, HEAD // 2, 1) * sine


def project(
    tokens, w_qkv, w_out, out_grad, smalls, cosine, sine, w_gate, w_up, w_down, experts, collective_id
):
    rows, width = tokens.shape
    parts, depth, columns = w_qkv.shape
    heads = columns // HEAD
    tensors = NX * NC
    back = WINDOW // rows
    low, f32 = jnp.bfloat16, jnp.float32
    QUERY, KEY, VALUE, SMALL, OUT, GRAD, REST = 0, 1, 2, 3, 4, 5, 6
    out_half = w_out.shape[0] // 2
    out_rows, out_columns = w_out.shape
    quarter = width // tensors

    def kernel(
        tok_ref, w_ref, out_ref, grad_in, small_ref, cos_ref, sin_ref, gate_in, up_in, down_in,
        w_all, out_all, grad_all, h1_out, raw_out, gate_up, down_out, gain_ref, router_ref, chosen_ref, scale_ref, q_ref, context,
        small_all, h1_ref, raw_ref, wide_in, wide_low, down_f, down_low, own_w, own_out, weights, total, part_k, land_k, part_q, land_q,
        send_sem, recv_sem, out_sem, small_sem, kept, ks_s, ks_r, qs_s, qs_r, c_s, c_r, hx_s, hx_r, hc_s, hc_r, wide_s,
    ):
        z, y, x, c = place()
        e, t = lax.axis_index("expert"), lax.axis_index("tensor")
        wide_loads = [
            pltpu.make_async_copy(source.at[k], wide_in.at[2 * n + k], wide_s.at[2 * n + k])
            for n, source in enumerate((gate_in, up_in))
            for k in range(2)
        ]
        for copy in wide_loads:
            copy.start()
        mates = [(e, lax.rem(t + k, tensors)) for k in range(1, tensors)]
        beside, above = device(z, 1 - y, x, c), device(z + 1, y, x, c)
        views = [
            lambda b: weights.at[QUERY, block_rows(b, depth), :],
            lambda b: weights.at[KEY, block_rows(b, depth), :],
            lambda b: weights.at[VALUE, block_rows(b, depth), :],
            lambda b: small_all.at[b],
            lambda b: out_all.at[pl.ds(0, out_half), block_rows(b, out_columns)],
            lambda b: grad_view(b, x, c),
            lambda b: out_all.at[pl.ds(out_half, out_half), block_rows(b, out_columns)],
        ]
        across, twin = device(z, y, 1 - x, c), device(z, y, x, 1 - c)

        def quarter_at(xx, cc):
            return pl.ds(pl.multiple_of((xx * NC + cc) * quarter, quarter), quarter)

        def grad_view(b, xx, cc):
            return grad_all.at[block_rows(b, rows), quarter_at(xx, cc)]

        def grad_across(b, landing=False):
            piece = grad_view(b, 1 - x if landing else x, c)
            return remote(piece, piece, hx_s.at[b], hx_r.at[b], across)

        def grad_twin(b, relayed, landing=False):
            piece = grad_view(b, 1 - x if relayed else x, 1 - c if landing else c)
            return remote(piece, piece, hc_s.at[b, relayed], hc_r.at[b, relayed], twin)

        line = LineGather(
            [SMALL, VALUE, KEY, QUERY, OUT, GRAD, REST],
            [
                own_w.at[0], own_w.at[1], own_w.at[2], small_ref, own_out.at[pl.ds(0, out_half)],
                grad_in.at[:, quarter_at(x, c)], own_out.at[pl.ds(out_half, out_half)],
            ],
            views, send_sem, recv_sem, y_first=(OUT,),
        )
        greet(line.partners() + [(mate, None) for mate in mates])
        line.start(SMALL, 0)
        for part in (VALUE, KEY, QUERY):
            def cast(i, carry, part=part):
                r = pl.ds(pl.multiple_of(i * 32, 32), 32)
                own_w[part, r, :] = w_ref[part, r, :].astype(low)
                return carry

            lax.fori_loop(0, depth // 32, cast, 0)
            if part != QUERY:
                line.start(part, 0)

        def cast_out(i, carry):
            r = pl.ds(pl.multiple_of(i * 32, 32), 32)
            own_out[r, :] = out_ref[r, :].astype(low)
            return carry

        lax.fori_loop(0, out_rows // 32, cast_out, 0)
        keep_out = pltpu.make_async_copy(own_out, out_all.at[:, block_rows(line.block(0), out_columns)], kept.at[0])
        keep_out.start()
        keep_grad = pltpu.make_async_copy(grad_in, grad_all.at[block_rows(line.block(0), rows), :], kept.at[1])
        keep_grad.start()

        def square(i, carry):
            r = pl.ds(pl.multiple_of(i * 32, 32), 32)
            value = tok_ref[r, :].astype(f32)
            scale_ref[r, 0:1] = lax.rsqrt(jnp.mean(value * value, axis=-1, keepdims=True) + EPS)
            return carry

        lax.fori_loop(0, rows // 32, square, 0)
        total[...] = jnp.zeros_like(total)
        own_small = pltpu.make_async_copy(small_ref, small_all.at[line.block(0)], small_sem)
        own_small.start()

        def use(stream, rel):
            b = line.block(rel)
            at = pl.ds(pl.multiple_of(b * depth, depth), depth)
            if stream == SMALL:
                gain = small_ref[0:1, :] if rel == 0 else small_all[b, 0:1, :]
                h1_ref[:, at] = (tok_ref[:, at].astype(f32) * scale_ref[:, 0:1] * gain).astype(low)
                return
            block = own_w[stream] if rel == 0 else weights[stream, block_rows(b, depth), :]
            total[stream] += dot(h1_ref[:, at], block, (1, 0))

        def event(stream, rel):
            def body():
                line.arrive(stream, rel)
                if line.forwards(stream, rel):
                    marks = len(line.pending)
                    line.start(stream, rel)
                    late = line.pending[marks:]
                    del line.pending[marks:]
                    line.finish_later(late, rel)
                if stream == GRAD:
                    b = line.block(rel)
                    grad_across(b).start()
                    grad_twin(b, 0).start()
                elif stream not in (OUT, REST):
                    use(stream, rel)
            run_if(line.exists(rel), body)

        use(SMALL, 0)
        use(VALUE, 0)
        own_small.wait()

        units = down_in.shape[1]
        for n, copy in enumerate(wide_loads):
            copy.wait()

            def round_wide(i, carry, n=n):
                r = pl.ds(pl.multiple_of(i * 64, 64), 64)
                wide_low[r, pl.ds(n * units, units)] = wide_in[n, r, :].astype(low)
                return carry

            lax.fori_loop(0, width // 64, round_wide, 0)
        wide_out = pltpu.make_async_copy(wide_low, gate_up, wide_s.at[0])
        wide_out.start()
        down_loads = [
            pltpu.make_async_copy(down_in.at[k], down_f.at[pl.ds(k * units, units), :], wide_s.at[1 + k])
            for k in range(2)
        ]
        for copy in down_loads:
            copy.start()

        use(KEY, 0)
        def events(*pairs):
            for stream, rels in pairs:
                for rel in rels:
                    event(stream, rel)

        for rel in (7, 1, 4, 2, 5):
            event(SMALL, rel)
            event(VALUE, rel)
        for copy in down_loads:
            copy.wait()

        def round_down(i, carry):
            r = pl.ds(pl.multiple_of(i * 32, 32), 32)
            down_low[r, :] = down_f[r, :].astype(low)
            return carry

        lax.fori_loop(0, 2 * units // 32, round_down, 0)
        down_copy = pltpu.make_async_copy(down_low, down_out, wide_s.at[3])
        down_copy.start()
        line.start(QUERY, 0)
        for rel in (3, 6):
            event(SMALL, rel)
            event(VALUE, rel)
        events((KEY, (7, 1, 4)))
        for rel in (8, 11, 9, 12, 10, 13):
            event(SMALL, rel)
            event(VALUE, rel)

        slices = HEAD // GROUPS
        for b in range(GROUPS):
            at = pl.ds(b * depth, depth)
            gain_ref[0:2, at] = small_all[b, 0:2, :]
            router_ref[:, at] = small_all[b, 8 : 8 + experts, :].astype(low)
            tall = jnp.concatenate(
                [small_all[b, 8 + experts : 8 + 2 * experts, :], jnp.zeros((128 - experts, depth), f32)], axis=0
            )
            chosen_ref[pl.ds(b * depth, depth), :] = jnp.transpose(tall)[:, :experts].astype(low)
        for which in range(2):
            for head in range(heads):
                start = (which * heads + head) * slices
                gain_ref[2 + which : 3 + which, pl.ds(head * HEAD, HEAD)] = jnp.concatenate(
                    [small_all[b, 2:3, start : start + slices] for b in range(GROUPS)], axis=1
                )

        def context_copy(which, k):
            if k == 2:
                source, target = 0, above
            elif k == 4:
                source, target = 2, above
            else:
                source, target = jnp.where(y == 0, k - 1, k + 1), beside
            return remote(
                context.at[source, which], context.at[k, which], c_s.at[which, k], c_r.at[which, k], target
            )

        sends = {2: z < NZ - 1, 4: (z >= 1) & (z < NZ - 1), 1: (y == 0) | (z >= 1), 3: z >= 1 + y}
        takes = {2: z >= 1, 4: z >= 2, 1: (y == 1) | (z >= 1), 3: z >= 2 - y}

        def context_send(which, k):
            run_if(sends[k], lambda: context_copy(which, k).start())

        def context_take(which, k):
            run_if(takes[k], lambda: context_copy(which, k).wait_recv())

        for k in range(1, back + 1):
            def clear(k=k):
                context[k] = jnp.zeros_like(context[k])
            run_if(jnp.logical_not(takes[k]), clear)

        context[0, 1] = total[VALUE].astype(low)
        context_send(1, 2)
        run_if(y == 0, lambda: context_copy(1, 1).start())
        events((KEY, (2, 5, 3, 6)), (QUERY, (7, 1, 4)))
        line.start(GRAD, 0)
        line.start(OUT, 0)
        line.start(REST, 0)
        events((KEY, (8, 11, 9, 12, 10, 13)))
        key_raw = total[KEY]
        raw_ref[1] = key_raw
        exchange_rows(jnp.sum(key_raw * key_raw, axis=-1, keepdims=True), part_k, land_k, ks_s, ks_r, mates)
        use(QUERY, 0)
        events((QUERY, (2, 5)))
        key_scale = lax.rsqrt(exchanged_rows(part_k, land_k, ks_s, ks_r, mates) / width + EPS)
        scale_ref[:, 2:3] = key_scale
        def rotated(which, scale, store):
            for head in range(heads):
                at = pl.ds(head * HEAD, HEAD)
                value = total[which, :, at] * scale * gain_ref[2 + which : 3 + which, at]
                store(at, turn(value, cos_ref[...], sin_ref[...]).astype(low))

        def store_key(at, value):
            context[0, 0, :, at] = value

        rotated(KEY, key_scale, store_key)
        context_send(0, 2)
        run_if(y == 0, lambda: context_copy(0, 1).start())

        def relay_two(which):
            context_take(which, 2)
            context_send(which, 4)
            run_if((y == 1) & (z >= 1), lambda: context_copy(which, 1).start())
            run_if((y == 0) & sends[3], lambda: context_copy(which, 3).start())

        def relay_four(which):
            context_take(which, 4)
            run_if((y == 1) & sends[3], lambda: context_copy(which, 3).start())

        relay_two(1)
        events((QUERY, (3, 6)), (GRAD, (7, 1, 4)), (OUT, (7, 1, 4)), (REST, (7, 1, 4)))
        relay_four(1)
        events((QUERY, (8, 11)), (GRAD, (2, 5)), (OUT, (8, 11, 2, 5)), (REST, (2, 5)))
        relay_two(0)
        events((QUERY, (9, 12, 10, 13)))
        query_raw = total[QUERY]
        raw_ref[0] = query_raw
        exchange_rows(jnp.sum(query_raw * query_raw, axis=-1, keepdims=True), part_q, land_q, qs_s, qs_r, mates)
        for part in range(parts):
            weights[part, block_rows(line.block(0), depth), :] = own_w[part]
        keep = pltpu.make_async_copy(weights, w_all, out_sem)
        keep.start()
        keep_more = [
            pltpu.make_async_copy(h1_ref, h1_out, kept.at[2]),
            pltpu.make_async_copy(raw_ref, raw_out, kept.at[3]),
        ]
        for copy in keep_more:
            copy.start()
        events((GRAD, (3, 6)), (OUT, (9, 12, 3, 6)), (REST, (3, 6, 8, 11)))
        relay_four(0)
        query_scale = lax.rsqrt(exchanged_rows(part_q, land_q, qs_s, qs_r, mates) / width + EPS)
        scale_ref[:, 1:2] = query_scale

        def store_query(at, value):
            q_ref[:, at] = value

        rotated(QUERY, query_scale, store_query)
        events((GRAD, (8, 11, 9, 12)), (OUT, (10, 13)), (REST, (9, 12, 10, 13)), (GRAD, (10, 13)))
        for which in (1, 0):
            for k in (1, 3):
                context_take(which, k)
        for rel in line.order():
            def relay(rel=rel):
                b = line.block(rel)
                grad_across(b, True).wait_recv()
                grad_twin(b, 1).start()
            run_if(line.exists(rel), relay)
        for rel in line.order():
            def landed(rel=rel):
                b = line.block(rel)
                grad_across(b).wait_send()
                for relayed in range(2):
                    grad_twin(b, relayed, True).wait_recv()
                    grad_twin(b, relayed).wait_send()
            run_if(line.exists(rel), landed)
        line.finish()
        for copy in keep_more:
            copy.wait()
        wide_out.wait()
        down_copy.wait()
        keep_out.wait()
        keep_grad.wait()
        for which in range(2):
            for k in range(1, back + 1):
                run_if(sends[k], lambda which=which, k=k: context_copy(which, k).wait_send())
        drain_rows(part_k, land_k, ks_s, ks_r, mates)
        drain_rows(part_q, land_q, qs_s, qs_r, mates)
        keep.wait()

    shape, dma = jax.ShapeDtypeStruct, pltpu.SemaphoreType.DMA
    return pl.pallas_call(
        kernel,
        out_shape=(
            shape((parts, depth * GROUPS, columns), low),
            shape((out_rows, out_columns * GROUPS), low),
            shape((rows * GROUPS, width), low),
            shape((rows, width), low),
            shape((2, rows, columns), f32),
            shape((width, 4 * w_down.shape[1]), low),
            shape((2 * w_down.shape[1], width), low),
            shape((8, width), f32),
            shape((experts, width), low),
            shape((rows * GROUPS, experts), low),
            shape((rows, 128), f32),
            shape((rows, columns), low),
            shape((back + 1, 2, rows, columns), low),
        ),
        in_specs=[VMEM, VMEM, VMEM, HBM, VMEM, VMEM, VMEM, HBM, HBM, HBM],
        out_specs=(HBM,) * 7 + (VMEM,) * 6,
        scratch_shapes=[
            pltpu.VMEM((GROUPS,) + smalls.shape, f32),
            pltpu.VMEM((rows, width), low),
            pltpu.VMEM((2, rows, columns), f32),
            pltpu.VMEM((4, width, w_down.shape[1]), f32),
            pltpu.VMEM((width, 4 * w_down.shape[1]), low),
            pltpu.VMEM((2 * w_down.shape[1], width), f32),
            pltpu.VMEM((2 * w_down.shape[1], width), low),
            pltpu.VMEM((parts, depth, columns), low),
            pltpu.VMEM((out_rows, out_columns), low),
            pltpu.VMEM((parts, depth * GROUPS, columns), low),
            pltpu.VMEM((parts, rows, columns), f32),
            pltpu.VMEM((8, rows), f32),
            pltpu.VMEM((tensors - 1, 8, rows), f32),
            pltpu.VMEM((8, rows), f32),
            pltpu.VMEM((tensors - 1, 8, rows), f32),
            dma((7, 14, 3)), dma((7, 14)), dma, dma, dma((4,)),
            dma((tensors - 1,)), dma((tensors - 1,)), dma((tensors - 1,)), dma((tensors - 1,)),
            dma((2, back + 1)), dma((2, back + 1)),
            dma((GROUPS,)), dma((GROUPS,)), dma((GROUPS, 2)), dma((GROUPS, 2)), dma((4,)),
        ],
        compiler_params=comm_params(collective_id, 56),
        cost_estimate=cost(100),
        name="project",
    )(tokens, w_qkv, w_out, out_grad, smalls, cosine, sine, w_gate, w_up, w_down)


def attend(query, context, segment_query, segment_keys, tokens, out_low, gain, collective_id):
    rows, columns = query.shape
    width = tokens.shape[1]
    blocks = context.shape[0]
    heads = columns // HEAD
    half, quarter = width // 2, width // 4
    low, f32 = jnp.bfloat16, jnp.float32

    def kernel(
        q_ref, context_ref, sq_ref, sk_ref, tok_ref, out_ref, gain_ref,
        o_ref, lse_ref, x1_ref, h2_ref, scale_ref,
        part, full, core_buf, x_buf, send_sem, recv_sem,
    ):
        z, y, x, c = place()
        across, twin = device(z, y, 1 - x, c), device(z, y, x, 1 - c)
        greet([(across, None), (twin, None)])
        row = lax.broadcasted_iota(jnp.int32, (rows, rows), 0)
        column = lax.broadcasted_iota(jnp.int32, (rows, rows), 1)
        allowed = []
        for k in range(blocks):
            distance = row - column + k * rows
            allowed.append(
                (sq_ref[...] == sk_ref[k : k + 1, :]) & (distance >= 0) & (distance < WINDOW)
            )
        line = lax.broadcasted_iota(jnp.int32, (rows, 128), 1)
        lse = jnp.zeros((rows, 128), f32)
        for head in range(heads):
            at = pl.ds(head * HEAD, HEAD)
            scores = [
                jnp.where(
                    allowed[k], dot(q_ref[:, at], context_ref[k, 0, :, at], (1, 1)) * HEAD ** (-0.5), -1e30
                )
                for k in range(blocks)
            ]
            largest = scores[0]
            for k in range(1, blocks):
                largest = jnp.maximum(largest, scores[k])
            largest = jnp.max(largest, axis=-1, keepdims=True)
            weights = [jnp.exp(s - largest) for s in scores]
            amount = weights[0]
            for k in range(1, blocks):
                amount = amount + weights[k]
            amount = jnp.sum(amount, axis=-1, keepdims=True)
            inverse = 1.0 / amount
            value = jnp.zeros((rows, HEAD), f32)
            for k in range(blocks):
                value = value + dot((weights[k] * inverse).astype(low), context_ref[k, 1, :, at], (1, 0))
            o_ref[:, at] = value.astype(low)
            lse = jnp.where(line == head, largest + jnp.log(amount), lse)
        lse_ref[...] = lse

        def half_of(cc):
            return pl.ds(pl.multiple_of(cc * half, half), half)

        def fill(cc):
            def body(k, carry):
                at = pl.ds(pl.multiple_of(cc * half + k * quarter, quarter), quarter)
                part[:, at] = dot(o_ref[...], out_ref[:, at], (1, 0)).astype(low)
                return carry

            lax.fori_loop(0, 2, body, 0)

        fill(1 - c)
        group_sum(part, full, core_buf, x_buf, send_sem, recv_sem, lambda: fill(c))

        def norm(i, carry):
            r = pl.ds(pl.multiple_of(i * 32, 32), 32)
            value = tok_ref[r, :].astype(f32) + full[r, :].astype(f32)
            scale = lax.rsqrt(jnp.mean(value * value, axis=-1, keepdims=True) + EPS)
            x1_ref[r, :] = value
            scale_ref[r, :] = jnp.broadcast_to(scale, (32, 128))
            h2_ref[r, :] = (value * scale * gain_ref[1:2, :]).astype(low)
            return carry

        lax.fori_loop(0, rows // 32, norm, 0)

    shape, dma = jax.ShapeDtypeStruct, pltpu.SemaphoreType.DMA
    return pl.pallas_call(
        kernel,
        out_shape=(
            shape((rows, columns), low),
            shape((rows, 128), f32),
            shape((rows, width), f32),
            shape((rows, width), low),
            shape((rows, 128), f32),
        ),
        in_specs=[VMEM] * 7,
        out_specs=(VMEM,) * 5,
        scratch_shapes=[
            pltpu.VMEM((rows, width), low),
            pltpu.VMEM((rows, width), low),
            pltpu.VMEM((rows, half), low),
            pltpu.VMEM((rows, quarter), low),
            dma((5,)), dma((5,)),
        ],
        compiler_params=comm_params(collective_id, 40),
        cost_estimate=cost(40),
        name="attend",
    )(query, context, segment_query, segment_keys, tokens, out_low, gain)


def attend_back(
    grad_hidden, grad_probs, router_t, hidden_two, residual, scale_two, gains, out_grad,
    query, context, segment_query, segment_keys, attended, log_sums, raw, scales,
    cosine, sine, hidden_one, tokens, qkv_low, out_low, collective_id,
):
    rows, width = tokens.shape
    columns = query.shape[1]
    heads = columns // HEAD
    experts = router_t.shape[0]
    blocks = context.shape[0]
    depth = width // GROUPS
    small_rows = 8 + experts
    tensors = NX * NC
    half, quarter = width // 2, width // 4
    low, f32 = jnp.bfloat16, jnp.float32
    QUERY, KEY, VALUE, OUT, SMALL = 0, 1, 2, 3, 4

    def kernel(
        dh_ref, gates_ref, router_ref, h2_ref, x1_ref, s2_ref, gain_ref, dy_ref,
        q_ref, context_ref, sq_ref, sk_ref, o_ref, lse_ref, raw_ref, scale_ref,
        cos_ref, sin_ref, h1_ref, tok_ref, w_hbm, out_ref,
        tok_grad, qkv_sum, out_sum, small_sum,
        weights, dx1, da, do, dot_sums, dq, dkv, scaled, proj, send_kv, land_y, land_z,
        part, full, core_buf, x_buf, small, line_sum,
        main_buf, out_acc, out_lo, out_hi, out_land, small_buf, part_k, land_k, part_q, land_q,
        w_sem, y_s, y_r, z_s, z_r, group_s, group_r, ks_s, ks_r, qs_s, qs_r, line_s, line_r, out_s, out_r, out_y_s, out_y_r,
    ):
        z, y, x, c = place()
        e, t = lax.axis_index("expert"), lax.axis_index("tensor")
        mates = [(e, lax.rem(t + k, tensors)) for k in range(1, tensors)]
        beside, below = device(z, 1 - y, x, c), device(z - 1, y, x, c)
        fetch = pltpu.make_async_copy(w_hbm, weights, w_sem)
        fetch.start()

        def own_part(s, b):
            if s == SMALL:
                return small[b]
            at = pl.ds(pl.multiple_of(b * depth, depth), depth)
            return dot(h1_ref[:, at], proj[s], (0, 0))

        def out_copy(zz, yy, way):
            landing = (out_lo if way == 0 else out_hi).at[zz, yy]
            target = device(z + 1, y, x, c) if way == 0 else below
            return remote(out_acc.at[zz, yy], landing, out_s.at[zz, yy, way], out_r.at[zz, yy, way], target)

        def out_take(zz, yy, way):
            out_copy(zz, yy, way).wait_recv()
            total = out_acc.at[zz, yy]
            add_to(total, total, (out_lo if way == 0 else out_hi).at[zz, yy])

        def out_hop(k):
            for zz in Z_ORDER:
                for yy in range(NY):
                    def upward(zz=zz, yy=yy):
                        if k > 0:
                            out_take(zz, yy, 0)
                        out_copy(zz, yy, 0).start()

                    def downward(zz=zz, yy=yy):
                        if k > 0:
                            out_take(zz, yy, 1)
                        out_copy(zz, yy, 1).start()

                    if k < zz:
                        run_if((z < zz) & (z == k), upward)
                    if NZ - 1 - k > zz:
                        run_if((z > zz) & (NZ - 1 - z == k), downward)

        def out_beside():
            return remote(out_acc.at[z, 1 - y], out_land, out_y_s, out_y_r, beside)

        def out_start():
            for zz in range(NZ):
                for yy in range(NY):
                    at = pl.ds((zz * NY + yy) * depth, depth)
                    out_acc[zz, yy] = dot(o_ref[...], da[:, at], (0, 0)).astype(low)

        def out_home():
            for yy in range(NY):
                run_if(z > 0, lambda yy=yy: out_take(z, yy, 0))
                run_if(z < NZ - 1, lambda yy=yy: out_take(z, yy, 1))
            out_beside().start()

        def out_end():
            out_beside().wait_recv()
            out_sum[...] = out_acc[z, y].astype(f32) + out_land[...].astype(f32)
            out_beside().wait_send()
            for zz in range(NZ):
                for yy in range(NY):
                    run_if(z < zz, lambda zz=zz, yy=yy: out_copy(zz, yy, 0).wait_send())
                    run_if(z > zz, lambda zz=zz, yy=yy: out_copy(zz, yy, 1).wait_send())

        def slot(kind):
            def view(s, zz):
                if s == SMALL:
                    return small_buf.at[kind, zz]
                return main_buf.at[kind, zz, s]
            return view

        line = LineReduce([], lambda s, zz, yy: slot(3)(s, zz), slot(0), slot(1), slot(2), line_s, line_r)
        greet(line.partners() + [(mate, None) for mate in mates])

        grad_probs = gates_ref[...]
        logits = dot(h2_ref[...], router_ref[...], (1, 1))
        shifted = jnp.exp(logits - jnp.max(logits, axis=-1, keepdims=True))
        probs = shifted / jnp.sum(shifted, axis=-1, keepdims=True)
        grad_logits = probs * (grad_probs - jnp.sum(probs * grad_probs, axis=-1, keepdims=True))
        tall = jnp.transpose(
            jnp.concatenate([grad_logits, jnp.zeros((rows, 128 - experts), f32)], axis=1)
        )
        grad_logits = grad_logits.astype(low)
        tall = tall.astype(low)
        for b in range(GROUPS):
            small[b] = jnp.zeros_like(small[b])
            small[b, 8 : 8 + experts, :] = dot(tall, h2_ref[:, pl.ds(b * depth, depth)], (1, 0))[:experts]
        dx1[...] = dot(grad_logits, router_ref[...], (1, 0))
        line_sum[...] = jnp.zeros_like(line_sum)

        def norm_two(i, carry):
            r = pl.ds(pl.multiple_of(i * 32, 32), 32)
            grad = dh_ref[r, :].astype(f32) + dx1[r, :]
            value, scale = x1_ref[r, :], s2_ref[r, 0:1]
            line_sum[0:1, :] += jnp.sum(grad * (value * scale), axis=0, keepdims=True)
            grad = grad * gain_ref[1:2, :]
            inner = jnp.mean(grad * value, axis=-1, keepdims=True)
            result = dy_ref[r, :].astype(f32) + scale * grad - value * (scale * scale * scale) * inner
            dx1[r, :] = result
            da[r, :] = result.astype(low)
            return carry

        lax.fori_loop(0, rows // 32, norm_two, 0)

        out_start()
        out_hop(0)

        do[...] = dot(da[...], out_ref[...], (1, 1)).astype(low)
        wide = lax.broadcasted_iota(jnp.int32, (rows, 128), 1)
        sums = jnp.zeros((rows, 128), f32)
        for head in range(heads):
            at = pl.ds(head * HEAD, HEAD)
            inner = jnp.sum(do[:, at].astype(f32) * o_ref[:, at].astype(f32), axis=-1, keepdims=True)
            sums = jnp.where(wide == head, inner, sums)
        dot_sums[...] = sums
        dq[...] = jnp.zeros_like(dq)
        row = lax.broadcasted_iota(jnp.int32, (rows, rows), 0)
        column = lax.broadcasted_iota(jnp.int32, (rows, rows), 1)

        def attention_block(k):
            distance = row - column + k * rows
            allowed = (sq_ref[...] == sk_ref[k : k + 1, :]) & (distance >= 0) & (distance < WINDOW)
            for head in range(heads):
                at = pl.ds(head * HEAD, HEAD)
                queries, keys, values = q_ref[:, at], context_ref[k, 0, :, at], context_ref[k, 1, :, at]
                scores = dot(queries, keys, (1, 1)) * HEAD ** (-0.5)
                weight = jnp.where(allowed, jnp.exp(scores - lse_ref[:, head : head + 1]), 0.0)
                grad_weight = dot(do[:, at], values, (1, 1))
                grad_score = (
                    weight * (grad_weight - dot_sums[:, head : head + 1]) * HEAD ** (-0.5)
                ).astype(low)
                dq[:, at] += dot(grad_score, keys, (1, 0))
                dkv[k, 0, :, at] = dot(grad_score, queries, (0, 0))
                dkv[k, 1, :, at] = dot(weight.astype(low), do[:, at], (0, 0))

        exists = {0: None, 1: (y == 1) | (z >= 1), 2: z >= 1, 3: z >= 2 - y, 4: z >= 2}
        comes = {1: (y == 0) | (z >= 1), 3: z >= 1 + y}

        def kv_copy(which, k):
            if k in (1, 3):
                landing, target = land_y.at[k // 2, which], beside
                return remote(send_kv.at[k - 1, which], landing, y_s.at[k // 2, which], y_r.at[k // 2, which], target)
            landing = land_z.at[k // 2 - 1, which]
            return remote(
                send_kv.at[k - 1, which], landing, z_s.at[k // 2 - 1, which], z_r.at[k // 2 - 1, which], below
            )

        def kv_send(which, k):
            send_kv[k - 1, which] = dkv[k, which].astype(low)
            kv_copy(which, k).start()

        def merge(into, which, landed):
            add_to(dkv.at[into, which], dkv.at[into, which], landed, 32)

        for k in (3, 1, 4, 2, 0):
            def one(k=k):
                attention_block(k)
                if k in (1, 3):
                    kv_send(1, k)
                    kv_send(0, k)
            run_if(exists[k], one)

        def take_three(which):
            def land():
                kv_copy(which, 3).wait_recv()
                pl.when(y == 1)(lambda: merge(4, which, land_y.at[1, which]))
                pl.when(y == 0)(lambda: merge(2, which, land_y.at[1, which]))
            run_if(comes[3], land)
            run_if(exists[4], lambda: kv_send(which, 4))

        def take_one(which):
            def land():
                kv_copy(which, 1).wait_recv()
                pl.when(y == 1)(lambda: merge(2, which, land_y.at[0, which]))
                pl.when(y == 0)(lambda: merge(0, which, land_y.at[0, which]))
            run_if(comes[1], land)

        def take_four(which):
            def land():
                kv_copy(which, 4).wait_recv()
                merge(2, which, land_z.at[1, which])
            run_if((z >= 1) & (z < NZ - 1), land)
            run_if(exists[2], lambda: kv_send(which, 2))

        def take_two(which):
            def land():
                kv_copy(which, 2).wait_recv()
                merge(0, which, land_z.at[0, which])
            run_if(z < NZ - 1, land)

        def unturn(which, grad_of):
            inner = jnp.zeros((rows, 1), f32)
            for head in range(heads):
                at = pl.ds(head * HEAD, HEAD)
                grad = turn(grad_of(at), cos_ref[...], -sin_ref[...])
                value = raw_ref[which, :, at]
                line_sum[1 + which : 2 + which, at] = jnp.sum(
                    grad * (value * scale_ref[:, 1 + which : 2 + which]), axis=0, keepdims=True
                )
                grad = grad * gain_ref[2 + which : 3 + which, at]
                scaled[which, :, at] = grad
                inner = inner + jnp.sum(grad * value, axis=-1, keepdims=True)
            return inner

        def denorm(which, inner):
            scale = scale_ref[:, 1 + which : 2 + which]
            rest = scale * scale * scale * inner / width
            for head in range(heads):
                at = pl.ds(head * HEAD, HEAD)
                proj[which, :, at] = (
                    scale * scaled[which, :, at] - raw_ref[which, :, at] * rest
                ).astype(low)

        def send_beside(s):
            for zz in Z_ORDER:
                buffer = slot(3)(s, zz)
                buffer[...] = own_part(s, zz * NY + 1 - y).astype(buffer.dtype)
                line.to_y(s, zz)

        exchange_rows(unturn(QUERY, lambda at: dq[:, at]), part_q, land_q, qs_s, qs_r, mates)
        take_three(1)
        take_three(0)
        denorm(QUERY, exchanged_rows(part_q, land_q, qs_s, qs_r, mates))
        send_beside(QUERY)
        out_hop(1)
        take_one(1)
        take_one(0)
        take_four(1)
        take_four(0)
        take_two(1)
        proj[VALUE] = dkv[0, 1].astype(low)
        send_beside(VALUE)
        take_two(0)
        out_hop(2)
        exchange_rows(unturn(KEY, lambda at: dkv[0, 0, :, at]), part_k, land_k, ks_s, ks_r, mates)
        denorm(KEY, exchanged_rows(part_k, land_k, ks_s, ks_r, mates))
        send_beside(KEY)
        out_home()
        fetch.wait()

        def half_of(cc):
            def body(i, carry):
                at = pl.ds(pl.multiple_of(cc * half + i * quarter, quarter), quarter)
                value = dot(proj[0], weights[0, at, :], (1, 1))
                for s in (1, 2):
                    value = value + dot(proj[s], weights[s, at, :], (1, 1))
                part[:, at] = value.astype(low)
                return carry

            lax.fori_loop(0, 2, body, 0)

        stages = group_stages(part, full, core_buf, x_buf, group_s, group_r)
        half_of(1 - c)
        stages[0]()
        half_of(c)
        stages[1]()

        def hop(s, zz, k):
            def upward():
                if k > 0:
                    line.take(s, zz, 1)
                line.copy(s, zz, 1).start()

            def downward():
                if k > 0:
                    line.take(s, zz, 2)
                line.copy(s, zz, 2).start()

            if k < zz:
                run_if((z < zz) & (z == k), upward)
            if NZ - 1 - k > zz:
                run_if((z > zz) & (NZ - 1 - z == k), downward)

        def receive(s, zz):
            line.copy(s, zz, 0).wait_recv()
            buffer = slot(0)(s, zz)
            buffer[...] = (buffer[...].astype(f32) + own_part(s, zz * NY + y)).astype(buffer.dtype)

        units = []

        def run_units(s):
            for zz in Z_ORDER:
                receive(s, zz)
                hop(s, zz, 0)
                units.append((s, zz))
                for k in (1, 2):
                    if len(units) > k:
                        hop(*units[-1 - k], k)

        def norm_one(i, carry):
            r = pl.ds(pl.multiple_of(i * 32, 32), 32)
            grad, value, scale = full[r, :].astype(f32), tok_ref[r, :].astype(f32), scale_ref[r, 0:1]
            line_sum[3:4, :] += jnp.sum(grad * (value * scale), axis=0, keepdims=True)
            grad = grad * gain_ref[0:1, :]
            inner = jnp.mean(grad * value, axis=-1, keepdims=True)
            tok_grad[r, :] = (
                dx1[r, :] + scale * grad - value * (scale * scale * scale) * inner
            ).astype(low)
            return carry

        run_units(QUERY)
        stages[2]()
        run_units(VALUE)
        stages[3]()
        stages[4]()
        lax.fori_loop(0, rows // 32, norm_one, 0)
        for b in range(GROUPS):
            at = pl.ds(b * depth, depth)
            small[b, 0:1, :] = line_sum[3:4, at]
            small[b, 1:2, :] = line_sum[0:1, at]
            for which in range(2):
                for k in range(columns // depth):
                    small[b, 2 + 2 * which + k : 3 + 2 * which + k, :] = line_sum[
                        1 + which : 2 + which, pl.ds(k * depth, depth)
                    ]
        send_beside(SMALL)
        run_units(KEY)
        run_units(SMALL)
        out_end()
        hop(*units[-1], 1)
        hop(*units[-2], 2)
        hop(*units[-1], 2)

        def done(s, total):
            target = qkv_sum.at[s] if s < OUT else small_sum
            target[...] = total[...].astype(f32)

        line.streams = [QUERY, VALUE, KEY, SMALL]
        line.home(done)
        line.finish()
        for which in range(2):
            for k in (1, 2, 3, 4):
                run_if(exists[k], lambda which=which, k=k: kv_copy(which, k).wait_send())
        drain_rows(part_k, land_k, ks_s, ks_r, mates)
        drain_rows(part_q, land_q, qs_s, qs_r, mates)

    shape, dma, vmem = jax.ShapeDtypeStruct, pltpu.SemaphoreType.DMA, pltpu.VMEM
    return pl.pallas_call(
        kernel,
        out_shape=(
            shape((rows, width), low),
            shape((3, depth, columns), f32),
            shape((columns, depth), f32),
            shape((small_rows, depth), f32),
        ),
        in_specs=[VMEM] * 20 + [HBM, VMEM],
        out_specs=(VMEM,) * 4,
        scratch_shapes=[
            vmem(qkv_low.shape, low),
            vmem((rows, width), f32),
            vmem((rows, width), low),
            vmem((rows, columns), low),
            vmem((rows, 128), f32),
            vmem((rows, columns), f32),
            vmem((blocks, 2, rows, columns), f32),
            vmem((2, rows, columns), f32),
            vmem((3, rows, columns), low),
            vmem((blocks - 1, 2, rows, columns), low),
            vmem((2, 2, rows, columns), low),
            vmem((2, 2, rows, columns), low),
            vmem((rows, width), low),
            vmem((rows, width), low),
            vmem((rows, half), low),
            vmem((rows, quarter), low),
            vmem((GROUPS, small_rows, depth), f32),
            vmem((8, width), f32),
            vmem((4, NZ, 3, depth, columns), low),
            vmem((NZ, NY, columns, depth), low),
            vmem((NZ, NY, columns, depth), low),
            vmem((NZ, NY, columns, depth), low),
            vmem((columns, depth), low),
            vmem((4, NZ, small_rows, depth), f32),
            vmem((8, rows), f32),
            vmem((tensors - 1, 8, rows), f32),
            vmem((8, rows), f32),
            vmem((tensors - 1, 8, rows), f32),
            dma, dma((2, 2)), dma((2, 2)), dma((2, 2)), dma((2, 2)), dma((5,)), dma((5,)),
            dma((tensors - 1,)), dma((tensors - 1,)), dma((tensors - 1,)), dma((tensors - 1,)),
            dma((5, NZ, 3)), dma((5, NZ, 3)), dma((NZ, NY, 2)), dma((NZ, NY, 2)), dma, dma,
        ],
        compiler_params=comm_params(collective_id, 62),
        cost_estimate=cost(130),
        name="attend_back",
    )(
        grad_hidden, grad_probs, router_t, hidden_two, residual, scale_two, gains, out_grad,
        query, context, segment_query, segment_keys, attended, log_sums, raw, scales,
        cosine, sine, hidden_one, tokens, qkv_low, out_low,
    )


def fast_shards(
    tokens_in,
    out_grad,
    w_qkv,
    w_attn_out,
    attn_gain,
    ffn_gain,
    qk_gain,
    w_router,
    w_gate,
    w_up,
    w_down,
    routes,
    segments,
):
    row_count, model_width = tokens_in.shape
    experts = w_router.shape[1]
    local_experts = w_gate.shape[0]
    heads_here = qk_gain.shape[1]
    local_width = heads_here * HEAD
    groups = lax.axis_size("expert")
    device_index = lax.axis_index("expert")
    tensor_index = lax.axis_index("tensor")
    quarter = model_width // lax.axis_size("tensor")
    hop_count = WINDOW // row_count
    score_scale = HEAD ** (-0.5)
    low = jnp.bfloat16

    chosen = jnp.any(
        routes[:, :, None] == jnp.arange(experts, dtype=jnp.int32)[None, None, :], axis=1
    ).astype(jnp.float32)
    qk_row = qk_gain.reshape(1, -1)

    def rounded(v):
        return lax.reduce_precision(v, 8, 7)

    smalls = jnp.concatenate(
        [
            rounded(attn_gain)[None, :],
            rounded(ffn_gain)[None, :],
            jnp.pad(rounded(qk_row), ((0, 0), (0, row_count - qk_row.shape[1]))),
            jnp.zeros((5, row_count), jnp.float32),
            w_router.T,
            chosen.T,
        ],
        axis=0,
    )
    global_rows = device_index * row_count + jnp.arange(row_count, dtype=jnp.int32)
    cosine_table, sine_table = angles(global_rows % SEQ, HEAD)
    wide_cosine = jnp.concatenate([cosine_table[:, 0], cosine_table[:, 0]], axis=1)
    wide_sine = jnp.concatenate([-sine_table[:, 0], sine_table[:, 0]], axis=1)
    (
        qkv_low, out_low, grad_out_all, hidden_one, raw, gate_up, down_low, gains, router_t, chosen_all,
        scales, query_low, context_blocks,
    ) = project(
        tokens_in, w_qkv, w_attn_out, out_grad, smalls, wide_cosine, wide_sine, w_gate, w_up, w_down,
        experts, 0,
    )
    segment_window = lax.dynamic_slice_in_dim(
        jnp.concatenate([jnp.full((WINDOW,), -1, jnp.int32), segments]),
        device_index * row_count, (hop_count + 1) * row_count,
    )
    segment_query = segment_window[WINDOW:]
    segment_keys = segment_window.reshape(hop_count + 1, row_count)[::-1]
    attended, log_sums, residual, hidden_two, scale_two_wide = attend(
        query_low, context_blocks, segment_query[:, None], segment_keys, tokens_in, out_low,
        gains, 2,
    )
    block_out, grad_hidden_sum, grad_gate_sum, grad_gate_w, grad_up_w, grad_down = expert_layer(
        hidden_two, grad_out_all, gate_up, down_low, router_t, chosen_all, residual, 5
    )
    grad_probs = grad_gate_sum[:, :local_experts].reshape(experts, row_count).T * chosen
    grad_tokens, qkv_sum, out_sum, small_sum = attend_back(
        grad_hidden_sum, grad_probs, router_t, hidden_two, residual, scale_two_wide,
        gains, out_grad, query_low, context_blocks, segment_query[:, None], segment_keys,
        attended, log_sums, raw, scales, wide_cosine, wide_sine, hidden_one, tokens_in, qkv_low, out_low, 8,
    )
    return (
        block_out,
        grad_tokens,
        qkv_sum,
        out_sum,
        small_sum[0],
        small_sum[1],
        lax.dynamic_slice_in_dim(
            small_sum[2:6].reshape(2, heads_here, HEAD),
            device_index * qk_gain.shape[2], qk_gain.shape[2], axis=2,
        ),
        small_sum[8 : 8 + experts].T,
        grad_gate_w,
        grad_up_w,
        grad_down,
    )


def solution(mesh):
    placed = (
        P("expert", None),
        P("expert", None),
        P(None, "expert", "tensor"),
        P("tensor", "expert"),
        P("expert"),
        P("expert"),
        P(None, "tensor", "expert"),
        P("expert", None),
        P("expert", None, "tensor"),
        P("expert", None, "tensor"),
        P("expert", "tensor", None),
        P("expert", None),
        P(),
    )
    compact = (mesh.shape["expert"], mesh.shape["tensor"]) == (GROUPS, NX * NC)
    return jax.shard_map(
        fast_shards if compact else shards,
        mesh=mesh,
        in_specs=placed,
        out_specs=(
            P("expert", None),
            P("expert", None),
            P(None, "expert", "tensor"),
            P("tensor", "expert"),
            P("expert"),
            P("expert"),
            P(None, "tensor", "expert"),
            P("expert", None),
            P("expert", None, "tensor"),
            P("expert", None, "tensor"),
            P("expert", "tensor", None),
        ),
        check_vma=False,
    )
```

```python
import jax
import jax.numpy as jnp
from jax import lax
from jax.experimental import pallas as pl
from jax.experimental.pallas import tpu as pltpu
from jax.sharding import PartitionSpec as P

HEAD = 128
WINDOW = 1024
SEQ = 2048


EPS = 1e-05
THETA = 10000.0


def from_behind(value, axis, steps):
    count = lax.axis_size(axis)
    initial, last = (max(0, -steps), min(count, count - steps))
    return lax.ppermute(value, axis, [(source, source + steps) for source in range(initial, last)])


def angles(position, head_size):
    half_size = head_size // 2
    frequency = THETA ** (-(jnp.arange(half_size, dtype=jnp.float32) * 2.0 / head_size))
    phase_angle = position.astype(jnp.float32)[:, None] * frequency[None, :]
    return (jnp.cos(phase_angle)[:, None, :], jnp.sin(phase_angle)[:, None, :])


def rotate(rotated_in, cosine_table, sine_table):
    half_size = rotated_in.shape[-1] // 2
    first_half = rotated_in[..., :half_size]
    second_half = rotated_in[..., half_size:]
    return jnp.concatenate(
        [
            first_half * cosine_table - second_half * sine_table,
            second_half * cosine_table + first_half * sine_table,
        ],
        axis=-1,
    )


def slot_layout(block_routes, experts, capacity):
    flat_routes = block_routes.reshape(-1)
    onehot = (flat_routes[:, None] == jnp.arange(experts, dtype=jnp.int32)[None, :]).astype(
        jnp.int32
    )
    before = jnp.cumsum(onehot, axis=0) - onehot
    rank_within = jnp.sum(before * onehot, axis=1)
    slot_index = flat_routes * capacity + rank_within
    slot_table = (
        jnp.zeros((experts * capacity,), jnp.int32)
        .at[slot_index]
        .set(jnp.arange(flat_routes.shape[0], dtype=jnp.int32) + 1)
    )
    return (slot_index, slot_table)


def shards(
    tokens_in,
    out_grad,
    w_qkv,
    w_attn_out,
    attn_gain,
    ffn_gain,
    qk_gain,
    w_router,
    w_gate,
    w_up,
    w_down,
    routes,
    segments,
):
    row_count, model_width = tokens_in.shape
    experts = w_router.shape[1]
    per_token = routes.shape[1]
    local_experts = w_gate.shape[0]
    heads_here = qk_gain.shape[1]
    local_width = heads_here * HEAD
    groups = lax.axis_size("expert")
    device = lax.axis_index("expert")
    capacity = row_count * per_token * 3 // (2 * experts)
    hop_count = WINDOW // row_count
    buffer_shape = (groups, local_experts, capacity, model_width)
    score_scale = HEAD ** (-0.5)

    def fetch_weights():
        return (
            lax.all_gather(w_qkv.astype(jnp.bfloat16), "expert", axis=1, tiled=True),
            lax.all_gather(w_attn_out.astype(jnp.bfloat16), "expert", axis=1, tiled=True),
            lax.all_gather(w_router.astype(jnp.bfloat16), "expert", axis=0, tiled=True),
            lax.all_gather(attn_gain.astype(jnp.bfloat16), "expert", axis=0, tiled=True),
            lax.all_gather(ffn_gain.astype(jnp.bfloat16), "expert", axis=0, tiled=True),
            lax.all_gather(qk_gain.astype(jnp.bfloat16), "expert", axis=2, tiled=True),
        )

    def prepare(pieces):
        return (
            pieces[0],
            pieces[1],
            pieces[2],
            pieces[3].astype(jnp.float32),
            pieces[4].astype(jnp.float32),
            pieces[5].astype(jnp.float32).reshape(2, local_width),
        )

    qkv_low, out_low, router_low, gain_one_f, gain_two_f, qk_gains = prepare(fetch_weights())
    tokens_f = tokens_in.astype(jnp.float32)
    scale_one = lax.rsqrt(jnp.mean(tokens_f * tokens_f, axis=-1, keepdims=True) + EPS)
    hidden_one = (tokens_f * scale_one * gain_one_f).astype(jnp.bfloat16)
    projected = jnp.einsum("td,jde->jte", hidden_one, qkv_low, preferred_element_type=jnp.float32)
    query_raw = projected[0]
    key_raw = projected[1]
    query_sq, key_sq = lax.psum(
        (jnp.sum(query_raw * query_raw, axis=-1), jnp.sum(key_raw * key_raw, axis=-1)), "tensor"
    )
    query_scale = lax.rsqrt(query_sq / model_width + EPS)[:, None]
    key_scale = lax.rsqrt(key_sq / model_width + EPS)[:, None]
    normed_query = query_raw * query_scale
    normed_key = key_raw * key_scale
    global_rows = device * row_count + jnp.arange(row_count, dtype=jnp.int32)
    cosine_table, sine_table = angles(global_rows % SEQ, HEAD)
    query_low = rotate(
        (normed_query * qk_gains[0]).reshape(row_count, heads_here, HEAD), cosine_table, sine_table
    ).astype(jnp.bfloat16)
    key_low = rotate(
        (normed_key * qk_gains[1]).reshape(row_count, heads_here, HEAD), cosine_table, sine_table
    ).astype(jnp.bfloat16)
    value_low = projected[2].astype(jnp.bfloat16).reshape(row_count, heads_here, HEAD)
    own_pair = jnp.stack([key_low, value_low])
    earlier = []
    for steps_back in range(hop_count, 0, -1):
        earlier.append(from_behind(own_pair, "expert", steps_back))
    context = jnp.concatenate(earlier + [own_pair], axis=1)
    key_rows = (device - hop_count) * row_count + jnp.arange(
        (hop_count + 1) * row_count, dtype=jnp.int32
    )
    segment_keys = segments[jnp.maximum(key_rows, 0)]
    segment_query = segments[global_rows]
    distance = global_rows[:, None] - key_rows[None, :]
    allowed = (
        (key_rows[None, :] >= 0)
        & (segment_query[:, None] == segment_keys[None, :])
        & (distance >= 0)
        & (distance < WINDOW)
    )

    def score_block():
        raw_scores = (
            jnp.einsum("qhd,khd->hqk", query_low, context[0], preferred_element_type=jnp.float32)
            * score_scale
        )
        return jnp.where(allowed[None], raw_scores, -1e30)

    scores = score_block()
    largest = jnp.max(scores, axis=-1, keepdims=True)
    exp_scores = jnp.exp(scores - largest)
    exp_total = jnp.sum(exp_scores, axis=-1, keepdims=True)
    log_total = largest + jnp.log(exp_total)
    attn_probs = (exp_scores / exp_total).astype(jnp.bfloat16)
    attended = (
        jnp.einsum("hqk,khd->qhd", attn_probs, context[1], preferred_element_type=jnp.float32)
        .reshape(row_count, local_width)
        .astype(jnp.bfloat16)
    )
    attention_out = lax.psum(
        jnp.dot(attended, out_low, preferred_element_type=jnp.float32).astype(jnp.bfloat16),
        "tensor",
    ).astype(jnp.float32)
    residual = tokens_f + attention_out
    scale_two = lax.rsqrt(jnp.mean(residual * residual, axis=-1, keepdims=True) + EPS)
    normed_two = residual * scale_two
    hidden_two = (normed_two * gain_two_f).astype(jnp.bfloat16)
    logits = jnp.dot(hidden_two, router_low, preferred_element_type=jnp.float32)
    logit_exp = jnp.exp(logits - jnp.max(logits, axis=-1, keepdims=True))
    router_probs = logit_exp / jnp.sum(logit_exp, axis=-1, keepdims=True)
    chosen = routes[:, :, None] == jnp.arange(experts, dtype=jnp.int32)[None, None, :]
    gate_probs = jnp.sum(jnp.where(chosen, router_probs[:, None, :], 0.0), axis=-1)
    slot_index, slot_table = slot_layout(routes, experts, capacity)
    present = (slot_table > 0)[:, None]
    assigned = jnp.maximum(slot_table - 1, 0)
    row_of_slot = assigned // per_token
    gate_low = w_gate.astype(jnp.bfloat16)
    up_low = w_up.astype(jnp.bfloat16)
    down_low = w_down.astype(jnp.bfloat16)

    def send_rows():
        buffer_rows = jnp.where(
            present, hidden_two[row_of_slot], jnp.zeros((), jnp.bfloat16)
        ).reshape(buffer_shape)
        return lax.all_to_all(buffer_rows, "expert", split_axis=0, concat_axis=0, tiled=True)

    def expert_front(arrived):
        gate_pre = jnp.einsum(
            "secd,edh->sech", arrived, gate_low, preferred_element_type=jnp.float32
        )
        up_pre = jnp.einsum("secd,edh->sech", arrived, up_low, preferred_element_type=jnp.float32)
        return (gate_pre, up_pre)

    received = send_rows()
    gate_pre, up_pre = expert_front(received)
    activated = (gate_pre * jax.nn.sigmoid(gate_pre) * up_pre).astype(jnp.bfloat16)
    partial_value = jnp.einsum(
        "sech,ehd->secd", activated, down_low, preferred_element_type=jnp.float32
    ).astype(jnp.bfloat16)
    returned = lax.all_to_all(
        partial_value, "expert", split_axis=0, concat_axis=0, tiled=True
    ).reshape(experts * capacity, model_width)
    expert_rows = returned[slot_index].reshape(row_count, per_token, model_width)
    expert_part = jnp.einsum(
        "tk,tkd->td", gate_probs, expert_rows, preferred_element_type=jnp.float32
    )
    block_out = residual + lax.psum(expert_part.astype(jnp.bfloat16), "tensor").astype(jnp.float32)
    qkv_low, out_low, router_low, gain_one_f, gain_two_f, qk_gains = prepare(fetch_weights())
    grad_out = out_grad.astype(jnp.float32)
    grad_gate_part = jnp.einsum(
        "td,tkd->tk", grad_out, expert_rows, preferred_element_type=jnp.float32
    )
    slot_grads = (
        (gate_probs[:, :, None] * grad_out[:, None, :])
        .astype(jnp.bfloat16)
        .reshape(row_count * per_token, model_width)
    )
    grad_buffer = jnp.where(present, slot_grads[assigned], jnp.zeros((), jnp.bfloat16)).reshape(
        buffer_shape
    )
    grad_received = lax.all_to_all(grad_buffer, "expert", split_axis=0, concat_axis=0, tiled=True)
    received = send_rows()
    gate_pre, up_pre = expert_front(received)
    sigmoid_gate = jax.nn.sigmoid(gate_pre)
    swish_gate = gate_pre * sigmoid_gate
    activated = (swish_gate * up_pre).astype(jnp.bfloat16)
    grad_act = jnp.einsum(
        "secd,ehd->sech", grad_received, down_low, preferred_element_type=jnp.float32
    )
    grad_down = jnp.einsum(
        "sech,secd->ehd", activated, grad_received, preferred_element_type=jnp.float32
    )
    grad_gate_pre = (
        grad_act * up_pre * sigmoid_gate * (1.0 + gate_pre * (1.0 - sigmoid_gate))
    ).astype(jnp.bfloat16)
    grad_up_pre = (grad_act * swish_gate).astype(jnp.bfloat16)
    grad_gate_w = jnp.einsum(
        "secd,sech->edh", received, grad_gate_pre, preferred_element_type=jnp.float32
    )
    grad_up_w = jnp.einsum(
        "secd,sech->edh", received, grad_up_pre, preferred_element_type=jnp.float32
    )
    grad_rows = (
        jnp.einsum("sech,edh->secd", grad_gate_pre, gate_low, preferred_element_type=jnp.float32)
        + jnp.einsum("sech,edh->secd", grad_up_pre, up_low, preferred_element_type=jnp.float32)
    ).astype(jnp.bfloat16)
    grad_back = lax.all_to_all(
        grad_rows, "expert", split_axis=0, concat_axis=0, tiled=True
    ).reshape(experts * capacity, model_width)
    grad_hidden_part = jnp.sum(
        grad_back[slot_index].reshape(row_count, per_token, model_width), axis=1, dtype=jnp.float32
    )
    grad_hidden_sum, grad_gates = (
        lax.psum(grad_hidden_part.astype(jnp.bfloat16), "tensor").astype(jnp.float32),
        lax.psum(grad_gate_part.astype(jnp.bfloat16), "tensor").astype(jnp.float32),
    )
    grad_probs = jnp.sum(jnp.where(chosen, grad_gates[:, :, None], 0.0), axis=1)
    grad_logits = (
        router_probs * (grad_probs - jnp.sum(router_probs * grad_probs, axis=-1, keepdims=True))
    ).astype(jnp.bfloat16)
    grad_hidden_two = grad_hidden_sum + jnp.dot(
        grad_logits, router_low.T, preferred_element_type=jnp.float32
    )
    grad_router = jnp.dot(hidden_two.T, grad_logits, preferred_element_type=jnp.float32)
    grad_gain_two = jnp.sum(grad_hidden_two * normed_two, axis=0)
    scaled_two = grad_hidden_two * gain_two_f
    grad_residual = (
        grad_out
        + scale_two * scaled_two
        - residual
        * (scale_two * scale_two * scale_two)
        * jnp.mean(scaled_two * residual, axis=-1, keepdims=True)
    )
    grad_attn = grad_residual.astype(jnp.bfloat16)
    grad_out_w = jnp.dot(attended.T, grad_attn, preferred_element_type=jnp.float32)
    grad_attended = (
        jnp.dot(grad_attn, out_low.T, preferred_element_type=jnp.float32)
        .astype(jnp.bfloat16)
        .reshape(row_count, heads_here, HEAD)
    )
    attn_weights = jnp.where(allowed[None], jnp.exp(score_block() - log_total), 0.0)
    grad_weights = jnp.einsum(
        "qhd,khd->hqk", grad_attended, context[1], preferred_element_type=jnp.float32
    )
    inner_sum = jnp.sum(attn_weights * grad_weights, axis=-1, keepdims=True)
    grad_scores = (attn_weights * (grad_weights - inner_sum) * score_scale).astype(jnp.bfloat16)
    grad_query = jnp.einsum(
        "hqk,khd->qhd", grad_scores, context[0], preferred_element_type=jnp.float32
    )
    grad_keys = jnp.einsum(
        "hqk,qhd->khd", grad_scores, query_low, preferred_element_type=jnp.float32
    )
    grad_values = jnp.einsum(
        "hqk,qhd->khd",
        attn_weights.astype(jnp.bfloat16),
        grad_attended,
        preferred_element_type=jnp.float32,
    )
    grad_pair = jnp.stack([grad_keys, grad_values]).reshape(
        2, hop_count + 1, row_count, heads_here, HEAD
    )
    own_grad = grad_pair[:, hop_count]
    for steps_back in range(1, hop_count + 1):
        own_grad = own_grad + from_behind(
            grad_pair[:, hop_count - steps_back].astype(jnp.bfloat16), "expert", -steps_back
        ).astype(jnp.float32)
    grad_query_norm = rotate(grad_query, cosine_table, -sine_table).reshape(row_count, local_width)
    grad_key_norm = rotate(own_grad[0], cosine_table, -sine_table).reshape(row_count, local_width)
    grad_gain_query = jnp.sum(grad_query_norm * normed_query, axis=0)
    grad_gain_key = jnp.sum(grad_key_norm * normed_key, axis=0)
    scaled_query = grad_query_norm * qk_gains[0]
    scaled_key = grad_key_norm * qk_gains[1]
    query_inner, key_inner = lax.psum(
        (jnp.sum(scaled_query * query_raw, axis=-1), jnp.sum(scaled_key * key_raw, axis=-1)),
        "tensor",
    )
    grad_query_raw = (
        query_scale * scaled_query
        - query_raw * (query_scale * query_scale * query_scale) * query_inner[:, None] / model_width
    ).astype(jnp.bfloat16)
    grad_key_raw = (
        key_scale * scaled_key
        - key_raw * (key_scale * key_scale * key_scale) * key_inner[:, None] / model_width
    ).astype(jnp.bfloat16)
    grad_value_raw = own_grad[1].reshape(row_count, local_width).astype(jnp.bfloat16)
    grad_proj = jnp.stack([grad_query_raw, grad_key_raw, grad_value_raw])
    grad_qkv = jnp.einsum("td,jte->jde", hidden_one, grad_proj, preferred_element_type=jnp.float32)
    grad_hidden_one = lax.psum(
        jnp.einsum("jte,jde->td", grad_proj, qkv_low, preferred_element_type=jnp.float32).astype(
            jnp.bfloat16
        ),
        "tensor",
    ).astype(jnp.float32)
    grad_gain_one = jnp.sum(grad_hidden_one * tokens_f * scale_one, axis=0)
    scaled_one = grad_hidden_one * gain_one_f
    grad_tokens = (
        grad_residual
        + scale_one * scaled_one
        - tokens_f
        * (scale_one * scale_one * scale_one)
        * jnp.mean(scaled_one * tokens_f, axis=-1, keepdims=True)
    )
    grad_qk = jnp.stack([grad_gain_query, grad_gain_key]).reshape(2, heads_here, HEAD)
    reduced = (
        lax.psum_scatter(
            grad_qkv.astype(jnp.bfloat16), "expert", scatter_dimension=1, tiled=True
        ).astype(jnp.float32),
        lax.psum_scatter(
            grad_out_w.astype(jnp.bfloat16), "expert", scatter_dimension=1, tiled=True
        ).astype(jnp.float32),
        lax.psum_scatter(
            grad_router.astype(jnp.bfloat16), "expert", scatter_dimension=0, tiled=True
        ).astype(jnp.float32),
        lax.psum_scatter(
            grad_gain_one.astype(jnp.bfloat16), "expert", scatter_dimension=0, tiled=True
        ).astype(jnp.float32),
        lax.psum_scatter(
            grad_gain_two.astype(jnp.bfloat16), "expert", scatter_dimension=0, tiled=True
        ).astype(jnp.float32),
        lax.psum_scatter(
            grad_qk.astype(jnp.bfloat16), "expert", scatter_dimension=2, tiled=True
        ).astype(jnp.float32),
    )
    return (
        block_out.astype(jnp.bfloat16),
        grad_tokens.astype(jnp.bfloat16),
        reduced[0],
        reduced[1],
        reduced[3],
        reduced[4],
        reduced[5],
        reduced[2],
        grad_gate_w,
        grad_up_w,
        grad_down,
    )


MESH_ID = pl.DeviceIdType.MESH
HBM = pl.BlockSpec(memory_space=pl.ANY)
VMEM = pl.BlockSpec(memory_space=pltpu.VMEM)
NZ, NY, NX, NC = 4, 2, 2, 2
GROUPS = NZ * NY


def place():
    e = lax.axis_index("expert")
    t = lax.axis_index("tensor")
    return lax.div(e, NY), lax.rem(e, NY), lax.div(t, NC), lax.rem(t, NC)


def device(z, y, x, c):
    return (z * NY + y, x * NC + c)


def run_if(condition, body):
    if condition is None:
        body()
    else:
        pl.when(condition)(body)


def greet(partners):
    barrier = pltpu.get_barrier_semaphore()
    for target, condition in partners:
        run_if(
            condition,
            lambda target=target: pl.semaphore_signal(
                barrier, inc=1, device_id=target, device_id_type=MESH_ID
            ),
        )
    count = sum(1 for _, condition in partners if condition is None)
    for _, condition in partners:
        if condition is not None:
            count = count + condition.astype(jnp.int32)
    pl.semaphore_wait(barrier, count)


def remote(source, target_ref, send_sem, recv_sem, target):
    return pltpu.make_async_remote_copy(
        src_ref=source,
        dst_ref=target_ref,
        send_sem=send_sem,
        recv_sem=recv_sem,
        device_id=target,
        device_id_type=MESH_ID,
    )


def block_rows(block, rows):
    return pl.ds(pl.multiple_of(block * rows, rows), rows)


class LineGather:
    def __init__(self, streams, sources, views, send_sem, recv_sem, y_first=()):
        self.z, self.y, self.x, self.c = place()
        self.streams, self.sources, self.views = streams, sources, views
        self.send_sem, self.recv_sem = send_sem, recv_sem
        self.y_first = y_first
        self.has_up, self.has_down = self.z < NZ - 1, self.z > 0
        self.pending = []

    def partners(self):
        z, y, x, c = self.z, self.y, self.x, self.c
        return [
            (device(z + 1, y, x, c), z < NZ - 1),
            (device(z - 1, y, x, c), z > 0),
            (device(z, 1 - y, x, c), None),
        ]

    def exists(self, rel):
        rel = rel % 7
        if rel == 0:
            return None
        return self.z >= rel if rel < 4 else self.z + (rel - 3) < NZ

    def block(self, rel):
        y = self.y if rel < 7 else 1 - self.y
        rel = rel % 7
        z = self.z if rel == 0 else (self.z - rel if rel < 4 else self.z + (rel - 3))
        return z * NY + y

    def send(self, stream, rel, way):
        z, y, x, c = self.z, self.y, self.x, self.c
        block = self.block(rel)
        there = self.views[stream](block)
        source = self.sources[stream] if rel == 0 else there
        near = rel % 7 == 0
        if way == 0:
            target, landing = device(z + 1, y, x, c), rel + 1
        elif way == 1:
            target, landing = device(z - 1, y, x, c), rel + (4 if near else 1)
        else:
            target, landing = device(z, 1 - y, x, c), 7 + rel
        return remote(
            source,
            there,
            self.send_sem.at[stream, rel, way],
            self.recv_sem.at[stream, landing],
            target,
        )

    def forwards(self, stream, rel):
        return rel < 7 or stream in self.y_first

    def start(self, stream, rel):
        if rel % 7 < 4:
            run = self.has_up
            run_if(run, lambda: self.send(stream, rel, 0).start())
            self.pending.append((stream, rel, 0, run))
        if rel % 7 == 0 or rel % 7 >= 4:
            run = self.has_down
            run_if(run, lambda: self.send(stream, rel, 1).start())
            self.pending.append((stream, rel, 1, run))
        if rel == 0 or stream not in self.y_first:
            self.send(stream, rel, 2).start()
            self.pending.append((stream, rel, 2, None))

    def arrive(self, stream, rel):
        there = self.views[stream](self.block(rel))
        remote(
            there,
            there,
            self.send_sem.at[stream, 0, 0],
            self.recv_sem.at[stream, rel],
            device(self.z, 1 - self.y, self.x, self.c),
        ).wait_recv()

    def order(self):
        return [7, 1, 4, 8, 11, 2, 5, 9, 12, 3, 6, 10, 13]

    def run(self, hook=None):
        for stream in self.streams:
            self.start(stream, 0)
        for rel in self.order():
            def step(rel=rel):
                marks = len(self.pending)
                for stream in self.streams:
                    self.arrive(stream, rel)
                    if rel < 7:
                        self.start(stream, rel)
                    if hook is not None:
                        hook(stream, rel)
                if rel < 7:
                    late = self.pending[marks:]
                    del self.pending[marks:]
                    self.finish_later(late, rel)
            run_if(self.exists(rel), step)

    def finish_later(self, late, rel):
        self.late = getattr(self, "late", []) + [(rel, late)]

    def finish(self):
        for stream, rel, way, run in self.pending:
            run_if(run, lambda s=stream, r=rel, w=way: self.send(s, r, w).wait_send())
        for rel, late in getattr(self, "late", []):
            def body(late=late):
                for stream, rel, way, run in late:
                    run_if(run, lambda s=stream, r=rel, w=way: self.send(s, r, w).wait_send())
            run_if(self.exists(rel), body)


def cost(microseconds):
    return pl.CostEstimate(flops=0, bytes_accessed=int(microseconds * 3.0e6), transcendentals=0)


def comm_params(collective_id, megabytes=56):
    return pltpu.CompilerParams(
        collective_id=collective_id,
        has_side_effects=True,
        vmem_limit_bytes=megabytes * 1024 * 1024,
    )


def weight_gather(qkv_low, out_low, smalls, collective_id):
    parts, rows, width = qkv_low.shape
    depth, columns = out_low.shape

    def kernel(qkv, out, small, qkv_all, out_all, small_all, send_sem, recv_sem, local_sem):
        views = [
            lambda b: qkv_all.at[:, block_rows(b, rows), :],
            lambda b: out_all.at[:, block_rows(b, columns)],
            lambda b: small_all.at[b],
        ]
        line = LineGather([2, 0, 1], [qkv, out, small], views, send_sem, recv_sem)
        greet(line.partners())
        own = line.block(0)
        keep = [
            pltpu.make_async_copy(source, view(own), local_sem.at[i])
            for i, (source, view) in enumerate(zip([qkv, out, small], views))
        ]
        for copy in keep:
            copy.start()
        line.run()
        line.finish()
        for copy in keep:
            copy.wait()

    return pl.pallas_call(
        kernel,
        out_shape=(
            jax.ShapeDtypeStruct((parts, rows * GROUPS, width), jnp.bfloat16),
            jax.ShapeDtypeStruct((depth, columns * GROUPS), jnp.bfloat16),
            jax.ShapeDtypeStruct((GROUPS,) + smalls.shape, jnp.float32),
        ),
        in_specs=[HBM] * 3,
        out_specs=(HBM, HBM, HBM),
        scratch_shapes=[
            pltpu.SemaphoreType.DMA((3, 14, 3)),
            pltpu.SemaphoreType.DMA((3, 14)),
            pltpu.SemaphoreType.DMA((3,)),
        ],
        compiler_params=comm_params(collective_id),
        cost_estimate=cost(100),
        name="weight_gather",
    )(qkv_low, out_low, smalls)


def token_gather(block, collective_id):
    rows, width = block.shape
    a_cols, c_cols = width * 3 // 16, width // 8

    def kernel(own_ref, all_ref, send_sem, recv_sem, x_send, x_recv, core_send, core_recv, local_sem):
        z, y, x, c = place()

        def a_at(xx, cc):
            return pl.ds(pl.multiple_of(xx * (2 * a_cols) + cc * a_cols, 128), a_cols)

        def c_at(cc):
            return pl.ds(pl.multiple_of(4 * a_cols + cc * c_cols, 128), c_cols)

        def view(b, columns):
            return all_ref.at[block_rows(b, rows), columns]

        sources = [own_ref.at[:, a_at(x, c)], own_ref.at[:, c_at(c)]]
        views = [lambda b: view(b, a_at(x, c)), lambda b: view(b, c_at(c))]
        line = LineGather([0, 1], sources, views, send_sem, recv_sem)
        across, twin = device(z, y, 1 - x, c), device(z, y, x, 1 - c)
        greet(line.partners() + [(across, None), (twin, None)])
        keep = pltpu.make_async_copy(own_ref, all_ref.at[block_rows(line.block(0), rows), :], local_sem)
        keep.start()

        def to_twin(rel, stream, landing=False):
            b = line.block(rel)
            columns = [a_at(x, c), c_at(c), a_at(1 - x, c)][stream]
            other = [a_at(x, 1 - c), c_at(1 - c), a_at(1 - x, 1 - c)][stream]
            piece = view(b, other if landing else columns)
            return remote(piece, piece, core_send.at[rel, stream], core_recv.at[rel, stream], twin)

        def to_across(rel, landing=False):
            b = line.block(rel)
            piece = view(b, a_at(1 - x if landing else x, c))
            return remote(piece, piece, x_send.at[rel], x_recv.at[rel], across)

        def hook(stream, rel):
            if stream == 0:
                to_across(rel).start()
            to_twin(rel, stream).start()

        line.run(hook)
        for rel in line.order():
            def relay(rel=rel):
                to_across(rel, True).wait_recv()
                to_twin(rel, 2).start()
            run_if(line.exists(rel), relay)
        for rel in line.order():
            def end(rel=rel):
                to_across(rel).wait_send()
                for stream in range(3):
                    to_twin(rel, stream, True).wait_recv()
                    to_twin(rel, stream).wait_send()
            run_if(line.exists(rel), end)
        line.finish()
        keep.wait()

    return pl.pallas_call(
        kernel,
        out_shape=jax.ShapeDtypeStruct((rows * GROUPS, width), block.dtype),
        in_specs=[HBM],
        out_specs=HBM,
        scratch_shapes=[
            pltpu.SemaphoreType.DMA((2, 14, 3)),
            pltpu.SemaphoreType.DMA((2, 14)),
            pltpu.SemaphoreType.DMA((14,)),
            pltpu.SemaphoreType.DMA((14,)),
            pltpu.SemaphoreType.DMA((14, 3)),
            pltpu.SemaphoreType.DMA((14, 3)),
            pltpu.SemaphoreType.DMA,
        ],
        compiler_params=comm_params(collective_id),
        cost_estimate=cost(45),
        name="token_gather",
    )(block)


def add_into(rows, step, store):
    def body(i, carry):
        store(pl.ds(pl.multiple_of(i * step, step), step))
        return carry

    lax.fori_loop(0, rows // step, body, 0)


def group_stages(part_ref, out_ref, core_buf, x_buf, send_sem, recv_sem):
    rows, width = part_ref.shape
    half, quarter = width // 2, width // 4
    z, y, x, c = place()
    across, twin = device(z, y, 1 - x, c), device(z, y, x, 1 - c)

    def half_of(cc):
        return pl.ds(pl.multiple_of(cc * half, half), half)

    def quarter_of(xx, cc):
        return pl.ds(pl.multiple_of(cc * half + xx * quarter, quarter), quarter)

    own, from_x = out_ref.at[:, quarter_of(x, c)], out_ref.at[:, quarter_of(1 - x, c)]
    to_x = core_buf.at[:, pl.ds(pl.multiple_of((1 - x) * quarter, quarter), quarter)]
    sources = [part_ref.at[:, half_of(1 - c)], to_x, own, own, from_x]
    landings = [core_buf, x_buf, own, own, from_x]
    targets = [twin, across, across, twin, twin]

    def copy(k):
        return remote(sources[k], landings[k], send_sem.at[k], recv_sem.at[k], targets[k])

    def arrive(k, landing):
        remote(landing, landing, send_sem.at[k], recv_sem.at[k], targets[k]).wait_recv()

    def begin():
        copy(0).start()

    def core_step():
        copy(0).wait_recv()
        add_to(core_buf, core_buf, part_ref.at[:, half_of(c)], 32)
        copy(1).start()

    def x_step():
        copy(1).wait_recv()
        add_to(own, x_buf, core_buf.at[:, pl.ds(pl.multiple_of(x * quarter, quarter), quarter)], 32)
        copy(2).start()
        copy(3).start()

    def spread():
        arrive(2, from_x)
        copy(4).start()

    def end():
        arrive(3, out_ref.at[:, quarter_of(x, 1 - c)])
        arrive(4, out_ref.at[:, quarter_of(1 - x, 1 - c)])
        for k in range(5):
            copy(k).wait_send()

    return [begin, core_step, x_step, spread, end]


def group_sum(part_ref, out_ref, core_buf, x_buf, send_sem, recv_sem, meanwhile=None):
    stages = group_stages(part_ref, out_ref, core_buf, x_buf, send_sem, recv_sem)
    stages[0]()
    if meanwhile is not None:
        meanwhile()
    for stage in stages[1:]:
        stage()


def tensor_sum(part, collective_id):
    rows, width = part.shape

    def kernel(part_ref, out_ref, core_buf, x_buf, send_sem, recv_sem):
        z, y, x, c = place()
        greet([(device(z, y, 1 - x, c), None), (device(z, y, x, 1 - c), None)])
        group_sum(part_ref, out_ref, core_buf, x_buf, send_sem, recv_sem)

    return pl.pallas_call(
        kernel,
        out_shape=jax.ShapeDtypeStruct((rows, width), jnp.bfloat16),
        in_specs=[VMEM],
        out_specs=VMEM,
        scratch_shapes=[
            pltpu.VMEM((rows, width // 2), jnp.bfloat16),
            pltpu.VMEM((rows, width // 4), jnp.bfloat16),
            pltpu.SemaphoreType.DMA((5,)),
            pltpu.SemaphoreType.DMA((5,)),
        ],
        compiler_params=comm_params(collective_id, 16),
        cost_estimate=cost(17),
        name="tensor_sum",
    )(part)


Z_ORDER = (3, 0, 2, 1)


def accumulate(into, addend, step=64):
    rows = into.shape[0]
    step = min(step, rows)

    def body(i, carry):
        r = pl.ds(pl.multiple_of(i * step, step), step)
        total = into[r, :].astype(jnp.float32) + addend[r, :].astype(jnp.float32)
        into[r, :] = total.astype(into.dtype)
        return carry

    lax.fori_loop(0, rows // step, body, 0)


class LineReduce:
    def __init__(self, streams, own, y_buf, lo_buf, hi_buf, send_sem, recv_sem):
        self.z, self.y, self.x, self.c = place()
        self.streams = streams
        self.own, self.y_buf, self.lo_buf, self.hi_buf = own, y_buf, lo_buf, hi_buf
        self.send_sem, self.recv_sem = send_sem, recv_sem

    def partners(self):
        z, y, x, c = self.z, self.y, self.x, self.c
        return [
            (device(z + 1, y, x, c), z < NZ - 1),
            (device(z - 1, y, x, c), z > 0),
            (device(z, 1 - y, x, c), None),
        ]

    def copy(self, s, zz, way):
        z, y, x, c = self.z, self.y, self.x, self.c
        if way == 0:
            source, landing, target = self.own(s, zz, 1 - y), self.y_buf, device(z, 1 - y, x, c)
        elif way == 1:
            source, landing, target = self.y_buf(s, zz), self.lo_buf, device(z + 1, y, x, c)
        else:
            source, landing, target = self.y_buf(s, zz), self.hi_buf, device(z - 1, y, x, c)
        return remote(
            source, landing(s, zz), self.send_sem.at[s, zz, way], self.recv_sem.at[s, zz, way], target
        )

    def to_y(self, s, zz):
        self.copy(s, zz, 0).start()

    def take(self, s, zz, way):
        self.copy(s, zz, way).wait_recv()
        accumulate(self.y_buf(s, zz), (self.lo_buf if way == 1 else self.hi_buf)(s, zz))

    def along_z(self, s, zz):
        z = self.z
        self.copy(s, zz, 0).wait_recv()
        accumulate(self.y_buf(s, zz), self.own(s, zz, self.y))

        def upward():
            run_if(z > 0, lambda: self.take(s, zz, 1))
            self.copy(s, zz, 1).start()

        def downward():
            run_if(z < NZ - 1, lambda: self.take(s, zz, 2))
            self.copy(s, zz, 2).start()

        run_if(z < zz, upward)
        run_if(z > zz, downward)

    def home(self, done):
        for zz in range(NZ):
            def land(zz=zz):
                for s in self.streams:
                    if zz > 0:
                        self.take(s, zz, 1)
                    if zz < NZ - 1:
                        self.take(s, zz, 2)
                    done(s, self.y_buf(s, zz))
            run_if(self.z == zz, land)

    def finish(self):
        for zz in range(NZ):
            for s in self.streams:
                self.copy(s, zz, 0).wait_send()
                run_if(self.z < zz, lambda s=s, zz=zz: self.copy(s, zz, 1).wait_send())
                run_if(self.z > zz, lambda s=s, zz=zz: self.copy(s, zz, 2).wait_send())


def weight_reduce(qkv, out, smalls, collective_id):
    parts, depth, width = qkv.shape
    rows = depth // GROUPS
    out_rows, columns = out.shape[0], out.shape[1] // GROUPS

    def kernel(qkv_ref, out_ref, small_ref, qkv_sum, out_sum, small_sum,
               qkv_buf, out_buf, small_buf, send_sem, recv_sem):
        def own(s, zz, yy):
            b = zz * NY + yy
            if s < parts:
                return qkv_ref.at[s, block_rows(b, rows), :]
            if s == parts:
                return out_ref.at[:, block_rows(b, columns)]
            return small_ref.at[b]

        def slot(kind):
            def view(s, zz):
                if s < parts:
                    return qkv_buf.at[kind, zz, s]
                if s == parts:
                    return out_buf.at[kind, zz]
                return small_buf.at[kind, zz]
            return view

        streams = list(range(parts + 2))
        line = LineReduce(streams, own, slot(0), slot(1), slot(2), send_sem, recv_sem)
        greet(line.partners())
        work = [(s, zz) for s in [parts + 1, parts] + list(range(parts)) for zz in Z_ORDER]
        for s, zz in work:
            line.to_y(s, zz)
        for s, zz in work:
            line.along_z(s, zz)

        def done(s, total):
            target = qkv_sum.at[s] if s < parts else (out_sum if s == parts else small_sum)
            step = min(64, target.shape[0])

            def body(i, carry):
                r = pl.ds(pl.multiple_of(i * step, step), step)
                target[r, :] = total[r, :].astype(jnp.float32)
                return carry

            lax.fori_loop(0, target.shape[0] // step, body, 0)

        line.home(done)
        line.finish()

    return pl.pallas_call(
        kernel,
        out_shape=(
            jax.ShapeDtypeStruct((parts, rows, width), jnp.float32),
            jax.ShapeDtypeStruct((out_rows, columns), jnp.float32),
            jax.ShapeDtypeStruct(smalls.shape[1:], jnp.float32),
        ),
        in_specs=[VMEM] * 3,
        out_specs=(VMEM,) * 3,
        scratch_shapes=[
            pltpu.VMEM((3, NZ, parts, rows, width), jnp.bfloat16),
            pltpu.VMEM((3, NZ, out_rows, columns), jnp.bfloat16),
            pltpu.VMEM((3, NZ) + smalls.shape[1:], jnp.float32),
            pltpu.SemaphoreType.DMA((parts + 2, NZ, 3)),
            pltpu.SemaphoreType.DMA((parts + 2, NZ, 3)),
        ],
        compiler_params=comm_params(collective_id),
        cost_estimate=cost(120),
        name="weight_reduce",
    )(qkv, out, smalls)


def token_reduce(part, collective_id, pairs=None):
    tokens, width = part.shape
    rows = tokens // GROUPS
    half, quarter = width // 2, width // 4

    def kernel(part_ref, out_ref, core_buf, x_buf, y_buf, lo_buf, hi_buf,
               core_send, core_recv, x_send, x_recv, send_sem, recv_sem):
        z, y, x, c = place()
        across, twin = device(z, y, 1 - x, c), device(z, y, x, 1 - c)

        line = LineReduce(
            [0], lambda s, zz, yy: x_buf.at[zz * NY + yy], lambda s, zz: y_buf.at[zz],
            lambda s, zz: lo_buf.at[zz], lambda s, zz: hi_buf.at[zz], send_sem, recv_sem,
        )
        greet(line.partners() + [(across, None), (twin, None)])
        order = [(zz, flip) for zz in Z_ORDER for flip in (1, 0)]

        def number(zz, flip):
            return zz * NY + (1 - y if flip else y)

        def to_twin(zz, flip):
            b = number(zz, flip)
            return remote(
                part_ref.at[block_rows(b, rows), pl.ds(pl.multiple_of((1 - c) * half, half), half)],
                core_buf.at[b], core_send.at[zz, flip], core_recv.at[zz, flip], twin,
            )

        def to_across(zz, flip):
            b = number(zz, flip)
            return remote(
                core_buf.at[b, :, pl.ds(pl.multiple_of((1 - x) * quarter, quarter), quarter)],
                x_buf.at[b], x_send.at[zz, flip], x_recv.at[zz, flip], across,
            )

        def add_core(zz, flip):
            b = number(zz, flip)

            def store(r):
                at = pl.ds(pl.multiple_of(b * rows + r.start, 16), r.size)
                core_buf[b, r, :] = (
                    core_buf[b, r, :].astype(jnp.float32)
                    + part_ref[at, pl.ds(pl.multiple_of(c * half, half), half)].astype(jnp.float32)
                ).astype(jnp.bfloat16)

            add_into(rows, 32, store)

        def add_across(zz, flip):
            b = number(zz, flip)

            def store(r):
                x_buf[b, r, :] = (
                    x_buf[b, r, :].astype(jnp.float32)
                    + core_buf[b, r, pl.ds(pl.multiple_of(x * quarter, quarter), quarter)].astype(jnp.float32)
                ).astype(jnp.bfloat16)

            add_into(rows, 64, store)

        def stage_twin(i):
            to_twin(*order[i]).wait_recv()
            add_core(*order[i])
            to_across(*order[i]).start()

        def stage_across(i):
            zz, flip = order[i]
            to_across(zz, flip).wait_recv()
            add_across(zz, flip)
            if flip:
                line.to_y(0, zz)

        def stage_y(zz):
            line.along_z(0, zz)

        for zz, flip in order:
            to_twin(zz, flip).start()
        count = len(order)
        for i in range(count + 4):
            if i < count:
                stage_twin(i)
            if 0 <= i - 1 < count:
                stage_across(i - 1)
            if i >= 3 and (i - 3) % 2 == 0 and (i - 3) // 2 < NZ:
                stage_y(Z_ORDER[(i - 3) // 2])

        def done(s, total):
            def store(r):
                out_ref[r, :] = total[r, :]

            add_into(rows, 64, store)

        line.home(done)
        for zz, flip in order:
            to_twin(zz, flip).wait_send()
            to_across(zz, flip).wait_send()
        line.finish()

    return pl.pallas_call(
        kernel,
        out_shape=jax.ShapeDtypeStruct((rows, quarter), jnp.bfloat16),
        in_specs=[VMEM],
        out_specs=VMEM,
        scratch_shapes=[
            pltpu.VMEM((GROUPS, rows, half), jnp.bfloat16),
            pltpu.VMEM((GROUPS, rows, quarter), jnp.bfloat16),
            pltpu.VMEM((NZ, rows, quarter), jnp.bfloat16),
            pltpu.VMEM((NZ, rows, quarter), jnp.bfloat16),
            pltpu.VMEM((NZ, rows, quarter), jnp.bfloat16),
            pltpu.SemaphoreType.DMA((NZ, 2)),
            pltpu.SemaphoreType.DMA((NZ, 2)),
            pltpu.SemaphoreType.DMA((NZ, 2)),
            pltpu.SemaphoreType.DMA((NZ, 2)),
            pltpu.SemaphoreType.DMA((1, NZ, 3)),
            pltpu.SemaphoreType.DMA((1, NZ, 3)),
        ],
        compiler_params=comm_params(collective_id),
        cost_estimate=cost(60),
        name="token_reduce",
    )(part)


def gate_exchange(part, collective_id):
    groups = part.shape[0]
    tensors = NX * NC

    def kernel(part_ref, out_ref, landing, total, send_t, recv_t, send_e, recv_e):
        e = lax.axis_index("expert")
        t = lax.axis_index("tensor")
        mates = [(e, lax.rem(t + k, tensors)) for k in range(1, tensors)]
        peers = [(lax.rem(e + k, groups), t) for k in range(1, groups)]
        greet([(target, None) for target in mates + peers])
        near = [
            remote(part_ref, landing.at[k], send_t.at[k], recv_t.at[k], mates[k])
            for k in range(tensors - 1)
        ]
        for copy in near:
            copy.start()
        for copy in near:
            copy.wait_recv()
        value = part_ref[...]
        for k in range(tensors - 1):
            value = value + landing[k]
        total[...] = value
        far = [
            remote(
                total.at[lax.rem(e + k, groups)], out_ref.at[e], send_e.at[k - 1], recv_e.at[k - 1],
                peers[k - 1],
            )
            for k in range(1, groups)
        ]
        for copy in far:
            copy.start()
        out_ref[e] = total[e]
        for k in range(1, groups):
            source = out_ref.at[lax.rem(e + groups - k, groups)]
            remote(source, source, send_e.at[k - 1], recv_e.at[k - 1], peers[k - 1]).wait_recv()
        for copy in near + far:
            copy.wait_send()

    return pl.pallas_call(
        kernel,
        out_shape=jax.ShapeDtypeStruct(part.shape, jnp.float32),
        in_specs=[VMEM],
        out_specs=VMEM,
        scratch_shapes=[
            pltpu.VMEM((tensors - 1,) + part.shape, jnp.float32),
            pltpu.VMEM(part.shape, jnp.float32),
            pltpu.SemaphoreType.DMA((tensors - 1,)),
            pltpu.SemaphoreType.DMA((tensors - 1,)),
            pltpu.SemaphoreType.DMA((groups - 1,)),
            pltpu.SemaphoreType.DMA((groups - 1,)),
        ],
        compiler_params=comm_params(collective_id, 16),
        cost_estimate=cost(10),
        name="gate_exchange",
    )(part)


def dot(a, b, dims):
    return lax.dot_general(a, b, ((dims[:1], dims[1:]), ((), ())), preferred_element_type=jnp.float32)


def add_to(target, first, second, step=64):
    rows = target.shape[0]

    def body(i, carry):
        r = pl.ds(pl.multiple_of(i * step, step), step)
        total = first[r, :].astype(jnp.float32) + second[r, :].astype(jnp.float32)
        target[r, :] = total.astype(target.dtype)
        return carry

    lax.fori_loop(0, rows // step, body, 0)


def expert_layer(
    hidden_two, grad_out_all, gate_up, down, router_t, chosen_all, residual, collective_id
):
    rows, width = hidden_two.shape
    tokens = rows * GROUPS
    units = down.shape[0]
    local = 2
    hidden = units // local
    experts = router_t.shape[0]
    half, part, piece = width // 2, width // 4, width // 8
    tensors = NX * NC
    steps = GROUPS + 4
    a_cols, c_cols = width // 8, width // 4
    low = jnp.bfloat16
    wide = width // 4

    def kernel(
        own_in, dy_in, gu_ref, down_ref, router_ref, chosen_ref, x1_in,
        block_out, dh_out, gates_out, gate_w, up_w, down_w,
        h, dy, gated, dgu, dx, y_part, yc_buf, ypx_buf, ypy_buf, yqy_buf, yqx_buf, yz_sum,
        ylo_buf, yhi_buf, x1, gu_stage, d_stage,
        core_buf, px_buf, py_buf, qy_buf, qx_buf, z_sum, lo_buf, hi_buf, gate_part, gate_land,
        in_sem, own_sem, line_s, line_r, hx_s, hx_r, hc_s, hc_r, x1_sem, yc_s, yc_r, ypx_s, ypx_r, ypy_s, ypy_r,
        yqy_s, yqy_r, yqx_s, yqx_r, yz_s, yz_r, gu_sem, d_sem, core_s, core_r, px_s, px_r, py_s, py_r, qy_s, qy_r, qx_s, qx_r,
        z_s, z_r, near_s, near_r, far_s, far_r, end_s, end_r,
    ):
        z, y, x, c = place()
        e, t = lax.axis_index("expert"), lax.axis_index("tensor")
        across, twin, beside = device(z, y, 1 - x, c), device(z, y, x, 1 - c), device(z, 1 - y, x, c)
        mates = [(e, lax.rem(t + k, tensors)) for k in range(1, tensors)]
        peers = [(lax.rem(e + k, GROUPS), t) for k in range(1, GROUPS)]
        greet([(target, None) for target in mates + peers])

        def pick(values, index):
            result = values[-1]
            for k in range(len(values) - 1):
                result = jnp.where(index == k, values[k], result)
            return result

        def zz_of(j):
            return pick([z, pick([1, 0, 3, 2], z), pick([3, 3, 0, 0], z), pick([2, 2, 1, 1], z)], j)

        def is_own(i):
            return (i == 0) | ((i >= 2) & (lax.rem(i, 2) == 1))

        def block_of(i):
            return zz_of(lax.div(i, 2)) * NY + jnp.where(is_own(i), y, 1 - y)

        def flip_block(j):
            return zz_of(j) * NY + 1 - y

        def own_block(j):
            return zz_of(j) * NY + y

        def a_at(xx, cc):
            return pl.ds(pl.multiple_of(xx * (2 * a_cols) + cc * a_cols, 128), a_cols)

        def c_at(cc):
            return pl.ds(pl.multiple_of(4 * a_cols + cc * c_cols, 128), c_cols)

        def h_view(b, columns):
            return h.at[block_rows(b, rows), columns]

        line = LineGather(
            [0, 1], [own_in.at[:, a_at(x, c)], own_in.at[:, c_at(c)]],
            [lambda b: h_view(b, a_at(x, c)), lambda b: h_view(b, c_at(c))], line_s, line_r,
        )

        def h_twin(b, stream, landing=False):
            cc = 1 - c if landing else c
            piece = h_view(b, [a_at(x, cc), c_at(cc), a_at(1 - x, cc)][stream])
            return remote(piece, piece, hc_s.at[b, stream], hc_r.at[b, stream], twin)

        def h_across(b, landing=False):
            piece = h_view(b, a_at(1 - x if landing else x, c))
            return remote(piece, piece, hx_s.at[b], hx_r.at[b], across)

        def gather_event(rel):
            def body():
                b = line.block(rel)
                marks = len(line.pending)
                for stream in (0, 1):
                    line.arrive(stream, rel)
                    if rel < 7:
                        line.start(stream, rel)
                    if stream == 0:
                        h_across(b).start()
                    h_twin(b, stream).start()
                late = line.pending[marks:]
                del line.pending[marks:]
                line.finish_later(late, rel)
            run_if(line.exists(rel), body)

        def relay(i):
            b = block_of(i)
            h_across(b, True).wait_recv()
            h_twin(b, 2).start()

        for stream in (0, 1):
            line.start(stream, 0)
        keep = pltpu.make_async_copy(own_in, h.at[block_rows(z * NY + y, rows), :], own_sem)
        keep.start()

        def load(i):
            r = block_rows(block_of(i), rows)
            return pltpu.make_async_copy(dy_in.at[r, :], dy.at[r, :], in_sem.at[i])

        def start_load(i, carry):
            load(i).start()
            return carry

        lax.fori_loop(0, GROUPS, start_load, 0)
        x1_copies = [
            pltpu.make_async_copy(
                x1_in.at[:, pl.ds(pl.multiple_of(c * half + s * part + x * piece, piece), piece)],
                x1.at[:, pl.ds(s * piece, piece)], x1_sem.at[s],
            )
            for s in range(2)
        ]
        for copy in x1_copies:
            copy.start()

        def to_twin(i):
            b = block_of(i)
            return remote(
                dx.at[lax.rem(i, 2), :, pl.ds(pl.multiple_of((1 - c) * half, half), half)],
                core_buf.at[b], core_s.at[i], core_r.at[i], twin,
            )

        def p_across(i):
            b = block_of(i)
            return remote(
                core_buf.at[b, :, pl.ds(pl.multiple_of((1 - x) * piece, piece), piece)],
                px_buf.at[b], px_s.at[i], px_r.at[i], across,
            )

        def p_beside(j):
            return remote(px_buf.at[flip_block(j)], py_buf.at[j], py_s.at[j], py_r.at[j], beside)

        def q_beside(j):
            return remote(
                core_buf.at[flip_block(j), :, pl.ds(part, part)], qy_buf.at[j], qy_s.at[j], qy_r.at[j], beside
            )

        def q_across(j):
            return remote(
                qy_buf.at[j, :, pl.ds(pl.multiple_of((1 - x) * piece, piece), piece)],
                qx_buf.at[j], qx_s.at[j], qx_r.at[j], across,
            )

        def up(j, s):
            return remote(z_sum.at[s, j], lo_buf.at[s, j], z_s.at[0, s, j], z_r.at[0, s, j], device(z + 1, y, x, c))

        def down_z(j, s):
            return remote(z_sum.at[s, j], hi_buf.at[s, j], z_s.at[1, s, j], z_r.at[1, s, j], device(z - 1, y, x, c))

        def take_twin(i):
            to_twin(i).wait_recv()
            b = block_of(i)
            mine = core_buf.at[b]
            add_to(mine, mine, dx.at[lax.rem(i, 2), :, pl.ds(pl.multiple_of(c * half, half), half)], 32)
            p_across(i).start()
            pl.when(jnp.logical_not(is_own(i)))(lambda: q_beside(lax.div(i, 2)).start())

        def take_p_across(i):
            p_across(i).wait_recv()
            b = block_of(i)
            add_to(
                px_buf.at[b], px_buf.at[b],
                core_buf.at[b, :, pl.ds(pl.multiple_of(x * piece, piece), piece)],
            )

        def take_q_beside(j):
            q_beside(j).wait_recv()
            add_to(qy_buf.at[j], qy_buf.at[j], core_buf.at[own_block(j), :, pl.ds(part, part)])
            q_across(j).start()

        def take_q_across(j):
            q_across(j).wait_recv()
            add_to(
                z_sum.at[1, zz_of(j)], qx_buf.at[j], qy_buf.at[j, :, pl.ds(pl.multiple_of(x * piece, piece), piece)]
            )

        def take_p_beside(j):
            p_beside(j).wait_recv()
            add_to(z_sum.at[0, zz_of(j)], py_buf.at[j], px_buf.at[own_block(j)])

        def hop(j, k):
            zz = zz_of(j)

            def upward():
                for s in range(2):
                    if k > 0:
                        up(zz, s).wait_recv()
                        add_to(z_sum.at[s, zz], z_sum.at[s, zz], lo_buf.at[s, zz])
                    up(zz, s).start()

            def downward():
                for s in range(2):
                    if k > 0:
                        down_z(zz, s).wait_recv()
                        add_to(z_sum.at[s, zz], z_sum.at[s, zz], hi_buf.at[s, zz])
                    down_z(zz, s).start()

            pl.when((z < zz) & (z == k))(upward)
            pl.when((z > zz) & (NZ - 1 - z == k))(downward)

        def y_twin(i):
            return remote(
                y_part.at[lax.rem(i, 2), :, pl.ds(pl.multiple_of((1 - c) * half, half), half)],
                yc_buf.at[block_of(i)], yc_s.at[i], yc_r.at[i], twin,
            )

        def yp_across(i):
            b = block_of(i)
            return remote(
                yc_buf.at[b, :, pl.ds(pl.multiple_of((1 - x) * piece, piece), piece)],
                ypx_buf.at[b], ypx_s.at[i], ypx_r.at[i], across,
            )

        def yp_beside(j):
            return remote(ypx_buf.at[flip_block(j)], ypy_buf.at[j], ypy_s.at[j], ypy_r.at[j], beside)

        def yq_beside(j):
            return remote(
                yc_buf.at[flip_block(j), :, pl.ds(part, part)], yqy_buf.at[j], yqy_s.at[j], yqy_r.at[j], beside
            )

        def yq_across(j):
            return remote(
                yqy_buf.at[j, :, pl.ds(pl.multiple_of((1 - x) * piece, piece), piece)],
                yqx_buf.at[j], yqx_s.at[j], yqx_r.at[j], across,
            )

        def y_up(zz, s):
            return remote(
                yz_sum.at[s, zz], ylo_buf.at[s, zz], yz_s.at[0, s, zz], yz_r.at[0, s, zz], device(z + 1, y, x, c)
            )

        def y_down(zz, s):
            return remote(
                yz_sum.at[s, zz], yhi_buf.at[s, zz], yz_s.at[1, s, zz], yz_r.at[1, s, zz], device(z - 1, y, x, c)
            )

        def take_y_twin(i):
            y_twin(i).wait_recv()
            mine = yc_buf.at[block_of(i)]
            add_to(mine, mine, y_part.at[lax.rem(i, 2), :, pl.ds(pl.multiple_of(c * half, half), half)], 32)
            yp_across(i).start()
            pl.when(jnp.logical_not(is_own(i)))(lambda: yq_beside(lax.div(i, 2)).start())

        def take_yp_across(i):
            yp_across(i).wait_recv()
            b = block_of(i)
            add_to(
                ypx_buf.at[b], ypx_buf.at[b],
                yc_buf.at[b, :, pl.ds(pl.multiple_of(x * piece, piece), piece)],
            )
            pl.when(jnp.logical_not(is_own(i)))(lambda: yp_beside(lax.div(i, 2)).start())

        def take_yq_beside(j):
            yq_beside(j).wait_recv()
            add_to(yqy_buf.at[j], yqy_buf.at[j], yc_buf.at[own_block(j), :, pl.ds(part, part)])
            yq_across(j).start()

        def take_y_sums(j):
            zz = zz_of(j)
            yq_across(j).wait_recv()
            add_to(
                yz_sum.at[1, zz], yqx_buf.at[j], yqy_buf.at[j, :, pl.ds(pl.multiple_of(x * piece, piece), piece)]
            )
            yp_beside(j).wait_recv()
            add_to(yz_sum.at[0, zz], ypy_buf.at[j], ypx_buf.at[own_block(j)])

        def y_take(zz, s, copy, landed):
            copy(zz, s).wait_recv()
            add_to(yz_sum.at[s, zz], yz_sum.at[s, zz], landed.at[s, zz])

        def y_hop(j, k):
            zz = zz_of(j)

            def upward():
                for s in range(2):
                    if k > 0:
                        y_take(zz, s, y_up, ylo_buf)
                    y_up(zz, s).start()

            def downward():
                for s in range(2):
                    if k > 0:
                        y_take(zz, s, y_down, yhi_buf)
                    y_down(zz, s).start()

            pl.when((z < zz) & (z == k))(upward)
            pl.when((z > zz) & (NZ - 1 - z == k))(downward)

        def front(i):
            load(i).wait()
            b = block_of(i)
            pl.when(i == 0)(keep.wait)

            def landed():
                for stream in range(3):
                    h_twin(b, stream, True).wait_recv()

            pl.when(i > 0)(landed)
            r = block_rows(b, rows)
            rows_h, rows_dy = h[r, :], dy[r, :]
            logits = dot(rows_h, router_ref[...], (1, 1))
            shifted = jnp.exp(logits - jnp.max(logits, axis=-1, keepdims=True))
            probs = shifted / jnp.sum(shifted, axis=-1, keepdims=True) * chosen_ref[r, :].astype(jnp.float32)
            lane = lax.broadcasted_iota(jnp.int32, probs.shape, 1)
            line = lax.broadcasted_iota(jnp.int32, (rows, 128), 1)
            found = jnp.zeros((rows, 128), jnp.float32)
            for expert in range(local):
                at, up_at = pl.ds(expert * hidden, hidden), pl.ds((local + expert) * hidden, hidden)
                gate = jnp.sum(jnp.where(lane == e * local + expert, probs, 0.0), axis=-1, keepdims=True)
                pre = dot(rows_h, gu_ref[:, at], (1, 0))
                scale = dot(rows_h, gu_ref[:, up_at], (1, 0))
                back = dot(rows_dy, down_ref[at, :], (1, 1))
                sigmoid = jax.nn.sigmoid(pre)
                swish = pre * sigmoid
                active = swish * scale
                gated[r, at] = (active * gate).astype(low)
                found = jnp.where(line == expert, jnp.sum(active * back, axis=-1, keepdims=True), found)
                back = back * gate
                dgu[r, at] = (back * scale * sigmoid * (1.0 + pre * (1.0 - sigmoid))).astype(low)
                dgu[r, up_at] = (back * swish).astype(low)
            gate_part[b] = jnp.transpose(found)[:8, :]

        def rear(i):
            r = block_rows(block_of(i), rows)
            slot = lax.rem(i, 2)
            pl.when(i >= 2)(lambda: to_twin(i - 2).wait_send())

            def columns(k, carry):
                at = pl.ds(pl.multiple_of(k * wide, wide), wide)
                dx[slot, :, at] = dot(dgu[r, :], gu_ref[at, :], (1, 1)).astype(low)
                return carry

            lax.fori_loop(0, width // wide, columns, 0)
            to_twin(i).start()
            pl.when(i >= 2)(lambda: y_twin(i - 2).wait_send())

            def y_columns(k, carry):
                at = pl.ds(pl.multiple_of(k * wide, wide), wide)
                y_part[slot, :, at] = dot(gated[r, :], down_ref[:, at], (1, 0)).astype(low)
                return carry

            lax.fori_loop(0, width // wide, y_columns, 0)
            y_twin(i).start()

        tile_width = piece // 2
        tiles = width // tile_width // 4
        d_width = width // 8

        def gu_copies(n):
            slot = lax.rem(n, 2)
            at = pl.ds(pl.multiple_of(n * tile_width, tile_width), tile_width)
            return [
                pltpu.make_async_copy(
                    gu_stage.at[slot, :, pl.ds(k * hidden, hidden)],
                    (gate_w if k < local else up_w).at[k % local, at, :],
                    gu_sem.at[slot, k],
                )
                for k in range(2 * local)
            ]

        def d_copies(n):
            slot = lax.rem(n, 2)
            at = pl.ds(pl.multiple_of(n * d_width, d_width), d_width)
            return [
                pltpu.make_async_copy(
                    d_stage.at[slot, pl.ds(k * hidden, hidden), :], down_w.at[k, :, at], d_sem.at[slot, k]
                )
                for k in range(local)
            ]

        def each(copies, what):
            for copy in copies:
                getattr(copy, what)()

        def weight_grads(q):
            def tile(k, carry):
                n = q * tiles + k
                pl.when(n >= 2)(lambda: each(gu_copies(n - 2), "wait"))
                at = pl.ds(pl.multiple_of(n * tile_width, tile_width), tile_width)
                gu_stage[lax.rem(n, 2)] = dot(h[:, at], dgu[...], (0, 0))
                each(gu_copies(n), "start")
                return carry

            lax.fori_loop(0, tiles, tile, 0)

            def d_tile(k, carry):
                n = q * 2 + k
                pl.when(n >= 2)(lambda: each(d_copies(n - 2), "wait"))
                at = pl.ds(pl.multiple_of(n * d_width, d_width), d_width)
                d_stage[lax.rem(n, 2)] = dot(gated[...], dy[:, at], (0, 0))
                each(d_copies(n), "start")
                return carry

            lax.fori_loop(0, 2, d_tile, 0)

        near = [
            remote(gate_part, gate_land.at[k], near_s.at[k], near_r.at[k], mates[k])
            for k in range(tensors - 1)
        ]

        def far(k):
            return remote(
                gate_land.at[tensors - 1, lax.rem(e + k, GROUPS)], gates_out.at[e],
                far_s.at[k - 1], far_r.at[k - 1], peers[k - 1],
            )

        def sum_near():
            for copy in near:
                copy.wait_recv()
            total = gate_part[...]
            for k in range(tensors - 1):
                total = total + gate_land[k]
            gate_land[tensors - 1] = total
            for k in range(1, GROUPS):
                far(k).start()
            gates_out[e] = gate_land[tensors - 1, e]

        def step(i, carry):
            def at(number, body):
                pl.when(i == number)(body)

            odd, even = lax.rem(i, 2) == 1, lax.rem(i, 2) == 0
            j_even, j_odd = lax.div(i, 2) - 1, lax.div(i - 1, 2) - 1
            pl.when(i < GROUPS)(lambda: front(i))

            def events(*rels):
                for rel in rels:
                    gather_event(rel)

            at(1, lambda: events(2, 5, 8, 11))
            at(2, lambda: events(3, 6))
            at(3, lambda: events(10, 13))

            pl.when((i >= 1) & (i <= GROUPS))(lambda: take_twin(i - 1))
            pl.when(even & (i >= 4) & (i <= GROUPS))(lambda: take_q_beside(j_even))
            at(3, lambda: take_q_beside(0))
            at(4, lambda: take_q_across(0))

            def late():
                take_p_across(i - 2)
                pl.when(i > 3)(lambda: take_q_across(j_odd))
                pl.when(i == 3)(lambda: p_beside(0).start())

            pl.when(odd & (i >= 3) & (i <= GROUPS + 1))(late)
            at(GROUPS, lambda: each(near, "start"))
            at(GROUPS + 1, sum_near)
            pl.when(i < GROUPS)(lambda: rear(i))
            pl.when(i >= GROUPS)(lambda: weight_grads(i - GROUPS))
            at(0, lambda: events(7, 1, 4))
            at(2, lambda: events(9, 12))
            pl.when(i < GROUPS - 1)(lambda: relay(i + 1))

            def pass_p():
                take_p_across(i - 2)
                pl.when(i > 2)(lambda: p_beside(j_even).start())

            pl.when(even & (i >= 2) & (i <= GROUPS))(pass_p)
            at(4, lambda: take_p_beside(0))

            def join():
                take_p_beside(j_odd)
                hop(j_odd, 0)

            pl.when(odd & (i >= 5) & (i <= GROUPS + 1))(join)
            pl.when((i == GROUPS) | (i == GROUPS + 2))(lambda: hop(j_even - 1, 1))
            at(GROUPS + 1, lambda: hop(1, 2))
            pl.when((i >= 2) & (i <= GROUPS + 1))(lambda: take_yp_across(i - 2))
            pl.when((i >= 1) & (i <= GROUPS))(lambda: take_y_twin(i - 1))
            pl.when(even & (i >= 4) & (i <= GROUPS))(lambda: take_yq_beside(j_even))
            at(3, lambda: take_yq_beside(0))
            at(5, lambda: take_y_sums(0))

            def join_y():
                take_y_sums(j_even - 1)
                y_hop(j_even - 1, 0)

            pl.when(even & (i >= 6) & (i <= GROUPS + 2))(join_y)
            pl.when((i == GROUPS + 1) | (i == GROUPS + 3))(lambda: y_hop(j_odd - 1, 1))
            at(GROUPS + 2, lambda: y_hop(1, 2))
            return carry

        lax.fori_loop(0, steps, step, 0)

        def columns_of(s, xx, cc):
            return pl.ds(pl.multiple_of(cc * half + s * part + xx * piece, piece), piece)

        mine = z
        for s in range(2):
            def below(s=s):
                up(mine, s).wait_recv()
                add_to(z_sum.at[s, mine], z_sum.at[s, mine], lo_buf.at[s, mine])

            def above(s=s):
                down_z(mine, s).wait_recv()
                add_to(z_sum.at[s, mine], z_sum.at[s, mine], hi_buf.at[s, mine])

            pl.when(z > 0)(below)
            pl.when(z < NZ - 1)(above)
            own = dh_out.at[:, columns_of(s, x, c)]

            def keep(k, carry, s=s, own=own):
                r = pl.ds(pl.multiple_of(k * 64, 64), 64)
                own[r, :] = z_sum[s, mine, r, :]
                return carry

            lax.fori_loop(0, rows // 64, keep, 0)
            remote(own, own, end_s.at[0, s], end_r.at[0, s], across).start()
            remote(own, own, end_s.at[1, s], end_r.at[1, s], twin).start()
        for copy in x1_copies:
            copy.wait()
        for s in range(2):
            pl.when(z > 0)(lambda s=s: y_take(z, s, y_up, ylo_buf))
            pl.when(z < NZ - 1)(lambda s=s: y_take(z, s, y_down, yhi_buf))
            y_own = block_out.at[:, columns_of(s, x, c)]

            def finish(k, carry, s=s, y_own=y_own):
                r = pl.ds(pl.multiple_of(k * 64, 64), 64)
                y_own[r, :] = (
                    x1[r, pl.ds(s * piece, piece)] + yz_sum[s, z, r, :].astype(jnp.float32)
                ).astype(low)
                return carry

            lax.fori_loop(0, rows // 64, finish, 0)
            remote(y_own, y_own, end_s.at[0, 2 + s], end_r.at[0, 2 + s], across).start()
            remote(y_own, y_own, end_s.at[1, 2 + s], end_r.at[1, 2 + s], twin).start()
        for s in range(2):
            there = dh_out.at[:, columns_of(s, 1 - x, c)]
            remote(there, there, end_s.at[0, s], end_r.at[0, s], across).wait_recv()
            remote(there, there, end_s.at[2, s], end_r.at[2, s], twin).start()
        for s in range(2):
            there = block_out.at[:, columns_of(s, 1 - x, c)]
            remote(there, there, end_s.at[0, 2 + s], end_r.at[0, 2 + s], across).wait_recv()
            remote(there, there, end_s.at[2, 2 + s], end_r.at[2, 2 + s], twin).start()
        for n, result in ((0, dh_out), (2, block_out)):
            for s in range(2):
                for k, xx in ((1, x), (2, 1 - x)):
                    there = result.at[:, columns_of(s, xx, 1 - c)]
                    remote(there, there, end_s.at[k, n + s], end_r.at[k, n + s], twin).wait_recv()
                for k, target in ((0, across), (1, twin), (2, twin)):
                    there = result.at[:, columns_of(s, 1 - x if k == 2 else x, c)]
                    remote(there, there, end_s.at[k, n + s], end_r.at[k, n + s], target).wait_send()
        for k in range(1, GROUPS):
            there = gates_out.at[lax.rem(e + GROUPS - k, GROUPS)]
            remote(there, there, far_s.at[k - 1], far_r.at[k - 1], peers[k - 1]).wait_recv()
            far(k).wait_send()
        each(near, "wait_send")

        def drain(i, carry):
            pl.when(i >= GROUPS - 2)(lambda: to_twin(i).wait_send())
            pl.when(i >= GROUPS - 2)(lambda: y_twin(i).wait_send())
            p_across(i).wait_send()
            yp_across(i).wait_send()
            return carry

        lax.fori_loop(0, GROUPS, drain, 0)

        def drain_pair(j, carry):
            p_beside(j).wait_send()
            q_beside(j).wait_send()
            q_across(j).wait_send()
            yp_beside(j).wait_send()
            yq_beside(j).wait_send()
            yq_across(j).wait_send()
            for s in range(2):
                pl.when(z < j)(lambda s=s: up(j, s).wait_send())
                pl.when(z > j)(lambda s=s: down_z(j, s).wait_send())
                pl.when(z < j)(lambda s=s: y_up(j, s).wait_send())
                pl.when(z > j)(lambda s=s: y_down(j, s).wait_send())
            return carry

        lax.fori_loop(0, NZ, drain_pair, 0)

        def drain_rows_of(i, carry):
            b = block_of(i)
            h_across(b).wait_send()
            for stream in range(3):
                h_twin(b, stream).wait_send()
            return carry

        lax.fori_loop(1, GROUPS, drain_rows_of, 0)
        line.finish()
        for k in range(2):
            each(gu_copies(4 * tiles - 2 + k), "wait")
            each(d_copies(6 + k), "wait")

    shape = jax.ShapeDtypeStruct
    dma = pltpu.SemaphoreType.DMA
    f32 = jnp.float32
    return pl.pallas_call(
        kernel,
        out_shape=(
            shape((rows, width), low),
            shape((rows, width), low),
            shape((GROUPS, 8, rows), f32),
            shape((local, width, hidden), f32),
            shape((local, width, hidden), f32),
            shape((local, hidden, width), f32),
        ),
        in_specs=[HBM, HBM, VMEM, VMEM, VMEM, VMEM, HBM],
        out_specs=(VMEM, VMEM, VMEM, HBM, HBM, HBM),
        scratch_shapes=[
            pltpu.VMEM((tokens, width), low),
            pltpu.VMEM((tokens, width), low),
            pltpu.VMEM((tokens, units), low),
            pltpu.VMEM((tokens, 2 * units), low),
            pltpu.VMEM((2, rows, width), low),
            pltpu.VMEM((2, rows, width), low),
            pltpu.VMEM((GROUPS, rows, half), low),
            pltpu.VMEM((GROUPS, rows, piece), low),
            pltpu.VMEM((NZ, rows, piece), low),
            pltpu.VMEM((NZ, rows, part), low),
            pltpu.VMEM((NZ, rows, piece), low),
            pltpu.VMEM((2, NZ, rows, piece), low),
            pltpu.VMEM((2, NZ, rows, piece), low),
            pltpu.VMEM((2, NZ, rows, piece), low),
            pltpu.VMEM((rows, part), f32),
            pltpu.VMEM((2, piece // 2, 2 * units), f32),
            pltpu.VMEM((2, units, width // 8), f32),
            pltpu.VMEM((GROUPS, rows, half), low),
            pltpu.VMEM((GROUPS, rows, piece), low),
            pltpu.VMEM((NZ, rows, piece), low),
            pltpu.VMEM((NZ, rows, part), low),
            pltpu.VMEM((NZ, rows, piece), low),
            pltpu.VMEM((2, NZ, rows, piece), low),
            pltpu.VMEM((2, NZ, rows, piece), low),
            pltpu.VMEM((2, NZ, rows, piece), low),
            pltpu.VMEM((GROUPS, 8, rows), f32),
            pltpu.VMEM((tensors, GROUPS, 8, rows), f32),
            dma((GROUPS,)), dma, dma((2, 14, 3)), dma((2, 14)), dma((GROUPS,)), dma((GROUPS,)),
            dma((GROUPS, 3)), dma((GROUPS, 3)), dma((2,)), dma((GROUPS,)), dma((GROUPS,)), dma((GROUPS,)), dma((GROUPS,)),
            dma((NZ,)), dma((NZ,)), dma((NZ,)), dma((NZ,)), dma((NZ,)), dma((NZ,)),
            dma((2, 2, NZ)), dma((2, 2, NZ)), dma((2, 2 * local)), dma((2, local)),
            dma((GROUPS,)), dma((GROUPS,)), dma((GROUPS,)), dma((GROUPS,)),
            dma((NZ,)), dma((NZ,)), dma((NZ,)), dma((NZ,)), dma((NZ,)), dma((NZ,)),
            dma((2, 2, NZ)), dma((2, 2, NZ)),
            dma((tensors - 1,)), dma((tensors - 1,)), dma((GROUPS - 1,)), dma((GROUPS - 1,)),
            dma((3, 4)), dma((3, 4)),
        ],
        compiler_params=comm_params(collective_id, 62),
        cost_estimate=cost(80),
        name="expert_layer",
    )(hidden_two, grad_out_all, gate_up, down, router_t, chosen_all, residual)


def exchange_rows(value, part_ref, land_ref, send_sem, recv_sem, mates):
    rows = value.shape[0]
    line = lax.broadcasted_iota(jnp.int32, (rows, 128), 1)
    part_ref[...] = jnp.transpose(jnp.where(line == 0, value, 0.0))[:8, :]
    for k, mate in enumerate(mates):
        remote(part_ref, land_ref.at[k], send_sem.at[k], recv_sem.at[k], mate).start()


def exchanged_rows(part_ref, land_ref, send_sem, recv_sem, mates):
    total = part_ref[...]
    for k, mate in enumerate(mates):
        remote(part_ref, land_ref.at[k], send_sem.at[k], recv_sem.at[k], mate).wait_recv()
    for k in range(len(mates)):
        total = total + land_ref[k]
    rows = part_ref.shape[1]
    tall = jnp.concatenate([total, jnp.zeros((120, rows), jnp.float32)], axis=0)
    return jnp.transpose(tall)[:, :1]


def drain_rows(part_ref, land_ref, send_sem, recv_sem, mates):
    for k, mate in enumerate(mates):
        remote(part_ref, land_ref.at[k], send_sem.at[k], recv_sem.at[k], mate).wait_send()


def turn(value, cosine, sine):
    return value * cosine + pltpu.roll(value, HEAD // 2, 1) * sine


def project(
    tokens, w_qkv, w_out, out_grad, smalls, cosine, sine, w_gate, w_up, w_down, experts, collective_id
):
    rows, width = tokens.shape
    parts, depth, columns = w_qkv.shape
    heads = columns // HEAD
    tensors = NX * NC
    back = WINDOW // rows
    low, f32 = jnp.bfloat16, jnp.float32
    QUERY, KEY, VALUE, SMALL, OUT, GRAD, REST = 0, 1, 2, 3, 4, 5, 6
    out_half = w_out.shape[0] // 2
    out_rows, out_columns = w_out.shape
    quarter = width // tensors

    def kernel(
        tok_ref, w_ref, out_ref, grad_in, small_ref, cos_ref, sin_ref, gate_in, up_in, down_in,
        w_all, out_all, grad_all, h1_out, raw_out, gate_up, down_out, gain_ref, router_ref, chosen_ref, scale_ref, q_ref, context,
        small_all, h1_ref, raw_ref, wide_in, wide_low, down_f, down_low, own_w, own_out, weights, total, part_k, land_k, part_q, land_q,
        send_sem, recv_sem, out_sem, small_sem, kept, ks_s, ks_r, qs_s, qs_r, c_s, c_r, hx_s, hx_r, hc_s, hc_r, wide_s,
    ):
        z, y, x, c = place()
        e, t = lax.axis_index("expert"), lax.axis_index("tensor")
        wide_loads = [
            pltpu.make_async_copy(source.at[k], wide_in.at[2 * n + k], wide_s.at[2 * n + k])
            for n, source in enumerate((gate_in, up_in))
            for k in range(2)
        ]
        for copy in wide_loads:
            copy.start()
        mates = [(e, lax.rem(t + k, tensors)) for k in range(1, tensors)]
        beside, above = device(z, 1 - y, x, c), device(z + 1, y, x, c)
        views = [
            lambda b: weights.at[QUERY, block_rows(b, depth), :],
            lambda b: weights.at[KEY, block_rows(b, depth), :],
            lambda b: weights.at[VALUE, block_rows(b, depth), :],
            lambda b: small_all.at[b],
            lambda b: out_all.at[pl.ds(0, out_half), block_rows(b, out_columns)],
            lambda b: grad_view(b, x, c),
            lambda b: out_all.at[pl.ds(out_half, out_half), block_rows(b, out_columns)],
        ]
        across, twin = device(z, y, 1 - x, c), device(z, y, x, 1 - c)

        def quarter_at(xx, cc):
            return pl.ds(pl.multiple_of((xx * NC + cc) * quarter, quarter), quarter)

        def grad_view(b, xx, cc):
            return grad_all.at[block_rows(b, rows), quarter_at(xx, cc)]

        def grad_across(b, landing=False):
            piece = grad_view(b, 1 - x if landing else x, c)
            return remote(piece, piece, hx_s.at[b], hx_r.at[b], across)

        def grad_twin(b, relayed, landing=False):
            piece = grad_view(b, 1 - x if relayed else x, 1 - c if landing else c)
            return remote(piece, piece, hc_s.at[b, relayed], hc_r.at[b, relayed], twin)

        line = LineGather(
            [SMALL, VALUE, KEY, QUERY, OUT, GRAD, REST],
            [
                own_w.at[0], own_w.at[1], own_w.at[2], small_ref, own_out.at[pl.ds(0, out_half)],
                grad_in.at[:, quarter_at(x, c)], own_out.at[pl.ds(out_half, out_half)],
            ],
            views, send_sem, recv_sem, y_first=(OUT,),
        )
        greet(line.partners() + [(mate, None) for mate in mates])
        line.start(SMALL, 0)
        for part in (VALUE, KEY, QUERY):
            def cast(i, carry, part=part):
                r = pl.ds(pl.multiple_of(i * 32, 32), 32)
                own_w[part, r, :] = w_ref[part, r, :].astype(low)
                return carry

            lax.fori_loop(0, depth // 32, cast, 0)
            if part != QUERY:
                line.start(part, 0)

        def cast_out(i, carry):
            r = pl.ds(pl.multiple_of(i * 32, 32), 32)
            own_out[r, :] = out_ref[r, :].astype(low)
            return carry

        lax.fori_loop(0, out_rows // 32, cast_out, 0)
        keep_out = pltpu.make_async_copy(own_out, out_all.at[:, block_rows(line.block(0), out_columns)], kept.at[0])
        keep_out.start()
        keep_grad = pltpu.make_async_copy(grad_in, grad_all.at[block_rows(line.block(0), rows), :], kept.at[1])
        keep_grad.start()

        def square(i, carry):
            r = pl.ds(pl.multiple_of(i * 32, 32), 32)
            value = tok_ref[r, :].astype(f32)
            scale_ref[r, 0:1] = lax.rsqrt(jnp.mean(value * value, axis=-1, keepdims=True) + EPS)
            return carry

        lax.fori_loop(0, rows // 32, square, 0)
        total[...] = jnp.zeros_like(total)
        own_small = pltpu.make_async_copy(small_ref, small_all.at[line.block(0)], small_sem)
        own_small.start()

        def use(stream, rel):
            b = line.block(rel)
            at = pl.ds(pl.multiple_of(b * depth, depth), depth)
            if stream == SMALL:
                gain = small_ref[0:1, :] if rel == 0 else small_all[b, 0:1, :]
                h1_ref[:, at] = (tok_ref[:, at].astype(f32) * scale_ref[:, 0:1] * gain).astype(low)
                return
            block = own_w[stream] if rel == 0 else weights[stream, block_rows(b, depth), :]
            total[stream] += dot(h1_ref[:, at], block, (1, 0))

        def event(stream, rel):
            def body():
                line.arrive(stream, rel)
                if line.forwards(stream, rel):
                    marks = len(line.pending)
                    line.start(stream, rel)
                    late = line.pending[marks:]
                    del line.pending[marks:]
                    line.finish_later(late, rel)
                if stream == GRAD:
                    b = line.block(rel)
                    grad_across(b).start()
                    grad_twin(b, 0).start()
                elif stream not in (OUT, REST):
                    use(stream, rel)
            run_if(line.exists(rel), body)

        use(SMALL, 0)
        use(VALUE, 0)
        own_small.wait()

        units = down_in.shape[1]
        for n, copy in enumerate(wide_loads):
            copy.wait()

            def round_wide(i, carry, n=n):
                r = pl.ds(pl.multiple_of(i * 64, 64), 64)
                wide_low[r, pl.ds(n * units, units)] = wide_in[n, r, :].astype(low)
                return carry

            lax.fori_loop(0, width // 64, round_wide, 0)
        wide_out = pltpu.make_async_copy(wide_low, gate_up, wide_s.at[0])
        wide_out.start()
        down_loads = [
            pltpu.make_async_copy(down_in.at[k], down_f.at[pl.ds(k * units, units), :], wide_s.at[1 + k])
            for k in range(2)
        ]
        for copy in down_loads:
            copy.start()

        use(KEY, 0)
        def events(*pairs):
            for stream, rels in pairs:
                for rel in rels:
                    event(stream, rel)

        for rel in (7, 1, 4, 2, 5):
            event(SMALL, rel)
            event(VALUE, rel)
        for copy in down_loads:
            copy.wait()

        def round_down(i, carry):
            r = pl.ds(pl.multiple_of(i * 32, 32), 32)
            down_low[r, :] = down_f[r, :].astype(low)
            return carry

        lax.fori_loop(0, 2 * units // 32, round_down, 0)
        down_copy = pltpu.make_async_copy(down_low, down_out, wide_s.at[3])
        down_copy.start()
        line.start(QUERY, 0)
        for rel in (3, 6):
            event(SMALL, rel)
            event(VALUE, rel)
        events((KEY, (7, 1, 4)))
        for rel in (8, 11, 9, 12, 10, 13):
            event(SMALL, rel)
            event(VALUE, rel)

        slices = HEAD // GROUPS
        for b in range(GROUPS):
            at = pl.ds(b * depth, depth)
            gain_ref[0:2, at] = small_all[b, 0:2, :]
            router_ref[:, at] = small_all[b, 8 : 8 + experts, :].astype(low)
            tall = jnp.concatenate(
                [small_all[b, 8 + experts : 8 + 2 * experts, :], jnp.zeros((128 - experts, depth), f32)], axis=0
            )
            chosen_ref[pl.ds(b * depth, depth), :] = jnp.transpose(tall)[:, :experts].astype(low)
        for which in range(2):
            for head in range(heads):
                start = (which * heads + head) * slices
                gain_ref[2 + which : 3 + which, pl.ds(head * HEAD, HEAD)] = jnp.concatenate(
                    [small_all[b, 2:3, start : start + slices] for b in range(GROUPS)], axis=1
                )

        def context_copy(which, k):
            if k == 2:
                source, target = 0, above
            elif k == 4:
                source, target = 2, above
            else:
                source, target = jnp.where(y == 0, k - 1, k + 1), beside
            return remote(
                context.at[source, which], context.at[k, which], c_s.at[which, k], c_r.at[which, k], target
            )

        sends = {2: z < NZ - 1, 4: (z >= 1) & (z < NZ - 1), 1: (y == 0) | (z >= 1), 3: z >= 1 + y}
        takes = {2: z >= 1, 4: z >= 2, 1: (y == 1) | (z >= 1), 3: z >= 2 - y}

        def context_send(which, k):
            run_if(sends[k], lambda: context_copy(which, k).start())

        def context_take(which, k):
            run_if(takes[k], lambda: context_copy(which, k).wait_recv())

        for k in range(1, back + 1):
            def clear(k=k):
                context[k] = jnp.zeros_like(context[k])
            run_if(jnp.logical_not(takes[k]), clear)

        context[0, 1] = total[VALUE].astype(low)
        context_send(1, 2)
        run_if(y == 0, lambda: context_copy(1, 1).start())
        events((KEY, (2, 5, 3, 6)), (QUERY, (7, 1, 4)))
        line.start(GRAD, 0)
        line.start(OUT, 0)
        line.start(REST, 0)
        events((KEY, (8, 11, 9, 12, 10, 13)))
        key_raw = total[KEY]
        raw_ref[1] = key_raw
        exchange_rows(jnp.sum(key_raw * key_raw, axis=-1, keepdims=True), part_k, land_k, ks_s, ks_r, mates)
        use(QUERY, 0)
        events((QUERY, (2, 5)))
        key_scale = lax.rsqrt(exchanged_rows(part_k, land_k, ks_s, ks_r, mates) / width + EPS)
        scale_ref[:, 2:3] = key_scale
        def rotated(which, scale, store):
            for head in range(heads):
                at = pl.ds(head * HEAD, HEAD)
                value = total[which, :, at] * scale * gain_ref[2 + which : 3 + which, at]
                store(at, turn(value, cos_ref[...], sin_ref[...]).astype(low))

        def store_key(at, value):
            context[0, 0, :, at] = value

        rotated(KEY, key_scale, store_key)
        context_send(0, 2)
        run_if(y == 0, lambda: context_copy(0, 1).start())

        def relay_two(which):
            context_take(which, 2)
            context_send(which, 4)
            run_if((y == 1) & (z >= 1), lambda: context_copy(which, 1).start())
            run_if((y == 0) & sends[3], lambda: context_copy(which, 3).start())

        def relay_four(which):
            context_take(which, 4)
            run_if((y == 1) & sends[3], lambda: context_copy(which, 3).start())

        relay_two(1)
        events((QUERY, (3, 6)), (GRAD, (7, 1, 4)), (OUT, (7, 1, 4)), (REST, (7, 1, 4)))
        relay_four(1)
        events((QUERY, (8, 11)), (GRAD, (2, 5)), (OUT, (8, 11, 2, 5)), (REST, (2, 5)))
        relay_two(0)
        events((QUERY, (9, 12, 10, 13)))
        query_raw = total[QUERY]
        raw_ref[0] = query_raw
        exchange_rows(jnp.sum(query_raw * query_raw, axis=-1, keepdims=True), part_q, land_q, qs_s, qs_r, mates)
        for part in range(parts):
            weights[part, block_rows(line.block(0), depth), :] = own_w[part]
        keep = pltpu.make_async_copy(weights, w_all, out_sem)
        keep.start()
        keep_more = [
            pltpu.make_async_copy(h1_ref, h1_out, kept.at[2]),
            pltpu.make_async_copy(raw_ref, raw_out, kept.at[3]),
        ]
        for copy in keep_more:
            copy.start()
        events((GRAD, (3, 6)), (OUT, (9, 12, 3, 6)), (REST, (3, 6, 8, 11)))
        relay_four(0)
        query_scale = lax.rsqrt(exchanged_rows(part_q, land_q, qs_s, qs_r, mates) / width + EPS)
        scale_ref[:, 1:2] = query_scale

        def store_query(at, value):
            q_ref[:, at] = value

        rotated(QUERY, query_scale, store_query)
        events((GRAD, (8, 11, 9, 12)), (OUT, (10, 13)), (REST, (9, 12, 10, 13)), (GRAD, (10, 13)))
        for which in (1, 0):
            for k in (1, 3):
                context_take(which, k)
        for rel in line.order():
            def relay(rel=rel):
                b = line.block(rel)
                grad_across(b, True).wait_recv()
                grad_twin(b, 1).start()
            run_if(line.exists(rel), relay)
        for rel in line.order():
            def landed(rel=rel):
                b = line.block(rel)
                grad_across(b).wait_send()
                for relayed in range(2):
                    grad_twin(b, relayed, True).wait_recv()
                    grad_twin(b, relayed).wait_send()
            run_if(line.exists(rel), landed)
        line.finish()
        for copy in keep_more:
            copy.wait()
        wide_out.wait()
        down_copy.wait()
        keep_out.wait()
        keep_grad.wait()
        for which in range(2):
            for k in range(1, back + 1):
                run_if(sends[k], lambda which=which, k=k: context_copy(which, k).wait_send())
        drain_rows(part_k, land_k, ks_s, ks_r, mates)
        drain_rows(part_q, land_q, qs_s, qs_r, mates)
        keep.wait()

    shape, dma = jax.ShapeDtypeStruct, pltpu.SemaphoreType.DMA
    return pl.pallas_call(
        kernel,
        out_shape=(
            shape((parts, depth * GROUPS, columns), low),
            shape((out_rows, out_columns * GROUPS), low),
            shape((rows * GROUPS, width), low),
            shape((rows, width), low),
            shape((2, rows, columns), f32),
            shape((width, 4 * w_down.shape[1]), low),
            shape((2 * w_down.shape[1], width), low),
            shape((8, width), f32),
            shape((experts, width), low),
            shape((rows * GROUPS, experts), low),
            shape((rows, 128), f32),
            shape((rows, columns), low),
            shape((back + 1, 2, rows, columns), low),
        ),
        in_specs=[VMEM, VMEM, VMEM, HBM, VMEM, VMEM, VMEM, HBM, HBM, HBM],
        out_specs=(HBM,) * 7 + (VMEM,) * 6,
        scratch_shapes=[
            pltpu.VMEM((GROUPS,) + smalls.shape, f32),
            pltpu.VMEM((rows, width), low),
            pltpu.VMEM((2, rows, columns), f32),
            pltpu.VMEM((4, width, w_down.shape[1]), f32),
            pltpu.VMEM((width, 4 * w_down.shape[1]), low),
            pltpu.VMEM((2 * w_down.shape[1], width), f32),
            pltpu.VMEM((2 * w_down.shape[1], width), low),
            pltpu.VMEM((parts, depth, columns), low),
            pltpu.VMEM((out_rows, out_columns), low),
            pltpu.VMEM((parts, depth * GROUPS, columns), low),
            pltpu.VMEM((parts, rows, columns), f32),
            pltpu.VMEM((8, rows), f32),
            pltpu.VMEM((tensors - 1, 8, rows), f32),
            pltpu.VMEM((8, rows), f32),
            pltpu.VMEM((tensors - 1, 8, rows), f32),
            dma((7, 14, 3)), dma((7, 14)), dma, dma, dma((4,)),
            dma((tensors - 1,)), dma((tensors - 1,)), dma((tensors - 1,)), dma((tensors - 1,)),
            dma((2, back + 1)), dma((2, back + 1)),
            dma((GROUPS,)), dma((GROUPS,)), dma((GROUPS, 2)), dma((GROUPS, 2)), dma((4,)),
        ],
        compiler_params=comm_params(collective_id, 56),
        cost_estimate=cost(100),
        name="project",
    )(tokens, w_qkv, w_out, out_grad, smalls, cosine, sine, w_gate, w_up, w_down)


def attend(query, context, segment_query, segment_keys, tokens, out_low, gain, collective_id):
    rows, columns = query.shape
    width = tokens.shape[1]
    blocks = context.shape[0]
    heads = columns // HEAD
    half, quarter = width // 2, width // 4
    low, f32 = jnp.bfloat16, jnp.float32

    def kernel(
        q_ref, context_ref, sq_ref, sk_ref, tok_ref, out_ref, gain_ref,
        o_ref, lse_ref, x1_ref, h2_ref, scale_ref,
        part, full, core_buf, x_buf, send_sem, recv_sem,
    ):
        z, y, x, c = place()
        across, twin = device(z, y, 1 - x, c), device(z, y, x, 1 - c)
        greet([(across, None), (twin, None)])
        row = lax.broadcasted_iota(jnp.int32, (rows, rows), 0)
        column = lax.broadcasted_iota(jnp.int32, (rows, rows), 1)
        allowed = []
        for k in range(blocks):
            distance = row - column + k * rows
            allowed.append(
                (sq_ref[...] == sk_ref[k : k + 1, :]) & (distance >= 0) & (distance < WINDOW)
            )
        line = lax.broadcasted_iota(jnp.int32, (rows, 128), 1)
        lse = jnp.zeros((rows, 128), f32)
        for head in range(heads):
            at = pl.ds(head * HEAD, HEAD)
            scores = [
                jnp.where(
                    allowed[k], dot(q_ref[:, at], context_ref[k, 0, :, at], (1, 1)) * HEAD ** (-0.5), -1e30
                )
                for k in range(blocks)
            ]
            largest = scores[0]
            for k in range(1, blocks):
                largest = jnp.maximum(largest, scores[k])
            largest = jnp.max(largest, axis=-1, keepdims=True)
            weights = [jnp.exp(s - largest) for s in scores]
            amount = weights[0]
            for k in range(1, blocks):
                amount = amount + weights[k]
            amount = jnp.sum(amount, axis=-1, keepdims=True)
            inverse = 1.0 / amount
            value = jnp.zeros((rows, HEAD), f32)
            for k in range(blocks):
                value = value + dot((weights[k] * inverse).astype(low), context_ref[k, 1, :, at], (1, 0))
            o_ref[:, at] = value.astype(low)
            lse = jnp.where(line == head, largest + jnp.log(amount), lse)
        lse_ref[...] = lse

        def half_of(cc):
            return pl.ds(pl.multiple_of(cc * half, half), half)

        def fill(cc):
            def body(k, carry):
                at = pl.ds(pl.multiple_of(cc * half + k * quarter, quarter), quarter)
                part[:, at] = dot(o_ref[...], out_ref[:, at], (1, 0)).astype(low)
                return carry

            lax.fori_loop(0, 2, body, 0)

        fill(1 - c)
        group_sum(part, full, core_buf, x_buf, send_sem, recv_sem, lambda: fill(c))

        def norm(i, carry):
            r = pl.ds(pl.multiple_of(i * 32, 32), 32)
            value = tok_ref[r, :].astype(f32) + full[r, :].astype(f32)
            scale = lax.rsqrt(jnp.mean(value * value, axis=-1, keepdims=True) + EPS)
            x1_ref[r, :] = value
            scale_ref[r, :] = jnp.broadcast_to(scale, (32, 128))
            h2_ref[r, :] = (value * scale * gain_ref[1:2, :]).astype(low)
            return carry

        lax.fori_loop(0, rows // 32, norm, 0)

    shape, dma = jax.ShapeDtypeStruct, pltpu.SemaphoreType.DMA
    return pl.pallas_call(
        kernel,
        out_shape=(
            shape((rows, columns), low),
            shape((rows, 128), f32),
            shape((rows, width), f32),
            shape((rows, width), low),
            shape((rows, 128), f32),
        ),
        in_specs=[VMEM] * 7,
        out_specs=(VMEM,) * 5,
        scratch_shapes=[
            pltpu.VMEM((rows, width), low),
            pltpu.VMEM((rows, width), low),
            pltpu.VMEM((rows, half), low),
            pltpu.VMEM((rows, quarter), low),
            dma((5,)), dma((5,)),
        ],
        compiler_params=comm_params(collective_id, 40),
        cost_estimate=cost(40),
        name="attend",
    )(query, context, segment_query, segment_keys, tokens, out_low, gain)


def attend_back(
    grad_hidden, grad_probs, router_t, hidden_two, residual, scale_two, gains, out_grad,
    query, context, segment_query, segment_keys, attended, log_sums, raw, scales,
    cosine, sine, hidden_one, tokens, qkv_low, out_low, collective_id,
):
    rows, width = tokens.shape
    columns = query.shape[1]
    heads = columns // HEAD
    experts = router_t.shape[0]
    blocks = context.shape[0]
    depth = width // GROUPS
    small_rows = 8 + experts
    tensors = NX * NC
    half, quarter = width // 2, width // 4
    low, f32 = jnp.bfloat16, jnp.float32
    QUERY, KEY, VALUE, OUT, SMALL = 0, 1, 2, 3, 4

    def kernel(
        dh_ref, gates_ref, router_ref, h2_ref, x1_ref, s2_ref, gain_ref, dy_ref,
        q_ref, context_ref, sq_ref, sk_ref, o_ref, lse_ref, raw_ref, scale_ref,
        cos_ref, sin_ref, h1_ref, tok_ref, w_hbm, out_ref,
        tok_grad, qkv_sum, out_sum, small_sum,
        weights, dx1, da, do, dot_sums, dq, dkv, scaled, proj, send_kv, land_y, land_z,
        part, full, core_buf, x_buf, small, line_sum,
        main_buf, out_acc, out_lo, out_hi, out_land, small_buf, part_k, land_k, part_q, land_q,
        w_sem, y_s, y_r, z_s, z_r, group_s, group_r, ks_s, ks_r, qs_s, qs_r, line_s, line_r, out_s, out_r, out_y_s, out_y_r,
    ):
        z, y, x, c = place()
        e, t = lax.axis_index("expert"), lax.axis_index("tensor")
        mates = [(e, lax.rem(t + k, tensors)) for k in range(1, tensors)]
        beside, below = device(z, 1 - y, x, c), device(z - 1, y, x, c)
        fetch = pltpu.make_async_copy(w_hbm, weights, w_sem)
        fetch.start()

        def own_part(s, b):
            if s == SMALL:
                return small[b]
            at = pl.ds(pl.multiple_of(b * depth, depth), depth)
            return dot(h1_ref[:, at], proj[s], (0, 0))

        def out_copy(zz, yy, way):
            landing = (out_lo if way == 0 else out_hi).at[zz, yy]
            target = device(z + 1, y, x, c) if way == 0 else below
            return remote(out_acc.at[zz, yy], landing, out_s.at[zz, yy, way], out_r.at[zz, yy, way], target)

        def out_take(zz, yy, way):
            out_copy(zz, yy, way).wait_recv()
            total = out_acc.at[zz, yy]
            add_to(total, total, (out_lo if way == 0 else out_hi).at[zz, yy])

        def out_hop(k, way):
            for zz in Z_ORDER:
                for yy in range(NY):
                    def upward(zz=zz, yy=yy):
                        if k > 0:
                            out_take(zz, yy, 0)
                        out_copy(zz, yy, 0).start()

                    def downward(zz=zz, yy=yy):
                        if k > 0:
                            out_take(zz, yy, 1)
                        out_copy(zz, yy, 1).start()

                    if k < zz and way == 0:
                        run_if((z < zz) & (z == k), upward)
                    if NZ - 1 - k > zz and way == 1:
                        run_if((z > zz) & (NZ - 1 - z == k), downward)

        def out_beside():
            return remote(out_acc.at[z, 1 - y], out_land, out_y_s, out_y_r, beside)

        def out_start():
            for zz in range(NZ):
                for yy in range(NY):
                    at = pl.ds((zz * NY + yy) * depth, depth)
                    out_acc[zz, yy] = dot(o_ref[...], da[:, at], (0, 0)).astype(low)

        def out_home():
            for yy in range(NY):
                run_if(z > 0, lambda yy=yy: out_take(z, yy, 0))
                run_if(z < NZ - 1, lambda yy=yy: out_take(z, yy, 1))
            out_beside().start()

        def out_end():
            out_beside().wait_recv()
            out_sum[...] = out_acc[z, y].astype(f32) + out_land[...].astype(f32)
            out_beside().wait_send()
            for zz in range(NZ):
                for yy in range(NY):
                    run_if(z < zz, lambda zz=zz, yy=yy: out_copy(zz, yy, 0).wait_send())
                    run_if(z > zz, lambda zz=zz, yy=yy: out_copy(zz, yy, 1).wait_send())

        def slot(kind):
            def view(s, zz):
                if s == SMALL:
                    return small_buf.at[kind, zz]
                return main_buf.at[kind, zz, s]
            return view

        line = LineReduce([], lambda s, zz, yy: slot(3)(s, zz), slot(0), slot(1), slot(2), line_s, line_r)
        greet(line.partners() + [(mate, None) for mate in mates])

        grad_probs = gates_ref[...]
        logits = dot(h2_ref[...], router_ref[...], (1, 1))
        shifted = jnp.exp(logits - jnp.max(logits, axis=-1, keepdims=True))
        probs = shifted / jnp.sum(shifted, axis=-1, keepdims=True)
        grad_logits = probs * (grad_probs - jnp.sum(probs * grad_probs, axis=-1, keepdims=True))
        tall = jnp.transpose(
            jnp.concatenate([grad_logits, jnp.zeros((rows, 128 - experts), f32)], axis=1)
        )
        grad_logits = grad_logits.astype(low)
        tall = tall.astype(low)
        for b in range(GROUPS):
            small[b] = jnp.zeros_like(small[b])
            small[b, 8 : 8 + experts, :] = dot(tall, h2_ref[:, pl.ds(b * depth, depth)], (1, 0))[:experts]
        dx1[...] = dot(grad_logits, router_ref[...], (1, 0))
        line_sum[...] = jnp.zeros_like(line_sum)

        def norm_two(i, carry):
            r = pl.ds(pl.multiple_of(i * 32, 32), 32)
            grad = dh_ref[r, :].astype(f32) + dx1[r, :]
            value, scale = x1_ref[r, :], s2_ref[r, 0:1]
            line_sum[0:1, :] += jnp.sum(grad * (value * scale), axis=0, keepdims=True)
            grad = grad * gain_ref[1:2, :]
            inner = jnp.mean(grad * value, axis=-1, keepdims=True)
            result = dy_ref[r, :].astype(f32) + scale * grad - value * (scale * scale * scale) * inner
            dx1[r, :] = result
            da[r, :] = result.astype(low)
            return carry

        lax.fori_loop(0, rows // 32, norm_two, 0)

        out_start()
        out_hop(0, 0)

        do[...] = dot(da[...], out_ref[...], (1, 1)).astype(low)
        wide = lax.broadcasted_iota(jnp.int32, (rows, 128), 1)
        sums = jnp.zeros((rows, 128), f32)
        for head in range(heads):
            at = pl.ds(head * HEAD, HEAD)
            inner = jnp.sum(do[:, at].astype(f32) * o_ref[:, at].astype(f32), axis=-1, keepdims=True)
            sums = jnp.where(wide == head, inner, sums)
        dot_sums[...] = sums
        dq[...] = jnp.zeros_like(dq)
        row = lax.broadcasted_iota(jnp.int32, (rows, rows), 0)
        column = lax.broadcasted_iota(jnp.int32, (rows, rows), 1)

        def attention_block(k):
            distance = row - column + k * rows
            allowed = (sq_ref[...] == sk_ref[k : k + 1, :]) & (distance >= 0) & (distance < WINDOW)
            for head in range(heads):
                at = pl.ds(head * HEAD, HEAD)
                queries, keys, values = q_ref[:, at], context_ref[k, 0, :, at], context_ref[k, 1, :, at]
                scores = dot(queries, keys, (1, 1)) * HEAD ** (-0.5)
                weight = jnp.where(allowed, jnp.exp(scores - lse_ref[:, head : head + 1]), 0.0)
                grad_weight = dot(do[:, at], values, (1, 1))
                grad_score = (
                    weight * (grad_weight - dot_sums[:, head : head + 1]) * HEAD ** (-0.5)
                ).astype(low)
                dq[:, at] += dot(grad_score, keys, (1, 0))
                dkv[k, 0, :, at] = dot(grad_score, queries, (0, 0))
                dkv[k, 1, :, at] = dot(weight.astype(low), do[:, at], (0, 0))

        exists = {0: None, 1: (y == 1) | (z >= 1), 2: z >= 1, 3: z >= 2 - y, 4: z >= 2}
        comes = {1: (y == 0) | (z >= 1), 3: z >= 1 + y}

        def kv_copy(which, k):
            if k in (1, 3):
                landing, target = land_y.at[k // 2, which], beside
                return remote(send_kv.at[k - 1, which], landing, y_s.at[k // 2, which], y_r.at[k // 2, which], target)
            landing = land_z.at[k // 2 - 1, which]
            return remote(
                send_kv.at[k - 1, which], landing, z_s.at[k // 2 - 1, which], z_r.at[k // 2 - 1, which], below
            )

        def kv_send(which, k):
            send_kv[k - 1, which] = dkv[k, which].astype(low)
            kv_copy(which, k).start()

        def merge(into, which, landed):
            add_to(dkv.at[into, which], dkv.at[into, which], landed, 32)

        for k in (3, 1, 4, 2, 0):
            def one(k=k):
                attention_block(k)
                if k in (1, 3):
                    kv_send(1, k)
                    kv_send(0, k)
            run_if(exists[k], one)

        def take_three(which):
            def land():
                kv_copy(which, 3).wait_recv()
                pl.when(y == 1)(lambda: merge(4, which, land_y.at[1, which]))
                pl.when(y == 0)(lambda: merge(2, which, land_y.at[1, which]))
            run_if(comes[3], land)
            run_if(exists[4], lambda: kv_send(which, 4))

        def take_one(which):
            def land():
                kv_copy(which, 1).wait_recv()
                pl.when(y == 1)(lambda: merge(2, which, land_y.at[0, which]))
                pl.when(y == 0)(lambda: merge(0, which, land_y.at[0, which]))
            run_if(comes[1], land)

        def take_four(which):
            def land():
                kv_copy(which, 4).wait_recv()
                merge(2, which, land_z.at[1, which])
            run_if((z >= 1) & (z < NZ - 1), land)
            run_if(exists[2], lambda: kv_send(which, 2))

        def take_two(which):
            def land():
                kv_copy(which, 2).wait_recv()
                merge(0, which, land_z.at[0, which])
            run_if(z < NZ - 1, land)

        def unturn(which, grad_of):
            inner = jnp.zeros((rows, 1), f32)
            for head in range(heads):
                at = pl.ds(head * HEAD, HEAD)
                grad = turn(grad_of(at), cos_ref[...], -sin_ref[...])
                value = raw_ref[which, :, at]
                line_sum[1 + which : 2 + which, at] = jnp.sum(
                    grad * (value * scale_ref[:, 1 + which : 2 + which]), axis=0, keepdims=True
                )
                grad = grad * gain_ref[2 + which : 3 + which, at]
                scaled[which, :, at] = grad
                inner = inner + jnp.sum(grad * value, axis=-1, keepdims=True)
            return inner

        def denorm(which, inner):
            scale = scale_ref[:, 1 + which : 2 + which]
            rest = scale * scale * scale * inner / width
            for head in range(heads):
                at = pl.ds(head * HEAD, HEAD)
                proj[which, :, at] = (
                    scale * scaled[which, :, at] - raw_ref[which, :, at] * rest
                ).astype(low)

        def send_beside(s):
            for zz in Z_ORDER:
                buffer = slot(3)(s, zz)
                buffer[...] = own_part(s, zz * NY + 1 - y).astype(buffer.dtype)
                line.to_y(s, zz)

        exchange_rows(unturn(QUERY, lambda at: dq[:, at]), part_q, land_q, qs_s, qs_r, mates)
        take_three(1)
        take_three(0)
        denorm(QUERY, exchanged_rows(part_q, land_q, qs_s, qs_r, mates))
        send_beside(QUERY)
        out_hop(1, 0)
        take_one(1)
        take_one(0)
        take_four(1)
        take_four(0)
        out_hop(0, 1)
        take_two(1)
        proj[VALUE] = dkv[0, 1].astype(low)
        send_beside(VALUE)
        take_two(0)
        out_hop(2, 0)
        exchange_rows(unturn(KEY, lambda at: dkv[0, 0, :, at]), part_k, land_k, ks_s, ks_r, mates)
        denorm(KEY, exchanged_rows(part_k, land_k, ks_s, ks_r, mates))
        send_beside(KEY)
        out_hop(1, 1)
        fetch.wait()

        def half_of(cc):
            def body(i, carry):
                at = pl.ds(pl.multiple_of(cc * half + i * quarter, quarter), quarter)
                value = dot(proj[0], weights[0, at, :], (1, 1))
                for s in (1, 2):
                    value = value + dot(proj[s], weights[s, at, :], (1, 1))
                part[:, at] = value.astype(low)
                return carry

            lax.fori_loop(0, 2, body, 0)

        stages = group_stages(part, full, core_buf, x_buf, group_s, group_r)
        half_of(1 - c)
        stages[0]()
        half_of(c)
        stages[1]()

        def hop(s, zz, k):
            def upward():
                if k > 0:
                    line.take(s, zz, 1)
                line.copy(s, zz, 1).start()

            def downward():
                if k > 0:
                    line.take(s, zz, 2)
                line.copy(s, zz, 2).start()

            if k < zz:
                run_if((z < zz) & (z == k), upward)
            if NZ - 1 - k > zz:
                run_if((z > zz) & (NZ - 1 - z == k), downward)

        def receive(s, zz):
            line.copy(s, zz, 0).wait_recv()
            buffer = slot(0)(s, zz)
            buffer[...] = (buffer[...].astype(f32) + own_part(s, zz * NY + y)).astype(buffer.dtype)

        units = []

        def run_units(s):
            for zz in Z_ORDER:
                receive(s, zz)
                hop(s, zz, 0)
                units.append((s, zz))
                for k in (1, 2):
                    if len(units) > k:
                        hop(*units[-1 - k], k)

        def norm_one(i, carry):
            r = pl.ds(pl.multiple_of(i * 32, 32), 32)
            grad, value, scale = full[r, :].astype(f32), tok_ref[r, :].astype(f32), scale_ref[r, 0:1]
            line_sum[3:4, :] += jnp.sum(grad * (value * scale), axis=0, keepdims=True)
            grad = grad * gain_ref[0:1, :]
            inner = jnp.mean(grad * value, axis=-1, keepdims=True)
            tok_grad[r, :] = (
                dx1[r, :] + scale * grad - value * (scale * scale * scale) * inner
            ).astype(low)
            return carry

        run_units(QUERY)
        out_hop(2, 1)
        stages[2]()
        run_units(VALUE)
        out_home()
        stages[3]()
        stages[4]()
        lax.fori_loop(0, rows // 32, norm_one, 0)
        for b in range(GROUPS):
            at = pl.ds(b * depth, depth)
            small[b, 0:1, :] = line_sum[3:4, at]
            small[b, 1:2, :] = line_sum[0:1, at]
            for which in range(2):
                for k in range(columns // depth):
                    small[b, 2 + 2 * which + k : 3 + 2 * which + k, :] = line_sum[
                        1 + which : 2 + which, pl.ds(k * depth, depth)
                    ]
        send_beside(SMALL)
        run_units(KEY)
        run_units(SMALL)
        out_end()
        hop(*units[-1], 1)
        hop(*units[-2], 2)
        hop(*units[-1], 2)

        def done(s, total):
            target = qkv_sum.at[s] if s < OUT else small_sum
            target[...] = total[...].astype(f32)

        line.streams = [QUERY, VALUE, KEY, SMALL]
        line.home(done)
        line.finish()
        for which in range(2):
            for k in (1, 2, 3, 4):
                run_if(exists[k], lambda which=which, k=k: kv_copy(which, k).wait_send())
        drain_rows(part_k, land_k, ks_s, ks_r, mates)
        drain_rows(part_q, land_q, qs_s, qs_r, mates)

    shape, dma, vmem = jax.ShapeDtypeStruct, pltpu.SemaphoreType.DMA, pltpu.VMEM
    return pl.pallas_call(
        kernel,
        out_shape=(
            shape((rows, width), low),
            shape((3, depth, columns), f32),
            shape((columns, depth), f32),
            shape((small_rows, depth), f32),
        ),
        in_specs=[VMEM] * 20 + [HBM, VMEM],
        out_specs=(VMEM,) * 4,
        scratch_shapes=[
            vmem(qkv_low.shape, low),
            vmem((rows, width), f32),
            vmem((rows, width), low),
            vmem((rows, columns), low),
            vmem((rows, 128), f32),
            vmem((rows, columns), f32),
            vmem((blocks, 2, rows, columns), f32),
            vmem((2, rows, columns), f32),
            vmem((3, rows, columns), low),
            vmem((blocks - 1, 2, rows, columns), low),
            vmem((2, 2, rows, columns), low),
            vmem((2, 2, rows, columns), low),
            vmem((rows, width), low),
            vmem((rows, width), low),
            vmem((rows, half), low),
            vmem((rows, quarter), low),
            vmem((GROUPS, small_rows, depth), f32),
            vmem((8, width), f32),
            vmem((4, NZ, 3, depth, columns), low),
            vmem((NZ, NY, columns, depth), low),
            vmem((NZ, NY, columns, depth), low),
            vmem((NZ, NY, columns, depth), low),
            vmem((columns, depth), low),
            vmem((4, NZ, small_rows, depth), f32),
            vmem((8, rows), f32),
            vmem((tensors - 1, 8, rows), f32),
            vmem((8, rows), f32),
            vmem((tensors - 1, 8, rows), f32),
            dma, dma((2, 2)), dma((2, 2)), dma((2, 2)), dma((2, 2)), dma((5,)), dma((5,)),
            dma((tensors - 1,)), dma((tensors - 1,)), dma((tensors - 1,)), dma((tensors - 1,)),
            dma((5, NZ, 3)), dma((5, NZ, 3)), dma((NZ, NY, 2)), dma((NZ, NY, 2)), dma, dma,
        ],
        compiler_params=comm_params(collective_id, 62),
        cost_estimate=cost(130),
        name="attend_back",
    )(
        grad_hidden, grad_probs, router_t, hidden_two, residual, scale_two, gains, out_grad,
        query, context, segment_query, segment_keys, attended, log_sums, raw, scales,
        cosine, sine, hidden_one, tokens, qkv_low, out_low,
    )


def fast_shards(
    tokens_in,
    out_grad,
    w_qkv,
    w_attn_out,
    attn_gain,
    ffn_gain,
    qk_gain,
    w_router,
    w_gate,
    w_up,
    w_down,
    routes,
    segments,
):
    row_count, model_width = tokens_in.shape
    experts = w_router.shape[1]
    local_experts = w_gate.shape[0]
    heads_here = qk_gain.shape[1]
    local_width = heads_here * HEAD
    groups = lax.axis_size("expert")
    device_index = lax.axis_index("expert")
    tensor_index = lax.axis_index("tensor")
    quarter = model_width // lax.axis_size("tensor")
    hop_count = WINDOW // row_count
    score_scale = HEAD ** (-0.5)
    low = jnp.bfloat16

    chosen = jnp.any(
        routes[:, :, None] == jnp.arange(experts, dtype=jnp.int32)[None, None, :], axis=1
    ).astype(jnp.float32)
    qk_row = qk_gain.reshape(1, -1)

    def rounded(v):
        return lax.reduce_precision(v, 8, 7)

    smalls = jnp.concatenate(
        [
            rounded(attn_gain)[None, :],
            rounded(ffn_gain)[None, :],
            jnp.pad(rounded(qk_row), ((0, 0), (0, row_count - qk_row.shape[1]))),
            jnp.zeros((5, row_count), jnp.float32),
            w_router.T,
            chosen.T,
        ],
        axis=0,
    )
    global_rows = device_index * row_count + jnp.arange(row_count, dtype=jnp.int32)
    cosine_table, sine_table = angles(global_rows % SEQ, HEAD)
    wide_cosine = jnp.concatenate([cosine_table[:, 0], cosine_table[:, 0]], axis=1)
    wide_sine = jnp.concatenate([-sine_table[:, 0], sine_table[:, 0]], axis=1)
    (
        qkv_low, out_low, grad_out_all, hidden_one, raw, gate_up, down_low, gains, router_t, chosen_all,
        scales, query_low, context_blocks,
    ) = project(
        tokens_in, w_qkv, w_attn_out, out_grad, smalls, wide_cosine, wide_sine, w_gate, w_up, w_down,
        experts, 0,
    )
    segment_window = lax.dynamic_slice_in_dim(
        jnp.concatenate([jnp.full((WINDOW,), -1, jnp.int32), segments]),
        device_index * row_count, (hop_count + 1) * row_count,
    )
    segment_query = segment_window[WINDOW:]
    segment_keys = segment_window.reshape(hop_count + 1, row_count)[::-1]
    attended, log_sums, residual, hidden_two, scale_two_wide = attend(
        query_low, context_blocks, segment_query[:, None], segment_keys, tokens_in, out_low,
        gains, 2,
    )
    block_out, grad_hidden_sum, grad_gate_sum, grad_gate_w, grad_up_w, grad_down = expert_layer(
        hidden_two, grad_out_all, gate_up, down_low, router_t, chosen_all, residual, 5
    )
    grad_probs = grad_gate_sum[:, :local_experts].reshape(experts, row_count).T * chosen
    grad_tokens, qkv_sum, out_sum, small_sum = attend_back(
        grad_hidden_sum, grad_probs, router_t, hidden_two, residual, scale_two_wide,
        gains, out_grad, query_low, context_blocks, segment_query[:, None], segment_keys,
        attended, log_sums, raw, scales, wide_cosine, wide_sine, hidden_one, tokens_in, qkv_low, out_low, 8,
    )
    return (
        block_out,
        grad_tokens,
        qkv_sum,
        out_sum,
        small_sum[0],
        small_sum[1],
        lax.dynamic_slice_in_dim(
            small_sum[2:6].reshape(2, heads_here, HEAD),
            device_index * qk_gain.shape[2], qk_gain.shape[2], axis=2,
        ),
        small_sum[8 : 8 + experts].T,
        grad_gate_w,
        grad_up_w,
        grad_down,
    )


def solution(mesh):
    placed = (
        P("expert", None),
        P("expert", None),
        P(None, "expert", "tensor"),
        P("tensor", "expert"),
        P("expert"),
        P("expert"),
        P(None, "tensor", "expert"),
        P("expert", None),
        P("expert", None, "tensor"),
        P("expert", None, "tensor"),
        P("expert", "tensor", None),
        P("expert", None),
        P(),
    )
    compact = (mesh.shape["expert"], mesh.shape["tensor"]) == (GROUPS, NX * NC)
    return jax.shard_map(
        fast_shards if compact else shards,
        mesh=mesh,
        in_specs=placed,
        out_specs=(
            P("expert", None),
            P("expert", None),
            P(None, "expert", "tensor"),
            P("tensor", "expert"),
            P("expert"),
            P("expert"),
            P(None, "tensor", "expert"),
            P("expert", None),
            P("expert", None, "tensor"),
            P("expert", None, "tensor"),
            P("expert", "tensor", None),
        ),
        check_vma=False,
    )
```

```python
import jax
import jax.numpy as jnp
from jax import lax
from jax.experimental import pallas as pl
from jax.experimental.pallas import tpu as pltpu
from jax.sharding import PartitionSpec as P

HEAD = 128
WINDOW = 1024
SEQ = 2048


EPS = 1e-05
THETA = 10000.0


def from_behind(value, axis, steps):
    count = lax.axis_size(axis)
    initial, last = (max(0, -steps), min(count, count - steps))
    return lax.ppermute(value, axis, [(source, source + steps) for source in range(initial, last)])


def angles(position, head_size):
    half_size = head_size // 2
    frequency = THETA ** (-(jnp.arange(half_size, dtype=jnp.float32) * 2.0 / head_size))
    phase_angle = position.astype(jnp.float32)[:, None] * frequency[None, :]
    return (jnp.cos(phase_angle)[:, None, :], jnp.sin(phase_angle)[:, None, :])


def rotate(rotated_in, cosine_table, sine_table):
    half_size = rotated_in.shape[-1] // 2
    first_half = rotated_in[..., :half_size]
    second_half = rotated_in[..., half_size:]
    return jnp.concatenate(
        [
            first_half * cosine_table - second_half * sine_table,
            second_half * cosine_table + first_half * sine_table,
        ],
        axis=-1,
    )


def slot_layout(block_routes, experts, capacity):
    flat_routes = block_routes.reshape(-1)
    onehot = (flat_routes[:, None] == jnp.arange(experts, dtype=jnp.int32)[None, :]).astype(
        jnp.int32
    )
    before = jnp.cumsum(onehot, axis=0) - onehot
    rank_within = jnp.sum(before * onehot, axis=1)
    slot_index = flat_routes * capacity + rank_within
    slot_table = (
        jnp.zeros((experts * capacity,), jnp.int32)
        .at[slot_index]
        .set(jnp.arange(flat_routes.shape[0], dtype=jnp.int32) + 1)
    )
    return (slot_index, slot_table)


def shards(
    tokens_in,
    out_grad,
    w_qkv,
    w_attn_out,
    attn_gain,
    ffn_gain,
    qk_gain,
    w_router,
    w_gate,
    w_up,
    w_down,
    routes,
    segments,
):
    row_count, model_width = tokens_in.shape
    experts = w_router.shape[1]
    per_token = routes.shape[1]
    local_experts = w_gate.shape[0]
    heads_here = qk_gain.shape[1]
    local_width = heads_here * HEAD
    groups = lax.axis_size("expert")
    device = lax.axis_index("expert")
    capacity = row_count * per_token * 3 // (2 * experts)
    hop_count = WINDOW // row_count
    buffer_shape = (groups, local_experts, capacity, model_width)
    score_scale = HEAD ** (-0.5)

    def fetch_weights():
        return (
            lax.all_gather(w_qkv.astype(jnp.bfloat16), "expert", axis=1, tiled=True),
            lax.all_gather(w_attn_out.astype(jnp.bfloat16), "expert", axis=1, tiled=True),
            lax.all_gather(w_router.astype(jnp.bfloat16), "expert", axis=0, tiled=True),
            lax.all_gather(attn_gain.astype(jnp.bfloat16), "expert", axis=0, tiled=True),
            lax.all_gather(ffn_gain.astype(jnp.bfloat16), "expert", axis=0, tiled=True),
            lax.all_gather(qk_gain.astype(jnp.bfloat16), "expert", axis=2, tiled=True),
        )

    def prepare(pieces):
        return (
            pieces[0],
            pieces[1],
            pieces[2],
            pieces[3].astype(jnp.float32),
            pieces[4].astype(jnp.float32),
            pieces[5].astype(jnp.float32).reshape(2, local_width),
        )

    qkv_low, out_low, router_low, gain_one_f, gain_two_f, qk_gains = prepare(fetch_weights())
    tokens_f = tokens_in.astype(jnp.float32)
    scale_one = lax.rsqrt(jnp.mean(tokens_f * tokens_f, axis=-1, keepdims=True) + EPS)
    hidden_one = (tokens_f * scale_one * gain_one_f).astype(jnp.bfloat16)
    projected = jnp.einsum("td,jde->jte", hidden_one, qkv_low, preferred_element_type=jnp.float32)
    query_raw = projected[0]
    key_raw = projected[1]
    query_sq, key_sq = lax.psum(
        (jnp.sum(query_raw * query_raw, axis=-1), jnp.sum(key_raw * key_raw, axis=-1)), "tensor"
    )
    query_scale = lax.rsqrt(query_sq / model_width + EPS)[:, None]
    key_scale = lax.rsqrt(key_sq / model_width + EPS)[:, None]
    normed_query = query_raw * query_scale
    normed_key = key_raw * key_scale
    global_rows = device * row_count + jnp.arange(row_count, dtype=jnp.int32)
    cosine_table, sine_table = angles(global_rows % SEQ, HEAD)
    query_low = rotate(
        (normed_query * qk_gains[0]).reshape(row_count, heads_here, HEAD), cosine_table, sine_table
    ).astype(jnp.bfloat16)
    key_low = rotate(
        (normed_key * qk_gains[1]).reshape(row_count, heads_here, HEAD), cosine_table, sine_table
    ).astype(jnp.bfloat16)
    value_low = projected[2].astype(jnp.bfloat16).reshape(row_count, heads_here, HEAD)
    own_pair = jnp.stack([key_low, value_low])
    earlier = []
    for steps_back in range(hop_count, 0, -1):
        earlier.append(from_behind(own_pair, "expert", steps_back))
    context = jnp.concatenate(earlier + [own_pair], axis=1)
    key_rows = (device - hop_count) * row_count + jnp.arange(
        (hop_count + 1) * row_count, dtype=jnp.int32
    )
    segment_keys = segments[jnp.maximum(key_rows, 0)]
    segment_query = segments[global_rows]
    distance = global_rows[:, None] - key_rows[None, :]
    allowed = (
        (key_rows[None, :] >= 0)
        & (segment_query[:, None] == segment_keys[None, :])
        & (distance >= 0)
        & (distance < WINDOW)
    )

    def score_block():
        raw_scores = (
            jnp.einsum("qhd,khd->hqk", query_low, context[0], preferred_element_type=jnp.float32)
            * score_scale
        )
        return jnp.where(allowed[None], raw_scores, -1e30)

    scores = score_block()
    largest = jnp.max(scores, axis=-1, keepdims=True)
    exp_scores = jnp.exp(scores - largest)
    exp_total = jnp.sum(exp_scores, axis=-1, keepdims=True)
    log_total = largest + jnp.log(exp_total)
    attn_probs = (exp_scores / exp_total).astype(jnp.bfloat16)
    attended = (
        jnp.einsum("hqk,khd->qhd", attn_probs, context[1], preferred_element_type=jnp.float32)
        .reshape(row_count, local_width)
        .astype(jnp.bfloat16)
    )
    attention_out = lax.psum(
        jnp.dot(attended, out_low, preferred_element_type=jnp.float32).astype(jnp.bfloat16),
        "tensor",
    ).astype(jnp.float32)
    residual = tokens_f + attention_out
    scale_two = lax.rsqrt(jnp.mean(residual * residual, axis=-1, keepdims=True) + EPS)
    normed_two = residual * scale_two
    hidden_two = (normed_two * gain_two_f).astype(jnp.bfloat16)
    logits = jnp.dot(hidden_two, router_low, preferred_element_type=jnp.float32)
    logit_exp = jnp.exp(logits - jnp.max(logits, axis=-1, keepdims=True))
    router_probs = logit_exp / jnp.sum(logit_exp, axis=-1, keepdims=True)
    chosen = routes[:, :, None] == jnp.arange(experts, dtype=jnp.int32)[None, None, :]
    gate_probs = jnp.sum(jnp.where(chosen, router_probs[:, None, :], 0.0), axis=-1)
    slot_index, slot_table = slot_layout(routes, experts, capacity)
    present = (slot_table > 0)[:, None]
    assigned = jnp.maximum(slot_table - 1, 0)
    row_of_slot = assigned // per_token
    gate_low = w_gate.astype(jnp.bfloat16)
    up_low = w_up.astype(jnp.bfloat16)
    down_low = w_down.astype(jnp.bfloat16)

    def send_rows():
        buffer_rows = jnp.where(
            present, hidden_two[row_of_slot], jnp.zeros((), jnp.bfloat16)
        ).reshape(buffer_shape)
        return lax.all_to_all(buffer_rows, "expert", split_axis=0, concat_axis=0, tiled=True)

    def expert_front(arrived):
        gate_pre = jnp.einsum(
            "secd,edh->sech", arrived, gate_low, preferred_element_type=jnp.float32
        )
        up_pre = jnp.einsum("secd,edh->sech", arrived, up_low, preferred_element_type=jnp.float32)
        return (gate_pre, up_pre)

    received = send_rows()
    gate_pre, up_pre = expert_front(received)
    activated = (gate_pre * jax.nn.sigmoid(gate_pre) * up_pre).astype(jnp.bfloat16)
    partial_value = jnp.einsum(
        "sech,ehd->secd", activated, down_low, preferred_element_type=jnp.float32
    ).astype(jnp.bfloat16)
    returned = lax.all_to_all(
        partial_value, "expert", split_axis=0, concat_axis=0, tiled=True
    ).reshape(experts * capacity, model_width)
    expert_rows = returned[slot_index].reshape(row_count, per_token, model_width)
    expert_part = jnp.einsum(
        "tk,tkd->td", gate_probs, expert_rows, preferred_element_type=jnp.float32
    )
    block_out = residual + lax.psum(expert_part.astype(jnp.bfloat16), "tensor").astype(jnp.float32)
    qkv_low, out_low, router_low, gain_one_f, gain_two_f, qk_gains = prepare(fetch_weights())
    grad_out = out_grad.astype(jnp.float32)
    grad_gate_part = jnp.einsum(
        "td,tkd->tk", grad_out, expert_rows, preferred_element_type=jnp.float32
    )
    slot_grads = (
        (gate_probs[:, :, None] * grad_out[:, None, :])
        .astype(jnp.bfloat16)
        .reshape(row_count * per_token, model_width)
    )
    grad_buffer = jnp.where(present, slot_grads[assigned], jnp.zeros((), jnp.bfloat16)).reshape(
        buffer_shape
    )
    grad_received = lax.all_to_all(grad_buffer, "expert", split_axis=0, concat_axis=0, tiled=True)
    received = send_rows()
    gate_pre, up_pre = expert_front(received)
    sigmoid_gate = jax.nn.sigmoid(gate_pre)
    swish_gate = gate_pre * sigmoid_gate
    activated = (swish_gate * up_pre).astype(jnp.bfloat16)
    grad_act = jnp.einsum(
        "secd,ehd->sech", grad_received, down_low, preferred_element_type=jnp.float32
    )
    grad_down = jnp.einsum(
        "sech,secd->ehd", activated, grad_received, preferred_element_type=jnp.float32
    )
    grad_gate_pre = (
        grad_act * up_pre * sigmoid_gate * (1.0 + gate_pre * (1.0 - sigmoid_gate))
    ).astype(jnp.bfloat16)
    grad_up_pre = (grad_act * swish_gate).astype(jnp.bfloat16)
    grad_gate_w = jnp.einsum(
        "secd,sech->edh", received, grad_gate_pre, preferred_element_type=jnp.float32
    )
    grad_up_w = jnp.einsum(
        "secd,sech->edh", received, grad_up_pre, preferred_element_type=jnp.float32
    )
    grad_rows = (
        jnp.einsum("sech,edh->secd", grad_gate_pre, gate_low, preferred_element_type=jnp.float32)
        + jnp.einsum("sech,edh->secd", grad_up_pre, up_low, preferred_element_type=jnp.float32)
    ).astype(jnp.bfloat16)
    grad_back = lax.all_to_all(
        grad_rows, "expert", split_axis=0, concat_axis=0, tiled=True
    ).reshape(experts * capacity, model_width)
    grad_hidden_part = jnp.sum(
        grad_back[slot_index].reshape(row_count, per_token, model_width), axis=1, dtype=jnp.float32
    )
    grad_hidden_sum, grad_gates = (
        lax.psum(grad_hidden_part.astype(jnp.bfloat16), "tensor").astype(jnp.float32),
        lax.psum(grad_gate_part.astype(jnp.bfloat16), "tensor").astype(jnp.float32),
    )
    grad_probs = jnp.sum(jnp.where(chosen, grad_gates[:, :, None], 0.0), axis=1)
    grad_logits = (
        router_probs * (grad_probs - jnp.sum(router_probs * grad_probs, axis=-1, keepdims=True))
    ).astype(jnp.bfloat16)
    grad_hidden_two = grad_hidden_sum + jnp.dot(
        grad_logits, router_low.T, preferred_element_type=jnp.float32
    )
    grad_router = jnp.dot(hidden_two.T, grad_logits, preferred_element_type=jnp.float32)
    grad_gain_two = jnp.sum(grad_hidden_two * normed_two, axis=0)
    scaled_two = grad_hidden_two * gain_two_f
    grad_residual = (
        grad_out
        + scale_two * scaled_two
        - residual
        * (scale_two * scale_two * scale_two)
        * jnp.mean(scaled_two * residual, axis=-1, keepdims=True)
    )
    grad_attn = grad_residual.astype(jnp.bfloat16)
    grad_out_w = jnp.dot(attended.T, grad_attn, preferred_element_type=jnp.float32)
    grad_attended = (
        jnp.dot(grad_attn, out_low.T, preferred_element_type=jnp.float32)
        .astype(jnp.bfloat16)
        .reshape(row_count, heads_here, HEAD)
    )
    attn_weights = jnp.where(allowed[None], jnp.exp(score_block() - log_total), 0.0)
    grad_weights = jnp.einsum(
        "qhd,khd->hqk", grad_attended, context[1], preferred_element_type=jnp.float32
    )
    inner_sum = jnp.sum(attn_weights * grad_weights, axis=-1, keepdims=True)
    grad_scores = (attn_weights * (grad_weights - inner_sum) * score_scale).astype(jnp.bfloat16)
    grad_query = jnp.einsum(
        "hqk,khd->qhd", grad_scores, context[0], preferred_element_type=jnp.float32
    )
    grad_keys = jnp.einsum(
        "hqk,qhd->khd", grad_scores, query_low, preferred_element_type=jnp.float32
    )
    grad_values = jnp.einsum(
        "hqk,qhd->khd",
        attn_weights.astype(jnp.bfloat16),
        grad_attended,
        preferred_element_type=jnp.float32,
    )
    grad_pair = jnp.stack([grad_keys, grad_values]).reshape(
        2, hop_count + 1, row_count, heads_here, HEAD
    )
    own_grad = grad_pair[:, hop_count]
    for steps_back in range(1, hop_count + 1):
        own_grad = own_grad + from_behind(
            grad_pair[:, hop_count - steps_back].astype(jnp.bfloat16), "expert", -steps_back
        ).astype(jnp.float32)
    grad_query_norm = rotate(grad_query, cosine_table, -sine_table).reshape(row_count, local_width)
    grad_key_norm = rotate(own_grad[0], cosine_table, -sine_table).reshape(row_count, local_width)
    grad_gain_query = jnp.sum(grad_query_norm * normed_query, axis=0)
    grad_gain_key = jnp.sum(grad_key_norm * normed_key, axis=0)
    scaled_query = grad_query_norm * qk_gains[0]
    scaled_key = grad_key_norm * qk_gains[1]
    query_inner, key_inner = lax.psum(
        (jnp.sum(scaled_query * query_raw, axis=-1), jnp.sum(scaled_key * key_raw, axis=-1)),
        "tensor",
    )
    grad_query_raw = (
        query_scale * scaled_query
        - query_raw * (query_scale * query_scale * query_scale) * query_inner[:, None] / model_width
    ).astype(jnp.bfloat16)
    grad_key_raw = (
        key_scale * scaled_key
        - key_raw * (key_scale * key_scale * key_scale) * key_inner[:, None] / model_width
    ).astype(jnp.bfloat16)
    grad_value_raw = own_grad[1].reshape(row_count, local_width).astype(jnp.bfloat16)
    grad_proj = jnp.stack([grad_query_raw, grad_key_raw, grad_value_raw])
    grad_qkv = jnp.einsum("td,jte->jde", hidden_one, grad_proj, preferred_element_type=jnp.float32)
    grad_hidden_one = lax.psum(
        jnp.einsum("jte,jde->td", grad_proj, qkv_low, preferred_element_type=jnp.float32).astype(
            jnp.bfloat16
        ),
        "tensor",
    ).astype(jnp.float32)
    grad_gain_one = jnp.sum(grad_hidden_one * tokens_f * scale_one, axis=0)
    scaled_one = grad_hidden_one * gain_one_f
    grad_tokens = (
        grad_residual
        + scale_one * scaled_one
        - tokens_f
        * (scale_one * scale_one * scale_one)
        * jnp.mean(scaled_one * tokens_f, axis=-1, keepdims=True)
    )
    grad_qk = jnp.stack([grad_gain_query, grad_gain_key]).reshape(2, heads_here, HEAD)
    reduced = (
        lax.psum_scatter(
            grad_qkv.astype(jnp.bfloat16), "expert", scatter_dimension=1, tiled=True
        ).astype(jnp.float32),
        lax.psum_scatter(
            grad_out_w.astype(jnp.bfloat16), "expert", scatter_dimension=1, tiled=True
        ).astype(jnp.float32),
        lax.psum_scatter(
            grad_router.astype(jnp.bfloat16), "expert", scatter_dimension=0, tiled=True
        ).astype(jnp.float32),
        lax.psum_scatter(
            grad_gain_one.astype(jnp.bfloat16), "expert", scatter_dimension=0, tiled=True
        ).astype(jnp.float32),
        lax.psum_scatter(
            grad_gain_two.astype(jnp.bfloat16), "expert", scatter_dimension=0, tiled=True
        ).astype(jnp.float32),
        lax.psum_scatter(
            grad_qk.astype(jnp.bfloat16), "expert", scatter_dimension=2, tiled=True
        ).astype(jnp.float32),
    )
    return (
        block_out.astype(jnp.bfloat16),
        grad_tokens.astype(jnp.bfloat16),
        reduced[0],
        reduced[1],
        reduced[3],
        reduced[4],
        reduced[5],
        reduced[2],
        grad_gate_w,
        grad_up_w,
        grad_down,
    )


MESH_ID = pl.DeviceIdType.MESH
HBM = pl.BlockSpec(memory_space=pltpu.HBM)
VMEM = pl.BlockSpec(memory_space=pltpu.VMEM)
NZ, NY, NX, NC = 4, 2, 2, 2
GROUPS = NZ * NY


def place():
    e = lax.axis_index("expert")
    t = lax.axis_index("tensor")
    return lax.div(e, NY), lax.rem(e, NY), lax.div(t, NC), lax.rem(t, NC)


def device(z, y, x, c):
    return (z * NY + y, x * NC + c)


def run_if(condition, body):
    if condition is None:
        body()
    else:
        pl.when(condition)(body)


def greet(partners):
    barrier = pltpu.get_barrier_semaphore()
    for target, condition in partners:
        run_if(
            condition,
            lambda target=target: pl.semaphore_signal(
                barrier, inc=1, device_id=target, device_id_type=MESH_ID
            ),
        )
    count = sum(1 for _, condition in partners if condition is None)
    for _, condition in partners:
        if condition is not None:
            count = count + condition.astype(jnp.int32)
    pl.semaphore_wait(barrier, count)


def remote(source, target_ref, send_sem, recv_sem, target):
    return pltpu.make_async_remote_copy(
        src_ref=source,
        dst_ref=target_ref,
        send_sem=send_sem,
        recv_sem=recv_sem,
        device_id=target,
        device_id_type=MESH_ID,
    )


def block_rows(block, rows):
    return pl.ds(pl.multiple_of(block * rows, rows), rows)


class LineGather:
    def __init__(self, streams, sources, views, send_sem, recv_sem, y_first=()):
        self.z, self.y, self.x, self.c = place()
        self.streams, self.sources, self.views = streams, sources, views
        self.send_sem, self.recv_sem = send_sem, recv_sem
        self.y_first = y_first
        self.has_up, self.has_down = self.z < NZ - 1, self.z > 0
        self.pending = []

    def partners(self):
        z, y, x, c = self.z, self.y, self.x, self.c
        return [
            (device(z + 1, y, x, c), z < NZ - 1),
            (device(z - 1, y, x, c), z > 0),
            (device(z, 1 - y, x, c), None),
        ]

    def exists(self, rel):
        rel = rel % 7
        if rel == 0:
            return None
        return self.z >= rel if rel < 4 else self.z + (rel - 3) < NZ

    def block(self, rel):
        y = self.y if rel < 7 else 1 - self.y
        rel = rel % 7
        z = self.z if rel == 0 else (self.z - rel if rel < 4 else self.z + (rel - 3))
        return z * NY + y

    def send(self, stream, rel, way):
        z, y, x, c = self.z, self.y, self.x, self.c
        block = self.block(rel)
        there = self.views[stream](block)
        source = self.sources[stream] if rel == 0 else there
        near = rel % 7 == 0
        if way == 0:
            target, landing = device(z + 1, y, x, c), rel + 1
        elif way == 1:
            target, landing = device(z - 1, y, x, c), rel + (4 if near else 1)
        else:
            target, landing = device(z, 1 - y, x, c), 7 + rel
        return remote(
            source,
            there,
            self.send_sem.at[stream, rel, way],
            self.recv_sem.at[stream, landing],
            target,
        )

    def forwards(self, stream, rel):
        return rel < 7 or stream in self.y_first

    def start(self, stream, rel):
        if rel % 7 < 4:
            run = self.has_up
            run_if(run, lambda: self.send(stream, rel, 0).start())
            self.pending.append((stream, rel, 0, run))
        if rel % 7 == 0 or rel % 7 >= 4:
            run = self.has_down
            run_if(run, lambda: self.send(stream, rel, 1).start())
            self.pending.append((stream, rel, 1, run))
        if rel == 0 or stream not in self.y_first:
            self.send(stream, rel, 2).start()
            self.pending.append((stream, rel, 2, None))

    def arrive(self, stream, rel):
        there = self.views[stream](self.block(rel))
        remote(
            there,
            there,
            self.send_sem.at[stream, 0, 0],
            self.recv_sem.at[stream, rel],
            device(self.z, 1 - self.y, self.x, self.c),
        ).wait_recv()

    def order(self):
        return [7, 1, 4, 8, 11, 2, 5, 9, 12, 3, 6, 10, 13]

    def run(self, hook=None):
        for stream in self.streams:
            self.start(stream, 0)
        for rel in self.order():
            def step(rel=rel):
                marks = len(self.pending)
                for stream in self.streams:
                    self.arrive(stream, rel)
                    if rel < 7:
                        self.start(stream, rel)
                    if hook is not None:
                        hook(stream, rel)
                if rel < 7:
                    late = self.pending[marks:]
                    del self.pending[marks:]
                    self.finish_later(late, rel)
            run_if(self.exists(rel), step)

    def finish_later(self, late, rel):
        self.late = getattr(self, "late", []) + [(rel, late)]

    def finish(self):
        for stream, rel, way, run in self.pending:
            run_if(run, lambda s=stream, r=rel, w=way: self.send(s, r, w).wait_send())
        for rel, late in getattr(self, "late", []):
            def body(late=late):
                for stream, rel, way, run in late:
                    run_if(run, lambda s=stream, r=rel, w=way: self.send(s, r, w).wait_send())
            run_if(self.exists(rel), body)


def cost(microseconds):
    return pl.CostEstimate(flops=0, bytes_accessed=int(microseconds * 3.0e6), transcendentals=0)


def comm_params(collective_id, megabytes=56):
    return pltpu.CompilerParams(
        collective_id=collective_id,
        has_side_effects=True,
        vmem_limit_bytes=megabytes * 1024 * 1024,
    )


def weight_gather(qkv_low, out_low, smalls, collective_id):
    parts, rows, width = qkv_low.shape
    depth, columns = out_low.shape

    def kernel(qkv, out, small, qkv_all, out_all, small_all, send_sem, recv_sem, local_sem):
        views = [
            lambda b: qkv_all.at[:, block_rows(b, rows), :],
            lambda b: out_all.at[:, block_rows(b, columns)],
            lambda b: small_all.at[b],
        ]
        line = LineGather([2, 0, 1], [qkv, out, small], views, send_sem, recv_sem)
        greet(line.partners())
        own = line.block(0)
        keep = [
            pltpu.make_async_copy(source, view(own), local_sem.at[i])
            for i, (source, view) in enumerate(zip([qkv, out, small], views))
        ]
        for copy in keep:
            copy.start()
        line.run()
        line.finish()
        for copy in keep:
            copy.wait()

    return pl.pallas_call(
        kernel,
        out_shape=(
            jax.ShapeDtypeStruct((parts, rows * GROUPS, width), jnp.bfloat16),
            jax.ShapeDtypeStruct((depth, columns * GROUPS), jnp.bfloat16),
            jax.ShapeDtypeStruct((GROUPS,) + smalls.shape, jnp.float32),
        ),
        in_specs=[HBM] * 3,
        out_specs=(HBM, HBM, HBM),
        scratch_shapes=[
            pltpu.SemaphoreType.DMA((3, 14, 3)),
            pltpu.SemaphoreType.DMA((3, 14)),
            pltpu.SemaphoreType.DMA((3,)),
        ],
        compiler_params=comm_params(collective_id),
        cost_estimate=cost(100),
        name="weight_gather",
    )(qkv_low, out_low, smalls)


def token_gather(block, collective_id):
    rows, width = block.shape
    a_cols, c_cols = width * 3 // 16, width // 8

    def kernel(own_ref, all_ref, send_sem, recv_sem, x_send, x_recv, core_send, core_recv, local_sem):
        z, y, x, c = place()

        def a_at(xx, cc):
            return pl.ds(pl.multiple_of(xx * (2 * a_cols) + cc * a_cols, 128), a_cols)

        def c_at(cc):
            return pl.ds(pl.multiple_of(4 * a_cols + cc * c_cols, 128), c_cols)

        def view(b, columns):
            return all_ref.at[block_rows(b, rows), columns]

        sources = [own_ref.at[:, a_at(x, c)], own_ref.at[:, c_at(c)]]
        views = [lambda b: view(b, a_at(x, c)), lambda b: view(b, c_at(c))]
        line = LineGather([0, 1], sources, views, send_sem, recv_sem)
        across, twin = device(z, y, 1 - x, c), device(z, y, x, 1 - c)
        greet(line.partners() + [(across, None), (twin, None)])
        keep = pltpu.make_async_copy(own_ref, all_ref.at[block_rows(line.block(0), rows), :], local_sem)
        keep.start()

        def to_twin(rel, stream, landing=False):
            b = line.block(rel)
            columns = [a_at(x, c), c_at(c), a_at(1 - x, c)][stream]
            other = [a_at(x, 1 - c), c_at(1 - c), a_at(1 - x, 1 - c)][stream]
            piece = view(b, other if landing else columns)
            return remote(piece, piece, core_send.at[rel, stream], core_recv.at[rel, stream], twin)

        def to_across(rel, landing=False):
            b = line.block(rel)
            piece = view(b, a_at(1 - x if landing else x, c))
            return remote(piece, piece, x_send.at[rel], x_recv.at[rel], across)

        def hook(stream, rel):
            if stream == 0:
                to_across(rel).start()
            to_twin(rel, stream).start()

        line.run(hook)
        for rel in line.order():
            def relay(rel=rel):
                to_across(rel, True).wait_recv()
                to_twin(rel, 2).start()
            run_if(line.exists(rel), relay)
        for rel in line.order():
            def end(rel=rel):
                to_across(rel).wait_send()
                for stream in range(3):
                    to_twin(rel, stream, True).wait_recv()
                    to_twin(rel, stream).wait_send()
            run_if(line.exists(rel), end)
        line.finish()
        keep.wait()

    return pl.pallas_call(
        kernel,
        out_shape=jax.ShapeDtypeStruct((rows * GROUPS, width), block.dtype),
        in_specs=[HBM],
        out_specs=HBM,
        scratch_shapes=[
            pltpu.SemaphoreType.DMA((2, 14, 3)),
            pltpu.SemaphoreType.DMA((2, 14)),
            pltpu.SemaphoreType.DMA((14,)),
            pltpu.SemaphoreType.DMA((14,)),
            pltpu.SemaphoreType.DMA((14, 3)),
            pltpu.SemaphoreType.DMA((14, 3)),
            pltpu.SemaphoreType.DMA,
        ],
        compiler_params=comm_params(collective_id),
        cost_estimate=cost(45),
        name="token_gather",
    )(block)


def add_into(rows, step, store):
    def body(i, carry):
        store(pl.ds(pl.multiple_of(i * step, step), step))
        return carry

    lax.fori_loop(0, rows // step, body, 0)


def group_stages(part_ref, out_ref, core_buf, x_buf, send_sem, recv_sem):
    rows, width = part_ref.shape
    half, quarter = width // 2, width // 4
    z, y, x, c = place()
    across, twin = device(z, y, 1 - x, c), device(z, y, x, 1 - c)

    def half_of(cc):
        return pl.ds(pl.multiple_of(cc * half, half), half)

    def quarter_of(xx, cc):
        return pl.ds(pl.multiple_of(cc * half + xx * quarter, quarter), quarter)

    own, from_x = out_ref.at[:, quarter_of(x, c)], out_ref.at[:, quarter_of(1 - x, c)]
    to_x = core_buf.at[:, pl.ds(pl.multiple_of((1 - x) * quarter, quarter), quarter)]
    sources = [part_ref.at[:, half_of(1 - c)], to_x, own, own, from_x]
    landings = [core_buf, x_buf, own, own, from_x]
    targets = [twin, across, across, twin, twin]

    def copy(k):
        return remote(sources[k], landings[k], send_sem.at[k], recv_sem.at[k], targets[k])

    def arrive(k, landing):
        remote(landing, landing, send_sem.at[k], recv_sem.at[k], targets[k]).wait_recv()

    def begin():
        copy(0).start()

    def core_step():
        copy(0).wait_recv()
        add_to(core_buf, core_buf, part_ref.at[:, half_of(c)], 32)
        copy(1).start()

    def x_step():
        copy(1).wait_recv()
        add_to(own, x_buf, core_buf.at[:, pl.ds(pl.multiple_of(x * quarter, quarter), quarter)], 32)
        copy(2).start()
        copy(3).start()

    def spread():
        arrive(2, from_x)
        copy(4).start()

    def end():
        arrive(3, out_ref.at[:, quarter_of(x, 1 - c)])
        arrive(4, out_ref.at[:, quarter_of(1 - x, 1 - c)])
        for k in range(5):
            copy(k).wait_send()

    return [begin, core_step, x_step, spread, end]


def group_sum(part_ref, out_ref, core_buf, x_buf, send_sem, recv_sem, meanwhile=None):
    stages = group_stages(part_ref, out_ref, core_buf, x_buf, send_sem, recv_sem)
    stages[0]()
    if meanwhile is not None:
        meanwhile()
    for stage in stages[1:]:
        stage()


def tensor_sum(part, collective_id):
    rows, width = part.shape

    def kernel(part_ref, out_ref, core_buf, x_buf, send_sem, recv_sem):
        z, y, x, c = place()
        greet([(device(z, y, 1 - x, c), None), (device(z, y, x, 1 - c), None)])
        group_sum(part_ref, out_ref, core_buf, x_buf, send_sem, recv_sem)

    return pl.pallas_call(
        kernel,
        out_shape=jax.ShapeDtypeStruct((rows, width), jnp.bfloat16),
        in_specs=[VMEM],
        out_specs=VMEM,
        scratch_shapes=[
            pltpu.VMEM((rows, width // 2), jnp.bfloat16),
            pltpu.VMEM((rows, width // 4), jnp.bfloat16),
            pltpu.SemaphoreType.DMA((5,)),
            pltpu.SemaphoreType.DMA((5,)),
        ],
        compiler_params=comm_params(collective_id, 16),
        cost_estimate=cost(17),
        name="tensor_sum",
    )(part)


Z_ORDER = (3, 0, 2, 1)


def accumulate(into, addend, step=64):
    rows = into.shape[0]
    step = min(step, rows)

    def body(i, carry):
        r = pl.ds(pl.multiple_of(i * step, step), step)
        total = into[r, :].astype(jnp.float32) + addend[r, :].astype(jnp.float32)
        into[r, :] = total.astype(into.dtype)
        return carry

    lax.fori_loop(0, rows // step, body, 0)


class LineReduce:
    def __init__(self, streams, own, y_buf, lo_buf, hi_buf, send_sem, recv_sem):
        self.z, self.y, self.x, self.c = place()
        self.streams = streams
        self.own, self.y_buf, self.lo_buf, self.hi_buf = own, y_buf, lo_buf, hi_buf
        self.send_sem, self.recv_sem = send_sem, recv_sem

    def partners(self):
        z, y, x, c = self.z, self.y, self.x, self.c
        return [
            (device(z + 1, y, x, c), z < NZ - 1),
            (device(z - 1, y, x, c), z > 0),
            (device(z, 1 - y, x, c), None),
        ]

    def copy(self, s, zz, way):
        z, y, x, c = self.z, self.y, self.x, self.c
        if way == 0:
            source, landing, target = self.own(s, zz, 1 - y), self.y_buf, device(z, 1 - y, x, c)
        elif way == 1:
            source, landing, target = self.y_buf(s, zz), self.lo_buf, device(z + 1, y, x, c)
        else:
            source, landing, target = self.y_buf(s, zz), self.hi_buf, device(z - 1, y, x, c)
        return remote(
            source, landing(s, zz), self.send_sem.at[s, zz, way], self.recv_sem.at[s, zz, way], target
        )

    def to_y(self, s, zz):
        self.copy(s, zz, 0).start()

    def take(self, s, zz, way):
        self.copy(s, zz, way).wait_recv()
        accumulate(self.y_buf(s, zz), (self.lo_buf if way == 1 else self.hi_buf)(s, zz))

    def along_z(self, s, zz):
        z = self.z
        self.copy(s, zz, 0).wait_recv()
        accumulate(self.y_buf(s, zz), self.own(s, zz, self.y))

        def upward():
            run_if(z > 0, lambda: self.take(s, zz, 1))
            self.copy(s, zz, 1).start()

        def downward():
            run_if(z < NZ - 1, lambda: self.take(s, zz, 2))
            self.copy(s, zz, 2).start()

        run_if(z < zz, upward)
        run_if(z > zz, downward)

    def home(self, done):
        for zz in range(NZ):
            def land(zz=zz):
                for s in self.streams:
                    if zz > 0:
                        self.take(s, zz, 1)
                    if zz < NZ - 1:
                        self.take(s, zz, 2)
                    done(s, self.y_buf(s, zz))
            run_if(self.z == zz, land)

    def finish(self):
        for zz in range(NZ):
            for s in self.streams:
                self.copy(s, zz, 0).wait_send()
                run_if(self.z < zz, lambda s=s, zz=zz: self.copy(s, zz, 1).wait_send())
                run_if(self.z > zz, lambda s=s, zz=zz: self.copy(s, zz, 2).wait_send())


def weight_reduce(qkv, out, smalls, collective_id):
    parts, depth, width = qkv.shape
    rows = depth // GROUPS
    out_rows, columns = out.shape[0], out.shape[1] // GROUPS

    def kernel(qkv_ref, out_ref, small_ref, qkv_sum, out_sum, small_sum,
               qkv_buf, out_buf, small_buf, send_sem, recv_sem):
        def own(s, zz, yy):
            b = zz * NY + yy
            if s < parts:
                return qkv_ref.at[s, block_rows(b, rows), :]
            if s == parts:
                return out_ref.at[:, block_rows(b, columns)]
            return small_ref.at[b]

        def slot(kind):
            def view(s, zz):
                if s < parts:
                    return qkv_buf.at[kind, zz, s]
                if s == parts:
                    return out_buf.at[kind, zz]
                return small_buf.at[kind, zz]
            return view

        streams = list(range(parts + 2))
        line = LineReduce(streams, own, slot(0), slot(1), slot(2), send_sem, recv_sem)
        greet(line.partners())
        work = [(s, zz) for s in [parts + 1, parts] + list(range(parts)) for zz in Z_ORDER]
        for s, zz in work:
            line.to_y(s, zz)
        for s, zz in work:
            line.along_z(s, zz)

        def done(s, total):
            target = qkv_sum.at[s] if s < parts else (out_sum if s == parts else small_sum)
            step = min(64, target.shape[0])

            def body(i, carry):
                r = pl.ds(pl.multiple_of(i * step, step), step)
                target[r, :] = total[r, :].astype(jnp.float32)
                return carry

            lax.fori_loop(0, target.shape[0] // step, body, 0)

        line.home(done)
        line.finish()

    return pl.pallas_call(
        kernel,
        out_shape=(
            jax.ShapeDtypeStruct((parts, rows, width), jnp.float32),
            jax.ShapeDtypeStruct((out_rows, columns), jnp.float32),
            jax.ShapeDtypeStruct(smalls.shape[1:], jnp.float32),
        ),
        in_specs=[VMEM] * 3,
        out_specs=(VMEM,) * 3,
        scratch_shapes=[
            pltpu.VMEM((3, NZ, parts, rows, width), jnp.bfloat16),
            pltpu.VMEM((3, NZ, out_rows, columns), jnp.bfloat16),
            pltpu.VMEM((3, NZ) + smalls.shape[1:], jnp.float32),
            pltpu.SemaphoreType.DMA((parts + 2, NZ, 3)),
            pltpu.SemaphoreType.DMA((parts + 2, NZ, 3)),
        ],
        compiler_params=comm_params(collective_id),
        cost_estimate=cost(120),
        name="weight_reduce",
    )(qkv, out, smalls)


def token_reduce(part, collective_id, pairs=None):
    tokens, width = part.shape
    rows = tokens // GROUPS
    half, quarter = width // 2, width // 4

    def kernel(part_ref, out_ref, core_buf, x_buf, y_buf, lo_buf, hi_buf,
               core_send, core_recv, x_send, x_recv, send_sem, recv_sem):
        z, y, x, c = place()
        across, twin = device(z, y, 1 - x, c), device(z, y, x, 1 - c)

        line = LineReduce(
            [0], lambda s, zz, yy: x_buf.at[zz * NY + yy], lambda s, zz: y_buf.at[zz],
            lambda s, zz: lo_buf.at[zz], lambda s, zz: hi_buf.at[zz], send_sem, recv_sem,
        )
        greet(line.partners() + [(across, None), (twin, None)])
        order = [(zz, flip) for zz in Z_ORDER for flip in (1, 0)]

        def number(zz, flip):
            return zz * NY + (1 - y if flip else y)

        def to_twin(zz, flip):
            b = number(zz, flip)
            return remote(
                part_ref.at[block_rows(b, rows), pl.ds(pl.multiple_of((1 - c) * half, half), half)],
                core_buf.at[b], core_send.at[zz, flip], core_recv.at[zz, flip], twin,
            )

        def to_across(zz, flip):
            b = number(zz, flip)
            return remote(
                core_buf.at[b, :, pl.ds(pl.multiple_of((1 - x) * quarter, quarter), quarter)],
                x_buf.at[b], x_send.at[zz, flip], x_recv.at[zz, flip], across,
            )

        def add_core(zz, flip):
            b = number(zz, flip)

            def store(r):
                at = pl.ds(pl.multiple_of(b * rows + r.start, 16), r.size)
                core_buf[b, r, :] = (
                    core_buf[b, r, :].astype(jnp.float32)
                    + part_ref[at, pl.ds(pl.multiple_of(c * half, half), half)].astype(jnp.float32)
                ).astype(jnp.bfloat16)

            add_into(rows, 32, store)

        def add_across(zz, flip):
            b = number(zz, flip)

            def store(r):
                x_buf[b, r, :] = (
                    x_buf[b, r, :].astype(jnp.float32)
                    + core_buf[b, r, pl.ds(pl.multiple_of(x * quarter, quarter), quarter)].astype(jnp.float32)
                ).astype(jnp.bfloat16)

            add_into(rows, 64, store)

        def stage_twin(i):
            to_twin(*order[i]).wait_recv()
            add_core(*order[i])
            to_across(*order[i]).start()

        def stage_across(i):
            zz, flip = order[i]
            to_across(zz, flip).wait_recv()
            add_across(zz, flip)
            if flip:
                line.to_y(0, zz)

        def stage_y(zz):
            line.along_z(0, zz)

        for zz, flip in order:
            to_twin(zz, flip).start()
        count = len(order)
        for i in range(count + 4):
            if i < count:
                stage_twin(i)
            if 0 <= i - 1 < count:
                stage_across(i - 1)
            if i >= 3 and (i - 3) % 2 == 0 and (i - 3) // 2 < NZ:
                stage_y(Z_ORDER[(i - 3) // 2])

        def done(s, total):
            def store(r):
                out_ref[r, :] = total[r, :]

            add_into(rows, 64, store)

        line.home(done)
        for zz, flip in order:
            to_twin(zz, flip).wait_send()
            to_across(zz, flip).wait_send()
        line.finish()

    return pl.pallas_call(
        kernel,
        out_shape=jax.ShapeDtypeStruct((rows, quarter), jnp.bfloat16),
        in_specs=[VMEM],
        out_specs=VMEM,
        scratch_shapes=[
            pltpu.VMEM((GROUPS, rows, half), jnp.bfloat16),
            pltpu.VMEM((GROUPS, rows, quarter), jnp.bfloat16),
            pltpu.VMEM((NZ, rows, quarter), jnp.bfloat16),
            pltpu.VMEM((NZ, rows, quarter), jnp.bfloat16),
            pltpu.VMEM((NZ, rows, quarter), jnp.bfloat16),
            pltpu.SemaphoreType.DMA((NZ, 2)),
            pltpu.SemaphoreType.DMA((NZ, 2)),
            pltpu.SemaphoreType.DMA((NZ, 2)),
            pltpu.SemaphoreType.DMA((NZ, 2)),
            pltpu.SemaphoreType.DMA((1, NZ, 3)),
            pltpu.SemaphoreType.DMA((1, NZ, 3)),
        ],
        compiler_params=comm_params(collective_id),
        cost_estimate=cost(60),
        name="token_reduce",
    )(part)


def gate_exchange(part, collective_id):
    groups = part.shape[0]
    tensors = NX * NC

    def kernel(part_ref, out_ref, landing, total, send_t, recv_t, send_e, recv_e):
        e = lax.axis_index("expert")
        t = lax.axis_index("tensor")
        mates = [(e, lax.rem(t + k, tensors)) for k in range(1, tensors)]
        peers = [(lax.rem(e + k, groups), t) for k in range(1, groups)]
        greet([(target, None) for target in mates + peers])
        near = [
            remote(part_ref, landing.at[k], send_t.at[k], recv_t.at[k], mates[k])
            for k in range(tensors - 1)
        ]
        for copy in near:
            copy.start()
        for copy in near:
            copy.wait_recv()
        value = part_ref[...]
        for k in range(tensors - 1):
            value = value + landing[k]
        total[...] = value
        far = [
            remote(
                total.at[lax.rem(e + k, groups)], out_ref.at[e], send_e.at[k - 1], recv_e.at[k - 1],
                peers[k - 1],
            )
            for k in range(1, groups)
        ]
        for copy in far:
            copy.start()
        out_ref[e] = total[e]
        for k in range(1, groups):
            source = out_ref.at[lax.rem(e + groups - k, groups)]
            remote(source, source, send_e.at[k - 1], recv_e.at[k - 1], peers[k - 1]).wait_recv()
        for copy in near + far:
            copy.wait_send()

    return pl.pallas_call(
        kernel,
        out_shape=jax.ShapeDtypeStruct(part.shape, jnp.float32),
        in_specs=[VMEM],
        out_specs=VMEM,
        scratch_shapes=[
            pltpu.VMEM((tensors - 1,) + part.shape, jnp.float32),
            pltpu.VMEM(part.shape, jnp.float32),
            pltpu.SemaphoreType.DMA((tensors - 1,)),
            pltpu.SemaphoreType.DMA((tensors - 1,)),
            pltpu.SemaphoreType.DMA((groups - 1,)),
            pltpu.SemaphoreType.DMA((groups - 1,)),
        ],
        compiler_params=comm_params(collective_id, 16),
        cost_estimate=cost(10),
        name="gate_exchange",
    )(part)


def dot(a, b, dims):
    return lax.dot_general(a, b, ((dims[:1], dims[1:]), ((), ())), preferred_element_type=jnp.float32)


def add_to(target, first, second, step=64):
    rows = target.shape[0]

    def body(i, carry):
        r = pl.ds(pl.multiple_of(i * step, step), step)
        total = first[r, :].astype(jnp.float32) + second[r, :].astype(jnp.float32)
        target[r, :] = total.astype(target.dtype)
        return carry

    lax.fori_loop(0, rows // step, body, 0)


def expert_layer(
    hidden_two, grad_out_all, gate_up, down, router_t, chosen_all, residual, attended, collective_id
):
    rows, width = hidden_two.shape
    tokens = rows * GROUPS
    units = down.shape[0]
    local = 2
    hidden = units // local
    experts = router_t.shape[0]
    half, part, piece = width // 2, width // 4, width // 8
    tensors = NX * NC
    steps = GROUPS + 4
    a_cols, c_cols = width // 8, width // 4
    low = jnp.bfloat16
    wide = width // 4

    def kernel(
        own_in, dy_in, gu_ref, down_ref, router_ref, chosen_ref, x1_in, o_in,
        block_out, dh_out, gates_out, gate_w, up_w, down_w, o_all,
        h, dy, gated, dgu, dx, y_part, yc_buf, ypx_buf, ypy_buf, yqy_buf, yqx_buf, yz_sum,
        ylo_buf, yhi_buf, x1, gu_stage, d_stage,
        core_buf, px_buf, py_buf, qy_buf, qx_buf, z_sum, lo_buf, hi_buf, gate_part, gate_land,
        in_sem, own_sem, o_sem, line_s, line_r, hx_s, hx_r, hc_s, hc_r, x1_sem, yc_s, yc_r, ypx_s, ypx_r, ypy_s, ypy_r,
        yqy_s, yqy_r, yqx_s, yqx_r, yz_s, yz_r, gu_sem, d_sem, core_s, core_r, px_s, px_r, py_s, py_r, qy_s, qy_r, qx_s, qx_r,
        z_s, z_r, near_s, near_r, far_s, far_r, end_s, end_r,
    ):
        z, y, x, c = place()
        e, t = lax.axis_index("expert"), lax.axis_index("tensor")
        across, twin, beside = device(z, y, 1 - x, c), device(z, y, x, 1 - c), device(z, 1 - y, x, c)
        mates = [(e, lax.rem(t + k, tensors)) for k in range(1, tensors)]
        peers = [(lax.rem(e + k, GROUPS), t) for k in range(1, GROUPS)]
        greet([(target, None) for target in mates + peers])

        def pick(values, index):
            result = values[-1]
            for k in range(len(values) - 1):
                result = jnp.where(index == k, values[k], result)
            return result

        def zz_of(j):
            return pick([z, pick([1, 0, 3, 2], z), pick([3, 3, 0, 0], z), pick([2, 2, 1, 1], z)], j)

        def is_own(i):
            return (i == 0) | ((i >= 2) & (lax.rem(i, 2) == 1))

        def block_of(i):
            return zz_of(lax.div(i, 2)) * NY + jnp.where(is_own(i), y, 1 - y)

        def flip_block(j):
            return zz_of(j) * NY + 1 - y

        def own_block(j):
            return zz_of(j) * NY + y

        def a_at(xx, cc):
            return pl.ds(pl.multiple_of(xx * (2 * a_cols) + cc * a_cols, 128), a_cols)

        def c_at(cc):
            return pl.ds(pl.multiple_of(4 * a_cols + cc * c_cols, 128), c_cols)

        def h_view(b, columns):
            return h.at[block_rows(b, rows), columns]

        line = LineGather(
            [0, 1, 2], [own_in.at[:, a_at(x, c)], own_in.at[:, c_at(c)], o_in],
            [
                lambda b: h_view(b, a_at(x, c)),
                lambda b: h_view(b, c_at(c)),
                lambda b: o_all.at[block_rows(b, rows), :],
            ],
            line_s, line_r,
        )

        def h_twin(b, stream, landing=False):
            cc = 1 - c if landing else c
            piece = h_view(b, [a_at(x, cc), c_at(cc), a_at(1 - x, cc)][stream])
            return remote(piece, piece, hc_s.at[b, stream], hc_r.at[b, stream], twin)

        def h_across(b, landing=False):
            piece = h_view(b, a_at(1 - x if landing else x, c))
            return remote(piece, piece, hx_s.at[b], hx_r.at[b], across)

        def gather_event(rel):
            def body():
                b = line.block(rel)
                marks = len(line.pending)
                for stream in (0, 1):
                    line.arrive(stream, rel)
                    if rel < 7:
                        line.start(stream, rel)
                    if stream == 0:
                        h_across(b).start()
                    h_twin(b, stream).start()
                late = line.pending[marks:]
                del line.pending[marks:]
                line.finish_later(late, rel)
            run_if(line.exists(rel), body)

        def attended_event(rel):
            def body():
                marks = len(line.pending)
                line.arrive(2, rel)
                if rel < 7:
                    line.start(2, rel)
                late = line.pending[marks:]
                del line.pending[marks:]
                line.finish_later(late, rel)
            run_if(line.exists(rel), body)

        def relay(i):
            b = block_of(i)
            h_across(b, True).wait_recv()
            h_twin(b, 2).start()

        for stream in (0, 1):
            line.start(stream, 0)
        keep = pltpu.make_async_copy(own_in, h.at[block_rows(z * NY + y, rows), :], own_sem)
        keep.start()
        keep_o = pltpu.make_async_copy(o_in, o_all.at[block_rows(z * NY + y, rows), :], o_sem)
        keep_o.start()

        def load(i):
            r = block_rows(block_of(i), rows)
            return pltpu.make_async_copy(dy_in.at[r, :], dy.at[r, :], in_sem.at[i])

        def start_load(i, carry):
            load(i).start()
            return carry

        lax.fori_loop(0, GROUPS, start_load, 0)
        x1_copies = [
            pltpu.make_async_copy(
                x1_in.at[:, pl.ds(pl.multiple_of(c * half + s * part + x * piece, piece), piece)],
                x1.at[:, pl.ds(s * piece, piece)], x1_sem.at[s],
            )
            for s in range(2)
        ]
        for copy in x1_copies:
            copy.start()

        def to_twin(i):
            b = block_of(i)
            return remote(
                dx.at[lax.rem(i, 2), :, pl.ds(pl.multiple_of((1 - c) * half, half), half)],
                core_buf.at[b], core_s.at[i], core_r.at[i], twin,
            )

        def p_across(i):
            b = block_of(i)
            return remote(
                core_buf.at[b, :, pl.ds(pl.multiple_of((1 - x) * piece, piece), piece)],
                px_buf.at[b], px_s.at[i], px_r.at[i], across,
            )

        def p_beside(j):
            return remote(px_buf.at[flip_block(j)], py_buf.at[j], py_s.at[j], py_r.at[j], beside)

        def q_beside(j):
            return remote(
                core_buf.at[flip_block(j), :, pl.ds(part, part)], qy_buf.at[j], qy_s.at[j], qy_r.at[j], beside
            )

        def q_across(j):
            return remote(
                qy_buf.at[j, :, pl.ds(pl.multiple_of((1 - x) * piece, piece), piece)],
                qx_buf.at[j], qx_s.at[j], qx_r.at[j], across,
            )

        def up(j, s):
            return remote(z_sum.at[s, j], lo_buf.at[s, j], z_s.at[0, s, j], z_r.at[0, s, j], device(z + 1, y, x, c))

        def down_z(j, s):
            return remote(z_sum.at[s, j], hi_buf.at[s, j], z_s.at[1, s, j], z_r.at[1, s, j], device(z - 1, y, x, c))

        def take_twin(i):
            to_twin(i).wait_recv()
            b = block_of(i)
            mine = core_buf.at[b]
            add_to(mine, mine, dx.at[lax.rem(i, 2), :, pl.ds(pl.multiple_of(c * half, half), half)], 32)
            p_across(i).start()
            pl.when(jnp.logical_not(is_own(i)))(lambda: q_beside(lax.div(i, 2)).start())

        def take_p_across(i):
            p_across(i).wait_recv()
            b = block_of(i)
            add_to(
                px_buf.at[b], px_buf.at[b],
                core_buf.at[b, :, pl.ds(pl.multiple_of(x * piece, piece), piece)],
            )

        def take_q_beside(j):
            q_beside(j).wait_recv()
            add_to(qy_buf.at[j], qy_buf.at[j], core_buf.at[own_block(j), :, pl.ds(part, part)])
            q_across(j).start()

        def take_q_across(j):
            q_across(j).wait_recv()
            add_to(
                z_sum.at[1, zz_of(j)], qx_buf.at[j], qy_buf.at[j, :, pl.ds(pl.multiple_of(x * piece, piece), piece)]
            )

        def take_p_beside(j):
            p_beside(j).wait_recv()
            add_to(z_sum.at[0, zz_of(j)], py_buf.at[j], px_buf.at[own_block(j)])

        def hop(j, k):
            zz = zz_of(j)

            def upward():
                for s in range(2):
                    if k > 0:
                        up(zz, s).wait_recv()
                        add_to(z_sum.at[s, zz], z_sum.at[s, zz], lo_buf.at[s, zz])
                    up(zz, s).start()

            def downward():
                for s in range(2):
                    if k > 0:
                        down_z(zz, s).wait_recv()
                        add_to(z_sum.at[s, zz], z_sum.at[s, zz], hi_buf.at[s, zz])
                    down_z(zz, s).start()

            pl.when((z < zz) & (z == k))(upward)
            pl.when((z > zz) & (NZ - 1 - z == k))(downward)

        def y_twin(i):
            return remote(
                y_part.at[lax.rem(i, 2), :, pl.ds(pl.multiple_of((1 - c) * half, half), half)],
                yc_buf.at[block_of(i)], yc_s.at[i], yc_r.at[i], twin,
            )

        def yp_across(i):
            b = block_of(i)
            return remote(
                yc_buf.at[b, :, pl.ds(pl.multiple_of((1 - x) * piece, piece), piece)],
                ypx_buf.at[b], ypx_s.at[i], ypx_r.at[i], across,
            )

        def yp_beside(j):
            return remote(ypx_buf.at[flip_block(j)], ypy_buf.at[j], ypy_s.at[j], ypy_r.at[j], beside)

        def yq_beside(j):
            return remote(
                yc_buf.at[flip_block(j), :, pl.ds(part, part)], yqy_buf.at[j], yqy_s.at[j], yqy_r.at[j], beside
            )

        def yq_across(j):
            return remote(
                yqy_buf.at[j, :, pl.ds(pl.multiple_of((1 - x) * piece, piece), piece)],
                yqx_buf.at[j], yqx_s.at[j], yqx_r.at[j], across,
            )

        def y_up(zz, s):
            return remote(
                yz_sum.at[s, zz], ylo_buf.at[s, zz], yz_s.at[0, s, zz], yz_r.at[0, s, zz], device(z + 1, y, x, c)
            )

        def y_down(zz, s):
            return remote(
                yz_sum.at[s, zz], yhi_buf.at[s, zz], yz_s.at[1, s, zz], yz_r.at[1, s, zz], device(z - 1, y, x, c)
            )

        def take_y_twin(i):
            y_twin(i).wait_recv()
            mine = yc_buf.at[block_of(i)]
            add_to(mine, mine, y_part.at[lax.rem(i, 2), :, pl.ds(pl.multiple_of(c * half, half), half)], 32)
            yp_across(i).start()
            pl.when(jnp.logical_not(is_own(i)))(lambda: yq_beside(lax.div(i, 2)).start())

        def take_yp_across(i):
            yp_across(i).wait_recv()
            b = block_of(i)
            add_to(
                ypx_buf.at[b], ypx_buf.at[b],
                yc_buf.at[b, :, pl.ds(pl.multiple_of(x * piece, piece), piece)],
            )
            pl.when(jnp.logical_not(is_own(i)))(lambda: yp_beside(lax.div(i, 2)).start())

        def take_yq_beside(j):
            yq_beside(j).wait_recv()
            add_to(yqy_buf.at[j], yqy_buf.at[j], yc_buf.at[own_block(j), :, pl.ds(part, part)])
            yq_across(j).start()

        def take_y_sums(j):
            zz = zz_of(j)
            yq_across(j).wait_recv()
            add_to(
                yz_sum.at[1, zz], yqx_buf.at[j], yqy_buf.at[j, :, pl.ds(pl.multiple_of(x * piece, piece), piece)]
            )
            yp_beside(j).wait_recv()
            add_to(yz_sum.at[0, zz], ypy_buf.at[j], ypx_buf.at[own_block(j)])

        def y_take(zz, s, copy, landed):
            copy(zz, s).wait_recv()
            add_to(yz_sum.at[s, zz], yz_sum.at[s, zz], landed.at[s, zz])

        def y_hop(j, k):
            zz = zz_of(j)

            def upward():
                for s in range(2):
                    if k > 0:
                        y_take(zz, s, y_up, ylo_buf)
                    y_up(zz, s).start()

            def downward():
                for s in range(2):
                    if k > 0:
                        y_take(zz, s, y_down, yhi_buf)
                    y_down(zz, s).start()

            pl.when((z < zz) & (z == k))(upward)
            pl.when((z > zz) & (NZ - 1 - z == k))(downward)

        def front(i):
            load(i).wait()
            b = block_of(i)
            pl.when(i == 0)(keep.wait)

            def landed():
                for stream in range(3):
                    h_twin(b, stream, True).wait_recv()

            pl.when(i > 0)(landed)
            r = block_rows(b, rows)
            rows_h, rows_dy = h[r, :], dy[r, :]
            logits = dot(rows_h, router_ref[...], (1, 1))
            shifted = jnp.exp(logits - jnp.max(logits, axis=-1, keepdims=True))
            probs = shifted / jnp.sum(shifted, axis=-1, keepdims=True) * chosen_ref[r, :].astype(jnp.float32)
            lane = lax.broadcasted_iota(jnp.int32, probs.shape, 1)
            line = lax.broadcasted_iota(jnp.int32, (rows, 128), 1)
            found = jnp.zeros((rows, 128), jnp.float32)
            for expert in range(local):
                at, up_at = pl.ds(expert * hidden, hidden), pl.ds((local + expert) * hidden, hidden)
                gate = jnp.sum(jnp.where(lane == e * local + expert, probs, 0.0), axis=-1, keepdims=True)
                pre = dot(rows_h, gu_ref[:, at], (1, 0))
                scale = dot(rows_h, gu_ref[:, up_at], (1, 0))
                back = dot(rows_dy, down_ref[at, :], (1, 1))
                sigmoid = jax.nn.sigmoid(pre)
                swish = pre * sigmoid
                active = swish * scale
                gated[r, at] = (active * gate).astype(low)
                found = jnp.where(line == expert, jnp.sum(active * back, axis=-1, keepdims=True), found)
                back = back * gate
                dgu[r, at] = (back * scale * sigmoid * (1.0 + pre * (1.0 - sigmoid))).astype(low)
                dgu[r, up_at] = (back * swish).astype(low)
            gate_part[b] = jnp.transpose(found)[:8, :]

        def rear(i):
            r = block_rows(block_of(i), rows)
            slot = lax.rem(i, 2)
            pl.when(i >= 2)(lambda: to_twin(i - 2).wait_send())

            def columns(k, carry):
                at = pl.ds(pl.multiple_of(k * wide, wide), wide)
                dx[slot, :, at] = dot(dgu[r, :], gu_ref[at, :], (1, 1)).astype(low)
                return carry

            lax.fori_loop(0, width // wide, columns, 0)
            to_twin(i).start()
            pl.when(i >= 2)(lambda: y_twin(i - 2).wait_send())

            def y_columns(k, carry):
                at = pl.ds(pl.multiple_of(k * wide, wide), wide)
                y_part[slot, :, at] = dot(gated[r, :], down_ref[:, at], (1, 0)).astype(low)
                return carry

            lax.fori_loop(0, width // wide, y_columns, 0)
            y_twin(i).start()

        tile_width = piece // 2
        tiles = width // tile_width // 4
        d_width = width // 8

        def gu_copies(n):
            slot = lax.rem(n, 2)
            at = pl.ds(pl.multiple_of(n * tile_width, tile_width), tile_width)
            return [
                pltpu.make_async_copy(
                    gu_stage.at[slot, :, pl.ds(k * hidden, hidden)],
                    (gate_w if k < local else up_w).at[k % local, at, :],
                    gu_sem.at[slot, k],
                )
                for k in range(2 * local)
            ]

        def d_copies(n):
            slot = lax.rem(n, 2)
            at = pl.ds(pl.multiple_of(n * d_width, d_width), d_width)
            return [
                pltpu.make_async_copy(
                    d_stage.at[slot, pl.ds(k * hidden, hidden), :], down_w.at[k, :, at], d_sem.at[slot, k]
                )
                for k in range(local)
            ]

        def each(copies, what):
            for copy in copies:
                getattr(copy, what)()

        def weight_grads(q):
            def tile(k, carry):
                n = q * tiles + k
                pl.when(n >= 2)(lambda: each(gu_copies(n - 2), "wait"))
                at = pl.ds(pl.multiple_of(n * tile_width, tile_width), tile_width)
                gu_stage[lax.rem(n, 2)] = dot(h[:, at], dgu[...], (0, 0))
                each(gu_copies(n), "start")
                return carry

            lax.fori_loop(0, tiles, tile, 0)

            def d_tile(k, carry):
                n = q * 2 + k
                pl.when(n >= 2)(lambda: each(d_copies(n - 2), "wait"))
                at = pl.ds(pl.multiple_of(n * d_width, d_width), d_width)
                d_stage[lax.rem(n, 2)] = dot(gated[...], dy[:, at], (0, 0))
                each(d_copies(n), "start")
                return carry

            lax.fori_loop(0, 2, d_tile, 0)

        near = [
            remote(gate_part, gate_land.at[k], near_s.at[k], near_r.at[k], mates[k])
            for k in range(tensors - 1)
        ]

        def far(k):
            return remote(
                gate_land.at[tensors - 1, lax.rem(e + k, GROUPS)], gates_out.at[e],
                far_s.at[k - 1], far_r.at[k - 1], peers[k - 1],
            )

        def sum_near():
            for copy in near:
                copy.wait_recv()
            total = gate_part[...]
            for k in range(tensors - 1):
                total = total + gate_land[k]
            gate_land[tensors - 1] = total
            for k in range(1, GROUPS):
                far(k).start()
            gates_out[e] = gate_land[tensors - 1, e]

        def step(i, carry):
            def at(number, body):
                pl.when(i == number)(body)

            odd, even = lax.rem(i, 2) == 1, lax.rem(i, 2) == 0
            j_even, j_odd = lax.div(i, 2) - 1, lax.div(i - 1, 2) - 1
            pl.when(i < GROUPS)(lambda: front(i))

            def events(*rels):
                for rel in rels:
                    gather_event(rel)

            at(1, lambda: events(2, 5, 8, 11))
            at(2, lambda: events(3, 6))
            at(3, lambda: events(10, 13))

            def attended_events(*rels):
                for rel in rels:
                    attended_event(rel)

            at(8, lambda: attended_events(1, 4))
            at(9, lambda: attended_events(2, 5))
            at(10, lambda: attended_events(3, 6))
            at(11, lambda: attended_events(7, 8, 11))

            pl.when((i >= 1) & (i <= GROUPS))(lambda: take_twin(i - 1))
            pl.when(even & (i >= 4) & (i <= GROUPS))(lambda: take_q_beside(j_even))
            at(3, lambda: take_q_beside(0))
            at(4, lambda: take_q_across(0))

            def late():
                take_p_across(i - 2)
                pl.when(i > 3)(lambda: take_q_across(j_odd))
                pl.when(i == 3)(lambda: p_beside(0).start())

            pl.when(odd & (i >= 3) & (i <= GROUPS + 1))(late)
            at(GROUPS, lambda: each(near, "start"))
            at(GROUPS + 1, sum_near)
            pl.when(i < GROUPS)(lambda: rear(i))
            pl.when(i >= GROUPS)(lambda: weight_grads(i - GROUPS))
            at(0, lambda: events(7, 1, 4))
            at(2, lambda: events(9, 12))
            at(6, lambda: line.start(2, 0))
            pl.when(i < GROUPS - 1)(lambda: relay(i + 1))

            def pass_p():
                take_p_across(i - 2)
                pl.when(i > 2)(lambda: p_beside(j_even).start())

            pl.when(even & (i >= 2) & (i <= GROUPS))(pass_p)
            at(4, lambda: take_p_beside(0))

            def join():
                take_p_beside(j_odd)
                hop(j_odd, 0)

            pl.when(odd & (i >= 5) & (i <= GROUPS + 1))(join)
            pl.when((i == GROUPS) | (i == GROUPS + 2))(lambda: hop(j_even - 1, 1))
            at(GROUPS + 1, lambda: hop(1, 2))
            pl.when((i >= 2) & (i <= GROUPS + 1))(lambda: take_yp_across(i - 2))
            pl.when((i >= 1) & (i <= GROUPS))(lambda: take_y_twin(i - 1))
            pl.when(even & (i >= 4) & (i <= GROUPS))(lambda: take_yq_beside(j_even))
            at(3, lambda: take_yq_beside(0))
            at(5, lambda: take_y_sums(0))

            def join_y():
                take_y_sums(j_even - 1)
                y_hop(j_even - 1, 0)

            pl.when(even & (i >= 6) & (i <= GROUPS + 2))(join_y)
            pl.when((i == GROUPS + 1) | (i == GROUPS + 3))(lambda: y_hop(j_odd - 1, 1))
            at(GROUPS + 2, lambda: y_hop(1, 2))
            return carry

        lax.fori_loop(0, steps, step, 0)

        for rel in (9, 12, 10, 13):
            attended_event(rel)

        def columns_of(s, xx, cc):
            return pl.ds(pl.multiple_of(cc * half + s * part + xx * piece, piece), piece)

        mine = z
        for s in range(2):
            def below(s=s):
                up(mine, s).wait_recv()
                add_to(z_sum.at[s, mine], z_sum.at[s, mine], lo_buf.at[s, mine])

            def above(s=s):
                down_z(mine, s).wait_recv()
                add_to(z_sum.at[s, mine], z_sum.at[s, mine], hi_buf.at[s, mine])

            pl.when(z > 0)(below)
            pl.when(z < NZ - 1)(above)
            own = dh_out.at[:, columns_of(s, x, c)]

            def keep(k, carry, s=s, own=own):
                r = pl.ds(pl.multiple_of(k * 64, 64), 64)
                own[r, :] = z_sum[s, mine, r, :]
                return carry

            lax.fori_loop(0, rows // 64, keep, 0)
            remote(own, own, end_s.at[0, s], end_r.at[0, s], across).start()
            remote(own, own, end_s.at[1, s], end_r.at[1, s], twin).start()
        for copy in x1_copies:
            copy.wait()
        for s in range(2):
            pl.when(z > 0)(lambda s=s: y_take(z, s, y_up, ylo_buf))
            pl.when(z < NZ - 1)(lambda s=s: y_take(z, s, y_down, yhi_buf))
            y_own = block_out.at[:, columns_of(s, x, c)]

            def finish(k, carry, s=s, y_own=y_own):
                r = pl.ds(pl.multiple_of(k * 64, 64), 64)
                y_own[r, :] = (
                    x1[r, pl.ds(s * piece, piece)] + yz_sum[s, z, r, :].astype(jnp.float32)
                ).astype(low)
                return carry

            lax.fori_loop(0, rows // 64, finish, 0)
            remote(y_own, y_own, end_s.at[0, 2 + s], end_r.at[0, 2 + s], across).start()
            remote(y_own, y_own, end_s.at[1, 2 + s], end_r.at[1, 2 + s], twin).start()
        for s in range(2):
            there = dh_out.at[:, columns_of(s, 1 - x, c)]
            remote(there, there, end_s.at[0, s], end_r.at[0, s], across).wait_recv()
            remote(there, there, end_s.at[2, s], end_r.at[2, s], twin).start()
        for s in range(2):
            there = block_out.at[:, columns_of(s, 1 - x, c)]
            remote(there, there, end_s.at[0, 2 + s], end_r.at[0, 2 + s], across).wait_recv()
            remote(there, there, end_s.at[2, 2 + s], end_r.at[2, 2 + s], twin).start()
        for n, result in ((0, dh_out), (2, block_out)):
            for s in range(2):
                for k, xx in ((1, x), (2, 1 - x)):
                    there = result.at[:, columns_of(s, xx, 1 - c)]
                    remote(there, there, end_s.at[k, n + s], end_r.at[k, n + s], twin).wait_recv()
                for k, target in ((0, across), (1, twin), (2, twin)):
                    there = result.at[:, columns_of(s, 1 - x if k == 2 else x, c)]
                    remote(there, there, end_s.at[k, n + s], end_r.at[k, n + s], target).wait_send()
        for k in range(1, GROUPS):
            there = gates_out.at[lax.rem(e + GROUPS - k, GROUPS)]
            remote(there, there, far_s.at[k - 1], far_r.at[k - 1], peers[k - 1]).wait_recv()
            far(k).wait_send()
        each(near, "wait_send")

        def drain(i, carry):
            pl.when(i >= GROUPS - 2)(lambda: to_twin(i).wait_send())
            pl.when(i >= GROUPS - 2)(lambda: y_twin(i).wait_send())
            p_across(i).wait_send()
            yp_across(i).wait_send()
            return carry

        lax.fori_loop(0, GROUPS, drain, 0)

        def drain_pair(j, carry):
            p_beside(j).wait_send()
            q_beside(j).wait_send()
            q_across(j).wait_send()
            yp_beside(j).wait_send()
            yq_beside(j).wait_send()
            yq_across(j).wait_send()
            for s in range(2):
                pl.when(z < j)(lambda s=s: up(j, s).wait_send())
                pl.when(z > j)(lambda s=s: down_z(j, s).wait_send())
                pl.when(z < j)(lambda s=s: y_up(j, s).wait_send())
                pl.when(z > j)(lambda s=s: y_down(j, s).wait_send())
            return carry

        lax.fori_loop(0, NZ, drain_pair, 0)

        def drain_rows_of(i, carry):
            b = block_of(i)
            h_across(b).wait_send()
            for stream in range(3):
                h_twin(b, stream).wait_send()
            return carry

        lax.fori_loop(1, GROUPS, drain_rows_of, 0)
        line.finish()
        keep_o.wait()
        for k in range(2):
            each(gu_copies(4 * tiles - 2 + k), "wait")
            each(d_copies(6 + k), "wait")

    shape = jax.ShapeDtypeStruct
    dma = pltpu.SemaphoreType.DMA
    f32 = jnp.float32
    return pl.pallas_call(
        kernel,
        out_shape=(
            shape((rows, width), low),
            shape((rows, width), low),
            shape((GROUPS, 8, rows), f32),
            shape((local, width, hidden), f32),
            shape((local, width, hidden), f32),
            shape((local, hidden, width), f32),
            shape((tokens,) + attended.shape[1:], low),
        ),
        in_specs=[HBM, HBM, VMEM, VMEM, VMEM, VMEM, HBM, HBM],
        out_specs=(VMEM, VMEM, VMEM, HBM, HBM, HBM, HBM),
        scratch_shapes=[
            pltpu.VMEM((tokens, width), low),
            pltpu.VMEM((tokens, width), low),
            pltpu.VMEM((tokens, units), low),
            pltpu.VMEM((tokens, 2 * units), low),
            pltpu.VMEM((2, rows, width), low),
            pltpu.VMEM((2, rows, width), low),
            pltpu.VMEM((GROUPS, rows, half), low),
            pltpu.VMEM((GROUPS, rows, piece), low),
            pltpu.VMEM((NZ, rows, piece), low),
            pltpu.VMEM((NZ, rows, part), low),
            pltpu.VMEM((NZ, rows, piece), low),
            pltpu.VMEM((2, NZ, rows, piece), low),
            pltpu.VMEM((2, NZ, rows, piece), low),
            pltpu.VMEM((2, NZ, rows, piece), low),
            pltpu.VMEM((rows, part), f32),
            pltpu.VMEM((2, piece // 2, 2 * units), f32),
            pltpu.VMEM((2, units, width // 8), f32),
            pltpu.VMEM((GROUPS, rows, half), low),
            pltpu.VMEM((GROUPS, rows, piece), low),
            pltpu.VMEM((NZ, rows, piece), low),
            pltpu.VMEM((NZ, rows, part), low),
            pltpu.VMEM((NZ, rows, piece), low),
            pltpu.VMEM((2, NZ, rows, piece), low),
            pltpu.VMEM((2, NZ, rows, piece), low),
            pltpu.VMEM((2, NZ, rows, piece), low),
            pltpu.VMEM((GROUPS, 8, rows), f32),
            pltpu.VMEM((tensors, GROUPS, 8, rows), f32),
            dma((GROUPS,)), dma, dma, dma((3, 14, 3)), dma((3, 14)), dma((GROUPS,)), dma((GROUPS,)),
            dma((GROUPS, 3)), dma((GROUPS, 3)), dma((2,)), dma((GROUPS,)), dma((GROUPS,)), dma((GROUPS,)), dma((GROUPS,)),
            dma((NZ,)), dma((NZ,)), dma((NZ,)), dma((NZ,)), dma((NZ,)), dma((NZ,)),
            dma((2, 2, NZ)), dma((2, 2, NZ)), dma((2, 2 * local)), dma((2, local)),
            dma((GROUPS,)), dma((GROUPS,)), dma((GROUPS,)), dma((GROUPS,)),
            dma((NZ,)), dma((NZ,)), dma((NZ,)), dma((NZ,)), dma((NZ,)), dma((NZ,)),
            dma((2, 2, NZ)), dma((2, 2, NZ)),
            dma((tensors - 1,)), dma((tensors - 1,)), dma((GROUPS - 1,)), dma((GROUPS - 1,)),
            dma((3, 4)), dma((3, 4)),
        ],
        compiler_params=comm_params(collective_id, 62),
        cost_estimate=cost(80),
        name="expert_layer",
    )(hidden_two, grad_out_all, gate_up, down, router_t, chosen_all, residual, attended)


def exchange_rows(value, part_ref, land_ref, send_sem, recv_sem, mates):
    rows = value.shape[0]
    line = lax.broadcasted_iota(jnp.int32, (rows, 128), 1)
    part_ref[...] = jnp.transpose(jnp.where(line == 0, value, 0.0))[:8, :]
    for k, mate in enumerate(mates):
        remote(part_ref, land_ref.at[k], send_sem.at[k], recv_sem.at[k], mate).start()


def exchanged_rows(part_ref, land_ref, send_sem, recv_sem, mates):
    total = part_ref[...]
    for k, mate in enumerate(mates):
        remote(part_ref, land_ref.at[k], send_sem.at[k], recv_sem.at[k], mate).wait_recv()
    for k in range(len(mates)):
        total = total + land_ref[k]
    rows = part_ref.shape[1]
    tall = jnp.concatenate([total, jnp.zeros((120, rows), jnp.float32)], axis=0)
    return jnp.transpose(tall)[:, :1]


def drain_rows(part_ref, land_ref, send_sem, recv_sem, mates):
    for k, mate in enumerate(mates):
        remote(part_ref, land_ref.at[k], send_sem.at[k], recv_sem.at[k], mate).wait_send()


def turn(value, cosine, sine):
    return value * cosine + pltpu.roll(value, HEAD // 2, 1) * sine


def project(
    tokens, w_qkv, w_out, out_grad, smalls, cosine, sine, w_gate, w_up, w_down, experts, collective_id
):
    rows, width = tokens.shape
    parts, depth, columns = w_qkv.shape
    heads = columns // HEAD
    tensors = NX * NC
    back = WINDOW // rows
    low, f32 = jnp.bfloat16, jnp.float32
    QUERY, KEY, VALUE, SMALL, OUT, GRAD, REST = 0, 1, 2, 3, 4, 5, 6
    out_half = w_out.shape[0] // 2
    out_rows, out_columns = w_out.shape
    quarter = width // tensors

    def kernel(
        tok_ref, w_ref, out_ref, grad_in, small_ref, cos_ref, sin_ref, gate_in, up_in, down_in,
        w_all, out_all, grad_all, h1_out, raw_out, gate_up, down_out, gain_ref, router_ref, chosen_ref, scale_ref, q_ref, context,
        small_all, h1_ref, raw_ref, wide_in, wide_low, down_f, down_low, own_w, own_out, weights, total, part_k, land_k, part_q, land_q,
        send_sem, recv_sem, out_sem, small_sem, kept, ks_s, ks_r, qs_s, qs_r, c_s, c_r, hx_s, hx_r, hc_s, hc_r, wide_s,
    ):
        z, y, x, c = place()
        e, t = lax.axis_index("expert"), lax.axis_index("tensor")
        wide_loads = [
            pltpu.make_async_copy(source.at[k], wide_in.at[2 * n + k], wide_s.at[2 * n + k])
            for n, source in enumerate((gate_in, up_in))
            for k in range(2)
        ]
        for copy in wide_loads:
            copy.start()
        mates = [(e, lax.rem(t + k, tensors)) for k in range(1, tensors)]
        beside, above = device(z, 1 - y, x, c), device(z + 1, y, x, c)
        views = [
            lambda b: weights.at[QUERY, block_rows(b, depth), :],
            lambda b: weights.at[KEY, block_rows(b, depth), :],
            lambda b: weights.at[VALUE, block_rows(b, depth), :],
            lambda b: small_all.at[b],
            lambda b: out_all.at[pl.ds(0, out_half), block_rows(b, out_columns)],
            lambda b: grad_view(b, x, c),
            lambda b: out_all.at[pl.ds(out_half, out_half), block_rows(b, out_columns)],
        ]
        across, twin = device(z, y, 1 - x, c), device(z, y, x, 1 - c)

        def quarter_at(xx, cc):
            return pl.ds(pl.multiple_of((xx * NC + cc) * quarter, quarter), quarter)

        def grad_view(b, xx, cc):
            return grad_all.at[block_rows(b, rows), quarter_at(xx, cc)]

        def grad_across(b, landing=False):
            piece = grad_view(b, 1 - x if landing else x, c)
            return remote(piece, piece, hx_s.at[b], hx_r.at[b], across)

        def grad_twin(b, relayed, landing=False):
            piece = grad_view(b, 1 - x if relayed else x, 1 - c if landing else c)
            return remote(piece, piece, hc_s.at[b, relayed], hc_r.at[b, relayed], twin)

        line = LineGather(
            [SMALL, VALUE, KEY, QUERY, OUT, GRAD, REST],
            [
                own_w.at[0], own_w.at[1], own_w.at[2], small_ref, own_out.at[pl.ds(0, out_half)],
                grad_in.at[:, quarter_at(x, c)], own_out.at[pl.ds(out_half, out_half)],
            ],
            views, send_sem, recv_sem, y_first=(OUT,),
        )
        greet(line.partners() + [(mate, None) for mate in mates])
        line.start(SMALL, 0)
        for part in (VALUE, KEY, QUERY):
            def cast(i, carry, part=part):
                r = pl.ds(pl.multiple_of(i * 32, 32), 32)
                own_w[part, r, :] = w_ref[part, r, :].astype(low)
                return carry

            lax.fori_loop(0, depth // 32, cast, 0)
            if part != QUERY:
                line.start(part, 0)

        def cast_out(i, carry):
            r = pl.ds(pl.multiple_of(i * 32, 32), 32)
            own_out[r, :] = out_ref[r, :].astype(low)
            return carry

        lax.fori_loop(0, out_rows // 32, cast_out, 0)
        keep_out = pltpu.make_async_copy(own_out, out_all.at[:, block_rows(line.block(0), out_columns)], kept.at[0])
        keep_out.start()
        keep_grad = pltpu.make_async_copy(grad_in, grad_all.at[block_rows(line.block(0), rows), :], kept.at[1])
        keep_grad.start()

        def square(i, carry):
            r = pl.ds(pl.multiple_of(i * 32, 32), 32)
            value = tok_ref[r, :].astype(f32)
            scale_ref[r, 0:1] = lax.rsqrt(jnp.mean(value * value, axis=-1, keepdims=True) + EPS)
            return carry

        lax.fori_loop(0, rows // 32, square, 0)
        total[...] = jnp.zeros_like(total)
        own_small = pltpu.make_async_copy(small_ref, small_all.at[line.block(0)], small_sem)
        own_small.start()

        def use(stream, rel):
            b = line.block(rel)
            at = pl.ds(pl.multiple_of(b * depth, depth), depth)
            if stream == SMALL:
                gain = small_ref[0:1, :] if rel == 0 else small_all[b, 0:1, :]
                h1_ref[:, at] = (tok_ref[:, at].astype(f32) * scale_ref[:, 0:1] * gain).astype(low)
                return
            block = own_w[stream] if rel == 0 else weights[stream, block_rows(b, depth), :]
            total[stream] += dot(h1_ref[:, at], block, (1, 0))

        def event(stream, rel):
            def body():
                line.arrive(stream, rel)
                if line.forwards(stream, rel):
                    marks = len(line.pending)
                    line.start(stream, rel)
                    late = line.pending[marks:]
                    del line.pending[marks:]
                    line.finish_later(late, rel)
                if stream == GRAD:
                    b = line.block(rel)
                    grad_across(b).start()
                    grad_twin(b, 0).start()
                elif stream not in (OUT, REST):
                    use(stream, rel)
            run_if(line.exists(rel), body)

        use(SMALL, 0)
        use(VALUE, 0)
        own_small.wait()

        units = down_in.shape[1]
        for n, copy in enumerate(wide_loads):
            copy.wait()

            def round_wide(i, carry, n=n):
                r = pl.ds(pl.multiple_of(i * 64, 64), 64)
                wide_low[r, pl.ds(n * units, units)] = wide_in[n, r, :].astype(low)
                return carry

            lax.fori_loop(0, width // 64, round_wide, 0)
        wide_out = pltpu.make_async_copy(wide_low, gate_up, wide_s.at[0])
        wide_out.start()
        down_loads = [
            pltpu.make_async_copy(down_in.at[k], down_f.at[pl.ds(k * units, units), :], wide_s.at[1 + k])
            for k in range(2)
        ]
        for copy in down_loads:
            copy.start()

        use(KEY, 0)
        def events(*pairs):
            for stream, rels in pairs:
                for rel in rels:
                    event(stream, rel)

        for rel in (7, 1, 4, 2, 5):
            event(SMALL, rel)
            event(VALUE, rel)
        for copy in down_loads:
            copy.wait()

        def round_down(i, carry):
            r = pl.ds(pl.multiple_of(i * 32, 32), 32)
            down_low[r, :] = down_f[r, :].astype(low)
            return carry

        lax.fori_loop(0, 2 * units // 32, round_down, 0)
        down_copy = pltpu.make_async_copy(down_low, down_out, wide_s.at[3])
        down_copy.start()
        line.start(QUERY, 0)
        for rel in (3, 6):
            event(SMALL, rel)
            event(VALUE, rel)
        events((KEY, (7, 1, 4)))
        for rel in (8, 11, 9, 12, 10, 13):
            event(SMALL, rel)
            event(VALUE, rel)

        slices = HEAD // GROUPS
        for b in range(GROUPS):
            at = pl.ds(b * depth, depth)
            gain_ref[0:2, at] = small_all[b, 0:2, :]
            router_ref[:, at] = small_all[b, 8 : 8 + experts, :].astype(low)
            tall = jnp.concatenate(
                [small_all[b, 8 + experts : 8 + 2 * experts, :], jnp.zeros((128 - experts, depth), f32)], axis=0
            )
            chosen_ref[pl.ds(b * depth, depth), :] = jnp.transpose(tall)[:, :experts].astype(low)
        for which in range(2):
            for head in range(heads):
                start = (which * heads + head) * slices
                gain_ref[2 + which : 3 + which, pl.ds(head * HEAD, HEAD)] = jnp.concatenate(
                    [small_all[b, 2:3, start : start + slices] for b in range(GROUPS)], axis=1
                )

        def context_copy(which, k):
            if k == 2:
                source, target = 0, above
            elif k == 4:
                source, target = 2, above
            else:
                source, target = jnp.where(y == 0, k - 1, k + 1), beside
            return remote(
                context.at[source, which], context.at[k, which], c_s.at[which, k], c_r.at[which, k], target
            )

        sends = {2: z < NZ - 1, 4: (z >= 1) & (z < NZ - 1), 1: (y == 0) | (z >= 1), 3: z >= 1 + y}
        takes = {2: z >= 1, 4: z >= 2, 1: (y == 1) | (z >= 1), 3: z >= 2 - y}

        def context_send(which, k):
            run_if(sends[k], lambda: context_copy(which, k).start())

        def context_take(which, k):
            run_if(takes[k], lambda: context_copy(which, k).wait_recv())

        for k in range(1, back + 1):
            def clear(k=k):
                context[k] = jnp.zeros_like(context[k])
            run_if(jnp.logical_not(takes[k]), clear)

        context[0, 1] = total[VALUE].astype(low)
        context_send(1, 2)
        run_if(y == 0, lambda: context_copy(1, 1).start())
        events((KEY, (2, 5, 3, 6)), (QUERY, (7, 1, 4)))
        line.start(GRAD, 0)
        line.start(OUT, 0)
        line.start(REST, 0)
        events((KEY, (8, 11, 9, 12, 10, 13)))
        key_raw = total[KEY]
        raw_ref[1] = key_raw
        exchange_rows(jnp.sum(key_raw * key_raw, axis=-1, keepdims=True), part_k, land_k, ks_s, ks_r, mates)
        use(QUERY, 0)
        events((QUERY, (2, 5)))
        key_scale = lax.rsqrt(exchanged_rows(part_k, land_k, ks_s, ks_r, mates) / width + EPS)
        scale_ref[:, 2:3] = key_scale
        def rotated(which, scale, store):
            for head in range(heads):
                at = pl.ds(head * HEAD, HEAD)
                value = total[which, :, at] * scale * gain_ref[2 + which : 3 + which, at]
                store(at, turn(value, cos_ref[...], sin_ref[...]).astype(low))

        def store_key(at, value):
            context[0, 0, :, at] = value

        rotated(KEY, key_scale, store_key)
        context_send(0, 2)
        run_if(y == 0, lambda: context_copy(0, 1).start())

        def relay_two(which):
            context_take(which, 2)
            context_send(which, 4)
            run_if((y == 1) & (z >= 1), lambda: context_copy(which, 1).start())
            run_if((y == 0) & sends[3], lambda: context_copy(which, 3).start())

        def relay_four(which):
            context_take(which, 4)
            run_if((y == 1) & sends[3], lambda: context_copy(which, 3).start())

        relay_two(1)
        events((QUERY, (3, 6)), (GRAD, (7, 1, 4)), (OUT, (7, 1, 4)), (REST, (7, 1, 4)))
        relay_four(1)
        events((QUERY, (8, 11)), (GRAD, (2, 5)), (OUT, (8, 11, 2, 5)), (REST, (2, 5)))
        relay_two(0)
        events((QUERY, (9, 12, 10, 13)))
        query_raw = total[QUERY]
        raw_ref[0] = query_raw
        exchange_rows(jnp.sum(query_raw * query_raw, axis=-1, keepdims=True), part_q, land_q, qs_s, qs_r, mates)
        for part in range(parts):
            weights[part, block_rows(line.block(0), depth), :] = own_w[part]
        keep = pltpu.make_async_copy(weights, w_all, out_sem)
        keep.start()
        keep_more = [
            pltpu.make_async_copy(h1_ref, h1_out, kept.at[2]),
            pltpu.make_async_copy(raw_ref, raw_out, kept.at[3]),
        ]
        for copy in keep_more:
            copy.start()
        events((GRAD, (3, 6)), (OUT, (9, 12, 3, 6)), (REST, (3, 6, 8, 11)))
        relay_four(0)
        query_scale = lax.rsqrt(exchanged_rows(part_q, land_q, qs_s, qs_r, mates) / width + EPS)
        scale_ref[:, 1:2] = query_scale

        def store_query(at, value):
            q_ref[:, at] = value

        rotated(QUERY, query_scale, store_query)
        events((GRAD, (8, 11, 9, 12)), (OUT, (10, 13)), (REST, (9, 12, 10, 13)), (GRAD, (10, 13)))
        for which in (1, 0):
            for k in (1, 3):
                context_take(which, k)
        for rel in line.order():
            def relay(rel=rel):
                b = line.block(rel)
                grad_across(b, True).wait_recv()
                grad_twin(b, 1).start()
            run_if(line.exists(rel), relay)
        for rel in line.order():
            def landed(rel=rel):
                b = line.block(rel)
                grad_across(b).wait_send()
                for relayed in range(2):
                    grad_twin(b, relayed, True).wait_recv()
                    grad_twin(b, relayed).wait_send()
            run_if(line.exists(rel), landed)
        line.finish()
        for copy in keep_more:
            copy.wait()
        wide_out.wait()
        down_copy.wait()
        keep_out.wait()
        keep_grad.wait()
        for which in range(2):
            for k in range(1, back + 1):
                run_if(sends[k], lambda which=which, k=k: context_copy(which, k).wait_send())
        drain_rows(part_k, land_k, ks_s, ks_r, mates)
        drain_rows(part_q, land_q, qs_s, qs_r, mates)
        keep.wait()

    shape, dma = jax.ShapeDtypeStruct, pltpu.SemaphoreType.DMA
    return pl.pallas_call(
        kernel,
        out_shape=(
            shape((parts, depth * GROUPS, columns), low),
            shape((out_rows, out_columns * GROUPS), low),
            shape((rows * GROUPS, width), low),
            shape((rows, width), low),
            shape((2, rows, columns), f32),
            shape((width, 4 * w_down.shape[1]), low),
            shape((2 * w_down.shape[1], width), low),
            shape((8, width), f32),
            shape((experts, width), low),
            shape((rows * GROUPS, experts), low),
            shape((rows, 128), f32),
            shape((rows, columns), low),
            shape((back + 1, 2, rows, columns), low),
        ),
        in_specs=[VMEM, VMEM, VMEM, HBM, VMEM, VMEM, VMEM, HBM, HBM, HBM],
        out_specs=(HBM,) * 7 + (VMEM,) * 6,
        scratch_shapes=[
            pltpu.VMEM((GROUPS,) + smalls.shape, f32),
            pltpu.VMEM((rows, width), low),
            pltpu.VMEM((2, rows, columns), f32),
            pltpu.VMEM((4, width, w_down.shape[1]), f32),
            pltpu.VMEM((width, 4 * w_down.shape[1]), low),
            pltpu.VMEM((2 * w_down.shape[1], width), f32),
            pltpu.VMEM((2 * w_down.shape[1], width), low),
            pltpu.VMEM((parts, depth, columns), low),
            pltpu.VMEM((out_rows, out_columns), low),
            pltpu.VMEM((parts, depth * GROUPS, columns), low),
            pltpu.VMEM((parts, rows, columns), f32),
            pltpu.VMEM((8, rows), f32),
            pltpu.VMEM((tensors - 1, 8, rows), f32),
            pltpu.VMEM((8, rows), f32),
            pltpu.VMEM((tensors - 1, 8, rows), f32),
            dma((7, 14, 3)), dma((7, 14)), dma, dma, dma((4,)),
            dma((tensors - 1,)), dma((tensors - 1,)), dma((tensors - 1,)), dma((tensors - 1,)),
            dma((2, back + 1)), dma((2, back + 1)),
            dma((GROUPS,)), dma((GROUPS,)), dma((GROUPS, 2)), dma((GROUPS, 2)), dma((4,)),
        ],
        compiler_params=comm_params(collective_id, 62),
        cost_estimate=cost(100),
        name="project",
    )(tokens, w_qkv, w_out, out_grad, smalls, cosine, sine, w_gate, w_up, w_down)


def attend(query, context, segment_query, segment_keys, tokens, out_low, gain, collective_id):
    rows, columns = query.shape
    width = tokens.shape[1]
    blocks = context.shape[0]
    heads = columns // HEAD
    half, quarter = width // 2, width // 4
    low, f32 = jnp.bfloat16, jnp.float32

    def kernel(
        q_ref, context_in, sq_ref, sk_ref, tok_ref, out_in, gain_ref,
        o_ref, lse_ref, x1_out, h2_out, scale_ref,
        context_ref, out_ref, x1_ref, h2_ref, copy_sem, part, full, core_buf, x_buf, send_sem, recv_sem,
    ):
        z, y, x, c = place()
        across, twin = device(z, y, 1 - x, c), device(z, y, x, 1 - c)
        context_load = pltpu.make_async_copy(context_in, context_ref, copy_sem.at[0])
        context_load.start()
        out_load = pltpu.make_async_copy(out_in, out_ref, copy_sem.at[1])
        out_load.start()
        greet([(across, None), (twin, None)])
        row = lax.broadcasted_iota(jnp.int32, (rows, rows), 0)
        column = lax.broadcasted_iota(jnp.int32, (rows, rows), 1)
        allowed = []
        for k in range(blocks):
            distance = row - column + k * rows
            allowed.append(
                (sq_ref[...] == sk_ref[k : k + 1, :]) & (distance >= 0) & (distance < WINDOW)
            )
        line = lax.broadcasted_iota(jnp.int32, (rows, 128), 1)
        lse = jnp.zeros((rows, 128), f32)
        context_load.wait()
        for head in range(heads):
            at = pl.ds(head * HEAD, HEAD)
            scores = [
                jnp.where(
                    allowed[k], dot(q_ref[:, at], context_ref[k, 0, :, at], (1, 1)) * HEAD ** (-0.5), -1e30
                )
                for k in range(blocks)
            ]
            largest = scores[0]
            for k in range(1, blocks):
                largest = jnp.maximum(largest, scores[k])
            largest = jnp.max(largest, axis=-1, keepdims=True)
            weights = [jnp.exp(s - largest) for s in scores]
            amount = weights[0]
            for k in range(1, blocks):
                amount = amount + weights[k]
            amount = jnp.sum(amount, axis=-1, keepdims=True)
            inverse = 1.0 / amount
            value = jnp.zeros((rows, HEAD), f32)
            for k in range(blocks):
                value = value + dot((weights[k] * inverse).astype(low), context_ref[k, 1, :, at], (1, 0))
            o_ref[:, at] = value.astype(low)
            lse = jnp.where(line == head, largest + jnp.log(amount), lse)
        lse_ref[...] = lse

        def half_of(cc):
            return pl.ds(pl.multiple_of(cc * half, half), half)

        def fill(cc):
            def body(k, carry):
                at = pl.ds(pl.multiple_of(cc * half + k * quarter, quarter), quarter)
                part[:, at] = dot(o_ref[...], out_ref[:, at], (1, 0)).astype(low)
                return carry

            lax.fori_loop(0, 2, body, 0)

        out_load.wait()
        fill(1 - c)
        group_sum(part, full, core_buf, x_buf, send_sem, recv_sem, lambda: fill(c))

        def norm(i, carry):
            r = pl.ds(pl.multiple_of(i * 32, 32), 32)
            value = tok_ref[r, :].astype(f32) + full[r, :].astype(f32)
            scale = lax.rsqrt(jnp.mean(value * value, axis=-1, keepdims=True) + EPS)
            x1_ref[r, :] = value
            scale_ref[r, :] = jnp.broadcast_to(scale, (32, 128))
            h2_ref[r, :] = (value * scale * gain_ref[1:2, :]).astype(low)
            return carry

        lax.fori_loop(0, rows // 32, norm, 0)
        keep = [
            pltpu.make_async_copy(x1_ref, x1_out, copy_sem.at[2]),
            pltpu.make_async_copy(h2_ref, h2_out, copy_sem.at[3]),
        ]
        for copy in keep:
            copy.start()
        for copy in keep:
            copy.wait()

    shape, dma = jax.ShapeDtypeStruct, pltpu.SemaphoreType.DMA
    return pl.pallas_call(
        kernel,
        out_shape=(
            shape((rows, columns), low),
            shape((rows, 128), f32),
            shape((rows, width), f32),
            shape((rows, width), low),
            shape((rows, 128), f32),
        ),
        in_specs=[VMEM, HBM, VMEM, VMEM, VMEM, HBM, VMEM],
        out_specs=(VMEM, VMEM, HBM, HBM, VMEM),
        scratch_shapes=[
            pltpu.VMEM(context.shape, low),
            pltpu.VMEM(out_low.shape, low),
            pltpu.VMEM((rows, width), f32),
            pltpu.VMEM((rows, width), low),
            dma((4,)),
            pltpu.VMEM((rows, width), low),
            pltpu.VMEM((rows, width), low),
            pltpu.VMEM((rows, half), low),
            pltpu.VMEM((rows, quarter), low),
            dma((5,)), dma((5,)),
        ],
        compiler_params=comm_params(collective_id, 62),
        cost_estimate=cost(40),
        name="attend",
    )(query, context, segment_query, segment_keys, tokens, out_low, gain)


def attend_back(
    grad_hidden, grad_probs, router_t, hidden_two, residual, scale_two, gains, out_grad,
    query, context, segment_query, segment_keys, attended, log_sums, raw, scales,
    cosine, sine, hidden_one, tokens, attended_all, qkv_low, out_low, collective_id,
):
    rows, width = tokens.shape
    columns = query.shape[1]
    heads = columns // HEAD
    experts = router_t.shape[0]
    blocks = context.shape[0]
    depth = width // GROUPS
    small_rows = 8 + experts
    tensors = NX * NC
    half, quarter = width // 2, width // 4
    low, f32 = jnp.bfloat16, jnp.float32
    QUERY, KEY, VALUE, OUT, SMALL = 0, 1, 2, 3, 4

    def kernel(
        dh_ref, gates_ref, router_ref, h2_ref, x1_ref, s2_ref, gain_ref, dy_ref,
        q_ref, context_ref, sq_ref, sk_ref, o_ref, lse_ref, raw_ref, scale_ref,
        cos_ref, sin_ref, h1_ref, tok_ref, o_all, w_hbm, out_ref,
        tok_grad, qkv_sum, out_sum, small_sum,
        weights, dx1, da, do, dot_sums, dq, dkv, scaled, proj, send_kv, land_y, land_z,
        part, full, core_buf, x_buf, small, line_sum,
        main_buf, da_all, small_buf, part_k, land_k, part_q, land_q,
        w_sem, y_s, y_r, z_s, z_r, group_s, group_r, ks_s, ks_r, qs_s, qs_r, line_s, line_r, far_s, far_r, near_s, near_r,
    ):
        z, y, x, c = place()
        e, t = lax.axis_index("expert"), lax.axis_index("tensor")
        mates = [(e, lax.rem(t + k, tensors)) for k in range(1, tensors)]
        beside, below = device(z, 1 - y, x, c), device(z - 1, y, x, c)
        fetch = pltpu.make_async_copy(w_hbm, weights, w_sem)
        fetch.start()

        def own_part(s, b):
            if s == SMALL:
                return small[b]
            at = pl.ds(pl.multiple_of(b * depth, depth), depth)
            return dot(h1_ref[:, at], proj[s], (0, 0))

        peers = [(lax.rem(e + k, GROUPS), t) for k in range(1, GROUPS)]
        share = rows // tensors
        share_at = pl.ds(pl.multiple_of(t * share, share), share)

        def columns_of(owner):
            return pl.ds(pl.multiple_of(owner * depth, depth), depth)

        def da_far(k):
            owner = lax.rem(e + k, GROUPS)
            return remote(
                da.at[share_at, columns_of(owner)], da_all.at[e, share_at, :], far_s.at[k - 1], far_r.at[k - 1],
                peers[k - 1],
            )

        def da_near(k):
            piece = da_all.at[:, share_at, :]
            return remote(piece, piece, near_s.at[k], near_r.at[k], mates[k])

        def da_start():
            for k in range(1, GROUPS):
                da_far(k).start()
            da_all[e, share_at, :] = da[share_at, columns_of(e)]

        def da_spread():
            for k in range(1, GROUPS):
                landing = da_all.at[lax.rem(e + GROUPS - k, GROUPS), share_at, :]
                remote(landing, landing, far_s.at[k - 1], far_r.at[k - 1], peers[k - 1]).wait_recv()
            for k in range(tensors - 1):
                da_near(k).start()

        def da_end():
            for k in range(tensors - 1):
                theirs = lax.rem(t + tensors - 1 - k, tensors)
                landing = da_all.at[:, pl.ds(pl.multiple_of(theirs * share, share), share), :]
                remote(landing, landing, near_s.at[k], near_r.at[k], mates[k]).wait_recv()
            result = jnp.zeros((columns, depth), f32)
            for b in range(GROUPS):
                result = result + dot(o_all[pl.ds(b * rows, rows), :], da_all[b], (0, 0))
            out_sum[...] = result
            for k in range(1, GROUPS):
                da_far(k).wait_send()
            for k in range(tensors - 1):
                da_near(k).wait_send()

        def slot(kind):
            def view(s, zz):
                if s == SMALL:
                    return small_buf.at[kind, zz]
                return main_buf.at[kind, zz, s]
            return view

        line = LineReduce([], lambda s, zz, yy: slot(3)(s, zz), slot(0), slot(1), slot(2), line_s, line_r)
        greet([(target, None) for target in mates + peers])

        grad_probs = gates_ref[...]
        logits = dot(h2_ref[...], router_ref[...], (1, 1))
        shifted = jnp.exp(logits - jnp.max(logits, axis=-1, keepdims=True))
        probs = shifted / jnp.sum(shifted, axis=-1, keepdims=True)
        grad_logits = probs * (grad_probs - jnp.sum(probs * grad_probs, axis=-1, keepdims=True))
        tall = jnp.transpose(
            jnp.concatenate([grad_logits, jnp.zeros((rows, 128 - experts), f32)], axis=1)
        )
        grad_logits = grad_logits.astype(low)
        tall = tall.astype(low)
        for b in range(GROUPS):
            small[b] = jnp.zeros_like(small[b])
            small[b, 8 : 8 + experts, :] = dot(tall, h2_ref[:, pl.ds(b * depth, depth)], (1, 0))[:experts]
        dx1[...] = dot(grad_logits, router_ref[...], (1, 0))
        line_sum[...] = jnp.zeros_like(line_sum)

        def norm_two(i, carry):
            r = pl.ds(pl.multiple_of(i * 32, 32), 32)
            grad = dh_ref[r, :].astype(f32) + dx1[r, :]
            value, scale = x1_ref[r, :], s2_ref[r, 0:1]
            line_sum[0:1, :] += jnp.sum(grad * (value * scale), axis=0, keepdims=True)
            grad = grad * gain_ref[1:2, :]
            inner = jnp.mean(grad * value, axis=-1, keepdims=True)
            result = dy_ref[r, :].astype(f32) + scale * grad - value * (scale * scale * scale) * inner
            dx1[r, :] = result
            da[r, :] = result.astype(low)
            return carry

        lax.fori_loop(0, rows // 32, norm_two, 0)

        da_start()

        do[...] = dot(da[...], out_ref[...], (1, 1)).astype(low)
        wide = lax.broadcasted_iota(jnp.int32, (rows, 128), 1)
        sums = jnp.zeros((rows, 128), f32)
        for head in range(heads):
            at = pl.ds(head * HEAD, HEAD)
            inner = jnp.sum(do[:, at].astype(f32) * o_ref[:, at].astype(f32), axis=-1, keepdims=True)
            sums = jnp.where(wide == head, inner, sums)
        dot_sums[...] = sums
        dq[...] = jnp.zeros_like(dq)
        row = lax.broadcasted_iota(jnp.int32, (rows, rows), 0)
        column = lax.broadcasted_iota(jnp.int32, (rows, rows), 1)

        def attention_block(k):
            distance = row - column + k * rows
            allowed = (sq_ref[...] == sk_ref[k : k + 1, :]) & (distance >= 0) & (distance < WINDOW)
            for head in range(heads):
                at = pl.ds(head * HEAD, HEAD)
                queries, keys, values = q_ref[:, at], context_ref[k, 0, :, at], context_ref[k, 1, :, at]
                scores = dot(queries, keys, (1, 1)) * HEAD ** (-0.5)
                weight = jnp.where(allowed, jnp.exp(scores - lse_ref[:, head : head + 1]), 0.0)
                grad_weight = dot(do[:, at], values, (1, 1))
                grad_score = (
                    weight * (grad_weight - dot_sums[:, head : head + 1]) * HEAD ** (-0.5)
                ).astype(low)
                dq[:, at] += dot(grad_score, keys, (1, 0))
                dkv[k, 0, :, at] = dot(grad_score, queries, (0, 0))
                dkv[k, 1, :, at] = dot(weight.astype(low), do[:, at], (0, 0))

        exists = {0: None, 1: (y == 1) | (z >= 1), 2: z >= 1, 3: z >= 2 - y, 4: z >= 2}
        comes = {1: (y == 0) | (z >= 1), 3: z >= 1 + y}

        def kv_copy(which, k):
            if k in (1, 3):
                landing, target = land_y.at[k // 2, which], beside
                return remote(send_kv.at[k - 1, which], landing, y_s.at[k // 2, which], y_r.at[k // 2, which], target)
            landing = land_z.at[k // 2 - 1, which]
            return remote(
                send_kv.at[k - 1, which], landing, z_s.at[k // 2 - 1, which], z_r.at[k // 2 - 1, which], below
            )

        def kv_send(which, k):
            send_kv[k - 1, which] = dkv[k, which].astype(low)
            kv_copy(which, k).start()

        def merge(into, which, landed):
            add_to(dkv.at[into, which], dkv.at[into, which], landed, 32)

        for k in (3, 1, 4, 2, 0):
            def one(k=k):
                attention_block(k)
                if k in (1, 3):
                    kv_send(1, k)
                    kv_send(0, k)
            run_if(exists[k], one)

        def take_three(which):
            def land():
                kv_copy(which, 3).wait_recv()
                pl.when(y == 1)(lambda: merge(4, which, land_y.at[1, which]))
                pl.when(y == 0)(lambda: merge(2, which, land_y.at[1, which]))
            run_if(comes[3], land)
            run_if(exists[4], lambda: kv_send(which, 4))

        def take_one(which):
            def land():
                kv_copy(which, 1).wait_recv()
                pl.when(y == 1)(lambda: merge(2, which, land_y.at[0, which]))
                pl.when(y == 0)(lambda: merge(0, which, land_y.at[0, which]))
            run_if(comes[1], land)

        def take_four(which):
            def land():
                kv_copy(which, 4).wait_recv()
                merge(2, which, land_z.at[1, which])
            run_if((z >= 1) & (z < NZ - 1), land)
            run_if(exists[2], lambda: kv_send(which, 2))

        def take_two(which):
            def land():
                kv_copy(which, 2).wait_recv()
                merge(0, which, land_z.at[0, which])
            run_if(z < NZ - 1, land)

        def unturn(which, grad_of):
            inner = jnp.zeros((rows, 1), f32)
            for head in range(heads):
                at = pl.ds(head * HEAD, HEAD)
                grad = turn(grad_of(at), cos_ref[...], -sin_ref[...])
                value = raw_ref[which, :, at]
                line_sum[1 + which : 2 + which, at] = jnp.sum(
                    grad * (value * scale_ref[:, 1 + which : 2 + which]), axis=0, keepdims=True
                )
                grad = grad * gain_ref[2 + which : 3 + which, at]
                scaled[which, :, at] = grad
                inner = inner + jnp.sum(grad * value, axis=-1, keepdims=True)
            return inner

        def denorm(which, inner):
            scale = scale_ref[:, 1 + which : 2 + which]
            rest = scale * scale * scale * inner / width
            for head in range(heads):
                at = pl.ds(head * HEAD, HEAD)
                proj[which, :, at] = (
                    scale * scaled[which, :, at] - raw_ref[which, :, at] * rest
                ).astype(low)

        def send_beside(s):
            for zz in Z_ORDER:
                buffer = slot(3)(s, zz)
                buffer[...] = own_part(s, zz * NY + 1 - y).astype(buffer.dtype)
                line.to_y(s, zz)

        exchange_rows(unturn(QUERY, lambda at: dq[:, at]), part_q, land_q, qs_s, qs_r, mates)
        take_three(1)
        take_three(0)
        denorm(QUERY, exchanged_rows(part_q, land_q, qs_s, qs_r, mates))
        send_beside(QUERY)
        da_spread()
        take_one(1)
        take_one(0)
        take_four(1)
        take_four(0)
        take_two(1)
        proj[VALUE] = dkv[0, 1].astype(low)
        send_beside(VALUE)
        take_two(0)
        exchange_rows(unturn(KEY, lambda at: dkv[0, 0, :, at]), part_k, land_k, ks_s, ks_r, mates)
        denorm(KEY, exchanged_rows(part_k, land_k, ks_s, ks_r, mates))
        send_beside(KEY)
        fetch.wait()

        def half_of(cc):
            def body(i, carry):
                at = pl.ds(pl.multiple_of(cc * half + i * quarter, quarter), quarter)
                value = dot(proj[0], weights[0, at, :], (1, 1))
                for s in (1, 2):
                    value = value + dot(proj[s], weights[s, at, :], (1, 1))
                part[:, at] = value.astype(low)
                return carry

            lax.fori_loop(0, 2, body, 0)

        stages = group_stages(part, full, core_buf, x_buf, group_s, group_r)
        half_of(1 - c)
        stages[0]()
        half_of(c)
        stages[1]()

        def hop(s, zz, k):
            def upward():
                if k > 0:
                    line.take(s, zz, 1)
                line.copy(s, zz, 1).start()

            def downward():
                if k > 0:
                    line.take(s, zz, 2)
                line.copy(s, zz, 2).start()

            if k < zz:
                run_if((z < zz) & (z == k), upward)
            if NZ - 1 - k > zz:
                run_if((z > zz) & (NZ - 1 - z == k), downward)

        def receive(s, zz):
            line.copy(s, zz, 0).wait_recv()
            buffer = slot(0)(s, zz)
            buffer[...] = (buffer[...].astype(f32) + own_part(s, zz * NY + y)).astype(buffer.dtype)

        units = []

        def run_units(s):
            for zz in Z_ORDER:
                receive(s, zz)
                hop(s, zz, 0)
                units.append((s, zz))
                for k in (1, 2):
                    if len(units) > k:
                        hop(*units[-1 - k], k)

        def norm_one(i, carry):
            r = pl.ds(pl.multiple_of(i * 32, 32), 32)
            grad, value, scale = full[r, :].astype(f32), tok_ref[r, :].astype(f32), scale_ref[r, 0:1]
            line_sum[3:4, :] += jnp.sum(grad * (value * scale), axis=0, keepdims=True)
            grad = grad * gain_ref[0:1, :]
            inner = jnp.mean(grad * value, axis=-1, keepdims=True)
            tok_grad[r, :] = (
                dx1[r, :] + scale * grad - value * (scale * scale * scale) * inner
            ).astype(low)
            return carry

        run_units(QUERY)
        stages[2]()
        run_units(VALUE)
        da_end()
        stages[3]()
        stages[4]()
        lax.fori_loop(0, rows // 32, norm_one, 0)
        for b in range(GROUPS):
            at = pl.ds(b * depth, depth)
            small[b, 0:1, :] = line_sum[3:4, at]
            small[b, 1:2, :] = line_sum[0:1, at]
            for which in range(2):
                for k in range(columns // depth):
                    small[b, 2 + 2 * which + k : 3 + 2 * which + k, :] = line_sum[
                        1 + which : 2 + which, pl.ds(k * depth, depth)
                    ]
        send_beside(SMALL)
        run_units(KEY)
        run_units(SMALL)
        hop(*units[-1], 1)
        hop(*units[-2], 2)
        hop(*units[-1], 2)

        def done(s, total):
            target = qkv_sum.at[s] if s < OUT else small_sum
            target[...] = total[...].astype(f32)

        line.streams = [QUERY, VALUE, KEY, SMALL]
        line.home(done)
        line.finish()
        for which in range(2):
            for k in (1, 2, 3, 4):
                run_if(exists[k], lambda which=which, k=k: kv_copy(which, k).wait_send())
        drain_rows(part_k, land_k, ks_s, ks_r, mates)
        drain_rows(part_q, land_q, qs_s, qs_r, mates)

    shape, dma, vmem = jax.ShapeDtypeStruct, pltpu.SemaphoreType.DMA, pltpu.VMEM
    return pl.pallas_call(
        kernel,
        out_shape=(
            shape((rows, width), low),
            shape((3, depth, columns), f32),
            shape((columns, depth), f32),
            shape((small_rows, depth), f32),
        ),
        in_specs=[VMEM] * 21 + [HBM, VMEM],
        out_specs=(VMEM,) * 4,
        scratch_shapes=[
            vmem(qkv_low.shape, low),
            vmem((rows, width), f32),
            vmem((rows, width), low),
            vmem((rows, columns), low),
            vmem((rows, 128), f32),
            vmem((rows, columns), f32),
            vmem((blocks, 2, rows, columns), f32),
            vmem((2, rows, columns), f32),
            vmem((3, rows, columns), low),
            vmem((blocks - 1, 2, rows, columns), low),
            vmem((2, 2, rows, columns), low),
            vmem((2, 2, rows, columns), low),
            vmem((rows, width), low),
            vmem((rows, width), low),
            vmem((rows, half), low),
            vmem((rows, quarter), low),
            vmem((GROUPS, small_rows, depth), f32),
            vmem((8, width), f32),
            vmem((4, NZ, 3, depth, columns), low),
            vmem((GROUPS, rows, depth), low),
            vmem((4, NZ, small_rows, depth), f32),
            vmem((8, rows), f32),
            vmem((tensors - 1, 8, rows), f32),
            vmem((8, rows), f32),
            vmem((tensors - 1, 8, rows), f32),
            dma, dma((2, 2)), dma((2, 2)), dma((2, 2)), dma((2, 2)), dma((5,)), dma((5,)),
            dma((tensors - 1,)), dma((tensors - 1,)), dma((tensors - 1,)), dma((tensors - 1,)),
            dma((5, NZ, 3)), dma((5, NZ, 3)), dma((GROUPS - 1,)), dma((GROUPS - 1,)), dma((tensors - 1,)), dma((tensors - 1,)),
        ],
        compiler_params=comm_params(collective_id, 62),
        cost_estimate=cost(130),
        name="attend_back",
    )(
        grad_hidden, grad_probs, router_t, hidden_two, residual, scale_two, gains, out_grad,
        query, context, segment_query, segment_keys, attended, log_sums, raw, scales,
        cosine, sine, hidden_one, tokens, attended_all, qkv_low, out_low,
    )


def fast_shards(
    tokens_in,
    out_grad,
    w_qkv,
    w_attn_out,
    attn_gain,
    ffn_gain,
    qk_gain,
    w_router,
    w_gate,
    w_up,
    w_down,
    routes,
    segments,
):
    row_count, model_width = tokens_in.shape
    experts = w_router.shape[1]
    local_experts = w_gate.shape[0]
    heads_here = qk_gain.shape[1]
    local_width = heads_here * HEAD
    groups = lax.axis_size("expert")
    device_index = lax.axis_index("expert")
    tensor_index = lax.axis_index("tensor")
    quarter = model_width // lax.axis_size("tensor")
    hop_count = WINDOW // row_count
    score_scale = HEAD ** (-0.5)
    low = jnp.bfloat16

    chosen = jnp.any(
        routes[:, :, None] == jnp.arange(experts, dtype=jnp.int32)[None, None, :], axis=1
    ).astype(jnp.float32)
    qk_row = qk_gain.reshape(1, -1)

    def rounded(v):
        return lax.reduce_precision(v, 8, 7)

    smalls = jnp.concatenate(
        [
            rounded(attn_gain)[None, :],
            rounded(ffn_gain)[None, :],
            jnp.pad(rounded(qk_row), ((0, 0), (0, row_count - qk_row.shape[1]))),
            jnp.zeros((5, row_count), jnp.float32),
            w_router.T,
            chosen.T,
        ],
        axis=0,
    )
    global_rows = device_index * row_count + jnp.arange(row_count, dtype=jnp.int32)
    cosine_table, sine_table = angles(global_rows % SEQ, HEAD)
    wide_cosine = jnp.concatenate([cosine_table[:, 0], cosine_table[:, 0]], axis=1)
    wide_sine = jnp.concatenate([-sine_table[:, 0], sine_table[:, 0]], axis=1)
    (
        qkv_low, out_low, grad_out_all, hidden_one, raw, gate_up, down_low, gains, router_t, chosen_all,
        scales, query_low, context_blocks,
    ) = project(
        tokens_in, w_qkv, w_attn_out, out_grad, smalls, wide_cosine, wide_sine, w_gate, w_up, w_down,
        experts, 0,
    )
    segment_window = lax.dynamic_slice_in_dim(
        jnp.concatenate([jnp.full((WINDOW,), -1, jnp.int32), segments]),
        device_index * row_count, (hop_count + 1) * row_count,
    )
    segment_query = segment_window[WINDOW:]
    segment_keys = segment_window.reshape(hop_count + 1, row_count)[::-1]
    attended, log_sums, residual, hidden_two, scale_two_wide = attend(
        query_low, context_blocks, segment_query[:, None], segment_keys, tokens_in, out_low,
        gains, 2,
    )
    (
        block_out, grad_hidden_sum, grad_gate_sum, grad_gate_w, grad_up_w, grad_down, attended_all
    ) = expert_layer(
        hidden_two, grad_out_all, gate_up, down_low, router_t, chosen_all, residual, attended, 5
    )
    grad_probs = grad_gate_sum[:, :local_experts].reshape(experts, row_count).T * chosen
    grad_tokens, qkv_sum, out_sum, small_sum = attend_back(
        grad_hidden_sum, grad_probs, router_t, hidden_two, residual, scale_two_wide,
        gains, out_grad, query_low, context_blocks, segment_query[:, None], segment_keys,
        attended, log_sums, raw, scales, wide_cosine, wide_sine, hidden_one, tokens_in, attended_all,
        qkv_low, out_low, 8,
    )
    return (
        block_out,
        grad_tokens,
        qkv_sum,
        out_sum,
        small_sum[0],
        small_sum[1],
        lax.dynamic_slice_in_dim(
            small_sum[2:6].reshape(2, heads_here, HEAD),
            device_index * qk_gain.shape[2], qk_gain.shape[2], axis=2,
        ),
        small_sum[8 : 8 + experts].T,
        grad_gate_w,
        grad_up_w,
        grad_down,
    )


def solution(mesh):
    placed = (
        P("expert", None),
        P("expert", None),
        P(None, "expert", "tensor"),
        P("tensor", "expert"),
        P("expert"),
        P("expert"),
        P(None, "tensor", "expert"),
        P("expert", None),
        P("expert", None, "tensor"),
        P("expert", None, "tensor"),
        P("expert", "tensor", None),
        P("expert", None),
        P(),
    )
    compact = (mesh.shape["expert"], mesh.shape["tensor"]) == (GROUPS, NX * NC)
    return jax.shard_map(
        fast_shards if compact else shards,
        mesh=mesh,
        in_specs=placed,
        out_specs=(
            P("expert", None),
            P("expert", None),
            P(None, "expert", "tensor"),
            P("tensor", "expert"),
            P("expert"),
            P("expert"),
            P(None, "tensor", "expert"),
            P("expert", None),
            P("expert", None, "tensor"),
            P("expert", None, "tensor"),
            P("expert", "tensor", None),
        ),
        check_vma=False,
    )
```

```python
import jax
import jax.numpy as jnp
from jax import lax
from jax.experimental import pallas as pl
from jax.experimental.pallas import tpu as pltpu
from jax.sharding import PartitionSpec as P

HEAD = 128
WINDOW = 1024
SEQ = 2048


EPS = 1e-05
THETA = 10000.0


def from_behind(value, axis, steps):
    count = lax.axis_size(axis)
    initial, last = (max(0, -steps), min(count, count - steps))
    return lax.ppermute(value, axis, [(source, source + steps) for source in range(initial, last)])


def angles(position, head_size):
    half_size = head_size // 2
    frequency = THETA ** (-(jnp.arange(half_size, dtype=jnp.float32) * 2.0 / head_size))
    phase_angle = position.astype(jnp.float32)[:, None] * frequency[None, :]
    return (jnp.cos(phase_angle)[:, None, :], jnp.sin(phase_angle)[:, None, :])


def rotate(rotated_in, cosine_table, sine_table):
    half_size = rotated_in.shape[-1] // 2
    first_half = rotated_in[..., :half_size]
    second_half = rotated_in[..., half_size:]
    return jnp.concatenate(
        [
            first_half * cosine_table - second_half * sine_table,
            second_half * cosine_table + first_half * sine_table,
        ],
        axis=-1,
    )


def slot_layout(block_routes, experts, capacity):
    flat_routes = block_routes.reshape(-1)
    onehot = (flat_routes[:, None] == jnp.arange(experts, dtype=jnp.int32)[None, :]).astype(
        jnp.int32
    )
    before = jnp.cumsum(onehot, axis=0) - onehot
    rank_within = jnp.sum(before * onehot, axis=1)
    slot_index = flat_routes * capacity + rank_within
    slot_table = (
        jnp.zeros((experts * capacity,), jnp.int32)
        .at[slot_index]
        .set(jnp.arange(flat_routes.shape[0], dtype=jnp.int32) + 1)
    )
    return (slot_index, slot_table)


def shards(
    tokens_in,
    out_grad,
    w_qkv,
    w_attn_out,
    attn_gain,
    ffn_gain,
    qk_gain,
    w_router,
    w_gate,
    w_up,
    w_down,
    routes,
    segments,
):
    row_count, model_width = tokens_in.shape
    experts = w_router.shape[1]
    per_token = routes.shape[1]
    local_experts = w_gate.shape[0]
    heads_here = qk_gain.shape[1]
    local_width = heads_here * HEAD
    groups = lax.axis_size("expert")
    device = lax.axis_index("expert")
    capacity = row_count * per_token * 3 // (2 * experts)
    hop_count = WINDOW // row_count
    buffer_shape = (groups, local_experts, capacity, model_width)
    score_scale = HEAD ** (-0.5)

    def fetch_weights():
        return (
            lax.all_gather(w_qkv.astype(jnp.bfloat16), "expert", axis=1, tiled=True),
            lax.all_gather(w_attn_out.astype(jnp.bfloat16), "expert", axis=1, tiled=True),
            lax.all_gather(w_router.astype(jnp.bfloat16), "expert", axis=0, tiled=True),
            lax.all_gather(attn_gain.astype(jnp.bfloat16), "expert", axis=0, tiled=True),
            lax.all_gather(ffn_gain.astype(jnp.bfloat16), "expert", axis=0, tiled=True),
            lax.all_gather(qk_gain.astype(jnp.bfloat16), "expert", axis=2, tiled=True),
        )

    def prepare(pieces):
        return (
            pieces[0],
            pieces[1],
            pieces[2],
            pieces[3].astype(jnp.float32),
            pieces[4].astype(jnp.float32),
            pieces[5].astype(jnp.float32).reshape(2, local_width),
        )

    qkv_low, out_low, router_low, gain_one_f, gain_two_f, qk_gains = prepare(fetch_weights())
    tokens_f = tokens_in.astype(jnp.float32)
    scale_one = lax.rsqrt(jnp.mean(tokens_f * tokens_f, axis=-1, keepdims=True) + EPS)
    hidden_one = (tokens_f * scale_one * gain_one_f).astype(jnp.bfloat16)
    projected = jnp.einsum("td,jde->jte", hidden_one, qkv_low, preferred_element_type=jnp.float32)
    query_raw = projected[0]
    key_raw = projected[1]
    query_sq, key_sq = lax.psum(
        (jnp.sum(query_raw * query_raw, axis=-1), jnp.sum(key_raw * key_raw, axis=-1)), "tensor"
    )
    query_scale = lax.rsqrt(query_sq / model_width + EPS)[:, None]
    key_scale = lax.rsqrt(key_sq / model_width + EPS)[:, None]
    normed_query = query_raw * query_scale
    normed_key = key_raw * key_scale
    global_rows = device * row_count + jnp.arange(row_count, dtype=jnp.int32)
    cosine_table, sine_table = angles(global_rows % SEQ, HEAD)
    query_low = rotate(
        (normed_query * qk_gains[0]).reshape(row_count, heads_here, HEAD), cosine_table, sine_table
    ).astype(jnp.bfloat16)
    key_low = rotate(
        (normed_key * qk_gains[1]).reshape(row_count, heads_here, HEAD), cosine_table, sine_table
    ).astype(jnp.bfloat16)
    value_low = projected[2].astype(jnp.bfloat16).reshape(row_count, heads_here, HEAD)
    own_pair = jnp.stack([key_low, value_low])
    earlier = []
    for steps_back in range(hop_count, 0, -1):
        earlier.append(from_behind(own_pair, "expert", steps_back))
    context = jnp.concatenate(earlier + [own_pair], axis=1)
    key_rows = (device - hop_count) * row_count + jnp.arange(
        (hop_count + 1) * row_count, dtype=jnp.int32
    )
    segment_keys = segments[jnp.maximum(key_rows, 0)]
    segment_query = segments[global_rows]
    distance = global_rows[:, None] - key_rows[None, :]
    allowed = (
        (key_rows[None, :] >= 0)
        & (segment_query[:, None] == segment_keys[None, :])
        & (distance >= 0)
        & (distance < WINDOW)
    )

    def score_block():
        raw_scores = (
            jnp.einsum("qhd,khd->hqk", query_low, context[0], preferred_element_type=jnp.float32)
            * score_scale
        )
        return jnp.where(allowed[None], raw_scores, -1e30)

    scores = score_block()
    largest = jnp.max(scores, axis=-1, keepdims=True)
    exp_scores = jnp.exp(scores - largest)
    exp_total = jnp.sum(exp_scores, axis=-1, keepdims=True)
    log_total = largest + jnp.log(exp_total)
    attn_probs = (exp_scores / exp_total).astype(jnp.bfloat16)
    attended = (
        jnp.einsum("hqk,khd->qhd", attn_probs, context[1], preferred_element_type=jnp.float32)
        .reshape(row_count, local_width)
        .astype(jnp.bfloat16)
    )
    attention_out = lax.psum(
        jnp.dot(attended, out_low, preferred_element_type=jnp.float32).astype(jnp.bfloat16),
        "tensor",
    ).astype(jnp.float32)
    residual = tokens_f + attention_out
    scale_two = lax.rsqrt(jnp.mean(residual * residual, axis=-1, keepdims=True) + EPS)
    normed_two = residual * scale_two
    hidden_two = (normed_two * gain_two_f).astype(jnp.bfloat16)
    logits = jnp.dot(hidden_two, router_low, preferred_element_type=jnp.float32)
    logit_exp = jnp.exp(logits - jnp.max(logits, axis=-1, keepdims=True))
    router_probs = logit_exp / jnp.sum(logit_exp, axis=-1, keepdims=True)
    chosen = routes[:, :, None] == jnp.arange(experts, dtype=jnp.int32)[None, None, :]
    gate_probs = jnp.sum(jnp.where(chosen, router_probs[:, None, :], 0.0), axis=-1)
    slot_index, slot_table = slot_layout(routes, experts, capacity)
    present = (slot_table > 0)[:, None]
    assigned = jnp.maximum(slot_table - 1, 0)
    row_of_slot = assigned // per_token
    gate_low = w_gate.astype(jnp.bfloat16)
    up_low = w_up.astype(jnp.bfloat16)
    down_low = w_down.astype(jnp.bfloat16)

    def send_rows():
        buffer_rows = jnp.where(
            present, hidden_two[row_of_slot], jnp.zeros((), jnp.bfloat16)
        ).reshape(buffer_shape)
        return lax.all_to_all(buffer_rows, "expert", split_axis=0, concat_axis=0, tiled=True)

    def expert_front(arrived):
        gate_pre = jnp.einsum(
            "secd,edh->sech", arrived, gate_low, preferred_element_type=jnp.float32
        )
        up_pre = jnp.einsum("secd,edh->sech", arrived, up_low, preferred_element_type=jnp.float32)
        return (gate_pre, up_pre)

    received = send_rows()
    gate_pre, up_pre = expert_front(received)
    activated = (gate_pre * jax.nn.sigmoid(gate_pre) * up_pre).astype(jnp.bfloat16)
    partial_value = jnp.einsum(
        "sech,ehd->secd", activated, down_low, preferred_element_type=jnp.float32
    ).astype(jnp.bfloat16)
    returned = lax.all_to_all(
        partial_value, "expert", split_axis=0, concat_axis=0, tiled=True
    ).reshape(experts * capacity, model_width)
    expert_rows = returned[slot_index].reshape(row_count, per_token, model_width)
    expert_part = jnp.einsum(
        "tk,tkd->td", gate_probs, expert_rows, preferred_element_type=jnp.float32
    )
    block_out = residual + lax.psum(expert_part.astype(jnp.bfloat16), "tensor").astype(jnp.float32)
    qkv_low, out_low, router_low, gain_one_f, gain_two_f, qk_gains = prepare(fetch_weights())
    grad_out = out_grad.astype(jnp.float32)
    grad_gate_part = jnp.einsum(
        "td,tkd->tk", grad_out, expert_rows, preferred_element_type=jnp.float32
    )
    slot_grads = (
        (gate_probs[:, :, None] * grad_out[:, None, :])
        .astype(jnp.bfloat16)
        .reshape(row_count * per_token, model_width)
    )
    grad_buffer = jnp.where(present, slot_grads[assigned], jnp.zeros((), jnp.bfloat16)).reshape(
        buffer_shape
    )
    grad_received = lax.all_to_all(grad_buffer, "expert", split_axis=0, concat_axis=0, tiled=True)
    received = send_rows()
    gate_pre, up_pre = expert_front(received)
    sigmoid_gate = jax.nn.sigmoid(gate_pre)
    swish_gate = gate_pre * sigmoid_gate
    activated = (swish_gate * up_pre).astype(jnp.bfloat16)
    grad_act = jnp.einsum(
        "secd,ehd->sech", grad_received, down_low, preferred_element_type=jnp.float32
    )
    grad_down = jnp.einsum(
        "sech,secd->ehd", activated, grad_received, preferred_element_type=jnp.float32
    )
    grad_gate_pre = (
        grad_act * up_pre * sigmoid_gate * (1.0 + gate_pre * (1.0 - sigmoid_gate))
    ).astype(jnp.bfloat16)
    grad_up_pre = (grad_act * swish_gate).astype(jnp.bfloat16)
    grad_gate_w = jnp.einsum(
        "secd,sech->edh", received, grad_gate_pre, preferred_element_type=jnp.float32
    )
    grad_up_w = jnp.einsum(
        "secd,sech->edh", received, grad_up_pre, preferred_element_type=jnp.float32
    )
    grad_rows = (
        jnp.einsum("sech,edh->secd", grad_gate_pre, gate_low, preferred_element_type=jnp.float32)
        + jnp.einsum("sech,edh->secd", grad_up_pre, up_low, preferred_element_type=jnp.float32)
    ).astype(jnp.bfloat16)
    grad_back = lax.all_to_all(
        grad_rows, "expert", split_axis=0, concat_axis=0, tiled=True
    ).reshape(experts * capacity, model_width)
    grad_hidden_part = jnp.sum(
        grad_back[slot_index].reshape(row_count, per_token, model_width), axis=1, dtype=jnp.float32
    )
    grad_hidden_sum, grad_gates = (
        lax.psum(grad_hidden_part.astype(jnp.bfloat16), "tensor").astype(jnp.float32),
        lax.psum(grad_gate_part.astype(jnp.bfloat16), "tensor").astype(jnp.float32),
    )
    grad_probs = jnp.sum(jnp.where(chosen, grad_gates[:, :, None], 0.0), axis=1)
    grad_logits = (
        router_probs * (grad_probs - jnp.sum(router_probs * grad_probs, axis=-1, keepdims=True))
    ).astype(jnp.bfloat16)
    grad_hidden_two = grad_hidden_sum + jnp.dot(
        grad_logits, router_low.T, preferred_element_type=jnp.float32
    )
    grad_router = jnp.dot(hidden_two.T, grad_logits, preferred_element_type=jnp.float32)
    grad_gain_two = jnp.sum(grad_hidden_two * normed_two, axis=0)
    scaled_two = grad_hidden_two * gain_two_f
    grad_residual = (
        grad_out
        + scale_two * scaled_two
        - residual
        * (scale_two * scale_two * scale_two)
        * jnp.mean(scaled_two * residual, axis=-1, keepdims=True)
    )
    grad_attn = grad_residual.astype(jnp.bfloat16)
    grad_out_w = jnp.dot(attended.T, grad_attn, preferred_element_type=jnp.float32)
    grad_attended = (
        jnp.dot(grad_attn, out_low.T, preferred_element_type=jnp.float32)
        .astype(jnp.bfloat16)
        .reshape(row_count, heads_here, HEAD)
    )
    attn_weights = jnp.where(allowed[None], jnp.exp(score_block() - log_total), 0.0)
    grad_weights = jnp.einsum(
        "qhd,khd->hqk", grad_attended, context[1], preferred_element_type=jnp.float32
    )
    inner_sum = jnp.sum(attn_weights * grad_weights, axis=-1, keepdims=True)
    grad_scores = (attn_weights * (grad_weights - inner_sum) * score_scale).astype(jnp.bfloat16)
    grad_query = jnp.einsum(
        "hqk,khd->qhd", grad_scores, context[0], preferred_element_type=jnp.float32
    )
    grad_keys = jnp.einsum(
        "hqk,qhd->khd", grad_scores, query_low, preferred_element_type=jnp.float32
    )
    grad_values = jnp.einsum(
        "hqk,qhd->khd",
        attn_weights.astype(jnp.bfloat16),
        grad_attended,
        preferred_element_type=jnp.float32,
    )
    grad_pair = jnp.stack([grad_keys, grad_values]).reshape(
        2, hop_count + 1, row_count, heads_here, HEAD
    )
    own_grad = grad_pair[:, hop_count]
    for steps_back in range(1, hop_count + 1):
        own_grad = own_grad + from_behind(
            grad_pair[:, hop_count - steps_back].astype(jnp.bfloat16), "expert", -steps_back
        ).astype(jnp.float32)
    grad_query_norm = rotate(grad_query, cosine_table, -sine_table).reshape(row_count, local_width)
    grad_key_norm = rotate(own_grad[0], cosine_table, -sine_table).reshape(row_count, local_width)
    grad_gain_query = jnp.sum(grad_query_norm * normed_query, axis=0)
    grad_gain_key = jnp.sum(grad_key_norm * normed_key, axis=0)
    scaled_query = grad_query_norm * qk_gains[0]
    scaled_key = grad_key_norm * qk_gains[1]
    query_inner, key_inner = lax.psum(
        (jnp.sum(scaled_query * query_raw, axis=-1), jnp.sum(scaled_key * key_raw, axis=-1)),
        "tensor",
    )
    grad_query_raw = (
        query_scale * scaled_query
        - query_raw * (query_scale * query_scale * query_scale) * query_inner[:, None] / model_width
    ).astype(jnp.bfloat16)
    grad_key_raw = (
        key_scale * scaled_key
        - key_raw * (key_scale * key_scale * key_scale) * key_inner[:, None] / model_width
    ).astype(jnp.bfloat16)
    grad_value_raw = own_grad[1].reshape(row_count, local_width).astype(jnp.bfloat16)
    grad_proj = jnp.stack([grad_query_raw, grad_key_raw, grad_value_raw])
    grad_qkv = jnp.einsum("td,jte->jde", hidden_one, grad_proj, preferred_element_type=jnp.float32)
    grad_hidden_one = lax.psum(
        jnp.einsum("jte,jde->td", grad_proj, qkv_low, preferred_element_type=jnp.float32).astype(
            jnp.bfloat16
        ),
        "tensor",
    ).astype(jnp.float32)
    grad_gain_one = jnp.sum(grad_hidden_one * tokens_f * scale_one, axis=0)
    scaled_one = grad_hidden_one * gain_one_f
    grad_tokens = (
        grad_residual
        + scale_one * scaled_one
        - tokens_f
        * (scale_one * scale_one * scale_one)
        * jnp.mean(scaled_one * tokens_f, axis=-1, keepdims=True)
    )
    grad_qk = jnp.stack([grad_gain_query, grad_gain_key]).reshape(2, heads_here, HEAD)
    reduced = (
        lax.psum_scatter(
            grad_qkv.astype(jnp.bfloat16), "expert", scatter_dimension=1, tiled=True
        ).astype(jnp.float32),
        lax.psum_scatter(
            grad_out_w.astype(jnp.bfloat16), "expert", scatter_dimension=1, tiled=True
        ).astype(jnp.float32),
        lax.psum_scatter(
            grad_router.astype(jnp.bfloat16), "expert", scatter_dimension=0, tiled=True
        ).astype(jnp.float32),
        lax.psum_scatter(
            grad_gain_one.astype(jnp.bfloat16), "expert", scatter_dimension=0, tiled=True
        ).astype(jnp.float32),
        lax.psum_scatter(
            grad_gain_two.astype(jnp.bfloat16), "expert", scatter_dimension=0, tiled=True
        ).astype(jnp.float32),
        lax.psum_scatter(
            grad_qk.astype(jnp.bfloat16), "expert", scatter_dimension=2, tiled=True
        ).astype(jnp.float32),
    )
    return (
        block_out.astype(jnp.bfloat16),
        grad_tokens.astype(jnp.bfloat16),
        reduced[0],
        reduced[1],
        reduced[3],
        reduced[4],
        reduced[5],
        reduced[2],
        grad_gate_w,
        grad_up_w,
        grad_down,
    )


MESH_ID = pl.DeviceIdType.MESH
HBM = pl.BlockSpec(memory_space=pltpu.HBM)
VMEM = pl.BlockSpec(memory_space=pltpu.VMEM)
NZ, NY, NX, NC = 4, 2, 2, 2
GROUPS = NZ * NY


def place():
    e = lax.axis_index("expert")
    t = lax.axis_index("tensor")
    return lax.div(e, NY), lax.rem(e, NY), lax.div(t, NC), lax.rem(t, NC)


def device(z, y, x, c):
    return (z * NY + y, x * NC + c)


def run_if(condition, body):
    if condition is None:
        body()
    else:
        pl.when(condition)(body)


def greet(partners):
    barrier = pltpu.get_barrier_semaphore()
    for target, condition in partners:
        run_if(
            condition,
            lambda target=target: pl.semaphore_signal(
                barrier, inc=1, device_id=target, device_id_type=MESH_ID
            ),
        )
    count = sum(1 for _, condition in partners if condition is None)
    for _, condition in partners:
        if condition is not None:
            count = count + condition.astype(jnp.int32)
    pl.semaphore_wait(barrier, count)


def remote(source, target_ref, send_sem, recv_sem, target):
    return pltpu.make_async_remote_copy(
        src_ref=source,
        dst_ref=target_ref,
        send_sem=send_sem,
        recv_sem=recv_sem,
        device_id=target,
        device_id_type=MESH_ID,
    )


def block_rows(block, rows):
    return pl.ds(pl.multiple_of(block * rows, rows), rows)


class LineGather:
    def __init__(self, streams, sources, views, send_sem, recv_sem, y_first=()):
        self.z, self.y, self.x, self.c = place()
        self.streams, self.sources, self.views = streams, sources, views
        self.send_sem, self.recv_sem = send_sem, recv_sem
        self.y_first = y_first
        self.has_up, self.has_down = self.z < NZ - 1, self.z > 0
        self.pending = []

    def partners(self):
        z, y, x, c = self.z, self.y, self.x, self.c
        return [
            (device(z + 1, y, x, c), z < NZ - 1),
            (device(z - 1, y, x, c), z > 0),
            (device(z, 1 - y, x, c), None),
        ]

    def exists(self, rel):
        rel = rel % 7
        if rel == 0:
            return None
        return self.z >= rel if rel < 4 else self.z + (rel - 3) < NZ

    def block(self, rel):
        y = self.y if rel < 7 else 1 - self.y
        rel = rel % 7
        z = self.z if rel == 0 else (self.z - rel if rel < 4 else self.z + (rel - 3))
        return z * NY + y

    def send(self, stream, rel, way):
        z, y, x, c = self.z, self.y, self.x, self.c
        block = self.block(rel)
        there = self.views[stream](block)
        source = self.sources[stream] if rel == 0 else there
        near = rel % 7 == 0
        if way == 0:
            target, landing = device(z + 1, y, x, c), rel + 1
        elif way == 1:
            target, landing = device(z - 1, y, x, c), rel + (4 if near else 1)
        else:
            target, landing = device(z, 1 - y, x, c), 7 + rel
        return remote(
            source,
            there,
            self.send_sem.at[stream, rel, way],
            self.recv_sem.at[stream, landing],
            target,
        )

    def forwards(self, stream, rel):
        return rel < 7 or stream in self.y_first

    def start(self, stream, rel):
        if rel % 7 < 4:
            run = self.has_up
            run_if(run, lambda: self.send(stream, rel, 0).start())
            self.pending.append((stream, rel, 0, run))
        if rel % 7 == 0 or rel % 7 >= 4:
            run = self.has_down
            run_if(run, lambda: self.send(stream, rel, 1).start())
            self.pending.append((stream, rel, 1, run))
        if rel == 0 or stream not in self.y_first:
            self.send(stream, rel, 2).start()
            self.pending.append((stream, rel, 2, None))

    def arrive(self, stream, rel):
        there = self.views[stream](self.block(rel))
        remote(
            there,
            there,
            self.send_sem.at[stream, 0, 0],
            self.recv_sem.at[stream, rel],
            device(self.z, 1 - self.y, self.x, self.c),
        ).wait_recv()

    def order(self):
        return [7, 1, 4, 8, 11, 2, 5, 9, 12, 3, 6, 10, 13]

    def run(self, hook=None):
        for stream in self.streams:
            self.start(stream, 0)
        for rel in self.order():
            def step(rel=rel):
                marks = len(self.pending)
                for stream in self.streams:
                    self.arrive(stream, rel)
                    if rel < 7:
                        self.start(stream, rel)
                    if hook is not None:
                        hook(stream, rel)
                if rel < 7:
                    late = self.pending[marks:]
                    del self.pending[marks:]
                    self.finish_later(late, rel)
            run_if(self.exists(rel), step)

    def finish_later(self, late, rel):
        self.late = getattr(self, "late", []) + [(rel, late)]

    def finish(self):
        for stream, rel, way, run in self.pending:
            run_if(run, lambda s=stream, r=rel, w=way: self.send(s, r, w).wait_send())
        for rel, late in getattr(self, "late", []):
            def body(late=late):
                for stream, rel, way, run in late:
                    run_if(run, lambda s=stream, r=rel, w=way: self.send(s, r, w).wait_send())
            run_if(self.exists(rel), body)


def cost(microseconds):
    return pl.CostEstimate(flops=0, bytes_accessed=int(microseconds * 3.0e6), transcendentals=0)


def comm_params(collective_id, megabytes=56):
    return pltpu.CompilerParams(
        collective_id=collective_id,
        has_side_effects=True,
        vmem_limit_bytes=megabytes * 1024 * 1024,
    )


def weight_gather(qkv_low, out_low, smalls, collective_id):
    parts, rows, width = qkv_low.shape
    depth, columns = out_low.shape

    def kernel(qkv, out, small, qkv_all, out_all, small_all, send_sem, recv_sem, local_sem):
        views = [
            lambda b: qkv_all.at[:, block_rows(b, rows), :],
            lambda b: out_all.at[:, block_rows(b, columns)],
            lambda b: small_all.at[b],
        ]
        line = LineGather([2, 0, 1], [qkv, out, small], views, send_sem, recv_sem)
        greet(line.partners())
        own = line.block(0)
        keep = [
            pltpu.make_async_copy(source, view(own), local_sem.at[i])
            for i, (source, view) in enumerate(zip([qkv, out, small], views))
        ]
        for copy in keep:
            copy.start()
        line.run()
        line.finish()
        for copy in keep:
            copy.wait()

    return pl.pallas_call(
        kernel,
        out_shape=(
            jax.ShapeDtypeStruct((parts, rows * GROUPS, width), jnp.bfloat16),
            jax.ShapeDtypeStruct((depth, columns * GROUPS), jnp.bfloat16),
            jax.ShapeDtypeStruct((GROUPS,) + smalls.shape, jnp.float32),
        ),
        in_specs=[HBM] * 3,
        out_specs=(HBM, HBM, HBM),
        scratch_shapes=[
            pltpu.SemaphoreType.DMA((3, 14, 3)),
            pltpu.SemaphoreType.DMA((3, 14)),
            pltpu.SemaphoreType.DMA((3,)),
        ],
        compiler_params=comm_params(collective_id),
        cost_estimate=cost(100),
        name="weight_gather",
    )(qkv_low, out_low, smalls)


def token_gather(block, collective_id):
    rows, width = block.shape
    a_cols, c_cols = width * 3 // 16, width // 8

    def kernel(own_ref, all_ref, send_sem, recv_sem, x_send, x_recv, core_send, core_recv, local_sem):
        z, y, x, c = place()

        def a_at(xx, cc):
            return pl.ds(pl.multiple_of(xx * (2 * a_cols) + cc * a_cols, 128), a_cols)

        def c_at(cc):
            return pl.ds(pl.multiple_of(4 * a_cols + cc * c_cols, 128), c_cols)

        def view(b, columns):
            return all_ref.at[block_rows(b, rows), columns]

        sources = [own_ref.at[:, a_at(x, c)], own_ref.at[:, c_at(c)]]
        views = [lambda b: view(b, a_at(x, c)), lambda b: view(b, c_at(c))]
        line = LineGather([0, 1], sources, views, send_sem, recv_sem)
        across, twin = device(z, y, 1 - x, c), device(z, y, x, 1 - c)
        greet(line.partners() + [(across, None), (twin, None)])
        keep = pltpu.make_async_copy(own_ref, all_ref.at[block_rows(line.block(0), rows), :], local_sem)
        keep.start()

        def to_twin(rel, stream, landing=False):
            b = line.block(rel)
            columns = [a_at(x, c), c_at(c), a_at(1 - x, c)][stream]
            other = [a_at(x, 1 - c), c_at(1 - c), a_at(1 - x, 1 - c)][stream]
            piece = view(b, other if landing else columns)
            return remote(piece, piece, core_send.at[rel, stream], core_recv.at[rel, stream], twin)

        def to_across(rel, landing=False):
            b = line.block(rel)
            piece = view(b, a_at(1 - x if landing else x, c))
            return remote(piece, piece, x_send.at[rel], x_recv.at[rel], across)

        def hook(stream, rel):
            if stream == 0:
                to_across(rel).start()
            to_twin(rel, stream).start()

        line.run(hook)
        for rel in line.order():
            def relay(rel=rel):
                to_across(rel, True).wait_recv()
                to_twin(rel, 2).start()
            run_if(line.exists(rel), relay)
        for rel in line.order():
            def end(rel=rel):
                to_across(rel).wait_send()
                for stream in range(3):
                    to_twin(rel, stream, True).wait_recv()
                    to_twin(rel, stream).wait_send()
            run_if(line.exists(rel), end)
        line.finish()
        keep.wait()

    return pl.pallas_call(
        kernel,
        out_shape=jax.ShapeDtypeStruct((rows * GROUPS, width), block.dtype),
        in_specs=[HBM],
        out_specs=HBM,
        scratch_shapes=[
            pltpu.SemaphoreType.DMA((2, 14, 3)),
            pltpu.SemaphoreType.DMA((2, 14)),
            pltpu.SemaphoreType.DMA((14,)),
            pltpu.SemaphoreType.DMA((14,)),
            pltpu.SemaphoreType.DMA((14, 3)),
            pltpu.SemaphoreType.DMA((14, 3)),
            pltpu.SemaphoreType.DMA,
        ],
        compiler_params=comm_params(collective_id),
        cost_estimate=cost(45),
        name="token_gather",
    )(block)


def add_into(rows, step, store):
    def body(i, carry):
        store(pl.ds(pl.multiple_of(i * step, step), step))
        return carry

    lax.fori_loop(0, rows // step, body, 0)


def group_stages(part_ref, out_ref, core_buf, x_buf, send_sem, recv_sem):
    rows, width = part_ref.shape
    half, quarter = width // 2, width // 4
    z, y, x, c = place()
    across, twin = device(z, y, 1 - x, c), device(z, y, x, 1 - c)

    def half_of(cc):
        return pl.ds(pl.multiple_of(cc * half, half), half)

    def quarter_of(xx, cc):
        return pl.ds(pl.multiple_of(cc * half + xx * quarter, quarter), quarter)

    own, from_x = out_ref.at[:, quarter_of(x, c)], out_ref.at[:, quarter_of(1 - x, c)]
    to_x = core_buf.at[:, pl.ds(pl.multiple_of((1 - x) * quarter, quarter), quarter)]
    sources = [part_ref.at[:, half_of(1 - c)], to_x, own, own, from_x]
    landings = [core_buf, x_buf, own, own, from_x]
    targets = [twin, across, across, twin, twin]

    def copy(k):
        return remote(sources[k], landings[k], send_sem.at[k], recv_sem.at[k], targets[k])

    def arrive(k, landing):
        remote(landing, landing, send_sem.at[k], recv_sem.at[k], targets[k]).wait_recv()

    def begin():
        copy(0).start()

    def core_step():
        copy(0).wait_recv()
        add_to(core_buf, core_buf, part_ref.at[:, half_of(c)], 32)
        copy(1).start()

    def x_step():
        copy(1).wait_recv()
        add_to(own, x_buf, core_buf.at[:, pl.ds(pl.multiple_of(x * quarter, quarter), quarter)], 32)
        copy(2).start()
        copy(3).start()

    def spread():
        arrive(2, from_x)
        copy(4).start()

    def end():
        arrive(3, out_ref.at[:, quarter_of(x, 1 - c)])
        arrive(4, out_ref.at[:, quarter_of(1 - x, 1 - c)])
        for k in range(5):
            copy(k).wait_send()

    return [begin, core_step, x_step, spread, end]


def group_sum(part_ref, out_ref, core_buf, x_buf, send_sem, recv_sem, meanwhile=None):
    stages = group_stages(part_ref, out_ref, core_buf, x_buf, send_sem, recv_sem)
    stages[0]()
    if meanwhile is not None:
        meanwhile()
    for stage in stages[1:]:
        stage()


def tensor_sum(part, collective_id):
    rows, width = part.shape

    def kernel(part_ref, out_ref, core_buf, x_buf, send_sem, recv_sem):
        z, y, x, c = place()
        greet([(device(z, y, 1 - x, c), None), (device(z, y, x, 1 - c), None)])
        group_sum(part_ref, out_ref, core_buf, x_buf, send_sem, recv_sem)

    return pl.pallas_call(
        kernel,
        out_shape=jax.ShapeDtypeStruct((rows, width), jnp.bfloat16),
        in_specs=[VMEM],
        out_specs=VMEM,
        scratch_shapes=[
            pltpu.VMEM((rows, width // 2), jnp.bfloat16),
            pltpu.VMEM((rows, width // 4), jnp.bfloat16),
            pltpu.SemaphoreType.DMA((5,)),
            pltpu.SemaphoreType.DMA((5,)),
        ],
        compiler_params=comm_params(collective_id, 16),
        cost_estimate=cost(17),
        name="tensor_sum",
    )(part)


Z_ORDER = (3, 0, 2, 1)


def accumulate(into, addend, step=64):
    rows = into.shape[0]
    step = min(step, rows)

    def body(i, carry):
        r = pl.ds(pl.multiple_of(i * step, step), step)
        total = into[r, :].astype(jnp.float32) + addend[r, :].astype(jnp.float32)
        into[r, :] = total.astype(into.dtype)
        return carry

    lax.fori_loop(0, rows // step, body, 0)


class LineReduce:
    def __init__(self, streams, own, y_buf, lo_buf, hi_buf, send_sem, recv_sem):
        self.z, self.y, self.x, self.c = place()
        self.streams = streams
        self.own, self.y_buf, self.lo_buf, self.hi_buf = own, y_buf, lo_buf, hi_buf
        self.send_sem, self.recv_sem = send_sem, recv_sem

    def partners(self):
        z, y, x, c = self.z, self.y, self.x, self.c
        return [
            (device(z + 1, y, x, c), z < NZ - 1),
            (device(z - 1, y, x, c), z > 0),
            (device(z, 1 - y, x, c), None),
        ]

    def copy(self, s, zz, way):
        z, y, x, c = self.z, self.y, self.x, self.c
        if way == 0:
            source, landing, target = self.own(s, zz, 1 - y), self.y_buf, device(z, 1 - y, x, c)
        elif way == 1:
            source, landing, target = self.y_buf(s, zz), self.lo_buf, device(z + 1, y, x, c)
        else:
            source, landing, target = self.y_buf(s, zz), self.hi_buf, device(z - 1, y, x, c)
        return remote(
            source, landing(s, zz), self.send_sem.at[s, zz, way], self.recv_sem.at[s, zz, way], target
        )

    def to_y(self, s, zz):
        self.copy(s, zz, 0).start()

    def take(self, s, zz, way):
        self.copy(s, zz, way).wait_recv()
        accumulate(self.y_buf(s, zz), (self.lo_buf if way == 1 else self.hi_buf)(s, zz))

    def along_z(self, s, zz):
        z = self.z
        self.copy(s, zz, 0).wait_recv()
        accumulate(self.y_buf(s, zz), self.own(s, zz, self.y))

        def upward():
            run_if(z > 0, lambda: self.take(s, zz, 1))
            self.copy(s, zz, 1).start()

        def downward():
            run_if(z < NZ - 1, lambda: self.take(s, zz, 2))
            self.copy(s, zz, 2).start()

        run_if(z < zz, upward)
        run_if(z > zz, downward)

    def home(self, done):
        for zz in range(NZ):
            def land(zz=zz):
                for s in self.streams:
                    if zz > 0:
                        self.take(s, zz, 1)
                    if zz < NZ - 1:
                        self.take(s, zz, 2)
                    done(s, self.y_buf(s, zz))
            run_if(self.z == zz, land)

    def finish(self):
        for zz in range(NZ):
            for s in self.streams:
                self.copy(s, zz, 0).wait_send()
                run_if(self.z < zz, lambda s=s, zz=zz: self.copy(s, zz, 1).wait_send())
                run_if(self.z > zz, lambda s=s, zz=zz: self.copy(s, zz, 2).wait_send())


def weight_reduce(qkv, out, smalls, collective_id):
    parts, depth, width = qkv.shape
    rows = depth // GROUPS
    out_rows, columns = out.shape[0], out.shape[1] // GROUPS

    def kernel(qkv_ref, out_ref, small_ref, qkv_sum, out_sum, small_sum,
               qkv_buf, out_buf, small_buf, send_sem, recv_sem):
        def own(s, zz, yy):
            b = zz * NY + yy
            if s < parts:
                return qkv_ref.at[s, block_rows(b, rows), :]
            if s == parts:
                return out_ref.at[:, block_rows(b, columns)]
            return small_ref.at[b]

        def slot(kind):
            def view(s, zz):
                if s < parts:
                    return qkv_buf.at[kind, zz, s]
                if s == parts:
                    return out_buf.at[kind, zz]
                return small_buf.at[kind, zz]
            return view

        streams = list(range(parts + 2))
        line = LineReduce(streams, own, slot(0), slot(1), slot(2), send_sem, recv_sem)
        greet(line.partners())
        work = [(s, zz) for s in [parts + 1, parts] + list(range(parts)) for zz in Z_ORDER]
        for s, zz in work:
            line.to_y(s, zz)
        for s, zz in work:
            line.along_z(s, zz)

        def done(s, total):
            target = qkv_sum.at[s] if s < parts else (out_sum if s == parts else small_sum)
            step = min(64, target.shape[0])

            def body(i, carry):
                r = pl.ds(pl.multiple_of(i * step, step), step)
                target[r, :] = total[r, :].astype(jnp.float32)
                return carry

            lax.fori_loop(0, target.shape[0] // step, body, 0)

        line.home(done)
        line.finish()

    return pl.pallas_call(
        kernel,
        out_shape=(
            jax.ShapeDtypeStruct((parts, rows, width), jnp.float32),
            jax.ShapeDtypeStruct((out_rows, columns), jnp.float32),
            jax.ShapeDtypeStruct(smalls.shape[1:], jnp.float32),
        ),
        in_specs=[VMEM] * 3,
        out_specs=(VMEM,) * 3,
        scratch_shapes=[
            pltpu.VMEM((3, NZ, parts, rows, width), jnp.bfloat16),
            pltpu.VMEM((3, NZ, out_rows, columns), jnp.bfloat16),
            pltpu.VMEM((3, NZ) + smalls.shape[1:], jnp.float32),
            pltpu.SemaphoreType.DMA((parts + 2, NZ, 3)),
            pltpu.SemaphoreType.DMA((parts + 2, NZ, 3)),
        ],
        compiler_params=comm_params(collective_id),
        cost_estimate=cost(120),
        name="weight_reduce",
    )(qkv, out, smalls)


def token_reduce(part, collective_id, pairs=None):
    tokens, width = part.shape
    rows = tokens // GROUPS
    half, quarter = width // 2, width // 4

    def kernel(part_ref, out_ref, core_buf, x_buf, y_buf, lo_buf, hi_buf,
               core_send, core_recv, x_send, x_recv, send_sem, recv_sem):
        z, y, x, c = place()
        across, twin = device(z, y, 1 - x, c), device(z, y, x, 1 - c)

        line = LineReduce(
            [0], lambda s, zz, yy: x_buf.at[zz * NY + yy], lambda s, zz: y_buf.at[zz],
            lambda s, zz: lo_buf.at[zz], lambda s, zz: hi_buf.at[zz], send_sem, recv_sem,
        )
        greet(line.partners() + [(across, None), (twin, None)])
        order = [(zz, flip) for zz in Z_ORDER for flip in (1, 0)]

        def number(zz, flip):
            return zz * NY + (1 - y if flip else y)

        def to_twin(zz, flip):
            b = number(zz, flip)
            return remote(
                part_ref.at[block_rows(b, rows), pl.ds(pl.multiple_of((1 - c) * half, half), half)],
                core_buf.at[b], core_send.at[zz, flip], core_recv.at[zz, flip], twin,
            )

        def to_across(zz, flip):
            b = number(zz, flip)
            return remote(
                core_buf.at[b, :, pl.ds(pl.multiple_of((1 - x) * quarter, quarter), quarter)],
                x_buf.at[b], x_send.at[zz, flip], x_recv.at[zz, flip], across,
            )

        def add_core(zz, flip):
            b = number(zz, flip)

            def store(r):
                at = pl.ds(pl.multiple_of(b * rows + r.start, 16), r.size)
                core_buf[b, r, :] = (
                    core_buf[b, r, :].astype(jnp.float32)
                    + part_ref[at, pl.ds(pl.multiple_of(c * half, half), half)].astype(jnp.float32)
                ).astype(jnp.bfloat16)

            add_into(rows, 32, store)

        def add_across(zz, flip):
            b = number(zz, flip)

            def store(r):
                x_buf[b, r, :] = (
                    x_buf[b, r, :].astype(jnp.float32)
                    + core_buf[b, r, pl.ds(pl.multiple_of(x * quarter, quarter), quarter)].astype(jnp.float32)
                ).astype(jnp.bfloat16)

            add_into(rows, 64, store)

        def stage_twin(i):
            to_twin(*order[i]).wait_recv()
            add_core(*order[i])
            to_across(*order[i]).start()

        def stage_across(i):
            zz, flip = order[i]
            to_across(zz, flip).wait_recv()
            add_across(zz, flip)
            if flip:
                line.to_y(0, zz)

        def stage_y(zz):
            line.along_z(0, zz)

        for zz, flip in order:
            to_twin(zz, flip).start()
        count = len(order)
        for i in range(count + 4):
            if i < count:
                stage_twin(i)
            if 0 <= i - 1 < count:
                stage_across(i - 1)
            if i >= 3 and (i - 3) % 2 == 0 and (i - 3) // 2 < NZ:
                stage_y(Z_ORDER[(i - 3) // 2])

        def done(s, total):
            def store(r):
                out_ref[r, :] = total[r, :]

            add_into(rows, 64, store)

        line.home(done)
        for zz, flip in order:
            to_twin(zz, flip).wait_send()
            to_across(zz, flip).wait_send()
        line.finish()

    return pl.pallas_call(
        kernel,
        out_shape=jax.ShapeDtypeStruct((rows, quarter), jnp.bfloat16),
        in_specs=[VMEM],
        out_specs=VMEM,
        scratch_shapes=[
            pltpu.VMEM((GROUPS, rows, half), jnp.bfloat16),
            pltpu.VMEM((GROUPS, rows, quarter), jnp.bfloat16),
            pltpu.VMEM((NZ, rows, quarter), jnp.bfloat16),
            pltpu.VMEM((NZ, rows, quarter), jnp.bfloat16),
            pltpu.VMEM((NZ, rows, quarter), jnp.bfloat16),
            pltpu.SemaphoreType.DMA((NZ, 2)),
            pltpu.SemaphoreType.DMA((NZ, 2)),
            pltpu.SemaphoreType.DMA((NZ, 2)),
            pltpu.SemaphoreType.DMA((NZ, 2)),
            pltpu.SemaphoreType.DMA((1, NZ, 3)),
            pltpu.SemaphoreType.DMA((1, NZ, 3)),
        ],
        compiler_params=comm_params(collective_id),
        cost_estimate=cost(60),
        name="token_reduce",
    )(part)


def gate_exchange(part, collective_id):
    groups = part.shape[0]
    tensors = NX * NC

    def kernel(part_ref, out_ref, landing, total, send_t, recv_t, send_e, recv_e):
        e = lax.axis_index("expert")
        t = lax.axis_index("tensor")
        mates = [(e, lax.rem(t + k, tensors)) for k in range(1, tensors)]
        peers = [(lax.rem(e + k, groups), t) for k in range(1, groups)]
        greet([(target, None) for target in mates + peers])
        near = [
            remote(part_ref, landing.at[k], send_t.at[k], recv_t.at[k], mates[k])
            for k in range(tensors - 1)
        ]
        for copy in near:
            copy.start()
        for copy in near:
            copy.wait_recv()
        value = part_ref[...]
        for k in range(tensors - 1):
            value = value + landing[k]
        total[...] = value
        far = [
            remote(
                total.at[lax.rem(e + k, groups)], out_ref.at[e], send_e.at[k - 1], recv_e.at[k - 1],
                peers[k - 1],
            )
            for k in range(1, groups)
        ]
        for copy in far:
            copy.start()
        out_ref[e] = total[e]
        for k in range(1, groups):
            source = out_ref.at[lax.rem(e + groups - k, groups)]
            remote(source, source, send_e.at[k - 1], recv_e.at[k - 1], peers[k - 1]).wait_recv()
        for copy in near + far:
            copy.wait_send()

    return pl.pallas_call(
        kernel,
        out_shape=jax.ShapeDtypeStruct(part.shape, jnp.float32),
        in_specs=[VMEM],
        out_specs=VMEM,
        scratch_shapes=[
            pltpu.VMEM((tensors - 1,) + part.shape, jnp.float32),
            pltpu.VMEM(part.shape, jnp.float32),
            pltpu.SemaphoreType.DMA((tensors - 1,)),
            pltpu.SemaphoreType.DMA((tensors - 1,)),
            pltpu.SemaphoreType.DMA((groups - 1,)),
            pltpu.SemaphoreType.DMA((groups - 1,)),
        ],
        compiler_params=comm_params(collective_id, 16),
        cost_estimate=cost(10),
        name="gate_exchange",
    )(part)


def dot(a, b, dims):
    return lax.dot_general(a, b, ((dims[:1], dims[1:]), ((), ())), preferred_element_type=jnp.float32)


def add_to(target, first, second, step=64):
    rows = target.shape[0]

    def body(i, carry):
        r = pl.ds(pl.multiple_of(i * step, step), step)
        total = first[r, :].astype(jnp.float32) + second[r, :].astype(jnp.float32)
        target[r, :] = total.astype(target.dtype)
        return carry

    lax.fori_loop(0, rows // step, body, 0)


def expert_layer(
    hidden_two, grad_out_all, gate_up, down, router_t, chosen_all, residual, attended, collective_id
):
    rows, width = hidden_two.shape
    tokens = rows * GROUPS
    units = down.shape[0]
    local = 2
    hidden = units // local
    experts = router_t.shape[0]
    half, part, piece = width // 2, width // 4, width // 8
    tensors = NX * NC
    steps = GROUPS + 4
    a_cols, c_cols = width // 8, width // 4
    low = jnp.bfloat16
    wide = width // 4

    def kernel(
        own_in, dy_in, gu_ref, down_ref, router_ref, chosen_ref, x1_in, o_in,
        block_out, dh_out, gates_out, gate_w, up_w, down_w, o_all,
        h, dy, gated, dgu, dx, y_part, yc_buf, ypx_buf, ypy_buf, yqy_buf, yqx_buf, yz_sum,
        ylo_buf, yhi_buf, x1, gu_stage, d_stage,
        core_buf, px_buf, py_buf, qy_buf, qx_buf, z_sum, lo_buf, hi_buf, gate_part, gate_land,
        in_sem, own_sem, o_sem, line_s, line_r, hx_s, hx_r, hc_s, hc_r, x1_sem, yc_s, yc_r, ypx_s, ypx_r, ypy_s, ypy_r,
        yqy_s, yqy_r, yqx_s, yqx_r, yz_s, yz_r, gu_sem, d_sem, core_s, core_r, px_s, px_r, py_s, py_r, qy_s, qy_r, qx_s, qx_r,
        z_s, z_r, near_s, near_r, far_s, far_r, end_s, end_r,
    ):
        z, y, x, c = place()
        e, t = lax.axis_index("expert"), lax.axis_index("tensor")
        across, twin, beside = device(z, y, 1 - x, c), device(z, y, x, 1 - c), device(z, 1 - y, x, c)
        mates = [(e, lax.rem(t + k, tensors)) for k in range(1, tensors)]
        peers = [(lax.rem(e + k, GROUPS), t) for k in range(1, GROUPS)]
        greet([(target, None) for target in mates + peers])

        def pick(values, index):
            result = values[-1]
            for k in range(len(values) - 1):
                result = jnp.where(index == k, values[k], result)
            return result

        def zz_of(j):
            return pick([z, pick([1, 0, 3, 2], z), pick([3, 3, 0, 0], z), pick([2, 2, 1, 1], z)], j)

        def is_own(i):
            return (i == 0) | ((i >= 2) & (lax.rem(i, 2) == 1))

        def block_of(i):
            return zz_of(lax.div(i, 2)) * NY + jnp.where(is_own(i), y, 1 - y)

        def flip_block(j):
            return zz_of(j) * NY + 1 - y

        def own_block(j):
            return zz_of(j) * NY + y

        def a_at(xx, cc):
            return pl.ds(pl.multiple_of(xx * (2 * a_cols) + cc * a_cols, 128), a_cols)

        def c_at(cc):
            return pl.ds(pl.multiple_of(4 * a_cols + cc * c_cols, 128), c_cols)

        def h_view(b, columns):
            return h.at[block_rows(b, rows), columns]

        line = LineGather(
            [0, 1, 2], [own_in.at[:, a_at(x, c)], own_in.at[:, c_at(c)], o_in],
            [
                lambda b: h_view(b, a_at(x, c)),
                lambda b: h_view(b, c_at(c)),
                lambda b: o_all.at[block_rows(b, rows), :],
            ],
            line_s, line_r,
        )

        def h_twin(b, stream, landing=False):
            cc = 1 - c if landing else c
            piece = h_view(b, [a_at(x, cc), c_at(cc), a_at(1 - x, cc)][stream])
            return remote(piece, piece, hc_s.at[b, stream], hc_r.at[b, stream], twin)

        def h_across(b, landing=False):
            piece = h_view(b, a_at(1 - x if landing else x, c))
            return remote(piece, piece, hx_s.at[b], hx_r.at[b], across)

        def gather_event(rel):
            def body():
                b = line.block(rel)
                marks = len(line.pending)
                for stream in (0, 1):
                    line.arrive(stream, rel)
                    if rel < 7:
                        line.start(stream, rel)
                    if stream == 0:
                        h_across(b).start()
                    h_twin(b, stream).start()
                late = line.pending[marks:]
                del line.pending[marks:]
                line.finish_later(late, rel)
            run_if(line.exists(rel), body)

        def attended_event(rel):
            def body():
                marks = len(line.pending)
                line.arrive(2, rel)
                if rel < 7:
                    line.start(2, rel)
                late = line.pending[marks:]
                del line.pending[marks:]
                line.finish_later(late, rel)
            run_if(line.exists(rel), body)

        def relay(i):
            b = block_of(i)
            h_across(b, True).wait_recv()
            h_twin(b, 2).start()

        for stream in (0, 1):
            line.start(stream, 0)
        keep = pltpu.make_async_copy(own_in, h.at[block_rows(z * NY + y, rows), :], own_sem)
        keep.start()
        keep_o = pltpu.make_async_copy(o_in, o_all.at[block_rows(z * NY + y, rows), :], o_sem)
        keep_o.start()

        def load(i):
            r = block_rows(block_of(i), rows)
            return pltpu.make_async_copy(dy_in.at[r, :], dy.at[r, :], in_sem.at[i])

        def start_load(i, carry):
            load(i).start()
            return carry

        lax.fori_loop(0, GROUPS, start_load, 0)
        x1_copies = [
            pltpu.make_async_copy(
                x1_in.at[:, pl.ds(pl.multiple_of(c * half + s * part + x * piece, piece), piece)],
                x1.at[:, pl.ds(s * piece, piece)], x1_sem.at[s],
            )
            for s in range(2)
        ]
        for copy in x1_copies:
            copy.start()

        def to_twin(i):
            b = block_of(i)
            return remote(
                dx.at[lax.rem(i, 2), :, pl.ds(pl.multiple_of((1 - c) * half, half), half)],
                core_buf.at[b], core_s.at[i], core_r.at[i], twin,
            )

        def p_across(i):
            b = block_of(i)
            return remote(
                core_buf.at[b, :, pl.ds(pl.multiple_of((1 - x) * piece, piece), piece)],
                px_buf.at[b], px_s.at[i], px_r.at[i], across,
            )

        def p_beside(j):
            return remote(px_buf.at[flip_block(j)], py_buf.at[j], py_s.at[j], py_r.at[j], beside)

        def q_beside(j):
            return remote(
                core_buf.at[flip_block(j), :, pl.ds(part, part)], qy_buf.at[j], qy_s.at[j], qy_r.at[j], beside
            )

        def q_across(j):
            return remote(
                qy_buf.at[j, :, pl.ds(pl.multiple_of((1 - x) * piece, piece), piece)],
                qx_buf.at[j], qx_s.at[j], qx_r.at[j], across,
            )

        def up(j, s):
            return remote(z_sum.at[s, j], lo_buf.at[s, j], z_s.at[0, s, j], z_r.at[0, s, j], device(z + 1, y, x, c))

        def down_z(j, s):
            return remote(z_sum.at[s, j], hi_buf.at[s, j], z_s.at[1, s, j], z_r.at[1, s, j], device(z - 1, y, x, c))

        def take_twin(i):
            to_twin(i).wait_recv()
            b = block_of(i)
            mine = core_buf.at[b]
            add_to(mine, mine, dx.at[lax.rem(i, 2), :, pl.ds(pl.multiple_of(c * half, half), half)], 32)
            p_across(i).start()
            pl.when(jnp.logical_not(is_own(i)))(lambda: q_beside(lax.div(i, 2)).start())

        def take_p_across(i):
            p_across(i).wait_recv()
            b = block_of(i)
            add_to(
                px_buf.at[b], px_buf.at[b],
                core_buf.at[b, :, pl.ds(pl.multiple_of(x * piece, piece), piece)],
            )

        def take_q_beside(j):
            q_beside(j).wait_recv()
            add_to(qy_buf.at[j], qy_buf.at[j], core_buf.at[own_block(j), :, pl.ds(part, part)])
            q_across(j).start()

        def take_q_across(j):
            q_across(j).wait_recv()
            add_to(
                z_sum.at[1, zz_of(j)], qx_buf.at[j], qy_buf.at[j, :, pl.ds(pl.multiple_of(x * piece, piece), piece)]
            )

        def take_p_beside(j):
            p_beside(j).wait_recv()
            add_to(z_sum.at[0, zz_of(j)], py_buf.at[j], px_buf.at[own_block(j)])

        def hop(j, k):
            zz = zz_of(j)

            def upward():
                for s in range(2):
                    if k > 0:
                        up(zz, s).wait_recv()
                        add_to(z_sum.at[s, zz], z_sum.at[s, zz], lo_buf.at[s, zz])
                    up(zz, s).start()

            def downward():
                for s in range(2):
                    if k > 0:
                        down_z(zz, s).wait_recv()
                        add_to(z_sum.at[s, zz], z_sum.at[s, zz], hi_buf.at[s, zz])
                    down_z(zz, s).start()

            pl.when((z < zz) & (z == k))(upward)
            pl.when((z > zz) & (NZ - 1 - z == k))(downward)

        def y_twin(i):
            return remote(
                y_part.at[lax.rem(i, 2), :, pl.ds(pl.multiple_of((1 - c) * half, half), half)],
                yc_buf.at[block_of(i)], yc_s.at[i], yc_r.at[i], twin,
            )

        def yp_across(i):
            b = block_of(i)
            return remote(
                yc_buf.at[b, :, pl.ds(pl.multiple_of((1 - x) * piece, piece), piece)],
                ypx_buf.at[b], ypx_s.at[i], ypx_r.at[i], across,
            )

        def yp_beside(j):
            return remote(ypx_buf.at[flip_block(j)], ypy_buf.at[j], ypy_s.at[j], ypy_r.at[j], beside)

        def yq_beside(j):
            return remote(
                yc_buf.at[flip_block(j), :, pl.ds(part, part)], yqy_buf.at[j], yqy_s.at[j], yqy_r.at[j], beside
            )

        def yq_across(j):
            return remote(
                yqy_buf.at[j, :, pl.ds(pl.multiple_of((1 - x) * piece, piece), piece)],
                yqx_buf.at[j], yqx_s.at[j], yqx_r.at[j], across,
            )

        def y_up(zz, s):
            return remote(
                yz_sum.at[s, zz], ylo_buf.at[s, zz], yz_s.at[0, s, zz], yz_r.at[0, s, zz], device(z + 1, y, x, c)
            )

        def y_down(zz, s):
            return remote(
                yz_sum.at[s, zz], yhi_buf.at[s, zz], yz_s.at[1, s, zz], yz_r.at[1, s, zz], device(z - 1, y, x, c)
            )

        def take_y_twin(i):
            y_twin(i).wait_recv()
            mine = yc_buf.at[block_of(i)]
            add_to(mine, mine, y_part.at[lax.rem(i, 2), :, pl.ds(pl.multiple_of(c * half, half), half)], 32)
            yp_across(i).start()
            pl.when(jnp.logical_not(is_own(i)))(lambda: yq_beside(lax.div(i, 2)).start())

        def take_yp_across(i):
            yp_across(i).wait_recv()
            b = block_of(i)
            add_to(
                ypx_buf.at[b], ypx_buf.at[b],
                yc_buf.at[b, :, pl.ds(pl.multiple_of(x * piece, piece), piece)],
            )
            pl.when(jnp.logical_not(is_own(i)))(lambda: yp_beside(lax.div(i, 2)).start())

        def take_yq_beside(j):
            yq_beside(j).wait_recv()
            add_to(yqy_buf.at[j], yqy_buf.at[j], yc_buf.at[own_block(j), :, pl.ds(part, part)])
            yq_across(j).start()

        def take_y_sums(j):
            zz = zz_of(j)
            yq_across(j).wait_recv()
            add_to(
                yz_sum.at[1, zz], yqx_buf.at[j], yqy_buf.at[j, :, pl.ds(pl.multiple_of(x * piece, piece), piece)]
            )
            yp_beside(j).wait_recv()
            add_to(yz_sum.at[0, zz], ypy_buf.at[j], ypx_buf.at[own_block(j)])

        def y_take(zz, s, copy, landed):
            copy(zz, s).wait_recv()
            add_to(yz_sum.at[s, zz], yz_sum.at[s, zz], landed.at[s, zz])

        def y_hop(j, k):
            zz = zz_of(j)

            def upward():
                for s in range(2):
                    if k > 0:
                        y_take(zz, s, y_up, ylo_buf)
                    y_up(zz, s).start()

            def downward():
                for s in range(2):
                    if k > 0:
                        y_take(zz, s, y_down, yhi_buf)
                    y_down(zz, s).start()

            pl.when((z < zz) & (z == k))(upward)
            pl.when((z > zz) & (NZ - 1 - z == k))(downward)

        def front(i):
            load(i).wait()
            b = block_of(i)
            pl.when(i == 0)(keep.wait)

            def landed():
                for stream in range(3):
                    h_twin(b, stream, True).wait_recv()

            pl.when(i > 0)(landed)
            r = block_rows(b, rows)
            rows_h, rows_dy = h[r, :], dy[r, :]
            logits = dot(rows_h, router_ref[...], (1, 1))
            shifted = jnp.exp(logits - jnp.max(logits, axis=-1, keepdims=True))
            probs = shifted / jnp.sum(shifted, axis=-1, keepdims=True) * chosen_ref[r, :].astype(jnp.float32)
            lane = lax.broadcasted_iota(jnp.int32, probs.shape, 1)
            line = lax.broadcasted_iota(jnp.int32, (rows, 128), 1)
            found = jnp.zeros((rows, 128), jnp.float32)
            for expert in range(local):
                at, up_at = pl.ds(expert * hidden, hidden), pl.ds((local + expert) * hidden, hidden)
                gate = jnp.sum(jnp.where(lane == e * local + expert, probs, 0.0), axis=-1, keepdims=True)
                pre = dot(rows_h, gu_ref[:, at], (1, 0))
                scale = dot(rows_h, gu_ref[:, up_at], (1, 0))
                back = dot(rows_dy, down_ref[at, :], (1, 1))
                sigmoid = jax.nn.sigmoid(pre)
                swish = pre * sigmoid
                active = swish * scale
                gated[r, at] = (active * gate).astype(low)
                found = jnp.where(line == expert, jnp.sum(active * back, axis=-1, keepdims=True), found)
                back = back * gate
                dgu[r, at] = (back * scale * sigmoid * (1.0 + pre * (1.0 - sigmoid))).astype(low)
                dgu[r, up_at] = (back * swish).astype(low)
            gate_part[b] = jnp.transpose(found)[:8, :]

        def rear(i):
            r = block_rows(block_of(i), rows)
            slot = lax.rem(i, 2)
            pl.when(i >= 2)(lambda: to_twin(i - 2).wait_send())

            def columns(k, carry):
                at = pl.ds(pl.multiple_of(k * wide, wide), wide)
                dx[slot, :, at] = dot(dgu[r, :], gu_ref[at, :], (1, 1)).astype(low)
                return carry

            lax.fori_loop(0, width // wide, columns, 0)
            to_twin(i).start()
            pl.when(i >= 2)(lambda: y_twin(i - 2).wait_send())

            def y_columns(k, carry):
                at = pl.ds(pl.multiple_of(k * wide, wide), wide)
                y_part[slot, :, at] = dot(gated[r, :], down_ref[:, at], (1, 0)).astype(low)
                return carry

            lax.fori_loop(0, width // wide, y_columns, 0)
            y_twin(i).start()

        tile_width = piece // 2
        tiles = width // tile_width // 4
        d_width = width // 8

        def gu_copies(n):
            slot = lax.rem(n, 2)
            at = pl.ds(pl.multiple_of(n * tile_width, tile_width), tile_width)
            return [
                pltpu.make_async_copy(
                    gu_stage.at[slot, :, pl.ds(k * hidden, hidden)],
                    (gate_w if k < local else up_w).at[k % local, at, :],
                    gu_sem.at[slot, k],
                )
                for k in range(2 * local)
            ]

        def d_copies(n):
            slot = lax.rem(n, 2)
            at = pl.ds(pl.multiple_of(n * d_width, d_width), d_width)
            return [
                pltpu.make_async_copy(
                    d_stage.at[slot, pl.ds(k * hidden, hidden), :], down_w.at[k, :, at], d_sem.at[slot, k]
                )
                for k in range(local)
            ]

        def each(copies, what):
            for copy in copies:
                getattr(copy, what)()

        def weight_grads(q):
            def tile(k, carry):
                n = q * tiles + k
                pl.when(n >= 2)(lambda: each(gu_copies(n - 2), "wait"))
                at = pl.ds(pl.multiple_of(n * tile_width, tile_width), tile_width)
                gu_stage[lax.rem(n, 2)] = dot(h[:, at], dgu[...], (0, 0))
                each(gu_copies(n), "start")
                return carry

            lax.fori_loop(0, tiles, tile, 0)

            def d_tile(k, carry):
                n = q * 2 + k
                pl.when(n >= 2)(lambda: each(d_copies(n - 2), "wait"))
                at = pl.ds(pl.multiple_of(n * d_width, d_width), d_width)
                d_stage[lax.rem(n, 2)] = dot(gated[...], dy[:, at], (0, 0))
                each(d_copies(n), "start")
                return carry

            lax.fori_loop(0, 2, d_tile, 0)

        near = [
            remote(gate_part, gate_land.at[k], near_s.at[k], near_r.at[k], mates[k])
            for k in range(tensors - 1)
        ]

        def far(k):
            return remote(
                gate_land.at[tensors - 1, lax.rem(e + k, GROUPS)], gates_out.at[e],
                far_s.at[k - 1], far_r.at[k - 1], peers[k - 1],
            )

        def sum_near():
            for copy in near:
                copy.wait_recv()
            total = gate_part[...]
            for k in range(tensors - 1):
                total = total + gate_land[k]
            gate_land[tensors - 1] = total
            for k in range(1, GROUPS):
                far(k).start()
            gates_out[e] = gate_land[tensors - 1, e]

        def step(i, carry):
            def at(number, body):
                pl.when(i == number)(body)

            odd, even = lax.rem(i, 2) == 1, lax.rem(i, 2) == 0
            j_even, j_odd = lax.div(i, 2) - 1, lax.div(i - 1, 2) - 1
            pl.when(i < GROUPS)(lambda: front(i))

            def events(*rels):
                for rel in rels:
                    gather_event(rel)

            at(1, lambda: events(2, 5, 8, 11))
            at(2, lambda: events(3, 6))
            at(3, lambda: events(10, 13))

            def attended_events(*rels):
                for rel in rels:
                    attended_event(rel)

            at(8, lambda: attended_events(1, 4))
            at(9, lambda: attended_events(2, 5))
            at(10, lambda: attended_events(3, 6))
            at(11, lambda: attended_events(7, 8, 11))

            pl.when((i >= 1) & (i <= GROUPS))(lambda: take_twin(i - 1))
            pl.when(even & (i >= 4) & (i <= GROUPS))(lambda: take_q_beside(j_even))
            at(3, lambda: take_q_beside(0))
            at(4, lambda: take_q_across(0))

            def late():
                take_p_across(i - 2)
                pl.when(i > 3)(lambda: take_q_across(j_odd))
                pl.when(i == 3)(lambda: p_beside(0).start())

            pl.when(odd & (i >= 3) & (i <= GROUPS + 1))(late)
            at(GROUPS, lambda: each(near, "start"))
            at(GROUPS + 1, sum_near)
            pl.when(i < GROUPS)(lambda: rear(i))
            pl.when(i >= GROUPS)(lambda: weight_grads(i - GROUPS))
            at(0, lambda: events(7, 1, 4))
            at(2, lambda: events(9, 12))
            at(6, lambda: line.start(2, 0))
            pl.when(i < GROUPS - 1)(lambda: relay(i + 1))

            def pass_p():
                take_p_across(i - 2)
                pl.when(i > 2)(lambda: p_beside(j_even).start())

            pl.when(even & (i >= 2) & (i <= GROUPS))(pass_p)
            at(4, lambda: take_p_beside(0))

            def join():
                take_p_beside(j_odd)
                hop(j_odd, 0)

            pl.when(odd & (i >= 5) & (i <= GROUPS + 1))(join)
            pl.when((i == GROUPS) | (i == GROUPS + 2))(lambda: hop(j_even - 1, 1))
            at(GROUPS + 1, lambda: hop(1, 2))
            pl.when((i >= 2) & (i <= GROUPS + 1))(lambda: take_yp_across(i - 2))
            pl.when((i >= 1) & (i <= GROUPS))(lambda: take_y_twin(i - 1))
            pl.when(even & (i >= 4) & (i <= GROUPS))(lambda: take_yq_beside(j_even))
            at(3, lambda: take_yq_beside(0))
            at(5, lambda: take_y_sums(0))

            def join_y():
                take_y_sums(j_even - 1)
                y_hop(j_even - 1, 0)

            pl.when(even & (i >= 6) & (i <= GROUPS + 2))(join_y)
            pl.when((i == GROUPS + 1) | (i == GROUPS + 3))(lambda: y_hop(j_odd - 1, 1))
            at(GROUPS + 2, lambda: y_hop(1, 2))
            return carry

        lax.fori_loop(0, steps, step, 0)

        for rel in (9, 12, 10, 13):
            attended_event(rel)

        def columns_of(s, xx, cc):
            return pl.ds(pl.multiple_of(cc * half + s * part + xx * piece, piece), piece)

        mine = z
        for s in range(2):
            def below(s=s):
                up(mine, s).wait_recv()
                add_to(z_sum.at[s, mine], z_sum.at[s, mine], lo_buf.at[s, mine])

            def above(s=s):
                down_z(mine, s).wait_recv()
                add_to(z_sum.at[s, mine], z_sum.at[s, mine], hi_buf.at[s, mine])

            pl.when(z > 0)(below)
            pl.when(z < NZ - 1)(above)
            own = dh_out.at[:, columns_of(s, x, c)]

            def keep(k, carry, s=s, own=own):
                r = pl.ds(pl.multiple_of(k * 64, 64), 64)
                own[r, :] = z_sum[s, mine, r, :]
                return carry

            lax.fori_loop(0, rows // 64, keep, 0)
            remote(own, own, end_s.at[0, s], end_r.at[0, s], across).start()
            remote(own, own, end_s.at[1, s], end_r.at[1, s], twin).start()
        for copy in x1_copies:
            copy.wait()
        for s in range(2):
            pl.when(z > 0)(lambda s=s: y_take(z, s, y_up, ylo_buf))
            pl.when(z < NZ - 1)(lambda s=s: y_take(z, s, y_down, yhi_buf))
            y_own = block_out.at[:, columns_of(s, x, c)]

            def finish(k, carry, s=s, y_own=y_own):
                r = pl.ds(pl.multiple_of(k * 64, 64), 64)
                y_own[r, :] = (
                    x1[r, pl.ds(s * piece, piece)] + yz_sum[s, z, r, :].astype(jnp.float32)
                ).astype(low)
                return carry

            lax.fori_loop(0, rows // 64, finish, 0)
            remote(y_own, y_own, end_s.at[0, 2 + s], end_r.at[0, 2 + s], across).start()
            remote(y_own, y_own, end_s.at[1, 2 + s], end_r.at[1, 2 + s], twin).start()
        for s in range(2):
            there = dh_out.at[:, columns_of(s, 1 - x, c)]
            remote(there, there, end_s.at[0, s], end_r.at[0, s], across).wait_recv()
            remote(there, there, end_s.at[2, s], end_r.at[2, s], twin).start()
        for s in range(2):
            there = block_out.at[:, columns_of(s, 1 - x, c)]
            remote(there, there, end_s.at[0, 2 + s], end_r.at[0, 2 + s], across).wait_recv()
            remote(there, there, end_s.at[2, 2 + s], end_r.at[2, 2 + s], twin).start()
        for n, result in ((0, dh_out), (2, block_out)):
            for s in range(2):
                for k, xx in ((1, x), (2, 1 - x)):
                    there = result.at[:, columns_of(s, xx, 1 - c)]
                    remote(there, there, end_s.at[k, n + s], end_r.at[k, n + s], twin).wait_recv()
                for k, target in ((0, across), (1, twin), (2, twin)):
                    there = result.at[:, columns_of(s, 1 - x if k == 2 else x, c)]
                    remote(there, there, end_s.at[k, n + s], end_r.at[k, n + s], target).wait_send()
        for k in range(1, GROUPS):
            there = gates_out.at[lax.rem(e + GROUPS - k, GROUPS)]
            remote(there, there, far_s.at[k - 1], far_r.at[k - 1], peers[k - 1]).wait_recv()
            far(k).wait_send()
        each(near, "wait_send")

        def drain(i, carry):
            pl.when(i >= GROUPS - 2)(lambda: to_twin(i).wait_send())
            pl.when(i >= GROUPS - 2)(lambda: y_twin(i).wait_send())
            p_across(i).wait_send()
            yp_across(i).wait_send()
            return carry

        lax.fori_loop(0, GROUPS, drain, 0)

        def drain_pair(j, carry):
            p_beside(j).wait_send()
            q_beside(j).wait_send()
            q_across(j).wait_send()
            yp_beside(j).wait_send()
            yq_beside(j).wait_send()
            yq_across(j).wait_send()
            for s in range(2):
                pl.when(z < j)(lambda s=s: up(j, s).wait_send())
                pl.when(z > j)(lambda s=s: down_z(j, s).wait_send())
                pl.when(z < j)(lambda s=s: y_up(j, s).wait_send())
                pl.when(z > j)(lambda s=s: y_down(j, s).wait_send())
            return carry

        lax.fori_loop(0, NZ, drain_pair, 0)

        def drain_rows_of(i, carry):
            b = block_of(i)
            h_across(b).wait_send()
            for stream in range(3):
                h_twin(b, stream).wait_send()
            return carry

        lax.fori_loop(1, GROUPS, drain_rows_of, 0)
        line.finish()
        keep_o.wait()
        for k in range(2):
            each(gu_copies(4 * tiles - 2 + k), "wait")
            each(d_copies(6 + k), "wait")

    shape = jax.ShapeDtypeStruct
    dma = pltpu.SemaphoreType.DMA
    f32 = jnp.float32
    return pl.pallas_call(
        kernel,
        out_shape=(
            shape((rows, width), low),
            shape((rows, width), low),
            shape((GROUPS, 8, rows), f32),
            shape((local, width, hidden), f32),
            shape((local, width, hidden), f32),
            shape((local, hidden, width), f32),
            shape((tokens,) + attended.shape[1:], low),
        ),
        in_specs=[HBM, HBM, VMEM, VMEM, VMEM, VMEM, HBM, HBM],
        out_specs=(VMEM, VMEM, VMEM, HBM, HBM, HBM, HBM),
        scratch_shapes=[
            pltpu.VMEM((tokens, width), low),
            pltpu.VMEM((tokens, width), low),
            pltpu.VMEM((tokens, units), low),
            pltpu.VMEM((tokens, 2 * units), low),
            pltpu.VMEM((2, rows, width), low),
            pltpu.VMEM((2, rows, width), low),
            pltpu.VMEM((GROUPS, rows, half), low),
            pltpu.VMEM((GROUPS, rows, piece), low),
            pltpu.VMEM((NZ, rows, piece), low),
            pltpu.VMEM((NZ, rows, part), low),
            pltpu.VMEM((NZ, rows, piece), low),
            pltpu.VMEM((2, NZ, rows, piece), low),
            pltpu.VMEM((2, NZ, rows, piece), low),
            pltpu.VMEM((2, NZ, rows, piece), low),
            pltpu.VMEM((rows, part), f32),
            pltpu.VMEM((2, piece // 2, 2 * units), f32),
            pltpu.VMEM((2, units, width // 8), f32),
            pltpu.VMEM((GROUPS, rows, half), low),
            pltpu.VMEM((GROUPS, rows, piece), low),
            pltpu.VMEM((NZ, rows, piece), low),
            pltpu.VMEM((NZ, rows, part), low),
            pltpu.VMEM((NZ, rows, piece), low),
            pltpu.VMEM((2, NZ, rows, piece), low),
            pltpu.VMEM((2, NZ, rows, piece), low),
            pltpu.VMEM((2, NZ, rows, piece), low),
            pltpu.VMEM((GROUPS, 8, rows), f32),
            pltpu.VMEM((tensors, GROUPS, 8, rows), f32),
            dma((GROUPS,)), dma, dma, dma((3, 14, 3)), dma((3, 14)), dma((GROUPS,)), dma((GROUPS,)),
            dma((GROUPS, 3)), dma((GROUPS, 3)), dma((2,)), dma((GROUPS,)), dma((GROUPS,)), dma((GROUPS,)), dma((GROUPS,)),
            dma((NZ,)), dma((NZ,)), dma((NZ,)), dma((NZ,)), dma((NZ,)), dma((NZ,)),
            dma((2, 2, NZ)), dma((2, 2, NZ)), dma((2, 2 * local)), dma((2, local)),
            dma((GROUPS,)), dma((GROUPS,)), dma((GROUPS,)), dma((GROUPS,)),
            dma((NZ,)), dma((NZ,)), dma((NZ,)), dma((NZ,)), dma((NZ,)), dma((NZ,)),
            dma((2, 2, NZ)), dma((2, 2, NZ)),
            dma((tensors - 1,)), dma((tensors - 1,)), dma((GROUPS - 1,)), dma((GROUPS - 1,)),
            dma((3, 4)), dma((3, 4)),
        ],
        compiler_params=comm_params(collective_id, 62),
        cost_estimate=cost(80),
        name="expert_layer",
    )(hidden_two, grad_out_all, gate_up, down, router_t, chosen_all, residual, attended)


def exchange_rows(value, part_ref, land_ref, send_sem, recv_sem, mates):
    rows = value.shape[0]
    line = lax.broadcasted_iota(jnp.int32, (rows, 128), 1)
    part_ref[...] = jnp.transpose(jnp.where(line == 0, value, 0.0))[:8, :]
    for k, mate in enumerate(mates):
        remote(part_ref, land_ref.at[k], send_sem.at[k], recv_sem.at[k], mate).start()


def exchanged_rows(part_ref, land_ref, send_sem, recv_sem, mates):
    total = part_ref[...]
    for k, mate in enumerate(mates):
        remote(part_ref, land_ref.at[k], send_sem.at[k], recv_sem.at[k], mate).wait_recv()
    for k in range(len(mates)):
        total = total + land_ref[k]
    rows = part_ref.shape[1]
    tall = jnp.concatenate([total, jnp.zeros((120, rows), jnp.float32)], axis=0)
    return jnp.transpose(tall)[:, :1]


def drain_rows(part_ref, land_ref, send_sem, recv_sem, mates):
    for k, mate in enumerate(mates):
        remote(part_ref, land_ref.at[k], send_sem.at[k], recv_sem.at[k], mate).wait_send()


def turn(value, cosine, sine):
    return value * cosine + pltpu.roll(value, HEAD // 2, 1) * sine


def project(
    tokens, w_qkv, w_out, out_grad, gain_one, gain_two, qk_gain, w_router, routes, cosine, sine,
    w_gate, w_up, w_down, collective_id,
):
    rows, width = tokens.shape
    parts, depth, columns = w_qkv.shape
    heads = columns // HEAD
    tensors = NX * NC
    back = WINDOW // rows
    low, f32 = jnp.bfloat16, jnp.float32
    QUERY, KEY, VALUE, SMALL, OUT, GRAD, REST = 0, 1, 2, 3, 4, 5, 6
    out_half = w_out.shape[0] // 2
    out_rows, out_columns = w_out.shape
    quarter = width // tensors
    experts = w_router.shape[0]
    small_shape = (8 + 2 * experts, depth)

    def kernel(
        tok_ref, w_ref, out_ref, grad_in, gain_one_ref, gain_two_ref, qk_ref, w_router_ref, routes_ref, cos_ref, sin_ref, gate_in, up_in, down_in,
        w_all, out_all, grad_all, h1_out, raw_out, gate_up, down_out, gain_ref, router_ref, chosen_ref, scale_ref, q_ref, context,
        small_ref, small_all, h1_ref, raw_ref, wide_in, wide_low, down_f, down_low, own_w, own_out, weights, total, part_k, land_k, part_q, land_q,
        send_sem, recv_sem, out_sem, small_sem, kept, ks_s, ks_r, qs_s, qs_r, c_s, c_r, hx_s, hx_r, hc_s, hc_r, wide_s,
    ):
        z, y, x, c = place()
        e, t = lax.axis_index("expert"), lax.axis_index("tensor")
        wide_loads = [
            pltpu.make_async_copy(source.at[k], wide_in.at[2 * n + k], wide_s.at[2 * n + k])
            for n, source in enumerate((gate_in, up_in))
            for k in range(2)
        ]
        for copy in wide_loads:
            copy.start()
        mates = [(e, lax.rem(t + k, tensors)) for k in range(1, tensors)]
        beside, above = device(z, 1 - y, x, c), device(z + 1, y, x, c)
        views = [
            lambda b: weights.at[QUERY, block_rows(b, depth), :],
            lambda b: weights.at[KEY, block_rows(b, depth), :],
            lambda b: weights.at[VALUE, block_rows(b, depth), :],
            lambda b: small_all.at[b],
            lambda b: out_all.at[pl.ds(0, out_half), block_rows(b, out_columns)],
            lambda b: grad_view(b, x, c),
            lambda b: out_all.at[pl.ds(out_half, out_half), block_rows(b, out_columns)],
        ]
        across, twin = device(z, y, 1 - x, c), device(z, y, x, 1 - c)

        def quarter_at(xx, cc):
            return pl.ds(pl.multiple_of((xx * NC + cc) * quarter, quarter), quarter)

        def grad_view(b, xx, cc):
            return grad_all.at[block_rows(b, rows), quarter_at(xx, cc)]

        def grad_across(b, landing=False):
            piece = grad_view(b, 1 - x if landing else x, c)
            return remote(piece, piece, hx_s.at[b], hx_r.at[b], across)

        def grad_twin(b, relayed, landing=False):
            piece = grad_view(b, 1 - x if relayed else x, 1 - c if landing else c)
            return remote(piece, piece, hc_s.at[b, relayed], hc_r.at[b, relayed], twin)

        line = LineGather(
            [SMALL, VALUE, KEY, QUERY, OUT, GRAD, REST],
            [
                own_w.at[0], own_w.at[1], own_w.at[2], small_ref, own_out.at[pl.ds(0, out_half)],
                grad_in.at[:, quarter_at(x, c)], own_out.at[pl.ds(out_half, out_half)],
            ],
            views, send_sem, recv_sem, y_first=(OUT,),
        )
        small_ref[...] = jnp.zeros_like(small_ref)
        small_ref[0:1, :] = gain_one_ref[...].astype(low).astype(f32)
        small_ref[1:2, :] = gain_two_ref[...].astype(low).astype(f32)
        small_ref[2:3, : qk_gain.shape[1]] = qk_ref[...].astype(low).astype(f32)
        small_ref[8 : 8 + experts, :] = w_router_ref[...]
        expert_row = lax.broadcasted_iota(jnp.int32, (experts, rows), 0)
        named = jnp.zeros((experts, rows), f32)
        for k in range(routes.shape[0]):
            named = jnp.where(routes_ref[k : k + 1, :] == expert_row, 1.0, named)
        small_ref[8 + experts : 8 + 2 * experts, :] = named
        greet(line.partners() + [(mate, None) for mate in mates])
        line.start(SMALL, 0)
        for part in (VALUE, KEY, QUERY):
            def cast(i, carry, part=part):
                r = pl.ds(pl.multiple_of(i * 32, 32), 32)
                own_w[part, r, :] = w_ref[part, r, :].astype(low)
                return carry

            lax.fori_loop(0, depth // 32, cast, 0)
            if part != QUERY:
                line.start(part, 0)

        def cast_out(i, carry):
            r = pl.ds(pl.multiple_of(i * 32, 32), 32)
            own_out[r, :] = out_ref[r, :].astype(low)
            return carry

        lax.fori_loop(0, out_rows // 32, cast_out, 0)
        keep_out = pltpu.make_async_copy(own_out, out_all.at[:, block_rows(line.block(0), out_columns)], kept.at[0])
        keep_out.start()
        keep_grad = pltpu.make_async_copy(grad_in, grad_all.at[block_rows(line.block(0), rows), :], kept.at[1])
        keep_grad.start()

        def square(i, carry):
            r = pl.ds(pl.multiple_of(i * 32, 32), 32)
            value = tok_ref[r, :].astype(f32)
            scale_ref[r, 0:1] = lax.rsqrt(jnp.mean(value * value, axis=-1, keepdims=True) + EPS)
            return carry

        lax.fori_loop(0, rows // 32, square, 0)
        total[...] = jnp.zeros_like(total)
        own_small = pltpu.make_async_copy(small_ref, small_all.at[line.block(0)], small_sem)
        own_small.start()

        def use(stream, rel):
            b = line.block(rel)
            at = pl.ds(pl.multiple_of(b * depth, depth), depth)
            if stream == SMALL:
                gain = small_ref[0:1, :] if rel == 0 else small_all[b, 0:1, :]
                h1_ref[:, at] = (tok_ref[:, at].astype(f32) * scale_ref[:, 0:1] * gain).astype(low)
                return
            block = own_w[stream] if rel == 0 else weights[stream, block_rows(b, depth), :]
            total[stream] += dot(h1_ref[:, at], block, (1, 0))

        def event(stream, rel):
            def body():
                line.arrive(stream, rel)
                if line.forwards(stream, rel):
                    marks = len(line.pending)
                    line.start(stream, rel)
                    late = line.pending[marks:]
                    del line.pending[marks:]
                    line.finish_later(late, rel)
                if stream == GRAD:
                    b = line.block(rel)
                    grad_across(b).start()
                    grad_twin(b, 0).start()
                elif stream not in (OUT, REST):
                    use(stream, rel)
            run_if(line.exists(rel), body)

        use(SMALL, 0)
        use(VALUE, 0)
        own_small.wait()

        units = down_in.shape[1]
        for n, copy in enumerate(wide_loads):
            copy.wait()

            def round_wide(i, carry, n=n):
                r = pl.ds(pl.multiple_of(i * 64, 64), 64)
                wide_low[r, pl.ds(n * units, units)] = wide_in[n, r, :].astype(low)
                return carry

            lax.fori_loop(0, width // 64, round_wide, 0)
        wide_out = pltpu.make_async_copy(wide_low, gate_up, wide_s.at[0])
        wide_out.start()
        down_loads = [
            pltpu.make_async_copy(down_in.at[k], down_f.at[pl.ds(k * units, units), :], wide_s.at[1 + k])
            for k in range(2)
        ]
        for copy in down_loads:
            copy.start()

        use(KEY, 0)
        def events(*pairs):
            for stream, rels in pairs:
                for rel in rels:
                    event(stream, rel)

        for rel in (7, 1, 4, 2, 5):
            event(SMALL, rel)
            event(VALUE, rel)
        for copy in down_loads:
            copy.wait()

        def round_down(i, carry):
            r = pl.ds(pl.multiple_of(i * 32, 32), 32)
            down_low[r, :] = down_f[r, :].astype(low)
            return carry

        lax.fori_loop(0, 2 * units // 32, round_down, 0)
        down_copy = pltpu.make_async_copy(down_low, down_out, wide_s.at[3])
        down_copy.start()
        line.start(QUERY, 0)
        for rel in (3, 6):
            event(SMALL, rel)
            event(VALUE, rel)
        events((KEY, (7, 1, 4)))
        for rel in (8, 11, 9, 12, 10, 13):
            event(SMALL, rel)
            event(VALUE, rel)

        slices = HEAD // GROUPS
        for b in range(GROUPS):
            at = pl.ds(b * depth, depth)
            gain_ref[0:2, at] = small_all[b, 0:2, :]
            router_ref[:, at] = small_all[b, 8 : 8 + experts, :].astype(low)
            tall = jnp.concatenate(
                [small_all[b, 8 + experts : 8 + 2 * experts, :], jnp.zeros((128 - experts, depth), f32)], axis=0
            )
            chosen_ref[pl.ds(b * depth, depth), :] = jnp.transpose(tall)[:, :experts].astype(low)
        for which in range(2):
            for head in range(heads):
                start = (which * heads + head) * slices
                gain_ref[2 + which : 3 + which, pl.ds(head * HEAD, HEAD)] = jnp.concatenate(
                    [small_all[b, 2:3, start : start + slices] for b in range(GROUPS)], axis=1
                )

        def context_copy(which, k):
            if k == 2:
                source, target = 0, above
            elif k == 4:
                source, target = 2, above
            else:
                source, target = jnp.where(y == 0, k - 1, k + 1), beside
            return remote(
                context.at[source, which], context.at[k, which], c_s.at[which, k], c_r.at[which, k], target
            )

        sends = {2: z < NZ - 1, 4: (z >= 1) & (z < NZ - 1), 1: (y == 0) | (z >= 1), 3: z >= 1 + y}
        takes = {2: z >= 1, 4: z >= 2, 1: (y == 1) | (z >= 1), 3: z >= 2 - y}

        def context_send(which, k):
            run_if(sends[k], lambda: context_copy(which, k).start())

        def context_take(which, k):
            run_if(takes[k], lambda: context_copy(which, k).wait_recv())

        for k in range(1, back + 1):
            def clear(k=k):
                context[k] = jnp.zeros_like(context[k])
            run_if(jnp.logical_not(takes[k]), clear)

        context[0, 1] = total[VALUE].astype(low)
        context_send(1, 2)
        run_if(y == 0, lambda: context_copy(1, 1).start())
        events((KEY, (2, 5, 3, 6)), (QUERY, (7, 1, 4)))
        line.start(GRAD, 0)
        line.start(OUT, 0)
        line.start(REST, 0)
        events((KEY, (8, 11, 9, 12, 10, 13)))
        key_raw = total[KEY]
        raw_ref[1] = key_raw
        exchange_rows(jnp.sum(key_raw * key_raw, axis=-1, keepdims=True), part_k, land_k, ks_s, ks_r, mates)
        use(QUERY, 0)
        events((QUERY, (2, 5)))
        key_scale = lax.rsqrt(exchanged_rows(part_k, land_k, ks_s, ks_r, mates) / width + EPS)
        scale_ref[:, 2:3] = key_scale
        def rotated(which, scale, store):
            for head in range(heads):
                at = pl.ds(head * HEAD, HEAD)
                value = total[which, :, at] * scale * gain_ref[2 + which : 3 + which, at]
                store(at, turn(value, cos_ref[...], sin_ref[...]).astype(low))

        def store_key(at, value):
            context[0, 0, :, at] = value

        rotated(KEY, key_scale, store_key)
        context_send(0, 2)
        run_if(y == 0, lambda: context_copy(0, 1).start())

        def relay_two(which):
            context_take(which, 2)
            context_send(which, 4)
            run_if((y == 1) & (z >= 1), lambda: context_copy(which, 1).start())
            run_if((y == 0) & sends[3], lambda: context_copy(which, 3).start())

        def relay_four(which):
            context_take(which, 4)
            run_if((y == 1) & sends[3], lambda: context_copy(which, 3).start())

        relay_two(1)
        events((QUERY, (3, 6)), (GRAD, (7, 1, 4)), (OUT, (7, 1, 4)), (REST, (7, 1, 4)))
        relay_four(1)
        events((QUERY, (8, 11)), (GRAD, (2, 5)), (OUT, (8, 11, 2, 5)), (REST, (2, 5)))
        relay_two(0)
        events((QUERY, (9, 12, 10, 13)))
        query_raw = total[QUERY]
        raw_ref[0] = query_raw
        exchange_rows(jnp.sum(query_raw * query_raw, axis=-1, keepdims=True), part_q, land_q, qs_s, qs_r, mates)
        for part in range(parts):
            weights[part, block_rows(line.block(0), depth), :] = own_w[part]
        keep = pltpu.make_async_copy(weights, w_all, out_sem)
        keep.start()
        keep_more = [
            pltpu.make_async_copy(h1_ref, h1_out, kept.at[2]),
            pltpu.make_async_copy(raw_ref, raw_out, kept.at[3]),
        ]
        for copy in keep_more:
            copy.start()
        events((GRAD, (3, 6)), (OUT, (9, 12, 3, 6)), (REST, (3, 6, 8, 11)))
        relay_four(0)
        query_scale = lax.rsqrt(exchanged_rows(part_q, land_q, qs_s, qs_r, mates) / width + EPS)
        scale_ref[:, 1:2] = query_scale

        def store_query(at, value):
            q_ref[:, at] = value

        rotated(QUERY, query_scale, store_query)
        events((GRAD, (8, 11, 9, 12)), (OUT, (10, 13)), (REST, (9, 12, 10, 13)), (GRAD, (10, 13)))
        for which in (1, 0):
            for k in (1, 3):
                context_take(which, k)
        for rel in line.order():
            def relay(rel=rel):
                b = line.block(rel)
                grad_across(b, True).wait_recv()
                grad_twin(b, 1).start()
            run_if(line.exists(rel), relay)
        for rel in line.order():
            def landed(rel=rel):
                b = line.block(rel)
                grad_across(b).wait_send()
                for relayed in range(2):
                    grad_twin(b, relayed, True).wait_recv()
                    grad_twin(b, relayed).wait_send()
            run_if(line.exists(rel), landed)
        line.finish()
        for copy in keep_more:
            copy.wait()
        wide_out.wait()
        down_copy.wait()
        keep_out.wait()
        keep_grad.wait()
        for which in range(2):
            for k in range(1, back + 1):
                run_if(sends[k], lambda which=which, k=k: context_copy(which, k).wait_send())
        drain_rows(part_k, land_k, ks_s, ks_r, mates)
        drain_rows(part_q, land_q, qs_s, qs_r, mates)
        keep.wait()

    shape, dma = jax.ShapeDtypeStruct, pltpu.SemaphoreType.DMA
    return pl.pallas_call(
        kernel,
        out_shape=(
            shape((parts, depth * GROUPS, columns), low),
            shape((out_rows, out_columns * GROUPS), low),
            shape((rows * GROUPS, width), low),
            shape((rows, width), low),
            shape((2, rows, columns), f32),
            shape((width, 4 * w_down.shape[1]), low),
            shape((2 * w_down.shape[1], width), low),
            shape((8, width), f32),
            shape((experts, width), low),
            shape((rows * GROUPS, experts), low),
            shape((rows, 128), f32),
            shape((rows, columns), low),
            shape((back + 1, 2, rows, columns), low),
        ),
        in_specs=[VMEM, VMEM, VMEM, HBM] + [VMEM] * 7 + [HBM, HBM, HBM],
        out_specs=(HBM,) * 7 + (VMEM,) * 6,
        scratch_shapes=[
            pltpu.VMEM(small_shape, f32),
            pltpu.VMEM((GROUPS,) + small_shape, f32),
            pltpu.VMEM((rows, width), low),
            pltpu.VMEM((2, rows, columns), f32),
            pltpu.VMEM((4, width, w_down.shape[1]), f32),
            pltpu.VMEM((width, 4 * w_down.shape[1]), low),
            pltpu.VMEM((2 * w_down.shape[1], width), f32),
            pltpu.VMEM((2 * w_down.shape[1], width), low),
            pltpu.VMEM((parts, depth, columns), low),
            pltpu.VMEM((out_rows, out_columns), low),
            pltpu.VMEM((parts, depth * GROUPS, columns), low),
            pltpu.VMEM((parts, rows, columns), f32),
            pltpu.VMEM((8, rows), f32),
            pltpu.VMEM((tensors - 1, 8, rows), f32),
            pltpu.VMEM((8, rows), f32),
            pltpu.VMEM((tensors - 1, 8, rows), f32),
            dma((7, 14, 3)), dma((7, 14)), dma, dma, dma((4,)),
            dma((tensors - 1,)), dma((tensors - 1,)), dma((tensors - 1,)), dma((tensors - 1,)),
            dma((2, back + 1)), dma((2, back + 1)),
            dma((GROUPS,)), dma((GROUPS,)), dma((GROUPS, 2)), dma((GROUPS, 2)), dma((4,)),
        ],
        compiler_params=comm_params(collective_id, 62),
        cost_estimate=cost(100),
        name="project",
    )(
        tokens, w_qkv, w_out, out_grad, gain_one, gain_two, qk_gain, w_router, routes, cosine, sine,
        w_gate, w_up, w_down,
    )


def attend(query, context, segment_query, segment_keys, tokens, out_low, gain, collective_id):
    rows, columns = query.shape
    width = tokens.shape[1]
    blocks = context.shape[0]
    heads = columns // HEAD
    half, quarter = width // 2, width // 4
    low, f32 = jnp.bfloat16, jnp.float32

    def kernel(
        q_ref, context_in, sq_ref, sk_ref, tok_ref, out_in, gain_ref,
        o_ref, lse_ref, x1_out, h2_out, scale_ref,
        context_ref, out_ref, x1_ref, h2_ref, copy_sem, part, full, core_buf, x_buf, send_sem, recv_sem,
    ):
        z, y, x, c = place()
        across, twin = device(z, y, 1 - x, c), device(z, y, x, 1 - c)
        context_load = pltpu.make_async_copy(context_in, context_ref, copy_sem.at[0])
        context_load.start()
        out_load = pltpu.make_async_copy(out_in, out_ref, copy_sem.at[1])
        out_load.start()
        greet([(across, None), (twin, None)])
        row = lax.broadcasted_iota(jnp.int32, (rows, rows), 0)
        column = lax.broadcasted_iota(jnp.int32, (rows, rows), 1)
        allowed = []
        for k in range(blocks):
            distance = row - column + k * rows
            allowed.append(
                (sq_ref[...] == sk_ref[k : k + 1, :]) & (distance >= 0) & (distance < WINDOW)
            )
        line = lax.broadcasted_iota(jnp.int32, (rows, 128), 1)
        lse = jnp.zeros((rows, 128), f32)
        context_load.wait()
        for head in range(heads):
            at = pl.ds(head * HEAD, HEAD)
            scores = [
                jnp.where(
                    allowed[k], dot(q_ref[:, at], context_ref[k, 0, :, at], (1, 1)) * HEAD ** (-0.5), -1e30
                )
                for k in range(blocks)
            ]
            largest = scores[0]
            for k in range(1, blocks):
                largest = jnp.maximum(largest, scores[k])
            largest = jnp.max(largest, axis=-1, keepdims=True)
            weights = [jnp.exp(s - largest) for s in scores]
            amount = weights[0]
            for k in range(1, blocks):
                amount = amount + weights[k]
            amount = jnp.sum(amount, axis=-1, keepdims=True)
            inverse = 1.0 / amount
            value = jnp.zeros((rows, HEAD), f32)
            for k in range(blocks):
                value = value + dot((weights[k] * inverse).astype(low), context_ref[k, 1, :, at], (1, 0))
            o_ref[:, at] = value.astype(low)
            lse = jnp.where(line == head, largest + jnp.log(amount), lse)
        lse_ref[...] = lse

        def half_of(cc):
            return pl.ds(pl.multiple_of(cc * half, half), half)

        def fill(cc):
            def body(k, carry):
                at = pl.ds(pl.multiple_of(cc * half + k * quarter, quarter), quarter)
                part[:, at] = dot(o_ref[...], out_ref[:, at], (1, 0)).astype(low)
                return carry

            lax.fori_loop(0, 2, body, 0)

        out_load.wait()
        fill(1 - c)
        group_sum(part, full, core_buf, x_buf, send_sem, recv_sem, lambda: fill(c))

        def norm(i, carry):
            r = pl.ds(pl.multiple_of(i * 32, 32), 32)
            value = tok_ref[r, :].astype(f32) + full[r, :].astype(f32)
            scale = lax.rsqrt(jnp.mean(value * value, axis=-1, keepdims=True) + EPS)
            x1_ref[r, :] = value
            scale_ref[r, :] = jnp.broadcast_to(scale, (32, 128))
            h2_ref[r, :] = (value * scale * gain_ref[1:2, :]).astype(low)
            return carry

        lax.fori_loop(0, rows // 32, norm, 0)
        keep = [
            pltpu.make_async_copy(x1_ref, x1_out, copy_sem.at[2]),
            pltpu.make_async_copy(h2_ref, h2_out, copy_sem.at[3]),
        ]
        for copy in keep:
            copy.start()
        for copy in keep:
            copy.wait()

    shape, dma = jax.ShapeDtypeStruct, pltpu.SemaphoreType.DMA
    return pl.pallas_call(
        kernel,
        out_shape=(
            shape((rows, columns), low),
            shape((rows, 128), f32),
            shape((rows, width), f32),
            shape((rows, width), low),
            shape((rows, 128), f32),
        ),
        in_specs=[VMEM, HBM, VMEM, VMEM, VMEM, HBM, VMEM],
        out_specs=(VMEM, VMEM, HBM, HBM, VMEM),
        scratch_shapes=[
            pltpu.VMEM(context.shape, low),
            pltpu.VMEM(out_low.shape, low),
            pltpu.VMEM((rows, width), f32),
            pltpu.VMEM((rows, width), low),
            dma((4,)),
            pltpu.VMEM((rows, width), low),
            pltpu.VMEM((rows, width), low),
            pltpu.VMEM((rows, half), low),
            pltpu.VMEM((rows, quarter), low),
            dma((5,)), dma((5,)),
        ],
        compiler_params=comm_params(collective_id, 62),
        cost_estimate=cost(40),
        name="attend",
    )(query, context, segment_query, segment_keys, tokens, out_low, gain)


def attend_back(
    grad_hidden, grad_probs, router_t, hidden_two, residual, scale_two, gains, out_grad,
    query, context, segment_query, segment_keys, attended, log_sums, raw, scales,
    cosine, sine, hidden_one, tokens, attended_all, qkv_low, out_low, collective_id,
):
    rows, width = tokens.shape
    columns = query.shape[1]
    heads = columns // HEAD
    experts = router_t.shape[0]
    blocks = context.shape[0]
    depth = width // GROUPS
    small_rows = 8 + experts
    tensors = NX * NC
    half, quarter = width // 2, width // 4
    low, f32 = jnp.bfloat16, jnp.float32
    QUERY, KEY, VALUE, OUT, SMALL = 0, 1, 2, 3, 4

    def kernel(
        dh_ref, gates_ref, router_ref, h2_ref, x1_ref, s2_ref, gain_ref, dy_ref,
        q_ref, context_ref, sq_ref, sk_ref, o_ref, lse_ref, raw_ref, scale_ref,
        cos_ref, sin_ref, h1_ref, tok_ref, o_all, w_hbm, out_ref,
        tok_grad, qkv_sum, out_sum, small_sum,
        weights, dx1, da, do, dot_sums, dq, dkv, scaled, proj, send_kv, land_y, land_z,
        part, full, core_buf, x_buf, small, line_sum,
        main_buf, da_all, small_buf, part_k, land_k, part_q, land_q,
        w_sem, y_s, y_r, z_s, z_r, group_s, group_r, ks_s, ks_r, qs_s, qs_r, line_s, line_r, far_s, far_r, near_s, near_r,
    ):
        z, y, x, c = place()
        e, t = lax.axis_index("expert"), lax.axis_index("tensor")
        mates = [(e, lax.rem(t + k, tensors)) for k in range(1, tensors)]
        beside, below = device(z, 1 - y, x, c), device(z - 1, y, x, c)
        fetch = pltpu.make_async_copy(w_hbm, weights, w_sem)
        fetch.start()

        def own_part(s, b):
            if s == SMALL:
                return small[b]
            at = pl.ds(pl.multiple_of(b * depth, depth), depth)
            return dot(h1_ref[:, at], proj[s], (0, 0))

        peers = [(lax.rem(e + k, GROUPS), t) for k in range(1, GROUPS)]
        share = rows // tensors
        share_at = pl.ds(pl.multiple_of(t * share, share), share)

        def columns_of(owner):
            return pl.ds(pl.multiple_of(owner * depth, depth), depth)

        def da_far(k):
            owner = lax.rem(e + k, GROUPS)
            return remote(
                da.at[share_at, columns_of(owner)], da_all.at[e, share_at, :], far_s.at[k - 1], far_r.at[k - 1],
                peers[k - 1],
            )

        def da_near(k):
            piece = da_all.at[:, share_at, :]
            return remote(piece, piece, near_s.at[k], near_r.at[k], mates[k])

        def da_start():
            for k in range(1, GROUPS):
                da_far(k).start()
            da_all[e, share_at, :] = da[share_at, columns_of(e)]

        def da_spread():
            for k in range(1, GROUPS):
                landing = da_all.at[lax.rem(e + GROUPS - k, GROUPS), share_at, :]
                remote(landing, landing, far_s.at[k - 1], far_r.at[k - 1], peers[k - 1]).wait_recv()
            for k in range(tensors - 1):
                da_near(k).start()

        def da_end():
            for k in range(tensors - 1):
                theirs = lax.rem(t + tensors - 1 - k, tensors)
                landing = da_all.at[:, pl.ds(pl.multiple_of(theirs * share, share), share), :]
                remote(landing, landing, near_s.at[k], near_r.at[k], mates[k]).wait_recv()
            result = jnp.zeros((columns, depth), f32)
            for b in range(GROUPS):
                result = result + dot(o_all[pl.ds(b * rows, rows), :], da_all[b], (0, 0))
            out_sum[...] = result
            for k in range(1, GROUPS):
                da_far(k).wait_send()
            for k in range(tensors - 1):
                da_near(k).wait_send()

        def slot(kind):
            def view(s, zz):
                if s == SMALL:
                    return small_buf.at[kind, zz]
                return main_buf.at[kind, zz, s]
            return view

        line = LineReduce([], lambda s, zz, yy: slot(3)(s, zz), slot(0), slot(1), slot(2), line_s, line_r)
        greet([(target, None) for target in mates + peers])

        grad_probs = gates_ref[...]
        logits = dot(h2_ref[...], router_ref[...], (1, 1))
        shifted = jnp.exp(logits - jnp.max(logits, axis=-1, keepdims=True))
        probs = shifted / jnp.sum(shifted, axis=-1, keepdims=True)
        grad_logits = probs * (grad_probs - jnp.sum(probs * grad_probs, axis=-1, keepdims=True))
        tall = jnp.transpose(
            jnp.concatenate([grad_logits, jnp.zeros((rows, 128 - experts), f32)], axis=1)
        )
        grad_logits = grad_logits.astype(low)
        tall = tall.astype(low)
        for b in range(GROUPS):
            small[b] = jnp.zeros_like(small[b])
            small[b, 8 : 8 + experts, :] = dot(tall, h2_ref[:, pl.ds(b * depth, depth)], (1, 0))[:experts]
        dx1[...] = dot(grad_logits, router_ref[...], (1, 0))
        line_sum[...] = jnp.zeros_like(line_sum)

        def norm_two(i, carry):
            r = pl.ds(pl.multiple_of(i * 32, 32), 32)
            grad = dh_ref[r, :].astype(f32) + dx1[r, :]
            value, scale = x1_ref[r, :], s2_ref[r, 0:1]
            line_sum[0:1, :] += jnp.sum(grad * (value * scale), axis=0, keepdims=True)
            grad = grad * gain_ref[1:2, :]
            inner = jnp.mean(grad * value, axis=-1, keepdims=True)
            result = dy_ref[r, :].astype(f32) + scale * grad - value * (scale * scale * scale) * inner
            dx1[r, :] = result
            da[r, :] = result.astype(low)
            return carry

        lax.fori_loop(0, rows // 32, norm_two, 0)

        da_start()

        do[...] = dot(da[...], out_ref[...], (1, 1)).astype(low)
        wide = lax.broadcasted_iota(jnp.int32, (rows, 128), 1)
        sums = jnp.zeros((rows, 128), f32)
        for head in range(heads):
            at = pl.ds(head * HEAD, HEAD)
            inner = jnp.sum(do[:, at].astype(f32) * o_ref[:, at].astype(f32), axis=-1, keepdims=True)
            sums = jnp.where(wide == head, inner, sums)
        dot_sums[...] = sums
        dq[...] = jnp.zeros_like(dq)
        row = lax.broadcasted_iota(jnp.int32, (rows, rows), 0)
        column = lax.broadcasted_iota(jnp.int32, (rows, rows), 1)

        def attention_block(k):
            distance = row - column + k * rows
            allowed = (sq_ref[...] == sk_ref[k : k + 1, :]) & (distance >= 0) & (distance < WINDOW)
            for head in range(heads):
                at = pl.ds(head * HEAD, HEAD)
                queries, keys, values = q_ref[:, at], context_ref[k, 0, :, at], context_ref[k, 1, :, at]
                scores = dot(queries, keys, (1, 1)) * HEAD ** (-0.5)
                weight = jnp.where(allowed, jnp.exp(scores - lse_ref[:, head : head + 1]), 0.0)
                grad_weight = dot(do[:, at], values, (1, 1))
                grad_score = (
                    weight * (grad_weight - dot_sums[:, head : head + 1]) * HEAD ** (-0.5)
                ).astype(low)
                dq[:, at] += dot(grad_score, keys, (1, 0))
                dkv[k, 0, :, at] = dot(grad_score, queries, (0, 0))
                dkv[k, 1, :, at] = dot(weight.astype(low), do[:, at], (0, 0))

        exists = {0: None, 1: (y == 1) | (z >= 1), 2: z >= 1, 3: z >= 2 - y, 4: z >= 2}
        comes = {1: (y == 0) | (z >= 1), 3: z >= 1 + y}

        def kv_copy(which, k):
            if k in (1, 3):
                landing, target = land_y.at[k // 2, which], beside
                return remote(send_kv.at[k - 1, which], landing, y_s.at[k // 2, which], y_r.at[k // 2, which], target)
            landing = land_z.at[k // 2 - 1, which]
            return remote(
                send_kv.at[k - 1, which], landing, z_s.at[k // 2 - 1, which], z_r.at[k // 2 - 1, which], below
            )

        def kv_send(which, k):
            send_kv[k - 1, which] = dkv[k, which].astype(low)
            kv_copy(which, k).start()

        def merge(into, which, landed):
            add_to(dkv.at[into, which], dkv.at[into, which], landed, 32)

        for k in (3, 1, 4, 2, 0):
            def one(k=k):
                attention_block(k)
                if k in (1, 3):
                    kv_send(1, k)
                    kv_send(0, k)
            run_if(exists[k], one)

        def take_three(which):
            def land():
                kv_copy(which, 3).wait_recv()
                pl.when(y == 1)(lambda: merge(4, which, land_y.at[1, which]))
                pl.when(y == 0)(lambda: merge(2, which, land_y.at[1, which]))
            run_if(comes[3], land)
            run_if(exists[4], lambda: kv_send(which, 4))

        def take_one(which):
            def land():
                kv_copy(which, 1).wait_recv()
                pl.when(y == 1)(lambda: merge(2, which, land_y.at[0, which]))
                pl.when(y == 0)(lambda: merge(0, which, land_y.at[0, which]))
            run_if(comes[1], land)

        def take_four(which):
            def land():
                kv_copy(which, 4).wait_recv()
                merge(2, which, land_z.at[1, which])
            run_if((z >= 1) & (z < NZ - 1), land)
            run_if(exists[2], lambda: kv_send(which, 2))

        def take_two(which):
            def land():
                kv_copy(which, 2).wait_recv()
                merge(0, which, land_z.at[0, which])
            run_if(z < NZ - 1, land)

        def unturn(which, grad_of):
            inner = jnp.zeros((rows, 1), f32)
            for head in range(heads):
                at = pl.ds(head * HEAD, HEAD)
                grad = turn(grad_of(at), cos_ref[...], -sin_ref[...])
                value = raw_ref[which, :, at]
                line_sum[1 + which : 2 + which, at] = jnp.sum(
                    grad * (value * scale_ref[:, 1 + which : 2 + which]), axis=0, keepdims=True
                )
                grad = grad * gain_ref[2 + which : 3 + which, at]
                scaled[which, :, at] = grad
                inner = inner + jnp.sum(grad * value, axis=-1, keepdims=True)
            return inner

        def denorm(which, inner):
            scale = scale_ref[:, 1 + which : 2 + which]
            rest = scale * scale * scale * inner / width
            for head in range(heads):
                at = pl.ds(head * HEAD, HEAD)
                proj[which, :, at] = (
                    scale * scaled[which, :, at] - raw_ref[which, :, at] * rest
                ).astype(low)

        def send_beside(s):
            for zz in Z_ORDER:
                buffer = slot(3)(s, zz)
                buffer[...] = own_part(s, zz * NY + 1 - y).astype(buffer.dtype)
                line.to_y(s, zz)

        exchange_rows(unturn(QUERY, lambda at: dq[:, at]), part_q, land_q, qs_s, qs_r, mates)
        take_three(1)
        take_three(0)
        denorm(QUERY, exchanged_rows(part_q, land_q, qs_s, qs_r, mates))
        send_beside(QUERY)
        da_spread()
        take_one(1)
        take_one(0)
        take_four(1)
        take_four(0)
        take_two(1)
        proj[VALUE] = dkv[0, 1].astype(low)
        send_beside(VALUE)
        take_two(0)
        exchange_rows(unturn(KEY, lambda at: dkv[0, 0, :, at]), part_k, land_k, ks_s, ks_r, mates)
        denorm(KEY, exchanged_rows(part_k, land_k, ks_s, ks_r, mates))
        send_beside(KEY)
        fetch.wait()

        def half_of(cc):
            def body(i, carry):
                at = pl.ds(pl.multiple_of(cc * half + i * quarter, quarter), quarter)
                value = dot(proj[0], weights[0, at, :], (1, 1))
                for s in (1, 2):
                    value = value + dot(proj[s], weights[s, at, :], (1, 1))
                part[:, at] = value.astype(low)
                return carry

            lax.fori_loop(0, 2, body, 0)

        stages = group_stages(part, full, core_buf, x_buf, group_s, group_r)
        half_of(1 - c)
        stages[0]()
        half_of(c)
        stages[1]()

        def hop(s, zz, k):
            def upward():
                if k > 0:
                    line.take(s, zz, 1)
                line.copy(s, zz, 1).start()

            def downward():
                if k > 0:
                    line.take(s, zz, 2)
                line.copy(s, zz, 2).start()

            if k < zz:
                run_if((z < zz) & (z == k), upward)
            if NZ - 1 - k > zz:
                run_if((z > zz) & (NZ - 1 - z == k), downward)

        def receive(s, zz):
            line.copy(s, zz, 0).wait_recv()
            buffer = slot(0)(s, zz)
            buffer[...] = (buffer[...].astype(f32) + own_part(s, zz * NY + y)).astype(buffer.dtype)

        units = []

        def run_units(s):
            for zz in Z_ORDER:
                receive(s, zz)
                hop(s, zz, 0)
                units.append((s, zz))
                for k in (1, 2):
                    if len(units) > k:
                        hop(*units[-1 - k], k)

        def norm_one(i, carry):
            r = pl.ds(pl.multiple_of(i * 32, 32), 32)
            grad, value, scale = full[r, :].astype(f32), tok_ref[r, :].astype(f32), scale_ref[r, 0:1]
            line_sum[3:4, :] += jnp.sum(grad * (value * scale), axis=0, keepdims=True)
            grad = grad * gain_ref[0:1, :]
            inner = jnp.mean(grad * value, axis=-1, keepdims=True)
            tok_grad[r, :] = (
                dx1[r, :] + scale * grad - value * (scale * scale * scale) * inner
            ).astype(low)
            return carry

        run_units(QUERY)
        stages[2]()
        run_units(VALUE)
        da_end()
        stages[3]()
        stages[4]()
        lax.fori_loop(0, rows // 32, norm_one, 0)
        for b in range(GROUPS):
            at = pl.ds(b * depth, depth)
            small[b, 0:1, :] = line_sum[3:4, at]
            small[b, 1:2, :] = line_sum[0:1, at]
            for which in range(2):
                for k in range(columns // depth):
                    small[b, 2 + 2 * which + k : 3 + 2 * which + k, :] = line_sum[
                        1 + which : 2 + which, pl.ds(k * depth, depth)
                    ]
        send_beside(SMALL)
        run_units(KEY)
        run_units(SMALL)
        hop(*units[-1], 1)
        hop(*units[-2], 2)
        hop(*units[-1], 2)

        def done(s, total):
            target = qkv_sum.at[s] if s < OUT else small_sum
            target[...] = total[...].astype(f32)

        line.streams = [QUERY, VALUE, KEY, SMALL]
        line.home(done)
        line.finish()
        for which in range(2):
            for k in (1, 2, 3, 4):
                run_if(exists[k], lambda which=which, k=k: kv_copy(which, k).wait_send())
        drain_rows(part_k, land_k, ks_s, ks_r, mates)
        drain_rows(part_q, land_q, qs_s, qs_r, mates)

    shape, dma, vmem = jax.ShapeDtypeStruct, pltpu.SemaphoreType.DMA, pltpu.VMEM
    return pl.pallas_call(
        kernel,
        out_shape=(
            shape((rows, width), low),
            shape((3, depth, columns), f32),
            shape((columns, depth), f32),
            shape((small_rows, depth), f32),
        ),
        in_specs=[VMEM] * 21 + [HBM, VMEM],
        out_specs=(VMEM,) * 4,
        scratch_shapes=[
            vmem(qkv_low.shape, low),
            vmem((rows, width), f32),
            vmem((rows, width), low),
            vmem((rows, columns), low),
            vmem((rows, 128), f32),
            vmem((rows, columns), f32),
            vmem((blocks, 2, rows, columns), f32),
            vmem((2, rows, columns), f32),
            vmem((3, rows, columns), low),
            vmem((blocks - 1, 2, rows, columns), low),
            vmem((2, 2, rows, columns), low),
            vmem((2, 2, rows, columns), low),
            vmem((rows, width), low),
            vmem((rows, width), low),
            vmem((rows, half), low),
            vmem((rows, quarter), low),
            vmem((GROUPS, small_rows, depth), f32),
            vmem((8, width), f32),
            vmem((4, NZ, 3, depth, columns), low),
            vmem((GROUPS, rows, depth), low),
            vmem((4, NZ, small_rows, depth), f32),
            vmem((8, rows), f32),
            vmem((tensors - 1, 8, rows), f32),
            vmem((8, rows), f32),
            vmem((tensors - 1, 8, rows), f32),
            dma, dma((2, 2)), dma((2, 2)), dma((2, 2)), dma((2, 2)), dma((5,)), dma((5,)),
            dma((tensors - 1,)), dma((tensors - 1,)), dma((tensors - 1,)), dma((tensors - 1,)),
            dma((5, NZ, 3)), dma((5, NZ, 3)), dma((GROUPS - 1,)), dma((GROUPS - 1,)), dma((tensors - 1,)), dma((tensors - 1,)),
        ],
        compiler_params=comm_params(collective_id, 62),
        cost_estimate=cost(130),
        name="attend_back",
    )(
        grad_hidden, grad_probs, router_t, hidden_two, residual, scale_two, gains, out_grad,
        query, context, segment_query, segment_keys, attended, log_sums, raw, scales,
        cosine, sine, hidden_one, tokens, attended_all, qkv_low, out_low,
    )


def fast_shards(
    tokens_in,
    out_grad,
    w_qkv,
    w_attn_out,
    attn_gain,
    ffn_gain,
    qk_gain,
    w_router,
    w_gate,
    w_up,
    w_down,
    routes,
    segments,
):
    row_count, model_width = tokens_in.shape
    experts = w_router.shape[1]
    local_experts = w_gate.shape[0]
    heads_here = qk_gain.shape[1]
    local_width = heads_here * HEAD
    groups = lax.axis_size("expert")
    device_index = lax.axis_index("expert")
    tensor_index = lax.axis_index("tensor")
    quarter = model_width // lax.axis_size("tensor")
    hop_count = WINDOW // row_count
    score_scale = HEAD ** (-0.5)
    low = jnp.bfloat16

    chosen = jnp.any(
        routes[:, :, None] == jnp.arange(experts, dtype=jnp.int32)[None, None, :], axis=1
    ).astype(jnp.float32)
    qk_row = qk_gain.reshape(1, -1)

    global_rows = device_index * row_count + jnp.arange(row_count, dtype=jnp.int32)
    cosine_table, sine_table = angles(global_rows % SEQ, HEAD)
    wide_cosine = jnp.concatenate([cosine_table[:, 0], cosine_table[:, 0]], axis=1)
    wide_sine = jnp.concatenate([-sine_table[:, 0], sine_table[:, 0]], axis=1)
    (
        qkv_low, out_low, grad_out_all, hidden_one, raw, gate_up, down_low, gains, router_t, chosen_all,
        scales, query_low, context_blocks,
    ) = project(
        tokens_in, w_qkv, w_attn_out, out_grad, attn_gain[None, :], ffn_gain[None, :], qk_row, w_router.T, routes.T,
        wide_cosine, wide_sine, w_gate, w_up, w_down, 0,
    )
    segment_window = lax.dynamic_slice_in_dim(
        jnp.concatenate([jnp.full((WINDOW,), -1, jnp.int32), segments]),
        device_index * row_count, (hop_count + 1) * row_count,
    )
    segment_query = segment_window[WINDOW:]
    segment_keys = segment_window.reshape(hop_count + 1, row_count)[::-1]
    attended, log_sums, residual, hidden_two, scale_two_wide = attend(
        query_low, context_blocks, segment_query[:, None], segment_keys, tokens_in, out_low,
        gains, 2,
    )
    (
        block_out, grad_hidden_sum, grad_gate_sum, grad_gate_w, grad_up_w, grad_down, attended_all
    ) = expert_layer(
        hidden_two, grad_out_all, gate_up, down_low, router_t, chosen_all, residual, attended, 5
    )
    grad_probs = grad_gate_sum[:, :local_experts].reshape(experts, row_count).T * chosen
    grad_tokens, qkv_sum, out_sum, small_sum = attend_back(
        grad_hidden_sum, grad_probs, router_t, hidden_two, residual, scale_two_wide,
        gains, out_grad, query_low, context_blocks, segment_query[:, None], segment_keys,
        attended, log_sums, raw, scales, wide_cosine, wide_sine, hidden_one, tokens_in, attended_all,
        qkv_low, out_low, 8,
    )
    return (
        block_out,
        grad_tokens,
        qkv_sum,
        out_sum,
        small_sum[0],
        small_sum[1],
        lax.dynamic_slice_in_dim(
            small_sum[2:6].reshape(2, heads_here, HEAD),
            device_index * qk_gain.shape[2], qk_gain.shape[2], axis=2,
        ),
        small_sum[8 : 8 + experts].T,
        grad_gate_w,
        grad_up_w,
        grad_down,
    )


def solution(mesh):
    placed = (
        P("expert", None),
        P("expert", None),
        P(None, "expert", "tensor"),
        P("tensor", "expert"),
        P("expert"),
        P("expert"),
        P(None, "tensor", "expert"),
        P("expert", None),
        P("expert", None, "tensor"),
        P("expert", None, "tensor"),
        P("expert", "tensor", None),
        P("expert", None),
        P(),
    )
    compact = (mesh.shape["expert"], mesh.shape["tensor"]) == (GROUPS, NX * NC)
    return jax.shard_map(
        fast_shards if compact else shards,
        mesh=mesh,
        in_specs=placed,
        out_specs=(
            P("expert", None),
            P("expert", None),
            P(None, "expert", "tensor"),
            P("tensor", "expert"),
            P("expert"),
            P("expert"),
            P(None, "tensor", "expert"),
            P("expert", None),
            P("expert", None, "tensor"),
            P("expert", None, "tensor"),
            P("expert", "tensor", None),
        ),
        check_vma=False,
    )
```

```python
import jax
import jax.numpy as jnp
from jax import lax
from jax.experimental import pallas as pl
from jax.experimental.pallas import tpu as pltpu
from jax.sharding import PartitionSpec as P

HEAD = 128
WINDOW = 1024
SEQ = 2048


EPS = 1e-05
THETA = 10000.0


def from_behind(value, axis, steps):
    count = lax.axis_size(axis)
    initial, last = (max(0, -steps), min(count, count - steps))
    return lax.ppermute(value, axis, [(source, source + steps) for source in range(initial, last)])


def angles(position, head_size):
    half_size = head_size // 2
    frequency = THETA ** (-(jnp.arange(half_size, dtype=jnp.float32) * 2.0 / head_size))
    phase_angle = position.astype(jnp.float32)[:, None] * frequency[None, :]
    return (jnp.cos(phase_angle)[:, None, :], jnp.sin(phase_angle)[:, None, :])


def rotate(rotated_in, cosine_table, sine_table):
    half_size = rotated_in.shape[-1] // 2
    first_half = rotated_in[..., :half_size]
    second_half = rotated_in[..., half_size:]
    return jnp.concatenate(
        [
            first_half * cosine_table - second_half * sine_table,
            second_half * cosine_table + first_half * sine_table,
        ],
        axis=-1,
    )


def slot_layout(block_routes, experts, capacity):
    flat_routes = block_routes.reshape(-1)
    onehot = (flat_routes[:, None] == jnp.arange(experts, dtype=jnp.int32)[None, :]).astype(
        jnp.int32
    )
    before = jnp.cumsum(onehot, axis=0) - onehot
    rank_within = jnp.sum(before * onehot, axis=1)
    slot_index = flat_routes * capacity + rank_within
    slot_table = (
        jnp.zeros((experts * capacity,), jnp.int32)
        .at[slot_index]
        .set(jnp.arange(flat_routes.shape[0], dtype=jnp.int32) + 1)
    )
    return (slot_index, slot_table)


def shards(
    tokens_in,
    out_grad,
    w_qkv,
    w_attn_out,
    attn_gain,
    ffn_gain,
    qk_gain,
    w_router,
    w_gate,
    w_up,
    w_down,
    routes,
    segments,
):
    row_count, model_width = tokens_in.shape
    experts = w_router.shape[1]
    per_token = routes.shape[1]
    local_experts = w_gate.shape[0]
    heads_here = qk_gain.shape[1]
    local_width = heads_here * HEAD
    groups = lax.axis_size("expert")
    device = lax.axis_index("expert")
    capacity = row_count * per_token * 3 // (2 * experts)
    hop_count = WINDOW // row_count
    buffer_shape = (groups, local_experts, capacity, model_width)
    score_scale = HEAD ** (-0.5)

    def fetch_weights():
        return (
            lax.all_gather(w_qkv.astype(jnp.bfloat16), "expert", axis=1, tiled=True),
            lax.all_gather(w_attn_out.astype(jnp.bfloat16), "expert", axis=1, tiled=True),
            lax.all_gather(w_router.astype(jnp.bfloat16), "expert", axis=0, tiled=True),
            lax.all_gather(attn_gain.astype(jnp.bfloat16), "expert", axis=0, tiled=True),
            lax.all_gather(ffn_gain.astype(jnp.bfloat16), "expert", axis=0, tiled=True),
            lax.all_gather(qk_gain.astype(jnp.bfloat16), "expert", axis=2, tiled=True),
        )

    def prepare(pieces):
        return (
            pieces[0],
            pieces[1],
            pieces[2],
            pieces[3].astype(jnp.float32),
            pieces[4].astype(jnp.float32),
            pieces[5].astype(jnp.float32).reshape(2, local_width),
        )

    qkv_low, out_low, router_low, gain_one_f, gain_two_f, qk_gains = prepare(fetch_weights())
    tokens_f = tokens_in.astype(jnp.float32)
    scale_one = lax.rsqrt(jnp.mean(tokens_f * tokens_f, axis=-1, keepdims=True) + EPS)
    hidden_one = (tokens_f * scale_one * gain_one_f).astype(jnp.bfloat16)
    projected = jnp.einsum("td,jde->jte", hidden_one, qkv_low, preferred_element_type=jnp.float32)
    query_raw = projected[0]
    key_raw = projected[1]
    query_sq, key_sq = lax.psum(
        (jnp.sum(query_raw * query_raw, axis=-1), jnp.sum(key_raw * key_raw, axis=-1)), "tensor"
    )
    query_scale = lax.rsqrt(query_sq / model_width + EPS)[:, None]
    key_scale = lax.rsqrt(key_sq / model_width + EPS)[:, None]
    normed_query = query_raw * query_scale
    normed_key = key_raw * key_scale
    global_rows = device * row_count + jnp.arange(row_count, dtype=jnp.int32)
    cosine_table, sine_table = angles(global_rows % SEQ, HEAD)
    query_low = rotate(
        (normed_query * qk_gains[0]).reshape(row_count, heads_here, HEAD), cosine_table, sine_table
    ).astype(jnp.bfloat16)
    key_low = rotate(
        (normed_key * qk_gains[1]).reshape(row_count, heads_here, HEAD), cosine_table, sine_table
    ).astype(jnp.bfloat16)
    value_low = projected[2].astype(jnp.bfloat16).reshape(row_count, heads_here, HEAD)
    own_pair = jnp.stack([key_low, value_low])
    earlier = []
    for steps_back in range(hop_count, 0, -1):
        earlier.append(from_behind(own_pair, "expert", steps_back))
    context = jnp.concatenate(earlier + [own_pair], axis=1)
    key_rows = (device - hop_count) * row_count + jnp.arange(
        (hop_count + 1) * row_count, dtype=jnp.int32
    )
    segment_keys = segments[jnp.maximum(key_rows, 0)]
    segment_query = segments[global_rows]
    distance = global_rows[:, None] - key_rows[None, :]
    allowed = (
        (key_rows[None, :] >= 0)
        & (segment_query[:, None] == segment_keys[None, :])
        & (distance >= 0)
        & (distance < WINDOW)
    )

    def score_block():
        raw_scores = (
            jnp.einsum("qhd,khd->hqk", query_low, context[0], preferred_element_type=jnp.float32)
            * score_scale
        )
        return jnp.where(allowed[None], raw_scores, -1e30)

    scores = score_block()
    largest = jnp.max(scores, axis=-1, keepdims=True)
    exp_scores = jnp.exp(scores - largest)
    exp_total = jnp.sum(exp_scores, axis=-1, keepdims=True)
    log_total = largest + jnp.log(exp_total)
    attn_probs = (exp_scores / exp_total).astype(jnp.bfloat16)
    attended = (
        jnp.einsum("hqk,khd->qhd", attn_probs, context[1], preferred_element_type=jnp.float32)
        .reshape(row_count, local_width)
        .astype(jnp.bfloat16)
    )
    attention_out = lax.psum(
        jnp.dot(attended, out_low, preferred_element_type=jnp.float32).astype(jnp.bfloat16),
        "tensor",
    ).astype(jnp.float32)
    residual = tokens_f + attention_out
    scale_two = lax.rsqrt(jnp.mean(residual * residual, axis=-1, keepdims=True) + EPS)
    normed_two = residual * scale_two
    hidden_two = (normed_two * gain_two_f).astype(jnp.bfloat16)
    logits = jnp.dot(hidden_two, router_low, preferred_element_type=jnp.float32)
    logit_exp = jnp.exp(logits - jnp.max(logits, axis=-1, keepdims=True))
    router_probs = logit_exp / jnp.sum(logit_exp, axis=-1, keepdims=True)
    chosen = routes[:, :, None] == jnp.arange(experts, dtype=jnp.int32)[None, None, :]
    gate_probs = jnp.sum(jnp.where(chosen, router_probs[:, None, :], 0.0), axis=-1)
    slot_index, slot_table = slot_layout(routes, experts, capacity)
    present = (slot_table > 0)[:, None]
    assigned = jnp.maximum(slot_table - 1, 0)
    row_of_slot = assigned // per_token
    gate_low = w_gate.astype(jnp.bfloat16)
    up_low = w_up.astype(jnp.bfloat16)
    down_low = w_down.astype(jnp.bfloat16)

    def send_rows():
        buffer_rows = jnp.where(
            present, hidden_two[row_of_slot], jnp.zeros((), jnp.bfloat16)
        ).reshape(buffer_shape)
        return lax.all_to_all(buffer_rows, "expert", split_axis=0, concat_axis=0, tiled=True)

    def expert_front(arrived):
        gate_pre = jnp.einsum(
            "secd,edh->sech", arrived, gate_low, preferred_element_type=jnp.float32
        )
        up_pre = jnp.einsum("secd,edh->sech", arrived, up_low, preferred_element_type=jnp.float32)
        return (gate_pre, up_pre)

    received = send_rows()
    gate_pre, up_pre = expert_front(received)
    activated = (gate_pre * jax.nn.sigmoid(gate_pre) * up_pre).astype(jnp.bfloat16)
    partial_value = jnp.einsum(
        "sech,ehd->secd", activated, down_low, preferred_element_type=jnp.float32
    ).astype(jnp.bfloat16)
    returned = lax.all_to_all(
        partial_value, "expert", split_axis=0, concat_axis=0, tiled=True
    ).reshape(experts * capacity, model_width)
    expert_rows = returned[slot_index].reshape(row_count, per_token, model_width)
    expert_part = jnp.einsum(
        "tk,tkd->td", gate_probs, expert_rows, preferred_element_type=jnp.float32
    )
    block_out = residual + lax.psum(expert_part.astype(jnp.bfloat16), "tensor").astype(jnp.float32)
    qkv_low, out_low, router_low, gain_one_f, gain_two_f, qk_gains = prepare(fetch_weights())
    grad_out = out_grad.astype(jnp.float32)
    grad_gate_part = jnp.einsum(
        "td,tkd->tk", grad_out, expert_rows, preferred_element_type=jnp.float32
    )
    slot_grads = (
        (gate_probs[:, :, None] * grad_out[:, None, :])
        .astype(jnp.bfloat16)
        .reshape(row_count * per_token, model_width)
    )
    grad_buffer = jnp.where(present, slot_grads[assigned], jnp.zeros((), jnp.bfloat16)).reshape(
        buffer_shape
    )
    grad_received = lax.all_to_all(grad_buffer, "expert", split_axis=0, concat_axis=0, tiled=True)
    received = send_rows()
    gate_pre, up_pre = expert_front(received)
    sigmoid_gate = jax.nn.sigmoid(gate_pre)
    swish_gate = gate_pre * sigmoid_gate
    activated = (swish_gate * up_pre).astype(jnp.bfloat16)
    grad_act = jnp.einsum(
        "secd,ehd->sech", grad_received, down_low, preferred_element_type=jnp.float32
    )
    grad_down = jnp.einsum(
        "sech,secd->ehd", activated, grad_received, preferred_element_type=jnp.float32
    )
    grad_gate_pre = (
        grad_act * up_pre * sigmoid_gate * (1.0 + gate_pre * (1.0 - sigmoid_gate))
    ).astype(jnp.bfloat16)
    grad_up_pre = (grad_act * swish_gate).astype(jnp.bfloat16)
    grad_gate_w = jnp.einsum(
        "secd,sech->edh", received, grad_gate_pre, preferred_element_type=jnp.float32
    )
    grad_up_w = jnp.einsum(
        "secd,sech->edh", received, grad_up_pre, preferred_element_type=jnp.float32
    )
    grad_rows = (
        jnp.einsum("sech,edh->secd", grad_gate_pre, gate_low, preferred_element_type=jnp.float32)
        + jnp.einsum("sech,edh->secd", grad_up_pre, up_low, preferred_element_type=jnp.float32)
    ).astype(jnp.bfloat16)
    grad_back = lax.all_to_all(
        grad_rows, "expert", split_axis=0, concat_axis=0, tiled=True
    ).reshape(experts * capacity, model_width)
    grad_hidden_part = jnp.sum(
        grad_back[slot_index].reshape(row_count, per_token, model_width), axis=1, dtype=jnp.float32
    )
    grad_hidden_sum, grad_gates = (
        lax.psum(grad_hidden_part.astype(jnp.bfloat16), "tensor").astype(jnp.float32),
        lax.psum(grad_gate_part.astype(jnp.bfloat16), "tensor").astype(jnp.float32),
    )
    grad_probs = jnp.sum(jnp.where(chosen, grad_gates[:, :, None], 0.0), axis=1)
    grad_logits = (
        router_probs * (grad_probs - jnp.sum(router_probs * grad_probs, axis=-1, keepdims=True))
    ).astype(jnp.bfloat16)
    grad_hidden_two = grad_hidden_sum + jnp.dot(
        grad_logits, router_low.T, preferred_element_type=jnp.float32
    )
    grad_router = jnp.dot(hidden_two.T, grad_logits, preferred_element_type=jnp.float32)
    grad_gain_two = jnp.sum(grad_hidden_two * normed_two, axis=0)
    scaled_two = grad_hidden_two * gain_two_f
    grad_residual = (
        grad_out
        + scale_two * scaled_two
        - residual
        * (scale_two * scale_two * scale_two)
        * jnp.mean(scaled_two * residual, axis=-1, keepdims=True)
    )
    grad_attn = grad_residual.astype(jnp.bfloat16)
    grad_out_w = jnp.dot(attended.T, grad_attn, preferred_element_type=jnp.float32)
    grad_attended = (
        jnp.dot(grad_attn, out_low.T, preferred_element_type=jnp.float32)
        .astype(jnp.bfloat16)
        .reshape(row_count, heads_here, HEAD)
    )
    attn_weights = jnp.where(allowed[None], jnp.exp(score_block() - log_total), 0.0)
    grad_weights = jnp.einsum(
        "qhd,khd->hqk", grad_attended, context[1], preferred_element_type=jnp.float32
    )
    inner_sum = jnp.sum(attn_weights * grad_weights, axis=-1, keepdims=True)
    grad_scores = (attn_weights * (grad_weights - inner_sum) * score_scale).astype(jnp.bfloat16)
    grad_query = jnp.einsum(
        "hqk,khd->qhd", grad_scores, context[0], preferred_element_type=jnp.float32
    )
    grad_keys = jnp.einsum(
        "hqk,qhd->khd", grad_scores, query_low, preferred_element_type=jnp.float32
    )
    grad_values = jnp.einsum(
        "hqk,qhd->khd",
        attn_weights.astype(jnp.bfloat16),
        grad_attended,
        preferred_element_type=jnp.float32,
    )
    grad_pair = jnp.stack([grad_keys, grad_values]).reshape(
        2, hop_count + 1, row_count, heads_here, HEAD
    )
    own_grad = grad_pair[:, hop_count]
    for steps_back in range(1, hop_count + 1):
        own_grad = own_grad + from_behind(
            grad_pair[:, hop_count - steps_back].astype(jnp.bfloat16), "expert", -steps_back
        ).astype(jnp.float32)
    grad_query_norm = rotate(grad_query, cosine_table, -sine_table).reshape(row_count, local_width)
    grad_key_norm = rotate(own_grad[0], cosine_table, -sine_table).reshape(row_count, local_width)
    grad_gain_query = jnp.sum(grad_query_norm * normed_query, axis=0)
    grad_gain_key = jnp.sum(grad_key_norm * normed_key, axis=0)
    scaled_query = grad_query_norm * qk_gains[0]
    scaled_key = grad_key_norm * qk_gains[1]
    query_inner, key_inner = lax.psum(
        (jnp.sum(scaled_query * query_raw, axis=-1), jnp.sum(scaled_key * key_raw, axis=-1)),
        "tensor",
    )
    grad_query_raw = (
        query_scale * scaled_query
        - query_raw * (query_scale * query_scale * query_scale) * query_inner[:, None] / model_width
    ).astype(jnp.bfloat16)
    grad_key_raw = (
        key_scale * scaled_key
        - key_raw * (key_scale * key_scale * key_scale) * key_inner[:, None] / model_width
    ).astype(jnp.bfloat16)
    grad_value_raw = own_grad[1].reshape(row_count, local_width).astype(jnp.bfloat16)
    grad_proj = jnp.stack([grad_query_raw, grad_key_raw, grad_value_raw])
    grad_qkv = jnp.einsum("td,jte->jde", hidden_one, grad_proj, preferred_element_type=jnp.float32)
    grad_hidden_one = lax.psum(
        jnp.einsum("jte,jde->td", grad_proj, qkv_low, preferred_element_type=jnp.float32).astype(
            jnp.bfloat16
        ),
        "tensor",
    ).astype(jnp.float32)
    grad_gain_one = jnp.sum(grad_hidden_one * tokens_f * scale_one, axis=0)
    scaled_one = grad_hidden_one * gain_one_f
    grad_tokens = (
        grad_residual
        + scale_one * scaled_one
        - tokens_f
        * (scale_one * scale_one * scale_one)
        * jnp.mean(scaled_one * tokens_f, axis=-1, keepdims=True)
    )
    grad_qk = jnp.stack([grad_gain_query, grad_gain_key]).reshape(2, heads_here, HEAD)
    reduced = (
        lax.psum_scatter(
            grad_qkv.astype(jnp.bfloat16), "expert", scatter_dimension=1, tiled=True
        ).astype(jnp.float32),
        lax.psum_scatter(
            grad_out_w.astype(jnp.bfloat16), "expert", scatter_dimension=1, tiled=True
        ).astype(jnp.float32),
        lax.psum_scatter(
            grad_router.astype(jnp.bfloat16), "expert", scatter_dimension=0, tiled=True
        ).astype(jnp.float32),
        lax.psum_scatter(
            grad_gain_one.astype(jnp.bfloat16), "expert", scatter_dimension=0, tiled=True
        ).astype(jnp.float32),
        lax.psum_scatter(
            grad_gain_two.astype(jnp.bfloat16), "expert", scatter_dimension=0, tiled=True
        ).astype(jnp.float32),
        lax.psum_scatter(
            grad_qk.astype(jnp.bfloat16), "expert", scatter_dimension=2, tiled=True
        ).astype(jnp.float32),
    )
    return (
        block_out.astype(jnp.bfloat16),
        grad_tokens.astype(jnp.bfloat16),
        reduced[0],
        reduced[1],
        reduced[3],
        reduced[4],
        reduced[5],
        reduced[2],
        grad_gate_w,
        grad_up_w,
        grad_down,
    )


MESH_ID = pl.DeviceIdType.MESH
HBM = pl.BlockSpec(memory_space=pltpu.HBM)
VMEM = pl.BlockSpec(memory_space=pltpu.VMEM)
NZ, NY, NX, NC = 4, 2, 2, 2
GROUPS = NZ * NY


def place():
    e = lax.axis_index("expert")
    t = lax.axis_index("tensor")
    return lax.div(e, NY), lax.rem(e, NY), lax.div(t, NC), lax.rem(t, NC)


def device(z, y, x, c):
    return (z * NY + y, x * NC + c)


def run_if(condition, body):
    if condition is None:
        body()
    else:
        pl.when(condition)(body)


def greet(partners):
    barrier = pltpu.get_barrier_semaphore()
    for target, condition in partners:
        run_if(
            condition,
            lambda target=target: pl.semaphore_signal(
                barrier, inc=1, device_id=target, device_id_type=MESH_ID
            ),
        )
    count = sum(1 for _, condition in partners if condition is None)
    for _, condition in partners:
        if condition is not None:
            count = count + condition.astype(jnp.int32)
    pl.semaphore_wait(barrier, count)


def remote(source, target_ref, send_sem, recv_sem, target):
    return pltpu.make_async_remote_copy(
        src_ref=source,
        dst_ref=target_ref,
        send_sem=send_sem,
        recv_sem=recv_sem,
        device_id=target,
        device_id_type=MESH_ID,
    )


def block_rows(block, rows):
    return pl.ds(pl.multiple_of(block * rows, rows), rows)


class LineGather:
    def __init__(self, streams, sources, views, send_sem, recv_sem, y_first=()):
        self.z, self.y, self.x, self.c = place()
        self.streams, self.sources, self.views = streams, sources, views
        self.send_sem, self.recv_sem = send_sem, recv_sem
        self.y_first = y_first
        self.has_up, self.has_down = self.z < NZ - 1, self.z > 0
        self.pending = []

    def partners(self):
        z, y, x, c = self.z, self.y, self.x, self.c
        return [
            (device(z + 1, y, x, c), z < NZ - 1),
            (device(z - 1, y, x, c), z > 0),
            (device(z, 1 - y, x, c), None),
        ]

    def exists(self, rel):
        rel = rel % 7
        if rel == 0:
            return None
        return self.z >= rel if rel < 4 else self.z + (rel - 3) < NZ

    def block(self, rel):
        y = self.y if rel < 7 else 1 - self.y
        rel = rel % 7
        z = self.z if rel == 0 else (self.z - rel if rel < 4 else self.z + (rel - 3))
        return z * NY + y

    def send(self, stream, rel, way):
        z, y, x, c = self.z, self.y, self.x, self.c
        block = self.block(rel)
        there = self.views[stream](block)
        source = self.sources[stream] if rel == 0 else there
        near = rel % 7 == 0
        if way == 0:
            target, landing = device(z + 1, y, x, c), rel + 1
        elif way == 1:
            target, landing = device(z - 1, y, x, c), rel + (4 if near else 1)
        else:
            target, landing = device(z, 1 - y, x, c), 7 + rel
        return remote(
            source,
            there,
            self.send_sem.at[stream, rel, way],
            self.recv_sem.at[stream, landing],
            target,
        )

    def forwards(self, stream, rel):
        return rel < 7 or stream in self.y_first

    def start(self, stream, rel):
        if rel % 7 < 4:
            run = self.has_up
            run_if(run, lambda: self.send(stream, rel, 0).start())
            self.pending.append((stream, rel, 0, run))
        if rel % 7 == 0 or rel % 7 >= 4:
            run = self.has_down
            run_if(run, lambda: self.send(stream, rel, 1).start())
            self.pending.append((stream, rel, 1, run))
        if rel == 0 or stream not in self.y_first:
            self.send(stream, rel, 2).start()
            self.pending.append((stream, rel, 2, None))

    def arrive(self, stream, rel):
        there = self.views[stream](self.block(rel))
        remote(
            there,
            there,
            self.send_sem.at[stream, 0, 0],
            self.recv_sem.at[stream, rel],
            device(self.z, 1 - self.y, self.x, self.c),
        ).wait_recv()

    def order(self):
        return [7, 1, 4, 8, 11, 2, 5, 9, 12, 3, 6, 10, 13]

    def run(self, hook=None):
        for stream in self.streams:
            self.start(stream, 0)
        for rel in self.order():
            def step(rel=rel):
                marks = len(self.pending)
                for stream in self.streams:
                    self.arrive(stream, rel)
                    if rel < 7:
                        self.start(stream, rel)
                    if hook is not None:
                        hook(stream, rel)
                if rel < 7:
                    late = self.pending[marks:]
                    del self.pending[marks:]
                    self.finish_later(late, rel)
            run_if(self.exists(rel), step)

    def finish_later(self, late, rel):
        self.late = getattr(self, "late", []) + [(rel, late)]

    def finish(self):
        for stream, rel, way, run in self.pending:
            run_if(run, lambda s=stream, r=rel, w=way: self.send(s, r, w).wait_send())
        for rel, late in getattr(self, "late", []):
            def body(late=late):
                for stream, rel, way, run in late:
                    run_if(run, lambda s=stream, r=rel, w=way: self.send(s, r, w).wait_send())
            run_if(self.exists(rel), body)


def cost(microseconds):
    return pl.CostEstimate(flops=0, bytes_accessed=int(microseconds * 3.0e6), transcendentals=0)


def comm_params(collective_id, megabytes=56):
    return pltpu.CompilerParams(
        collective_id=collective_id,
        has_side_effects=True,
        vmem_limit_bytes=megabytes * 1024 * 1024,
    )


def weight_gather(qkv_low, out_low, smalls, collective_id):
    parts, rows, width = qkv_low.shape
    depth, columns = out_low.shape

    def kernel(qkv, out, small, qkv_all, out_all, small_all, send_sem, recv_sem, local_sem):
        views = [
            lambda b: qkv_all.at[:, block_rows(b, rows), :],
            lambda b: out_all.at[:, block_rows(b, columns)],
            lambda b: small_all.at[b],
        ]
        line = LineGather([2, 0, 1], [qkv, out, small], views, send_sem, recv_sem)
        greet(line.partners())
        own = line.block(0)
        keep = [
            pltpu.make_async_copy(source, view(own), local_sem.at[i])
            for i, (source, view) in enumerate(zip([qkv, out, small], views))
        ]
        for copy in keep:
            copy.start()
        line.run()
        line.finish()
        for copy in keep:
            copy.wait()

    return pl.pallas_call(
        kernel,
        out_shape=(
            jax.ShapeDtypeStruct((parts, rows * GROUPS, width), jnp.bfloat16),
            jax.ShapeDtypeStruct((depth, columns * GROUPS), jnp.bfloat16),
            jax.ShapeDtypeStruct((GROUPS,) + smalls.shape, jnp.float32),
        ),
        in_specs=[HBM] * 3,
        out_specs=(HBM, HBM, HBM),
        scratch_shapes=[
            pltpu.SemaphoreType.DMA((3, 14, 3)),
            pltpu.SemaphoreType.DMA((3, 14)),
            pltpu.SemaphoreType.DMA((3,)),
        ],
        compiler_params=comm_params(collective_id),
        cost_estimate=cost(100),
        name="weight_gather",
    )(qkv_low, out_low, smalls)


def token_gather(block, collective_id):
    rows, width = block.shape
    a_cols, c_cols = width * 3 // 16, width // 8

    def kernel(own_ref, all_ref, send_sem, recv_sem, x_send, x_recv, core_send, core_recv, local_sem):
        z, y, x, c = place()

        def a_at(xx, cc):
            return pl.ds(pl.multiple_of(xx * (2 * a_cols) + cc * a_cols, 128), a_cols)

        def c_at(cc):
            return pl.ds(pl.multiple_of(4 * a_cols + cc * c_cols, 128), c_cols)

        def view(b, columns):
            return all_ref.at[block_rows(b, rows), columns]

        sources = [own_ref.at[:, a_at(x, c)], own_ref.at[:, c_at(c)]]
        views = [lambda b: view(b, a_at(x, c)), lambda b: view(b, c_at(c))]
        line = LineGather([0, 1], sources, views, send_sem, recv_sem)
        across, twin = device(z, y, 1 - x, c), device(z, y, x, 1 - c)
        greet(line.partners() + [(across, None), (twin, None)])
        keep = pltpu.make_async_copy(own_ref, all_ref.at[block_rows(line.block(0), rows), :], local_sem)
        keep.start()

        def to_twin(rel, stream, landing=False):
            b = line.block(rel)
            columns = [a_at(x, c), c_at(c), a_at(1 - x, c)][stream]
            other = [a_at(x, 1 - c), c_at(1 - c), a_at(1 - x, 1 - c)][stream]
            piece = view(b, other if landing else columns)
            return remote(piece, piece, core_send.at[rel, stream], core_recv.at[rel, stream], twin)

        def to_across(rel, landing=False):
            b = line.block(rel)
            piece = view(b, a_at(1 - x if landing else x, c))
            return remote(piece, piece, x_send.at[rel], x_recv.at[rel], across)

        def hook(stream, rel):
            if stream == 0:
                to_across(rel).start()
            to_twin(rel, stream).start()

        line.run(hook)
        for rel in line.order():
            def relay(rel=rel):
                to_across(rel, True).wait_recv()
                to_twin(rel, 2).start()
            run_if(line.exists(rel), relay)
        for rel in line.order():
            def end(rel=rel):
                to_across(rel).wait_send()
                for stream in range(3):
                    to_twin(rel, stream, True).wait_recv()
                    to_twin(rel, stream).wait_send()
            run_if(line.exists(rel), end)
        line.finish()
        keep.wait()

    return pl.pallas_call(
        kernel,
        out_shape=jax.ShapeDtypeStruct((rows * GROUPS, width), block.dtype),
        in_specs=[HBM],
        out_specs=HBM,
        scratch_shapes=[
            pltpu.SemaphoreType.DMA((2, 14, 3)),
            pltpu.SemaphoreType.DMA((2, 14)),
            pltpu.SemaphoreType.DMA((14,)),
            pltpu.SemaphoreType.DMA((14,)),
            pltpu.SemaphoreType.DMA((14, 3)),
            pltpu.SemaphoreType.DMA((14, 3)),
            pltpu.SemaphoreType.DMA,
        ],
        compiler_params=comm_params(collective_id),
        cost_estimate=cost(45),
        name="token_gather",
    )(block)


def add_into(rows, step, store):
    def body(i, carry):
        store(pl.ds(pl.multiple_of(i * step, step), step))
        return carry

    lax.fori_loop(0, rows // step, body, 0)


def group_stages(part_ref, out_ref, core_buf, x_buf, send_sem, recv_sem):
    rows, width = part_ref.shape
    half, quarter = width // 2, width // 4
    z, y, x, c = place()
    across, twin = device(z, y, 1 - x, c), device(z, y, x, 1 - c)

    def half_of(cc):
        return pl.ds(pl.multiple_of(cc * half, half), half)

    def quarter_of(xx, cc):
        return pl.ds(pl.multiple_of(cc * half + xx * quarter, quarter), quarter)

    own, from_x = out_ref.at[:, quarter_of(x, c)], out_ref.at[:, quarter_of(1 - x, c)]
    to_x = core_buf.at[:, pl.ds(pl.multiple_of((1 - x) * quarter, quarter), quarter)]
    sources = [part_ref.at[:, half_of(1 - c)], to_x, own, own, from_x]
    landings = [core_buf, x_buf, own, own, from_x]
    targets = [twin, across, across, twin, twin]

    def copy(k):
        return remote(sources[k], landings[k], send_sem.at[k], recv_sem.at[k], targets[k])

    def arrive(k, landing):
        remote(landing, landing, send_sem.at[k], recv_sem.at[k], targets[k]).wait_recv()

    def begin():
        copy(0).start()

    def core_step():
        copy(0).wait_recv()
        add_to(core_buf, core_buf, part_ref.at[:, half_of(c)], 32)
        copy(1).start()

    def x_step():
        copy(1).wait_recv()
        add_to(own, x_buf, core_buf.at[:, pl.ds(pl.multiple_of(x * quarter, quarter), quarter)], 32)
        copy(2).start()
        copy(3).start()

    def spread():
        arrive(2, from_x)
        copy(4).start()

    def end():
        arrive(3, out_ref.at[:, quarter_of(x, 1 - c)])
        arrive(4, out_ref.at[:, quarter_of(1 - x, 1 - c)])
        for k in range(5):
            copy(k).wait_send()

    return [begin, core_step, x_step, spread, end]


def group_sum(part_ref, out_ref, core_buf, x_buf, send_sem, recv_sem, meanwhile=None):
    stages = group_stages(part_ref, out_ref, core_buf, x_buf, send_sem, recv_sem)
    stages[0]()
    if meanwhile is not None:
        meanwhile()
    for stage in stages[1:]:
        stage()


def tensor_sum(part, collective_id):
    rows, width = part.shape

    def kernel(part_ref, out_ref, core_buf, x_buf, send_sem, recv_sem):
        z, y, x, c = place()
        greet([(device(z, y, 1 - x, c), None), (device(z, y, x, 1 - c), None)])
        group_sum(part_ref, out_ref, core_buf, x_buf, send_sem, recv_sem)

    return pl.pallas_call(
        kernel,
        out_shape=jax.ShapeDtypeStruct((rows, width), jnp.bfloat16),
        in_specs=[VMEM],
        out_specs=VMEM,
        scratch_shapes=[
            pltpu.VMEM((rows, width // 2), jnp.bfloat16),
            pltpu.VMEM((rows, width // 4), jnp.bfloat16),
            pltpu.SemaphoreType.DMA((5,)),
            pltpu.SemaphoreType.DMA((5,)),
        ],
        compiler_params=comm_params(collective_id, 16),
        cost_estimate=cost(17),
        name="tensor_sum",
    )(part)


Z_ORDER = (3, 0, 2, 1)


def accumulate(into, addend, step=64):
    rows = into.shape[0]
    step = min(step, rows)

    def body(i, carry):
        r = pl.ds(pl.multiple_of(i * step, step), step)
        total = into[r, :].astype(jnp.float32) + addend[r, :].astype(jnp.float32)
        into[r, :] = total.astype(into.dtype)
        return carry

    lax.fori_loop(0, rows // step, body, 0)


class LineReduce:
    def __init__(self, streams, own, y_buf, lo_buf, hi_buf, send_sem, recv_sem):
        self.z, self.y, self.x, self.c = place()
        self.streams = streams
        self.own, self.y_buf, self.lo_buf, self.hi_buf = own, y_buf, lo_buf, hi_buf
        self.send_sem, self.recv_sem = send_sem, recv_sem

    def partners(self):
        z, y, x, c = self.z, self.y, self.x, self.c
        return [
            (device(z + 1, y, x, c), z < NZ - 1),
            (device(z - 1, y, x, c), z > 0),
            (device(z, 1 - y, x, c), None),
        ]

    def copy(self, s, zz, way):
        z, y, x, c = self.z, self.y, self.x, self.c
        if way == 0:
            source, landing, target = self.own(s, zz, 1 - y), self.y_buf, device(z, 1 - y, x, c)
        elif way == 1:
            source, landing, target = self.y_buf(s, zz), self.lo_buf, device(z + 1, y, x, c)
        else:
            source, landing, target = self.y_buf(s, zz), self.hi_buf, device(z - 1, y, x, c)
        return remote(
            source, landing(s, zz), self.send_sem.at[s, zz, way], self.recv_sem.at[s, zz, way], target
        )

    def to_y(self, s, zz):
        self.copy(s, zz, 0).start()

    def take(self, s, zz, way):
        self.copy(s, zz, way).wait_recv()
        accumulate(self.y_buf(s, zz), (self.lo_buf if way == 1 else self.hi_buf)(s, zz))

    def along_z(self, s, zz):
        z = self.z
        self.copy(s, zz, 0).wait_recv()
        accumulate(self.y_buf(s, zz), self.own(s, zz, self.y))

        def upward():
            run_if(z > 0, lambda: self.take(s, zz, 1))
            self.copy(s, zz, 1).start()

        def downward():
            run_if(z < NZ - 1, lambda: self.take(s, zz, 2))
            self.copy(s, zz, 2).start()

        run_if(z < zz, upward)
        run_if(z > zz, downward)

    def home(self, done):
        for zz in range(NZ):
            def land(zz=zz):
                for s in self.streams:
                    if zz > 0:
                        self.take(s, zz, 1)
                    if zz < NZ - 1:
                        self.take(s, zz, 2)
                    done(s, self.y_buf(s, zz))
            run_if(self.z == zz, land)

    def finish(self):
        for zz in range(NZ):
            for s in self.streams:
                self.copy(s, zz, 0).wait_send()
                run_if(self.z < zz, lambda s=s, zz=zz: self.copy(s, zz, 1).wait_send())
                run_if(self.z > zz, lambda s=s, zz=zz: self.copy(s, zz, 2).wait_send())


def weight_reduce(qkv, out, smalls, collective_id):
    parts, depth, width = qkv.shape
    rows = depth // GROUPS
    out_rows, columns = out.shape[0], out.shape[1] // GROUPS

    def kernel(qkv_ref, out_ref, small_ref, qkv_sum, out_sum, small_sum,
               qkv_buf, out_buf, small_buf, send_sem, recv_sem):
        def own(s, zz, yy):
            b = zz * NY + yy
            if s < parts:
                return qkv_ref.at[s, block_rows(b, rows), :]
            if s == parts:
                return out_ref.at[:, block_rows(b, columns)]
            return small_ref.at[b]

        def slot(kind):
            def view(s, zz):
                if s < parts:
                    return qkv_buf.at[kind, zz, s]
                if s == parts:
                    return out_buf.at[kind, zz]
                return small_buf.at[kind, zz]
            return view

        streams = list(range(parts + 2))
        line = LineReduce(streams, own, slot(0), slot(1), slot(2), send_sem, recv_sem)
        greet(line.partners())
        work = [(s, zz) for s in [parts + 1, parts] + list(range(parts)) for zz in Z_ORDER]
        for s, zz in work:
            line.to_y(s, zz)
        for s, zz in work:
            line.along_z(s, zz)

        def done(s, total):
            target = qkv_sum.at[s] if s < parts else (out_sum if s == parts else small_sum)
            step = min(64, target.shape[0])

            def body(i, carry):
                r = pl.ds(pl.multiple_of(i * step, step), step)
                target[r, :] = total[r, :].astype(jnp.float32)
                return carry

            lax.fori_loop(0, target.shape[0] // step, body, 0)

        line.home(done)
        line.finish()

    return pl.pallas_call(
        kernel,
        out_shape=(
            jax.ShapeDtypeStruct((parts, rows, width), jnp.float32),
            jax.ShapeDtypeStruct((out_rows, columns), jnp.float32),
            jax.ShapeDtypeStruct(smalls.shape[1:], jnp.float32),
        ),
        in_specs=[VMEM] * 3,
        out_specs=(VMEM,) * 3,
        scratch_shapes=[
            pltpu.VMEM((3, NZ, parts, rows, width), jnp.bfloat16),
            pltpu.VMEM((3, NZ, out_rows, columns), jnp.bfloat16),
            pltpu.VMEM((3, NZ) + smalls.shape[1:], jnp.float32),
            pltpu.SemaphoreType.DMA((parts + 2, NZ, 3)),
            pltpu.SemaphoreType.DMA((parts + 2, NZ, 3)),
        ],
        compiler_params=comm_params(collective_id),
        cost_estimate=cost(120),
        name="weight_reduce",
    )(qkv, out, smalls)


def token_reduce(part, collective_id, pairs=None):
    tokens, width = part.shape
    rows = tokens // GROUPS
    half, quarter = width // 2, width // 4

    def kernel(part_ref, out_ref, core_buf, x_buf, y_buf, lo_buf, hi_buf,
               core_send, core_recv, x_send, x_recv, send_sem, recv_sem):
        z, y, x, c = place()
        across, twin = device(z, y, 1 - x, c), device(z, y, x, 1 - c)

        line = LineReduce(
            [0], lambda s, zz, yy: x_buf.at[zz * NY + yy], lambda s, zz: y_buf.at[zz],
            lambda s, zz: lo_buf.at[zz], lambda s, zz: hi_buf.at[zz], send_sem, recv_sem,
        )
        greet(line.partners() + [(across, None), (twin, None)])
        order = [(zz, flip) for zz in Z_ORDER for flip in (1, 0)]

        def number(zz, flip):
            return zz * NY + (1 - y if flip else y)

        def to_twin(zz, flip):
            b = number(zz, flip)
            return remote(
                part_ref.at[block_rows(b, rows), pl.ds(pl.multiple_of((1 - c) * half, half), half)],
                core_buf.at[b], core_send.at[zz, flip], core_recv.at[zz, flip], twin,
            )

        def to_across(zz, flip):
            b = number(zz, flip)
            return remote(
                core_buf.at[b, :, pl.ds(pl.multiple_of((1 - x) * quarter, quarter), quarter)],
                x_buf.at[b], x_send.at[zz, flip], x_recv.at[zz, flip], across,
            )

        def add_core(zz, flip):
            b = number(zz, flip)

            def store(r):
                at = pl.ds(pl.multiple_of(b * rows + r.start, 16), r.size)
                core_buf[b, r, :] = (
                    core_buf[b, r, :].astype(jnp.float32)
                    + part_ref[at, pl.ds(pl.multiple_of(c * half, half), half)].astype(jnp.float32)
                ).astype(jnp.bfloat16)

            add_into(rows, 32, store)

        def add_across(zz, flip):
            b = number(zz, flip)

            def store(r):
                x_buf[b, r, :] = (
                    x_buf[b, r, :].astype(jnp.float32)
                    + core_buf[b, r, pl.ds(pl.multiple_of(x * quarter, quarter), quarter)].astype(jnp.float32)
                ).astype(jnp.bfloat16)

            add_into(rows, 64, store)

        def stage_twin(i):
            to_twin(*order[i]).wait_recv()
            add_core(*order[i])
            to_across(*order[i]).start()

        def stage_across(i):
            zz, flip = order[i]
            to_across(zz, flip).wait_recv()
            add_across(zz, flip)
            if flip:
                line.to_y(0, zz)

        def stage_y(zz):
            line.along_z(0, zz)

        for zz, flip in order:
            to_twin(zz, flip).start()
        count = len(order)
        for i in range(count + 4):
            if i < count:
                stage_twin(i)
            if 0 <= i - 1 < count:
                stage_across(i - 1)
            if i >= 3 and (i - 3) % 2 == 0 and (i - 3) // 2 < NZ:
                stage_y(Z_ORDER[(i - 3) // 2])

        def done(s, total):
            def store(r):
                out_ref[r, :] = total[r, :]

            add_into(rows, 64, store)

        line.home(done)
        for zz, flip in order:
            to_twin(zz, flip).wait_send()
            to_across(zz, flip).wait_send()
        line.finish()

    return pl.pallas_call(
        kernel,
        out_shape=jax.ShapeDtypeStruct((rows, quarter), jnp.bfloat16),
        in_specs=[VMEM],
        out_specs=VMEM,
        scratch_shapes=[
            pltpu.VMEM((GROUPS, rows, half), jnp.bfloat16),
            pltpu.VMEM((GROUPS, rows, quarter), jnp.bfloat16),
            pltpu.VMEM((NZ, rows, quarter), jnp.bfloat16),
            pltpu.VMEM((NZ, rows, quarter), jnp.bfloat16),
            pltpu.VMEM((NZ, rows, quarter), jnp.bfloat16),
            pltpu.SemaphoreType.DMA((NZ, 2)),
            pltpu.SemaphoreType.DMA((NZ, 2)),
            pltpu.SemaphoreType.DMA((NZ, 2)),
            pltpu.SemaphoreType.DMA((NZ, 2)),
            pltpu.SemaphoreType.DMA((1, NZ, 3)),
            pltpu.SemaphoreType.DMA((1, NZ, 3)),
        ],
        compiler_params=comm_params(collective_id),
        cost_estimate=cost(60),
        name="token_reduce",
    )(part)


def gate_exchange(part, collective_id):
    groups = part.shape[0]
    tensors = NX * NC

    def kernel(part_ref, out_ref, landing, total, send_t, recv_t, send_e, recv_e):
        e = lax.axis_index("expert")
        t = lax.axis_index("tensor")
        mates = [(e, lax.rem(t + k, tensors)) for k in range(1, tensors)]
        peers = [(lax.rem(e + k, groups), t) for k in range(1, groups)]
        greet([(target, None) for target in mates + peers])
        near = [
            remote(part_ref, landing.at[k], send_t.at[k], recv_t.at[k], mates[k])
            for k in range(tensors - 1)
        ]
        for copy in near:
            copy.start()
        for copy in near:
            copy.wait_recv()
        value = part_ref[...]
        for k in range(tensors - 1):
            value = value + landing[k]
        total[...] = value
        far = [
            remote(
                total.at[lax.rem(e + k, groups)], out_ref.at[e], send_e.at[k - 1], recv_e.at[k - 1],
                peers[k - 1],
            )
            for k in range(1, groups)
        ]
        for copy in far:
            copy.start()
        out_ref[e] = total[e]
        for k in range(1, groups):
            source = out_ref.at[lax.rem(e + groups - k, groups)]
            remote(source, source, send_e.at[k - 1], recv_e.at[k - 1], peers[k - 1]).wait_recv()
        for copy in near + far:
            copy.wait_send()

    return pl.pallas_call(
        kernel,
        out_shape=jax.ShapeDtypeStruct(part.shape, jnp.float32),
        in_specs=[VMEM],
        out_specs=VMEM,
        scratch_shapes=[
            pltpu.VMEM((tensors - 1,) + part.shape, jnp.float32),
            pltpu.VMEM(part.shape, jnp.float32),
            pltpu.SemaphoreType.DMA((tensors - 1,)),
            pltpu.SemaphoreType.DMA((tensors - 1,)),
            pltpu.SemaphoreType.DMA((groups - 1,)),
            pltpu.SemaphoreType.DMA((groups - 1,)),
        ],
        compiler_params=comm_params(collective_id, 16),
        cost_estimate=cost(10),
        name="gate_exchange",
    )(part)


def dot(a, b, dims):
    return lax.dot_general(a, b, ((dims[:1], dims[1:]), ((), ())), preferred_element_type=jnp.float32)


def add_to(target, first, second, step=64):
    rows = target.shape[0]

    def body(i, carry):
        r = pl.ds(pl.multiple_of(i * step, step), step)
        total = first[r, :].astype(jnp.float32) + second[r, :].astype(jnp.float32)
        target[r, :] = total.astype(target.dtype)
        return carry

    lax.fori_loop(0, rows // step, body, 0)


def expert_layer(
    hidden_two, grad_out_all, gate_up, down, router_t, chosen_all, residual, attended, collective_id
):
    rows, width = hidden_two.shape
    tokens = rows * GROUPS
    units = down.shape[0]
    local = 2
    hidden = units // local
    experts = router_t.shape[0]
    half, part, piece = width // 2, width // 4, width // 8
    tensors = NX * NC
    steps = GROUPS + 4
    a_cols, c_cols = width // 8, width // 4
    low = jnp.bfloat16
    wide = width // 4

    def kernel(
        own_in, dy_in, gu_in, down_in, router_ref, chosen_ref, x1_in, o_in,
        block_out, dh_out, gates_out, gate_w, up_w, down_w, o_all,
        gu_ref, down_ref, weight_sem, h, dy, gated, dgu, dx, y_part, yc_buf, ypx_buf, ypy_buf, yqy_buf, yqx_buf, yz_sum,
        ylo_buf, yhi_buf, x1, gu_stage, d_stage,
        core_buf, px_buf, py_buf, qy_buf, qx_buf, z_sum, lo_buf, hi_buf, gate_part, gate_land,
        in_sem, own_sem, o_sem, line_s, line_r, hx_s, hx_r, hc_s, hc_r, x1_sem, yc_s, yc_r, ypx_s, ypx_r, ypy_s, ypy_r,
        yqy_s, yqy_r, yqx_s, yqx_r, yz_s, yz_r, gu_sem, d_sem, core_s, core_r, px_s, px_r, py_s, py_r, qy_s, qy_r, qx_s, qx_r,
        z_s, z_r, near_s, near_r, far_s, far_r, end_s, end_r,
    ):
        z, y, x, c = place()
        e, t = lax.axis_index("expert"), lax.axis_index("tensor")
        across, twin, beside = device(z, y, 1 - x, c), device(z, y, x, 1 - c), device(z, 1 - y, x, c)
        mates = [(e, lax.rem(t + k, tensors)) for k in range(1, tensors)]
        peers = [(lax.rem(e + k, GROUPS), t) for k in range(1, GROUPS)]
        weight_loads = [
            pltpu.make_async_copy(gu_in, gu_ref, weight_sem.at[0]),
            pltpu.make_async_copy(down_in, down_ref, weight_sem.at[1]),
        ]
        for copy in weight_loads:
            copy.start()
        greet([(target, None) for target in mates + peers])

        def pick(values, index):
            result = values[-1]
            for k in range(len(values) - 1):
                result = jnp.where(index == k, values[k], result)
            return result

        def zz_of(j):
            return pick([z, pick([1, 0, 3, 2], z), pick([3, 3, 0, 0], z), pick([2, 2, 1, 1], z)], j)

        def is_own(i):
            return (i == 0) | ((i >= 2) & (lax.rem(i, 2) == 1))

        def block_of(i):
            return zz_of(lax.div(i, 2)) * NY + jnp.where(is_own(i), y, 1 - y)

        def flip_block(j):
            return zz_of(j) * NY + 1 - y

        def own_block(j):
            return zz_of(j) * NY + y

        def a_at(xx, cc):
            return pl.ds(pl.multiple_of(xx * (2 * a_cols) + cc * a_cols, 128), a_cols)

        def c_at(cc):
            return pl.ds(pl.multiple_of(4 * a_cols + cc * c_cols, 128), c_cols)

        def h_view(b, columns):
            return h.at[block_rows(b, rows), columns]

        line = LineGather(
            [0, 1, 2], [own_in.at[:, a_at(x, c)], own_in.at[:, c_at(c)], o_in],
            [
                lambda b: h_view(b, a_at(x, c)),
                lambda b: h_view(b, c_at(c)),
                lambda b: o_all.at[block_rows(b, rows), :],
            ],
            line_s, line_r,
        )

        def h_twin(b, stream, landing=False):
            cc = 1 - c if landing else c
            piece = h_view(b, [a_at(x, cc), c_at(cc), a_at(1 - x, cc)][stream])
            return remote(piece, piece, hc_s.at[b, stream], hc_r.at[b, stream], twin)

        def h_across(b, landing=False):
            piece = h_view(b, a_at(1 - x if landing else x, c))
            return remote(piece, piece, hx_s.at[b], hx_r.at[b], across)

        def gather_event(rel):
            def body():
                b = line.block(rel)
                marks = len(line.pending)
                for stream in (0, 1):
                    line.arrive(stream, rel)
                    if rel < 7:
                        line.start(stream, rel)
                    if stream == 0:
                        h_across(b).start()
                    h_twin(b, stream).start()
                late = line.pending[marks:]
                del line.pending[marks:]
                line.finish_later(late, rel)
            run_if(line.exists(rel), body)

        def attended_event(rel):
            def body():
                marks = len(line.pending)
                line.arrive(2, rel)
                if rel < 7:
                    line.start(2, rel)
                late = line.pending[marks:]
                del line.pending[marks:]
                line.finish_later(late, rel)
            run_if(line.exists(rel), body)

        def relay(i):
            b = block_of(i)
            h_across(b, True).wait_recv()
            h_twin(b, 2).start()

        for stream in (0, 1):
            line.start(stream, 0)
        keep = pltpu.make_async_copy(own_in, h.at[block_rows(z * NY + y, rows), :], own_sem)
        keep.start()
        keep_o = pltpu.make_async_copy(o_in, o_all.at[block_rows(z * NY + y, rows), :], o_sem)
        keep_o.start()

        def load(i):
            r = block_rows(block_of(i), rows)
            return pltpu.make_async_copy(dy_in.at[r, :], dy.at[r, :], in_sem.at[i])

        def start_load(i, carry):
            load(i).start()
            return carry

        lax.fori_loop(0, GROUPS, start_load, 0)
        x1_copies = [
            pltpu.make_async_copy(
                x1_in.at[:, pl.ds(pl.multiple_of(c * half + s * part + x * piece, piece), piece)],
                x1.at[:, pl.ds(s * piece, piece)], x1_sem.at[s],
            )
            for s in range(2)
        ]
        for copy in x1_copies:
            copy.start()

        def to_twin(i):
            b = block_of(i)
            return remote(
                dx.at[lax.rem(i, 2), :, pl.ds(pl.multiple_of((1 - c) * half, half), half)],
                core_buf.at[b], core_s.at[i], core_r.at[i], twin,
            )

        def p_across(i):
            b = block_of(i)
            return remote(
                core_buf.at[b, :, pl.ds(pl.multiple_of((1 - x) * piece, piece), piece)],
                px_buf.at[b], px_s.at[i], px_r.at[i], across,
            )

        def p_beside(j):
            return remote(px_buf.at[flip_block(j)], py_buf.at[j], py_s.at[j], py_r.at[j], beside)

        def q_beside(j):
            return remote(
                core_buf.at[flip_block(j), :, pl.ds(part, part)], qy_buf.at[j], qy_s.at[j], qy_r.at[j], beside
            )

        def q_across(j):
            return remote(
                qy_buf.at[j, :, pl.ds(pl.multiple_of((1 - x) * piece, piece), piece)],
                qx_buf.at[j], qx_s.at[j], qx_r.at[j], across,
            )

        def up(j, s):
            return remote(z_sum.at[s, j], lo_buf.at[s, j], z_s.at[0, s, j], z_r.at[0, s, j], device(z + 1, y, x, c))

        def down_z(j, s):
            return remote(z_sum.at[s, j], hi_buf.at[s, j], z_s.at[1, s, j], z_r.at[1, s, j], device(z - 1, y, x, c))

        def take_twin(i):
            to_twin(i).wait_recv()
            b = block_of(i)
            mine = core_buf.at[b]
            add_to(mine, mine, dx.at[lax.rem(i, 2), :, pl.ds(pl.multiple_of(c * half, half), half)], 32)
            p_across(i).start()
            pl.when(jnp.logical_not(is_own(i)))(lambda: q_beside(lax.div(i, 2)).start())

        def take_p_across(i):
            p_across(i).wait_recv()
            b = block_of(i)
            add_to(
                px_buf.at[b], px_buf.at[b],
                core_buf.at[b, :, pl.ds(pl.multiple_of(x * piece, piece), piece)],
            )

        def take_q_beside(j):
            q_beside(j).wait_recv()
            add_to(qy_buf.at[j], qy_buf.at[j], core_buf.at[own_block(j), :, pl.ds(part, part)])
            q_across(j).start()

        def take_q_across(j):
            q_across(j).wait_recv()
            add_to(
                z_sum.at[1, zz_of(j)], qx_buf.at[j], qy_buf.at[j, :, pl.ds(pl.multiple_of(x * piece, piece), piece)]
            )

        def take_p_beside(j):
            p_beside(j).wait_recv()
            add_to(z_sum.at[0, zz_of(j)], py_buf.at[j], px_buf.at[own_block(j)])

        def hop(j, k):
            zz = zz_of(j)

            def upward():
                for s in range(2):
                    if k > 0:
                        up(zz, s).wait_recv()
                        add_to(z_sum.at[s, zz], z_sum.at[s, zz], lo_buf.at[s, zz])
                    up(zz, s).start()

            def downward():
                for s in range(2):
                    if k > 0:
                        down_z(zz, s).wait_recv()
                        add_to(z_sum.at[s, zz], z_sum.at[s, zz], hi_buf.at[s, zz])
                    down_z(zz, s).start()

            pl.when((z < zz) & (z == k))(upward)
            pl.when((z > zz) & (NZ - 1 - z == k))(downward)

        def y_twin(i):
            return remote(
                y_part.at[lax.rem(i, 2), :, pl.ds(pl.multiple_of((1 - c) * half, half), half)],
                yc_buf.at[block_of(i)], yc_s.at[i], yc_r.at[i], twin,
            )

        def yp_across(i):
            b = block_of(i)
            return remote(
                yc_buf.at[b, :, pl.ds(pl.multiple_of((1 - x) * piece, piece), piece)],
                ypx_buf.at[b], ypx_s.at[i], ypx_r.at[i], across,
            )

        def yp_beside(j):
            return remote(ypx_buf.at[flip_block(j)], ypy_buf.at[j], ypy_s.at[j], ypy_r.at[j], beside)

        def yq_beside(j):
            return remote(
                yc_buf.at[flip_block(j), :, pl.ds(part, part)], yqy_buf.at[j], yqy_s.at[j], yqy_r.at[j], beside
            )

        def yq_across(j):
            return remote(
                yqy_buf.at[j, :, pl.ds(pl.multiple_of((1 - x) * piece, piece), piece)],
                yqx_buf.at[j], yqx_s.at[j], yqx_r.at[j], across,
            )

        def y_up(zz, s):
            return remote(
                yz_sum.at[s, zz], ylo_buf.at[s, zz], yz_s.at[0, s, zz], yz_r.at[0, s, zz], device(z + 1, y, x, c)
            )

        def y_down(zz, s):
            return remote(
                yz_sum.at[s, zz], yhi_buf.at[s, zz], yz_s.at[1, s, zz], yz_r.at[1, s, zz], device(z - 1, y, x, c)
            )

        def take_y_twin(i):
            y_twin(i).wait_recv()
            mine = yc_buf.at[block_of(i)]
            add_to(mine, mine, y_part.at[lax.rem(i, 2), :, pl.ds(pl.multiple_of(c * half, half), half)], 32)
            yp_across(i).start()
            pl.when(jnp.logical_not(is_own(i)))(lambda: yq_beside(lax.div(i, 2)).start())

        def take_yp_across(i):
            yp_across(i).wait_recv()
            b = block_of(i)
            add_to(
                ypx_buf.at[b], ypx_buf.at[b],
                yc_buf.at[b, :, pl.ds(pl.multiple_of(x * piece, piece), piece)],
            )
            pl.when(jnp.logical_not(is_own(i)))(lambda: yp_beside(lax.div(i, 2)).start())

        def take_yq_beside(j):
            yq_beside(j).wait_recv()
            add_to(yqy_buf.at[j], yqy_buf.at[j], yc_buf.at[own_block(j), :, pl.ds(part, part)])
            yq_across(j).start()

        def take_y_sums(j):
            zz = zz_of(j)
            yq_across(j).wait_recv()
            add_to(
                yz_sum.at[1, zz], yqx_buf.at[j], yqy_buf.at[j, :, pl.ds(pl.multiple_of(x * piece, piece), piece)]
            )
            yp_beside(j).wait_recv()
            add_to(yz_sum.at[0, zz], ypy_buf.at[j], ypx_buf.at[own_block(j)])

        def y_take(zz, s, copy, landed):
            copy(zz, s).wait_recv()
            add_to(yz_sum.at[s, zz], yz_sum.at[s, zz], landed.at[s, zz])

        def y_hop(j, k):
            zz = zz_of(j)

            def upward():
                for s in range(2):
                    if k > 0:
                        y_take(zz, s, y_up, ylo_buf)
                    y_up(zz, s).start()

            def downward():
                for s in range(2):
                    if k > 0:
                        y_take(zz, s, y_down, yhi_buf)
                    y_down(zz, s).start()

            pl.when((z < zz) & (z == k))(upward)
            pl.when((z > zz) & (NZ - 1 - z == k))(downward)

        def front(i):
            load(i).wait()
            b = block_of(i)
            pl.when(i == 0)(keep.wait)
            pl.when(i == 0)(lambda: each(weight_loads, "wait"))

            def landed():
                for stream in range(3):
                    h_twin(b, stream, True).wait_recv()

            pl.when(i > 0)(landed)
            r = block_rows(b, rows)
            rows_h, rows_dy = h[r, :], dy[r, :]
            logits = dot(rows_h, router_ref[...], (1, 1))
            shifted = jnp.exp(logits - jnp.max(logits, axis=-1, keepdims=True))
            probs = shifted / jnp.sum(shifted, axis=-1, keepdims=True) * chosen_ref[r, :].astype(jnp.float32)
            lane = lax.broadcasted_iota(jnp.int32, probs.shape, 1)
            line = lax.broadcasted_iota(jnp.int32, (rows, 128), 1)
            found = jnp.zeros((rows, 128), jnp.float32)
            for expert in range(local):
                at, up_at = pl.ds(expert * hidden, hidden), pl.ds((local + expert) * hidden, hidden)
                gate = jnp.sum(jnp.where(lane == e * local + expert, probs, 0.0), axis=-1, keepdims=True)
                pre = dot(rows_h, gu_ref[:, at], (1, 0))
                scale = dot(rows_h, gu_ref[:, up_at], (1, 0))
                back = dot(rows_dy, down_ref[at, :], (1, 1))
                sigmoid = jax.nn.sigmoid(pre)
                swish = pre * sigmoid
                active = swish * scale
                gated[r, at] = (active * gate).astype(low)
                found = jnp.where(line == expert, jnp.sum(active * back, axis=-1, keepdims=True), found)
                back = back * gate
                dgu[r, at] = (back * scale * sigmoid * (1.0 + pre * (1.0 - sigmoid))).astype(low)
                dgu[r, up_at] = (back * swish).astype(low)
            gate_part[b] = jnp.transpose(found)[:8, :]

        def rear(i):
            r = block_rows(block_of(i), rows)
            slot = lax.rem(i, 2)
            pl.when(i >= 2)(lambda: to_twin(i - 2).wait_send())

            def columns(k, carry):
                at = pl.ds(pl.multiple_of(k * wide, wide), wide)
                dx[slot, :, at] = dot(dgu[r, :], gu_ref[at, :], (1, 1)).astype(low)
                return carry

            lax.fori_loop(0, width // wide, columns, 0)
            to_twin(i).start()
            pl.when(i >= 2)(lambda: y_twin(i - 2).wait_send())

            def y_columns(k, carry):
                at = pl.ds(pl.multiple_of(k * wide, wide), wide)
                y_part[slot, :, at] = dot(gated[r, :], down_ref[:, at], (1, 0)).astype(low)
                return carry

            lax.fori_loop(0, width // wide, y_columns, 0)
            y_twin(i).start()

        tile_width = piece // 2
        tiles = width // tile_width // 4
        d_width = width // 8

        def gu_copies(n):
            slot = lax.rem(n, 2)
            at = pl.ds(pl.multiple_of(n * tile_width, tile_width), tile_width)
            return [
                pltpu.make_async_copy(
                    gu_stage.at[slot, :, pl.ds(k * hidden, hidden)],
                    (gate_w if k < local else up_w).at[k % local, at, :],
                    gu_sem.at[slot, k],
                )
                for k in range(2 * local)
            ]

        def d_copies(n):
            slot = lax.rem(n, 2)
            at = pl.ds(pl.multiple_of(n * d_width, d_width), d_width)
            return [
                pltpu.make_async_copy(
                    d_stage.at[slot, pl.ds(k * hidden, hidden), :], down_w.at[k, :, at], d_sem.at[slot, k]
                )
                for k in range(local)
            ]

        def each(copies, what):
            for copy in copies:
                getattr(copy, what)()

        def weight_grads(q):
            def tile(k, carry):
                n = q * tiles + k
                pl.when(n >= 2)(lambda: each(gu_copies(n - 2), "wait"))
                at = pl.ds(pl.multiple_of(n * tile_width, tile_width), tile_width)
                gu_stage[lax.rem(n, 2)] = dot(h[:, at], dgu[...], (0, 0))
                each(gu_copies(n), "start")
                return carry

            lax.fori_loop(0, tiles, tile, 0)

            def d_tile(k, carry):
                n = q * 2 + k
                pl.when(n >= 2)(lambda: each(d_copies(n - 2), "wait"))
                at = pl.ds(pl.multiple_of(n * d_width, d_width), d_width)
                d_stage[lax.rem(n, 2)] = dot(gated[...], dy[:, at], (0, 0))
                each(d_copies(n), "start")
                return carry

            lax.fori_loop(0, 2, d_tile, 0)

        near = [
            remote(gate_part, gate_land.at[k], near_s.at[k], near_r.at[k], mates[k])
            for k in range(tensors - 1)
        ]

        def far(k):
            return remote(
                gate_land.at[tensors - 1, lax.rem(e + k, GROUPS)], gates_out.at[e],
                far_s.at[k - 1], far_r.at[k - 1], peers[k - 1],
            )

        def sum_near():
            for copy in near:
                copy.wait_recv()
            total = gate_part[...]
            for k in range(tensors - 1):
                total = total + gate_land[k]
            gate_land[tensors - 1] = total
            for k in range(1, GROUPS):
                far(k).start()
            gates_out[e] = gate_land[tensors - 1, e]

        def step(i, carry):
            def at(number, body):
                pl.when(i == number)(body)

            odd, even = lax.rem(i, 2) == 1, lax.rem(i, 2) == 0
            j_even, j_odd = lax.div(i, 2) - 1, lax.div(i - 1, 2) - 1
            pl.when(i < GROUPS)(lambda: front(i))

            def events(*rels):
                for rel in rels:
                    gather_event(rel)

            at(1, lambda: events(2, 5, 8, 11))
            at(2, lambda: events(3, 6))
            at(3, lambda: events(10, 13))

            def attended_events(*rels):
                for rel in rels:
                    attended_event(rel)

            at(8, lambda: attended_events(1, 4))
            at(9, lambda: attended_events(2, 5))
            at(10, lambda: attended_events(3, 6))
            at(11, lambda: attended_events(7, 8, 11))

            pl.when((i >= 1) & (i <= GROUPS))(lambda: take_twin(i - 1))
            pl.when(even & (i >= 4) & (i <= GROUPS))(lambda: take_q_beside(j_even))
            at(3, lambda: take_q_beside(0))
            at(4, lambda: take_q_across(0))

            def late():
                take_p_across(i - 2)
                pl.when(i > 3)(lambda: take_q_across(j_odd))
                pl.when(i == 3)(lambda: p_beside(0).start())

            pl.when(odd & (i >= 3) & (i <= GROUPS + 1))(late)
            at(GROUPS, lambda: each(near, "start"))
            at(GROUPS + 1, sum_near)
            pl.when(i < GROUPS)(lambda: rear(i))
            pl.when(i >= GROUPS)(lambda: weight_grads(i - GROUPS))
            at(0, lambda: events(7, 1, 4))
            at(2, lambda: events(9, 12))
            at(6, lambda: line.start(2, 0))
            pl.when(i < GROUPS - 1)(lambda: relay(i + 1))

            def pass_p():
                take_p_across(i - 2)
                pl.when(i > 2)(lambda: p_beside(j_even).start())

            pl.when(even & (i >= 2) & (i <= GROUPS))(pass_p)
            at(4, lambda: take_p_beside(0))

            def join():
                take_p_beside(j_odd)
                hop(j_odd, 0)

            pl.when(odd & (i >= 5) & (i <= GROUPS + 1))(join)
            pl.when((i == GROUPS) | (i == GROUPS + 2))(lambda: hop(j_even - 1, 1))
            at(GROUPS + 1, lambda: hop(1, 2))
            pl.when((i >= 2) & (i <= GROUPS + 1))(lambda: take_yp_across(i - 2))
            pl.when((i >= 1) & (i <= GROUPS))(lambda: take_y_twin(i - 1))
            pl.when(even & (i >= 4) & (i <= GROUPS))(lambda: take_yq_beside(j_even))
            at(3, lambda: take_yq_beside(0))
            at(5, lambda: take_y_sums(0))

            def join_y():
                take_y_sums(j_even - 1)
                y_hop(j_even - 1, 0)

            pl.when(even & (i >= 6) & (i <= GROUPS + 2))(join_y)
            pl.when((i == GROUPS + 1) | (i == GROUPS + 3))(lambda: y_hop(j_odd - 1, 1))
            at(GROUPS + 2, lambda: y_hop(1, 2))
            return carry

        lax.fori_loop(0, steps, step, 0)

        for rel in (9, 12, 10, 13):
            attended_event(rel)

        def columns_of(s, xx, cc):
            return pl.ds(pl.multiple_of(cc * half + s * part + xx * piece, piece), piece)

        mine = z
        for s in range(2):
            def below(s=s):
                up(mine, s).wait_recv()
                add_to(z_sum.at[s, mine], z_sum.at[s, mine], lo_buf.at[s, mine])

            def above(s=s):
                down_z(mine, s).wait_recv()
                add_to(z_sum.at[s, mine], z_sum.at[s, mine], hi_buf.at[s, mine])

            pl.when(z > 0)(below)
            pl.when(z < NZ - 1)(above)
            own = dh_out.at[:, columns_of(s, x, c)]

            def keep(k, carry, s=s, own=own):
                r = pl.ds(pl.multiple_of(k * 64, 64), 64)
                own[r, :] = z_sum[s, mine, r, :]
                return carry

            lax.fori_loop(0, rows // 64, keep, 0)
            remote(own, own, end_s.at[0, s], end_r.at[0, s], across).start()
            remote(own, own, end_s.at[1, s], end_r.at[1, s], twin).start()
        for copy in x1_copies:
            copy.wait()
        for s in range(2):
            pl.when(z > 0)(lambda s=s: y_take(z, s, y_up, ylo_buf))
            pl.when(z < NZ - 1)(lambda s=s: y_take(z, s, y_down, yhi_buf))
            y_own = block_out.at[:, columns_of(s, x, c)]

            def finish(k, carry, s=s, y_own=y_own):
                r = pl.ds(pl.multiple_of(k * 64, 64), 64)
                y_own[r, :] = (
                    x1[r, pl.ds(s * piece, piece)] + yz_sum[s, z, r, :].astype(jnp.float32)
                ).astype(low)
                return carry

            lax.fori_loop(0, rows // 64, finish, 0)
            remote(y_own, y_own, end_s.at[0, 2 + s], end_r.at[0, 2 + s], across).start()
            remote(y_own, y_own, end_s.at[1, 2 + s], end_r.at[1, 2 + s], twin).start()
        for s in range(2):
            there = dh_out.at[:, columns_of(s, 1 - x, c)]
            remote(there, there, end_s.at[0, s], end_r.at[0, s], across).wait_recv()
            remote(there, there, end_s.at[2, s], end_r.at[2, s], twin).start()
        for s in range(2):
            there = block_out.at[:, columns_of(s, 1 - x, c)]
            remote(there, there, end_s.at[0, 2 + s], end_r.at[0, 2 + s], across).wait_recv()
            remote(there, there, end_s.at[2, 2 + s], end_r.at[2, 2 + s], twin).start()
        for n, result in ((0, dh_out), (2, block_out)):
            for s in range(2):
                for k, xx in ((1, x), (2, 1 - x)):
                    there = result.at[:, columns_of(s, xx, 1 - c)]
                    remote(there, there, end_s.at[k, n + s], end_r.at[k, n + s], twin).wait_recv()
                for k, target in ((0, across), (1, twin), (2, twin)):
                    there = result.at[:, columns_of(s, 1 - x if k == 2 else x, c)]
                    remote(there, there, end_s.at[k, n + s], end_r.at[k, n + s], target).wait_send()
        for k in range(1, GROUPS):
            there = gates_out.at[lax.rem(e + GROUPS - k, GROUPS)]
            remote(there, there, far_s.at[k - 1], far_r.at[k - 1], peers[k - 1]).wait_recv()
            far(k).wait_send()
        each(near, "wait_send")

        def drain(i, carry):
            pl.when(i >= GROUPS - 2)(lambda: to_twin(i).wait_send())
            pl.when(i >= GROUPS - 2)(lambda: y_twin(i).wait_send())
            p_across(i).wait_send()
            yp_across(i).wait_send()
            return carry

        lax.fori_loop(0, GROUPS, drain, 0)

        def drain_pair(j, carry):
            p_beside(j).wait_send()
            q_beside(j).wait_send()
            q_across(j).wait_send()
            yp_beside(j).wait_send()
            yq_beside(j).wait_send()
            yq_across(j).wait_send()
            for s in range(2):
                pl.when(z < j)(lambda s=s: up(j, s).wait_send())
                pl.when(z > j)(lambda s=s: down_z(j, s).wait_send())
                pl.when(z < j)(lambda s=s: y_up(j, s).wait_send())
                pl.when(z > j)(lambda s=s: y_down(j, s).wait_send())
            return carry

        lax.fori_loop(0, NZ, drain_pair, 0)

        def drain_rows_of(i, carry):
            b = block_of(i)
            h_across(b).wait_send()
            for stream in range(3):
                h_twin(b, stream).wait_send()
            return carry

        lax.fori_loop(1, GROUPS, drain_rows_of, 0)
        line.finish()
        keep_o.wait()
        for k in range(2):
            each(gu_copies(4 * tiles - 2 + k), "wait")
            each(d_copies(6 + k), "wait")

    shape = jax.ShapeDtypeStruct
    dma = pltpu.SemaphoreType.DMA
    f32 = jnp.float32
    return pl.pallas_call(
        kernel,
        out_shape=(
            shape((rows, width), low),
            shape((rows, width), low),
            shape((GROUPS, 8, rows), f32),
            shape((local, width, hidden), f32),
            shape((local, width, hidden), f32),
            shape((local, hidden, width), f32),
            shape((tokens,) + attended.shape[1:], low),
        ),
        in_specs=[HBM, HBM, HBM, HBM, VMEM, VMEM, HBM, HBM],
        out_specs=(VMEM, VMEM, VMEM, HBM, HBM, HBM, HBM),
        scratch_shapes=[
            pltpu.VMEM(gate_up.shape, low),
            pltpu.VMEM(down.shape, low),
            dma((2,)),
            pltpu.VMEM((tokens, width), low),
            pltpu.VMEM((tokens, width), low),
            pltpu.VMEM((tokens, units), low),
            pltpu.VMEM((tokens, 2 * units), low),
            pltpu.VMEM((2, rows, width), low),
            pltpu.VMEM((2, rows, width), low),
            pltpu.VMEM((GROUPS, rows, half), low),
            pltpu.VMEM((GROUPS, rows, piece), low),
            pltpu.VMEM((NZ, rows, piece), low),
            pltpu.VMEM((NZ, rows, part), low),
            pltpu.VMEM((NZ, rows, piece), low),
            pltpu.VMEM((2, NZ, rows, piece), low),
            pltpu.VMEM((2, NZ, rows, piece), low),
            pltpu.VMEM((2, NZ, rows, piece), low),
            pltpu.VMEM((rows, part), f32),
            pltpu.VMEM((2, piece // 2, 2 * units), f32),
            pltpu.VMEM((2, units, width // 8), f32),
            pltpu.VMEM((GROUPS, rows, half), low),
            pltpu.VMEM((GROUPS, rows, piece), low),
            pltpu.VMEM((NZ, rows, piece), low),
            pltpu.VMEM((NZ, rows, part), low),
            pltpu.VMEM((NZ, rows, piece), low),
            pltpu.VMEM((2, NZ, rows, piece), low),
            pltpu.VMEM((2, NZ, rows, piece), low),
            pltpu.VMEM((2, NZ, rows, piece), low),
            pltpu.VMEM((GROUPS, 8, rows), f32),
            pltpu.VMEM((tensors, GROUPS, 8, rows), f32),
            dma((GROUPS,)), dma, dma, dma((3, 14, 3)), dma((3, 14)), dma((GROUPS,)), dma((GROUPS,)),
            dma((GROUPS, 3)), dma((GROUPS, 3)), dma((2,)), dma((GROUPS,)), dma((GROUPS,)), dma((GROUPS,)), dma((GROUPS,)),
            dma((NZ,)), dma((NZ,)), dma((NZ,)), dma((NZ,)), dma((NZ,)), dma((NZ,)),
            dma((2, 2, NZ)), dma((2, 2, NZ)), dma((2, 2 * local)), dma((2, local)),
            dma((GROUPS,)), dma((GROUPS,)), dma((GROUPS,)), dma((GROUPS,)),
            dma((NZ,)), dma((NZ,)), dma((NZ,)), dma((NZ,)), dma((NZ,)), dma((NZ,)),
            dma((2, 2, NZ)), dma((2, 2, NZ)),
            dma((tensors - 1,)), dma((tensors - 1,)), dma((GROUPS - 1,)), dma((GROUPS - 1,)),
            dma((3, 4)), dma((3, 4)),
        ],
        compiler_params=comm_params(collective_id, 62),
        cost_estimate=cost(80),
        name="expert_layer",
    )(hidden_two, grad_out_all, gate_up, down, router_t, chosen_all, residual, attended)


def exchange_rows(value, part_ref, land_ref, send_sem, recv_sem, mates):
    rows = value.shape[0]
    line = lax.broadcasted_iota(jnp.int32, (rows, 128), 1)
    part_ref[...] = jnp.transpose(jnp.where(line == 0, value, 0.0))[:8, :]
    for k, mate in enumerate(mates):
        remote(part_ref, land_ref.at[k], send_sem.at[k], recv_sem.at[k], mate).start()


def exchanged_rows(part_ref, land_ref, send_sem, recv_sem, mates):
    total = part_ref[...]
    for k, mate in enumerate(mates):
        remote(part_ref, land_ref.at[k], send_sem.at[k], recv_sem.at[k], mate).wait_recv()
    for k in range(len(mates)):
        total = total + land_ref[k]
    rows = part_ref.shape[1]
    tall = jnp.concatenate([total, jnp.zeros((120, rows), jnp.float32)], axis=0)
    return jnp.transpose(tall)[:, :1]


def drain_rows(part_ref, land_ref, send_sem, recv_sem, mates):
    for k, mate in enumerate(mates):
        remote(part_ref, land_ref.at[k], send_sem.at[k], recv_sem.at[k], mate).wait_send()


def turn(value, cosine, sine):
    return value * cosine + pltpu.roll(value, HEAD // 2, 1) * sine


def project(
    tokens, w_qkv, w_out, out_grad, gain_one, gain_two, qk_gain, w_router, routes, cosine, sine,
    w_gate, w_up, w_down, collective_id,
):
    rows, width = tokens.shape
    parts, depth, columns = w_qkv.shape
    heads = columns // HEAD
    tensors = NX * NC
    back = WINDOW // rows
    low, f32 = jnp.bfloat16, jnp.float32
    QUERY, KEY, VALUE, SMALL, OUT, GRAD, REST = 0, 1, 2, 3, 4, 5, 6
    out_half = w_out.shape[0] // 2
    out_rows, out_columns = w_out.shape
    quarter = width // tensors
    experts = w_router.shape[0]
    small_shape = (8 + 2 * experts, depth)

    def kernel(
        tok_ref, w_ref, out_ref, grad_in, gain_one_ref, gain_two_ref, qk_ref, w_router_ref, routes_ref, cos_ref, sin_ref, gate_in, up_in, down_in,
        w_all, out_all, grad_all, h1_out, raw_out, gate_up, down_out, gain_ref, router_ref, chosen_ref, scale_ref, q_ref, context,
        small_ref, small_all, h1_ref, raw_ref, wide_in, wide_low, down_f, down_low, own_w, own_out, weights, total, part_k, land_k, part_q, land_q,
        send_sem, recv_sem, out_sem, small_sem, kept, ks_s, ks_r, qs_s, qs_r, c_s, c_r, hx_s, hx_r, hc_s, hc_r, wide_s,
    ):
        z, y, x, c = place()
        e, t = lax.axis_index("expert"), lax.axis_index("tensor")
        wide_loads = [
            pltpu.make_async_copy(source.at[k], wide_in.at[2 * n + k], wide_s.at[2 * n + k])
            for n, source in enumerate((gate_in, up_in))
            for k in range(2)
        ]
        for copy in wide_loads:
            copy.start()
        mates = [(e, lax.rem(t + k, tensors)) for k in range(1, tensors)]
        beside, above = device(z, 1 - y, x, c), device(z + 1, y, x, c)
        views = [
            lambda b: weights.at[QUERY, block_rows(b, depth), :],
            lambda b: weights.at[KEY, block_rows(b, depth), :],
            lambda b: weights.at[VALUE, block_rows(b, depth), :],
            lambda b: small_all.at[b],
            lambda b: out_all.at[pl.ds(0, out_half), block_rows(b, out_columns)],
            lambda b: grad_view(b, x, c),
            lambda b: out_all.at[pl.ds(out_half, out_half), block_rows(b, out_columns)],
        ]
        across, twin = device(z, y, 1 - x, c), device(z, y, x, 1 - c)

        def quarter_at(xx, cc):
            return pl.ds(pl.multiple_of((xx * NC + cc) * quarter, quarter), quarter)

        def grad_view(b, xx, cc):
            return grad_all.at[block_rows(b, rows), quarter_at(xx, cc)]

        def grad_across(b, landing=False):
            piece = grad_view(b, 1 - x if landing else x, c)
            return remote(piece, piece, hx_s.at[b], hx_r.at[b], across)

        def grad_twin(b, relayed, landing=False):
            piece = grad_view(b, 1 - x if relayed else x, 1 - c if landing else c)
            return remote(piece, piece, hc_s.at[b, relayed], hc_r.at[b, relayed], twin)

        line = LineGather(
            [SMALL, VALUE, KEY, QUERY, OUT, GRAD, REST],
            [
                own_w.at[0], own_w.at[1], own_w.at[2], small_ref, own_out.at[pl.ds(0, out_half)],
                grad_in.at[:, quarter_at(x, c)], own_out.at[pl.ds(out_half, out_half)],
            ],
            views, send_sem, recv_sem, y_first=(OUT,),
        )
        small_ref[...] = jnp.zeros_like(small_ref)
        small_ref[0:1, :] = gain_one_ref[...].astype(low).astype(f32)
        small_ref[1:2, :] = gain_two_ref[...].astype(low).astype(f32)
        small_ref[2:3, : qk_gain.shape[1]] = qk_ref[...].astype(low).astype(f32)
        small_ref[8 : 8 + experts, :] = w_router_ref[...]
        expert_row = lax.broadcasted_iota(jnp.int32, (experts, rows), 0)
        named = jnp.zeros((experts, rows), f32)
        for k in range(routes.shape[0]):
            named = jnp.where(routes_ref[k : k + 1, :] == expert_row, 1.0, named)
        small_ref[8 + experts : 8 + 2 * experts, :] = named
        greet(line.partners() + [(mate, None) for mate in mates])
        line.start(SMALL, 0)
        for part in (VALUE, KEY, QUERY):
            def cast(i, carry, part=part):
                r = pl.ds(pl.multiple_of(i * 32, 32), 32)
                own_w[part, r, :] = w_ref[part, r, :].astype(low)
                return carry

            lax.fori_loop(0, depth // 32, cast, 0)
            if part != QUERY:
                line.start(part, 0)

        def cast_out(i, carry):
            r = pl.ds(pl.multiple_of(i * 32, 32), 32)
            own_out[r, :] = out_ref[r, :].astype(low)
            return carry

        lax.fori_loop(0, out_rows // 32, cast_out, 0)
        keep_out = pltpu.make_async_copy(own_out, out_all.at[:, block_rows(line.block(0), out_columns)], kept.at[0])
        keep_out.start()
        keep_grad = pltpu.make_async_copy(grad_in, grad_all.at[block_rows(line.block(0), rows), :], kept.at[1])
        keep_grad.start()

        def square(i, carry):
            r = pl.ds(pl.multiple_of(i * 32, 32), 32)
            value = tok_ref[r, :].astype(f32)
            scale_ref[r, 0:1] = lax.rsqrt(jnp.mean(value * value, axis=-1, keepdims=True) + EPS)
            return carry

        lax.fori_loop(0, rows // 32, square, 0)
        total[...] = jnp.zeros_like(total)
        own_small = pltpu.make_async_copy(small_ref, small_all.at[line.block(0)], small_sem)
        own_small.start()

        def use(stream, rel):
            b = line.block(rel)
            at = pl.ds(pl.multiple_of(b * depth, depth), depth)
            if stream == SMALL:
                gain = small_ref[0:1, :] if rel == 0 else small_all[b, 0:1, :]
                h1_ref[:, at] = (tok_ref[:, at].astype(f32) * scale_ref[:, 0:1] * gain).astype(low)
                return
            block = own_w[stream] if rel == 0 else weights[stream, block_rows(b, depth), :]
            total[stream] += dot(h1_ref[:, at], block, (1, 0))

        def event(stream, rel):
            def body():
                line.arrive(stream, rel)
                if line.forwards(stream, rel):
                    marks = len(line.pending)
                    line.start(stream, rel)
                    late = line.pending[marks:]
                    del line.pending[marks:]
                    line.finish_later(late, rel)
                if stream == GRAD:
                    b = line.block(rel)
                    grad_across(b).start()
                    grad_twin(b, 0).start()
                elif stream not in (OUT, REST):
                    use(stream, rel)
            run_if(line.exists(rel), body)

        use(SMALL, 0)
        use(VALUE, 0)
        own_small.wait()

        units = down_in.shape[1]
        for n, copy in enumerate(wide_loads):
            copy.wait()

            def round_wide(i, carry, n=n):
                r = pl.ds(pl.multiple_of(i * 64, 64), 64)
                wide_low[r, pl.ds(n * units, units)] = wide_in[n, r, :].astype(low)
                return carry

            lax.fori_loop(0, width // 64, round_wide, 0)
        wide_out = pltpu.make_async_copy(wide_low, gate_up, wide_s.at[0])
        wide_out.start()
        down_loads = [
            pltpu.make_async_copy(down_in.at[k], down_f.at[pl.ds(k * units, units), :], wide_s.at[1 + k])
            for k in range(2)
        ]
        for copy in down_loads:
            copy.start()

        use(KEY, 0)
        def events(*pairs):
            for stream, rels in pairs:
                for rel in rels:
                    event(stream, rel)

        for rel in (7, 1, 4, 2, 5):
            event(SMALL, rel)
            event(VALUE, rel)
        for copy in down_loads:
            copy.wait()

        def round_down(i, carry):
            r = pl.ds(pl.multiple_of(i * 32, 32), 32)
            down_low[r, :] = down_f[r, :].astype(low)
            return carry

        lax.fori_loop(0, 2 * units // 32, round_down, 0)
        down_copy = pltpu.make_async_copy(down_low, down_out, wide_s.at[3])
        down_copy.start()
        line.start(QUERY, 0)
        for rel in (3, 6):
            event(SMALL, rel)
            event(VALUE, rel)
        events((KEY, (7, 1, 4)))
        for rel in (8, 11, 9, 12, 10, 13):
            event(SMALL, rel)
            event(VALUE, rel)

        slices = HEAD // GROUPS
        for b in range(GROUPS):
            at = pl.ds(b * depth, depth)
            gain_ref[0:2, at] = small_all[b, 0:2, :]
            router_ref[:, at] = small_all[b, 8 : 8 + experts, :].astype(low)
            tall = jnp.concatenate(
                [small_all[b, 8 + experts : 8 + 2 * experts, :], jnp.zeros((128 - experts, depth), f32)], axis=0
            )
            chosen_ref[pl.ds(b * depth, depth), :] = jnp.transpose(tall)[:, :experts].astype(low)
        for which in range(2):
            for head in range(heads):
                start = (which * heads + head) * slices
                gain_ref[2 + which : 3 + which, pl.ds(head * HEAD, HEAD)] = jnp.concatenate(
                    [small_all[b, 2:3, start : start + slices] for b in range(GROUPS)], axis=1
                )

        def context_copy(which, k):
            if k == 2:
                source, target = 0, above
            elif k == 4:
                source, target = 2, above
            else:
                source, target = jnp.where(y == 0, k - 1, k + 1), beside
            return remote(
                context.at[source, which], context.at[k, which], c_s.at[which, k], c_r.at[which, k], target
            )

        sends = {2: z < NZ - 1, 4: (z >= 1) & (z < NZ - 1), 1: (y == 0) | (z >= 1), 3: z >= 1 + y}
        takes = {2: z >= 1, 4: z >= 2, 1: (y == 1) | (z >= 1), 3: z >= 2 - y}

        def context_send(which, k):
            run_if(sends[k], lambda: context_copy(which, k).start())

        def context_take(which, k):
            run_if(takes[k], lambda: context_copy(which, k).wait_recv())

        for k in range(1, back + 1):
            def clear(k=k):
                context[k] = jnp.zeros_like(context[k])
            run_if(jnp.logical_not(takes[k]), clear)

        context[0, 1] = total[VALUE].astype(low)
        context_send(1, 2)
        run_if(y == 0, lambda: context_copy(1, 1).start())
        events((KEY, (2, 5, 3, 6)), (QUERY, (7, 1, 4)))
        line.start(GRAD, 0)
        line.start(OUT, 0)
        line.start(REST, 0)
        events((KEY, (8, 11, 9, 12, 10, 13)))
        key_raw = total[KEY]
        raw_ref[1] = key_raw
        exchange_rows(jnp.sum(key_raw * key_raw, axis=-1, keepdims=True), part_k, land_k, ks_s, ks_r, mates)
        use(QUERY, 0)
        events((QUERY, (2, 5)))
        key_scale = lax.rsqrt(exchanged_rows(part_k, land_k, ks_s, ks_r, mates) / width + EPS)
        scale_ref[:, 2:3] = key_scale
        def rotated(which, scale, store):
            for head in range(heads):
                at = pl.ds(head * HEAD, HEAD)
                value = total[which, :, at] * scale * gain_ref[2 + which : 3 + which, at]
                store(at, turn(value, cos_ref[...], sin_ref[...]).astype(low))

        def store_key(at, value):
            context[0, 0, :, at] = value

        rotated(KEY, key_scale, store_key)
        context_send(0, 2)
        run_if(y == 0, lambda: context_copy(0, 1).start())

        def relay_two(which):
            context_take(which, 2)
            context_send(which, 4)
            run_if((y == 1) & (z >= 1), lambda: context_copy(which, 1).start())
            run_if((y == 0) & sends[3], lambda: context_copy(which, 3).start())

        def relay_four(which):
            context_take(which, 4)
            run_if((y == 1) & sends[3], lambda: context_copy(which, 3).start())

        relay_two(1)
        events((QUERY, (3, 6)), (GRAD, (7, 1, 4)), (OUT, (7, 1, 4)), (REST, (7, 1, 4)))
        relay_four(1)
        events((QUERY, (8, 11)), (GRAD, (2, 5)), (OUT, (8, 11, 2, 5)), (REST, (2, 5)))
        relay_two(0)
        events((QUERY, (9, 12, 10, 13)))
        query_raw = total[QUERY]
        raw_ref[0] = query_raw
        exchange_rows(jnp.sum(query_raw * query_raw, axis=-1, keepdims=True), part_q, land_q, qs_s, qs_r, mates)
        for part in range(parts):
            weights[part, block_rows(line.block(0), depth), :] = own_w[part]
        keep = pltpu.make_async_copy(weights, w_all, out_sem)
        keep.start()
        keep_more = [
            pltpu.make_async_copy(h1_ref, h1_out, kept.at[2]),
            pltpu.make_async_copy(raw_ref, raw_out, kept.at[3]),
        ]
        for copy in keep_more:
            copy.start()
        events((GRAD, (3, 6)), (OUT, (9, 12, 3, 6)), (REST, (3, 6, 8, 11)))
        relay_four(0)
        query_scale = lax.rsqrt(exchanged_rows(part_q, land_q, qs_s, qs_r, mates) / width + EPS)
        scale_ref[:, 1:2] = query_scale

        def store_query(at, value):
            q_ref[:, at] = value

        rotated(QUERY, query_scale, store_query)
        events((GRAD, (8, 11, 9, 12)), (OUT, (10, 13)), (REST, (9, 12, 10, 13)), (GRAD, (10, 13)))
        for which in (1, 0):
            for k in (1, 3):
                context_take(which, k)
        for rel in line.order():
            def relay(rel=rel):
                b = line.block(rel)
                grad_across(b, True).wait_recv()
                grad_twin(b, 1).start()
            run_if(line.exists(rel), relay)
        for rel in line.order():
            def landed(rel=rel):
                b = line.block(rel)
                grad_across(b).wait_send()
                for relayed in range(2):
                    grad_twin(b, relayed, True).wait_recv()
                    grad_twin(b, relayed).wait_send()
            run_if(line.exists(rel), landed)
        line.finish()
        for copy in keep_more:
            copy.wait()
        wide_out.wait()
        down_copy.wait()
        keep_out.wait()
        keep_grad.wait()
        for which in range(2):
            for k in range(1, back + 1):
                run_if(sends[k], lambda which=which, k=k: context_copy(which, k).wait_send())
        drain_rows(part_k, land_k, ks_s, ks_r, mates)
        drain_rows(part_q, land_q, qs_s, qs_r, mates)
        keep.wait()

    shape, dma = jax.ShapeDtypeStruct, pltpu.SemaphoreType.DMA
    return pl.pallas_call(
        kernel,
        out_shape=(
            shape((parts, depth * GROUPS, columns), low),
            shape((out_rows, out_columns * GROUPS), low),
            shape((rows * GROUPS, width), low),
            shape((rows, width), low),
            shape((2, rows, columns), f32),
            shape((width, 4 * w_down.shape[1]), low),
            shape((2 * w_down.shape[1], width), low),
            shape((8, width), f32),
            shape((experts, width), low),
            shape((rows * GROUPS, experts), low),
            shape((rows, 128), f32),
            shape((rows, columns), low),
            shape((back + 1, 2, rows, columns), low),
        ),
        in_specs=[VMEM, VMEM, VMEM, HBM] + [VMEM] * 7 + [HBM, HBM, HBM],
        out_specs=(HBM,) * 7 + (VMEM,) * 6,
        scratch_shapes=[
            pltpu.VMEM(small_shape, f32),
            pltpu.VMEM((GROUPS,) + small_shape, f32),
            pltpu.VMEM((rows, width), low),
            pltpu.VMEM((2, rows, columns), f32),
            pltpu.VMEM((4, width, w_down.shape[1]), f32),
            pltpu.VMEM((width, 4 * w_down.shape[1]), low),
            pltpu.VMEM((2 * w_down.shape[1], width), f32),
            pltpu.VMEM((2 * w_down.shape[1], width), low),
            pltpu.VMEM((parts, depth, columns), low),
            pltpu.VMEM((out_rows, out_columns), low),
            pltpu.VMEM((parts, depth * GROUPS, columns), low),
            pltpu.VMEM((parts, rows, columns), f32),
            pltpu.VMEM((8, rows), f32),
            pltpu.VMEM((tensors - 1, 8, rows), f32),
            pltpu.VMEM((8, rows), f32),
            pltpu.VMEM((tensors - 1, 8, rows), f32),
            dma((7, 14, 3)), dma((7, 14)), dma, dma, dma((4,)),
            dma((tensors - 1,)), dma((tensors - 1,)), dma((tensors - 1,)), dma((tensors - 1,)),
            dma((2, back + 1)), dma((2, back + 1)),
            dma((GROUPS,)), dma((GROUPS,)), dma((GROUPS, 2)), dma((GROUPS, 2)), dma((4,)),
        ],
        compiler_params=comm_params(collective_id, 62),
        cost_estimate=cost(100),
        name="project",
    )(
        tokens, w_qkv, w_out, out_grad, gain_one, gain_two, qk_gain, w_router, routes, cosine, sine,
        w_gate, w_up, w_down,
    )


def attend(query, context, segment_query, segment_keys, tokens, out_low, gain, collective_id):
    rows, columns = query.shape
    width = tokens.shape[1]
    blocks = context.shape[0]
    heads = columns // HEAD
    half, quarter = width // 2, width // 4
    low, f32 = jnp.bfloat16, jnp.float32

    def kernel(
        q_ref, context_in, sq_ref, sk_ref, tok_ref, out_in, gain_ref,
        o_ref, lse_ref, x1_out, h2_out, scale_ref,
        context_ref, out_ref, x1_ref, h2_ref, copy_sem, part, full, core_buf, x_buf, send_sem, recv_sem,
    ):
        z, y, x, c = place()
        across, twin = device(z, y, 1 - x, c), device(z, y, x, 1 - c)
        context_load = pltpu.make_async_copy(context_in, context_ref, copy_sem.at[0])
        context_load.start()
        out_load = pltpu.make_async_copy(out_in, out_ref, copy_sem.at[1])
        out_load.start()
        greet([(across, None), (twin, None)])
        row = lax.broadcasted_iota(jnp.int32, (rows, rows), 0)
        column = lax.broadcasted_iota(jnp.int32, (rows, rows), 1)
        allowed = []
        for k in range(blocks):
            distance = row - column + k * rows
            allowed.append(
                (sq_ref[...] == sk_ref[k : k + 1, :]) & (distance >= 0) & (distance < WINDOW)
            )
        line = lax.broadcasted_iota(jnp.int32, (rows, 128), 1)
        lse = jnp.zeros((rows, 128), f32)
        context_load.wait()
        for head in range(heads):
            at = pl.ds(head * HEAD, HEAD)
            scores = [
                jnp.where(
                    allowed[k], dot(q_ref[:, at], context_ref[k, 0, :, at], (1, 1)) * HEAD ** (-0.5), -1e30
                )
                for k in range(blocks)
            ]
            largest = scores[0]
            for k in range(1, blocks):
                largest = jnp.maximum(largest, scores[k])
            largest = jnp.max(largest, axis=-1, keepdims=True)
            weights = [jnp.exp(s - largest) for s in scores]
            amount = weights[0]
            for k in range(1, blocks):
                amount = amount + weights[k]
            amount = jnp.sum(amount, axis=-1, keepdims=True)
            inverse = 1.0 / amount
            value = jnp.zeros((rows, HEAD), f32)
            for k in range(blocks):
                value = value + dot((weights[k] * inverse).astype(low), context_ref[k, 1, :, at], (1, 0))
            o_ref[:, at] = value.astype(low)
            lse = jnp.where(line == head, largest + jnp.log(amount), lse)
        lse_ref[...] = lse

        def half_of(cc):
            return pl.ds(pl.multiple_of(cc * half, half), half)

        def fill(cc):
            def body(k, carry):
                at = pl.ds(pl.multiple_of(cc * half + k * quarter, quarter), quarter)
                part[:, at] = dot(o_ref[...], out_ref[:, at], (1, 0)).astype(low)
                return carry

            lax.fori_loop(0, 2, body, 0)

        out_load.wait()
        fill(1 - c)
        group_sum(part, full, core_buf, x_buf, send_sem, recv_sem, lambda: fill(c))

        def norm(i, carry):
            r = pl.ds(pl.multiple_of(i * 32, 32), 32)
            value = tok_ref[r, :].astype(f32) + full[r, :].astype(f32)
            scale = lax.rsqrt(jnp.mean(value * value, axis=-1, keepdims=True) + EPS)
            x1_ref[r, :] = value
            scale_ref[r, :] = jnp.broadcast_to(scale, (32, 128))
            h2_ref[r, :] = (value * scale * gain_ref[1:2, :]).astype(low)
            return carry

        lax.fori_loop(0, rows // 32, norm, 0)
        keep = [
            pltpu.make_async_copy(x1_ref, x1_out, copy_sem.at[2]),
            pltpu.make_async_copy(h2_ref, h2_out, copy_sem.at[3]),
        ]
        for copy in keep:
            copy.start()
        for copy in keep:
            copy.wait()

    shape, dma = jax.ShapeDtypeStruct, pltpu.SemaphoreType.DMA
    return pl.pallas_call(
        kernel,
        out_shape=(
            shape((rows, columns), low),
            shape((rows, 128), f32),
            shape((rows, width), f32),
            shape((rows, width), low),
            shape((rows, 128), f32),
        ),
        in_specs=[VMEM, HBM, VMEM, VMEM, VMEM, HBM, VMEM],
        out_specs=(VMEM, VMEM, HBM, HBM, VMEM),
        scratch_shapes=[
            pltpu.VMEM(context.shape, low),
            pltpu.VMEM(out_low.shape, low),
            pltpu.VMEM((rows, width), f32),
            pltpu.VMEM((rows, width), low),
            dma((4,)),
            pltpu.VMEM((rows, width), low),
            pltpu.VMEM((rows, width), low),
            pltpu.VMEM((rows, half), low),
            pltpu.VMEM((rows, quarter), low),
            dma((5,)), dma((5,)),
        ],
        compiler_params=comm_params(collective_id, 62),
        cost_estimate=cost(40),
        name="attend",
    )(query, context, segment_query, segment_keys, tokens, out_low, gain)


def attend_back(
    grad_hidden, grad_probs, router_t, hidden_two, residual, scale_two, gains, out_grad,
    query, context, segment_query, segment_keys, attended, log_sums, raw, scales,
    cosine, sine, hidden_one, tokens, attended_all, qkv_low, out_low, collective_id,
):
    rows, width = tokens.shape
    columns = query.shape[1]
    heads = columns // HEAD
    experts = router_t.shape[0]
    blocks = context.shape[0]
    depth = width // GROUPS
    small_rows = 8 + experts
    tensors = NX * NC
    half, quarter = width // 2, width // 4
    low, f32 = jnp.bfloat16, jnp.float32
    QUERY, KEY, VALUE, OUT, SMALL = 0, 1, 2, 3, 4

    def kernel(
        dh_ref, gates_ref, router_ref, h2_ref, x1_ref, s2_ref, gain_ref, dy_ref,
        q_ref, context_in, sq_ref, sk_ref, o_ref, lse_ref, raw_in, scale_ref,
        cos_ref, sin_ref, h1_in, tok_in, o_all_in, w_hbm, out_ref,
        tok_grad, qkv_sum, out_sum, small_sum,
        context_ref, raw_ref, h1_ref, tok_ref, o_all, load_sem, weights, dx1, da, do, dot_sums, dq, dkv, scaled, proj, send_kv, land_y, land_z,
        part, full, core_buf, x_buf, small, line_sum,
        main_buf, da_all, small_buf, part_k, land_k, part_q, land_q,
        w_sem, y_s, y_r, z_s, z_r, group_s, group_r, ks_s, ks_r, qs_s, qs_r, line_s, line_r, far_s, far_r, near_s, near_r,
    ):
        z, y, x, c = place()
        e, t = lax.axis_index("expert"), lax.axis_index("tensor")
        mates = [(e, lax.rem(t + k, tensors)) for k in range(1, tensors)]
        beside, below = device(z, 1 - y, x, c), device(z - 1, y, x, c)
        fetch = pltpu.make_async_copy(w_hbm, weights, w_sem)
        fetch.start()
        loads = [
            pltpu.make_async_copy(source, target, load_sem.at[k])
            for k, (source, target) in enumerate(
                (
                    (context_in, context_ref), (raw_in, raw_ref), (h1_in, h1_ref), (tok_in, tok_ref),
                    (o_all_in, o_all),
                )
            )
        ]
        for copy in loads:
            copy.start()

        def own_part(s, b):
            if s == SMALL:
                return small[b]
            at = pl.ds(pl.multiple_of(b * depth, depth), depth)
            return dot(h1_ref[:, at], proj[s], (0, 0))

        peers = [(lax.rem(e + k, GROUPS), t) for k in range(1, GROUPS)]
        share = rows // tensors
        share_at = pl.ds(pl.multiple_of(t * share, share), share)

        def columns_of(owner):
            return pl.ds(pl.multiple_of(owner * depth, depth), depth)

        def da_far(k):
            owner = lax.rem(e + k, GROUPS)
            return remote(
                da.at[share_at, columns_of(owner)], da_all.at[e, share_at, :], far_s.at[k - 1], far_r.at[k - 1],
                peers[k - 1],
            )

        def da_near(k):
            piece = da_all.at[:, share_at, :]
            return remote(piece, piece, near_s.at[k], near_r.at[k], mates[k])

        def da_start():
            for k in range(1, GROUPS):
                da_far(k).start()
            da_all[e, share_at, :] = da[share_at, columns_of(e)]

        def da_spread():
            for k in range(1, GROUPS):
                landing = da_all.at[lax.rem(e + GROUPS - k, GROUPS), share_at, :]
                remote(landing, landing, far_s.at[k - 1], far_r.at[k - 1], peers[k - 1]).wait_recv()
            for k in range(tensors - 1):
                da_near(k).start()

        def da_end():
            for k in range(tensors - 1):
                theirs = lax.rem(t + tensors - 1 - k, tensors)
                landing = da_all.at[:, pl.ds(pl.multiple_of(theirs * share, share), share), :]
                remote(landing, landing, near_s.at[k], near_r.at[k], mates[k]).wait_recv()
            result = jnp.zeros((columns, depth), f32)
            for b in range(GROUPS):
                result = result + dot(o_all[pl.ds(b * rows, rows), :], da_all[b], (0, 0))
            out_sum[...] = result
            for k in range(1, GROUPS):
                da_far(k).wait_send()
            for k in range(tensors - 1):
                da_near(k).wait_send()

        def slot(kind):
            def view(s, zz):
                if s == SMALL:
                    return small_buf.at[kind, zz]
                return main_buf.at[kind, zz, s]
            return view

        line = LineReduce([], lambda s, zz, yy: slot(3)(s, zz), slot(0), slot(1), slot(2), line_s, line_r)
        greet([(target, None) for target in mates + peers])

        grad_probs = gates_ref[...]
        logits = dot(h2_ref[...], router_ref[...], (1, 1))
        shifted = jnp.exp(logits - jnp.max(logits, axis=-1, keepdims=True))
        probs = shifted / jnp.sum(shifted, axis=-1, keepdims=True)
        grad_logits = probs * (grad_probs - jnp.sum(probs * grad_probs, axis=-1, keepdims=True))
        tall = jnp.transpose(
            jnp.concatenate([grad_logits, jnp.zeros((rows, 128 - experts), f32)], axis=1)
        )
        grad_logits = grad_logits.astype(low)
        tall = tall.astype(low)
        for b in range(GROUPS):
            small[b] = jnp.zeros_like(small[b])
            small[b, 8 : 8 + experts, :] = dot(tall, h2_ref[:, pl.ds(b * depth, depth)], (1, 0))[:experts]
        dx1[...] = dot(grad_logits, router_ref[...], (1, 0))
        line_sum[...] = jnp.zeros_like(line_sum)

        def norm_two(i, carry):
            r = pl.ds(pl.multiple_of(i * 32, 32), 32)
            grad = dh_ref[r, :].astype(f32) + dx1[r, :]
            value, scale = x1_ref[r, :], s2_ref[r, 0:1]
            line_sum[0:1, :] += jnp.sum(grad * (value * scale), axis=0, keepdims=True)
            grad = grad * gain_ref[1:2, :]
            inner = jnp.mean(grad * value, axis=-1, keepdims=True)
            result = dy_ref[r, :].astype(f32) + scale * grad - value * (scale * scale * scale) * inner
            dx1[r, :] = result
            da[r, :] = result.astype(low)
            return carry

        lax.fori_loop(0, rows // 32, norm_two, 0)

        da_start()

        for copy in loads:
            copy.wait()
        do[...] = dot(da[...], out_ref[...], (1, 1)).astype(low)
        wide = lax.broadcasted_iota(jnp.int32, (rows, 128), 1)
        sums = jnp.zeros((rows, 128), f32)
        for head in range(heads):
            at = pl.ds(head * HEAD, HEAD)
            inner = jnp.sum(do[:, at].astype(f32) * o_ref[:, at].astype(f32), axis=-1, keepdims=True)
            sums = jnp.where(wide == head, inner, sums)
        dot_sums[...] = sums
        dq[...] = jnp.zeros_like(dq)
        row = lax.broadcasted_iota(jnp.int32, (rows, rows), 0)
        column = lax.broadcasted_iota(jnp.int32, (rows, rows), 1)

        def attention_block(k):
            distance = row - column + k * rows
            allowed = (sq_ref[...] == sk_ref[k : k + 1, :]) & (distance >= 0) & (distance < WINDOW)
            for head in range(heads):
                at = pl.ds(head * HEAD, HEAD)
                queries, keys, values = q_ref[:, at], context_ref[k, 0, :, at], context_ref[k, 1, :, at]
                scores = dot(queries, keys, (1, 1)) * HEAD ** (-0.5)
                weight = jnp.where(allowed, jnp.exp(scores - lse_ref[:, head : head + 1]), 0.0)
                grad_weight = dot(do[:, at], values, (1, 1))
                grad_score = (
                    weight * (grad_weight - dot_sums[:, head : head + 1]) * HEAD ** (-0.5)
                ).astype(low)
                dq[:, at] += dot(grad_score, keys, (1, 0))
                dkv[k, 0, :, at] = dot(grad_score, queries, (0, 0))
                dkv[k, 1, :, at] = dot(weight.astype(low), do[:, at], (0, 0))

        exists = {0: None, 1: (y == 1) | (z >= 1), 2: z >= 1, 3: z >= 2 - y, 4: z >= 2}
        comes = {1: (y == 0) | (z >= 1), 3: z >= 1 + y}

        def kv_copy(which, k):
            if k in (1, 3):
                landing, target = land_y.at[k // 2, which], beside
                return remote(send_kv.at[k - 1, which], landing, y_s.at[k // 2, which], y_r.at[k // 2, which], target)
            landing = land_z.at[k // 2 - 1, which]
            return remote(
                send_kv.at[k - 1, which], landing, z_s.at[k // 2 - 1, which], z_r.at[k // 2 - 1, which], below
            )

        def kv_send(which, k):
            send_kv[k - 1, which] = dkv[k, which].astype(low)
            kv_copy(which, k).start()

        def merge(into, which, landed):
            add_to(dkv.at[into, which], dkv.at[into, which], landed, 32)

        for k in (3, 1, 4, 2, 0):
            def one(k=k):
                attention_block(k)
                if k in (1, 3):
                    kv_send(1, k)
                    kv_send(0, k)
            run_if(exists[k], one)

        def take_three(which):
            def land():
                kv_copy(which, 3).wait_recv()
                pl.when(y == 1)(lambda: merge(4, which, land_y.at[1, which]))
                pl.when(y == 0)(lambda: merge(2, which, land_y.at[1, which]))
            run_if(comes[3], land)
            run_if(exists[4], lambda: kv_send(which, 4))

        def take_one(which):
            def land():
                kv_copy(which, 1).wait_recv()
                pl.when(y == 1)(lambda: merge(2, which, land_y.at[0, which]))
                pl.when(y == 0)(lambda: merge(0, which, land_y.at[0, which]))
            run_if(comes[1], land)

        def take_four(which):
            def land():
                kv_copy(which, 4).wait_recv()
                merge(2, which, land_z.at[1, which])
            run_if((z >= 1) & (z < NZ - 1), land)
            run_if(exists[2], lambda: kv_send(which, 2))

        def take_two(which):
            def land():
                kv_copy(which, 2).wait_recv()
                merge(0, which, land_z.at[0, which])
            run_if(z < NZ - 1, land)

        def unturn(which, grad_of):
            inner = jnp.zeros((rows, 1), f32)
            for head in range(heads):
                at = pl.ds(head * HEAD, HEAD)
                grad = turn(grad_of(at), cos_ref[...], -sin_ref[...])
                value = raw_ref[which, :, at]
                line_sum[1 + which : 2 + which, at] = jnp.sum(
                    grad * (value * scale_ref[:, 1 + which : 2 + which]), axis=0, keepdims=True
                )
                grad = grad * gain_ref[2 + which : 3 + which, at]
                scaled[which, :, at] = grad
                inner = inner + jnp.sum(grad * value, axis=-1, keepdims=True)
            return inner

        def denorm(which, inner):
            scale = scale_ref[:, 1 + which : 2 + which]
            rest = scale * scale * scale * inner / width
            for head in range(heads):
                at = pl.ds(head * HEAD, HEAD)
                proj[which, :, at] = (
                    scale * scaled[which, :, at] - raw_ref[which, :, at] * rest
                ).astype(low)

        def send_beside(s):
            for zz in Z_ORDER:
                buffer = slot(3)(s, zz)
                buffer[...] = own_part(s, zz * NY + 1 - y).astype(buffer.dtype)
                line.to_y(s, zz)

        exchange_rows(unturn(QUERY, lambda at: dq[:, at]), part_q, land_q, qs_s, qs_r, mates)
        take_three(1)
        take_three(0)
        denorm(QUERY, exchanged_rows(part_q, land_q, qs_s, qs_r, mates))
        send_beside(QUERY)
        da_spread()
        take_one(1)
        take_one(0)
        take_four(1)
        take_four(0)
        take_two(1)
        proj[VALUE] = dkv[0, 1].astype(low)
        send_beside(VALUE)
        take_two(0)
        exchange_rows(unturn(KEY, lambda at: dkv[0, 0, :, at]), part_k, land_k, ks_s, ks_r, mates)
        denorm(KEY, exchanged_rows(part_k, land_k, ks_s, ks_r, mates))
        send_beside(KEY)
        fetch.wait()

        def half_of(cc):
            def body(i, carry):
                at = pl.ds(pl.multiple_of(cc * half + i * quarter, quarter), quarter)
                value = dot(proj[0], weights[0, at, :], (1, 1))
                for s in (1, 2):
                    value = value + dot(proj[s], weights[s, at, :], (1, 1))
                part[:, at] = value.astype(low)
                return carry

            lax.fori_loop(0, 2, body, 0)

        stages = group_stages(part, full, core_buf, x_buf, group_s, group_r)
        half_of(1 - c)
        stages[0]()
        half_of(c)
        stages[1]()

        def hop(s, zz, k):
            def upward():
                if k > 0:
                    line.take(s, zz, 1)
                line.copy(s, zz, 1).start()

            def downward():
                if k > 0:
                    line.take(s, zz, 2)
                line.copy(s, zz, 2).start()

            if k < zz:
                run_if((z < zz) & (z == k), upward)
            if NZ - 1 - k > zz:
                run_if((z > zz) & (NZ - 1 - z == k), downward)

        def receive(s, zz):
            line.copy(s, zz, 0).wait_recv()
            buffer = slot(0)(s, zz)
            buffer[...] = (buffer[...].astype(f32) + own_part(s, zz * NY + y)).astype(buffer.dtype)

        units = []

        def run_units(s):
            for zz in Z_ORDER:
                receive(s, zz)
                hop(s, zz, 0)
                units.append((s, zz))
                for k in (1, 2):
                    if len(units) > k:
                        hop(*units[-1 - k], k)

        def norm_one(i, carry):
            r = pl.ds(pl.multiple_of(i * 32, 32), 32)
            grad, value, scale = full[r, :].astype(f32), tok_ref[r, :].astype(f32), scale_ref[r, 0:1]
            line_sum[3:4, :] += jnp.sum(grad * (value * scale), axis=0, keepdims=True)
            grad = grad * gain_ref[0:1, :]
            inner = jnp.mean(grad * value, axis=-1, keepdims=True)
            tok_grad[r, :] = (
                dx1[r, :] + scale * grad - value * (scale * scale * scale) * inner
            ).astype(low)
            return carry

        run_units(QUERY)
        stages[2]()
        run_units(VALUE)
        da_end()
        stages[3]()
        stages[4]()
        lax.fori_loop(0, rows // 32, norm_one, 0)
        for b in range(GROUPS):
            at = pl.ds(b * depth, depth)
            small[b, 0:1, :] = line_sum[3:4, at]
            small[b, 1:2, :] = line_sum[0:1, at]
            for which in range(2):
                for k in range(columns // depth):
                    small[b, 2 + 2 * which + k : 3 + 2 * which + k, :] = line_sum[
                        1 + which : 2 + which, pl.ds(k * depth, depth)
                    ]
        send_beside(SMALL)
        run_units(KEY)
        run_units(SMALL)
        hop(*units[-1], 1)
        hop(*units[-2], 2)
        hop(*units[-1], 2)

        def done(s, total):
            target = qkv_sum.at[s] if s < OUT else small_sum
            target[...] = total[...].astype(f32)

        line.streams = [QUERY, VALUE, KEY, SMALL]
        line.home(done)
        line.finish()
        for which in range(2):
            for k in (1, 2, 3, 4):
                run_if(exists[k], lambda which=which, k=k: kv_copy(which, k).wait_send())
        drain_rows(part_k, land_k, ks_s, ks_r, mates)
        drain_rows(part_q, land_q, qs_s, qs_r, mates)

    shape, dma, vmem = jax.ShapeDtypeStruct, pltpu.SemaphoreType.DMA, pltpu.VMEM
    return pl.pallas_call(
        kernel,
        out_shape=(
            shape((rows, width), low),
            shape((3, depth, columns), f32),
            shape((columns, depth), f32),
            shape((small_rows, depth), f32),
        ),
        in_specs=[HBM if k in (9, 14, 18, 19, 20, 21) else VMEM for k in range(23)],
        out_specs=(VMEM,) * 4,
        scratch_shapes=[
            vmem(context.shape, low),
            vmem(raw.shape, f32),
            vmem(hidden_one.shape, low),
            vmem(tokens.shape, low),
            vmem(attended_all.shape, low),
            dma((5,)),
            vmem(qkv_low.shape, low),
            vmem((rows, width), f32),
            vmem((rows, width), low),
            vmem((rows, columns), low),
            vmem((rows, 128), f32),
            vmem((rows, columns), f32),
            vmem((blocks, 2, rows, columns), f32),
            vmem((2, rows, columns), f32),
            vmem((3, rows, columns), low),
            vmem((blocks - 1, 2, rows, columns), low),
            vmem((2, 2, rows, columns), low),
            vmem((2, 2, rows, columns), low),
            vmem((rows, width), low),
            vmem((rows, width), low),
            vmem((rows, half), low),
            vmem((rows, quarter), low),
            vmem((GROUPS, small_rows, depth), f32),
            vmem((8, width), f32),
            vmem((4, NZ, 3, depth, columns), low),
            vmem((GROUPS, rows, depth), low),
            vmem((4, NZ, small_rows, depth), f32),
            vmem((8, rows), f32),
            vmem((tensors - 1, 8, rows), f32),
            vmem((8, rows), f32),
            vmem((tensors - 1, 8, rows), f32),
            dma, dma((2, 2)), dma((2, 2)), dma((2, 2)), dma((2, 2)), dma((5,)), dma((5,)),
            dma((tensors - 1,)), dma((tensors - 1,)), dma((tensors - 1,)), dma((tensors - 1,)),
            dma((5, NZ, 3)), dma((5, NZ, 3)), dma((GROUPS - 1,)), dma((GROUPS - 1,)), dma((tensors - 1,)), dma((tensors - 1,)),
        ],
        compiler_params=comm_params(collective_id, 62),
        cost_estimate=cost(130),
        name="attend_back",
    )(
        grad_hidden, grad_probs, router_t, hidden_two, residual, scale_two, gains, out_grad,
        query, context, segment_query, segment_keys, attended, log_sums, raw, scales,
        cosine, sine, hidden_one, tokens, attended_all, qkv_low, out_low,
    )


def fast_shards(
    tokens_in,
    out_grad,
    w_qkv,
    w_attn_out,
    attn_gain,
    ffn_gain,
    qk_gain,
    w_router,
    w_gate,
    w_up,
    w_down,
    routes,
    segments,
):
    row_count, model_width = tokens_in.shape
    experts = w_router.shape[1]
    local_experts = w_gate.shape[0]
    heads_here = qk_gain.shape[1]
    local_width = heads_here * HEAD
    groups = lax.axis_size("expert")
    device_index = lax.axis_index("expert")
    tensor_index = lax.axis_index("tensor")
    quarter = model_width // lax.axis_size("tensor")
    hop_count = WINDOW // row_count
    score_scale = HEAD ** (-0.5)
    low = jnp.bfloat16

    chosen = jnp.any(
        routes[:, :, None] == jnp.arange(experts, dtype=jnp.int32)[None, None, :], axis=1
    ).astype(jnp.float32)
    qk_row = qk_gain.reshape(1, -1)

    global_rows = device_index * row_count + jnp.arange(row_count, dtype=jnp.int32)
    cosine_table, sine_table = angles(global_rows % SEQ, HEAD)
    wide_cosine = jnp.concatenate([cosine_table[:, 0], cosine_table[:, 0]], axis=1)
    wide_sine = jnp.concatenate([-sine_table[:, 0], sine_table[:, 0]], axis=1)
    (
        qkv_low, out_low, grad_out_all, hidden_one, raw, gate_up, down_low, gains, router_t, chosen_all,
        scales, query_low, context_blocks,
    ) = project(
        tokens_in, w_qkv, w_attn_out, out_grad, attn_gain[None, :], ffn_gain[None, :], qk_row, w_router.T, routes.T,
        wide_cosine, wide_sine, w_gate, w_up, w_down, 0,
    )
    segment_window = lax.dynamic_slice_in_dim(
        jnp.concatenate([jnp.full((WINDOW,), -1, jnp.int32), segments]),
        device_index * row_count, (hop_count + 1) * row_count,
    )
    segment_query = segment_window[WINDOW:]
    segment_keys = segment_window.reshape(hop_count + 1, row_count)[::-1]
    attended, log_sums, residual, hidden_two, scale_two_wide = attend(
        query_low, context_blocks, segment_query[:, None], segment_keys, tokens_in, out_low,
        gains, 2,
    )
    (
        block_out, grad_hidden_sum, grad_gate_sum, grad_gate_w, grad_up_w, grad_down, attended_all
    ) = expert_layer(
        hidden_two, grad_out_all, gate_up, down_low, router_t, chosen_all, residual, attended, 5
    )
    grad_probs = grad_gate_sum[:, :local_experts].reshape(experts, row_count).T * chosen
    grad_tokens, qkv_sum, out_sum, small_sum = attend_back(
        grad_hidden_sum, grad_probs, router_t, hidden_two, residual, scale_two_wide,
        gains, out_grad, query_low, context_blocks, segment_query[:, None], segment_keys,
        attended, log_sums, raw, scales, wide_cosine, wide_sine, hidden_one, tokens_in, attended_all,
        qkv_low, out_low, 8,
    )
    return (
        block_out,
        grad_tokens,
        qkv_sum,
        out_sum,
        small_sum[0],
        small_sum[1],
        lax.dynamic_slice_in_dim(
            small_sum[2:6].reshape(2, heads_here, HEAD),
            device_index * qk_gain.shape[2], qk_gain.shape[2], axis=2,
        ),
        small_sum[8 : 8 + experts].T,
        grad_gate_w,
        grad_up_w,
        grad_down,
    )


def solution(mesh):
    placed = (
        P("expert", None),
        P("expert", None),
        P(None, "expert", "tensor"),
        P("tensor", "expert"),
        P("expert"),
        P("expert"),
        P(None, "tensor", "expert"),
        P("expert", None),
        P("expert", None, "tensor"),
        P("expert", None, "tensor"),
        P("expert", "tensor", None),
        P("expert", None),
        P(),
    )
    compact = (mesh.shape["expert"], mesh.shape["tensor"]) == (GROUPS, NX * NC)
    return jax.shard_map(
        fast_shards if compact else shards,
        mesh=mesh,
        in_specs=placed,
        out_specs=(
            P("expert", None),
            P("expert", None),
            P(None, "expert", "tensor"),
            P("tensor", "expert"),
            P("expert"),
            P("expert"),
            P(None, "tensor", "expert"),
            P("expert", None),
            P("expert", None, "tensor"),
            P("expert", None, "tensor"),
            P("expert", "tensor", None),
        ),
        check_vma=False,
    )
```

```python
import jax
import jax.numpy as jnp
from jax import lax
from jax.experimental import pallas as pl
from jax.experimental.pallas import tpu as pltpu
from jax.sharding import PartitionSpec as P

HEAD = 128
WINDOW = 1024
SEQ = 2048


EPS = 1e-05
THETA = 10000.0


def from_behind(value, axis, steps):
    count = lax.axis_size(axis)
    initial, last = (max(0, -steps), min(count, count - steps))
    return lax.ppermute(value, axis, [(source, source + steps) for source in range(initial, last)])


def angles(position, head_size):
    half_size = head_size // 2
    frequency = THETA ** (-(jnp.arange(half_size, dtype=jnp.float32) * 2.0 / head_size))
    phase_angle = position.astype(jnp.float32)[:, None] * frequency[None, :]
    return (jnp.cos(phase_angle)[:, None, :], jnp.sin(phase_angle)[:, None, :])


def rotate(rotated_in, cosine_table, sine_table):
    half_size = rotated_in.shape[-1] // 2
    first_half = rotated_in[..., :half_size]
    second_half = rotated_in[..., half_size:]
    return jnp.concatenate(
        [
            first_half * cosine_table - second_half * sine_table,
            second_half * cosine_table + first_half * sine_table,
        ],
        axis=-1,
    )


def slot_layout(block_routes, experts, capacity):
    flat_routes = block_routes.reshape(-1)
    onehot = (flat_routes[:, None] == jnp.arange(experts, dtype=jnp.int32)[None, :]).astype(
        jnp.int32
    )
    before = jnp.cumsum(onehot, axis=0) - onehot
    rank_within = jnp.sum(before * onehot, axis=1)
    slot_index = flat_routes * capacity + rank_within
    slot_table = (
        jnp.zeros((experts * capacity,), jnp.int32)
        .at[slot_index]
        .set(jnp.arange(flat_routes.shape[0], dtype=jnp.int32) + 1)
    )
    return (slot_index, slot_table)


def shards(
    tokens_in,
    out_grad,
    w_qkv,
    w_attn_out,
    attn_gain,
    ffn_gain,
    qk_gain,
    w_router,
    w_gate,
    w_up,
    w_down,
    routes,
    segments,
):
    row_count, model_width = tokens_in.shape
    experts = w_router.shape[1]
    per_token = routes.shape[1]
    local_experts = w_gate.shape[0]
    heads_here = qk_gain.shape[1]
    local_width = heads_here * HEAD
    groups = lax.axis_size("expert")
    device = lax.axis_index("expert")
    capacity = row_count * per_token * 3 // (2 * experts)
    hop_count = WINDOW // row_count
    buffer_shape = (groups, local_experts, capacity, model_width)
    score_scale = HEAD ** (-0.5)

    def fetch_weights():
        return (
            lax.all_gather(w_qkv.astype(jnp.bfloat16), "expert", axis=1, tiled=True),
            lax.all_gather(w_attn_out.astype(jnp.bfloat16), "expert", axis=1, tiled=True),
            lax.all_gather(w_router.astype(jnp.bfloat16), "expert", axis=0, tiled=True),
            lax.all_gather(attn_gain.astype(jnp.bfloat16), "expert", axis=0, tiled=True),
            lax.all_gather(ffn_gain.astype(jnp.bfloat16), "expert", axis=0, tiled=True),
            lax.all_gather(qk_gain.astype(jnp.bfloat16), "expert", axis=2, tiled=True),
        )

    def prepare(pieces):
        return (
            pieces[0],
            pieces[1],
            pieces[2],
            pieces[3].astype(jnp.float32),
            pieces[4].astype(jnp.float32),
            pieces[5].astype(jnp.float32).reshape(2, local_width),
        )

    qkv_low, out_low, router_low, gain_one_f, gain_two_f, qk_gains = prepare(fetch_weights())
    tokens_f = tokens_in.astype(jnp.float32)
    scale_one = lax.rsqrt(jnp.mean(tokens_f * tokens_f, axis=-1, keepdims=True) + EPS)
    hidden_one = (tokens_f * scale_one * gain_one_f).astype(jnp.bfloat16)
    projected = jnp.einsum("td,jde->jte", hidden_one, qkv_low, preferred_element_type=jnp.float32)
    query_raw = projected[0]
    key_raw = projected[1]
    query_sq, key_sq = lax.psum(
        (jnp.sum(query_raw * query_raw, axis=-1), jnp.sum(key_raw * key_raw, axis=-1)), "tensor"
    )
    query_scale = lax.rsqrt(query_sq / model_width + EPS)[:, None]
    key_scale = lax.rsqrt(key_sq / model_width + EPS)[:, None]
    normed_query = query_raw * query_scale
    normed_key = key_raw * key_scale
    global_rows = device * row_count + jnp.arange(row_count, dtype=jnp.int32)
    cosine_table, sine_table = angles(global_rows % SEQ, HEAD)
    query_low = rotate(
        (normed_query * qk_gains[0]).reshape(row_count, heads_here, HEAD), cosine_table, sine_table
    ).astype(jnp.bfloat16)
    key_low = rotate(
        (normed_key * qk_gains[1]).reshape(row_count, heads_here, HEAD), cosine_table, sine_table
    ).astype(jnp.bfloat16)
    value_low = projected[2].astype(jnp.bfloat16).reshape(row_count, heads_here, HEAD)
    own_pair = jnp.stack([key_low, value_low])
    earlier = []
    for steps_back in range(hop_count, 0, -1):
        earlier.append(from_behind(own_pair, "expert", steps_back))
    context = jnp.concatenate(earlier + [own_pair], axis=1)
    key_rows = (device - hop_count) * row_count + jnp.arange(
        (hop_count + 1) * row_count, dtype=jnp.int32
    )
    segment_keys = segments[jnp.maximum(key_rows, 0)]
    segment_query = segments[global_rows]
    distance = global_rows[:, None] - key_rows[None, :]
    allowed = (
        (key_rows[None, :] >= 0)
        & (segment_query[:, None] == segment_keys[None, :])
        & (distance >= 0)
        & (distance < WINDOW)
    )

    def score_block():
        raw_scores = (
            jnp.einsum("qhd,khd->hqk", query_low, context[0], preferred_element_type=jnp.float32)
            * score_scale
        )
        return jnp.where(allowed[None], raw_scores, -1e30)

    scores = score_block()
    largest = jnp.max(scores, axis=-1, keepdims=True)
    exp_scores = jnp.exp(scores - largest)
    exp_total = jnp.sum(exp_scores, axis=-1, keepdims=True)
    log_total = largest + jnp.log(exp_total)
    attn_probs = (exp_scores / exp_total).astype(jnp.bfloat16)
    attended = (
        jnp.einsum("hqk,khd->qhd", attn_probs, context[1], preferred_element_type=jnp.float32)
        .reshape(row_count, local_width)
        .astype(jnp.bfloat16)
    )
    attention_out = lax.psum(
        jnp.dot(attended, out_low, preferred_element_type=jnp.float32).astype(jnp.bfloat16),
        "tensor",
    ).astype(jnp.float32)
    residual = tokens_f + attention_out
    scale_two = lax.rsqrt(jnp.mean(residual * residual, axis=-1, keepdims=True) + EPS)
    normed_two = residual * scale_two
    hidden_two = (normed_two * gain_two_f).astype(jnp.bfloat16)
    logits = jnp.dot(hidden_two, router_low, preferred_element_type=jnp.float32)
    logit_exp = jnp.exp(logits - jnp.max(logits, axis=-1, keepdims=True))
    router_probs = logit_exp / jnp.sum(logit_exp, axis=-1, keepdims=True)
    chosen = routes[:, :, None] == jnp.arange(experts, dtype=jnp.int32)[None, None, :]
    gate_probs = jnp.sum(jnp.where(chosen, router_probs[:, None, :], 0.0), axis=-1)
    slot_index, slot_table = slot_layout(routes, experts, capacity)
    present = (slot_table > 0)[:, None]
    assigned = jnp.maximum(slot_table - 1, 0)
    row_of_slot = assigned // per_token
    gate_low = w_gate.astype(jnp.bfloat16)
    up_low = w_up.astype(jnp.bfloat16)
    down_low = w_down.astype(jnp.bfloat16)

    def send_rows():
        buffer_rows = jnp.where(
            present, hidden_two[row_of_slot], jnp.zeros((), jnp.bfloat16)
        ).reshape(buffer_shape)
        return lax.all_to_all(buffer_rows, "expert", split_axis=0, concat_axis=0, tiled=True)

    def expert_front(arrived):
        gate_pre = jnp.einsum(
            "secd,edh->sech", arrived, gate_low, preferred_element_type=jnp.float32
        )
        up_pre = jnp.einsum("secd,edh->sech", arrived, up_low, preferred_element_type=jnp.float32)
        return (gate_pre, up_pre)

    received = send_rows()
    gate_pre, up_pre = expert_front(received)
    activated = (gate_pre * jax.nn.sigmoid(gate_pre) * up_pre).astype(jnp.bfloat16)
    partial_value = jnp.einsum(
        "sech,ehd->secd", activated, down_low, preferred_element_type=jnp.float32
    ).astype(jnp.bfloat16)
    returned = lax.all_to_all(
        partial_value, "expert", split_axis=0, concat_axis=0, tiled=True
    ).reshape(experts * capacity, model_width)
    expert_rows = returned[slot_index].reshape(row_count, per_token, model_width)
    expert_part = jnp.einsum(
        "tk,tkd->td", gate_probs, expert_rows, preferred_element_type=jnp.float32
    )
    block_out = residual + lax.psum(expert_part.astype(jnp.bfloat16), "tensor").astype(jnp.float32)
    qkv_low, out_low, router_low, gain_one_f, gain_two_f, qk_gains = prepare(fetch_weights())
    grad_out = out_grad.astype(jnp.float32)
    grad_gate_part = jnp.einsum(
        "td,tkd->tk", grad_out, expert_rows, preferred_element_type=jnp.float32
    )
    slot_grads = (
        (gate_probs[:, :, None] * grad_out[:, None, :])
        .astype(jnp.bfloat16)
        .reshape(row_count * per_token, model_width)
    )
    grad_buffer = jnp.where(present, slot_grads[assigned], jnp.zeros((), jnp.bfloat16)).reshape(
        buffer_shape
    )
    grad_received = lax.all_to_all(grad_buffer, "expert", split_axis=0, concat_axis=0, tiled=True)
    received = send_rows()
    gate_pre, up_pre = expert_front(received)
    sigmoid_gate = jax.nn.sigmoid(gate_pre)
    swish_gate = gate_pre * sigmoid_gate
    activated = (swish_gate * up_pre).astype(jnp.bfloat16)
    grad_act = jnp.einsum(
        "secd,ehd->sech", grad_received, down_low, preferred_element_type=jnp.float32
    )
    grad_down = jnp.einsum(
        "sech,secd->ehd", activated, grad_received, preferred_element_type=jnp.float32
    )
    grad_gate_pre = (
        grad_act * up_pre * sigmoid_gate * (1.0 + gate_pre * (1.0 - sigmoid_gate))
    ).astype(jnp.bfloat16)
    grad_up_pre = (grad_act * swish_gate).astype(jnp.bfloat16)
    grad_gate_w = jnp.einsum(
        "secd,sech->edh", received, grad_gate_pre, preferred_element_type=jnp.float32
    )
    grad_up_w = jnp.einsum(
        "secd,sech->edh", received, grad_up_pre, preferred_element_type=jnp.float32
    )
    grad_rows = (
        jnp.einsum("sech,edh->secd", grad_gate_pre, gate_low, preferred_element_type=jnp.float32)
        + jnp.einsum("sech,edh->secd", grad_up_pre, up_low, preferred_element_type=jnp.float32)
    ).astype(jnp.bfloat16)
    grad_back = lax.all_to_all(
        grad_rows, "expert", split_axis=0, concat_axis=0, tiled=True
    ).reshape(experts * capacity, model_width)
    grad_hidden_part = jnp.sum(
        grad_back[slot_index].reshape(row_count, per_token, model_width), axis=1, dtype=jnp.float32
    )
    grad_hidden_sum, grad_gates = (
        lax.psum(grad_hidden_part.astype(jnp.bfloat16), "tensor").astype(jnp.float32),
        lax.psum(grad_gate_part.astype(jnp.bfloat16), "tensor").astype(jnp.float32),
    )
    grad_probs = jnp.sum(jnp.where(chosen, grad_gates[:, :, None], 0.0), axis=1)
    grad_logits = (
        router_probs * (grad_probs - jnp.sum(router_probs * grad_probs, axis=-1, keepdims=True))
    ).astype(jnp.bfloat16)
    grad_hidden_two = grad_hidden_sum + jnp.dot(
        grad_logits, router_low.T, preferred_element_type=jnp.float32
    )
    grad_router = jnp.dot(hidden_two.T, grad_logits, preferred_element_type=jnp.float32)
    grad_gain_two = jnp.sum(grad_hidden_two * normed_two, axis=0)
    scaled_two = grad_hidden_two * gain_two_f
    grad_residual = (
        grad_out
        + scale_two * scaled_two
        - residual
        * (scale_two * scale_two * scale_two)
        * jnp.mean(scaled_two * residual, axis=-1, keepdims=True)
    )
    grad_attn = grad_residual.astype(jnp.bfloat16)
    grad_out_w = jnp.dot(attended.T, grad_attn, preferred_element_type=jnp.float32)
    grad_attended = (
        jnp.dot(grad_attn, out_low.T, preferred_element_type=jnp.float32)
        .astype(jnp.bfloat16)
        .reshape(row_count, heads_here, HEAD)
    )
    attn_weights = jnp.where(allowed[None], jnp.exp(score_block() - log_total), 0.0)
    grad_weights = jnp.einsum(
        "qhd,khd->hqk", grad_attended, context[1], preferred_element_type=jnp.float32
    )
    inner_sum = jnp.sum(attn_weights * grad_weights, axis=-1, keepdims=True)
    grad_scores = (attn_weights * (grad_weights - inner_sum) * score_scale).astype(jnp.bfloat16)
    grad_query = jnp.einsum(
        "hqk,khd->qhd", grad_scores, context[0], preferred_element_type=jnp.float32
    )
    grad_keys = jnp.einsum(
        "hqk,qhd->khd", grad_scores, query_low, preferred_element_type=jnp.float32
    )
    grad_values = jnp.einsum(
        "hqk,qhd->khd",
        attn_weights.astype(jnp.bfloat16),
        grad_attended,
        preferred_element_type=jnp.float32,
    )
    grad_pair = jnp.stack([grad_keys, grad_values]).reshape(
        2, hop_count + 1, row_count, heads_here, HEAD
    )
    own_grad = grad_pair[:, hop_count]
    for steps_back in range(1, hop_count + 1):
        own_grad = own_grad + from_behind(
            grad_pair[:, hop_count - steps_back].astype(jnp.bfloat16), "expert", -steps_back
        ).astype(jnp.float32)
    grad_query_norm = rotate(grad_query, cosine_table, -sine_table).reshape(row_count, local_width)
    grad_key_norm = rotate(own_grad[0], cosine_table, -sine_table).reshape(row_count, local_width)
    grad_gain_query = jnp.sum(grad_query_norm * normed_query, axis=0)
    grad_gain_key = jnp.sum(grad_key_norm * normed_key, axis=0)
    scaled_query = grad_query_norm * qk_gains[0]
    scaled_key = grad_key_norm * qk_gains[1]
    query_inner, key_inner = lax.psum(
        (jnp.sum(scaled_query * query_raw, axis=-1), jnp.sum(scaled_key * key_raw, axis=-1)),
        "tensor",
    )
    grad_query_raw = (
        query_scale * scaled_query
        - query_raw * (query_scale * query_scale * query_scale) * query_inner[:, None] / model_width
    ).astype(jnp.bfloat16)
    grad_key_raw = (
        key_scale * scaled_key
        - key_raw * (key_scale * key_scale * key_scale) * key_inner[:, None] / model_width
    ).astype(jnp.bfloat16)
    grad_value_raw = own_grad[1].reshape(row_count, local_width).astype(jnp.bfloat16)
    grad_proj = jnp.stack([grad_query_raw, grad_key_raw, grad_value_raw])
    grad_qkv = jnp.einsum("td,jte->jde", hidden_one, grad_proj, preferred_element_type=jnp.float32)
    grad_hidden_one = lax.psum(
        jnp.einsum("jte,jde->td", grad_proj, qkv_low, preferred_element_type=jnp.float32).astype(
            jnp.bfloat16
        ),
        "tensor",
    ).astype(jnp.float32)
    grad_gain_one = jnp.sum(grad_hidden_one * tokens_f * scale_one, axis=0)
    scaled_one = grad_hidden_one * gain_one_f
    grad_tokens = (
        grad_residual
        + scale_one * scaled_one
        - tokens_f
        * (scale_one * scale_one * scale_one)
        * jnp.mean(scaled_one * tokens_f, axis=-1, keepdims=True)
    )
    grad_qk = jnp.stack([grad_gain_query, grad_gain_key]).reshape(2, heads_here, HEAD)
    reduced = (
        lax.psum_scatter(
            grad_qkv.astype(jnp.bfloat16), "expert", scatter_dimension=1, tiled=True
        ).astype(jnp.float32),
        lax.psum_scatter(
            grad_out_w.astype(jnp.bfloat16), "expert", scatter_dimension=1, tiled=True
        ).astype(jnp.float32),
        lax.psum_scatter(
            grad_router.astype(jnp.bfloat16), "expert", scatter_dimension=0, tiled=True
        ).astype(jnp.float32),
        lax.psum_scatter(
            grad_gain_one.astype(jnp.bfloat16), "expert", scatter_dimension=0, tiled=True
        ).astype(jnp.float32),
        lax.psum_scatter(
            grad_gain_two.astype(jnp.bfloat16), "expert", scatter_dimension=0, tiled=True
        ).astype(jnp.float32),
        lax.psum_scatter(
            grad_qk.astype(jnp.bfloat16), "expert", scatter_dimension=2, tiled=True
        ).astype(jnp.float32),
    )
    return (
        block_out.astype(jnp.bfloat16),
        grad_tokens.astype(jnp.bfloat16),
        reduced[0],
        reduced[1],
        reduced[3],
        reduced[4],
        reduced[5],
        reduced[2],
        grad_gate_w,
        grad_up_w,
        grad_down,
    )


MESH_ID = pl.DeviceIdType.MESH
HBM = pl.BlockSpec(memory_space=pltpu.HBM)
VMEM = pl.BlockSpec(memory_space=pltpu.VMEM)
NZ, NY, NX, NC = 4, 2, 2, 2
GROUPS = NZ * NY


def place():
    e = lax.axis_index("expert")
    t = lax.axis_index("tensor")
    return lax.div(e, NY), lax.rem(e, NY), lax.div(t, NC), lax.rem(t, NC)


def device(z, y, x, c):
    return (jnp.clip(z, 0, NZ - 1) * NY + y, x * NC + c)


def run_if(condition, body):
    if condition is None:
        body()
    else:
        pl.when(condition)(body)


def greet(partners):
    barrier = pltpu.get_barrier_semaphore()
    for target, condition in partners:
        run_if(
            condition,
            lambda target=target: pl.semaphore_signal(
                barrier, inc=1, device_id=target, device_id_type=MESH_ID
            ),
        )
    count = sum(1 for _, condition in partners if condition is None)
    for _, condition in partners:
        if condition is not None:
            count = count + condition.astype(jnp.int32)
    pl.semaphore_wait(barrier, count)


def remote(source, target_ref, send_sem, recv_sem, target):
    return pltpu.make_async_remote_copy(
        src_ref=source,
        dst_ref=target_ref,
        send_sem=send_sem,
        recv_sem=recv_sem,
        device_id=target,
        device_id_type=MESH_ID,
    )


def block_rows(block, rows):
    return pl.ds(pl.multiple_of(block * rows, rows), rows)


class LineGather:
    def __init__(self, streams, sources, views, send_sem, recv_sem, y_first=()):
        self.z, self.y, self.x, self.c = place()
        self.streams, self.sources, self.views = streams, sources, views
        self.send_sem, self.recv_sem = send_sem, recv_sem
        self.y_first = y_first
        self.has_up, self.has_down = self.z < NZ - 1, self.z > 0
        self.pending = []

    def partners(self):
        z, y, x, c = self.z, self.y, self.x, self.c
        return [
            (device(z + 1, y, x, c), z < NZ - 1),
            (device(z - 1, y, x, c), z > 0),
            (device(z, 1 - y, x, c), None),
        ]

    def exists(self, rel):
        rel = rel % 7
        if rel == 0:
            return None
        return self.z >= rel if rel < 4 else self.z + (rel - 3) < NZ

    def block(self, rel):
        y = self.y if rel < 7 else 1 - self.y
        rel = rel % 7
        z = self.z if rel == 0 else (self.z - rel if rel < 4 else self.z + (rel - 3))
        return z * NY + y

    def send(self, stream, rel, way):
        z, y, x, c = self.z, self.y, self.x, self.c
        block = self.block(rel)
        there = self.views[stream](block)
        source = self.sources[stream] if rel == 0 else there
        near = rel % 7 == 0
        if way == 0:
            target, landing = device(z + 1, y, x, c), rel + 1
        elif way == 1:
            target, landing = device(z - 1, y, x, c), rel + (4 if near else 1)
        else:
            target, landing = device(z, 1 - y, x, c), 7 + rel
        return remote(
            source,
            there,
            self.send_sem.at[stream, rel, way],
            self.recv_sem.at[stream, landing],
            target,
        )

    def forwards(self, stream, rel):
        return rel < 7 or stream in self.y_first

    def start(self, stream, rel):
        if rel % 7 < 4:
            run = self.has_up
            run_if(run, lambda: self.send(stream, rel, 0).start())
            self.pending.append((stream, rel, 0, run))
        if rel % 7 == 0 or rel % 7 >= 4:
            run = self.has_down
            run_if(run, lambda: self.send(stream, rel, 1).start())
            self.pending.append((stream, rel, 1, run))
        if rel == 0 or stream not in self.y_first:
            self.send(stream, rel, 2).start()
            self.pending.append((stream, rel, 2, None))

    def arrive(self, stream, rel):
        there = self.views[stream](self.block(rel))
        remote(
            there,
            there,
            self.send_sem.at[stream, 0, 0],
            self.recv_sem.at[stream, rel],
            device(self.z, 1 - self.y, self.x, self.c),
        ).wait_recv()

    def order(self):
        return [7, 1, 4, 8, 11, 2, 5, 9, 12, 3, 6, 10, 13]

    def run(self, hook=None):
        for stream in self.streams:
            self.start(stream, 0)
        for rel in self.order():
            def step(rel=rel):
                marks = len(self.pending)
                for stream in self.streams:
                    self.arrive(stream, rel)
                    if rel < 7:
                        self.start(stream, rel)
                    if hook is not None:
                        hook(stream, rel)
                if rel < 7:
                    late = self.pending[marks:]
                    del self.pending[marks:]
                    self.finish_later(late, rel)
            run_if(self.exists(rel), step)

    def finish_later(self, late, rel):
        self.late = getattr(self, "late", []) + [(rel, late)]

    def finish(self):
        for stream, rel, way, run in self.pending:
            run_if(run, lambda s=stream, r=rel, w=way: self.send(s, r, w).wait_send())
        for rel, late in getattr(self, "late", []):
            def body(late=late):
                for stream, rel, way, run in late:
                    run_if(run, lambda s=stream, r=rel, w=way: self.send(s, r, w).wait_send())
            run_if(self.exists(rel), body)


def cost(microseconds):
    return pl.CostEstimate(flops=0, bytes_accessed=int(microseconds * 3.0e6), transcendentals=0)


def comm_params(collective_id, megabytes=56):
    return pltpu.CompilerParams(
        collective_id=collective_id,
        has_side_effects=True,
        vmem_limit_bytes=megabytes * 1024 * 1024,
    )


def group_stages(part_ref, out_ref, core_buf, x_buf, send_sem, recv_sem):
    rows, width = part_ref.shape
    half, quarter = width // 2, width // 4
    z, y, x, c = place()
    across, twin = device(z, y, 1 - x, c), device(z, y, x, 1 - c)

    def half_of(cc):
        return pl.ds(pl.multiple_of(cc * half, half), half)

    def quarter_of(xx, cc):
        return pl.ds(pl.multiple_of(cc * half + xx * quarter, quarter), quarter)

    own, from_x = out_ref.at[:, quarter_of(x, c)], out_ref.at[:, quarter_of(1 - x, c)]
    to_x = core_buf.at[:, pl.ds(pl.multiple_of((1 - x) * quarter, quarter), quarter)]
    sources = [part_ref.at[:, half_of(1 - c)], to_x, own, own, from_x]
    landings = [core_buf, x_buf, own, own, from_x]
    targets = [twin, across, across, twin, twin]

    def copy(k):
        return remote(sources[k], landings[k], send_sem.at[k], recv_sem.at[k], targets[k])

    def arrive(k, landing):
        remote(landing, landing, send_sem.at[k], recv_sem.at[k], targets[k]).wait_recv()

    def begin():
        copy(0).start()

    def core_step():
        copy(0).wait_recv()
        add_to(core_buf, core_buf, part_ref.at[:, half_of(c)], 32)
        copy(1).start()

    def x_step():
        copy(1).wait_recv()
        add_to(own, x_buf, core_buf.at[:, pl.ds(pl.multiple_of(x * quarter, quarter), quarter)], 32)
        copy(2).start()
        copy(3).start()

    def spread():
        arrive(2, from_x)
        copy(4).start()

    def end():
        arrive(3, out_ref.at[:, quarter_of(x, 1 - c)])
        arrive(4, out_ref.at[:, quarter_of(1 - x, 1 - c)])
        for k in range(5):
            copy(k).wait_send()

    return [begin, core_step, x_step, spread, end]


def group_sum(part_ref, out_ref, core_buf, x_buf, send_sem, recv_sem, meanwhile=None):
    stages = group_stages(part_ref, out_ref, core_buf, x_buf, send_sem, recv_sem)
    stages[0]()
    if meanwhile is not None:
        meanwhile()
    for stage in stages[1:]:
        stage()


Z_ORDER = (3, 0, 2, 1)


def accumulate(into, addend, step=64):
    rows = into.shape[0]
    step = min(step, rows)

    def body(i, carry):
        r = pl.ds(pl.multiple_of(i * step, step), step)
        total = into[r, :].astype(jnp.float32) + addend[r, :].astype(jnp.float32)
        into[r, :] = total.astype(into.dtype)
        return carry

    lax.fori_loop(0, rows // step, body, 0)


class LineReduce:
    def __init__(self, streams, own, y_buf, lo_buf, hi_buf, send_sem, recv_sem):
        self.z, self.y, self.x, self.c = place()
        self.streams = streams
        self.own, self.y_buf, self.lo_buf, self.hi_buf = own, y_buf, lo_buf, hi_buf
        self.send_sem, self.recv_sem = send_sem, recv_sem

    def partners(self):
        z, y, x, c = self.z, self.y, self.x, self.c
        return [
            (device(z + 1, y, x, c), z < NZ - 1),
            (device(z - 1, y, x, c), z > 0),
            (device(z, 1 - y, x, c), None),
        ]

    def copy(self, s, zz, way):
        z, y, x, c = self.z, self.y, self.x, self.c
        if way == 0:
            source, landing, target = self.own(s, zz, 1 - y), self.y_buf, device(z, 1 - y, x, c)
        elif way == 1:
            source, landing, target = self.y_buf(s, zz), self.lo_buf, device(z + 1, y, x, c)
        else:
            source, landing, target = self.y_buf(s, zz), self.hi_buf, device(z - 1, y, x, c)
        return remote(
            source, landing(s, zz), self.send_sem.at[s, zz, way], self.recv_sem.at[s, zz, way], target
        )

    def to_y(self, s, zz):
        self.copy(s, zz, 0).start()

    def take(self, s, zz, way):
        self.copy(s, zz, way).wait_recv()
        accumulate(self.y_buf(s, zz), (self.lo_buf if way == 1 else self.hi_buf)(s, zz))

    def along_z(self, s, zz):
        z = self.z
        self.copy(s, zz, 0).wait_recv()
        accumulate(self.y_buf(s, zz), self.own(s, zz, self.y))

        def upward():
            run_if(z > 0, lambda: self.take(s, zz, 1))
            self.copy(s, zz, 1).start()

        def downward():
            run_if(z < NZ - 1, lambda: self.take(s, zz, 2))
            self.copy(s, zz, 2).start()

        run_if(z < zz, upward)
        run_if(z > zz, downward)

    def home(self, done):
        for zz in range(NZ):
            def land(zz=zz):
                for s in self.streams:
                    if zz > 0:
                        self.take(s, zz, 1)
                    if zz < NZ - 1:
                        self.take(s, zz, 2)
                    done(s, self.y_buf(s, zz))
            run_if(self.z == zz, land)

    def finish(self):
        for zz in range(NZ):
            for s in self.streams:
                self.copy(s, zz, 0).wait_send()
                run_if(self.z < zz, lambda s=s, zz=zz: self.copy(s, zz, 1).wait_send())
                run_if(self.z > zz, lambda s=s, zz=zz: self.copy(s, zz, 2).wait_send())


def dot(a, b, dims):
    return lax.dot_general(a, b, ((dims[:1], dims[1:]), ((), ())), preferred_element_type=jnp.float32)


def add_to(target, first, second, step=64):
    rows = target.shape[0]

    def body(i, carry):
        r = pl.ds(pl.multiple_of(i * step, step), step)
        total = first[r, :].astype(jnp.float32) + second[r, :].astype(jnp.float32)
        target[r, :] = total.astype(target.dtype)
        return carry

    lax.fori_loop(0, rows // step, body, 0)


def expert_layer(
    hidden_two, grad_out_all, gate_up, down, router_t, chosen_all, residual, attended, collective_id
):
    rows, width = hidden_two.shape
    tokens = rows * GROUPS
    units = down.shape[0]
    local = 2
    hidden = units // local
    experts = router_t.shape[0]
    half, part, piece = width // 2, width // 4, width // 8
    tensors = NX * NC
    steps = GROUPS + 4
    a_cols, c_cols = width // 8, width // 4
    low = jnp.bfloat16
    wide = width // 4

    def kernel(
        own_in, dy_in, gu_in, down_in, router_ref, chosen_ref, x1_in, o_in,
        block_out, dh_out, gates_out, gate_w, up_w, down_w, o_all,
        gu_ref, down_ref, weight_sem, h, dy, gated, dgu, dx, y_part, yc_buf, ypx_buf, ypy_buf, yqy_buf, yqx_buf, yz_sum,
        ylo_buf, yhi_buf, x1, gu_stage, d_stage,
        core_buf, px_buf, py_buf, qy_buf, qx_buf, z_sum, lo_buf, hi_buf, gate_part, gate_land,
        in_sem, own_sem, o_sem, line_s, line_r, hx_s, hx_r, hc_s, hc_r, x1_sem, yc_s, yc_r, ypx_s, ypx_r, ypy_s, ypy_r,
        yqy_s, yqy_r, yqx_s, yqx_r, yz_s, yz_r, gu_sem, d_sem, core_s, core_r, px_s, px_r, py_s, py_r, qy_s, qy_r, qx_s, qx_r,
        z_s, z_r, near_s, near_r, far_s, far_r, end_s, end_r,
    ):
        z, y, x, c = place()
        e, t = lax.axis_index("expert"), lax.axis_index("tensor")
        across, twin, beside = device(z, y, 1 - x, c), device(z, y, x, 1 - c), device(z, 1 - y, x, c)
        mates = [(e, lax.rem(t + k, tensors)) for k in range(1, tensors)]
        peers = [(lax.rem(e + k, GROUPS), t) for k in range(1, GROUPS)]
        weight_loads = [
            pltpu.make_async_copy(gu_in, gu_ref, weight_sem.at[0]),
            pltpu.make_async_copy(down_in, down_ref, weight_sem.at[1]),
        ]
        for copy in weight_loads:
            copy.start()
        greet([(target, None) for target in mates + peers])

        def pick(values, index):
            result = values[-1]
            for k in range(len(values) - 1):
                result = jnp.where(index == k, values[k], result)
            return result

        def zz_of(j):
            return pick([z, pick([1, 0, 3, 2], z), pick([3, 3, 0, 0], z), pick([2, 2, 1, 1], z)], j)

        def is_own(i):
            return (i == 0) | ((i >= 2) & (lax.rem(i, 2) == 1))

        def block_of(i):
            return zz_of(lax.div(i, 2)) * NY + jnp.where(is_own(i), y, 1 - y)

        def flip_block(j):
            return zz_of(j) * NY + 1 - y

        def own_block(j):
            return zz_of(j) * NY + y

        def a_at(xx, cc):
            return pl.ds(pl.multiple_of(xx * (2 * a_cols) + cc * a_cols, 128), a_cols)

        def c_at(cc):
            return pl.ds(pl.multiple_of(4 * a_cols + cc * c_cols, 128), c_cols)

        def h_view(b, columns):
            return h.at[block_rows(b, rows), columns]

        line = LineGather(
            [0, 1, 2], [own_in.at[:, a_at(x, c)], own_in.at[:, c_at(c)], o_in],
            [
                lambda b: h_view(b, a_at(x, c)),
                lambda b: h_view(b, c_at(c)),
                lambda b: o_all.at[block_rows(b, rows), :],
            ],
            line_s, line_r,
        )

        def h_twin(b, stream, landing=False):
            cc = 1 - c if landing else c
            piece = h_view(b, [a_at(x, cc), c_at(cc), a_at(1 - x, cc)][stream])
            return remote(piece, piece, hc_s.at[b, stream], hc_r.at[b, stream], twin)

        def h_across(b, landing=False):
            piece = h_view(b, a_at(1 - x if landing else x, c))
            return remote(piece, piece, hx_s.at[b], hx_r.at[b], across)

        def gather_event(rel):
            def body():
                b = line.block(rel)
                marks = len(line.pending)
                for stream in (0, 1):
                    line.arrive(stream, rel)
                    if rel < 7:
                        line.start(stream, rel)
                    if stream == 0:
                        h_across(b).start()
                    h_twin(b, stream).start()
                late = line.pending[marks:]
                del line.pending[marks:]
                line.finish_later(late, rel)
            run_if(line.exists(rel), body)

        def attended_event(rel):
            def body():
                marks = len(line.pending)
                line.arrive(2, rel)
                if rel < 7:
                    line.start(2, rel)
                late = line.pending[marks:]
                del line.pending[marks:]
                line.finish_later(late, rel)
            run_if(line.exists(rel), body)

        def relay(i):
            b = block_of(i)
            h_across(b, True).wait_recv()
            h_twin(b, 2).start()

        for stream in (0, 1):
            line.start(stream, 0)
        keep = pltpu.make_async_copy(own_in, h.at[block_rows(z * NY + y, rows), :], own_sem)
        keep.start()
        keep_o = pltpu.make_async_copy(o_in, o_all.at[block_rows(z * NY + y, rows), :], o_sem)
        keep_o.start()

        def load(i):
            r = block_rows(block_of(i), rows)
            return pltpu.make_async_copy(dy_in.at[r, :], dy.at[r, :], in_sem.at[i])

        def start_load(i, carry):
            load(i).start()
            return carry

        lax.fori_loop(0, GROUPS, start_load, 0)
        x1_copies = [
            pltpu.make_async_copy(
                x1_in.at[:, pl.ds(pl.multiple_of(c * half + s * part + x * piece, piece), piece)],
                x1.at[:, pl.ds(s * piece, piece)], x1_sem.at[s],
            )
            for s in range(2)
        ]
        for copy in x1_copies:
            copy.start()

        def to_twin(i):
            b = block_of(i)
            return remote(
                dx.at[lax.rem(i, 2), :, pl.ds(pl.multiple_of((1 - c) * half, half), half)],
                core_buf.at[b], core_s.at[i], core_r.at[i], twin,
            )

        def p_across(i):
            b = block_of(i)
            return remote(
                core_buf.at[b, :, pl.ds(pl.multiple_of((1 - x) * piece, piece), piece)],
                px_buf.at[b], px_s.at[i], px_r.at[i], across,
            )

        def p_beside(j):
            return remote(px_buf.at[flip_block(j)], py_buf.at[j], py_s.at[j], py_r.at[j], beside)

        def q_beside(j):
            return remote(
                core_buf.at[flip_block(j), :, pl.ds(part, part)], qy_buf.at[j], qy_s.at[j], qy_r.at[j], beside
            )

        def q_across(j):
            return remote(
                qy_buf.at[j, :, pl.ds(pl.multiple_of((1 - x) * piece, piece), piece)],
                qx_buf.at[j], qx_s.at[j], qx_r.at[j], across,
            )

        def up(j, s):
            return remote(z_sum.at[s, j], lo_buf.at[s, j], z_s.at[0, s, j], z_r.at[0, s, j], device(z + 1, y, x, c))

        def down_z(j, s):
            return remote(z_sum.at[s, j], hi_buf.at[s, j], z_s.at[1, s, j], z_r.at[1, s, j], device(z - 1, y, x, c))

        def take_twin(i):
            to_twin(i).wait_recv()
            b = block_of(i)
            mine = core_buf.at[b]
            add_to(mine, mine, dx.at[lax.rem(i, 2), :, pl.ds(pl.multiple_of(c * half, half), half)], 32)
            p_across(i).start()
            pl.when(jnp.logical_not(is_own(i)))(lambda: q_beside(lax.div(i, 2)).start())

        def take_p_across(i):
            p_across(i).wait_recv()
            b = block_of(i)
            add_to(
                px_buf.at[b], px_buf.at[b],
                core_buf.at[b, :, pl.ds(pl.multiple_of(x * piece, piece), piece)],
            )

        def take_q_beside(j):
            q_beside(j).wait_recv()
            add_to(qy_buf.at[j], qy_buf.at[j], core_buf.at[own_block(j), :, pl.ds(part, part)])
            q_across(j).start()

        def take_q_across(j):
            q_across(j).wait_recv()
            add_to(
                z_sum.at[1, zz_of(j)], qx_buf.at[j], qy_buf.at[j, :, pl.ds(pl.multiple_of(x * piece, piece), piece)]
            )

        def take_p_beside(j):
            p_beside(j).wait_recv()
            add_to(z_sum.at[0, zz_of(j)], py_buf.at[j], px_buf.at[own_block(j)])

        def hop(j, k):
            zz = zz_of(j)

            def upward():
                for s in range(2):
                    if k > 0:
                        up(zz, s).wait_recv()
                        add_to(z_sum.at[s, zz], z_sum.at[s, zz], lo_buf.at[s, zz])
                    up(zz, s).start()

            def downward():
                for s in range(2):
                    if k > 0:
                        down_z(zz, s).wait_recv()
                        add_to(z_sum.at[s, zz], z_sum.at[s, zz], hi_buf.at[s, zz])
                    down_z(zz, s).start()

            pl.when((z < zz) & (z == k))(upward)
            pl.when((z > zz) & (NZ - 1 - z == k))(downward)

        def y_twin(i):
            return remote(
                y_part.at[lax.rem(i, 2), :, pl.ds(pl.multiple_of((1 - c) * half, half), half)],
                yc_buf.at[block_of(i)], yc_s.at[i], yc_r.at[i], twin,
            )

        def yp_across(i):
            b = block_of(i)
            return remote(
                yc_buf.at[b, :, pl.ds(pl.multiple_of((1 - x) * piece, piece), piece)],
                ypx_buf.at[b], ypx_s.at[i], ypx_r.at[i], across,
            )

        def yp_beside(j):
            return remote(ypx_buf.at[flip_block(j)], ypy_buf.at[j], ypy_s.at[j], ypy_r.at[j], beside)

        def yq_beside(j):
            return remote(
                yc_buf.at[flip_block(j), :, pl.ds(part, part)], yqy_buf.at[j], yqy_s.at[j], yqy_r.at[j], beside
            )

        def yq_across(j):
            return remote(
                yqy_buf.at[j, :, pl.ds(pl.multiple_of((1 - x) * piece, piece), piece)],
                yqx_buf.at[j], yqx_s.at[j], yqx_r.at[j], across,
            )

        def y_up(zz, s):
            return remote(
                yz_sum.at[s, zz], ylo_buf.at[s, zz], yz_s.at[0, s, zz], yz_r.at[0, s, zz], device(z + 1, y, x, c)
            )

        def y_down(zz, s):
            return remote(
                yz_sum.at[s, zz], yhi_buf.at[s, zz], yz_s.at[1, s, zz], yz_r.at[1, s, zz], device(z - 1, y, x, c)
            )

        def take_y_twin(i):
            y_twin(i).wait_recv()
            mine = yc_buf.at[block_of(i)]
            add_to(mine, mine, y_part.at[lax.rem(i, 2), :, pl.ds(pl.multiple_of(c * half, half), half)], 32)
            yp_across(i).start()
            pl.when(jnp.logical_not(is_own(i)))(lambda: yq_beside(lax.div(i, 2)).start())

        def take_yp_across(i):
            yp_across(i).wait_recv()
            b = block_of(i)
            add_to(
                ypx_buf.at[b], ypx_buf.at[b],
                yc_buf.at[b, :, pl.ds(pl.multiple_of(x * piece, piece), piece)],
            )
            pl.when(jnp.logical_not(is_own(i)))(lambda: yp_beside(lax.div(i, 2)).start())

        def take_yq_beside(j):
            yq_beside(j).wait_recv()
            add_to(yqy_buf.at[j], yqy_buf.at[j], yc_buf.at[own_block(j), :, pl.ds(part, part)])
            yq_across(j).start()

        def take_y_sums(j):
            zz = zz_of(j)
            yq_across(j).wait_recv()
            add_to(
                yz_sum.at[1, zz], yqx_buf.at[j], yqy_buf.at[j, :, pl.ds(pl.multiple_of(x * piece, piece), piece)]
            )
            yp_beside(j).wait_recv()
            add_to(yz_sum.at[0, zz], ypy_buf.at[j], ypx_buf.at[own_block(j)])

        def y_take(zz, s, copy, landed):
            copy(zz, s).wait_recv()
            add_to(yz_sum.at[s, zz], yz_sum.at[s, zz], landed.at[s, zz])

        def y_hop(j, k):
            zz = zz_of(j)

            def upward():
                for s in range(2):
                    if k > 0:
                        y_take(zz, s, y_up, ylo_buf)
                    y_up(zz, s).start()

            def downward():
                for s in range(2):
                    if k > 0:
                        y_take(zz, s, y_down, yhi_buf)
                    y_down(zz, s).start()

            pl.when((z < zz) & (z == k))(upward)
            pl.when((z > zz) & (NZ - 1 - z == k))(downward)

        def front(i):
            load(i).wait()
            b = block_of(i)
            pl.when(i == 0)(keep.wait)
            pl.when(i == 0)(lambda: each(weight_loads, "wait"))

            def landed():
                for stream in range(3):
                    h_twin(b, stream, True).wait_recv()

            pl.when(i > 0)(landed)
            r = block_rows(b, rows)
            rows_h, rows_dy = h[r, :], dy[r, :]
            logits = dot(rows_h, router_ref[...], (1, 1))
            shifted = jnp.exp(logits - jnp.max(logits, axis=-1, keepdims=True))
            probs = shifted / jnp.sum(shifted, axis=-1, keepdims=True) * chosen_ref[r, :].astype(jnp.float32)
            lane = lax.broadcasted_iota(jnp.int32, probs.shape, 1)
            line = lax.broadcasted_iota(jnp.int32, (rows, 128), 1)
            found = jnp.zeros((rows, 128), jnp.float32)
            for expert in range(local):
                at, up_at = pl.ds(expert * hidden, hidden), pl.ds((local + expert) * hidden, hidden)
                gate = jnp.sum(jnp.where(lane == e * local + expert, probs, 0.0), axis=-1, keepdims=True)
                pre = dot(rows_h, gu_ref[:, at], (1, 0))
                scale = dot(rows_h, gu_ref[:, up_at], (1, 0))
                back = dot(rows_dy, down_ref[at, :], (1, 1))
                sigmoid = jax.nn.sigmoid(pre)
                swish = pre * sigmoid
                active = swish * scale
                gated[r, at] = (active * gate).astype(low)
                found = jnp.where(line == expert, jnp.sum(active * back, axis=-1, keepdims=True), found)
                back = back * gate
                dgu[r, at] = (back * scale * sigmoid * (1.0 + pre * (1.0 - sigmoid))).astype(low)
                dgu[r, up_at] = (back * swish).astype(low)
            gate_part[b] = jnp.transpose(found)[:8, :]

        def rear(i):
            r = block_rows(block_of(i), rows)
            slot = lax.rem(i, 2)
            pl.when(i >= 2)(lambda: to_twin(i - 2).wait_send())

            def columns(k, carry):
                at = pl.ds(pl.multiple_of(k * wide, wide), wide)
                dx[slot, :, at] = dot(dgu[r, :], gu_ref[at, :], (1, 1)).astype(low)
                return carry

            lax.fori_loop(0, width // wide, columns, 0)
            to_twin(i).start()
            pl.when(i >= 2)(lambda: y_twin(i - 2).wait_send())

            def y_columns(k, carry):
                at = pl.ds(pl.multiple_of(k * wide, wide), wide)
                y_part[slot, :, at] = dot(gated[r, :], down_ref[:, at], (1, 0)).astype(low)
                return carry

            lax.fori_loop(0, width // wide, y_columns, 0)
            y_twin(i).start()

        tile_width = piece // 2
        tiles = width // tile_width // 4
        d_width = width // 8

        def gu_copies(n):
            slot = lax.rem(n, 2)
            at = pl.ds(pl.multiple_of(n * tile_width, tile_width), tile_width)
            return [
                pltpu.make_async_copy(
                    gu_stage.at[slot, :, pl.ds(k * hidden, hidden)],
                    (gate_w if k < local else up_w).at[k % local, at, :],
                    gu_sem.at[slot, k],
                )
                for k in range(2 * local)
            ]

        def d_copies(n):
            slot = lax.rem(n, 2)
            at = pl.ds(pl.multiple_of(n * d_width, d_width), d_width)
            return [
                pltpu.make_async_copy(
                    d_stage.at[slot, pl.ds(k * hidden, hidden), :], down_w.at[k, :, at], d_sem.at[slot, k]
                )
                for k in range(local)
            ]

        def each(copies, what):
            for copy in copies:
                getattr(copy, what)()

        def weight_grads(q):
            def tile(k, carry):
                n = q * tiles + k
                pl.when(n >= 2)(lambda: each(gu_copies(n - 2), "wait"))
                at = pl.ds(pl.multiple_of(n * tile_width, tile_width), tile_width)
                gu_stage[lax.rem(n, 2)] = dot(h[:, at], dgu[...], (0, 0))
                each(gu_copies(n), "start")
                return carry

            lax.fori_loop(0, tiles, tile, 0)

            def d_tile(k, carry):
                n = q * 2 + k
                pl.when(n >= 2)(lambda: each(d_copies(n - 2), "wait"))
                at = pl.ds(pl.multiple_of(n * d_width, d_width), d_width)
                d_stage[lax.rem(n, 2)] = dot(gated[...], dy[:, at], (0, 0))
                each(d_copies(n), "start")
                return carry

            lax.fori_loop(0, 2, d_tile, 0)

        near = [
            remote(gate_part, gate_land.at[k], near_s.at[k], near_r.at[k], mates[k])
            for k in range(tensors - 1)
        ]

        def far(k):
            return remote(
                gate_land.at[tensors - 1, lax.rem(e + k, GROUPS)], gates_out.at[e],
                far_s.at[k - 1], far_r.at[k - 1], peers[k - 1],
            )

        def sum_near():
            for copy in near:
                copy.wait_recv()
            total = gate_part[...]
            for k in range(tensors - 1):
                total = total + gate_land[k]
            gate_land[tensors - 1] = total
            for k in range(1, GROUPS):
                far(k).start()
            gates_out[e] = gate_land[tensors - 1, e]

        def step(i, carry):
            def at(number, body):
                pl.when(i == number)(body)

            odd, even = lax.rem(i, 2) == 1, lax.rem(i, 2) == 0
            j_even, j_odd = lax.div(i, 2) - 1, lax.div(i - 1, 2) - 1
            pl.when(i < GROUPS)(lambda: front(i))

            def events(*rels):
                for rel in rels:
                    gather_event(rel)

            at(1, lambda: events(2, 5, 8, 11))
            at(2, lambda: events(3, 6))
            at(3, lambda: events(10, 13))

            def attended_events(*rels):
                for rel in rels:
                    attended_event(rel)

            at(8, lambda: attended_events(1, 4))
            at(9, lambda: attended_events(2, 5))
            at(10, lambda: attended_events(3, 6))
            at(11, lambda: attended_events(7, 8, 11))

            pl.when((i >= 1) & (i <= GROUPS))(lambda: take_twin(i - 1))
            pl.when(even & (i >= 4) & (i <= GROUPS))(lambda: take_q_beside(j_even))
            at(3, lambda: take_q_beside(0))
            at(4, lambda: take_q_across(0))

            def late():
                take_p_across(i - 2)
                pl.when(i > 3)(lambda: take_q_across(j_odd))
                pl.when(i == 3)(lambda: p_beside(0).start())

            pl.when(odd & (i >= 3) & (i <= GROUPS + 1))(late)
            at(GROUPS, lambda: each(near, "start"))
            at(GROUPS + 1, sum_near)
            pl.when(i < GROUPS)(lambda: rear(i))
            pl.when(i >= GROUPS)(lambda: weight_grads(i - GROUPS))
            at(0, lambda: events(7, 1, 4))
            at(2, lambda: events(9, 12))
            at(6, lambda: line.start(2, 0))
            pl.when(i < GROUPS - 1)(lambda: relay(i + 1))

            def pass_p():
                take_p_across(i - 2)
                pl.when(i > 2)(lambda: p_beside(j_even).start())

            pl.when(even & (i >= 2) & (i <= GROUPS))(pass_p)
            at(4, lambda: take_p_beside(0))

            def join():
                take_p_beside(j_odd)
                hop(j_odd, 0)

            pl.when(odd & (i >= 5) & (i <= GROUPS + 1))(join)
            pl.when((i == GROUPS) | (i == GROUPS + 2))(lambda: hop(j_even - 1, 1))
            at(GROUPS + 1, lambda: hop(1, 2))
            pl.when((i >= 2) & (i <= GROUPS + 1))(lambda: take_yp_across(i - 2))
            pl.when((i >= 1) & (i <= GROUPS))(lambda: take_y_twin(i - 1))
            pl.when(even & (i >= 4) & (i <= GROUPS))(lambda: take_yq_beside(j_even))
            at(3, lambda: take_yq_beside(0))
            at(5, lambda: take_y_sums(0))

            def join_y():
                take_y_sums(j_even - 1)
                y_hop(j_even - 1, 0)

            pl.when(even & (i >= 6) & (i <= GROUPS + 2))(join_y)
            pl.when((i == GROUPS + 1) | (i == GROUPS + 3))(lambda: y_hop(j_odd - 1, 1))
            at(GROUPS + 2, lambda: y_hop(1, 2))
            return carry

        lax.fori_loop(0, steps, step, 0)

        for rel in (9, 12, 10, 13):
            attended_event(rel)

        def columns_of(s, xx, cc):
            return pl.ds(pl.multiple_of(cc * half + s * part + xx * piece, piece), piece)

        mine = z
        for s in range(2):
            def below(s=s):
                up(mine, s).wait_recv()
                add_to(z_sum.at[s, mine], z_sum.at[s, mine], lo_buf.at[s, mine])

            def above(s=s):
                down_z(mine, s).wait_recv()
                add_to(z_sum.at[s, mine], z_sum.at[s, mine], hi_buf.at[s, mine])

            pl.when(z > 0)(below)
            pl.when(z < NZ - 1)(above)
            own = dh_out.at[:, columns_of(s, x, c)]

            def keep(k, carry, s=s, own=own):
                r = pl.ds(pl.multiple_of(k * 64, 64), 64)
                own[r, :] = z_sum[s, mine, r, :]
                return carry

            lax.fori_loop(0, rows // 64, keep, 0)
            remote(own, own, end_s.at[0, s], end_r.at[0, s], across).start()
            remote(own, own, end_s.at[1, s], end_r.at[1, s], twin).start()
        for copy in x1_copies:
            copy.wait()
        for s in range(2):
            pl.when(z > 0)(lambda s=s: y_take(z, s, y_up, ylo_buf))
            pl.when(z < NZ - 1)(lambda s=s: y_take(z, s, y_down, yhi_buf))
            y_own = block_out.at[:, columns_of(s, x, c)]

            def finish(k, carry, s=s, y_own=y_own):
                r = pl.ds(pl.multiple_of(k * 64, 64), 64)
                y_own[r, :] = (
                    x1[r, pl.ds(s * piece, piece)] + yz_sum[s, z, r, :].astype(jnp.float32)
                ).astype(low)
                return carry

            lax.fori_loop(0, rows // 64, finish, 0)
            remote(y_own, y_own, end_s.at[0, 2 + s], end_r.at[0, 2 + s], across).start()
            remote(y_own, y_own, end_s.at[1, 2 + s], end_r.at[1, 2 + s], twin).start()
        for s in range(2):
            there = dh_out.at[:, columns_of(s, 1 - x, c)]
            remote(there, there, end_s.at[0, s], end_r.at[0, s], across).wait_recv()
            remote(there, there, end_s.at[2, s], end_r.at[2, s], twin).start()
        for s in range(2):
            there = block_out.at[:, columns_of(s, 1 - x, c)]
            remote(there, there, end_s.at[0, 2 + s], end_r.at[0, 2 + s], across).wait_recv()
            remote(there, there, end_s.at[2, 2 + s], end_r.at[2, 2 + s], twin).start()
        for n, result in ((0, dh_out), (2, block_out)):
            for s in range(2):
                for k, xx in ((1, x), (2, 1 - x)):
                    there = result.at[:, columns_of(s, xx, 1 - c)]
                    remote(there, there, end_s.at[k, n + s], end_r.at[k, n + s], twin).wait_recv()
                for k, target in ((0, across), (1, twin), (2, twin)):
                    there = result.at[:, columns_of(s, 1 - x if k == 2 else x, c)]
                    remote(there, there, end_s.at[k, n + s], end_r.at[k, n + s], target).wait_send()
        for k in range(1, GROUPS):
            there = gates_out.at[lax.rem(e + GROUPS - k, GROUPS)]
            remote(there, there, far_s.at[k - 1], far_r.at[k - 1], peers[k - 1]).wait_recv()
            far(k).wait_send()
        each(near, "wait_send")

        def drain(i, carry):
            pl.when(i >= GROUPS - 2)(lambda: to_twin(i).wait_send())
            pl.when(i >= GROUPS - 2)(lambda: y_twin(i).wait_send())
            p_across(i).wait_send()
            yp_across(i).wait_send()
            return carry

        lax.fori_loop(0, GROUPS, drain, 0)

        def drain_pair(j, carry):
            p_beside(j).wait_send()
            q_beside(j).wait_send()
            q_across(j).wait_send()
            yp_beside(j).wait_send()
            yq_beside(j).wait_send()
            yq_across(j).wait_send()
            for s in range(2):
                pl.when(z < j)(lambda s=s: up(j, s).wait_send())
                pl.when(z > j)(lambda s=s: down_z(j, s).wait_send())
                pl.when(z < j)(lambda s=s: y_up(j, s).wait_send())
                pl.when(z > j)(lambda s=s: y_down(j, s).wait_send())
            return carry

        lax.fori_loop(0, NZ, drain_pair, 0)

        def drain_rows_of(i, carry):
            b = block_of(i)
            h_across(b).wait_send()
            for stream in range(3):
                h_twin(b, stream).wait_send()
            return carry

        lax.fori_loop(1, GROUPS, drain_rows_of, 0)
        line.finish()
        keep_o.wait()
        for k in range(2):
            each(gu_copies(4 * tiles - 2 + k), "wait")
            each(d_copies(6 + k), "wait")

    shape = jax.ShapeDtypeStruct
    dma = pltpu.SemaphoreType.DMA
    f32 = jnp.float32
    return pl.pallas_call(
        kernel,
        out_shape=(
            shape((rows, width), low),
            shape((rows, width), low),
            shape((GROUPS, 8, rows), f32),
            shape((local, width, hidden), f32),
            shape((local, width, hidden), f32),
            shape((local, hidden, width), f32),
            shape((tokens,) + attended.shape[1:], low),
        ),
        in_specs=[HBM, HBM, HBM, HBM, VMEM, VMEM, HBM, HBM],
        out_specs=(VMEM, VMEM, VMEM, HBM, HBM, HBM, HBM),
        scratch_shapes=[
            pltpu.VMEM(gate_up.shape, low),
            pltpu.VMEM(down.shape, low),
            dma((2,)),
            pltpu.VMEM((tokens, width), low),
            pltpu.VMEM((tokens, width), low),
            pltpu.VMEM((tokens, units), low),
            pltpu.VMEM((tokens, 2 * units), low),
            pltpu.VMEM((2, rows, width), low),
            pltpu.VMEM((2, rows, width), low),
            pltpu.VMEM((GROUPS, rows, half), low),
            pltpu.VMEM((GROUPS, rows, piece), low),
            pltpu.VMEM((NZ, rows, piece), low),
            pltpu.VMEM((NZ, rows, part), low),
            pltpu.VMEM((NZ, rows, piece), low),
            pltpu.VMEM((2, NZ, rows, piece), low),
            pltpu.VMEM((2, NZ, rows, piece), low),
            pltpu.VMEM((2, NZ, rows, piece), low),
            pltpu.VMEM((rows, part), f32),
            pltpu.VMEM((2, piece // 2, 2 * units), f32),
            pltpu.VMEM((2, units, width // 8), f32),
            pltpu.VMEM((GROUPS, rows, half), low),
            pltpu.VMEM((GROUPS, rows, piece), low),
            pltpu.VMEM((NZ, rows, piece), low),
            pltpu.VMEM((NZ, rows, part), low),
            pltpu.VMEM((NZ, rows, piece), low),
            pltpu.VMEM((2, NZ, rows, piece), low),
            pltpu.VMEM((2, NZ, rows, piece), low),
            pltpu.VMEM((2, NZ, rows, piece), low),
            pltpu.VMEM((GROUPS, 8, rows), f32),
            pltpu.VMEM((tensors, GROUPS, 8, rows), f32),
            dma((GROUPS,)), dma, dma, dma((3, 14, 3)), dma((3, 14)), dma((GROUPS,)), dma((GROUPS,)),
            dma((GROUPS, 3)), dma((GROUPS, 3)), dma((2,)), dma((GROUPS,)), dma((GROUPS,)), dma((GROUPS,)), dma((GROUPS,)),
            dma((NZ,)), dma((NZ,)), dma((NZ,)), dma((NZ,)), dma((NZ,)), dma((NZ,)),
            dma((2, 2, NZ)), dma((2, 2, NZ)), dma((2, 2 * local)), dma((2, local)),
            dma((GROUPS,)), dma((GROUPS,)), dma((GROUPS,)), dma((GROUPS,)),
            dma((NZ,)), dma((NZ,)), dma((NZ,)), dma((NZ,)), dma((NZ,)), dma((NZ,)),
            dma((2, 2, NZ)), dma((2, 2, NZ)),
            dma((tensors - 1,)), dma((tensors - 1,)), dma((GROUPS - 1,)), dma((GROUPS - 1,)),
            dma((3, 4)), dma((3, 4)),
        ],
        compiler_params=comm_params(collective_id, 62),
        cost_estimate=cost(80),
        name="expert_layer",
    )(hidden_two, grad_out_all, gate_up, down, router_t, chosen_all, residual, attended)


def exchange_rows(value, part_ref, land_ref, send_sem, recv_sem, mates):
    rows = value.shape[0]
    line = lax.broadcasted_iota(jnp.int32, (rows, 128), 1)
    part_ref[...] = jnp.transpose(jnp.where(line == 0, value, 0.0))[:8, :]
    for k, mate in enumerate(mates):
        remote(part_ref, land_ref.at[k], send_sem.at[k], recv_sem.at[k], mate).start()


def exchanged_rows(part_ref, land_ref, send_sem, recv_sem, mates):
    total = part_ref[...]
    for k, mate in enumerate(mates):
        remote(part_ref, land_ref.at[k], send_sem.at[k], recv_sem.at[k], mate).wait_recv()
    for k in range(len(mates)):
        total = total + land_ref[k]
    rows = part_ref.shape[1]
    tall = jnp.concatenate([total, jnp.zeros((120, rows), jnp.float32)], axis=0)
    return jnp.transpose(tall)[:, :1]


def drain_rows(part_ref, land_ref, send_sem, recv_sem, mates):
    for k, mate in enumerate(mates):
        remote(part_ref, land_ref.at[k], send_sem.at[k], recv_sem.at[k], mate).wait_send()


def turn(value, cosine, sine):
    return value * cosine + pltpu.roll(value, HEAD // 2, 1) * sine


def project(
    tokens, w_qkv, w_out, out_grad, gain_one, gain_two, qk_gain, w_router, routes, cosine, sine,
    w_gate, w_up, w_down, collective_id,
):
    rows, width = tokens.shape
    parts, depth, columns = w_qkv.shape
    heads = columns // HEAD
    tensors = NX * NC
    back = WINDOW // rows
    low, f32 = jnp.bfloat16, jnp.float32
    QUERY, KEY, VALUE, SMALL, OUT, GRAD, REST = 0, 1, 2, 3, 4, 5, 6
    out_half = w_out.shape[0] // 2
    out_rows, out_columns = w_out.shape
    quarter = width // tensors
    experts = w_router.shape[0]
    small_shape = (8 + 2 * experts, depth)

    def kernel(
        tok_ref, w_ref, out_ref, grad_in, gain_one_ref, gain_two_ref, qk_ref, w_router_ref, routes_ref, cos_ref, sin_ref, gate_in, up_in, down_in,
        w_all, out_all, grad_all, h1_out, raw_out, gate_up, down_out, gain_ref, router_ref, chosen_ref, scale_ref, q_ref, context,
        small_ref, small_all, h1_ref, raw_ref, wide_in, wide_low, down_f, down_low, own_w, own_out, weights, total, part_k, land_k, part_q, land_q,
        send_sem, recv_sem, out_sem, small_sem, kept, ks_s, ks_r, qs_s, qs_r, c_s, c_r, hx_s, hx_r, hc_s, hc_r, wide_s,
    ):
        z, y, x, c = place()
        e, t = lax.axis_index("expert"), lax.axis_index("tensor")
        wide_loads = [
            pltpu.make_async_copy(source.at[k], wide_in.at[2 * n + k], wide_s.at[2 * n + k])
            for n, source in enumerate((gate_in, up_in))
            for k in range(2)
        ]
        for copy in wide_loads:
            copy.start()
        mates = [(e, lax.rem(t + k, tensors)) for k in range(1, tensors)]
        beside, above = device(z, 1 - y, x, c), device(z + 1, y, x, c)
        views = [
            lambda b: weights.at[QUERY, block_rows(b, depth), :],
            lambda b: weights.at[KEY, block_rows(b, depth), :],
            lambda b: weights.at[VALUE, block_rows(b, depth), :],
            lambda b: small_all.at[b],
            lambda b: out_all.at[pl.ds(0, out_half), block_rows(b, out_columns)],
            lambda b: grad_view(b, x, c),
            lambda b: out_all.at[pl.ds(out_half, out_half), block_rows(b, out_columns)],
        ]
        across, twin = device(z, y, 1 - x, c), device(z, y, x, 1 - c)

        def quarter_at(xx, cc):
            return pl.ds(pl.multiple_of((xx * NC + cc) * quarter, quarter), quarter)

        def grad_view(b, xx, cc):
            return grad_all.at[block_rows(b, rows), quarter_at(xx, cc)]

        def grad_across(b, landing=False):
            piece = grad_view(b, 1 - x if landing else x, c)
            return remote(piece, piece, hx_s.at[b], hx_r.at[b], across)

        def grad_twin(b, relayed, landing=False):
            piece = grad_view(b, 1 - x if relayed else x, 1 - c if landing else c)
            return remote(piece, piece, hc_s.at[b, relayed], hc_r.at[b, relayed], twin)

        line = LineGather(
            [SMALL, VALUE, KEY, QUERY, OUT, GRAD, REST],
            [
                own_w.at[0], own_w.at[1], own_w.at[2], small_ref, own_out.at[pl.ds(0, out_half)],
                grad_in.at[:, quarter_at(x, c)], own_out.at[pl.ds(out_half, out_half)],
            ],
            views, send_sem, recv_sem, y_first=(OUT,),
        )
        small_ref[...] = jnp.zeros_like(small_ref)
        small_ref[0:1, :] = gain_one_ref[...].astype(low).astype(f32)
        small_ref[1:2, :] = gain_two_ref[...].astype(low).astype(f32)
        small_ref[2:3, : qk_gain.shape[1]] = qk_ref[...].astype(low).astype(f32)
        small_ref[8 : 8 + experts, :] = w_router_ref[...]
        expert_row = lax.broadcasted_iota(jnp.int32, (experts, rows), 0)
        named = jnp.zeros((experts, rows), f32)
        for k in range(routes.shape[0]):
            named = jnp.where(routes_ref[k : k + 1, :] == expert_row, 1.0, named)
        small_ref[8 + experts : 8 + 2 * experts, :] = named
        greet(line.partners() + [(mate, None) for mate in mates])
        line.start(SMALL, 0)
        for part in (VALUE, KEY, QUERY):
            def cast(i, carry, part=part):
                r = pl.ds(pl.multiple_of(i * 32, 32), 32)
                own_w[part, r, :] = w_ref[part, r, :].astype(low)
                return carry

            lax.fori_loop(0, depth // 32, cast, 0)
            if part != QUERY:
                line.start(part, 0)

        def cast_out(i, carry):
            r = pl.ds(pl.multiple_of(i * 32, 32), 32)
            own_out[r, :] = out_ref[r, :].astype(low)
            return carry

        lax.fori_loop(0, out_rows // 32, cast_out, 0)
        keep_out = pltpu.make_async_copy(own_out, out_all.at[:, block_rows(line.block(0), out_columns)], kept.at[0])
        keep_out.start()
        keep_grad = pltpu.make_async_copy(grad_in, grad_all.at[block_rows(line.block(0), rows), :], kept.at[1])
        keep_grad.start()

        def square(i, carry):
            r = pl.ds(pl.multiple_of(i * 32, 32), 32)
            value = tok_ref[r, :].astype(f32)
            scale_ref[r, 0:1] = lax.rsqrt(jnp.mean(value * value, axis=-1, keepdims=True) + EPS)
            return carry

        lax.fori_loop(0, rows // 32, square, 0)
        total[...] = jnp.zeros_like(total)
        own_small = pltpu.make_async_copy(small_ref, small_all.at[line.block(0)], small_sem)
        own_small.start()

        def use(stream, rel):
            b = line.block(rel)
            at = pl.ds(pl.multiple_of(b * depth, depth), depth)
            if stream == SMALL:
                gain = small_ref[0:1, :] if rel == 0 else small_all[b, 0:1, :]
                h1_ref[:, at] = (tok_ref[:, at].astype(f32) * scale_ref[:, 0:1] * gain).astype(low)
                return
            block = own_w[stream] if rel == 0 else weights[stream, block_rows(b, depth), :]
            total[stream] += dot(h1_ref[:, at], block, (1, 0))

        def event(stream, rel):
            def body():
                line.arrive(stream, rel)
                if line.forwards(stream, rel):
                    marks = len(line.pending)
                    line.start(stream, rel)
                    late = line.pending[marks:]
                    del line.pending[marks:]
                    line.finish_later(late, rel)
                if stream == GRAD:
                    b = line.block(rel)
                    grad_across(b).start()
                    grad_twin(b, 0).start()
                elif stream not in (OUT, REST):
                    use(stream, rel)
            run_if(line.exists(rel), body)

        use(SMALL, 0)
        use(VALUE, 0)
        own_small.wait()

        units = down_in.shape[1]
        for n, copy in enumerate(wide_loads):
            copy.wait()

            def round_wide(i, carry, n=n):
                r = pl.ds(pl.multiple_of(i * 64, 64), 64)
                wide_low[r, pl.ds(n * units, units)] = wide_in[n, r, :].astype(low)
                return carry

            lax.fori_loop(0, width // 64, round_wide, 0)
        wide_out = pltpu.make_async_copy(wide_low, gate_up, wide_s.at[0])
        wide_out.start()
        down_loads = [
            pltpu.make_async_copy(down_in.at[k], down_f.at[pl.ds(k * units, units), :], wide_s.at[1 + k])
            for k in range(2)
        ]
        for copy in down_loads:
            copy.start()

        use(KEY, 0)
        def events(*pairs):
            for stream, rels in pairs:
                for rel in rels:
                    event(stream, rel)

        for rel in (7, 1, 4, 2, 5):
            event(SMALL, rel)
            event(VALUE, rel)
        for copy in down_loads:
            copy.wait()

        def round_down(i, carry):
            r = pl.ds(pl.multiple_of(i * 32, 32), 32)
            down_low[r, :] = down_f[r, :].astype(low)
            return carry

        lax.fori_loop(0, 2 * units // 32, round_down, 0)
        down_copy = pltpu.make_async_copy(down_low, down_out, wide_s.at[3])
        down_copy.start()
        line.start(QUERY, 0)
        for rel in (3, 6):
            event(SMALL, rel)
            event(VALUE, rel)
        events((KEY, (7, 1, 4)))
        for rel in (8, 11, 9, 12, 10, 13):
            event(SMALL, rel)
            event(VALUE, rel)

        slices = HEAD // GROUPS
        for b in range(GROUPS):
            at = pl.ds(b * depth, depth)
            gain_ref[0:2, at] = small_all[b, 0:2, :]
            router_ref[:, at] = small_all[b, 8 : 8 + experts, :].astype(low)
            tall = jnp.concatenate(
                [small_all[b, 8 + experts : 8 + 2 * experts, :], jnp.zeros((128 - experts, depth), f32)], axis=0
            )
            chosen_ref[pl.ds(b * depth, depth), :] = jnp.transpose(tall)[:, :experts].astype(low)
        for which in range(2):
            for head in range(heads):
                start = (which * heads + head) * slices
                gain_ref[2 + which : 3 + which, pl.ds(head * HEAD, HEAD)] = jnp.concatenate(
                    [small_all[b, 2:3, start : start + slices] for b in range(GROUPS)], axis=1
                )

        def context_copy(which, k):
            if k == 2:
                source, target = 0, above
            elif k == 4:
                source, target = 2, above
            else:
                source, target = jnp.where(y == 0, k - 1, k + 1), beside
            return remote(
                context.at[source, which], context.at[k, which], c_s.at[which, k], c_r.at[which, k], target
            )

        sends = {2: z < NZ - 1, 4: (z >= 1) & (z < NZ - 1), 1: (y == 0) | (z >= 1), 3: z >= 1 + y}
        takes = {2: z >= 1, 4: z >= 2, 1: (y == 1) | (z >= 1), 3: z >= 2 - y}

        def context_send(which, k):
            run_if(sends[k], lambda: context_copy(which, k).start())

        def context_take(which, k):
            run_if(takes[k], lambda: context_copy(which, k).wait_recv())

        for k in range(1, back + 1):
            def clear(k=k):
                context[k] = jnp.zeros_like(context[k])
            run_if(jnp.logical_not(takes[k]), clear)

        context[0, 1] = total[VALUE].astype(low)
        context_send(1, 2)
        run_if(y == 0, lambda: context_copy(1, 1).start())
        events((KEY, (2, 5, 3, 6)), (QUERY, (7, 1, 4)))
        line.start(GRAD, 0)
        line.start(OUT, 0)
        line.start(REST, 0)
        events((KEY, (8, 11, 9, 12, 10, 13)))
        key_raw = total[KEY]
        raw_ref[1] = key_raw
        exchange_rows(jnp.sum(key_raw * key_raw, axis=-1, keepdims=True), part_k, land_k, ks_s, ks_r, mates)
        use(QUERY, 0)
        events((QUERY, (2, 5)))
        key_scale = lax.rsqrt(exchanged_rows(part_k, land_k, ks_s, ks_r, mates) / width + EPS)
        scale_ref[:, 2:3] = key_scale
        def rotated(which, scale, store):
            for head in range(heads):
                at = pl.ds(head * HEAD, HEAD)
                value = total[which, :, at] * scale * gain_ref[2 + which : 3 + which, at]
                store(at, turn(value, cos_ref[...], sin_ref[...]).astype(low))

        def store_key(at, value):
            context[0, 0, :, at] = value

        rotated(KEY, key_scale, store_key)
        context_send(0, 2)
        run_if(y == 0, lambda: context_copy(0, 1).start())

        def relay_two(which):
            context_take(which, 2)
            context_send(which, 4)
            run_if((y == 1) & (z >= 1), lambda: context_copy(which, 1).start())
            run_if((y == 0) & sends[3], lambda: context_copy(which, 3).start())

        def relay_four(which):
            context_take(which, 4)
            run_if((y == 1) & sends[3], lambda: context_copy(which, 3).start())

        relay_two(1)
        events((QUERY, (3, 6)), (GRAD, (7, 1, 4)), (OUT, (7, 1, 4)), (REST, (7, 1, 4)))
        relay_four(1)
        events((QUERY, (8, 11)), (GRAD, (2, 5)), (OUT, (8, 11, 2, 5)), (REST, (2, 5)))
        relay_two(0)
        events((QUERY, (9, 12, 10, 13)))
        query_raw = total[QUERY]
        raw_ref[0] = query_raw
        exchange_rows(jnp.sum(query_raw * query_raw, axis=-1, keepdims=True), part_q, land_q, qs_s, qs_r, mates)
        for part in range(parts):
            weights[part, block_rows(line.block(0), depth), :] = own_w[part]
        keep = pltpu.make_async_copy(weights, w_all, out_sem)
        keep.start()
        keep_more = [
            pltpu.make_async_copy(h1_ref, h1_out, kept.at[2]),
            pltpu.make_async_copy(raw_ref, raw_out, kept.at[3]),
        ]
        for copy in keep_more:
            copy.start()
        events((GRAD, (3, 6)), (OUT, (9, 12, 3, 6)), (REST, (3, 6, 8, 11)))
        relay_four(0)
        query_scale = lax.rsqrt(exchanged_rows(part_q, land_q, qs_s, qs_r, mates) / width + EPS)
        scale_ref[:, 1:2] = query_scale

        def store_query(at, value):
            q_ref[:, at] = value

        rotated(QUERY, query_scale, store_query)
        events((GRAD, (8, 11, 9, 12)), (OUT, (10, 13)), (REST, (9, 12, 10, 13)), (GRAD, (10, 13)))
        for which in (1, 0):
            for k in (1, 3):
                context_take(which, k)
        for rel in line.order():
            def relay(rel=rel):
                b = line.block(rel)
                grad_across(b, True).wait_recv()
                grad_twin(b, 1).start()
            run_if(line.exists(rel), relay)
        for rel in line.order():
            def landed(rel=rel):
                b = line.block(rel)
                grad_across(b).wait_send()
                for relayed in range(2):
                    grad_twin(b, relayed, True).wait_recv()
                    grad_twin(b, relayed).wait_send()
            run_if(line.exists(rel), landed)
        line.finish()
        for copy in keep_more:
            copy.wait()
        wide_out.wait()
        down_copy.wait()
        keep_out.wait()
        keep_grad.wait()
        for which in range(2):
            for k in range(1, back + 1):
                run_if(sends[k], lambda which=which, k=k: context_copy(which, k).wait_send())
        drain_rows(part_k, land_k, ks_s, ks_r, mates)
        drain_rows(part_q, land_q, qs_s, qs_r, mates)
        keep.wait()

    shape, dma = jax.ShapeDtypeStruct, pltpu.SemaphoreType.DMA
    return pl.pallas_call(
        kernel,
        out_shape=(
            shape((parts, depth * GROUPS, columns), low),
            shape((out_rows, out_columns * GROUPS), low),
            shape((rows * GROUPS, width), low),
            shape((rows, width), low),
            shape((2, rows, columns), f32),
            shape((width, 4 * w_down.shape[1]), low),
            shape((2 * w_down.shape[1], width), low),
            shape((8, width), f32),
            shape((experts, width), low),
            shape((rows * GROUPS, experts), low),
            shape((rows, 128), f32),
            shape((rows, columns), low),
            shape((back + 1, 2, rows, columns), low),
        ),
        in_specs=[VMEM, VMEM, VMEM, HBM] + [VMEM] * 7 + [HBM, HBM, HBM],
        out_specs=(HBM,) * 7 + (VMEM,) * 6,
        scratch_shapes=[
            pltpu.VMEM(small_shape, f32),
            pltpu.VMEM((GROUPS,) + small_shape, f32),
            pltpu.VMEM((rows, width), low),
            pltpu.VMEM((2, rows, columns), f32),
            pltpu.VMEM((4, width, w_down.shape[1]), f32),
            pltpu.VMEM((width, 4 * w_down.shape[1]), low),
            pltpu.VMEM((2 * w_down.shape[1], width), f32),
            pltpu.VMEM((2 * w_down.shape[1], width), low),
            pltpu.VMEM((parts, depth, columns), low),
            pltpu.VMEM((out_rows, out_columns), low),
            pltpu.VMEM((parts, depth * GROUPS, columns), low),
            pltpu.VMEM((parts, rows, columns), f32),
            pltpu.VMEM((8, rows), f32),
            pltpu.VMEM((tensors - 1, 8, rows), f32),
            pltpu.VMEM((8, rows), f32),
            pltpu.VMEM((tensors - 1, 8, rows), f32),
            dma((7, 14, 3)), dma((7, 14)), dma, dma, dma((4,)),
            dma((tensors - 1,)), dma((tensors - 1,)), dma((tensors - 1,)), dma((tensors - 1,)),
            dma((2, back + 1)), dma((2, back + 1)),
            dma((GROUPS,)), dma((GROUPS,)), dma((GROUPS, 2)), dma((GROUPS, 2)), dma((4,)),
        ],
        compiler_params=comm_params(collective_id, 62),
        cost_estimate=cost(100),
        name="project",
    )(
        tokens, w_qkv, w_out, out_grad, gain_one, gain_two, qk_gain, w_router, routes, cosine, sine,
        w_gate, w_up, w_down,
    )


def attend(query, context, segment_query, segment_keys, tokens, out_low, gain, collective_id):
    rows, columns = query.shape
    width = tokens.shape[1]
    blocks = context.shape[0]
    heads = columns // HEAD
    half, quarter = width // 2, width // 4
    low, f32 = jnp.bfloat16, jnp.float32

    def kernel(
        q_ref, context_in, sq_ref, sk_ref, tok_ref, out_in, gain_ref,
        o_ref, lse_ref, x1_out, h2_out, scale_ref,
        context_ref, out_ref, x1_ref, h2_ref, copy_sem, part, full, core_buf, x_buf, send_sem, recv_sem,
    ):
        z, y, x, c = place()
        across, twin = device(z, y, 1 - x, c), device(z, y, x, 1 - c)
        context_load = pltpu.make_async_copy(context_in, context_ref, copy_sem.at[0])
        context_load.start()
        out_load = pltpu.make_async_copy(out_in, out_ref, copy_sem.at[1])
        out_load.start()
        greet([(across, None), (twin, None)])
        row = lax.broadcasted_iota(jnp.int32, (rows, rows), 0)
        column = lax.broadcasted_iota(jnp.int32, (rows, rows), 1)
        allowed = []
        for k in range(blocks):
            distance = row - column + k * rows
            allowed.append(
                (sq_ref[...] == sk_ref[k : k + 1, :]) & (distance >= 0) & (distance < WINDOW)
            )
        line = lax.broadcasted_iota(jnp.int32, (rows, 128), 1)
        lse = jnp.zeros((rows, 128), f32)
        context_load.wait()
        for head in range(heads):
            at = pl.ds(head * HEAD, HEAD)
            scores = [
                jnp.where(
                    allowed[k], dot(q_ref[:, at], context_ref[k, 0, :, at], (1, 1)) * HEAD ** (-0.5), -1e30
                )
                for k in range(blocks)
            ]
            largest = scores[0]
            for k in range(1, blocks):
                largest = jnp.maximum(largest, scores[k])
            largest = jnp.max(largest, axis=-1, keepdims=True)
            weights = [jnp.exp(s - largest) for s in scores]
            amount = weights[0]
            for k in range(1, blocks):
                amount = amount + weights[k]
            amount = jnp.sum(amount, axis=-1, keepdims=True)
            inverse = 1.0 / amount
            value = jnp.zeros((rows, HEAD), f32)
            for k in range(blocks):
                value = value + dot((weights[k] * inverse).astype(low), context_ref[k, 1, :, at], (1, 0))
            o_ref[:, at] = value.astype(low)
            lse = jnp.where(line == head, largest + jnp.log(amount), lse)
        lse_ref[...] = lse

        def half_of(cc):
            return pl.ds(pl.multiple_of(cc * half, half), half)

        def fill(cc):
            def body(k, carry):
                at = pl.ds(pl.multiple_of(cc * half + k * quarter, quarter), quarter)
                part[:, at] = dot(o_ref[...], out_ref[:, at], (1, 0)).astype(low)
                return carry

            lax.fori_loop(0, 2, body, 0)

        out_load.wait()
        fill(1 - c)
        group_sum(part, full, core_buf, x_buf, send_sem, recv_sem, lambda: fill(c))

        def norm(i, carry):
            r = pl.ds(pl.multiple_of(i * 32, 32), 32)
            value = tok_ref[r, :].astype(f32) + full[r, :].astype(f32)
            scale = lax.rsqrt(jnp.mean(value * value, axis=-1, keepdims=True) + EPS)
            x1_ref[r, :] = value
            scale_ref[r, :] = jnp.broadcast_to(scale, (32, 128))
            h2_ref[r, :] = (value * scale * gain_ref[1:2, :]).astype(low)
            return carry

        lax.fori_loop(0, rows // 32, norm, 0)
        keep = [
            pltpu.make_async_copy(x1_ref, x1_out, copy_sem.at[2]),
            pltpu.make_async_copy(h2_ref, h2_out, copy_sem.at[3]),
        ]
        for copy in keep:
            copy.start()
        for copy in keep:
            copy.wait()

    shape, dma = jax.ShapeDtypeStruct, pltpu.SemaphoreType.DMA
    return pl.pallas_call(
        kernel,
        out_shape=(
            shape((rows, columns), low),
            shape((rows, 128), f32),
            shape((rows, width), f32),
            shape((rows, width), low),
            shape((rows, 128), f32),
        ),
        in_specs=[VMEM, HBM, VMEM, VMEM, VMEM, HBM, VMEM],
        out_specs=(VMEM, VMEM, HBM, HBM, VMEM),
        scratch_shapes=[
            pltpu.VMEM(context.shape, low),
            pltpu.VMEM(out_low.shape, low),
            pltpu.VMEM((rows, width), f32),
            pltpu.VMEM((rows, width), low),
            dma((4,)),
            pltpu.VMEM((rows, width), low),
            pltpu.VMEM((rows, width), low),
            pltpu.VMEM((rows, half), low),
            pltpu.VMEM((rows, quarter), low),
            dma((5,)), dma((5,)),
        ],
        compiler_params=comm_params(collective_id, 62),
        cost_estimate=cost(40),
        name="attend",
    )(query, context, segment_query, segment_keys, tokens, out_low, gain)


def attend_back(
    grad_hidden, grad_probs, router_t, hidden_two, residual, scale_two, gains, out_grad,
    query, context, segment_query, segment_keys, attended, log_sums, raw, scales,
    cosine, sine, hidden_one, tokens, attended_all, qkv_low, out_low, collective_id,
):
    rows, width = tokens.shape
    columns = query.shape[1]
    heads = columns // HEAD
    experts = router_t.shape[0]
    blocks = context.shape[0]
    depth = width // GROUPS
    small_rows = 8 + experts
    tensors = NX * NC
    half, quarter = width // 2, width // 4
    low, f32 = jnp.bfloat16, jnp.float32
    QUERY, KEY, VALUE, OUT, SMALL = 0, 1, 2, 3, 4

    def kernel(
        dh_ref, gates_ref, router_ref, h2_ref, x1_ref, s2_ref, gain_ref, dy_ref,
        q_ref, context_in, sq_ref, sk_ref, o_ref, lse_ref, raw_in, scale_ref,
        cos_ref, sin_ref, h1_in, tok_in, o_all_in, w_hbm, out_ref,
        tok_grad, qkv_sum, out_sum, small_sum,
        context_ref, raw_ref, h1_ref, tok_ref, o_all, load_sem, weights, dx1, da, do, dot_sums, dq, dkv, scaled, proj, send_kv, land_y, land_z,
        part, full, core_buf, x_buf, small, line_sum,
        main_buf, da_all, small_buf, part_k, land_k, part_q, land_q,
        w_sem, y_s, y_r, z_s, z_r, group_s, group_r, ks_s, ks_r, qs_s, qs_r, line_s, line_r, far_s, far_r, near_s, near_r,
    ):
        z, y, x, c = place()
        e, t = lax.axis_index("expert"), lax.axis_index("tensor")
        mates = [(e, lax.rem(t + k, tensors)) for k in range(1, tensors)]
        beside, below = device(z, 1 - y, x, c), device(z - 1, y, x, c)
        fetch = pltpu.make_async_copy(w_hbm, weights, w_sem)
        fetch.start()
        loads = [
            pltpu.make_async_copy(source, target, load_sem.at[k])
            for k, (source, target) in enumerate(
                (
                    (context_in, context_ref), (raw_in, raw_ref), (h1_in, h1_ref), (tok_in, tok_ref),
                    (o_all_in, o_all),
                )
            )
        ]
        for copy in loads:
            copy.start()

        def own_part(s, b):
            if s == SMALL:
                return small[b]
            at = pl.ds(pl.multiple_of(b * depth, depth), depth)
            return dot(h1_ref[:, at], proj[s], (0, 0))

        peers = [(lax.rem(e + k, GROUPS), t) for k in range(1, GROUPS)]
        share = rows // tensors
        share_at = pl.ds(pl.multiple_of(t * share, share), share)

        def columns_of(owner):
            return pl.ds(pl.multiple_of(owner * depth, depth), depth)

        def da_far(k):
            owner = lax.rem(e + k, GROUPS)
            return remote(
                da.at[share_at, columns_of(owner)], da_all.at[e, share_at, :], far_s.at[k - 1], far_r.at[k - 1],
                peers[k - 1],
            )

        def da_near(k):
            piece = da_all.at[:, share_at, :]
            return remote(piece, piece, near_s.at[k], near_r.at[k], mates[k])

        def da_start():
            for k in range(1, GROUPS):
                da_far(k).start()
            da_all[e, share_at, :] = da[share_at, columns_of(e)]

        def da_spread():
            for k in range(1, GROUPS):
                landing = da_all.at[lax.rem(e + GROUPS - k, GROUPS), share_at, :]
                remote(landing, landing, far_s.at[k - 1], far_r.at[k - 1], peers[k - 1]).wait_recv()
            for k in range(tensors - 1):
                da_near(k).start()

        def da_end():
            for k in range(tensors - 1):
                theirs = lax.rem(t + tensors - 1 - k, tensors)
                landing = da_all.at[:, pl.ds(pl.multiple_of(theirs * share, share), share), :]
                remote(landing, landing, near_s.at[k], near_r.at[k], mates[k]).wait_recv()
            result = jnp.zeros((columns, depth), f32)
            for b in range(GROUPS):
                result = result + dot(o_all[pl.ds(b * rows, rows), :], da_all[b], (0, 0))
            out_sum[...] = result
            for k in range(1, GROUPS):
                da_far(k).wait_send()
            for k in range(tensors - 1):
                da_near(k).wait_send()

        def slot(kind):
            def view(s, zz):
                if s == SMALL:
                    return small_buf.at[kind, zz]
                return main_buf.at[kind, zz, s]
            return view

        line = LineReduce([], lambda s, zz, yy: slot(3)(s, zz), slot(0), slot(1), slot(2), line_s, line_r)
        greet([(target, None) for target in mates + peers])

        grad_probs = gates_ref[...]
        logits = dot(h2_ref[...], router_ref[...], (1, 1))
        shifted = jnp.exp(logits - jnp.max(logits, axis=-1, keepdims=True))
        probs = shifted / jnp.sum(shifted, axis=-1, keepdims=True)
        grad_logits = probs * (grad_probs - jnp.sum(probs * grad_probs, axis=-1, keepdims=True))
        tall = jnp.transpose(
            jnp.concatenate([grad_logits, jnp.zeros((rows, 128 - experts), f32)], axis=1)
        )
        grad_logits = grad_logits.astype(low)
        tall = tall.astype(low)
        for b in range(GROUPS):
            small[b] = jnp.zeros_like(small[b])
            small[b, 8 : 8 + experts, :] = dot(tall, h2_ref[:, pl.ds(b * depth, depth)], (1, 0))[:experts]
        dx1[...] = dot(grad_logits, router_ref[...], (1, 0))
        line_sum[...] = jnp.zeros_like(line_sum)

        def norm_two(i, carry):
            r = pl.ds(pl.multiple_of(i * 32, 32), 32)
            grad = dh_ref[r, :].astype(f32) + dx1[r, :]
            value, scale = x1_ref[r, :], s2_ref[r, 0:1]
            line_sum[0:1, :] += jnp.sum(grad * (value * scale), axis=0, keepdims=True)
            grad = grad * gain_ref[1:2, :]
            inner = jnp.mean(grad * value, axis=-1, keepdims=True)
            result = dy_ref[r, :].astype(f32) + scale * grad - value * (scale * scale * scale) * inner
            dx1[r, :] = result
            da[r, :] = result.astype(low)
            return carry

        lax.fori_loop(0, rows // 32, norm_two, 0)

        da_start()

        for copy in loads:
            copy.wait()
        do[...] = dot(da[...], out_ref[...], (1, 1)).astype(low)
        wide = lax.broadcasted_iota(jnp.int32, (rows, 128), 1)
        sums = jnp.zeros((rows, 128), f32)
        for head in range(heads):
            at = pl.ds(head * HEAD, HEAD)
            inner = jnp.sum(do[:, at].astype(f32) * o_ref[:, at].astype(f32), axis=-1, keepdims=True)
            sums = jnp.where(wide == head, inner, sums)
        dot_sums[...] = sums
        dq[...] = jnp.zeros_like(dq)
        row = lax.broadcasted_iota(jnp.int32, (rows, rows), 0)
        column = lax.broadcasted_iota(jnp.int32, (rows, rows), 1)

        def attention_block(k):
            distance = row - column + k * rows
            allowed = (sq_ref[...] == sk_ref[k : k + 1, :]) & (distance >= 0) & (distance < WINDOW)
            for head in range(heads):
                at = pl.ds(head * HEAD, HEAD)
                queries, keys, values = q_ref[:, at], context_ref[k, 0, :, at], context_ref[k, 1, :, at]
                scores = dot(queries, keys, (1, 1)) * HEAD ** (-0.5)
                weight = jnp.where(allowed, jnp.exp(scores - lse_ref[:, head : head + 1]), 0.0)
                grad_weight = dot(do[:, at], values, (1, 1))
                grad_score = (
                    weight * (grad_weight - dot_sums[:, head : head + 1]) * HEAD ** (-0.5)
                ).astype(low)
                dq[:, at] += dot(grad_score, keys, (1, 0))
                dkv[k, 0, :, at] = dot(grad_score, queries, (0, 0))
                dkv[k, 1, :, at] = dot(weight.astype(low), do[:, at], (0, 0))

        exists = {0: None, 1: (y == 1) | (z >= 1), 2: z >= 1, 3: z >= 2 - y, 4: z >= 2}
        comes = {1: (y == 0) | (z >= 1), 3: z >= 1 + y}

        def kv_copy(which, k):
            if k in (1, 3):
                landing, target = land_y.at[k // 2, which], beside
                return remote(send_kv.at[k - 1, which], landing, y_s.at[k // 2, which], y_r.at[k // 2, which], target)
            landing = land_z.at[k // 2 - 1, which]
            return remote(
                send_kv.at[k - 1, which], landing, z_s.at[k // 2 - 1, which], z_r.at[k // 2 - 1, which], below
            )

        def kv_send(which, k):
            send_kv[k - 1, which] = dkv[k, which].astype(low)
            kv_copy(which, k).start()

        def merge(into, which, landed):
            add_to(dkv.at[into, which], dkv.at[into, which], landed, 32)

        for k in (3, 1, 4, 2, 0):
            def one(k=k):
                attention_block(k)
                if k in (1, 3):
                    kv_send(1, k)
                    kv_send(0, k)
            run_if(exists[k], one)

        def take_three(which):
            def land():
                kv_copy(which, 3).wait_recv()
                pl.when(y == 1)(lambda: merge(4, which, land_y.at[1, which]))
                pl.when(y == 0)(lambda: merge(2, which, land_y.at[1, which]))
            run_if(comes[3], land)
            run_if(exists[4], lambda: kv_send(which, 4))

        def take_one(which):
            def land():
                kv_copy(which, 1).wait_recv()
                pl.when(y == 1)(lambda: merge(2, which, land_y.at[0, which]))
                pl.when(y == 0)(lambda: merge(0, which, land_y.at[0, which]))
            run_if(comes[1], land)

        def take_four(which):
            def land():
                kv_copy(which, 4).wait_recv()
                merge(2, which, land_z.at[1, which])
            run_if((z >= 1) & (z < NZ - 1), land)
            run_if(exists[2], lambda: kv_send(which, 2))

        def take_two(which):
            def land():
                kv_copy(which, 2).wait_recv()
                merge(0, which, land_z.at[0, which])
            run_if(z < NZ - 1, land)

        def unturn(which, grad_of):
            inner = jnp.zeros((rows, 1), f32)
            for head in range(heads):
                at = pl.ds(head * HEAD, HEAD)
                grad = turn(grad_of(at), cos_ref[...], -sin_ref[...])
                value = raw_ref[which, :, at]
                line_sum[1 + which : 2 + which, at] = jnp.sum(
                    grad * (value * scale_ref[:, 1 + which : 2 + which]), axis=0, keepdims=True
                )
                grad = grad * gain_ref[2 + which : 3 + which, at]
                scaled[which, :, at] = grad
                inner = inner + jnp.sum(grad * value, axis=-1, keepdims=True)
            return inner

        def denorm(which, inner):
            scale = scale_ref[:, 1 + which : 2 + which]
            rest = scale * scale * scale * inner / width
            for head in range(heads):
                at = pl.ds(head * HEAD, HEAD)
                proj[which, :, at] = (
                    scale * scaled[which, :, at] - raw_ref[which, :, at] * rest
                ).astype(low)

        def send_beside(s):
            for zz in Z_ORDER:
                buffer = slot(3)(s, zz)
                buffer[...] = own_part(s, zz * NY + 1 - y).astype(buffer.dtype)
                line.to_y(s, zz)

        exchange_rows(unturn(QUERY, lambda at: dq[:, at]), part_q, land_q, qs_s, qs_r, mates)
        take_three(1)
        take_three(0)
        denorm(QUERY, exchanged_rows(part_q, land_q, qs_s, qs_r, mates))
        send_beside(QUERY)
        da_spread()
        take_one(1)
        take_one(0)
        take_four(1)
        take_four(0)
        take_two(1)
        proj[VALUE] = dkv[0, 1].astype(low)
        send_beside(VALUE)
        take_two(0)
        exchange_rows(unturn(KEY, lambda at: dkv[0, 0, :, at]), part_k, land_k, ks_s, ks_r, mates)
        denorm(KEY, exchanged_rows(part_k, land_k, ks_s, ks_r, mates))
        send_beside(KEY)
        fetch.wait()

        def half_of(cc):
            def body(i, carry):
                at = pl.ds(pl.multiple_of(cc * half + i * quarter, quarter), quarter)
                value = dot(proj[0], weights[0, at, :], (1, 1))
                for s in (1, 2):
                    value = value + dot(proj[s], weights[s, at, :], (1, 1))
                part[:, at] = value.astype(low)
                return carry

            lax.fori_loop(0, 2, body, 0)

        stages = group_stages(part, full, core_buf, x_buf, group_s, group_r)
        half_of(1 - c)
        stages[0]()
        half_of(c)
        stages[1]()

        def hop(s, zz, k):
            def upward():
                if k > 0:
                    line.take(s, zz, 1)
                line.copy(s, zz, 1).start()

            def downward():
                if k > 0:
                    line.take(s, zz, 2)
                line.copy(s, zz, 2).start()

            if k < zz:
                run_if((z < zz) & (z == k), upward)
            if NZ - 1 - k > zz:
                run_if((z > zz) & (NZ - 1 - z == k), downward)

        def receive(s, zz):
            line.copy(s, zz, 0).wait_recv()
            buffer = slot(0)(s, zz)
            buffer[...] = (buffer[...].astype(f32) + own_part(s, zz * NY + y)).astype(buffer.dtype)

        units = []

        def run_units(s):
            for zz in Z_ORDER:
                receive(s, zz)
                hop(s, zz, 0)
                units.append((s, zz))
                for k in (1, 2):
                    if len(units) > k:
                        hop(*units[-1 - k], k)

        def norm_one(i, carry):
            r = pl.ds(pl.multiple_of(i * 32, 32), 32)
            grad, value, scale = full[r, :].astype(f32), tok_ref[r, :].astype(f32), scale_ref[r, 0:1]
            line_sum[3:4, :] += jnp.sum(grad * (value * scale), axis=0, keepdims=True)
            grad = grad * gain_ref[0:1, :]
            inner = jnp.mean(grad * value, axis=-1, keepdims=True)
            tok_grad[r, :] = (
                dx1[r, :] + scale * grad - value * (scale * scale * scale) * inner
            ).astype(low)
            return carry

        run_units(QUERY)
        stages[2]()
        run_units(VALUE)
        da_end()
        stages[3]()
        stages[4]()
        lax.fori_loop(0, rows // 32, norm_one, 0)
        for b in range(GROUPS):
            at = pl.ds(b * depth, depth)
            small[b, 0:1, :] = line_sum[3:4, at]
            small[b, 1:2, :] = line_sum[0:1, at]
            for which in range(2):
                for k in range(columns // depth):
                    small[b, 2 + 2 * which + k : 3 + 2 * which + k, :] = line_sum[
                        1 + which : 2 + which, pl.ds(k * depth, depth)
                    ]
        send_beside(SMALL)
        run_units(KEY)
        run_units(SMALL)
        hop(*units[-1], 1)
        hop(*units[-2], 2)
        hop(*units[-1], 2)

        def done(s, total):
            target = qkv_sum.at[s] if s < OUT else small_sum
            target[...] = total[...].astype(f32)

        line.streams = [QUERY, VALUE, KEY, SMALL]
        line.home(done)
        line.finish()
        for which in range(2):
            for k in (1, 2, 3, 4):
                run_if(exists[k], lambda which=which, k=k: kv_copy(which, k).wait_send())
        drain_rows(part_k, land_k, ks_s, ks_r, mates)
        drain_rows(part_q, land_q, qs_s, qs_r, mates)

    shape, dma, vmem = jax.ShapeDtypeStruct, pltpu.SemaphoreType.DMA, pltpu.VMEM
    return pl.pallas_call(
        kernel,
        out_shape=(
            shape((rows, width), low),
            shape((3, depth, columns), f32),
            shape((columns, depth), f32),
            shape((small_rows, depth), f32),
        ),
        in_specs=[HBM if k in (9, 14, 18, 19, 20, 21) else VMEM for k in range(23)],
        out_specs=(VMEM,) * 4,
        scratch_shapes=[
            vmem(context.shape, low),
            vmem(raw.shape, f32),
            vmem(hidden_one.shape, low),
            vmem(tokens.shape, low),
            vmem(attended_all.shape, low),
            dma((5,)),
            vmem(qkv_low.shape, low),
            vmem((rows, width), f32),
            vmem((rows, width), low),
            vmem((rows, columns), low),
            vmem((rows, 128), f32),
            vmem((rows, columns), f32),
            vmem((blocks, 2, rows, columns), f32),
            vmem((2, rows, columns), f32),
            vmem((3, rows, columns), low),
            vmem((blocks - 1, 2, rows, columns), low),
            vmem((2, 2, rows, columns), low),
            vmem((2, 2, rows, columns), low),
            vmem((rows, width), low),
            vmem((rows, width), low),
            vmem((rows, half), low),
            vmem((rows, quarter), low),
            vmem((GROUPS, small_rows, depth), f32),
            vmem((8, width), f32),
            vmem((4, NZ, 3, depth, columns), low),
            vmem((GROUPS, rows, depth), low),
            vmem((4, NZ, small_rows, depth), f32),
            vmem((8, rows), f32),
            vmem((tensors - 1, 8, rows), f32),
            vmem((8, rows), f32),
            vmem((tensors - 1, 8, rows), f32),
            dma, dma((2, 2)), dma((2, 2)), dma((2, 2)), dma((2, 2)), dma((5,)), dma((5,)),
            dma((tensors - 1,)), dma((tensors - 1,)), dma((tensors - 1,)), dma((tensors - 1,)),
            dma((5, NZ, 3)), dma((5, NZ, 3)), dma((GROUPS - 1,)), dma((GROUPS - 1,)), dma((tensors - 1,)), dma((tensors - 1,)),
        ],
        compiler_params=comm_params(collective_id, 62),
        cost_estimate=cost(130),
        name="attend_back",
    )(
        grad_hidden, grad_probs, router_t, hidden_two, residual, scale_two, gains, out_grad,
        query, context, segment_query, segment_keys, attended, log_sums, raw, scales,
        cosine, sine, hidden_one, tokens, attended_all, qkv_low, out_low,
    )


def fast_shards(
    tokens_in,
    out_grad,
    w_qkv,
    w_attn_out,
    attn_gain,
    ffn_gain,
    qk_gain,
    w_router,
    w_gate,
    w_up,
    w_down,
    routes,
    segments,
):
    row_count, model_width = tokens_in.shape
    experts = w_router.shape[1]
    local_experts = w_gate.shape[0]
    heads_here = qk_gain.shape[1]
    local_width = heads_here * HEAD
    groups = lax.axis_size("expert")
    device_index = lax.axis_index("expert")
    tensor_index = lax.axis_index("tensor")
    quarter = model_width // lax.axis_size("tensor")
    hop_count = WINDOW // row_count
    score_scale = HEAD ** (-0.5)
    low = jnp.bfloat16

    chosen = jnp.any(
        routes[:, :, None] == jnp.arange(experts, dtype=jnp.int32)[None, None, :], axis=1
    ).astype(jnp.float32)
    qk_row = qk_gain.reshape(1, -1)

    global_rows = device_index * row_count + jnp.arange(row_count, dtype=jnp.int32)
    cosine_table, sine_table = angles(global_rows % SEQ, HEAD)
    wide_cosine = jnp.concatenate([cosine_table[:, 0], cosine_table[:, 0]], axis=1)
    wide_sine = jnp.concatenate([-sine_table[:, 0], sine_table[:, 0]], axis=1)
    (
        qkv_low, out_low, grad_out_all, hidden_one, raw, gate_up, down_low, gains, router_t, chosen_all,
        scales, query_low, context_blocks,
    ) = project(
        tokens_in, w_qkv, w_attn_out, out_grad, attn_gain[None, :], ffn_gain[None, :], qk_row, w_router.T, routes.T,
        wide_cosine, wide_sine, w_gate, w_up, w_down, 0,
    )
    segment_window = lax.dynamic_slice_in_dim(
        jnp.concatenate([jnp.full((WINDOW,), -1, jnp.int32), segments]),
        device_index * row_count, (hop_count + 1) * row_count,
    )
    segment_query = segment_window[WINDOW:]
    segment_keys = segment_window.reshape(hop_count + 1, row_count)[::-1]
    attended, log_sums, residual, hidden_two, scale_two_wide = attend(
        query_low, context_blocks, segment_query[:, None], segment_keys, tokens_in, out_low,
        gains, 2,
    )
    (
        block_out, grad_hidden_sum, grad_gate_sum, grad_gate_w, grad_up_w, grad_down, attended_all
    ) = expert_layer(
        hidden_two, grad_out_all, gate_up, down_low, router_t, chosen_all, residual, attended, 5
    )
    grad_probs = grad_gate_sum[:, :local_experts].reshape(experts, row_count).T * chosen
    grad_tokens, qkv_sum, out_sum, small_sum = attend_back(
        grad_hidden_sum, grad_probs, router_t, hidden_two, residual, scale_two_wide,
        gains, out_grad, query_low, context_blocks, segment_query[:, None], segment_keys,
        attended, log_sums, raw, scales, wide_cosine, wide_sine, hidden_one, tokens_in, attended_all,
        qkv_low, out_low, 8,
    )
    return (
        block_out,
        grad_tokens,
        qkv_sum,
        out_sum,
        small_sum[0],
        small_sum[1],
        lax.dynamic_slice_in_dim(
            small_sum[2:6].reshape(2, heads_here, HEAD),
            device_index * qk_gain.shape[2], qk_gain.shape[2], axis=2,
        ),
        small_sum[8 : 8 + experts].T,
        grad_gate_w,
        grad_up_w,
        grad_down,
    )


def solution(mesh):
    placed = (
        P("expert", None),
        P("expert", None),
        P(None, "expert", "tensor"),
        P("tensor", "expert"),
        P("expert"),
        P("expert"),
        P(None, "tensor", "expert"),
        P("expert", None),
        P("expert", None, "tensor"),
        P("expert", None, "tensor"),
        P("expert", "tensor", None),
        P("expert", None),
        P(),
    )
    compact = (mesh.shape["expert"], mesh.shape["tensor"]) == (GROUPS, NX * NC)
    return jax.shard_map(
        fast_shards if compact else shards,
        mesh=mesh,
        in_specs=placed,
        out_specs=(
            P("expert", None),
            P("expert", None),
            P(None, "expert", "tensor"),
            P("tensor", "expert"),
            P("expert"),
            P("expert"),
            P(None, "tensor", "expert"),
            P("expert", None),
            P("expert", None, "tensor"),
            P("expert", None, "tensor"),
            P("expert", "tensor", None),
        ),
        check_vma=False,
    )
```

```python
import jax
import jax.numpy as jnp
from jax import lax
from jax.experimental import pallas as pl
from jax.experimental.pallas import tpu as pltpu
from jax.sharding import PartitionSpec as P

HEAD = 128
WINDOW = 1024
SEQ = 2048


EPS = 1e-05
THETA = 10000.0


def from_behind(value, axis, steps):
    count = lax.axis_size(axis)
    initial, last = (max(0, -steps), min(count, count - steps))
    return lax.ppermute(value, axis, [(source, source + steps) for source in range(initial, last)])


def angles(position, head_size):
    half_size = head_size // 2
    frequency = THETA ** (-(jnp.arange(half_size, dtype=jnp.float32) * 2.0 / head_size))
    phase_angle = position.astype(jnp.float32)[:, None] * frequency[None, :]
    return (jnp.cos(phase_angle)[:, None, :], jnp.sin(phase_angle)[:, None, :])


def rotate(rotated_in, cosine_table, sine_table):
    half_size = rotated_in.shape[-1] // 2
    first_half = rotated_in[..., :half_size]
    second_half = rotated_in[..., half_size:]
    return jnp.concatenate(
        [
            first_half * cosine_table - second_half * sine_table,
            second_half * cosine_table + first_half * sine_table,
        ],
        axis=-1,
    )


def slot_layout(block_routes, experts, capacity):
    flat_routes = block_routes.reshape(-1)
    onehot = (flat_routes[:, None] == jnp.arange(experts, dtype=jnp.int32)[None, :]).astype(
        jnp.int32
    )
    before = jnp.cumsum(onehot, axis=0) - onehot
    rank_within = jnp.sum(before * onehot, axis=1)
    slot_index = flat_routes * capacity + rank_within
    slot_table = (
        jnp.zeros((experts * capacity,), jnp.int32)
        .at[slot_index]
        .set(jnp.arange(flat_routes.shape[0], dtype=jnp.int32) + 1)
    )
    return (slot_index, slot_table)


def shards(
    tokens_in,
    out_grad,
    w_qkv,
    w_attn_out,
    attn_gain,
    ffn_gain,
    qk_gain,
    w_router,
    w_gate,
    w_up,
    w_down,
    routes,
    segments,
):
    row_count, model_width = tokens_in.shape
    experts = w_router.shape[1]
    per_token = routes.shape[1]
    local_experts = w_gate.shape[0]
    heads_here = qk_gain.shape[1]
    local_width = heads_here * HEAD
    groups = lax.axis_size("expert")
    device = lax.axis_index("expert")
    capacity = row_count * per_token * 3 // (2 * experts)
    hop_count = WINDOW // row_count
    buffer_shape = (groups, local_experts, capacity, model_width)
    score_scale = HEAD ** (-0.5)

    def fetch_weights():
        return (
            lax.all_gather(w_qkv.astype(jnp.bfloat16), "expert", axis=1, tiled=True),
            lax.all_gather(w_attn_out.astype(jnp.bfloat16), "expert", axis=1, tiled=True),
            lax.all_gather(w_router.astype(jnp.bfloat16), "expert", axis=0, tiled=True),
            lax.all_gather(attn_gain.astype(jnp.bfloat16), "expert", axis=0, tiled=True),
            lax.all_gather(ffn_gain.astype(jnp.bfloat16), "expert", axis=0, tiled=True),
            lax.all_gather(qk_gain.astype(jnp.bfloat16), "expert", axis=2, tiled=True),
        )

    def prepare(pieces):
        return (
            pieces[0],
            pieces[1],
            pieces[2],
            pieces[3].astype(jnp.float32),
            pieces[4].astype(jnp.float32),
            pieces[5].astype(jnp.float32).reshape(2, local_width),
        )

    qkv_low, out_low, router_low, gain_one_f, gain_two_f, qk_gains = prepare(fetch_weights())
    tokens_f = tokens_in.astype(jnp.float32)
    scale_one = lax.rsqrt(jnp.mean(tokens_f * tokens_f, axis=-1, keepdims=True) + EPS)
    hidden_one = (tokens_f * scale_one * gain_one_f).astype(jnp.bfloat16)
    projected = jnp.einsum("td,jde->jte", hidden_one, qkv_low, preferred_element_type=jnp.float32)
    query_raw = projected[0]
    key_raw = projected[1]
    query_sq, key_sq = lax.psum(
        (jnp.sum(query_raw * query_raw, axis=-1), jnp.sum(key_raw * key_raw, axis=-1)), "tensor"
    )
    query_scale = lax.rsqrt(query_sq / model_width + EPS)[:, None]
    key_scale = lax.rsqrt(key_sq / model_width + EPS)[:, None]
    normed_query = query_raw * query_scale
    normed_key = key_raw * key_scale
    global_rows = device * row_count + jnp.arange(row_count, dtype=jnp.int32)
    cosine_table, sine_table = angles(global_rows % SEQ, HEAD)
    query_low = rotate(
        (normed_query * qk_gains[0]).reshape(row_count, heads_here, HEAD), cosine_table, sine_table
    ).astype(jnp.bfloat16)
    key_low = rotate(
        (normed_key * qk_gains[1]).reshape(row_count, heads_here, HEAD), cosine_table, sine_table
    ).astype(jnp.bfloat16)
    value_low = projected[2].astype(jnp.bfloat16).reshape(row_count, heads_here, HEAD)
    own_pair = jnp.stack([key_low, value_low])
    earlier = []
    for steps_back in range(hop_count, 0, -1):
        earlier.append(from_behind(own_pair, "expert", steps_back))
    context = jnp.concatenate(earlier + [own_pair], axis=1)
    key_rows = (device - hop_count) * row_count + jnp.arange(
        (hop_count + 1) * row_count, dtype=jnp.int32
    )
    segment_keys = segments[jnp.maximum(key_rows, 0)]
    segment_query = segments[global_rows]
    distance = global_rows[:, None] - key_rows[None, :]
    allowed = (
        (key_rows[None, :] >= 0)
        & (segment_query[:, None] == segment_keys[None, :])
        & (distance >= 0)
        & (distance < WINDOW)
    )

    def score_block():
        raw_scores = (
            jnp.einsum("qhd,khd->hqk", query_low, context[0], preferred_element_type=jnp.float32)
            * score_scale
        )
        return jnp.where(allowed[None], raw_scores, -1e30)

    scores = score_block()
    largest = jnp.max(scores, axis=-1, keepdims=True)
    exp_scores = jnp.exp(scores - largest)
    exp_total = jnp.sum(exp_scores, axis=-1, keepdims=True)
    log_total = largest + jnp.log(exp_total)
    attn_probs = (exp_scores / exp_total).astype(jnp.bfloat16)
    attended = (
        jnp.einsum("hqk,khd->qhd", attn_probs, context[1], preferred_element_type=jnp.float32)
        .reshape(row_count, local_width)
        .astype(jnp.bfloat16)
    )
    attention_out = lax.psum(
        jnp.dot(attended, out_low, preferred_element_type=jnp.float32).astype(jnp.bfloat16),
        "tensor",
    ).astype(jnp.float32)
    residual = tokens_f + attention_out
    scale_two = lax.rsqrt(jnp.mean(residual * residual, axis=-1, keepdims=True) + EPS)
    normed_two = residual * scale_two
    hidden_two = (normed_two * gain_two_f).astype(jnp.bfloat16)
    logits = jnp.dot(hidden_two, router_low, preferred_element_type=jnp.float32)
    logit_exp = jnp.exp(logits - jnp.max(logits, axis=-1, keepdims=True))
    router_probs = logit_exp / jnp.sum(logit_exp, axis=-1, keepdims=True)
    chosen = routes[:, :, None] == jnp.arange(experts, dtype=jnp.int32)[None, None, :]
    gate_probs = jnp.sum(jnp.where(chosen, router_probs[:, None, :], 0.0), axis=-1)
    slot_index, slot_table = slot_layout(routes, experts, capacity)
    present = (slot_table > 0)[:, None]
    assigned = jnp.maximum(slot_table - 1, 0)
    row_of_slot = assigned // per_token
    gate_low = w_gate.astype(jnp.bfloat16)
    up_low = w_up.astype(jnp.bfloat16)
    down_low = w_down.astype(jnp.bfloat16)

    def send_rows():
        buffer_rows = jnp.where(
            present, hidden_two[row_of_slot], jnp.zeros((), jnp.bfloat16)
        ).reshape(buffer_shape)
        return lax.all_to_all(buffer_rows, "expert", split_axis=0, concat_axis=0, tiled=True)

    def expert_front(arrived):
        gate_pre = jnp.einsum(
            "secd,edh->sech", arrived, gate_low, preferred_element_type=jnp.float32
        )
        up_pre = jnp.einsum("secd,edh->sech", arrived, up_low, preferred_element_type=jnp.float32)
        return (gate_pre, up_pre)

    received = send_rows()
    gate_pre, up_pre = expert_front(received)
    activated = (gate_pre * jax.nn.sigmoid(gate_pre) * up_pre).astype(jnp.bfloat16)
    partial_value = jnp.einsum(
        "sech,ehd->secd", activated, down_low, preferred_element_type=jnp.float32
    ).astype(jnp.bfloat16)
    returned = lax.all_to_all(
        partial_value, "expert", split_axis=0, concat_axis=0, tiled=True
    ).reshape(experts * capacity, model_width)
    expert_rows = returned[slot_index].reshape(row_count, per_token, model_width)
    expert_part = jnp.einsum(
        "tk,tkd->td", gate_probs, expert_rows, preferred_element_type=jnp.float32
    )
    block_out = residual + lax.psum(expert_part.astype(jnp.bfloat16), "tensor").astype(jnp.float32)
    qkv_low, out_low, router_low, gain_one_f, gain_two_f, qk_gains = prepare(fetch_weights())
    grad_out = out_grad.astype(jnp.float32)
    grad_gate_part = jnp.einsum(
        "td,tkd->tk", grad_out, expert_rows, preferred_element_type=jnp.float32
    )
    slot_grads = (
        (gate_probs[:, :, None] * grad_out[:, None, :])
        .astype(jnp.bfloat16)
        .reshape(row_count * per_token, model_width)
    )
    grad_buffer = jnp.where(present, slot_grads[assigned], jnp.zeros((), jnp.bfloat16)).reshape(
        buffer_shape
    )
    grad_received = lax.all_to_all(grad_buffer, "expert", split_axis=0, concat_axis=0, tiled=True)
    received = send_rows()
    gate_pre, up_pre = expert_front(received)
    sigmoid_gate = jax.nn.sigmoid(gate_pre)
    swish_gate = gate_pre * sigmoid_gate
    activated = (swish_gate * up_pre).astype(jnp.bfloat16)
    grad_act = jnp.einsum(
        "secd,ehd->sech", grad_received, down_low, preferred_element_type=jnp.float32
    )
    grad_down = jnp.einsum(
        "sech,secd->ehd", activated, grad_received, preferred_element_type=jnp.float32
    )
    grad_gate_pre = (
        grad_act * up_pre * sigmoid_gate * (1.0 + gate_pre * (1.0 - sigmoid_gate))
    ).astype(jnp.bfloat16)
    grad_up_pre = (grad_act * swish_gate).astype(jnp.bfloat16)
    grad_gate_w = jnp.einsum(
        "secd,sech->edh", received, grad_gate_pre, preferred_element_type=jnp.float32
    )
    grad_up_w = jnp.einsum(
        "secd,sech->edh", received, grad_up_pre, preferred_element_type=jnp.float32
    )
    grad_rows = (
        jnp.einsum("sech,edh->secd", grad_gate_pre, gate_low, preferred_element_type=jnp.float32)
        + jnp.einsum("sech,edh->secd", grad_up_pre, up_low, preferred_element_type=jnp.float32)
    ).astype(jnp.bfloat16)
    grad_back = lax.all_to_all(
        grad_rows, "expert", split_axis=0, concat_axis=0, tiled=True
    ).reshape(experts * capacity, model_width)
    grad_hidden_part = jnp.sum(
        grad_back[slot_index].reshape(row_count, per_token, model_width), axis=1, dtype=jnp.float32
    )
    grad_hidden_sum, grad_gates = (
        lax.psum(grad_hidden_part.astype(jnp.bfloat16), "tensor").astype(jnp.float32),
        lax.psum(grad_gate_part.astype(jnp.bfloat16), "tensor").astype(jnp.float32),
    )
    grad_probs = jnp.sum(jnp.where(chosen, grad_gates[:, :, None], 0.0), axis=1)
    grad_logits = (
        router_probs * (grad_probs - jnp.sum(router_probs * grad_probs, axis=-1, keepdims=True))
    ).astype(jnp.bfloat16)
    grad_hidden_two = grad_hidden_sum + jnp.dot(
        grad_logits, router_low.T, preferred_element_type=jnp.float32
    )
    grad_router = jnp.dot(hidden_two.T, grad_logits, preferred_element_type=jnp.float32)
    grad_gain_two = jnp.sum(grad_hidden_two * normed_two, axis=0)
    scaled_two = grad_hidden_two * gain_two_f
    grad_residual = (
        grad_out
        + scale_two * scaled_two
        - residual
        * (scale_two * scale_two * scale_two)
        * jnp.mean(scaled_two * residual, axis=-1, keepdims=True)
    )
    grad_attn = grad_residual.astype(jnp.bfloat16)
    grad_out_w = jnp.dot(attended.T, grad_attn, preferred_element_type=jnp.float32)
    grad_attended = (
        jnp.dot(grad_attn, out_low.T, preferred_element_type=jnp.float32)
        .astype(jnp.bfloat16)
        .reshape(row_count, heads_here, HEAD)
    )
    attn_weights = jnp.where(allowed[None], jnp.exp(score_block() - log_total), 0.0)
    grad_weights = jnp.einsum(
        "qhd,khd->hqk", grad_attended, context[1], preferred_element_type=jnp.float32
    )
    inner_sum = jnp.sum(attn_weights * grad_weights, axis=-1, keepdims=True)
    grad_scores = (attn_weights * (grad_weights - inner_sum) * score_scale).astype(jnp.bfloat16)
    grad_query = jnp.einsum(
        "hqk,khd->qhd", grad_scores, context[0], preferred_element_type=jnp.float32
    )
    grad_keys = jnp.einsum(
        "hqk,qhd->khd", grad_scores, query_low, preferred_element_type=jnp.float32
    )
    grad_values = jnp.einsum(
        "hqk,qhd->khd",
        attn_weights.astype(jnp.bfloat16),
        grad_attended,
        preferred_element_type=jnp.float32,
    )
    grad_pair = jnp.stack([grad_keys, grad_values]).reshape(
        2, hop_count + 1, row_count, heads_here, HEAD
    )
    own_grad = grad_pair[:, hop_count]
    for steps_back in range(1, hop_count + 1):
        own_grad = own_grad + from_behind(
            grad_pair[:, hop_count - steps_back].astype(jnp.bfloat16), "expert", -steps_back
        ).astype(jnp.float32)
    grad_query_norm = rotate(grad_query, cosine_table, -sine_table).reshape(row_count, local_width)
    grad_key_norm = rotate(own_grad[0], cosine_table, -sine_table).reshape(row_count, local_width)
    grad_gain_query = jnp.sum(grad_query_norm * normed_query, axis=0)
    grad_gain_key = jnp.sum(grad_key_norm * normed_key, axis=0)
    scaled_query = grad_query_norm * qk_gains[0]
    scaled_key = grad_key_norm * qk_gains[1]
    query_inner, key_inner = lax.psum(
        (jnp.sum(scaled_query * query_raw, axis=-1), jnp.sum(scaled_key * key_raw, axis=-1)),
        "tensor",
    )
    grad_query_raw = (
        query_scale * scaled_query
        - query_raw * (query_scale * query_scale * query_scale) * query_inner[:, None] / model_width
    ).astype(jnp.bfloat16)
    grad_key_raw = (
        key_scale * scaled_key
        - key_raw * (key_scale * key_scale * key_scale) * key_inner[:, None] / model_width
    ).astype(jnp.bfloat16)
    grad_value_raw = own_grad[1].reshape(row_count, local_width).astype(jnp.bfloat16)
    grad_proj = jnp.stack([grad_query_raw, grad_key_raw, grad_value_raw])
    grad_qkv = jnp.einsum("td,jte->jde", hidden_one, grad_proj, preferred_element_type=jnp.float32)
    grad_hidden_one = lax.psum(
        jnp.einsum("jte,jde->td", grad_proj, qkv_low, preferred_element_type=jnp.float32).astype(
            jnp.bfloat16
        ),
        "tensor",
    ).astype(jnp.float32)
    grad_gain_one = jnp.sum(grad_hidden_one * tokens_f * scale_one, axis=0)
    scaled_one = grad_hidden_one * gain_one_f
    grad_tokens = (
        grad_residual
        + scale_one * scaled_one
        - tokens_f
        * (scale_one * scale_one * scale_one)
        * jnp.mean(scaled_one * tokens_f, axis=-1, keepdims=True)
    )
    grad_qk = jnp.stack([grad_gain_query, grad_gain_key]).reshape(2, heads_here, HEAD)
    reduced = (
        lax.psum_scatter(
            grad_qkv.astype(jnp.bfloat16), "expert", scatter_dimension=1, tiled=True
        ).astype(jnp.float32),
        lax.psum_scatter(
            grad_out_w.astype(jnp.bfloat16), "expert", scatter_dimension=1, tiled=True
        ).astype(jnp.float32),
        lax.psum_scatter(
            grad_router.astype(jnp.bfloat16), "expert", scatter_dimension=0, tiled=True
        ).astype(jnp.float32),
        lax.psum_scatter(
            grad_gain_one.astype(jnp.bfloat16), "expert", scatter_dimension=0, tiled=True
        ).astype(jnp.float32),
        lax.psum_scatter(
            grad_gain_two.astype(jnp.bfloat16), "expert", scatter_dimension=0, tiled=True
        ).astype(jnp.float32),
        lax.psum_scatter(
            grad_qk.astype(jnp.bfloat16), "expert", scatter_dimension=2, tiled=True
        ).astype(jnp.float32),
    )
    return (
        block_out.astype(jnp.bfloat16),
        grad_tokens.astype(jnp.bfloat16),
        reduced[0],
        reduced[1],
        reduced[3],
        reduced[4],
        reduced[5],
        reduced[2],
        grad_gate_w,
        grad_up_w,
        grad_down,
    )


MESH_ID = pl.DeviceIdType.MESH
HBM = pl.BlockSpec(memory_space=pltpu.HBM)
VMEM = pl.BlockSpec(memory_space=pltpu.VMEM)
NZ, NY, NX, NC = 4, 2, 2, 2
GROUPS = NZ * NY


def place():
    e = lax.axis_index("expert")
    t = lax.axis_index("tensor")
    return lax.div(e, NY), lax.rem(e, NY), lax.div(t, NC), lax.rem(t, NC)


def device(z, y, x, c):
    return (jnp.clip(z, 0, NZ - 1) * NY + y, x * NC + c)


def run_if(condition, body):
    if condition is None:
        body()
    else:
        pl.when(condition)(body)


def greet(partners):
    barrier = pltpu.get_barrier_semaphore()
    for target, condition in partners:
        run_if(
            condition,
            lambda target=target: pl.semaphore_signal(
                barrier, inc=1, device_id=target, device_id_type=MESH_ID
            ),
        )
    count = sum(1 for _, condition in partners if condition is None)
    for _, condition in partners:
        if condition is not None:
            count = count + condition.astype(jnp.int32)
    pl.semaphore_wait(barrier, count)


def remote(source, target_ref, send_sem, recv_sem, target):
    return pltpu.make_async_remote_copy(
        src_ref=source,
        dst_ref=target_ref,
        send_sem=send_sem,
        recv_sem=recv_sem,
        device_id=target,
        device_id_type=MESH_ID,
    )


def block_rows(block, rows):
    return pl.ds(pl.multiple_of(block * rows, rows), rows)


class LineGather:
    def __init__(self, streams, sources, views, send_sem, recv_sem, y_first=()):
        self.z, self.y, self.x, self.c = place()
        self.streams, self.sources, self.views = streams, sources, views
        self.send_sem, self.recv_sem = send_sem, recv_sem
        self.y_first = y_first
        self.has_up, self.has_down = self.z < NZ - 1, self.z > 0
        self.pending = []

    def partners(self):
        z, y, x, c = self.z, self.y, self.x, self.c
        return [
            (device(z + 1, y, x, c), z < NZ - 1),
            (device(z - 1, y, x, c), z > 0),
            (device(z, 1 - y, x, c), None),
        ]

    def exists(self, rel):
        rel = rel % 7
        if rel == 0:
            return None
        return self.z >= rel if rel < 4 else self.z + (rel - 3) < NZ

    def block(self, rel):
        y = self.y if rel < 7 else 1 - self.y
        rel = rel % 7
        z = self.z if rel == 0 else (self.z - rel if rel < 4 else self.z + (rel - 3))
        return z * NY + y

    def send(self, stream, rel, way):
        z, y, x, c = self.z, self.y, self.x, self.c
        block = self.block(rel)
        there = self.views[stream](block)
        source = self.sources[stream] if rel == 0 else there
        near = rel % 7 == 0
        if way == 0:
            target, landing = device(z + 1, y, x, c), rel + 1
        elif way == 1:
            target, landing = device(z - 1, y, x, c), rel + (4 if near else 1)
        else:
            target, landing = device(z, 1 - y, x, c), 7 + rel
        return remote(
            source,
            there,
            self.send_sem.at[stream, rel, way],
            self.recv_sem.at[stream, landing],
            target,
        )

    def forwards(self, stream, rel):
        return rel < 7 or stream in self.y_first

    def start(self, stream, rel):
        if rel % 7 < 4:
            run = self.has_up
            run_if(run, lambda: self.send(stream, rel, 0).start())
            self.pending.append((stream, rel, 0, run))
        if rel % 7 == 0 or rel % 7 >= 4:
            run = self.has_down
            run_if(run, lambda: self.send(stream, rel, 1).start())
            self.pending.append((stream, rel, 1, run))
        if rel == 0 or stream not in self.y_first:
            self.send(stream, rel, 2).start()
            self.pending.append((stream, rel, 2, None))

    def arrive(self, stream, rel):
        there = self.views[stream](self.block(rel))
        remote(
            there,
            there,
            self.send_sem.at[stream, 0, 0],
            self.recv_sem.at[stream, rel],
            device(self.z, 1 - self.y, self.x, self.c),
        ).wait_recv()

    def order(self):
        return [7, 1, 4, 8, 11, 2, 5, 9, 12, 3, 6, 10, 13]

    def run(self, hook=None):
        for stream in self.streams:
            self.start(stream, 0)
        for rel in self.order():
            def step(rel=rel):
                marks = len(self.pending)
                for stream in self.streams:
                    self.arrive(stream, rel)
                    if rel < 7:
                        self.start(stream, rel)
                    if hook is not None:
                        hook(stream, rel)
                if rel < 7:
                    late = self.pending[marks:]
                    del self.pending[marks:]
                    self.finish_later(late, rel)
            run_if(self.exists(rel), step)

    def finish_later(self, late, rel):
        self.late = getattr(self, "late", []) + [(rel, late)]

    def finish(self):
        for stream, rel, way, run in self.pending:
            run_if(run, lambda s=stream, r=rel, w=way: self.send(s, r, w).wait_send())
        for rel, late in getattr(self, "late", []):
            def body(late=late):
                for stream, rel, way, run in late:
                    run_if(run, lambda s=stream, r=rel, w=way: self.send(s, r, w).wait_send())
            run_if(self.exists(rel), body)


def cost(microseconds):
    return pl.CostEstimate(flops=0, bytes_accessed=int(microseconds * 3.0e6), transcendentals=0)


def comm_params(collective_id, megabytes=56):
    return pltpu.CompilerParams(
        collective_id=collective_id,
        has_side_effects=True,
        vmem_limit_bytes=megabytes * 1024 * 1024,
    )


def group_stages(part_ref, out_ref, core_buf, x_buf, send_sem, recv_sem):
    rows, width = part_ref.shape
    half, quarter = width // 2, width // 4
    z, y, x, c = place()
    across, twin = device(z, y, 1 - x, c), device(z, y, x, 1 - c)

    def half_of(cc):
        return pl.ds(pl.multiple_of(cc * half, half), half)

    def quarter_of(xx, cc):
        return pl.ds(pl.multiple_of(cc * half + xx * quarter, quarter), quarter)

    own, from_x = out_ref.at[:, quarter_of(x, c)], out_ref.at[:, quarter_of(1 - x, c)]
    to_x = core_buf.at[:, pl.ds(pl.multiple_of((1 - x) * quarter, quarter), quarter)]
    sources = [part_ref.at[:, half_of(1 - c)], to_x, own, own, from_x]
    landings = [core_buf, x_buf, own, own, from_x]
    targets = [twin, across, across, twin, twin]

    def copy(k):
        return remote(sources[k], landings[k], send_sem.at[k], recv_sem.at[k], targets[k])

    def arrive(k, landing):
        remote(landing, landing, send_sem.at[k], recv_sem.at[k], targets[k]).wait_recv()

    def begin():
        copy(0).start()

    def core_step():
        copy(0).wait_recv()
        add_to(core_buf, core_buf, part_ref.at[:, half_of(c)], 32)
        copy(1).start()

    def x_step():
        copy(1).wait_recv()
        add_to(own, x_buf, core_buf.at[:, pl.ds(pl.multiple_of(x * quarter, quarter), quarter)], 32)
        copy(2).start()
        copy(3).start()

    def spread():
        arrive(2, from_x)
        copy(4).start()

    def end():
        arrive(3, out_ref.at[:, quarter_of(x, 1 - c)])
        arrive(4, out_ref.at[:, quarter_of(1 - x, 1 - c)])
        for k in range(5):
            copy(k).wait_send()

    return [begin, core_step, x_step, spread, end]


def group_sum(part_ref, out_ref, core_buf, x_buf, send_sem, recv_sem, meanwhile=None):
    stages = group_stages(part_ref, out_ref, core_buf, x_buf, send_sem, recv_sem)
    stages[0]()
    if meanwhile is not None:
        meanwhile()
    for stage in stages[1:]:
        stage()


Z_ORDER = (3, 0, 2, 1)


def accumulate(into, addend, step=64):
    rows = into.shape[0]
    step = min(step, rows)

    def body(i, carry):
        r = pl.ds(pl.multiple_of(i * step, step), step)
        total = into[r, :].astype(jnp.float32) + addend[r, :].astype(jnp.float32)
        into[r, :] = total.astype(into.dtype)
        return carry

    lax.fori_loop(0, rows // step, body, 0)


class LineReduce:
    def __init__(self, streams, own, y_buf, lo_buf, hi_buf, send_sem, recv_sem):
        self.z, self.y, self.x, self.c = place()
        self.streams = streams
        self.own, self.y_buf, self.lo_buf, self.hi_buf = own, y_buf, lo_buf, hi_buf
        self.send_sem, self.recv_sem = send_sem, recv_sem

    def partners(self):
        z, y, x, c = self.z, self.y, self.x, self.c
        return [
            (device(z + 1, y, x, c), z < NZ - 1),
            (device(z - 1, y, x, c), z > 0),
            (device(z, 1 - y, x, c), None),
        ]

    def copy(self, s, zz, way):
        z, y, x, c = self.z, self.y, self.x, self.c
        if way == 0:
            source, landing, target = self.own(s, zz, 1 - y), self.y_buf, device(z, 1 - y, x, c)
        elif way == 1:
            source, landing, target = self.y_buf(s, zz), self.lo_buf, device(z + 1, y, x, c)
        else:
            source, landing, target = self.y_buf(s, zz), self.hi_buf, device(z - 1, y, x, c)
        return remote(
            source, landing(s, zz), self.send_sem.at[s, zz, way], self.recv_sem.at[s, zz, way], target
        )

    def to_y(self, s, zz):
        self.copy(s, zz, 0).start()

    def take(self, s, zz, way):
        self.copy(s, zz, way).wait_recv()
        accumulate(self.y_buf(s, zz), (self.lo_buf if way == 1 else self.hi_buf)(s, zz))

    def along_z(self, s, zz):
        z = self.z
        self.copy(s, zz, 0).wait_recv()
        accumulate(self.y_buf(s, zz), self.own(s, zz, self.y))

        def upward():
            run_if(z > 0, lambda: self.take(s, zz, 1))
            self.copy(s, zz, 1).start()

        def downward():
            run_if(z < NZ - 1, lambda: self.take(s, zz, 2))
            self.copy(s, zz, 2).start()

        run_if(z < zz, upward)
        run_if(z > zz, downward)

    def home(self, done):
        for zz in range(NZ):
            def land(zz=zz):
                for s in self.streams:
                    if zz > 0:
                        self.take(s, zz, 1)
                    if zz < NZ - 1:
                        self.take(s, zz, 2)
                    done(s, self.y_buf(s, zz))
            run_if(self.z == zz, land)

    def finish(self):
        for zz in range(NZ):
            for s in self.streams:
                self.copy(s, zz, 0).wait_send()
                run_if(self.z < zz, lambda s=s, zz=zz: self.copy(s, zz, 1).wait_send())
                run_if(self.z > zz, lambda s=s, zz=zz: self.copy(s, zz, 2).wait_send())


def dot(a, b, dims):
    return lax.dot_general(a, b, ((dims[:1], dims[1:]), ((), ())), preferred_element_type=jnp.float32)


def add_to(target, first, second, step=64):
    rows = target.shape[0]

    def body(i, carry):
        r = pl.ds(pl.multiple_of(i * step, step), step)
        total = first[r, :].astype(jnp.float32) + second[r, :].astype(jnp.float32)
        target[r, :] = total.astype(target.dtype)
        return carry

    lax.fori_loop(0, rows // step, body, 0)


def expert_layer(
    hidden_two, grad_out_all, gate_up, down, router_t, chosen_all, residual, attended, collective_id
):
    rows, width = hidden_two.shape
    tokens = rows * GROUPS
    units = down.shape[0]
    local = 2
    hidden = units // local
    experts = router_t.shape[0]
    half, part, piece = width // 2, width // 4, width // 8
    tensors = NX * NC
    steps = GROUPS + 4
    a_cols, c_cols = width // 8, width // 4
    low = jnp.bfloat16
    wide = width // 4

    def kernel(
        own_in, dy_in, gu_in, down_in, router_ref, chosen_ref, x1_in, o_in,
        block_out, dh_out, gates_out, gate_w, up_w, down_w, o_all,
        gu_ref, down_ref, weight_sem, h, dy, gated, dgu, dx, y_part, yc_buf, ypx_buf, ypy_buf, yqy_buf, yqx_buf, yz_sum,
        ylo_buf, yhi_buf, x1, gu_stage, d_stage,
        core_buf, px_buf, py_buf, qy_buf, qx_buf, z_sum, lo_buf, hi_buf, gate_part, gate_land,
        in_sem, own_sem, o_sem, line_s, line_r, hx_s, hx_r, hc_s, hc_r, x1_sem, yc_s, yc_r, ypx_s, ypx_r, ypy_s, ypy_r,
        yqy_s, yqy_r, yqx_s, yqx_r, yz_s, yz_r, gu_sem, d_sem, core_s, core_r, px_s, px_r, py_s, py_r, qy_s, qy_r, qx_s, qx_r,
        z_s, z_r, near_s, near_r, far_s, far_r, end_s, end_r,
    ):
        z, y, x, c = place()
        e, t = lax.axis_index("expert"), lax.axis_index("tensor")
        across, twin, beside = device(z, y, 1 - x, c), device(z, y, x, 1 - c), device(z, 1 - y, x, c)
        mates = [(e, lax.rem(t + k, tensors)) for k in range(1, tensors)]
        peers = [(lax.rem(e + k, GROUPS), t) for k in range(1, GROUPS)]
        weight_loads = [
            pltpu.make_async_copy(gu_in, gu_ref, weight_sem.at[0]),
            pltpu.make_async_copy(down_in, down_ref, weight_sem.at[1]),
        ]
        for copy in weight_loads:
            copy.start()
        greet([(target, None) for target in mates + peers])

        def pick(values, index):
            result = values[-1]
            for k in range(len(values) - 1):
                result = jnp.where(index == k, values[k], result)
            return result

        def zz_of(j):
            return pick([z, pick([1, 0, 3, 2], z), pick([3, 3, 0, 0], z), pick([2, 2, 1, 1], z)], j)

        def is_own(i):
            return (i == 0) | ((i >= 2) & (lax.rem(i, 2) == 1))

        def block_of(i):
            return zz_of(lax.div(i, 2)) * NY + jnp.where(is_own(i), y, 1 - y)

        def flip_block(j):
            return zz_of(j) * NY + 1 - y

        def own_block(j):
            return zz_of(j) * NY + y

        def a_at(xx, cc):
            return pl.ds(pl.multiple_of(xx * (2 * a_cols) + cc * a_cols, 128), a_cols)

        def c_at(cc):
            return pl.ds(pl.multiple_of(4 * a_cols + cc * c_cols, 128), c_cols)

        def h_view(b, columns):
            return h.at[block_rows(b, rows), columns]

        line = LineGather(
            [0, 1, 2], [own_in.at[:, a_at(x, c)], own_in.at[:, c_at(c)], o_in],
            [
                lambda b: h_view(b, a_at(x, c)),
                lambda b: h_view(b, c_at(c)),
                lambda b: o_all.at[block_rows(b, rows), :],
            ],
            line_s, line_r,
        )

        def h_twin(b, stream, landing=False):
            cc = 1 - c if landing else c
            piece = h_view(b, [a_at(x, cc), c_at(cc), a_at(1 - x, cc)][stream])
            return remote(piece, piece, hc_s.at[b, stream], hc_r.at[b, stream], twin)

        def h_across(b, landing=False):
            piece = h_view(b, a_at(1 - x if landing else x, c))
            return remote(piece, piece, hx_s.at[b], hx_r.at[b], across)

        def gather_event(rel):
            def body():
                b = line.block(rel)
                marks = len(line.pending)
                for stream in (0, 1):
                    line.arrive(stream, rel)
                    if rel < 7:
                        line.start(stream, rel)
                    if stream == 0:
                        h_across(b).start()
                    h_twin(b, stream).start()
                late = line.pending[marks:]
                del line.pending[marks:]
                line.finish_later(late, rel)
            run_if(line.exists(rel), body)

        def attended_event(rel):
            def body():
                marks = len(line.pending)
                line.arrive(2, rel)
                if rel < 7:
                    line.start(2, rel)
                late = line.pending[marks:]
                del line.pending[marks:]
                line.finish_later(late, rel)
            run_if(line.exists(rel), body)

        def relay(i):
            b = block_of(i)
            h_across(b, True).wait_recv()
            h_twin(b, 2).start()

        for stream in (0, 1):
            line.start(stream, 0)
        keep = pltpu.make_async_copy(own_in, h.at[block_rows(z * NY + y, rows), :], own_sem)
        keep.start()
        keep_o = pltpu.make_async_copy(o_in, o_all.at[block_rows(z * NY + y, rows), :], o_sem)
        keep_o.start()

        def load(i):
            r = block_rows(block_of(i), rows)
            return pltpu.make_async_copy(dy_in.at[r, :], dy.at[r, :], in_sem.at[i])

        def start_load(i, carry):
            load(i).start()
            return carry

        lax.fori_loop(0, GROUPS, start_load, 0)
        x1_copies = [
            pltpu.make_async_copy(
                x1_in.at[:, pl.ds(pl.multiple_of(c * half + s * part + x * piece, piece), piece)],
                x1.at[:, pl.ds(s * piece, piece)], x1_sem.at[s],
            )
            for s in range(2)
        ]
        for copy in x1_copies:
            copy.start()

        def to_twin(i):
            b = block_of(i)
            return remote(
                dx.at[lax.rem(i, 2), :, pl.ds(pl.multiple_of((1 - c) * half, half), half)],
                core_buf.at[b], core_s.at[i], core_r.at[i], twin,
            )

        def p_across(i):
            b = block_of(i)
            return remote(
                core_buf.at[b, :, pl.ds(pl.multiple_of((1 - x) * piece, piece), piece)],
                px_buf.at[b], px_s.at[i], px_r.at[i], across,
            )

        def p_beside(j):
            return remote(px_buf.at[flip_block(j)], py_buf.at[j], py_s.at[j], py_r.at[j], beside)

        def q_beside(j):
            return remote(
                core_buf.at[flip_block(j), :, pl.ds(part, part)], qy_buf.at[j], qy_s.at[j], qy_r.at[j], beside
            )

        def q_across(j):
            return remote(
                qy_buf.at[j, :, pl.ds(pl.multiple_of((1 - x) * piece, piece), piece)],
                qx_buf.at[j], qx_s.at[j], qx_r.at[j], across,
            )

        def up(j, s):
            return remote(z_sum.at[s, j], lo_buf.at[s, j], z_s.at[0, s, j], z_r.at[0, s, j], device(z + 1, y, x, c))

        def down_z(j, s):
            return remote(z_sum.at[s, j], hi_buf.at[s, j], z_s.at[1, s, j], z_r.at[1, s, j], device(z - 1, y, x, c))

        def take_twin(i):
            to_twin(i).wait_recv()
            b = block_of(i)
            mine = core_buf.at[b]
            add_to(mine, mine, dx.at[lax.rem(i, 2), :, pl.ds(pl.multiple_of(c * half, half), half)], 32)
            p_across(i).start()
            pl.when(jnp.logical_not(is_own(i)))(lambda: q_beside(lax.div(i, 2)).start())

        def take_p_across(i):
            p_across(i).wait_recv()
            b = block_of(i)
            add_to(
                px_buf.at[b], px_buf.at[b],
                core_buf.at[b, :, pl.ds(pl.multiple_of(x * piece, piece), piece)],
            )

        def take_q_beside(j):
            q_beside(j).wait_recv()
            add_to(qy_buf.at[j], qy_buf.at[j], core_buf.at[own_block(j), :, pl.ds(part, part)])
            q_across(j).start()

        def take_q_across(j):
            q_across(j).wait_recv()
            add_to(
                z_sum.at[1, zz_of(j)], qx_buf.at[j], qy_buf.at[j, :, pl.ds(pl.multiple_of(x * piece, piece), piece)]
            )

        def take_p_beside(j):
            p_beside(j).wait_recv()
            add_to(z_sum.at[0, zz_of(j)], py_buf.at[j], px_buf.at[own_block(j)])

        def hop(j, k):
            zz = zz_of(j)

            def upward():
                for s in range(2):
                    if k > 0:
                        up(zz, s).wait_recv()
                        add_to(z_sum.at[s, zz], z_sum.at[s, zz], lo_buf.at[s, zz])
                    up(zz, s).start()

            def downward():
                for s in range(2):
                    if k > 0:
                        down_z(zz, s).wait_recv()
                        add_to(z_sum.at[s, zz], z_sum.at[s, zz], hi_buf.at[s, zz])
                    down_z(zz, s).start()

            pl.when((z < zz) & (z == k))(upward)
            pl.when((z > zz) & (NZ - 1 - z == k))(downward)

        def y_twin(i):
            return remote(
                y_part.at[lax.rem(i, 2), :, pl.ds(pl.multiple_of((1 - c) * half, half), half)],
                yc_buf.at[block_of(i)], yc_s.at[i], yc_r.at[i], twin,
            )

        def yp_across(i):
            b = block_of(i)
            return remote(
                yc_buf.at[b, :, pl.ds(pl.multiple_of((1 - x) * piece, piece), piece)],
                ypx_buf.at[b], ypx_s.at[i], ypx_r.at[i], across,
            )

        def yp_beside(j):
            return remote(ypx_buf.at[flip_block(j)], ypy_buf.at[j], ypy_s.at[j], ypy_r.at[j], beside)

        def yq_beside(j):
            return remote(
                yc_buf.at[flip_block(j), :, pl.ds(part, part)], yqy_buf.at[j], yqy_s.at[j], yqy_r.at[j], beside
            )

        def yq_across(j):
            return remote(
                yqy_buf.at[j, :, pl.ds(pl.multiple_of((1 - x) * piece, piece), piece)],
                yqx_buf.at[j], yqx_s.at[j], yqx_r.at[j], across,
            )

        def y_up(zz, s):
            return remote(
                yz_sum.at[s, zz], ylo_buf.at[s, zz], yz_s.at[0, s, zz], yz_r.at[0, s, zz], device(z + 1, y, x, c)
            )

        def y_down(zz, s):
            return remote(
                yz_sum.at[s, zz], yhi_buf.at[s, zz], yz_s.at[1, s, zz], yz_r.at[1, s, zz], device(z - 1, y, x, c)
            )

        def take_y_twin(i):
            y_twin(i).wait_recv()
            mine = yc_buf.at[block_of(i)]
            add_to(mine, mine, y_part.at[lax.rem(i, 2), :, pl.ds(pl.multiple_of(c * half, half), half)], 32)
            yp_across(i).start()
            pl.when(jnp.logical_not(is_own(i)))(lambda: yq_beside(lax.div(i, 2)).start())

        def take_yp_across(i):
            yp_across(i).wait_recv()
            b = block_of(i)
            add_to(
                ypx_buf.at[b], ypx_buf.at[b],
                yc_buf.at[b, :, pl.ds(pl.multiple_of(x * piece, piece), piece)],
            )
            pl.when(jnp.logical_not(is_own(i)))(lambda: yp_beside(lax.div(i, 2)).start())

        def take_yq_beside(j):
            yq_beside(j).wait_recv()
            add_to(yqy_buf.at[j], yqy_buf.at[j], yc_buf.at[own_block(j), :, pl.ds(part, part)])
            yq_across(j).start()

        def take_y_sums(j):
            zz = zz_of(j)
            yq_across(j).wait_recv()
            add_to(
                yz_sum.at[1, zz], yqx_buf.at[j], yqy_buf.at[j, :, pl.ds(pl.multiple_of(x * piece, piece), piece)]
            )
            yp_beside(j).wait_recv()
            add_to(yz_sum.at[0, zz], ypy_buf.at[j], ypx_buf.at[own_block(j)])

        def y_take(zz, s, copy, landed):
            copy(zz, s).wait_recv()
            add_to(yz_sum.at[s, zz], yz_sum.at[s, zz], landed.at[s, zz])

        def y_hop(j, k):
            zz = zz_of(j)

            def upward():
                for s in range(2):
                    if k > 0:
                        y_take(zz, s, y_up, ylo_buf)
                    y_up(zz, s).start()

            def downward():
                for s in range(2):
                    if k > 0:
                        y_take(zz, s, y_down, yhi_buf)
                    y_down(zz, s).start()

            pl.when((z < zz) & (z == k))(upward)
            pl.when((z > zz) & (NZ - 1 - z == k))(downward)

        def front(i):
            load(i).wait()
            b = block_of(i)
            pl.when(i == 0)(keep.wait)
            pl.when(i == 0)(lambda: each(weight_loads, "wait"))

            def landed():
                for stream in range(3):
                    h_twin(b, stream, True).wait_recv()

            pl.when(i > 0)(landed)
            r = block_rows(b, rows)
            rows_h, rows_dy = h[r, :], dy[r, :]
            logits = dot(rows_h, router_ref[...], (1, 1))
            shifted = jnp.exp(logits - jnp.max(logits, axis=-1, keepdims=True))
            probs = shifted / jnp.sum(shifted, axis=-1, keepdims=True) * chosen_ref[r, :].astype(jnp.float32)
            lane = lax.broadcasted_iota(jnp.int32, probs.shape, 1)
            line = lax.broadcasted_iota(jnp.int32, (rows, 128), 1)
            found = jnp.zeros((rows, 128), jnp.float32)
            for expert in range(local):
                at, up_at = pl.ds(expert * hidden, hidden), pl.ds((local + expert) * hidden, hidden)
                gate = jnp.sum(jnp.where(lane == e * local + expert, probs, 0.0), axis=-1, keepdims=True)
                pre = dot(rows_h, gu_ref[:, at], (1, 0))
                scale = dot(rows_h, gu_ref[:, up_at], (1, 0))
                back = dot(rows_dy, down_ref[at, :], (1, 1))
                sigmoid = jax.nn.sigmoid(pre)
                swish = pre * sigmoid
                active = swish * scale
                gated[r, at] = (active * gate).astype(low)
                found = jnp.where(line == expert, jnp.sum(active * back, axis=-1, keepdims=True), found)
                back = back * gate
                dgu[r, at] = (back * scale * sigmoid * (1.0 + pre * (1.0 - sigmoid))).astype(low)
                dgu[r, up_at] = (back * swish).astype(low)
            gate_part[b] = jnp.transpose(found)[:8, :]

        def rear(i):
            r = block_rows(block_of(i), rows)
            slot = lax.rem(i, 2)
            pl.when(i >= 2)(lambda: to_twin(i - 2).wait_send())

            def columns(k, carry):
                at = pl.ds(pl.multiple_of(k * wide, wide), wide)
                dx[slot, :, at] = dot(dgu[r, :], gu_ref[at, :], (1, 1)).astype(low)
                return carry

            lax.fori_loop(0, width // wide, columns, 0)
            to_twin(i).start()
            pl.when(i >= 2)(lambda: y_twin(i - 2).wait_send())

            def y_columns(k, carry):
                at = pl.ds(pl.multiple_of(k * wide, wide), wide)
                y_part[slot, :, at] = dot(gated[r, :], down_ref[:, at], (1, 0)).astype(low)
                return carry

            lax.fori_loop(0, width // wide, y_columns, 0)
            y_twin(i).start()

        tile_width = piece // 2
        tiles = width // tile_width // 4
        d_width = width // 8

        def gu_copies(n):
            slot = lax.rem(n, 2)
            at = pl.ds(pl.multiple_of(n * tile_width, tile_width), tile_width)
            return [
                pltpu.make_async_copy(
                    gu_stage.at[slot, :, pl.ds(k * hidden, hidden)],
                    (gate_w if k < local else up_w).at[k % local, at, :],
                    gu_sem.at[slot, k],
                )
                for k in range(2 * local)
            ]

        def d_copies(n):
            slot = lax.rem(n, 2)
            at = pl.ds(pl.multiple_of(n * d_width, d_width), d_width)
            return [
                pltpu.make_async_copy(
                    d_stage.at[slot, pl.ds(k * hidden, hidden), :], down_w.at[k, :, at], d_sem.at[slot, k]
                )
                for k in range(local)
            ]

        def each(copies, what):
            for copy in copies:
                getattr(copy, what)()

        def weight_grads(q):
            def tile(k, carry):
                n = q * tiles + k
                pl.when(n >= 2)(lambda: each(gu_copies(n - 2), "wait"))
                at = pl.ds(pl.multiple_of(n * tile_width, tile_width), tile_width)
                gu_stage[lax.rem(n, 2)] = dot(h[:, at], dgu[...], (0, 0))
                each(gu_copies(n), "start")
                return carry

            lax.fori_loop(0, tiles, tile, 0)

            def d_tile(k, carry):
                n = q * 2 + k
                pl.when(n >= 2)(lambda: each(d_copies(n - 2), "wait"))
                at = pl.ds(pl.multiple_of(n * d_width, d_width), d_width)
                d_stage[lax.rem(n, 2)] = dot(gated[...], dy[:, at], (0, 0))
                each(d_copies(n), "start")
                return carry

            lax.fori_loop(0, 2, d_tile, 0)

        near = [
            remote(gate_part, gate_land.at[k], near_s.at[k], near_r.at[k], mates[k])
            for k in range(tensors - 1)
        ]

        def far(k):
            return remote(
                gate_land.at[tensors - 1, lax.rem(e + k, GROUPS)], gates_out.at[e],
                far_s.at[k - 1], far_r.at[k - 1], peers[k - 1],
            )

        def sum_near():
            for copy in near:
                copy.wait_recv()
            total = gate_part[...]
            for k in range(tensors - 1):
                total = total + gate_land[k]
            gate_land[tensors - 1] = total
            for k in range(1, GROUPS):
                far(k).start()
            gates_out[e] = gate_land[tensors - 1, e]

        def step(i, carry):
            def at(number, body):
                pl.when(i == number)(body)

            odd, even = lax.rem(i, 2) == 1, lax.rem(i, 2) == 0
            j_even, j_odd = lax.div(i, 2) - 1, lax.div(i - 1, 2) - 1
            pl.when(i < GROUPS)(lambda: front(i))

            def events(*rels):
                for rel in rels:
                    gather_event(rel)

            at(1, lambda: events(2, 5, 8, 11))
            at(2, lambda: events(3, 6))
            at(3, lambda: events(10, 13))

            def attended_events(*rels):
                for rel in rels:
                    attended_event(rel)

            at(8, lambda: attended_events(1, 4))
            at(9, lambda: attended_events(2, 5))
            at(10, lambda: attended_events(3, 6))
            at(11, lambda: attended_events(7, 8, 11))

            pl.when((i >= 1) & (i <= GROUPS))(lambda: take_twin(i - 1))
            pl.when(even & (i >= 4) & (i <= GROUPS))(lambda: take_q_beside(j_even))
            at(3, lambda: take_q_beside(0))
            at(4, lambda: take_q_across(0))

            def late():
                take_p_across(i - 2)
                pl.when(i > 3)(lambda: take_q_across(j_odd))
                pl.when(i == 3)(lambda: p_beside(0).start())

            pl.when(odd & (i >= 3) & (i <= GROUPS + 1))(late)
            at(GROUPS, lambda: each(near, "start"))
            at(GROUPS + 1, sum_near)
            pl.when(i < GROUPS)(lambda: rear(i))
            pl.when(i >= GROUPS)(lambda: weight_grads(i - GROUPS))
            at(0, lambda: events(7, 1, 4))
            at(2, lambda: events(9, 12))
            at(6, lambda: line.start(2, 0))
            pl.when(i < GROUPS - 1)(lambda: relay(i + 1))

            def pass_p():
                take_p_across(i - 2)
                pl.when(i > 2)(lambda: p_beside(j_even).start())

            pl.when(even & (i >= 2) & (i <= GROUPS))(pass_p)
            at(4, lambda: take_p_beside(0))

            def join():
                take_p_beside(j_odd)
                hop(j_odd, 0)

            pl.when(odd & (i >= 5) & (i <= GROUPS + 1))(join)
            pl.when((i == GROUPS) | (i == GROUPS + 2))(lambda: hop(j_even - 1, 1))
            at(GROUPS + 1, lambda: hop(1, 2))
            pl.when((i >= 2) & (i <= GROUPS + 1))(lambda: take_yp_across(i - 2))
            pl.when((i >= 1) & (i <= GROUPS))(lambda: take_y_twin(i - 1))
            pl.when(even & (i >= 4) & (i <= GROUPS))(lambda: take_yq_beside(j_even))
            at(3, lambda: take_yq_beside(0))
            at(5, lambda: take_y_sums(0))

            def join_y():
                take_y_sums(j_even - 1)
                y_hop(j_even - 1, 0)

            pl.when(even & (i >= 6) & (i <= GROUPS + 2))(join_y)
            pl.when((i == GROUPS + 1) | (i == GROUPS + 3))(lambda: y_hop(j_odd - 1, 1))
            at(GROUPS + 2, lambda: y_hop(1, 2))
            return carry

        lax.fori_loop(0, steps, step, 0)

        for rel in (9, 12, 10, 13):
            attended_event(rel)

        def columns_of(s, xx, cc):
            return pl.ds(pl.multiple_of(cc * half + s * part + xx * piece, piece), piece)

        mine = z
        for s in range(2):
            def below(s=s):
                up(mine, s).wait_recv()
                add_to(z_sum.at[s, mine], z_sum.at[s, mine], lo_buf.at[s, mine])

            def above(s=s):
                down_z(mine, s).wait_recv()
                add_to(z_sum.at[s, mine], z_sum.at[s, mine], hi_buf.at[s, mine])

            pl.when(z > 0)(below)
            pl.when(z < NZ - 1)(above)
            own = dh_out.at[:, columns_of(s, x, c)]

            def keep(k, carry, s=s, own=own):
                r = pl.ds(pl.multiple_of(k * 64, 64), 64)
                own[r, :] = z_sum[s, mine, r, :]
                return carry

            lax.fori_loop(0, rows // 64, keep, 0)
            remote(own, own, end_s.at[0, s], end_r.at[0, s], across).start()
            remote(own, own, end_s.at[1, s], end_r.at[1, s], twin).start()
        for copy in x1_copies:
            copy.wait()
        for s in range(2):
            pl.when(z > 0)(lambda s=s: y_take(z, s, y_up, ylo_buf))
            pl.when(z < NZ - 1)(lambda s=s: y_take(z, s, y_down, yhi_buf))
            y_own = block_out.at[:, columns_of(s, x, c)]

            def finish(k, carry, s=s, y_own=y_own):
                r = pl.ds(pl.multiple_of(k * 64, 64), 64)
                y_own[r, :] = (
                    x1[r, pl.ds(s * piece, piece)] + yz_sum[s, z, r, :].astype(jnp.float32)
                ).astype(low)
                return carry

            lax.fori_loop(0, rows // 64, finish, 0)
            remote(y_own, y_own, end_s.at[0, 2 + s], end_r.at[0, 2 + s], across).start()
            remote(y_own, y_own, end_s.at[1, 2 + s], end_r.at[1, 2 + s], twin).start()
        for s in range(2):
            there = dh_out.at[:, columns_of(s, 1 - x, c)]
            remote(there, there, end_s.at[0, s], end_r.at[0, s], across).wait_recv()
            remote(there, there, end_s.at[2, s], end_r.at[2, s], twin).start()
        for s in range(2):
            there = block_out.at[:, columns_of(s, 1 - x, c)]
            remote(there, there, end_s.at[0, 2 + s], end_r.at[0, 2 + s], across).wait_recv()
            remote(there, there, end_s.at[2, 2 + s], end_r.at[2, 2 + s], twin).start()
        for n, result in ((0, dh_out), (2, block_out)):
            for s in range(2):
                for k, xx in ((1, x), (2, 1 - x)):
                    there = result.at[:, columns_of(s, xx, 1 - c)]
                    remote(there, there, end_s.at[k, n + s], end_r.at[k, n + s], twin).wait_recv()
                for k, target in ((0, across), (1, twin), (2, twin)):
                    there = result.at[:, columns_of(s, 1 - x if k == 2 else x, c)]
                    remote(there, there, end_s.at[k, n + s], end_r.at[k, n + s], target).wait_send()
        for k in range(1, GROUPS):
            there = gates_out.at[lax.rem(e + GROUPS - k, GROUPS)]
            remote(there, there, far_s.at[k - 1], far_r.at[k - 1], peers[k - 1]).wait_recv()
            far(k).wait_send()
        each(near, "wait_send")

        def drain(i, carry):
            pl.when(i >= GROUPS - 2)(lambda: to_twin(i).wait_send())
            pl.when(i >= GROUPS - 2)(lambda: y_twin(i).wait_send())
            p_across(i).wait_send()
            yp_across(i).wait_send()
            return carry

        lax.fori_loop(0, GROUPS, drain, 0)

        def drain_pair(j, carry):
            p_beside(j).wait_send()
            q_beside(j).wait_send()
            q_across(j).wait_send()
            yp_beside(j).wait_send()
            yq_beside(j).wait_send()
            yq_across(j).wait_send()
            for s in range(2):
                pl.when(z < j)(lambda s=s: up(j, s).wait_send())
                pl.when(z > j)(lambda s=s: down_z(j, s).wait_send())
                pl.when(z < j)(lambda s=s: y_up(j, s).wait_send())
                pl.when(z > j)(lambda s=s: y_down(j, s).wait_send())
            return carry

        lax.fori_loop(0, NZ, drain_pair, 0)

        def drain_rows_of(i, carry):
            b = block_of(i)
            h_across(b).wait_send()
            for stream in range(3):
                h_twin(b, stream).wait_send()
            return carry

        lax.fori_loop(1, GROUPS, drain_rows_of, 0)
        line.finish()
        keep_o.wait()
        for k in range(2):
            each(gu_copies(4 * tiles - 2 + k), "wait")
            each(d_copies(6 + k), "wait")

    shape = jax.ShapeDtypeStruct
    dma = pltpu.SemaphoreType.DMA
    f32 = jnp.float32
    return pl.pallas_call(
        kernel,
        out_shape=(
            shape((rows, width), low),
            shape((rows, width), low),
            shape((GROUPS, 8, rows), f32),
            shape((local, width, hidden), f32),
            shape((local, width, hidden), f32),
            shape((local, hidden, width), f32),
            shape((tokens,) + attended.shape[1:], low),
        ),
        in_specs=[HBM, HBM, HBM, HBM, VMEM, VMEM, HBM, HBM],
        out_specs=(VMEM, VMEM, VMEM, HBM, HBM, HBM, HBM),
        scratch_shapes=[
            pltpu.VMEM(gate_up.shape, low),
            pltpu.VMEM(down.shape, low),
            dma((2,)),
            pltpu.VMEM((tokens, width), low),
            pltpu.VMEM((tokens, width), low),
            pltpu.VMEM((tokens, units), low),
            pltpu.VMEM((tokens, 2 * units), low),
            pltpu.VMEM((2, rows, width), low),
            pltpu.VMEM((2, rows, width), low),
            pltpu.VMEM((GROUPS, rows, half), low),
            pltpu.VMEM((GROUPS, rows, piece), low),
            pltpu.VMEM((NZ, rows, piece), low),
            pltpu.VMEM((NZ, rows, part), low),
            pltpu.VMEM((NZ, rows, piece), low),
            pltpu.VMEM((2, NZ, rows, piece), low),
            pltpu.VMEM((2, NZ, rows, piece), low),
            pltpu.VMEM((2, NZ, rows, piece), low),
            pltpu.VMEM((rows, part), f32),
            pltpu.VMEM((2, piece // 2, 2 * units), f32),
            pltpu.VMEM((2, units, width // 8), f32),
            pltpu.VMEM((GROUPS, rows, half), low),
            pltpu.VMEM((GROUPS, rows, piece), low),
            pltpu.VMEM((NZ, rows, piece), low),
            pltpu.VMEM((NZ, rows, part), low),
            pltpu.VMEM((NZ, rows, piece), low),
            pltpu.VMEM((2, NZ, rows, piece), low),
            pltpu.VMEM((2, NZ, rows, piece), low),
            pltpu.VMEM((2, NZ, rows, piece), low),
            pltpu.VMEM((GROUPS, 8, rows), f32),
            pltpu.VMEM((tensors, GROUPS, 8, rows), f32),
            dma((GROUPS,)), dma, dma, dma((3, 14, 3)), dma((3, 14)), dma((GROUPS,)), dma((GROUPS,)),
            dma((GROUPS, 3)), dma((GROUPS, 3)), dma((2,)), dma((GROUPS,)), dma((GROUPS,)), dma((GROUPS,)), dma((GROUPS,)),
            dma((NZ,)), dma((NZ,)), dma((NZ,)), dma((NZ,)), dma((NZ,)), dma((NZ,)),
            dma((2, 2, NZ)), dma((2, 2, NZ)), dma((2, 2 * local)), dma((2, local)),
            dma((GROUPS,)), dma((GROUPS,)), dma((GROUPS,)), dma((GROUPS,)),
            dma((NZ,)), dma((NZ,)), dma((NZ,)), dma((NZ,)), dma((NZ,)), dma((NZ,)),
            dma((2, 2, NZ)), dma((2, 2, NZ)),
            dma((tensors - 1,)), dma((tensors - 1,)), dma((GROUPS - 1,)), dma((GROUPS - 1,)),
            dma((3, 4)), dma((3, 4)),
        ],
        compiler_params=comm_params(collective_id, 62),
        cost_estimate=cost(80),
        name="expert_layer",
    )(hidden_two, grad_out_all, gate_up, down, router_t, chosen_all, residual, attended)


def exchange_rows(value, part_ref, land_ref, send_sem, recv_sem, mates):
    rows = value.shape[0]
    line = lax.broadcasted_iota(jnp.int32, (rows, 128), 1)
    part_ref[...] = jnp.transpose(jnp.where(line == 0, value, 0.0))[:8, :]
    for k, mate in enumerate(mates):
        remote(part_ref, land_ref.at[k], send_sem.at[k], recv_sem.at[k], mate).start()


def exchanged_rows(part_ref, land_ref, send_sem, recv_sem, mates):
    total = part_ref[...]
    for k, mate in enumerate(mates):
        remote(part_ref, land_ref.at[k], send_sem.at[k], recv_sem.at[k], mate).wait_recv()
    for k in range(len(mates)):
        total = total + land_ref[k]
    rows = part_ref.shape[1]
    tall = jnp.concatenate([total, jnp.zeros((120, rows), jnp.float32)], axis=0)
    return jnp.transpose(tall)[:, :1]


def drain_rows(part_ref, land_ref, send_sem, recv_sem, mates):
    for k, mate in enumerate(mates):
        remote(part_ref, land_ref.at[k], send_sem.at[k], recv_sem.at[k], mate).wait_send()


def turn(value, cosine, sine):
    return value * cosine + pltpu.roll(value, HEAD // 2, 1) * sine


def project(
    tokens, w_qkv, w_out, out_grad, gain_one, gain_two, qk_gain, w_router, routes, cosine, sine,
    w_gate, w_up, w_down, collective_id,
):
    rows, width = tokens.shape
    parts, depth, columns = w_qkv.shape
    heads = columns // HEAD
    tensors = NX * NC
    back = WINDOW // rows
    low, f32 = jnp.bfloat16, jnp.float32
    QUERY, KEY, VALUE, SMALL, OUT, GRAD, REST = 0, 1, 2, 3, 4, 5, 6
    out_half = w_out.shape[0] // 2
    out_rows, out_columns = w_out.shape
    quarter = width // tensors
    experts = w_router.shape[0]
    small_shape = (8 + 2 * experts, depth)

    def kernel(
        tok_ref, w_in, out_ref, grad_in, gain_one_ref, gain_two_ref, qk_ref, w_router_ref, routes_ref, cos_ref, sin_ref, gate_in, up_in, down_in,
        w_all, out_all, grad_all, h1_out, raw_out, gate_up, down_out, gain_ref, router_ref, chosen_ref, scale_ref, q_ref, context,
        w_ref, w_sem, small_ref, small_all, h1_ref, raw_ref, wide_in, wide_low, down_f, down_low, own_w, own_out, weights, total, part_k, land_k, part_q, land_q,
        send_sem, recv_sem, out_sem, small_sem, kept, ks_s, ks_r, qs_s, qs_r, c_s, c_r, hx_s, hx_r, hc_s, hc_r, wide_s,
    ):
        z, y, x, c = place()
        e, t = lax.axis_index("expert"), lax.axis_index("tensor")
        w_loads = [pltpu.make_async_copy(w_in.at[k], w_ref.at[k], w_sem.at[k]) for k in range(parts)]
        for part in (VALUE, KEY, QUERY):
            w_loads[part].start()
        wide_loads = [
            pltpu.make_async_copy(source.at[k], wide_in.at[2 * n + k], wide_s.at[2 * n + k])
            for n, source in enumerate((gate_in, up_in))
            for k in range(2)
        ]
        for copy in wide_loads:
            copy.start()
        mates = [(e, lax.rem(t + k, tensors)) for k in range(1, tensors)]
        beside, above = device(z, 1 - y, x, c), device(z + 1, y, x, c)
        views = [
            lambda b: weights.at[QUERY, block_rows(b, depth), :],
            lambda b: weights.at[KEY, block_rows(b, depth), :],
            lambda b: weights.at[VALUE, block_rows(b, depth), :],
            lambda b: small_all.at[b],
            lambda b: out_all.at[pl.ds(0, out_half), block_rows(b, out_columns)],
            lambda b: grad_view(b, x, c),
            lambda b: out_all.at[pl.ds(out_half, out_half), block_rows(b, out_columns)],
        ]
        across, twin = device(z, y, 1 - x, c), device(z, y, x, 1 - c)

        def quarter_at(xx, cc):
            return pl.ds(pl.multiple_of((xx * NC + cc) * quarter, quarter), quarter)

        def grad_view(b, xx, cc):
            return grad_all.at[block_rows(b, rows), quarter_at(xx, cc)]

        def grad_across(b, landing=False):
            piece = grad_view(b, 1 - x if landing else x, c)
            return remote(piece, piece, hx_s.at[b], hx_r.at[b], across)

        def grad_twin(b, relayed, landing=False):
            piece = grad_view(b, 1 - x if relayed else x, 1 - c if landing else c)
            return remote(piece, piece, hc_s.at[b, relayed], hc_r.at[b, relayed], twin)

        line = LineGather(
            [SMALL, VALUE, KEY, QUERY, OUT, GRAD, REST],
            [
                own_w.at[0], own_w.at[1], own_w.at[2], small_ref, own_out.at[pl.ds(0, out_half)],
                grad_in.at[:, quarter_at(x, c)], own_out.at[pl.ds(out_half, out_half)],
            ],
            views, send_sem, recv_sem, y_first=(OUT,),
        )
        small_ref[...] = jnp.zeros_like(small_ref)
        small_ref[0:1, :] = gain_one_ref[...].astype(low).astype(f32)
        small_ref[1:2, :] = gain_two_ref[...].astype(low).astype(f32)
        small_ref[2:3, : qk_gain.shape[1]] = qk_ref[...].astype(low).astype(f32)
        small_ref[8 : 8 + experts, :] = w_router_ref[...]
        expert_row = lax.broadcasted_iota(jnp.int32, (experts, rows), 0)
        named = jnp.zeros((experts, rows), f32)
        for k in range(routes.shape[0]):
            named = jnp.where(routes_ref[k : k + 1, :] == expert_row, 1.0, named)
        small_ref[8 + experts : 8 + 2 * experts, :] = named
        greet(line.partners() + [(mate, None) for mate in mates])
        line.start(SMALL, 0)
        for part in (VALUE, KEY, QUERY):
            w_loads[part].wait()

            def cast(i, carry, part=part):
                r = pl.ds(pl.multiple_of(i * 32, 32), 32)
                own_w[part, r, :] = w_ref[part, r, :].astype(low)
                return carry

            lax.fori_loop(0, depth // 32, cast, 0)
            if part != QUERY:
                line.start(part, 0)

        def cast_out(i, carry):
            r = pl.ds(pl.multiple_of(i * 32, 32), 32)
            own_out[r, :] = out_ref[r, :].astype(low)
            return carry

        lax.fori_loop(0, out_rows // 32, cast_out, 0)
        keep_out = pltpu.make_async_copy(own_out, out_all.at[:, block_rows(line.block(0), out_columns)], kept.at[0])
        keep_out.start()
        keep_grad = pltpu.make_async_copy(grad_in, grad_all.at[block_rows(line.block(0), rows), :], kept.at[1])
        keep_grad.start()

        def square(i, carry):
            r = pl.ds(pl.multiple_of(i * 32, 32), 32)
            value = tok_ref[r, :].astype(f32)
            scale_ref[r, 0:1] = lax.rsqrt(jnp.mean(value * value, axis=-1, keepdims=True) + EPS)
            return carry

        lax.fori_loop(0, rows // 32, square, 0)
        total[...] = jnp.zeros_like(total)
        own_small = pltpu.make_async_copy(small_ref, small_all.at[line.block(0)], small_sem)
        own_small.start()

        def use(stream, rel):
            b = line.block(rel)
            at = pl.ds(pl.multiple_of(b * depth, depth), depth)
            if stream == SMALL:
                gain = small_ref[0:1, :] if rel == 0 else small_all[b, 0:1, :]
                h1_ref[:, at] = (tok_ref[:, at].astype(f32) * scale_ref[:, 0:1] * gain).astype(low)
                return
            block = own_w[stream] if rel == 0 else weights[stream, block_rows(b, depth), :]
            total[stream] += dot(h1_ref[:, at], block, (1, 0))

        def event(stream, rel):
            def body():
                line.arrive(stream, rel)
                if line.forwards(stream, rel):
                    marks = len(line.pending)
                    line.start(stream, rel)
                    late = line.pending[marks:]
                    del line.pending[marks:]
                    line.finish_later(late, rel)
                if stream == GRAD:
                    b = line.block(rel)
                    grad_across(b).start()
                    grad_twin(b, 0).start()
                elif stream not in (OUT, REST):
                    use(stream, rel)
            run_if(line.exists(rel), body)

        use(SMALL, 0)
        use(VALUE, 0)
        own_small.wait()

        units = down_in.shape[1]
        for n, copy in enumerate(wide_loads):
            copy.wait()

            def round_wide(i, carry, n=n):
                r = pl.ds(pl.multiple_of(i * 64, 64), 64)
                wide_low[r, pl.ds(n * units, units)] = wide_in[n, r, :].astype(low)
                return carry

            lax.fori_loop(0, width // 64, round_wide, 0)
        wide_out = pltpu.make_async_copy(wide_low, gate_up, wide_s.at[0])
        wide_out.start()
        down_loads = [
            pltpu.make_async_copy(down_in.at[k], down_f.at[pl.ds(k * units, units), :], wide_s.at[1 + k])
            for k in range(2)
        ]
        for copy in down_loads:
            copy.start()

        use(KEY, 0)
        def events(*pairs):
            for stream, rels in pairs:
                for rel in rels:
                    event(stream, rel)

        for rel in (7, 1, 4, 2, 5):
            event(SMALL, rel)
            event(VALUE, rel)
        for copy in down_loads:
            copy.wait()

        def round_down(i, carry):
            r = pl.ds(pl.multiple_of(i * 32, 32), 32)
            down_low[r, :] = down_f[r, :].astype(low)
            return carry

        lax.fori_loop(0, 2 * units // 32, round_down, 0)
        down_copy = pltpu.make_async_copy(down_low, down_out, wide_s.at[3])
        down_copy.start()
        line.start(QUERY, 0)
        for rel in (3, 6):
            event(SMALL, rel)
            event(VALUE, rel)
        events((KEY, (7, 1, 4)))
        for rel in (8, 11, 9, 12, 10, 13):
            event(SMALL, rel)
            event(VALUE, rel)

        slices = HEAD // GROUPS
        for b in range(GROUPS):
            at = pl.ds(b * depth, depth)
            gain_ref[0:2, at] = small_all[b, 0:2, :]
            router_ref[:, at] = small_all[b, 8 : 8 + experts, :].astype(low)
            tall = jnp.concatenate(
                [small_all[b, 8 + experts : 8 + 2 * experts, :], jnp.zeros((128 - experts, depth), f32)], axis=0
            )
            chosen_ref[pl.ds(b * depth, depth), :] = jnp.transpose(tall)[:, :experts].astype(low)
        for which in range(2):
            for head in range(heads):
                start = (which * heads + head) * slices
                gain_ref[2 + which : 3 + which, pl.ds(head * HEAD, HEAD)] = jnp.concatenate(
                    [small_all[b, 2:3, start : start + slices] for b in range(GROUPS)], axis=1
                )

        def context_copy(which, k):
            if k == 2:
                source, target = 0, above
            elif k == 4:
                source, target = 2, above
            else:
                source, target = jnp.where(y == 0, k - 1, k + 1), beside
            return remote(
                context.at[source, which], context.at[k, which], c_s.at[which, k], c_r.at[which, k], target
            )

        sends = {2: z < NZ - 1, 4: (z >= 1) & (z < NZ - 1), 1: (y == 0) | (z >= 1), 3: z >= 1 + y}
        takes = {2: z >= 1, 4: z >= 2, 1: (y == 1) | (z >= 1), 3: z >= 2 - y}

        def context_send(which, k):
            run_if(sends[k], lambda: context_copy(which, k).start())

        def context_take(which, k):
            run_if(takes[k], lambda: context_copy(which, k).wait_recv())

        for k in range(1, back + 1):
            def clear(k=k):
                context[k] = jnp.zeros_like(context[k])
            run_if(jnp.logical_not(takes[k]), clear)

        context[0, 1] = total[VALUE].astype(low)
        context_send(1, 2)
        run_if(y == 0, lambda: context_copy(1, 1).start())
        events((KEY, (2, 5, 3, 6)), (QUERY, (7, 1, 4)))
        line.start(GRAD, 0)
        line.start(OUT, 0)
        line.start(REST, 0)
        events((KEY, (8, 11, 9, 12, 10, 13)))
        key_raw = total[KEY]
        raw_ref[1] = key_raw
        exchange_rows(jnp.sum(key_raw * key_raw, axis=-1, keepdims=True), part_k, land_k, ks_s, ks_r, mates)
        use(QUERY, 0)
        events((QUERY, (2, 5)))
        key_scale = lax.rsqrt(exchanged_rows(part_k, land_k, ks_s, ks_r, mates) / width + EPS)
        scale_ref[:, 2:3] = key_scale
        def rotated(which, scale, store):
            for head in range(heads):
                at = pl.ds(head * HEAD, HEAD)
                value = total[which, :, at] * scale * gain_ref[2 + which : 3 + which, at]
                store(at, turn(value, cos_ref[...], sin_ref[...]).astype(low))

        def store_key(at, value):
            context[0, 0, :, at] = value

        rotated(KEY, key_scale, store_key)
        context_send(0, 2)
        run_if(y == 0, lambda: context_copy(0, 1).start())

        def relay_two(which):
            context_take(which, 2)
            context_send(which, 4)
            run_if((y == 1) & (z >= 1), lambda: context_copy(which, 1).start())
            run_if((y == 0) & sends[3], lambda: context_copy(which, 3).start())

        def relay_four(which):
            context_take(which, 4)
            run_if((y == 1) & sends[3], lambda: context_copy(which, 3).start())

        relay_two(1)
        events((QUERY, (3, 6)), (GRAD, (7, 1, 4)), (OUT, (7, 1, 4)), (REST, (7, 1, 4)))
        relay_four(1)
        events((QUERY, (8, 11)), (GRAD, (2, 5)), (OUT, (8, 11, 2, 5)), (REST, (2, 5)))
        relay_two(0)
        events((QUERY, (9, 12, 10, 13)))
        query_raw = total[QUERY]
        raw_ref[0] = query_raw
        exchange_rows(jnp.sum(query_raw * query_raw, axis=-1, keepdims=True), part_q, land_q, qs_s, qs_r, mates)
        for part in range(parts):
            weights[part, block_rows(line.block(0), depth), :] = own_w[part]
        keep = pltpu.make_async_copy(weights, w_all, out_sem)
        keep.start()
        keep_more = [
            pltpu.make_async_copy(h1_ref, h1_out, kept.at[2]),
            pltpu.make_async_copy(raw_ref, raw_out, kept.at[3]),
        ]
        for copy in keep_more:
            copy.start()
        events((GRAD, (3, 6)), (OUT, (9, 12, 3, 6)), (REST, (3, 6, 8, 11)))
        relay_four(0)
        query_scale = lax.rsqrt(exchanged_rows(part_q, land_q, qs_s, qs_r, mates) / width + EPS)
        scale_ref[:, 1:2] = query_scale

        def store_query(at, value):
            q_ref[:, at] = value

        rotated(QUERY, query_scale, store_query)
        events((GRAD, (8, 11, 9, 12)), (OUT, (10, 13)), (REST, (9, 12, 10, 13)), (GRAD, (10, 13)))
        for which in (1, 0):
            for k in (1, 3):
                context_take(which, k)
        for rel in line.order():
            def relay(rel=rel):
                b = line.block(rel)
                grad_across(b, True).wait_recv()
                grad_twin(b, 1).start()
            run_if(line.exists(rel), relay)
        for rel in line.order():
            def landed(rel=rel):
                b = line.block(rel)
                grad_across(b).wait_send()
                for relayed in range(2):
                    grad_twin(b, relayed, True).wait_recv()
                    grad_twin(b, relayed).wait_send()
            run_if(line.exists(rel), landed)
        line.finish()
        for copy in keep_more:
            copy.wait()
        wide_out.wait()
        down_copy.wait()
        keep_out.wait()
        keep_grad.wait()
        for which in range(2):
            for k in range(1, back + 1):
                run_if(sends[k], lambda which=which, k=k: context_copy(which, k).wait_send())
        drain_rows(part_k, land_k, ks_s, ks_r, mates)
        drain_rows(part_q, land_q, qs_s, qs_r, mates)
        keep.wait()

    shape, dma = jax.ShapeDtypeStruct, pltpu.SemaphoreType.DMA
    return pl.pallas_call(
        kernel,
        out_shape=(
            shape((parts, depth * GROUPS, columns), low),
            shape((out_rows, out_columns * GROUPS), low),
            shape((rows * GROUPS, width), low),
            shape((rows, width), low),
            shape((2, rows, columns), f32),
            shape((width, 4 * w_down.shape[1]), low),
            shape((2 * w_down.shape[1], width), low),
            shape((8, width), f32),
            shape((experts, width), low),
            shape((rows * GROUPS, experts), low),
            shape((rows, 128), f32),
            shape((rows, columns), low),
            shape((back + 1, 2, rows, columns), low),
        ),
        in_specs=[VMEM, HBM, VMEM, HBM] + [VMEM] * 7 + [HBM, HBM, HBM],
        out_specs=(HBM,) * 7 + (VMEM,) * 6,
        scratch_shapes=[
            pltpu.VMEM((parts, depth, columns), f32),
            dma((parts,)),
            pltpu.VMEM(small_shape, f32),
            pltpu.VMEM((GROUPS,) + small_shape, f32),
            pltpu.VMEM((rows, width), low),
            pltpu.VMEM((2, rows, columns), f32),
            pltpu.VMEM((4, width, w_down.shape[1]), f32),
            pltpu.VMEM((width, 4 * w_down.shape[1]), low),
            pltpu.VMEM((2 * w_down.shape[1], width), f32),
            pltpu.VMEM((2 * w_down.shape[1], width), low),
            pltpu.VMEM((parts, depth, columns), low),
            pltpu.VMEM((out_rows, out_columns), low),
            pltpu.VMEM((parts, depth * GROUPS, columns), low),
            pltpu.VMEM((parts, rows, columns), f32),
            pltpu.VMEM((8, rows), f32),
            pltpu.VMEM((tensors - 1, 8, rows), f32),
            pltpu.VMEM((8, rows), f32),
            pltpu.VMEM((tensors - 1, 8, rows), f32),
            dma((7, 14, 3)), dma((7, 14)), dma, dma, dma((4,)),
            dma((tensors - 1,)), dma((tensors - 1,)), dma((tensors - 1,)), dma((tensors - 1,)),
            dma((2, back + 1)), dma((2, back + 1)),
            dma((GROUPS,)), dma((GROUPS,)), dma((GROUPS, 2)), dma((GROUPS, 2)), dma((4,)),
        ],
        compiler_params=comm_params(collective_id, 62),
        cost_estimate=cost(100),
        name="project",
    )(
        tokens, w_qkv, w_out, out_grad, gain_one, gain_two, qk_gain, w_router, routes, cosine, sine,
        w_gate, w_up, w_down,
    )


def attend(query, context, segment_query, segment_keys, tokens, out_low, gain, collective_id):
    rows, columns = query.shape
    width = tokens.shape[1]
    blocks = context.shape[0]
    heads = columns // HEAD
    half, quarter = width // 2, width // 4
    low, f32 = jnp.bfloat16, jnp.float32

    def kernel(
        q_ref, context_in, sq_ref, sk_ref, tok_ref, out_in, gain_ref,
        o_ref, lse_ref, x1_out, h2_out, scale_ref,
        context_ref, out_ref, x1_ref, h2_ref, copy_sem, part, full, core_buf, x_buf, send_sem, recv_sem,
    ):
        z, y, x, c = place()
        across, twin = device(z, y, 1 - x, c), device(z, y, x, 1 - c)
        context_load = pltpu.make_async_copy(context_in, context_ref, copy_sem.at[0])
        context_load.start()
        out_load = pltpu.make_async_copy(out_in, out_ref, copy_sem.at[1])
        out_load.start()
        greet([(across, None), (twin, None)])
        row = lax.broadcasted_iota(jnp.int32, (rows, rows), 0)
        column = lax.broadcasted_iota(jnp.int32, (rows, rows), 1)
        allowed = []
        for k in range(blocks):
            distance = row - column + k * rows
            allowed.append(
                (sq_ref[...] == sk_ref[k : k + 1, :]) & (distance >= 0) & (distance < WINDOW)
            )
        line = lax.broadcasted_iota(jnp.int32, (rows, 128), 1)
        lse = jnp.zeros((rows, 128), f32)
        context_load.wait()
        for head in range(heads):
            at = pl.ds(head * HEAD, HEAD)
            scores = [
                jnp.where(
                    allowed[k], dot(q_ref[:, at], context_ref[k, 0, :, at], (1, 1)) * HEAD ** (-0.5), -1e30
                )
                for k in range(blocks)
            ]
            largest = scores[0]
            for k in range(1, blocks):
                largest = jnp.maximum(largest, scores[k])
            largest = jnp.max(largest, axis=-1, keepdims=True)
            weights = [jnp.exp(s - largest) for s in scores]
            amount = weights[0]
            for k in range(1, blocks):
                amount = amount + weights[k]
            amount = jnp.sum(amount, axis=-1, keepdims=True)
            inverse = 1.0 / amount
            value = jnp.zeros((rows, HEAD), f32)
            for k in range(blocks):
                value = value + dot((weights[k] * inverse).astype(low), context_ref[k, 1, :, at], (1, 0))
            o_ref[:, at] = value.astype(low)
            lse = jnp.where(line == head, largest + jnp.log(amount), lse)
        lse_ref[...] = lse

        def half_of(cc):
            return pl.ds(pl.multiple_of(cc * half, half), half)

        def fill(cc):
            def body(k, carry):
                at = pl.ds(pl.multiple_of(cc * half + k * quarter, quarter), quarter)
                part[:, at] = dot(o_ref[...], out_ref[:, at], (1, 0)).astype(low)
                return carry

            lax.fori_loop(0, 2, body, 0)

        out_load.wait()
        fill(1 - c)
        group_sum(part, full, core_buf, x_buf, send_sem, recv_sem, lambda: fill(c))

        def norm(i, carry):
            r = pl.ds(pl.multiple_of(i * 32, 32), 32)
            value = tok_ref[r, :].astype(f32) + full[r, :].astype(f32)
            scale = lax.rsqrt(jnp.mean(value * value, axis=-1, keepdims=True) + EPS)
            x1_ref[r, :] = value
            scale_ref[r, :] = jnp.broadcast_to(scale, (32, 128))
            h2_ref[r, :] = (value * scale * gain_ref[1:2, :]).astype(low)
            return carry

        lax.fori_loop(0, rows // 32, norm, 0)
        keep = [
            pltpu.make_async_copy(x1_ref, x1_out, copy_sem.at[2]),
            pltpu.make_async_copy(h2_ref, h2_out, copy_sem.at[3]),
        ]
        for copy in keep:
            copy.start()
        for copy in keep:
            copy.wait()

    shape, dma = jax.ShapeDtypeStruct, pltpu.SemaphoreType.DMA
    return pl.pallas_call(
        kernel,
        out_shape=(
            shape((rows, columns), low),
            shape((rows, 128), f32),
            shape((rows, width), f32),
            shape((rows, width), low),
            shape((rows, 128), f32),
        ),
        in_specs=[VMEM, HBM, VMEM, VMEM, VMEM, HBM, VMEM],
        out_specs=(VMEM, VMEM, HBM, HBM, VMEM),
        scratch_shapes=[
            pltpu.VMEM(context.shape, low),
            pltpu.VMEM(out_low.shape, low),
            pltpu.VMEM((rows, width), f32),
            pltpu.VMEM((rows, width), low),
            dma((4,)),
            pltpu.VMEM((rows, width), low),
            pltpu.VMEM((rows, width), low),
            pltpu.VMEM((rows, half), low),
            pltpu.VMEM((rows, quarter), low),
            dma((5,)), dma((5,)),
        ],
        compiler_params=comm_params(collective_id, 62),
        cost_estimate=cost(40),
        name="attend",
    )(query, context, segment_query, segment_keys, tokens, out_low, gain)


def attend_back(
    grad_hidden, grad_probs, router_t, hidden_two, residual, scale_two, gains, out_grad,
    query, context, segment_query, segment_keys, attended, log_sums, raw, scales,
    cosine, sine, hidden_one, tokens, attended_all, qkv_low, out_low, collective_id,
):
    rows, width = tokens.shape
    columns = query.shape[1]
    heads = columns // HEAD
    experts = router_t.shape[0]
    blocks = context.shape[0]
    depth = width // GROUPS
    small_rows = 8 + experts
    tensors = NX * NC
    half, quarter = width // 2, width // 4
    low, f32 = jnp.bfloat16, jnp.float32
    QUERY, KEY, VALUE, OUT, SMALL = 0, 1, 2, 3, 4

    def kernel(
        dh_ref, gates_ref, router_ref, h2_ref, x1_ref, s2_ref, gain_ref, dy_ref,
        q_ref, context_in, sq_ref, sk_ref, o_ref, lse_ref, raw_in, scale_ref,
        cos_ref, sin_ref, h1_in, tok_in, o_all_in, w_hbm, out_in,
        tok_grad, qkv_sum, out_sum, small_sum,
        context_ref, raw_ref, h1_ref, tok_ref, o_all, out_ref, load_sem, weights, dx1, da, do, dot_sums, dq, dkv, scaled, proj, send_kv, land_y, land_z,
        part, full, core_buf, x_buf, small, line_sum,
        main_buf, da_all, small_buf, part_k, land_k, part_q, land_q,
        w_sem, y_s, y_r, z_s, z_r, group_s, group_r, ks_s, ks_r, qs_s, qs_r, line_s, line_r, far_s, far_r, near_s, near_r,
    ):
        z, y, x, c = place()
        e, t = lax.axis_index("expert"), lax.axis_index("tensor")
        mates = [(e, lax.rem(t + k, tensors)) for k in range(1, tensors)]
        beside, below = device(z, 1 - y, x, c), device(z - 1, y, x, c)
        fetch = pltpu.make_async_copy(w_hbm, weights, w_sem)
        fetch.start()
        loads = [
            pltpu.make_async_copy(source, target, load_sem.at[k])
            for k, (source, target) in enumerate(
                (
                    (out_in, out_ref), (context_in, context_ref), (raw_in, raw_ref), (h1_in, h1_ref), (tok_in, tok_ref),
                    (o_all_in, o_all),
                )
            )
        ]
        for copy in loads:
            copy.start()

        def own_part(s, b):
            if s == SMALL:
                return small[b]
            at = pl.ds(pl.multiple_of(b * depth, depth), depth)
            return dot(h1_ref[:, at], proj[s], (0, 0))

        peers = [(lax.rem(e + k, GROUPS), t) for k in range(1, GROUPS)]
        share = rows // tensors
        share_at = pl.ds(pl.multiple_of(t * share, share), share)

        def columns_of(owner):
            return pl.ds(pl.multiple_of(owner * depth, depth), depth)

        def da_far(k):
            owner = lax.rem(e + k, GROUPS)
            return remote(
                da.at[share_at, columns_of(owner)], da_all.at[e, share_at, :], far_s.at[k - 1], far_r.at[k - 1],
                peers[k - 1],
            )

        def da_near(k):
            piece = da_all.at[:, share_at, :]
            return remote(piece, piece, near_s.at[k], near_r.at[k], mates[k])

        def da_start():
            for k in range(1, GROUPS):
                da_far(k).start()
            da_all[e, share_at, :] = da[share_at, columns_of(e)]

        def da_spread():
            for k in range(1, GROUPS):
                landing = da_all.at[lax.rem(e + GROUPS - k, GROUPS), share_at, :]
                remote(landing, landing, far_s.at[k - 1], far_r.at[k - 1], peers[k - 1]).wait_recv()
            for k in range(tensors - 1):
                da_near(k).start()

        def da_end():
            for k in range(tensors - 1):
                theirs = lax.rem(t + tensors - 1 - k, tensors)
                landing = da_all.at[:, pl.ds(pl.multiple_of(theirs * share, share), share), :]
                remote(landing, landing, near_s.at[k], near_r.at[k], mates[k]).wait_recv()
            result = jnp.zeros((columns, depth), f32)
            for b in range(GROUPS):
                result = result + dot(o_all[pl.ds(b * rows, rows), :], da_all[b], (0, 0))
            out_sum[...] = result
            for k in range(1, GROUPS):
                da_far(k).wait_send()
            for k in range(tensors - 1):
                da_near(k).wait_send()

        def slot(kind):
            def view(s, zz):
                if s == SMALL:
                    return small_buf.at[kind, zz]
                return main_buf.at[kind, zz, s]
            return view

        line = LineReduce([], lambda s, zz, yy: slot(3)(s, zz), slot(0), slot(1), slot(2), line_s, line_r)
        greet([(target, None) for target in mates + peers])

        grad_probs = gates_ref[...]
        logits = dot(h2_ref[...], router_ref[...], (1, 1))
        shifted = jnp.exp(logits - jnp.max(logits, axis=-1, keepdims=True))
        probs = shifted / jnp.sum(shifted, axis=-1, keepdims=True)
        grad_logits = probs * (grad_probs - jnp.sum(probs * grad_probs, axis=-1, keepdims=True))
        tall = jnp.transpose(
            jnp.concatenate([grad_logits, jnp.zeros((rows, 128 - experts), f32)], axis=1)
        )
        grad_logits = grad_logits.astype(low)
        tall = tall.astype(low)
        for b in range(GROUPS):
            small[b] = jnp.zeros_like(small[b])
            small[b, 8 : 8 + experts, :] = dot(tall, h2_ref[:, pl.ds(b * depth, depth)], (1, 0))[:experts]
        dx1[...] = dot(grad_logits, router_ref[...], (1, 0))
        line_sum[...] = jnp.zeros_like(line_sum)

        def norm_two(i, carry):
            r = pl.ds(pl.multiple_of(i * 32, 32), 32)
            grad = dh_ref[r, :].astype(f32) + dx1[r, :]
            value, scale = x1_ref[r, :], s2_ref[r, 0:1]
            line_sum[0:1, :] += jnp.sum(grad * (value * scale), axis=0, keepdims=True)
            grad = grad * gain_ref[1:2, :]
            inner = jnp.mean(grad * value, axis=-1, keepdims=True)
            result = dy_ref[r, :].astype(f32) + scale * grad - value * (scale * scale * scale) * inner
            dx1[r, :] = result
            da[r, :] = result.astype(low)
            return carry

        lax.fori_loop(0, rows // 32, norm_two, 0)

        da_start()

        for copy in loads:
            copy.wait()
        do[...] = dot(da[...], out_ref[...], (1, 1)).astype(low)
        wide = lax.broadcasted_iota(jnp.int32, (rows, 128), 1)
        sums = jnp.zeros((rows, 128), f32)
        for head in range(heads):
            at = pl.ds(head * HEAD, HEAD)
            inner = jnp.sum(do[:, at].astype(f32) * o_ref[:, at].astype(f32), axis=-1, keepdims=True)
            sums = jnp.where(wide == head, inner, sums)
        dot_sums[...] = sums
        dq[...] = jnp.zeros_like(dq)
        row = lax.broadcasted_iota(jnp.int32, (rows, rows), 0)
        column = lax.broadcasted_iota(jnp.int32, (rows, rows), 1)

        def attention_block(k):
            distance = row - column + k * rows
            allowed = (sq_ref[...] == sk_ref[k : k + 1, :]) & (distance >= 0) & (distance < WINDOW)
            for head in range(heads):
                at = pl.ds(head * HEAD, HEAD)
                queries, keys, values = q_ref[:, at], context_ref[k, 0, :, at], context_ref[k, 1, :, at]
                scores = dot(queries, keys, (1, 1)) * HEAD ** (-0.5)
                weight = jnp.where(allowed, jnp.exp(scores - lse_ref[:, head : head + 1]), 0.0)
                grad_weight = dot(do[:, at], values, (1, 1))
                grad_score = (
                    weight * (grad_weight - dot_sums[:, head : head + 1]) * HEAD ** (-0.5)
                ).astype(low)
                dq[:, at] += dot(grad_score, keys, (1, 0))
                dkv[k, 0, :, at] = dot(grad_score, queries, (0, 0))
                dkv[k, 1, :, at] = dot(weight.astype(low), do[:, at], (0, 0))

        exists = {0: None, 1: (y == 1) | (z >= 1), 2: z >= 1, 3: z >= 2 - y, 4: z >= 2}
        comes = {1: (y == 0) | (z >= 1), 3: z >= 1 + y}

        def kv_copy(which, k):
            if k in (1, 3):
                landing, target = land_y.at[k // 2, which], beside
                return remote(send_kv.at[k - 1, which], landing, y_s.at[k // 2, which], y_r.at[k // 2, which], target)
            landing = land_z.at[k // 2 - 1, which]
            return remote(
                send_kv.at[k - 1, which], landing, z_s.at[k // 2 - 1, which], z_r.at[k // 2 - 1, which], below
            )

        def kv_send(which, k):
            send_kv[k - 1, which] = dkv[k, which].astype(low)
            kv_copy(which, k).start()

        def merge(into, which, landed):
            add_to(dkv.at[into, which], dkv.at[into, which], landed, 32)

        for k in (3, 1, 4, 2, 0):
            def one(k=k):
                attention_block(k)
                if k in (1, 3):
                    kv_send(1, k)
                    kv_send(0, k)
            run_if(exists[k], one)

        def take_three(which):
            def land():
                kv_copy(which, 3).wait_recv()
                pl.when(y == 1)(lambda: merge(4, which, land_y.at[1, which]))
                pl.when(y == 0)(lambda: merge(2, which, land_y.at[1, which]))
            run_if(comes[3], land)
            run_if(exists[4], lambda: kv_send(which, 4))

        def take_one(which):
            def land():
                kv_copy(which, 1).wait_recv()
                pl.when(y == 1)(lambda: merge(2, which, land_y.at[0, which]))
                pl.when(y == 0)(lambda: merge(0, which, land_y.at[0, which]))
            run_if(comes[1], land)

        def take_four(which):
            def land():
                kv_copy(which, 4).wait_recv()
                merge(2, which, land_z.at[1, which])
            run_if((z >= 1) & (z < NZ - 1), land)
            run_if(exists[2], lambda: kv_send(which, 2))

        def take_two(which):
            def land():
                kv_copy(which, 2).wait_recv()
                merge(0, which, land_z.at[0, which])
            run_if(z < NZ - 1, land)

        def unturn(which, grad_of):
            inner = jnp.zeros((rows, 1), f32)
            for head in range(heads):
                at = pl.ds(head * HEAD, HEAD)
                grad = turn(grad_of(at), cos_ref[...], -sin_ref[...])
                value = raw_ref[which, :, at]
                line_sum[1 + which : 2 + which, at] = jnp.sum(
                    grad * (value * scale_ref[:, 1 + which : 2 + which]), axis=0, keepdims=True
                )
                grad = grad * gain_ref[2 + which : 3 + which, at]
                scaled[which, :, at] = grad
                inner = inner + jnp.sum(grad * value, axis=-1, keepdims=True)
            return inner

        def denorm(which, inner):
            scale = scale_ref[:, 1 + which : 2 + which]
            rest = scale * scale * scale * inner / width
            for head in range(heads):
                at = pl.ds(head * HEAD, HEAD)
                proj[which, :, at] = (
                    scale * scaled[which, :, at] - raw_ref[which, :, at] * rest
                ).astype(low)

        def send_beside(s):
            for zz in Z_ORDER:
                buffer = slot(3)(s, zz)
                buffer[...] = own_part(s, zz * NY + 1 - y).astype(buffer.dtype)
                line.to_y(s, zz)

        exchange_rows(unturn(QUERY, lambda at: dq[:, at]), part_q, land_q, qs_s, qs_r, mates)
        take_three(1)
        take_three(0)
        denorm(QUERY, exchanged_rows(part_q, land_q, qs_s, qs_r, mates))
        send_beside(QUERY)
        da_spread()
        take_one(1)
        take_one(0)
        take_four(1)
        take_four(0)
        take_two(1)
        proj[VALUE] = dkv[0, 1].astype(low)
        send_beside(VALUE)
        take_two(0)
        exchange_rows(unturn(KEY, lambda at: dkv[0, 0, :, at]), part_k, land_k, ks_s, ks_r, mates)
        denorm(KEY, exchanged_rows(part_k, land_k, ks_s, ks_r, mates))
        send_beside(KEY)
        fetch.wait()

        def half_of(cc):
            def body(i, carry):
                at = pl.ds(pl.multiple_of(cc * half + i * quarter, quarter), quarter)
                value = dot(proj[0], weights[0, at, :], (1, 1))
                for s in (1, 2):
                    value = value + dot(proj[s], weights[s, at, :], (1, 1))
                part[:, at] = value.astype(low)
                return carry

            lax.fori_loop(0, 2, body, 0)

        stages = group_stages(part, full, core_buf, x_buf, group_s, group_r)
        half_of(1 - c)
        stages[0]()
        half_of(c)
        stages[1]()

        def hop(s, zz, k):
            def upward():
                if k > 0:
                    line.take(s, zz, 1)
                line.copy(s, zz, 1).start()

            def downward():
                if k > 0:
                    line.take(s, zz, 2)
                line.copy(s, zz, 2).start()

            if k < zz:
                run_if((z < zz) & (z == k), upward)
            if NZ - 1 - k > zz:
                run_if((z > zz) & (NZ - 1 - z == k), downward)

        def receive(s, zz):
            line.copy(s, zz, 0).wait_recv()
            buffer = slot(0)(s, zz)
            buffer[...] = (buffer[...].astype(f32) + own_part(s, zz * NY + y)).astype(buffer.dtype)

        units = []

        def run_units(s):
            for zz in Z_ORDER:
                receive(s, zz)
                hop(s, zz, 0)
                units.append((s, zz))
                for k in (1, 2):
                    if len(units) > k:
                        hop(*units[-1 - k], k)

        def norm_one(i, carry):
            r = pl.ds(pl.multiple_of(i * 32, 32), 32)
            grad, value, scale = full[r, :].astype(f32), tok_ref[r, :].astype(f32), scale_ref[r, 0:1]
            line_sum[3:4, :] += jnp.sum(grad * (value * scale), axis=0, keepdims=True)
            grad = grad * gain_ref[0:1, :]
            inner = jnp.mean(grad * value, axis=-1, keepdims=True)
            tok_grad[r, :] = (
                dx1[r, :] + scale * grad - value * (scale * scale * scale) * inner
            ).astype(low)
            return carry

        run_units(QUERY)
        stages[2]()
        run_units(VALUE)
        da_end()
        stages[3]()
        stages[4]()
        lax.fori_loop(0, rows // 32, norm_one, 0)
        for b in range(GROUPS):
            at = pl.ds(b * depth, depth)
            small[b, 0:1, :] = line_sum[3:4, at]
            small[b, 1:2, :] = line_sum[0:1, at]
            for which in range(2):
                for k in range(columns // depth):
                    small[b, 2 + 2 * which + k : 3 + 2 * which + k, :] = line_sum[
                        1 + which : 2 + which, pl.ds(k * depth, depth)
                    ]
        send_beside(SMALL)
        run_units(KEY)
        run_units(SMALL)
        hop(*units[-1], 1)
        hop(*units[-2], 2)
        hop(*units[-1], 2)

        def done(s, total):
            target = qkv_sum.at[s] if s < OUT else small_sum
            target[...] = total[...].astype(f32)

        line.streams = [QUERY, VALUE, KEY, SMALL]
        line.home(done)
        line.finish()
        for which in range(2):
            for k in (1, 2, 3, 4):
                run_if(exists[k], lambda which=which, k=k: kv_copy(which, k).wait_send())
        drain_rows(part_k, land_k, ks_s, ks_r, mates)
        drain_rows(part_q, land_q, qs_s, qs_r, mates)

    shape, dma, vmem = jax.ShapeDtypeStruct, pltpu.SemaphoreType.DMA, pltpu.VMEM
    return pl.pallas_call(
        kernel,
        out_shape=(
            shape((rows, width), low),
            shape((3, depth, columns), f32),
            shape((columns, depth), f32),
            shape((small_rows, depth), f32),
        ),
        in_specs=[HBM if k in (9, 14, 18, 19, 20, 21, 22) else VMEM for k in range(23)],
        out_specs=(VMEM,) * 4,
        scratch_shapes=[
            vmem(context.shape, low),
            vmem(raw.shape, f32),
            vmem(hidden_one.shape, low),
            vmem(tokens.shape, low),
            vmem(attended_all.shape, low),
            vmem(out_low.shape, low),
            dma((6,)),
            vmem(qkv_low.shape, low),
            vmem((rows, width), f32),
            vmem((rows, width), low),
            vmem((rows, columns), low),
            vmem((rows, 128), f32),
            vmem((rows, columns), f32),
            vmem((blocks, 2, rows, columns), f32),
            vmem((2, rows, columns), f32),
            vmem((3, rows, columns), low),
            vmem((blocks - 1, 2, rows, columns), low),
            vmem((2, 2, rows, columns), low),
            vmem((2, 2, rows, columns), low),
            vmem((rows, width), low),
            vmem((rows, width), low),
            vmem((rows, half), low),
            vmem((rows, quarter), low),
            vmem((GROUPS, small_rows, depth), f32),
            vmem((8, width), f32),
            vmem((4, NZ, 3, depth, columns), low),
            vmem((GROUPS, rows, depth), low),
            vmem((4, NZ, small_rows, depth), f32),
            vmem((8, rows), f32),
            vmem((tensors - 1, 8, rows), f32),
            vmem((8, rows), f32),
            vmem((tensors - 1, 8, rows), f32),
            dma, dma((2, 2)), dma((2, 2)), dma((2, 2)), dma((2, 2)), dma((5,)), dma((5,)),
            dma((tensors - 1,)), dma((tensors - 1,)), dma((tensors - 1,)), dma((tensors - 1,)),
            dma((5, NZ, 3)), dma((5, NZ, 3)), dma((GROUPS - 1,)), dma((GROUPS - 1,)), dma((tensors - 1,)), dma((tensors - 1,)),
        ],
        compiler_params=comm_params(collective_id, 62),
        cost_estimate=cost(130),
        name="attend_back",
    )(
        grad_hidden, grad_probs, router_t, hidden_two, residual, scale_two, gains, out_grad,
        query, context, segment_query, segment_keys, attended, log_sums, raw, scales,
        cosine, sine, hidden_one, tokens, attended_all, qkv_low, out_low,
    )


def fast_shards(
    tokens_in,
    out_grad,
    w_qkv,
    w_attn_out,
    attn_gain,
    ffn_gain,
    qk_gain,
    w_router,
    w_gate,
    w_up,
    w_down,
    routes,
    segments,
):
    row_count, model_width = tokens_in.shape
    experts = w_router.shape[1]
    local_experts = w_gate.shape[0]
    heads_here = qk_gain.shape[1]
    local_width = heads_here * HEAD
    groups = lax.axis_size("expert")
    device_index = lax.axis_index("expert")
    tensor_index = lax.axis_index("tensor")
    quarter = model_width // lax.axis_size("tensor")
    hop_count = WINDOW // row_count
    score_scale = HEAD ** (-0.5)
    low = jnp.bfloat16

    chosen = jnp.any(
        routes[:, :, None] == jnp.arange(experts, dtype=jnp.int32)[None, None, :], axis=1
    ).astype(jnp.float32)
    qk_row = qk_gain.reshape(1, -1)

    global_rows = device_index * row_count + jnp.arange(row_count, dtype=jnp.int32)
    cosine_table, sine_table = angles(global_rows % SEQ, HEAD)
    wide_cosine = jnp.concatenate([cosine_table[:, 0], cosine_table[:, 0]], axis=1)
    wide_sine = jnp.concatenate([-sine_table[:, 0], sine_table[:, 0]], axis=1)
    (
        qkv_low, out_low, grad_out_all, hidden_one, raw, gate_up, down_low, gains, router_t, chosen_all,
        scales, query_low, context_blocks,
    ) = project(
        tokens_in, w_qkv, w_attn_out, out_grad, attn_gain[None, :], ffn_gain[None, :], qk_row, w_router.T, routes.T,
        wide_cosine, wide_sine, w_gate, w_up, w_down, 0,
    )
    segment_window = lax.dynamic_slice_in_dim(
        jnp.concatenate([jnp.full((WINDOW,), -1, jnp.int32), segments]),
        device_index * row_count, (hop_count + 1) * row_count,
    )
    segment_query = segment_window[WINDOW:]
    segment_keys = segment_window.reshape(hop_count + 1, row_count)[::-1]
    attended, log_sums, residual, hidden_two, scale_two_wide = attend(
        query_low, context_blocks, segment_query[:, None], segment_keys, tokens_in, out_low,
        gains, 2,
    )
    (
        block_out, grad_hidden_sum, grad_gate_sum, grad_gate_w, grad_up_w, grad_down, attended_all
    ) = expert_layer(
        hidden_two, grad_out_all, gate_up, down_low, router_t, chosen_all, residual, attended, 5
    )
    grad_probs = grad_gate_sum[:, :local_experts].reshape(experts, row_count).T * chosen
    grad_tokens, qkv_sum, out_sum, small_sum = attend_back(
        grad_hidden_sum, grad_probs, router_t, hidden_two, residual, scale_two_wide,
        gains, out_grad, query_low, context_blocks, segment_query[:, None], segment_keys,
        attended, log_sums, raw, scales, wide_cosine, wide_sine, hidden_one, tokens_in, attended_all,
        qkv_low, out_low, 8,
    )
    return (
        block_out,
        grad_tokens,
        qkv_sum,
        out_sum,
        small_sum[0],
        small_sum[1],
        lax.dynamic_slice_in_dim(
            small_sum[2:6].reshape(2, heads_here, HEAD),
            device_index * qk_gain.shape[2], qk_gain.shape[2], axis=2,
        ),
        small_sum[8 : 8 + experts].T,
        grad_gate_w,
        grad_up_w,
        grad_down,
    )


def solution(mesh):
    placed = (
        P("expert", None),
        P("expert", None),
        P(None, "expert", "tensor"),
        P("tensor", "expert"),
        P("expert"),
        P("expert"),
        P(None, "tensor", "expert"),
        P("expert", None),
        P("expert", None, "tensor"),
        P("expert", None, "tensor"),
        P("expert", "tensor", None),
        P("expert", None),
        P(),
    )
    compact = (mesh.shape["expert"], mesh.shape["tensor"]) == (GROUPS, NX * NC)
    return jax.shard_map(
        fast_shards if compact else shards,
        mesh=mesh,
        in_specs=placed,
        out_specs=(
            P("expert", None),
            P("expert", None),
            P(None, "expert", "tensor"),
            P("tensor", "expert"),
            P("expert"),
            P("expert"),
            P(None, "tensor", "expert"),
            P("expert", None),
            P("expert", None, "tensor"),
            P("expert", None, "tensor"),
            P("expert", "tensor", None),
        ),
        check_vma=False,
    )
```
